32 devices in a mesh: wide: 16 (over z, y, x), narrow: 2 (over core).
Axes of the slice: x: 2, y: 2, z: 4, core: 2. Of those that a mesh axis runs over, the one named last changes fastest.
Arguments:
- tokens: int32 [128, 20, 16], P('wide'), may hold values from 0 to 511
- actions: int32 [128, 20], P('wide'), may hold values from 0 to 17
- game_ids: int32 [128], P('wide'), may hold values from 0 to 25
- valid_steps: int32 [128, 20], P('wide'), may hold values from 0 to 1, as said below
- rewards: int32 [128, 20], P('wide'), may hold values from 0 to 2
- end_flags: int32 [128, 20], P('wide'), may hold values from 0 to 1
- embed_table: float32 [896, 256], P(None, 'wide'), may hold values from -6 to 6
- table_first: float32 [896, 256], P(None, 'wide'), may hold values from -0.0009765625 to 0.0009765625
- table_second: float32 [896, 256], P(None, 'wide'), may hold values from 5.154044e-09 to 2.0616175e-08
- attn_weight: float32 [2, 3, 256, 256], P(None, None, 'wide', 'narrow'), may hold values from -0.375 to 0.375
- attn_first: float32 [2, 3, 256, 256], P(None, None, 'wide', 'narrow'), may hold values from -0.0009765625 to 0.0009765625
- attn_second: float32 [2, 3, 256, 256], P(None, None, 'wide', 'narrow'), may hold values from 5.154044e-09 to 2.0616175e-08
- proj_weight: float32 [2, 256, 256], P(None, 'narrow', 'wide'), may hold values from -3 to 3
- proj_first: float32 [2, 256, 256], P(None, 'narrow', 'wide'), may hold values from -0.0009765625 to 0.0009765625
- proj_second: float32 [2, 256, 256], P(None, 'narrow', 'wide'), may hold values from 5.154044e-09 to 2.0616175e-08
- up_weight: float32 [2, 256, 1024], P(None, 'wide', 'narrow'), may hold values from -0.375 to 0.375
- up_first: float32 [2, 256, 1024], P(None, 'wide', 'narrow'), may hold values from -0.0009765625 to 0.0009765625
- up_second: float32 [2, 256, 1024], P(None, 'wide', 'narrow'), may hold values from 5.154044e-09 to 2.0616175e-08
- up_bias: float32 [2, 1024], P(None, 'narrow'), may hold values from -0.35 to 0.35
- bias_first: float32 [2, 1024], P(None, 'narrow'), may hold values from -0.00030517578 to 0.00030517578
- bias_second: float32 [2, 1024], P(None, 'narrow'), may hold values from 4.1232354e-10 to 1.6492941e-09
- down_weight: float32 [2, 1024, 256], P(None, 'narrow', 'wide'), may hold values from -0.1875 to 0.1875
- down_first: float32 [2, 1024, 256], P(None, 'narrow', 'wide'), may hold values from -0.0009765625 to 0.0009765625
- down_second: float32 [2, 1024, 256], P(None, 'narrow', 'wide'), may hold values from 5.154044e-09 to 2.0616175e-08
- vectors: float32 [14, 256], replicated, may hold values from -0.5 to 2.4
- vectors_first: float32 [14, 256], replicated, may hold values from -0.0034179688 to 0.0034179688
- vectors_second: float32 [14, 256], replicated, may hold values from 4.6386397e-08 to 1.8554559e-07
- head_weight: float32 [256, 512], P('wide', 'narrow'), may hold values from -0.32 to 0.32
- head_first: float32 [256, 512], P('wide', 'narrow'), may hold values from -0.0009765625 to 0.0009765625
- head_second: float32 [256, 512], P('wide', 'narrow'), may hold values from 5.154044e-09 to 2.0616175e-08
- side_weight: float32 [256, 5], P('wide'), may hold values from -0.375 to 0.375
- side_first: float32 [256, 5], P('wide'), may hold values from -0.0009765625 to 0.0009765625
- side_second: float32 [256, 5], P('wide'), may hold values from 5.154044e-09 to 2.0616175e-08
Outputs:
- loss_sum: float32 [], replicated
- valid_total: float32 [], replicated
- grad_norm: float32 [], replicated
- table_new: float32 [896, 256], P(None, 'wide')
- table_first_new: float32 [896, 256], P(None, 'wide')
- table_second_new: float32 [896, 256], P(None, 'wide')
- attn_new: float32 [2, 3, 256, 256], P(None, None, 'wide', 'narrow')
- attn_first_new: float32 [2, 3, 256, 256], P(None, None, 'wide', 'narrow')
- attn_second_new: float32 [2, 3, 256, 256], P(None, None, 'wide', 'narrow')
- proj_new: float32 [2, 256, 256], P(None, 'narrow', 'wide')
- proj_first_new: float32 [2, 256, 256], P(None, 'narrow', 'wide')
- proj_second_new: float32 [2, 256, 256], P(None, 'narrow', 'wide')
- up_new: float32 [2, 256, 1024], P(None, 'wide', 'narrow')
- up_first_new: float32 [2, 256, 1024], P(None, 'wide', 'narrow')
- up_second_new: float32 [2, 256, 1024], P(None, 'wide', 'narrow')
- bias_new: float32 [2, 1024], P(None, 'narrow')
- bias_first_new: float32 [2, 1024], P(None, 'narrow')
- bias_second_new: float32 [2, 1024], P(None, 'narrow')
- down_new: float32 [2, 1024, 256], P(None, 'narrow', 'wide')
- down_first_new: float32 [2, 1024, 256], P(None, 'narrow', 'wide')
- down_second_new: float32 [2, 1024, 256], P(None, 'narrow', 'wide')
- vectors_new: float32 [14, 256], replicated
- vectors_first_new: float32 [14, 256], replicated
- vectors_second_new: float32 [14, 256], replicated
- head_new: float32 [256, 512], P('wide', 'narrow')
- head_first_new: float32 [256, 512], P('wide', 'narrow')
- head_second_new: float32 [256, 512], P('wide', 'narrow')
- side_new: float32 [256, 5], P('wide')
- side_first_new: float32 [256, 5], P('wide')
- side_second_new: float32 [256, 5], P('wide')
The draws below stay inside these ranges and needn't reach their ends.
Inputs may be any that keep to these rules, and one draw needn't show every extreme that they name: `valid_steps`: frame 0 of every sequence is valid.
All inputs are finite; a program needn't handle non-finite values.
Results may differ from the reference program's by a relative error of at most 0.0098.
Values may be sent and summed in bfloat16 or wider, within the bound.
No kernel may reach another device: no remote copies, remote signals or barrier semaphores. Data moves between devices by JAX's collectives and lax.ppermute only.
A program may use at most 192 MiB of HBM per device.

```python
import math
import jax
import jax.numpy as jnp
from jax import lax

D = 256
HEADS = 4
HEAD_DIM = 64
FF = 1024
VOCAB = 512
ACTIONS = 18
GAMES = 26
OBS = 16
FRAMES = 20
L = 2
STEP_NUMBER = 5
FRAME_TOKENS = 17
LENGTH = 340
SEQS = 128
ROWS = 896
NVEC = 14
NPARAM = 1940224
N_WIDE = 16


def draw_valid_steps(key, part):
    key = jax.random.fold_in(key, 11)
    rolls = jax.random.randint(key, (SEQS, FRAMES), 0, 100)
    order = jnp.arange(SEQS, dtype=jnp.int32)[:, None]
    limit = 25 + 60 * order // max(SEQS - 1, 1)
    picked = (rolls < limit).astype(jnp.int32)
    leading = (jnp.arange(FRAMES, dtype=jnp.int32) == 0)[None, :]
    return jnp.where(leading, 1, picked).astype(jnp.int32)


def draw_vectors(key, part):
    key = jax.random.fold_in(key, 12)
    key_gain, key_bias = jax.random.split(key)
    rows = jnp.arange(NVEC)[:, None]
    columns = jnp.arange(D, dtype=jnp.float32)[None, :] / (D - 1)
    is_gain = (rows < 6 * L) & ((rows % 6 == 0) | (rows % 6 == 3)) | (rows == 6 * L)
    noise = jax.random.uniform(key_gain, (NVEC, D), jnp.float32, 0.8, 1.2)
    ramp = 0.5 + columns
    biases = jax.random.uniform(key_bias, (NVEC, D), jnp.float32, -0.35, 0.35)
    return jnp.where(is_gain, ramp * noise, biases).astype(jnp.float32)


def draw_head_weight(key, part):
    key = jax.random.fold_in(key, 13)
    columns = jnp.arange(VOCAB, dtype=jnp.float32)[None, :] / (VOCAB - 1)
    base = jax.random.uniform(key, (D, VOCAB), jnp.float32, -1.7, 1.7)
    ramp = 1.0 + 2.0 * columns
    return (base * ramp * D ** (-0.5)).astype(jnp.float32)


def set_ends(entries, stream_key, least, largest):
    spot = [jax.random.randint(jax.random.fold_in(stream_key, axis), (), 0, length) for axis, length in enumerate(entries.shape)]
    widest = entries.shape.index(max(entries.shape))
    neighbour = spot[:widest] + [(spot[widest] + 1) % entries.shape[widest]] + spot[widest + 1:]
    return entries.at[tuple(spot)].set(least).at[tuple(neighbour)].set(largest)


def block_scale(stream_key, shape, cuts, low, top_value):
    level = 1.0
    for dim, parts in cuts:
        draws = jax.random.uniform(jax.random.fold_in(jax.random.fold_in(stream_key, 6), dim), (parts,), jnp.float32, low / len(cuts), top_value / len(cuts))
        level = level * jnp.repeat(jnp.exp(draws), shape[dim] // parts).reshape((-1,) + (1,) * (len(shape) - 1 - dim))
    return level


def scatter_about(stream_key, dims, spread, bound, cuts=(), held_as=jnp.bfloat16):
    level = block_scale(stream_key, dims, cuts, -0.22, 0.18) if cuts else 1.0
    result = jax.random.normal(stream_key, dims, jnp.float32) * spread * level
    return jnp.minimum(jnp.maximum(result, -bound), bound).astype(held_as)


def setup_inputs(seed: int = 0) -> dict:
    streams_of = jax.random.split(jax.random.key(seed), 34)
    return {
        "tokens": set_ends(jax.random.randint(streams_of[0], (SEQS, FRAMES, OBS), 0, VOCAB), jax.random.fold_in(streams_of[0], 1), 0, VOCAB - 1).astype(jnp.int32),
        "actions": set_ends(jax.random.randint(streams_of[1], (SEQS, FRAMES), 0, ACTIONS), jax.random.fold_in(streams_of[1], 1), 0, ACTIONS - 1).astype(jnp.int32),
        "game_ids": set_ends(jax.random.randint(streams_of[2], (SEQS,), 0, GAMES), jax.random.fold_in(streams_of[2], 1), 0, GAMES - 1).astype(jnp.int32),
        "valid_steps": draw_valid_steps(jax.random.fold_in(streams_of[33], 71), 0),
        "rewards": set_ends(jax.random.randint(streams_of[4], (SEQS, FRAMES), 0, 3), jax.random.fold_in(streams_of[4], 1), 0, 2).astype(jnp.int32),
        "end_flags": set_ends(jax.random.randint(streams_of[5], (SEQS, FRAMES), 0, 2), jax.random.fold_in(streams_of[5], 1), 0, 1).astype(jnp.int32),
        "embed_table": scatter_about(streams_of[6], (ROWS, D), 1.0, 6.0, ((1, 16),), jnp.float32),
        "table_first": scatter_about(streams_of[7], (ROWS, D), (0.1 * NPARAM ** -0.5), 0.0009765625, ((1, 16),), jnp.float32),
        "table_second": jnp.clip(jnp.exp(math.log(2.0616175433474382e-08) - 1.3862944 * jax.random.uniform(streams_of[8], (ROWS, D), jnp.float32) ** block_scale(streams_of[8], (ROWS, D), ((1, 16),), -0.2, 0.2)), 5.1540438583685955e-09, 2.0616175433474382e-08),
        "attn_weight": scatter_about(streams_of[9], (L, 3, D, D), D ** -0.5, 0.375, ((2, 16), (3, 2)), jnp.float32),
        "attn_first": scatter_about(streams_of[10], (L, 3, D, D), (0.1 * NPARAM ** -0.5), 0.0009765625, ((2, 16), (3, 2)), jnp.float32),
        "attn_second": jnp.clip(jnp.exp(math.log(2.0616175433474382e-08) - 1.3862944 * jax.random.uniform(streams_of[11], (L, 3, D, D), jnp.float32) ** block_scale(streams_of[11], (L, 3, D, D), ((2, 16), (3, 2)), -0.2, 0.2)), 5.1540438583685955e-09, 2.0616175433474382e-08),
        "proj_weight": scatter_about(streams_of[12], (L, D, D), (D // 64) ** -0.5, 3.0, ((1, 2), (2, 16)), jnp.float32),
        "proj_first": scatter_about(streams_of[13], (L, D, D), (0.1 * NPARAM ** -0.5), 0.0009765625, ((1, 2), (2, 16)), jnp.float32),
        "proj_second": jnp.clip(jnp.exp(math.log(2.0616175433474382e-08) - 1.3862944 * jax.random.uniform(streams_of[14], (L, D, D), jnp.float32) ** block_scale(streams_of[14], (L, D, D), ((1, 2), (2, 16)), -0.2, 0.2)), 5.1540438583685955e-09, 2.0616175433474382e-08),
        "up_weight": scatter_about(streams_of[15], (L, D, FF), D ** -0.5, 0.375, ((1, 16), (2, 2)), jnp.float32),
        "up_first": scatter_about(streams_of[16], (L, D, FF), (0.1 * NPARAM ** -0.5), 0.0009765625, ((1, 16), (2, 2)), jnp.float32),
        "up_second": jnp.clip(jnp.exp(math.log(2.0616175433474382e-08) - 1.3862944 * jax.random.uniform(streams_of[17], (L, D, FF), jnp.float32) ** block_scale(streams_of[17], (L, D, FF), ((1, 16), (2, 2)), -0.2, 0.2)), 5.1540438583685955e-09, 2.0616175433474382e-08),
        "up_bias": jnp.clip(jax.random.uniform(streams_of[18], (L, FF), jnp.float32, -0.35, 0.35) * block_scale(streams_of[18], (L, FF), ((1, 2),), -0.4, 0.0), -0.35, 0.35),
        "bias_first": scatter_about(streams_of[19], (L, FF), (0.03 * NPARAM ** -0.5), 0.00030517578, ((1, 2),), jnp.float32),
        "bias_second": jnp.clip(jnp.exp(math.log(1.649294145700253e-09) - 1.3862944 * jax.random.uniform(streams_of[20], (L, FF), jnp.float32) ** block_scale(streams_of[20], (L, FF), ((1, 2),), -0.2, 0.2)), 4.1232353642506325e-10, 1.649294145700253e-09),
        "down_weight": scatter_about(streams_of[21], (L, FF, D), FF ** -0.5, 0.1875, ((1, 2), (2, 16)), jnp.float32),
        "down_first": scatter_about(streams_of[22], (L, FF, D), (0.1 * NPARAM ** -0.5), 0.0009765625, ((1, 2), (2, 16)), jnp.float32),
        "down_second": jnp.clip(jnp.exp(math.log(2.0616175433474382e-08) - 1.3862944 * jax.random.uniform(streams_of[23], (L, FF, D), jnp.float32) ** block_scale(streams_of[23], (L, FF, D), ((1, 2), (2, 16)), -0.2, 0.2)), 5.1540438583685955e-09, 2.0616175433474382e-08),
        "vectors": draw_vectors(jax.random.fold_in(streams_of[33], 71), 0),
        "vectors_first": scatter_about(streams_of[25], (NVEC, D), (0.3 * NPARAM ** -0.5), 0.0034179688, (), jnp.float32),
        "vectors_second": jnp.clip(jnp.exp(jax.random.uniform(streams_of[26], (NVEC, D), jnp.float32, math.log(4.638639694576341e-08), math.log(1.8554558778305363e-07))), 4.638639694576341e-08, 1.8554558778305363e-07),
        "head_weight": draw_head_weight(jax.random.fold_in(streams_of[33], 71), 0),
        "head_first": scatter_about(streams_of[28], (D, VOCAB), (0.1 * NPARAM ** -0.5), 0.0009765625, ((0, 16), (1, 2)), jnp.float32),
        "head_second": jnp.clip(jnp.exp(math.log(2.0616175433474382e-08) - 1.3862944 * jax.random.uniform(streams_of[29], (D, VOCAB), jnp.float32) ** block_scale(streams_of[29], (D, VOCAB), ((0, 16), (1, 2)), -0.2, 0.2)), 5.1540438583685955e-09, 2.0616175433474382e-08),
        "side_weight": scatter_about(streams_of[30], (D, 5), D ** -0.5, 0.375, ((0, 16),), jnp.float32),
        "side_first": scatter_about(streams_of[31], (D, 5), (0.1 * NPARAM ** -0.5), 0.0009765625, ((0, 16),), jnp.float32),
        "side_second": jnp.clip(jnp.exp(math.log(2.0616175433474382e-08) - 1.3862944 * jax.random.uniform(streams_of[32], (D, 5), jnp.float32) ** block_scale(streams_of[32], (D, 5), ((0, 16),), -0.2, 0.2)), 5.1540438583685955e-09, 2.0616175433474382e-08),
    }


@jax.custom_vjp
def low(v):
    return lax.optimization_barrier(v.astype(jnp.bfloat16)).astype(jnp.float32)

@jax.custom_vjp
def low_back(v):
    return v

def low_keep(v):
    return (low(v), None)

def low_pass(kept, grad):
    return (grad,)

def back_keep(v):
    return (v, None)

def back_low(kept, grad):
    return (low(grad),)
low.defvjp(low_keep, low_pass)
low_back.defvjp(back_keep, back_low)
PRECISE = lax.Precision.HIGHEST
EPS_NORM = 1e-05
BETA_ONE = 0.5
BETA_TWO = 0.5
RATE_TABLE = 0.5
RATE_MATRIX = 0.05
RATE_VECTOR = 0.2
DECAY_RATE = 0.01
EPS_ADAM = 1e-08
CLIP_AT = 0.1

def layer_norm(stream, gain, offset):
    row_mean = lax.optimization_barrier(jnp.mean(stream, axis=-1, keepdims=True))
    centred = stream - row_mean
    variance = lax.optimization_barrier(jnp.mean(centred * centred, axis=-1, keepdims=True))
    return centred * lax.rsqrt(variance + EPS_NORM) * gain + offset

def arrange(tokens, actions, valid_steps):
    seq_count = tokens.shape[0]
    row_ids = jnp.concatenate([tokens, actions[:, :, None] + VOCAB], axis=2).reshape(seq_count, LENGTH)
    first_next = jnp.concatenate([tokens[:, 1:, 0], jnp.zeros((seq_count, 1), jnp.int32)], axis=1)
    targets = jnp.concatenate([tokens[:, :, 1:], jnp.zeros((seq_count, FRAMES, 1), jnp.int32), first_next[:, :, None]], axis=2).reshape(seq_count, LENGTH)
    valid_float = valid_steps.astype(jnp.float32)
    next_valid = jnp.concatenate([valid_float[:, 1:], jnp.zeros((seq_count, 1), jnp.float32)], axis=1)
    row_weight = jnp.concatenate([jnp.broadcast_to(valid_float[:, :, None], (seq_count, FRAMES, OBS - 1)), jnp.zeros((seq_count, FRAMES, 1), jnp.float32), next_valid[:, :, None]], axis=2).reshape(seq_count, LENGTH)
    return (row_ids, targets, row_weight, valid_float)

def side_loss(side_logits, rewards, end_flags, valid_float):
    reward_logits = side_logits[..., :3]
    end_logits = side_logits[..., 3:]
    reward_pick = lax.optimization_barrier(jnp.sum(jnp.where(rewards[..., None] == jnp.arange(3), reward_logits, 0.0), axis=-1))
    end_pick = lax.optimization_barrier(jnp.sum(jnp.where(end_flags[..., None] == jnp.arange(2), end_logits, 0.0), axis=-1))
    terms = jax.nn.logsumexp(reward_logits, axis=-1) - reward_pick + jax.nn.logsumexp(end_logits, axis=-1) - end_pick
    return jnp.sum(valid_float * terms)

def attention(query, keys, values):
    scores = low_back(jnp.einsum('sqhe,skhe->shqk', query, keys, precision=PRECISE) * 0.125)
    causal = jnp.arange(LENGTH)[:, None] >= jnp.arange(LENGTH)[None, :]
    scores = jnp.where(causal, scores, -1e+30)
    attn_probs = low(jax.nn.softmax(scores, axis=-1))
    return jnp.einsum('shqk,skhe->sqhe', attn_probs, values, precision=PRECISE)

def group_loss(params, batched):
    embed_table, attn_weight, proj_weight, up_weight, up_bias, down_weight, vectors, head_weight, side_weight = params
    row_ids, targets, row_weight, game_ids, valid_float, rewards, end_flags = batched
    seq_count = row_ids.shape[0]
    embedded = embed_table[row_ids] + embed_table[VOCAB + ACTIONS + game_ids][:, None, :] + embed_table[VOCAB + ACTIONS + GAMES + jnp.arange(LENGTH)][None, :, :]
    stream = low_back(embedded)
    for index in range(L):
        layer_vec = vectors[6 * index:6 * index + 6]
        normed = low(layer_norm(stream, layer_vec[0], layer_vec[1]))
        projected = low_back(low(jnp.einsum('spd,jde->jspe', normed, attn_weight[index], precision=PRECISE)))
        parts_qkv = projected.reshape(3, seq_count, LENGTH, HEADS, HEAD_DIM)
        head_out = low_back(low(attention(parts_qkv[0], parts_qkv[1], parts_qkv[2]).reshape(seq_count, LENGTH, D)))
        stream = stream + low_back(jnp.einsum('spd,de->spe', head_out, proj_weight[index], precision=PRECISE) + layer_vec[2])
        normed = low(layer_norm(stream, layer_vec[3], layer_vec[4]))
        up_proj = low_back(jnp.einsum('spd,df->spf', normed, up_weight[index], precision=PRECISE) + up_bias[index])
        hidden = low(jax.nn.gelu(up_proj))
        stream = stream + low_back(jnp.einsum('spf,fd->spd', hidden, down_weight[index], precision=PRECISE) + layer_vec[5])
    final_norm = low(layer_norm(stream, vectors[6 * L], vectors[6 * L + 1]))
    logits = low_back(jnp.einsum('spd,dv->spv', final_norm, head_weight, precision=PRECISE))
    picked = jnp.take_along_axis(logits, targets[:, :, None], axis=2)[:, :, 0]
    token_loss = jnp.sum(row_weight * (jax.nn.logsumexp(logits, axis=2) - picked))
    acting = final_norm.reshape(seq_count, FRAMES, FRAME_TOKENS, D)[:, :, OBS]
    side_logits = low_back(jnp.einsum('sfd,dc->sfc', acting, side_weight, precision=PRECISE))
    return token_loss + side_loss(side_logits, rewards, end_flags, valid_float)

def adam(weight, moment, second, gradient, step_rate, decay_rate):
    moment_new = BETA_ONE * moment + (1.0 - BETA_ONE) * gradient
    second_new = BETA_TWO * second + (1.0 - BETA_TWO) * gradient * gradient
    moment_hat = moment_new / (1.0 - BETA_ONE ** STEP_NUMBER)
    second_hat = second_new / (1.0 - BETA_TWO ** STEP_NUMBER)
    weight_new = weight - step_rate * (moment_hat / (jnp.sqrt(second_hat) + EPS_ADAM) + decay_rate * weight)
    return (weight_new, moment_new, second_new)

def reference(tokens, actions, game_ids, valid_steps, rewards, end_flags, embed_table, table_first, table_second, attn_weight, attn_first, attn_second, proj_weight, proj_first, proj_second, up_weight, up_first, up_second, up_bias, bias_first, bias_second, down_weight, down_first, down_second, vectors, vectors_first, vectors_second, head_weight, head_first, head_second, side_weight, side_first, side_second):
    row_ids, targets, row_weight, valid_float = arrange(tokens, actions, valid_steps)
    total_valid = jnp.sum(valid_float)
    group_count = N_WIDE

    def regroup(array):
        return array.reshape((group_count, array.shape[0] // group_count) + array.shape[1:])
    batched = tuple((regroup(array) for array in (row_ids, targets, row_weight, game_ids, valid_float, rewards, end_flags)))
    params = (embed_table, attn_weight, proj_weight, up_weight, up_bias, down_weight, vectors, head_weight, side_weight)

    def total_loss(params):
        lowered = tuple((member if position in (4, 6) else low(member) for position, member in enumerate(params)))

        def group_step(carry, piece):
            return (carry + jax.checkpoint(group_loss)(lowered, piece), None)
        loss_value, unused = lax.scan(group_step, jnp.zeros((), jnp.float32), batched)
        return loss_value
    loss_sum, pullback = jax.vjp(total_loss, params)
    grads = pullback(jnp.ones((), jnp.float32) / total_valid)[0]
    squares = sum((jnp.sum(member * member) for member in grads))
    grad_norm = jnp.sqrt(squares)
    clip_factor = jnp.minimum(1.0, CLIP_AT / (grad_norm + 1e-06))
    moments = ((table_first, table_second), (attn_first, attn_second), (proj_first, proj_second), (up_first, up_second), (bias_first, bias_second), (down_first, down_second), (vectors_first, vectors_second), (head_first, head_second), (side_first, side_second))
    results = []
    for position in range(9):
        vector_kind = position in (4, 6)
        step_rate = RATE_VECTOR if vector_kind else RATE_TABLE if position == 0 else RATE_MATRIX
        decay_rate = 0.0 if vector_kind else DECAY_RATE
        results.extend(adam(params[position], moments[position][0], moments[position][1], clip_factor * grads[position], step_rate, decay_rate))
    return (loss_sum, total_valid, grad_norm) + tuple(results)
```

```python
import functools

import jax
import jax.numpy as jnp
from jax import lax
from jax.experimental import pallas as pl
from jax.experimental.pallas import tpu as pltpu
from jax.sharding import PartitionSpec as P

D = 256
HEADS = 4
HEAD_DIM = 64
FF = 1024
VOCAB = 512
ACTIONS = 18
GAMES = 26
OBS = 16
FRAMES = 20
STEP_NUMBER = 5
FRAME_TOKENS = 17
LENGTH = 340
ROWS = 896
NVEC = 14

EPS_NORM = 1e-05
BETA_ONE = 0.5
BETA_TWO = 0.5
RATE_TABLE = 0.5
RATE_MATRIX = 0.05
RATE_VECTOR = 0.2
DECAY_RATE = 0.01
EPS_ADAM = 1e-08
CLIP_AT = 0.1

SEQ = 352
KEYS = 384
QBLOCKS = ((0, 128, 128), (128, 128, 256), (256, 96, 384))

COL_QKV, COL_PROJ, COL_UP, COL_DOWN, COL_LAYER = 0, 768, 1024, 2048, 3072
HALF_LAYER = (
    (0, 128, 0),
    (128, 128, 256),
    (256, 128, 512),
    (384, 128, COL_PROJ),
    (512, 512, COL_UP),
    (1024, 512, COL_DOWN),
)
HALF_LAYER_COLS = 1536
COL_TABLE, COL_SMALL, COL_FIRST = 3072, 3968, 4096
HALF_FIRST = HALF_LAYER + ((1536, 512, COL_TABLE),)
HALF_FIRST_COLS = 2048
COL_HEAD, COL_SECOND = 3072, 3584
HALF_SECOND = HALF_LAYER + ((1536, 256, COL_HEAD),)
HALF_SECOND_COLS = 1792
SMALL_BIAS, SMALL_SIDE, SMALL_SCALAR = 14, 22, 32

F32, BF16 = jnp.float32, jnp.bfloat16
VMEM_BYTES = 60 * 1024 * 1024


def dot_nn(a, b):
    return lax.dot_general(a, b, (((1,), (0,)), ((), ())), preferred_element_type=F32)


def dot_nt(a, b):
    return lax.dot_general(a, b, (((1,), (1,)), ((), ())), preferred_element_type=F32)


def dot_tn(a, b):
    return lax.dot_general(a, b, (((0,), (0,)), ((), ())), preferred_element_type=F32)


def normalise(x):
    centred = x - jnp.mean(x, axis=1, keepdims=True)
    scale = lax.rsqrt(jnp.mean(centred * centred, axis=1, keepdims=True) + EPS_NORM)
    return centred * scale, scale


def normalise_back(grad, xhat, scale, gain):
    inner = grad * gain
    mean_one = jnp.mean(inner, axis=1, keepdims=True)
    mean_two = jnp.mean(inner * xhat, axis=1, keepdims=True)
    return scale * (inner - mean_one - xhat * mean_two)


def column_sum(a):
    return jnp.sum(a, axis=0, keepdims=True)


def head_masks(a, scale=None):
    lane = lax.broadcasted_iota(jnp.int32, (1, D), 1)
    zero = jnp.zeros((), a.dtype)
    if scale is not None:
        a = a * jnp.asarray(scale, a.dtype)
    return [
        jnp.where((lane >= h * HEAD_DIM) & (lane < (h + 1) * HEAD_DIM), a, zero)
        for h in range(HEADS)
    ]


def assemble(pieces_mine, pieces_other, place_ref, w_ref, halves):
    me, core = place_ref[0], place_ref[1]
    is_first = core == 0
    for p in range(4):
        for z in range(4):
            row = pl.multiple_of((me ^ (4 * z + p)) * 16, 16)
            for src, width, dest in halves:
                mine = pieces_mine[p][z, :, src : src + width]
                other = pieces_other[p][z, :, src : src + width]
                w_ref[pl.ds(row, 16), dest : dest + width] = jnp.where(is_first, mine, other)
                w_ref[pl.ds(row, 16), dest + width : dest + 2 * width] = jnp.where(
                    is_first, other, mine
                )


def disperse(g_ref, place_ref, keep_ref, send_ref, halves):
    me, core = place_ref[0], place_ref[1]
    is_first = core == 0
    for p in range(4):
        for z in range(4):
            row = pl.multiple_of((me ^ (4 * z + p)) * 16, 16)
            for src, width, dest in halves:
                low = g_ref[pl.ds(row, 16), dest : dest + width]
                high = g_ref[pl.ds(row, 16), dest + width : dest + 2 * width]
                keep_ref[p, z, :, src : src + width] = jnp.where(is_first, low, high)
                send_ref[p, z, :, src : src + width] = jnp.where(is_first, high, low).astype(BF16)


def make_hits(meta):
    lane = lax.broadcasted_iota(jnp.int32, (SEQ, 640), 1)
    place = lax.broadcasted_iota(jnp.int32, (SEQ, ROWS), 0) + (VOCAB + ACTIONS + GAMES)
    place_hit = place == lax.broadcasted_iota(jnp.int32, (SEQ, ROWS), 1)
    hit = (lane == meta[:, 0:1]) | (lane == meta[:, 1:2]) | place_hit[:, :640]
    one, zero = jnp.ones((), F32), jnp.zeros((), F32)
    return jnp.concatenate(
        [jnp.where(hit, one, zero).astype(BF16), jnp.where(place_hit[:, 640:], one, zero).astype(BF16)],
        axis=1,
    )


def layer_forward(x, w_ref, vec, bias, kept):
    x_ref, qkv_ref, p_refs, o_ref, m_ref, h_ref, gp_ref = kept
    normed16 = (normalise(x)[0] * vec[0:1] + vec[1:2]).astype(BF16)
    qkv_ref[0:SEQ] = dot_nn(normed16, w_ref[:, COL_QKV : COL_QKV + 768]).astype(BF16)
    qkv_ref[SEQ:KEYS] = jnp.zeros((KEYS - SEQ, 768), BF16)
    values = head_masks(qkv_ref[:, 512:768])
    for (first, count, seen), p_ref in zip(QBLOCKS, p_refs):
        queries = jnp.concatenate(head_masks(qkv_ref[first : first + count, 0:256], 0.125), axis=0)
        scores = dot_nt(queries, qkv_ref[0:seen, 256:512]).reshape(HEADS, count, seen)
        row = lax.broadcasted_iota(jnp.int32, (count, seen), 0) + first
        causal = row >= lax.broadcasted_iota(jnp.int32, (count, seen), 1)
        scores = jnp.where(causal[None], scores, -1e30)
        expanded = jnp.exp(scores - jnp.max(scores, axis=2, keepdims=True))
        probs = expanded * (1.0 / jnp.sum(expanded, axis=2, keepdims=True))
        probs16 = probs.astype(BF16)
        p_ref[...] = probs16.reshape(HEADS * count, seen)
        out = dot_nn(
            jnp.concatenate([probs16[h] for h in range(HEADS)], axis=1),
            jnp.concatenate([values[h][0:seen] for h in range(HEADS)], axis=0),
        )
        o_ref[first : first + count] = out.astype(BF16)
    middle = x + (dot_nt(o_ref[...], w_ref[:, COL_PROJ : COL_PROJ + 256]) + vec[2:3])
    m_ref[...] = middle
    normed16 = (normalise(middle)[0] * vec[3:4] + vec[4:5]).astype(BF16)
    total = middle + vec[5:6]
    for chunk in range(4):
        cols = slice(256 * chunk, 256 * chunk + 256)
        up = dot_nn(normed16, w_ref[:, COL_UP + 256 * chunk : COL_UP + 256 * chunk + 256])
        up = up + bias[:, cols]
        square = up * up
        slope = 0.7978845608028654 + 0.1070322244089 * square
        bent = jnp.tanh(up * (0.7978845608028654 + 0.0356774081363 * square))
        half = 0.5 + 0.5 * bent
        hidden = up * half
        gp_ref[:, cols] = (half + hidden * (1.0 - bent) * slope).astype(BF16)
        hidden16 = hidden.astype(BF16)
        h_ref[:, cols] = hidden16
        total = total + dot_nt(
            hidden16, w_ref[:, COL_DOWN + 256 * chunk : COL_DOWN + 256 * chunk + 256]
        )
    return total


def layer_backward(grad_in, w_ref, vec, kept, g_ref, v_ref, v_row, bias_row, dkv_ref):
    x_ref, qkv_ref, p_refs, o_ref, m_ref, h_ref, gp_ref = kept
    grad_out16 = grad_in.astype(BF16)
    v_ref[v_row + 5 : v_row + 6] += column_sum(grad_out16.astype(F32))
    xhat, scale = normalise(m_ref[...])
    normed16 = (xhat * vec[3:4] + vec[4:5]).astype(BF16)
    grad_normed = None
    for chunk in range(4):
        cols = slice(256 * chunk, 256 * chunk + 256)
        cols_up = slice(COL_UP + 256 * chunk, COL_UP + 256 * chunk + 256)
        cols_down = slice(COL_DOWN + 256 * chunk, COL_DOWN + 256 * chunk + 256)
        grad_hidden = dot_nn(grad_out16, w_ref[:, cols_down])
        grad_up16 = (grad_hidden * gp_ref[:, cols].astype(F32)).astype(BF16)
        g_ref[:, cols_down] += dot_tn(grad_out16, h_ref[:, cols])
        g_ref[:, cols_up] += dot_tn(normed16, grad_up16)
        v_ref[bias_row + chunk : bias_row + chunk + 1] += column_sum(grad_up16.astype(F32))
        part = dot_nt(grad_up16, w_ref[:, cols_up])
        grad_normed = part if grad_normed is None else grad_normed + part
    v_ref[v_row + 3 : v_row + 4] += column_sum(grad_normed * xhat)
    v_ref[v_row + 4 : v_row + 5] += column_sum(grad_normed)
    grad_mid = grad_in + normalise_back(grad_normed, xhat, scale, vec[3:4])
    grad_att16 = grad_mid.astype(BF16)
    v_ref[v_row + 2 : v_row + 3] += column_sum(grad_att16.astype(F32))
    g_ref[:, COL_PROJ : COL_PROJ + 256] += dot_tn(grad_att16, o_ref[...])
    grad_heads = dot_nn(grad_att16, w_ref[:, COL_PROJ : COL_PROJ + 256]).astype(BF16)
    keys = head_masks(qkv_ref[:, 256:512], 0.125)
    dkv_ref[...] = jnp.zeros(dkv_ref.shape, F32)
    grad_query = []
    for (first, count, seen), p_ref in zip(QBLOCKS, p_refs):
        rows = slice(first, first + count)
        queries = jnp.concatenate(head_masks(qkv_ref[rows, 0:256], 0.125), axis=0)
        grads = jnp.concatenate(head_masks(grad_heads[rows]), axis=0)
        grad_probs = dot_nt(grads, qkv_ref[0:seen, 512:768])
        probs16 = p_ref[...]
        probs = probs16.astype(F32)
        inner = jnp.sum(probs * grad_probs, axis=1, keepdims=True)
        grad_scores = (probs * (grad_probs - inner)).astype(BF16)
        grad_query.append(
            dot_nn(
                jnp.concatenate(
                    [grad_scores[h * count : (h + 1) * count] for h in range(HEADS)], axis=1
                ),
                jnp.concatenate([keys[h][0:seen] for h in range(HEADS)], axis=0),
            ).astype(BF16)
        )
        dkv_ref[0:seen, 0:256] += dot_tn(grad_scores, queries)
        dkv_ref[0:seen, 256:512] += dot_tn(probs16, grads)
    grad_qkv = jnp.concatenate(
        [jnp.concatenate(grad_query, axis=0), dkv_ref[0:SEQ].astype(BF16)], axis=1
    )
    xhat, scale = normalise(x_ref[...])
    normed16 = (xhat * vec[0:1] + vec[1:2]).astype(BF16)
    g_ref[:, COL_QKV : COL_QKV + 768] += dot_tn(normed16, grad_qkv)
    grad_normed = dot_nt(grad_qkv, w_ref[:, COL_QKV : COL_QKV + 768])
    v_ref[v_row : v_row + 1] += column_sum(grad_normed * xhat)
    v_ref[v_row + 1 : v_row + 2] += column_sum(grad_normed)
    return grad_mid + normalise_back(grad_normed, xhat, scale, vec[0:1])


def first_forward_kernel(*refs):
    place_ref, meta_ref, vec_ref, bias_ref = refs[0:4]
    mine, other = refs[4:8], refs[8:12]
    w_out, next_ref = refs[12:14]
    x_ref, qkv_ref, p0, p1, p2, o_ref, m_ref, h_ref, gp_ref = refs[14:23]
    w_ref = refs[23]

    @pl.when(pl.program_id(0) == 0)
    def _():
        assemble(mine, other, place_ref, w_ref, HALF_FIRST)
        w_out[...] = w_ref[...]

    x = dot_nt(make_hits(meta_ref[0]), w_ref[:, COL_TABLE : COL_TABLE + ROWS])
    x_ref[0] = x
    kept = (
        x_ref.at[0],
        qkv_ref.at[0],
        (p0.at[0], p1.at[0], p2.at[0]),
        o_ref.at[0],
        m_ref.at[0],
        h_ref.at[0],
        gp_ref.at[0],
    )
    next_ref[0] = layer_forward(x, w_ref, vec_ref[0:6], bias_ref[0:1], kept)


def middle_kernel(*refs):
    place_ref, meta_ref, vec_ref, bias_ref, side_ref, in_ref = refs[0:6]
    mine, other = refs[6:10], refs[10:14]
    grad_ref, keep_ref, send_ref, v_out, side_out, scalar_ref = refs[14:20]
    w_ref, g_ref, v_ref, dkv_ref = refs[20:24]
    qkv_ref, p0, p1, p2, o_ref, m_ref, h_ref, gp_ref = refs[24:32]
    step = pl.program_id(0)

    @pl.when(step == 0)
    def _():
        assemble(mine, other, place_ref, w_ref, HALF_SECOND)
        w_ref[:, COL_SECOND:] = side_ref[...]
        g_ref[...] = jnp.zeros(g_ref.shape, F32)
        v_ref[...] = jnp.zeros(v_ref.shape, F32)
        scalar_ref[...] = jnp.zeros(scalar_ref.shape, F32)

    x_ref = in_ref.at[0]
    kept = (x_ref, qkv_ref, (p0, p1, p2), o_ref, m_ref, h_ref, gp_ref)
    last = layer_forward(x_ref[...], w_ref, vec_ref[6:12], bias_ref[1:2], kept)

    meta = meta_ref[0]
    xhat, scale = normalise(last)
    gain = vec_ref[12:13]
    final16 = (xhat * gain + vec_ref[13:14]).astype(BF16)
    both = dot_nn(final16, w_ref[:, COL_HEAD : COL_HEAD + VOCAB + 128])
    logits, side = both[:, :VOCAB], both[:, VOCAB:]
    weight = meta[:, 3:4].astype(F32)
    peak = jnp.max(logits, axis=1, keepdims=True)
    expanded = jnp.exp(logits - peak)
    total = jnp.sum(expanded, axis=1, keepdims=True)
    hit = lax.broadcasted_iota(jnp.int32, (SEQ, VOCAB), 1) == meta[:, 2:3]
    picked = jnp.sum(jnp.where(hit, logits, 0.0), axis=1, keepdims=True)
    loss = column_sum(weight * (peak + jnp.log(total) - picked))
    grad_logits = expanded * (weight / total) - jnp.where(hit, weight, 0.0)

    lane = lax.broadcasted_iota(jnp.int32, (SEQ, 128), 1)
    is_reward, is_end = lane < 3, (lane == 3) | (lane == 4)
    side_weight = meta[:, 4:5].astype(F32)
    reward_peak = jnp.max(jnp.where(is_reward, side, -1e30), axis=1, keepdims=True)
    end_peak = jnp.max(jnp.where(is_end, side, -1e30), axis=1, keepdims=True)
    side_peak = jnp.where(is_reward, reward_peak, end_peak)
    expanded = jnp.where(is_reward | is_end, jnp.exp(jnp.where(is_reward | is_end, side - side_peak, 0.0)), 0.0)
    reward_total = jnp.sum(jnp.where(is_reward, expanded, 0.0), axis=1, keepdims=True)
    end_total = jnp.sum(jnp.where(is_end, expanded, 0.0), axis=1, keepdims=True)
    side_hit = (lane == meta[:, 5:6]) | (lane == meta[:, 6:7])
    side_picked = jnp.sum(jnp.where(side_hit, side, 0.0), axis=1, keepdims=True)
    side_terms = reward_peak + jnp.log(reward_total) + end_peak + jnp.log(end_total) - side_picked
    loss = loss + column_sum(side_weight * side_terms)
    grad_side = expanded * jnp.where(is_reward, side_weight / reward_total, side_weight / end_total)
    grad_side = grad_side - jnp.where(side_hit, side_weight, 0.0)
    valid = column_sum(side_weight)
    scalar_lane = lax.broadcasted_iota(jnp.int32, (8, 128), 1)
    scalar_row = lax.broadcasted_iota(jnp.int32, (8, 128), 0) == 0
    scalar_ref[...] += jnp.where(scalar_row & (scalar_lane == SMALL_SCALAR), loss, 0.0)
    scalar_ref[...] += jnp.where(scalar_row & (scalar_lane == SMALL_SCALAR + 1), valid, 0.0)

    grad_both = jnp.concatenate([grad_logits.astype(BF16), grad_side.astype(BF16)], axis=1)
    g_ref[:, COL_HEAD : COL_HEAD + VOCAB + 128] += dot_tn(final16, grad_both)
    grad_final = dot_nt(grad_both, w_ref[:, COL_HEAD : COL_HEAD + VOCAB + 128])
    v_ref[12:13] += column_sum(grad_final * xhat)
    v_ref[13:14] += column_sum(grad_final)
    grad_last = normalise_back(grad_final, xhat, scale, gain)
    grad_ref[0] = layer_backward(
        grad_last, w_ref, vec_ref[6:12], kept, g_ref, v_ref, 6, SMALL_BIAS + 4, dkv_ref
    )

    @pl.when(step == pl.num_programs(0) - 1)
    def _():
        disperse(g_ref, place_ref, keep_ref, send_ref, HALF_SECOND)
        v_out[...] = v_ref[...]
        side_out[...] = g_ref[:, COL_SECOND:]


def first_backward_kernel(*refs):
    place_ref, meta_ref, vec_ref, w_ref, grad_ref, v_in, side_in = refs[0:7]
    x_ref, qkv_ref, p0, p1, p2, o_ref, m_ref, h_ref, gp_ref = refs[7:16]
    keep_ref, send_ref = refs[16:18]
    g_ref, v_ref, dkv_ref = refs[18:21]
    step = pl.program_id(0)

    @pl.when(step == 0)
    def _():
        g_ref[...] = jnp.zeros(g_ref.shape, F32)
        v_ref[...] = v_in[...]

    kept = (
        x_ref.at[0],
        qkv_ref.at[0],
        (p0.at[0], p1.at[0], p2.at[0]),
        o_ref.at[0],
        m_ref.at[0],
        h_ref.at[0],
        gp_ref.at[0],
    )
    grad_x = layer_backward(
        grad_ref[0], w_ref, vec_ref[0:6], kept, g_ref, v_ref, 0, SMALL_BIAS, dkv_ref
    )
    g_ref[:, COL_TABLE : COL_TABLE + ROWS] += dot_tn(grad_x.astype(BF16), make_hits(meta_ref[0]))

    @pl.when(step == pl.num_programs(0) - 1)
    def _():
        lane = lax.broadcasted_iota(jnp.int32, (D, 128), 1)
        small = jnp.transpose(v_ref[...])
        side = pltpu.roll(side_in[...], SMALL_SIDE, 1)
        g_ref[:, COL_SMALL:] = jnp.where(
            lane < SMALL_SIDE, small, jnp.where(lane < SMALL_SIDE + 5, side, 0.0)
        )
        disperse(g_ref, place_ref, keep_ref, send_ref, HALF_FIRST)


def pack_kernel(place_ref, table, attn, proj, up, down, head, side, first, second, pad_ref):
    is_first = place_ref[1] == 0
    rows = side.shape[0]
    eye = (
        lax.broadcasted_iota(jnp.int32, (rows, rows), 0)
        == lax.broadcasted_iota(jnp.int32, (rows, rows), 1)
    )
    eye = jnp.where(eye, 1.0, 0.0).astype(BF16)

    def turned(a):
        return dot_nt(eye, a.astype(BF16)).astype(BF16)

    for layer, out in enumerate((first, second)):
        for j in range(3):
            out[:, 128 * j : 128 * j + 128] = attn[layer, j].astype(BF16)
        out[:, 384:512] = turned(proj[layer])
        out[:, 512:1024] = up[layer].astype(BF16)
        out[:, 1024:1536] = turned(down[layer])
    second[:, 1536:1792] = head[...].astype(BF16)
    pad_ref[...] = jnp.zeros(pad_ref.shape, F32)
    pad_ref[:, 0:5] = side[...]
    low = turned(table[0:512])
    high = jnp.concatenate([turned(table[512:896]), pad_ref[...].astype(BF16)], axis=1)
    first[:, 1536:2048] = jnp.where(is_first, low, high)


def finish_kernel(*refs):
    count = (len(refs) - 4) // 2
    scalar_ref = refs[2 * count]
    out_first, out_second, message = refs[2 * count + 1 :]
    square = jnp.zeros((1, 1), F32)
    for pieces, out in ((refs[:count], out_first), (refs[count : 2 * count], out_second)):
        total = pieces[0][...]
        for piece in pieces[1:]:
            total = total + piece[...].astype(F32)
        out[...] = total
        square = square + jnp.sum(
            jnp.sum(total * total, axis=1, keepdims=True), axis=0, keepdims=True
        )
    message[:, 0:512] = out_first[:, 1536:2048]
    rows = message.shape[0]
    lane = lax.broadcasted_iota(jnp.int32, (rows, 128), 1)
    top = lax.broadcasted_iota(jnp.int32, (rows, 128), 0) == 0
    scalars = scalar_ref[0:1] + jnp.where(lane == SMALL_SCALAR + 2, square, 0.0)
    message[:, 512:640] = jnp.where(top, scalars, 0.0)


def adam_rule(weight, moment, second, gradient, step_rate, decay_rate):
    moment_new = BETA_ONE * moment + (1.0 - BETA_ONE) * gradient
    second_new = BETA_TWO * second + (1.0 - BETA_TWO) * gradient * gradient
    moment_hat = moment_new / (1.0 - BETA_ONE**STEP_NUMBER)
    second_hat = second_new / (1.0 - BETA_TWO**STEP_NUMBER)
    weight_new = weight - step_rate * (
        moment_hat / (jnp.sqrt(second_hat) + EPS_ADAM) + decay_rate * weight
    )
    return (weight_new, moment_new, second_new)


def adam_kernel(*refs):
    place_ref, first, second, swapped = refs[0:4]
    smalls = refs[4:8]
    params = [refs[8 + 3 * i : 11 + 3 * i] for i in range(9)]
    loss_ref, valid_ref, norm_ref = refs[35:38]
    outs = [refs[38 + 3 * i : 41 + 3 * i] for i in range(9)]
    small_ref, turn_ref = refs[65:67]
    me = place_ref[0]
    is_first = place_ref[1] == 0
    rows = first.shape[0]
    for z in range(4):
        for p in range(4):
            row = pl.multiple_of((me ^ (4 * z + p)) * 16, 16)
            small_ref[pl.ds(row, 16)] = smalls[z][p]
    small = jnp.transpose(small_ref[...])
    scalars = jnp.sum(small[SMALL_SCALAR : SMALL_SCALAR + 8], axis=1, keepdims=True)
    loss, valid, square = scalars[0:1], scalars[1:2], scalars[2:3]
    inverse = 1.0 / valid
    norm = jnp.sqrt(square) * inverse
    loss_ref[...], valid_ref[...], norm_ref[...] = loss, valid, norm
    factor = jnp.minimum(1.0, CLIP_AT / (norm + 1e-06)) * inverse
    table, attn, proj, up, bias, down, vectors, head, side = range(9)

    def update(which, index, gradient, step_rate, decay_rate):
        news = adam_rule(
            *(ref[index] for ref in params[which]), factor * gradient, step_rate, decay_rate
        )
        for ref, new in zip(outs[which], news):
            ref[index] = new

    def turned(a, width):
        turn_ref[0:rows, 0:width] = a
        return jnp.transpose(turn_ref[:, 0:width])[:, 0:rows]

    turn_ref[...] = jnp.zeros(turn_ref.shape, F32)
    for layer, grad in enumerate((first, second)):
        for j in range(3):
            update(attn, (layer, j), grad[:, 128 * j : 128 * j + 128], RATE_MATRIX, DECAY_RATE)
        update(proj, (layer,), turned(grad[:, 384:512], 128), RATE_MATRIX, DECAY_RATE)
        update(up, (layer,), grad[:, 512:1024], RATE_MATRIX, DECAY_RATE)
        update(down, (layer,), turned(grad[:, 1024:1536], 512), RATE_MATRIX, DECAY_RATE)
        for i in range(2):
            low = SMALL_BIAS + 4 * layer + i
            row = jnp.where(is_first, small[low : low + 1], small[low + 2 : low + 3])
            index = (slice(layer, layer + 1), slice(256 * i, 256 * i + 256))
            update(bias, index, row, RATE_VECTOR, 0.0)
    whole = (slice(None), slice(None))
    update(head, whole, second[:, 1536:1792], RATE_MATRIX, DECAY_RATE)
    mine, theirs = first[:, 1536:2048], swapped[:, 0:512]
    low, high = jnp.where(is_first, mine, theirs), jnp.where(is_first, theirs, mine)
    update(table, (slice(0, 512),), turned(low, 512), RATE_TABLE, DECAY_RATE)
    update(table, (slice(512, 896),), turned(high[:, 0:384], 384), RATE_TABLE, DECAY_RATE)
    update(vectors, whole, small[0:NVEC], RATE_VECTOR, 0.0)
    side_grad = high[:, 384 + SMALL_SIDE : 384 + SMALL_SIDE + 5]
    update(side, whole, side_grad, RATE_MATRIX, DECAY_RATE)


def swap(a, axis, distance):
    size = lax.axis_size(axis)
    return lax.ppermute(a, axis, [(i, i ^ distance) for i in range(size)])


def gather(piece, n_high):
    column = jnp.stack([piece] + [swap(piece, "wide", 4 * k) for k in range(1, n_high)])
    mine = [column] + [swap(column, "wide", p) for p in range(1, 4)]
    other = [swap(a, "narrow", 1) for a in mine]
    return mine, other


def in_blocks(parts, wide):
    n_high, rows, cols = parts[0].shape
    if rows == 16:
        return parts
    whole = jnp.stack(parts, axis=1).reshape(4 * n_high, rows, cols)
    whole = whole[wide ^ jnp.arange(4 * n_high)].reshape(4, 4, 16, cols)
    return [whole[:, p] for p in range(4)]


def in_pieces(blocks, wide, n_high):
    cols = blocks.shape[-1]
    if n_high == 4:
        return blocks
    rows = 64 // n_high
    whole = blocks.transpose(1, 0, 2, 3).reshape(4 * n_high, rows, cols)
    whole = whole[wide ^ jnp.arange(4 * n_high)]
    return whole.reshape(n_high, 4, rows, cols).transpose(1, 0, 2, 3)


def scatter(keep, send, n_high):
    received = swap(send, "narrow", 1)
    sums = [keep[p] + received[p].astype(F32) for p in range(4)]
    own = sums[0]
    for p in range(1, 4):
        own = own + swap(sums[p].astype(BF16), "wide", p).astype(F32)
    return [own[0]] + [swap(own[k].astype(BF16), "wide", 4 * k) for k in range(1, n_high)]


def full_spec(a):
    return pl.BlockSpec(a.shape, lambda *_: (0,) * len(a.shape))


def row_spec(shape):
    return pl.BlockSpec((1,) + shape, lambda i: (i,) + (0,) * len(shape))


def shaped(shape, dtype):
    return jax.ShapeDtypeStruct(shape, dtype)


VMEM_SPEC = pl.BlockSpec(memory_space=pltpu.VMEM)
SMEM_SPEC = pl.BlockSpec(memory_space=pltpu.SMEM)


def call(kernel, grid, in_specs, out_specs, out_shape, scratch, flops, bytes_accessed, name):
    extra = {"grid": grid} if grid else {}
    return pl.pallas_call(
        kernel,
        in_specs=in_specs,
        out_specs=out_specs,
        out_shape=out_shape,
        scratch_shapes=scratch,
        compiler_params=pltpu.CompilerParams(vmem_limit_bytes=VMEM_BYTES),
        cost_estimate=pl.CostEstimate(
            flops=flops, bytes_accessed=bytes_accessed, transcendentals=0
        ),
        name=name,
        **extra,
    )


KEPT = (
    ((SEQ, D), F32),
    ((KEYS, 768), BF16),
    ((HEADS * 128, 128), BF16),
    ((HEADS * 128, 256), BF16),
    ((HEADS * 96, 384), BF16),
    ((SEQ, D), BF16),
    ((SEQ, D), F32),
    ((SEQ, FF), BF16),
    ((SEQ, FF), BF16),
)


def make_meta(tokens, actions, game_ids, valid_steps, rewards, end_flags):
    count = tokens.shape[0]
    frames = tokens.shape[1]

    def last(a, fill):
        return jnp.concatenate(
            [jnp.full((count, frames, OBS), fill, jnp.int32), a[:, :, None]], axis=2
        )

    zero = jnp.zeros((count, 1), jnp.int32)
    ids = jnp.concatenate([tokens, actions[:, :, None] + VOCAB], axis=2)
    following = jnp.concatenate([tokens[:, 1:, 0], zero], axis=1)
    targets = jnp.concatenate(
        [tokens[:, :, 1:], jnp.zeros((count, frames, 1), jnp.int32), following[:, :, None]], axis=2
    )
    next_valid = jnp.concatenate([valid_steps[:, 1:], zero], axis=1)
    weights = jnp.concatenate(
        [
            jnp.broadcast_to(valid_steps[:, :, None], (count, frames, OBS - 1)),
            jnp.zeros((count, frames, 1), jnp.int32),
            next_valid[:, :, None],
        ],
        axis=2,
    )
    games = jnp.broadcast_to(
        (VOCAB + ACTIONS + game_ids)[:, None, None], (count, frames, FRAME_TOKENS)
    )
    columns = [ids, games, targets, weights, last(valid_steps, 0), last(rewards, 0), last(end_flags + 3, 3)]
    stacked = jnp.stack(columns + [jnp.zeros_like(ids)], axis=-1).reshape(count, LENGTH, 8)
    stacked = jnp.pad(stacked, ((0, 0), (0, SEQ - LENGTH), (0, 0)))
    padding = (jnp.arange(SEQ) >= LENGTH)[None, :, None] & (jnp.arange(8) < 2)
    return jnp.where(padding, -1, stacked)


def per_device(
    tokens,
    actions,
    game_ids,
    valid_steps,
    rewards,
    end_flags,
    embed_table,
    table_first,
    table_second,
    attn_weight,
    attn_first,
    attn_second,
    proj_weight,
    proj_first,
    proj_second,
    up_weight,
    up_first,
    up_second,
    up_bias,
    bias_first,
    bias_second,
    down_weight,
    down_first,
    down_second,
    vectors,
    vectors_first,
    vectors_second,
    head_weight,
    head_first,
    head_second,
    side_weight,
    side_first,
    side_second,
):
    n_high = lax.axis_size("wide") // 4
    wide, core = lax.axis_index("wide"), lax.axis_index("narrow")
    rows = side_weight.shape[0]
    place = jnp.stack([jnp.where(rows == 16, wide, 0), core]).astype(jnp.int32)

    matrices = (
        embed_table,
        attn_weight,
        proj_weight,
        up_weight,
        down_weight,
        head_weight,
        side_weight,
    )
    piece_first, piece_second = call(
        pack_kernel,
        None,
        [SMEM_SPEC] + [VMEM_SPEC] * 7,
        [VMEM_SPEC] * 2,
        [shaped((rows, HALF_FIRST_COLS), BF16), shaped((rows, HALF_SECOND_COLS), BF16)],
        [pltpu.VMEM((rows, 128), F32)],
        10**6,
        10**6,
        "pack",
    )(place, *matrices)
    first_parts = gather(piece_first, n_high)
    second_parts = gather(piece_second, n_high)
    first_parts = [in_blocks(parts, wide) for parts in first_parts]
    second_parts = [in_blocks(parts, wide) for parts in second_parts]

    count = tokens.shape[0] // lax.axis_size("narrow")
    own = [
        lax.dynamic_slice_in_dim(a, core * count, count, 0)
        for a in (tokens, actions, game_ids, valid_steps, rewards, end_flags)
    ]
    meta = make_meta(*own)
    other_bias = swap(up_bias, "narrow", 1)
    all_bias = jnp.where(
        core == 0,
        jnp.concatenate([up_bias, other_bias], axis=1),
        jnp.concatenate([other_bias, up_bias], axis=1),
    )

    kept_specs = [row_spec(shape) for shape, _ in KEPT]
    kept_shapes = [shaped((count,) + shape, dtype) for shape, dtype in KEPT]
    row_f32 = shaped((count, SEQ, D), F32)
    blocks_first = [full_spec(a) for a in first_parts[0] + first_parts[1]]
    blocks_second = [full_spec(a) for a in second_parts[0] + second_parts[1]]
    w_spec = pl.BlockSpec((D, COL_FIRST), lambda i: (0, 0))
    results = call(
        first_forward_kernel,
        (count,),
        [SMEM_SPEC, row_spec((SEQ, 8)), full_spec(vectors), full_spec(all_bias)] + blocks_first,
        [w_spec, row_spec((SEQ, D))] + kept_specs,
        [shaped((D, COL_FIRST), BF16), row_f32] + kept_shapes,
        [pltpu.VMEM((D, COL_FIRST), BF16)],
        4 * 10**9,
        20 * 10**6,
        "first_forward",
    )(place, meta, vectors, all_bias, *first_parts[0], *first_parts[1])
    w_first, stream = results[0:2]
    kept = results[2:]
    side_copy = w_first[:, COL_SMALL:]

    blocks = lambda cols: pl.BlockSpec((4, 4, 16, cols), lambda i: (0, 0, 0, 0))
    small_spec = pl.BlockSpec((128, D), lambda i: (0, 0))
    side_spec = pl.BlockSpec((D, 128), lambda i: (0, 0))
    scalar_spec = pl.BlockSpec((8, 128), lambda i: (0, 0))
    grad_stream, keep_second, send_second, small_grads, side_grad, scalars = call(
        middle_kernel,
        (count,),
        [
            SMEM_SPEC,
            row_spec((SEQ, 8)),
            full_spec(vectors),
            full_spec(all_bias),
            side_spec,
            row_spec((SEQ, D)),
        ]
        + blocks_second,
        [
            row_spec((SEQ, D)),
            blocks(HALF_SECOND_COLS),
            blocks(HALF_SECOND_COLS),
            small_spec,
            side_spec,
            scalar_spec,
        ],
        [
            row_f32,
            shaped((4, 4, 16, HALF_SECOND_COLS), F32),
            shaped((4, 4, 16, HALF_SECOND_COLS), BF16),
            shaped((128, D), F32),
            shaped((D, 128), F32),
            shaped((8, 128), F32),
        ],
        [
            pltpu.VMEM((D, COL_SECOND + 128), BF16),
            pltpu.VMEM((D, COL_SECOND + 128), F32),
            pltpu.VMEM((128, D), F32),
            pltpu.VMEM((KEYS, 512), F32),
        ]
        + [pltpu.VMEM(shape, dtype) for shape, dtype in KEPT[1:]],
        15 * 10**9,
        20 * 10**6,
        "middle",
    )(place, meta, vectors, all_bias, side_copy, stream, *second_parts[0], *second_parts[1])
    second_pieces = scatter(
        in_pieces(keep_second, wide, n_high), in_pieces(send_second, wide, n_high), n_high
    )

    keep_first, send_first = call(
        first_backward_kernel,
        (count,),
        [SMEM_SPEC, row_spec((SEQ, 8)), full_spec(vectors), w_spec, row_spec((SEQ, D)), small_spec, side_spec]
        + kept_specs,
        [blocks(HALF_FIRST_COLS), blocks(HALF_FIRST_COLS)],
        [
            shaped((4, 4, 16, HALF_FIRST_COLS), F32),
            shaped((4, 4, 16, HALF_FIRST_COLS), BF16),
        ],
        [
            pltpu.VMEM((D, COL_FIRST), F32),
            pltpu.VMEM((128, D), F32),
            pltpu.VMEM((KEYS, 512), F32),
        ],
        8 * 10**9,
        20 * 10**6,
        "first_backward",
    )(place, meta, vectors, w_first, grad_stream, small_grads, side_grad, *kept)
    first_pieces = scatter(
        in_pieces(keep_first, wide, n_high), in_pieces(send_first, wide, n_high), n_high
    )

    grad_first, grad_second, message = call(
        finish_kernel,
        None,
        [VMEM_SPEC] * (2 * n_high + 1),
        [VMEM_SPEC] * 3,
        [
            shaped((rows, HALF_FIRST_COLS), F32),
            shaped((rows, HALF_SECOND_COLS), F32),
            shaped((rows, 640), F32),
        ],
        [],
        10**6,
        10**6,
        "finish",
    )(*first_pieces, *second_pieces, scalars)
    swapped = swap(message, "narrow", 1)
    small = jnp.where(core == 1, message[:, 384:512], swapped[:, 384:512])
    small = small + message[:, 512:640] + swapped[:, 512:640]
    plane = jnp.stack([small] + [swap(small, "wide", p) for p in range(1, 4)])
    columns = [plane] + [swap(plane, "wide", 4 * k) for k in range(1, n_high)]
    if rows != 16:
        parts = in_blocks([jnp.stack([column[p] for column in columns]) for p in range(4)], wide)
        columns = [jnp.stack([parts[p][z] for p in range(4)]) for z in range(4)]

    params = (
        embed_table,
        table_first,
        table_second,
        attn_weight,
        attn_first,
        attn_second,
        proj_weight,
        proj_first,
        proj_second,
        up_weight,
        up_first,
        up_second,
        up_bias,
        bias_first,
        bias_second,
        down_weight,
        down_first,
        down_second,
        vectors,
        vectors_first,
        vectors_second,
        head_weight,
        head_first,
        head_second,
        side_weight,
        side_first,
        side_second,
    )
    results = call(
        adam_kernel,
        None,
        [SMEM_SPEC] + [VMEM_SPEC] * 34,
        [VMEM_SPEC] * 30,
        [shaped((1, 1), F32)] * 3 + [shaped(a.shape, F32) for a in params],
        [pltpu.VMEM((D, 128), F32), pltpu.VMEM((128, 512), F32)],
        10**6,
        10**6,
        "adam",
    )(place, grad_first, grad_second, swapped, *columns, *params)
    return tuple(a.reshape(()) for a in results[0:3]) + tuple(results[3:])


def solution(mesh):
    placed = (
        P("wide", None, None),
        P("wide", None),
        P("wide"),
        P("wide", None),
        P("wide", None),
        P("wide", None),
        P(None, "wide"),
        P(None, "wide"),
        P(None, "wide"),
        P(None, None, "wide", "narrow"),
        P(None, None, "wide", "narrow"),
        P(None, None, "wide", "narrow"),
        P(None, "narrow", "wide"),
        P(None, "narrow", "wide"),
        P(None, "narrow", "wide"),
        P(None, "wide", "narrow"),
        P(None, "wide", "narrow"),
        P(None, "wide", "narrow"),
        P(None, "narrow"),
        P(None, "narrow"),
        P(None, "narrow"),
        P(None, "narrow", "wide"),
        P(None, "narrow", "wide"),
        P(None, "narrow", "wide"),
        P(),
        P(),
        P(),
        P("wide", "narrow"),
        P("wide", "narrow"),
        P("wide", "narrow"),
        P("wide", None),
        P("wide", None),
        P("wide", None),
    )
    return jax.shard_map(
        per_device,
        mesh=mesh,
        in_specs=placed,
        out_specs=(P(), P(), P()) + placed[6:],
        check_vma=False,
    )
```

```python
import functools

import jax
import jax.numpy as jnp
from jax import lax
from jax.experimental import pallas as pl
from jax.experimental.pallas import tpu as pltpu
from jax.sharding import PartitionSpec as P

D = 256
HEADS = 4
HEAD_DIM = 64
FF = 1024
VOCAB = 512
ACTIONS = 18
GAMES = 26
OBS = 16
FRAMES = 20
STEP_NUMBER = 5
FRAME_TOKENS = 17
LENGTH = 340
ROWS = 896
NVEC = 14

EPS_NORM = 1e-05
BETA_ONE = 0.5
BETA_TWO = 0.5
RATE_TABLE = 0.5
RATE_MATRIX = 0.05
RATE_VECTOR = 0.2
DECAY_RATE = 0.01
EPS_ADAM = 1e-08
CLIP_AT = 0.1

SEQ = 352
KEYS = 384
QBLOCKS = ((0, 128, 128), (128, 128, 256), (256, 96, 384))

COL_QKV, COL_PROJ, COL_UP, COL_DOWN, COL_LAYER = 0, 768, 1024, 2048, 3072
HALF_ATTENTION = ((0, 128, 0), (128, 128, 256), (256, 128, 512), (384, 128, COL_PROJ))
HALF_LAYER = HALF_ATTENTION + ((512, 512, COL_UP), (1024, 512, COL_DOWN))
COL_TABLE, COL_SMALL, COL_FIRST = 3072, 3968, 4096
HALF_FIRST = HALF_LAYER + ((1536, 512, COL_TABLE),)
HALF_FIRST_COLS = 2048
COL_HEAD, COL_SECOND = 3072, 3584
HALF_SECOND = HALF_LAYER + ((1536, 256, COL_HEAD),)
HALF_SECOND_COLS = 1792
GRAD_UP, GRAD_DOWN = 0, 1024
HALF_GRAD_FF = ((0, 512, GRAD_UP), (512, 512, GRAD_DOWN))
GRAD_TABLE, GRAD_SMALL = 1024, 1920
HALF_GRAD_REST = HALF_ATTENTION + ((512, 512, GRAD_TABLE),)
HALF_GRAD_COLS = 1024
SMALL_ROWS, SMALL_BIAS, SMALL_SIDE = 32, 14, 22

F32, BF16 = jnp.float32, jnp.bfloat16
VMEM_BYTES = 60 * 1024 * 1024


def dot_nn(a, b):
    return lax.dot_general(a, b, (((1,), (0,)), ((), ())), preferred_element_type=F32)


def dot_nt(a, b):
    return lax.dot_general(a, b, (((1,), (1,)), ((), ())), preferred_element_type=F32)


def dot_tn(a, b):
    return lax.dot_general(a, b, (((0,), (0,)), ((), ())), preferred_element_type=F32)


def normalise(x):
    centred = x - jnp.mean(x, axis=1, keepdims=True)
    scale = lax.rsqrt(jnp.mean(centred * centred, axis=1, keepdims=True) + EPS_NORM)
    return centred * scale, scale


def normalise_back(grad, xhat, scale, gain):
    inner = grad * gain
    mean_one = jnp.mean(inner, axis=1, keepdims=True)
    mean_two = jnp.mean(inner * xhat, axis=1, keepdims=True)
    return scale * (inner - mean_one - xhat * mean_two)


def column_sum(a):
    return jnp.sum(a, axis=0, keepdims=True)


def head_masks(a, scale=None):
    lane = lax.broadcasted_iota(jnp.int32, (1, D), 1)
    zero = jnp.zeros((), a.dtype)
    if scale is not None:
        a = a * jnp.asarray(scale, a.dtype)
    return [
        jnp.where((lane >= h * HEAD_DIM) & (lane < (h + 1) * HEAD_DIM), a, zero)
        for h in range(HEADS)
    ]


def assemble(pieces_mine, pieces_other, place_ref, w_ref, halves):
    me, core = place_ref[0], place_ref[1]
    is_first = core == 0
    for p in range(4):
        for z in range(4):
            row = pl.multiple_of((me ^ (4 * z + p)) * 16, 16)
            for src, width, dest in halves:
                mine = pieces_mine[p][z, :, src : src + width]
                other = pieces_other[p][z, :, src : src + width]
                w_ref[pl.ds(row, 16), dest : dest + width] = jnp.where(is_first, mine, other)
                w_ref[pl.ds(row, 16), dest + width : dest + 2 * width] = jnp.where(
                    is_first, other, mine
                )


def disperse(g_ref, place_ref, keep_ref, send_ref, halves):
    me, core = place_ref[0], place_ref[1]
    is_first = core == 0
    for p in range(4):
        for z in range(4):
            row = pl.multiple_of((me ^ (4 * z + p)) * 16, 16)
            for src, width, dest in halves:
                low = g_ref[pl.ds(row, 16), dest : dest + width]
                high = g_ref[pl.ds(row, 16), dest + width : dest + 2 * width]
                keep_ref[p, z, :, src : src + width] = jnp.where(is_first, low, high)
                send_ref[p, z, :, src : src + width] = jnp.where(is_first, high, low).astype(BF16)


def make_hits(meta):
    lane = lax.broadcasted_iota(jnp.int32, (SEQ, 640), 1)
    place = lax.broadcasted_iota(jnp.int32, (SEQ, ROWS), 0) + (VOCAB + ACTIONS + GAMES)
    place_hit = place == lax.broadcasted_iota(jnp.int32, (SEQ, ROWS), 1)
    hit = (lane == meta[:, 0:1]) | (lane == meta[:, 1:2]) | place_hit[:, :640]
    one, zero = jnp.ones((), F32), jnp.zeros((), F32)
    return jnp.concatenate(
        [jnp.where(hit, one, zero).astype(BF16), jnp.where(place_hit[:, 640:], one, zero).astype(BF16)],
        axis=1,
    )


def layer_forward(x, w_ref, vec, bias, kept):
    x_ref, qkv_ref, p_refs, o_ref, m_ref, h_ref, gp_ref = kept
    normed16 = (normalise(x)[0] * vec[0:1] + vec[1:2]).astype(BF16)
    qkv_ref[0:SEQ] = dot_nn(normed16, w_ref[:, COL_QKV : COL_QKV + 768]).astype(BF16)
    qkv_ref[SEQ:KEYS] = jnp.zeros((KEYS - SEQ, 768), BF16)
    values = head_masks(qkv_ref[:, 512:768])
    for (first, count, seen), p_ref in zip(QBLOCKS, p_refs):
        queries = jnp.concatenate(head_masks(qkv_ref[first : first + count, 0:256], 0.125), axis=0)
        scores = dot_nt(queries, qkv_ref[0:seen, 256:512]).reshape(HEADS, count, seen)
        row = lax.broadcasted_iota(jnp.int32, (count, seen), 0) + first
        causal = row >= lax.broadcasted_iota(jnp.int32, (count, seen), 1)
        scores = jnp.where(causal[None], scores, -1e30)
        expanded = jnp.exp(scores - jnp.max(scores, axis=2, keepdims=True))
        probs = expanded * (1.0 / jnp.sum(expanded, axis=2, keepdims=True))
        probs16 = probs.astype(BF16)
        p_ref[...] = probs16.reshape(HEADS * count, seen)
        out = dot_nn(
            jnp.concatenate([probs16[h] for h in range(HEADS)], axis=1),
            jnp.concatenate([values[h][0:seen] for h in range(HEADS)], axis=0),
        )
        o_ref[first : first + count] = out.astype(BF16)
    middle = x + (dot_nt(o_ref[...], w_ref[:, COL_PROJ : COL_PROJ + 256]) + vec[2:3])
    m_ref[...] = middle
    normed16 = (normalise(middle)[0] * vec[3:4] + vec[4:5]).astype(BF16)
    total = middle + vec[5:6]
    for chunk in range(4):
        cols = slice(256 * chunk, 256 * chunk + 256)
        up = dot_nn(normed16, w_ref[:, COL_UP + 256 * chunk : COL_UP + 256 * chunk + 256])
        up = up + bias[:, cols]
        square = up * up
        slope = 0.7978845608028654 + 0.1070322244089 * square
        bent = jnp.tanh(up * (0.7978845608028654 + 0.0356774081363 * square))
        half = 0.5 + 0.5 * bent
        hidden = up * half
        gp_ref[:, cols] = (half + hidden * (1.0 - bent) * slope).astype(BF16)
        hidden16 = hidden.astype(BF16)
        h_ref[:, cols] = hidden16
        total = total + dot_nt(
            hidden16, w_ref[:, COL_DOWN + 256 * chunk : COL_DOWN + 256 * chunk + 256]
        )
    return total


def ff_backward(grad_in, w_ref, vec, kept, g_ref, g_up, g_down, v_ref, v_row, bias_row):
    m_ref, h_ref, gp_ref = kept
    grad_out16 = grad_in.astype(BF16)
    v_ref[v_row + 5 : v_row + 6] += column_sum(grad_out16.astype(F32))
    xhat, scale = normalise(m_ref[...])
    normed16 = (xhat * vec[3:4] + vec[4:5]).astype(BF16)
    grad_normed = None
    for chunk in range(4):
        start = 256 * chunk
        cols = slice(start, start + 256)
        grad_hidden = dot_nn(grad_out16, w_ref[:, COL_DOWN + start : COL_DOWN + start + 256])
        grad_up16 = (grad_hidden * gp_ref[:, cols].astype(F32)).astype(BF16)
        g_ref[:, g_down + start : g_down + start + 256] += dot_tn(grad_out16, h_ref[:, cols])
        g_ref[:, g_up + start : g_up + start + 256] += dot_tn(normed16, grad_up16)
        v_ref[bias_row + chunk : bias_row + chunk + 1] += column_sum(grad_up16.astype(F32))
        part = dot_nt(grad_up16, w_ref[:, COL_UP + start : COL_UP + start + 256])
        grad_normed = part if grad_normed is None else grad_normed + part
    v_ref[v_row + 3 : v_row + 4] += column_sum(grad_normed * xhat)
    v_ref[v_row + 4 : v_row + 5] += column_sum(grad_normed)
    return grad_in + normalise_back(grad_normed, xhat, scale, vec[3:4])


def attention_backward(grad_mid, w_ref, vec, kept, g_ref, v_ref, v_row, dkv_ref):
    x_ref, qkv_ref, p_refs, o_ref = kept
    grad_att16 = grad_mid.astype(BF16)
    v_ref[v_row + 2 : v_row + 3] += column_sum(grad_att16.astype(F32))
    g_ref[:, COL_PROJ : COL_PROJ + 256] += dot_tn(grad_att16, o_ref[...])
    grad_heads = dot_nn(grad_att16, w_ref[:, COL_PROJ : COL_PROJ + 256]).astype(BF16)
    keys = head_masks(qkv_ref[:, 256:512], 0.125)
    dkv_ref[...] = jnp.zeros(dkv_ref.shape, F32)
    grad_query = []
    for (first, count, seen), p_ref in zip(QBLOCKS, p_refs):
        rows = slice(first, first + count)
        queries = jnp.concatenate(head_masks(qkv_ref[rows, 0:256], 0.125), axis=0)
        grads = jnp.concatenate(head_masks(grad_heads[rows]), axis=0)
        grad_probs = dot_nt(grads, qkv_ref[0:seen, 512:768])
        probs16 = p_ref[...]
        probs = probs16.astype(F32)
        inner = jnp.sum(probs * grad_probs, axis=1, keepdims=True)
        grad_scores = (probs * (grad_probs - inner)).astype(BF16)
        grad_query.append(
            dot_nn(
                jnp.concatenate(
                    [grad_scores[h * count : (h + 1) * count] for h in range(HEADS)], axis=1
                ),
                jnp.concatenate([keys[h][0:seen] for h in range(HEADS)], axis=0),
            ).astype(BF16)
        )
        dkv_ref[0:seen, 0:256] += dot_tn(grad_scores, queries)
        dkv_ref[0:seen, 256:512] += dot_tn(probs16, grads)
    grad_qkv = jnp.concatenate(
        [jnp.concatenate(grad_query, axis=0), dkv_ref[0:SEQ].astype(BF16)], axis=1
    )
    xhat, scale = normalise(x_ref[...])
    normed16 = (xhat * vec[0:1] + vec[1:2]).astype(BF16)
    g_ref[:, COL_QKV : COL_QKV + 768] += dot_tn(normed16, grad_qkv)
    grad_normed = dot_nt(grad_qkv, w_ref[:, COL_QKV : COL_QKV + 768])
    v_ref[v_row : v_row + 1] += column_sum(grad_normed * xhat)
    v_ref[v_row + 1 : v_row + 2] += column_sum(grad_normed)
    return grad_mid + normalise_back(grad_normed, xhat, scale, vec[0:1])


def own_bias(place_ref, mine, other):
    is_first = place_ref[1] == 0
    return jnp.concatenate(
        [jnp.where(is_first, mine, other), jnp.where(is_first, other, mine)], axis=1
    )


def prepare_kernel(place_ref, games_ref, tokens, actions, valid, rewards, ends, after, out, x_ref):
    count = out.shape[0]
    frames = tokens.shape[2]
    base = place_ref[1] * count
    row = lax.broadcasted_iota(jnp.int32, (SEQ, frames), 0)
    start = lax.broadcasted_iota(jnp.int32, (SEQ, frames), 1) * FRAME_TOKENS
    here = jnp.where((row >= start) & (row < start + FRAME_TOKENS), 1.0, 0.0).astype(BF16)
    coming = jnp.where((row >= start - FRAME_TOKENS) & (row < start), 1.0, 0.0).astype(BF16)
    passed = jnp.sum(jnp.where(row >= start + FRAME_TOKENS, 1, 0), axis=1, keepdims=True)
    place = lax.broadcasted_iota(jnp.int32, (SEQ, 1), 0)
    spot = place - passed * FRAME_TOKENS
    lane = lax.broadcasted_iota(jnp.int32, (SEQ, 24), 1)
    wide_lane = lax.broadcasted_iota(jnp.int32, (SEQ, 128), 1)
    inside = place < LENGTH
    x_ref[...] = jnp.zeros(x_ref.shape, jnp.int32)
    for s in range(count):
        x_ref[0:OBS] = tokens[base + s]
        x_ref[16:17] = actions[pl.ds(base + s, 1)] + VOCAB
        x_ref[17:18] = valid[pl.ds(base + s, 1)]
        x_ref[18:19] = rewards[pl.ds(base + s, 1)]
        x_ref[19:20] = ends[pl.ds(base + s, 1)] + 3
        high = (x_ref[...] >> 4).astype(F32).astype(BF16)
        low = (x_ref[...] & 15).astype(F32).astype(BF16)
        now = dot_nt(here, high) * 16.0 + dot_nt(here, low)
        soon = dot_nt(coming, high) * 16.0 + dot_nt(coming, low)

        def pick(condition, a):
            return jnp.sum(jnp.where(condition, a, 0.0), axis=1, keepdims=True).astype(jnp.int32)

        ids = jnp.where(inside, pick(lane == spot, now), -1)
        game = jnp.where(inside, games_ref[base + s] + (VOCAB + ACTIONS), -1)
        target = pick((lane == spot + 1) & (spot < 15), now)
        target = target + pick((lane == 0) & (spot == 16), soon)
        weight = pick((lane == 17) & (spot < 15), now) + pick((lane == 17) & (spot == 16), soon)
        side = pick((lane == 17) & (spot == 16), now)
        reward, end = pick(lane == 18, now), pick(lane == 19, now)
        result = jnp.zeros((SEQ, 128), jnp.int32)
        for c, column in enumerate((ids, game, target, weight, side, reward, end)):
            result = jnp.where(wide_lane == c, column, result)
        out[s] = result


def first_forward_kernel(*refs):
    place_ref, meta_ref, vec_ref, bias_ref, bias_other = refs[0:5]
    mine, other = refs[5:9], refs[9:13]
    w_out, side_out, next_ref = refs[14:17]
    x_ref, qkv_ref, p0, p1, p2, o_ref, m_ref, h_ref, gp_ref = refs[17:26]
    w_ref = refs[26]

    @pl.when(pl.program_id(0) == 0)
    def _():
        assemble(mine, other, place_ref, w_ref, HALF_FIRST)
        w_out[...] = w_ref[...]
        side_out[...] = w_ref[:, COL_SMALL:]

    x = dot_nt(make_hits(meta_ref[0]), w_ref[:, COL_TABLE : COL_TABLE + ROWS])
    x_ref[0] = x
    kept = (
        x_ref.at[0],
        qkv_ref.at[0],
        (p0.at[0], p1.at[0], p2.at[0]),
        o_ref.at[0],
        m_ref.at[0],
        h_ref.at[0],
        gp_ref.at[0],
    )
    bias = own_bias(place_ref, bias_ref[0:1], bias_other[0:1])
    next_ref[0] = layer_forward(x, w_ref, vec_ref[0:6], bias, kept)


def middle_kernel(*refs):
    place_ref, meta_ref, vec_ref, bias_ref, bias_other, side_ref, in_ref = refs[0:7]
    mine, other = refs[7:11], refs[11:15]
    grad_ref, keep_ref, send_ref, v_out, scalar_ref = refs[15:20]
    w_ref, g_ref, v_ref, dkv_ref = refs[20:24]
    qkv_ref, p0, p1, p2, o_ref, m_ref, h_ref, gp_ref = refs[24:32]
    step = pl.program_id(0)

    @pl.when(step == 0)
    def _():
        assemble(mine, other, place_ref, w_ref, HALF_SECOND)
        w_ref[:, COL_SECOND:] = side_ref[...]
        g_ref[...] = jnp.zeros(g_ref.shape, F32)
        v_ref[...] = jnp.zeros(v_ref.shape, F32)
        scalar_ref[...] = jnp.zeros(scalar_ref.shape, F32)

    x_ref = in_ref.at[0]
    kept = (x_ref, qkv_ref, (p0, p1, p2), o_ref, m_ref, h_ref, gp_ref)
    bias = own_bias(place_ref, bias_ref[1:2], bias_other[1:2])
    last = layer_forward(x_ref[...], w_ref, vec_ref[6:12], bias, kept)

    meta = meta_ref[0]
    xhat, scale = normalise(last)
    gain = vec_ref[12:13]
    final16 = (xhat * gain + vec_ref[13:14]).astype(BF16)
    both = dot_nn(final16, w_ref[:, COL_HEAD : COL_HEAD + VOCAB + 128])
    logits, side = both[:, :VOCAB], both[:, VOCAB:]
    weight = meta[:, 3:4].astype(F32)
    peak = jnp.max(logits, axis=1, keepdims=True)
    expanded = jnp.exp(logits - peak)
    total = jnp.sum(expanded, axis=1, keepdims=True)
    hit = lax.broadcasted_iota(jnp.int32, (SEQ, VOCAB), 1) == meta[:, 2:3]
    picked = jnp.sum(jnp.where(hit, logits, 0.0), axis=1, keepdims=True)
    loss = column_sum(weight * (peak + jnp.log(total) - picked))
    grad_logits = expanded * (weight / total) - jnp.where(hit, weight, 0.0)

    lane = lax.broadcasted_iota(jnp.int32, (SEQ, 128), 1)
    is_reward, is_end = lane < 3, (lane == 3) | (lane == 4)
    side_weight = meta[:, 4:5].astype(F32)
    reward_peak = jnp.max(jnp.where(is_reward, side, -1e30), axis=1, keepdims=True)
    end_peak = jnp.max(jnp.where(is_end, side, -1e30), axis=1, keepdims=True)
    side_peak = jnp.where(is_reward, reward_peak, end_peak)
    is_side = is_reward | is_end
    expanded = jnp.where(is_side, jnp.exp(jnp.where(is_side, side - side_peak, 0.0)), 0.0)
    reward_total = jnp.sum(jnp.where(is_reward, expanded, 0.0), axis=1, keepdims=True)
    end_total = jnp.sum(jnp.where(is_end, expanded, 0.0), axis=1, keepdims=True)
    side_hit = (lane == meta[:, 5:6]) | (lane == meta[:, 6:7])
    side_picked = jnp.sum(jnp.where(side_hit, side, 0.0), axis=1, keepdims=True)
    side_terms = reward_peak + jnp.log(reward_total) + end_peak + jnp.log(end_total) - side_picked
    loss = loss + column_sum(side_weight * side_terms)
    grad_side = expanded * jnp.where(is_reward, side_weight / reward_total, side_weight / end_total)
    grad_side = grad_side - jnp.where(side_hit, side_weight, 0.0)
    valid = column_sum(side_weight)
    scalar_lane = lax.broadcasted_iota(jnp.int32, (8, 128), 1)
    scalar_row = lax.broadcasted_iota(jnp.int32, (8, 128), 0) == 0
    scalar_ref[...] += jnp.where(scalar_row & (scalar_lane == 0), loss, 0.0)
    scalar_ref[...] += jnp.where(scalar_row & (scalar_lane == 1), valid, 0.0)

    grad_both = jnp.concatenate([grad_logits.astype(BF16), grad_side.astype(BF16)], axis=1)
    g_ref[:, COL_HEAD : COL_HEAD + VOCAB + 128] += dot_tn(final16, grad_both)
    grad_final = dot_nt(grad_both, w_ref[:, COL_HEAD : COL_HEAD + VOCAB + 128])
    v_ref[12:13] += column_sum(grad_final * xhat)
    v_ref[13:14] += column_sum(grad_final)
    grad_last = normalise_back(grad_final, xhat, scale, gain)
    vec = vec_ref[6:12]
    grad_mid = ff_backward(
        grad_last,
        w_ref,
        vec,
        (m_ref, h_ref, gp_ref),
        g_ref,
        COL_UP,
        COL_DOWN,
        v_ref,
        6,
        SMALL_BIAS + 4,
    )
    grad_ref[0] = attention_backward(
        grad_mid, w_ref, vec, (x_ref, qkv_ref, (p0, p1, p2), o_ref), g_ref, v_ref, 6, dkv_ref
    )

    @pl.when(step == pl.num_programs(0) - 1)
    def _():
        disperse(g_ref, place_ref, keep_ref, send_ref, HALF_SECOND)
        v_ref[SMALL_SIDE : SMALL_SIDE + 5] = jnp.transpose(g_ref[:, COL_SECOND:])[0:5]
        v_out[...] = v_ref[...]


def ff_backward_kernel(*refs):
    place_ref, vec_ref, w_ref, grad_ref, v_in, m_ref, h_ref, gp_ref = refs[0:8]
    mid_ref, keep_ref, send_ref, v_out = refs[8:12]
    g_ref, v_ref = refs[12:14]
    step = pl.program_id(0)

    @pl.when(step == 0)
    def _():
        g_ref[...] = jnp.zeros(g_ref.shape, F32)
        v_ref[...] = v_in[...]

    mid_ref[0] = ff_backward(
        grad_ref[0],
        w_ref,
        vec_ref[0:6],
        (m_ref.at[0], h_ref.at[0], gp_ref.at[0]),
        g_ref,
        GRAD_UP,
        GRAD_DOWN,
        v_ref,
        0,
        SMALL_BIAS,
    )

    @pl.when(step == pl.num_programs(0) - 1)
    def _():
        disperse(g_ref, place_ref, keep_ref, send_ref, HALF_GRAD_FF)
        v_out[...] = v_ref[...]


def attention_backward_kernel(*refs):
    place_ref, meta_ref, vec_ref, w_ref, mid_ref, v_in = refs[0:6]
    x_ref, qkv_ref, p0, p1, p2, o_ref = refs[6:12]
    keep_ref, send_ref, v_out = refs[13:16]
    g_ref, v_ref, dkv_ref = refs[16:19]
    step = pl.program_id(0)

    @pl.when(step == 0)
    def _():
        g_ref[...] = jnp.zeros(g_ref.shape, F32)
        v_ref[...] = v_in[...]

    kept = (x_ref.at[0], qkv_ref.at[0], (p0.at[0], p1.at[0], p2.at[0]), o_ref.at[0])
    grad_x = attention_backward(
        mid_ref[0], w_ref, vec_ref[0:6], kept, g_ref, v_ref, 0, dkv_ref
    )
    g_ref[:, GRAD_TABLE : GRAD_TABLE + ROWS] += dot_tn(grad_x.astype(BF16), make_hits(meta_ref[0]))

    @pl.when(step == pl.num_programs(0) - 1)
    def _():
        for block in range(16):
            quarter = slice(8 * (block // 4), 8 * (block // 4) + 8)
            g_ref[16 * block : 16 * block + 8, GRAD_SMALL:] = v_ref[quarter, 0:128]
            g_ref[16 * block + 8 : 16 * block + 16, GRAD_SMALL:] = v_ref[quarter, 128:256]
        disperse(g_ref, place_ref, keep_ref, send_ref, HALF_GRAD_REST)
        v_out[...] = v_ref[...]


def pack_layer(attn, proj, up, down, layer, out):
    for j in range(3):
        out[:, 128 * j : 128 * j + 128] = attn[layer, j].astype(BF16)
    out[:, 384:512] = proj[layer].astype(BF16)
    out[:, 512:1024] = up[layer].astype(BF16)
    out[:, 1024:1536] = down[layer].astype(BF16)


def pack_first_kernel(place_ref, table, attn, proj, up, down, side, out, pad_ref):
    pack_layer(attn, proj, up, down, 0, out)
    rows = side.shape[1]
    eye = (
        lax.broadcasted_iota(jnp.int32, (rows, rows), 0)
        == lax.broadcasted_iota(jnp.int32, (rows, rows), 1)
    )
    eye = jnp.where(eye, 1.0, 0.0).astype(BF16)
    pad_ref[...] = jnp.zeros(pad_ref.shape, F32)
    pad_ref[:, 0:5] = dot_nt(eye, side[...].astype(BF16))
    high = jnp.concatenate([table[:, 512:896], pad_ref[...]], axis=1)
    out[:, 1536:2048] = jnp.where(place_ref[1] == 0, table[:, 0:512], high).astype(BF16)


def pack_second_kernel(attn, proj, up, down, head, after, out):
    pack_layer(attn, proj, up, down, 1, out)
    out[:, 1536:1792] = head[...].astype(BF16)


def finish_kernel(*refs):
    count = (len(refs) - 5) // 2
    place_ref = refs[0]
    scalar_ref = refs[2 * count + 1]
    out_rest, out_other, message = refs[2 * count + 2 :]
    square = jnp.zeros((1, 1), F32)
    for pieces, out in ((refs[1 : count + 1], out_rest), (refs[count + 1 : 2 * count + 1], out_other)):
        total = pieces[0][...]
        for piece in pieces[1:]:
            total = total + piece[...].astype(F32)
        out[...] = total
        square = square + column_sum(jnp.sum(total * total, axis=1, keepdims=True))
    small = out_rest[:, 896:1024]
    extra = column_sum(jnp.sum(small * small, axis=1, keepdims=True))
    square = square - jnp.where(place_ref[1] == 0, 0.0, extra)
    rows = message.shape[0]
    message[:, 0:512] = out_rest[:, 512:1024]
    lane = lax.broadcasted_iota(jnp.int32, (rows, 128), 1)
    top = lax.broadcasted_iota(jnp.int32, (rows, 128), 0) == 0
    scalars = scalar_ref[0:1] + jnp.where(lane == 2, square, 0.0)
    message[:, 512:640] = jnp.where(top, scalars, 0.0)


def adam_rule(weight, moment, second, gradient, step_rate, decay_rate):
    moment_new = BETA_ONE * moment + (1.0 - BETA_ONE) * gradient
    second_new = BETA_TWO * second + (1.0 - BETA_TWO) * gradient * gradient
    moment_hat = moment_new / (1.0 - BETA_ONE**STEP_NUMBER)
    second_hat = second_new / (1.0 - BETA_TWO**STEP_NUMBER)
    weight_new = weight - step_rate * (
        moment_hat / (jnp.sqrt(second_hat) + EPS_ADAM) + decay_rate * weight
    )
    return (weight_new, moment_new, second_new)


def adam_kernel(*refs):
    place_ref, rest, others, swapped, near, far = refs[0:6]
    params = [refs[6 + 3 * i : 9 + 3 * i] for i in range(9)]
    loss_ref, valid_ref, norm_ref = refs[33:36]
    outs = [refs[36 + 3 * i : 39 + 3 * i] for i in range(9)]
    small_ref = refs[63]
    me, wide = place_ref[0], place_ref[2]
    is_first = place_ref[1] == 0
    rows = rest.shape[0]
    for k in range(4):
        source, at = ((near, 0), (near, 16), (far, 0), (far, 16))[k]
        row = pl.multiple_of(((me >> 2) ^ k) * 8, 8)
        small_ref[pl.ds(row, 8), 0:128] = source[at : at + 8]
        small_ref[pl.ds(row, 8), 128:256] = source[at + 8 : at + 16]
    scalars = near[32:33] + far[32:33]
    small = small_ref[...]
    loss, valid, square = scalars[:, 0:1], scalars[:, 1:2], scalars[:, 2:3]
    square = square + column_sum(jnp.sum(small * small, axis=1, keepdims=True))
    inverse = 1.0 / valid
    norm = jnp.sqrt(square) * inverse
    loss_ref[...], valid_ref[...], norm_ref[...] = loss, valid, norm
    factor = jnp.minimum(1.0, CLIP_AT / (norm + 1e-06)) * inverse
    table, attn, proj, up, bias, down, vectors, head, side = range(9)

    def update(which, index, gradient, step_rate, decay_rate):
        news = adam_rule(
            *(ref[index] for ref in params[which]), factor * gradient, step_rate, decay_rate
        )
        for ref, new in zip(outs[which], news):
            ref[index] = new

    layers = ((rest, others, 1792), (others, others, 512))
    for layer, (attention, feed, at) in enumerate(layers):
        for j in range(3):
            update(attn, (layer, j), attention[:, 128 * j : 128 * j + 128], RATE_MATRIX, DECAY_RATE)
        update(proj, (layer,), attention[:, 384:512], RATE_MATRIX, DECAY_RATE)
        update(up, (layer,), feed[:, at : at + 512], RATE_MATRIX, DECAY_RATE)
        update(down, (layer,), feed[:, at + 512 : at + 1024], RATE_MATRIX, DECAY_RATE)
        for i in range(2):
            low = SMALL_BIAS + 4 * layer + i
            row = jnp.where(is_first, small[low : low + 1], small[low + 2 : low + 3])
            index = (slice(layer, layer + 1), slice(256 * i, 256 * i + 256))
            update(bias, index, row, RATE_VECTOR, 0.0)
    whole = (slice(None), slice(None))
    update(head, whole, others[:, 1536:1792], RATE_MATRIX, DECAY_RATE)
    mine, theirs = rest[:, 512:1024], swapped[:, 0:512]
    low, high = jnp.where(is_first, mine, theirs), jnp.where(is_first, theirs, mine)
    update(table, (slice(None), slice(0, 512)), low, RATE_TABLE, DECAY_RATE)
    update(table, (slice(None), slice(512, 896)), high[:, 0:384], RATE_TABLE, DECAY_RATE)
    update(vectors, whole, small[0:NVEC], RATE_VECTOR, 0.0)
    turned = pltpu.roll(small[SMALL_SIDE : SMALL_SIDE + 8], lax.rem(D - wide * rows, D), 1)
    update(side, whole, turned[0:5, 0:rows], RATE_MATRIX, DECAY_RATE)


def swap(a, axis, distance):
    size = lax.axis_size(axis)
    return lax.ppermute(a, axis, [(i, i ^ distance) for i in range(size)])


def gather_column(piece, n_high):
    return jnp.stack([piece] + [swap(piece, "wide", 4 * k) for k in range(1, n_high)])


def gather_plane(column):
    return [column] + [swap(column, "wide", p) for p in range(1, 4)]


def gather_cores(mine):
    return [swap(a, "narrow", 1) for a in mine]


def in_blocks(parts, wide):
    n_high, rows, cols = parts[0].shape
    if rows == 16:
        return parts
    whole = jnp.stack(parts, axis=1).reshape(4 * n_high, rows, cols)
    whole = whole[wide ^ jnp.arange(4 * n_high)].reshape(4, 4, 16, cols)
    return [whole[:, p] for p in range(4)]


def in_pieces(blocks, wide, n_high):
    cols = blocks.shape[-1]
    if n_high == 4:
        return blocks
    rows = 64 // n_high
    whole = blocks.transpose(1, 0, 2, 3).reshape(4 * n_high, rows, cols)
    whole = whole[wide ^ jnp.arange(4 * n_high)]
    return whole.reshape(n_high, 4, rows, cols).transpose(1, 0, 2, 3)


def add_cores(keep, send, wide, n_high):
    keep, send = in_pieces(keep, wide, n_high), in_pieces(send, wide, n_high)
    received = swap(send, "narrow", 1)
    return [keep[p] + received[p].astype(F32) for p in range(4)]


def swap_plane(sums):
    return [swap(sums[p].astype(BF16), "wide", p) for p in range(1, 4)]


def add_plane(own, received):
    for a in received:
        own = own + a.astype(F32)
    return own


def column_pieces(own):
    return [own[0]] + [swap(own[k].astype(BF16), "wide", 4 * k) for k in range(1, own.shape[0])]


def full_spec(a):
    return pl.BlockSpec(a.shape, lambda *_: (0,) * len(a.shape))


def row_spec(shape):
    return pl.BlockSpec((1,) + shape, lambda i: (i,) + (0,) * len(shape))


def shaped(shape, dtype):
    return jax.ShapeDtypeStruct(shape, dtype)


VMEM_SPEC = pl.BlockSpec(memory_space=pltpu.VMEM)
ANY_SPEC = pl.BlockSpec(memory_space=pl.ANY)
SMEM_SPEC = pl.BlockSpec(memory_space=pltpu.SMEM)


def call(kernel, grid, in_specs, out_specs, out_shape, scratch, flops, bytes_accessed, name):
    extra = {"grid": grid} if grid else {}
    return pl.pallas_call(
        kernel,
        in_specs=in_specs,
        out_specs=out_specs,
        out_shape=out_shape,
        scratch_shapes=scratch,
        compiler_params=pltpu.CompilerParams(vmem_limit_bytes=VMEM_BYTES),
        cost_estimate=pl.CostEstimate(
            flops=flops, bytes_accessed=bytes_accessed, transcendentals=0
        ),
        name=name,
        **extra,
    )


KEPT = (
    ((SEQ, D), F32),
    ((KEYS, 768), BF16),
    ((HEADS * 128, 128), BF16),
    ((HEADS * 128, 256), BF16),
    ((HEADS * 96, 384), BF16),
    ((SEQ, D), BF16),
    ((SEQ, D), F32),
    ((SEQ, FF), BF16),
    ((SEQ, FF), BF16),
)


def per_device(
    tokens,
    actions,
    game_ids,
    valid_steps,
    rewards,
    end_flags,
    embed_table,
    table_first,
    table_second,
    attn_weight,
    attn_first,
    attn_second,
    proj_weight,
    proj_first,
    proj_second,
    up_weight,
    up_first,
    up_second,
    up_bias,
    bias_first,
    bias_second,
    down_weight,
    down_first,
    down_second,
    vectors,
    vectors_first,
    vectors_second,
    head_weight,
    head_first,
    head_second,
    side_weight,
    side_first,
    side_second,
):
    n_high = lax.axis_size("wide") // 4
    wide, core = lax.axis_index("wide"), lax.axis_index("narrow")
    rows = side_weight.shape[0]
    fast = rows == 16
    place = jnp.stack([wide if fast else jnp.zeros_like(wide), core, wide]).astype(jnp.int32)

    def flat(a):
        return jnp.swapaxes(a, -1, -2)

    params = (
        (flat(embed_table), flat(table_first), flat(table_second)),
        (attn_weight, attn_first, attn_second),
        (flat(proj_weight), flat(proj_first), flat(proj_second)),
        (up_weight, up_first, up_second),
        (up_bias, bias_first, bias_second),
        (flat(down_weight), flat(down_first), flat(down_second)),
        (vectors, vectors_first, vectors_second),
        (head_weight, head_first, head_second),
        (flat(side_weight), flat(side_first), flat(side_second)),
    )
    table, attn, proj, up, _, down, _, head, side = (group[0] for group in params)

    piece_first = call(
        pack_first_kernel,
        None,
        [SMEM_SPEC] + [VMEM_SPEC] * 6,
        VMEM_SPEC,
        shaped((rows, HALF_FIRST_COLS), BF16),
        [pltpu.VMEM((rows, 128), F32)],
        10**6,
        10**6,
        "pack_first",
    )(place, table, attn, proj, up, down, side)
    first_mine = gather_plane(gather_column(piece_first, n_high))
    first_other = gather_cores(first_mine)
    piece_second = call(
        pack_second_kernel,
        None,
        [VMEM_SPEC] * 5 + [ANY_SPEC],
        VMEM_SPEC,
        shaped((rows, HALF_SECOND_COLS), BF16),
        [],
        10**6,
        10**6,
        "pack_second",
    )(attn, proj, up, down, head, first_mine[1])
    second_column = gather_column(piece_second, n_high)
    second_mine = gather_plane(second_column)
    first_parts = in_blocks(first_mine, wide) + in_blocks(first_other, wide)
    other_bias = swap(up_bias, "narrow", 1)

    count = tokens.shape[0] // lax.axis_size("narrow")
    meta = call(
        prepare_kernel,
        None,
        [SMEM_SPEC] * 2 + [VMEM_SPEC] * 5 + [ANY_SPEC],
        VMEM_SPEC,
        shaped((count, SEQ, 128), jnp.int32),
        [pltpu.VMEM((24, FRAMES), jnp.int32)],
        10**6,
        10**6,
        "prepare",
    )(place, game_ids, flat(tokens), actions, valid_steps, rewards, end_flags, first_mine[1])

    kept_specs = [row_spec(shape) for shape, _ in KEPT]
    kept_shapes = [shaped((count,) + shape, dtype) for shape, dtype in KEPT]
    row_f32 = shaped((count, SEQ, D), F32)
    meta_spec = row_spec((SEQ, 128))
    vec_specs = [full_spec(vectors), full_spec(up_bias), full_spec(up_bias)]
    w_spec = pl.BlockSpec((D, COL_FIRST), lambda i: (0, 0))
    side_spec = pl.BlockSpec((D, 128), lambda i: (0, 0))
    results = call(
        first_forward_kernel,
        (count,),
        [SMEM_SPEC, meta_spec] + vec_specs + [full_spec(a) for a in first_parts] + [ANY_SPEC],
        [w_spec, side_spec, row_spec((SEQ, D))] + kept_specs,
        [shaped((D, COL_FIRST), BF16), shaped((D, 128), BF16), row_f32] + kept_shapes,
        [pltpu.VMEM((D, COL_FIRST), BF16)],
        4 * 10**9,
        20 * 10**6,
        "first_forward",
    )(place, meta, vectors, up_bias, other_bias, *first_parts, second_column)
    w_first, side_copy, stream = results[0:3]
    kept = results[3:]
    received, side_copy = lax.optimization_barrier((second_mine[1:], side_copy))
    second_mine = second_mine[0:1] + received
    second_other = gather_cores(second_mine)
    second_parts = in_blocks(second_mine, wide) + in_blocks(second_other, wide)

    def blocks(cols):
        return pl.BlockSpec((4, 4, 16, cols), lambda i: (0, 0, 0, 0))

    def block_shapes(cols):
        return [shaped((4, 4, 16, cols), F32), shaped((4, 4, 16, cols), BF16)]

    small_spec = pl.BlockSpec((SMALL_ROWS, D), lambda i: (0, 0))
    small_shape = shaped((SMALL_ROWS, D), F32)
    scalar_spec = pl.BlockSpec((8, 128), lambda i: (0, 0))
    grad_stream, keep_second, send_second, small_grads, scalars = call(
        middle_kernel,
        (count,),
        [SMEM_SPEC, meta_spec]
        + vec_specs
        + [side_spec, row_spec((SEQ, D))]
        + [full_spec(a) for a in second_parts],
        [row_spec((SEQ, D))] + [blocks(HALF_SECOND_COLS)] * 2 + [small_spec, scalar_spec],
        [row_f32] + block_shapes(HALF_SECOND_COLS) + [small_shape, shaped((8, 128), F32)],
        [
            pltpu.VMEM((D, COL_SECOND + 128), BF16),
            pltpu.VMEM((D, COL_SECOND + 128), F32),
            pltpu.VMEM((SMALL_ROWS, D), F32),
            pltpu.VMEM((KEYS, 512), F32),
        ]
        + [pltpu.VMEM(shape, dtype) for shape, dtype in KEPT[1:]],
        15 * 10**9,
        20 * 10**6,
        "middle",
    )(place, meta, vectors, up_bias, other_bias, side_copy, stream, *second_parts)
    second_sums = add_cores(keep_second, send_second, wide, n_high)

    grad_mid, keep_ff, send_ff, small_grads = call(
        ff_backward_kernel,
        (count,),
        [SMEM_SPEC, full_spec(vectors), w_spec, row_spec((SEQ, D)), small_spec] + kept_specs[6:9],
        [row_spec((SEQ, D))] + [blocks(HALF_GRAD_COLS)] * 2 + [small_spec],
        [row_f32] + block_shapes(HALF_GRAD_COLS) + [small_shape],
        [pltpu.VMEM((D, 2048), F32), pltpu.VMEM((SMALL_ROWS, D), F32)],
        4 * 10**9,
        10 * 10**6,
        "ff_backward",
    )(place, vectors, w_first, grad_stream, small_grads, *kept[6:9])
    ff_sums = add_cores(keep_ff, send_ff, wide, n_high)
    other_sums = [jnp.concatenate(pair, axis=-1) for pair in zip(second_sums, ff_sums)]
    others_received = swap_plane(other_sums)

    keep_rest, send_rest, small_grads = call(
        attention_backward_kernel,
        (count,),
        [SMEM_SPEC, meta_spec, full_spec(vectors), w_spec, row_spec((SEQ, D)), small_spec]
        + kept_specs[0:6]
        + [ANY_SPEC],
        [blocks(HALF_GRAD_COLS)] * 2 + [small_spec],
        block_shapes(HALF_GRAD_COLS) + [small_shape],
        [
            pltpu.VMEM((D, 2048), F32),
            pltpu.VMEM((SMALL_ROWS, D), F32),
            pltpu.VMEM((KEYS, 512), F32),
        ],
        6 * 10**9,
        20 * 10**6,
        "attention_backward",
    )(place, meta, vectors, w_first, grad_mid, small_grads, *kept[0:6], other_sums[0])
    others_received, keep_rest = lax.optimization_barrier((others_received, keep_rest))
    rest_sums = add_cores(keep_rest, send_rest, wide, n_high)
    rest_received = swap_plane(rest_sums)
    other_pieces = column_pieces(add_plane(other_sums[0], others_received))
    rest_pieces = column_pieces(add_plane(rest_sums[0], rest_received))

    grad_rest, grad_others, message = call(
        finish_kernel,
        None,
        [SMEM_SPEC] + [VMEM_SPEC] * (2 * n_high + 1),
        [VMEM_SPEC] * 3,
        [
            shaped((rows, HALF_GRAD_COLS), F32),
            shaped((rows, HALF_GRAD_COLS + HALF_SECOND_COLS), F32),
            shaped((rows, 640), F32),
        ],
        [],
        10**6,
        10**6,
        "finish",
    )(place, *rest_pieces, *other_pieces, scalars)

    swapped = swap(message, "narrow", 1)
    if fast:
        sums = message[0:8, 512:640] + swapped[0:8, 512:640]
        quarter = jnp.where(core == 1, message[:, 384:512], swapped[:, 384:512])
        for distance in (1, 2):
            beside = swap(jnp.concatenate([quarter, sums]), "wide", distance)
            quarter = jnp.where(wide & distance == 0, quarter, beside[0:16])
            sums = sums + beside[16:24]
        beside = swap(jnp.concatenate([quarter, sums]), "wide", 4)
        near = jnp.concatenate([quarter, beside[0:16], sums + beside[16:24]])
        far = swap(near, "wide", 8)
    else:
        sums = lax.psum(message[:, 512:640], ("wide", "narrow"))
        total = lax.psum(small_grads, ("wide", "narrow"))
        total = total.reshape(4, 8, 2, 128).transpose(0, 2, 1, 3).reshape(4, 16, 128)
        ends = jnp.pad(sums, ((0, 8 - rows), (0, 0)))
        near = jnp.concatenate([total[0], total[1], ends])
        far = jnp.concatenate([total[2], total[3], jnp.zeros_like(ends)])

    flat_params = [a for group in params for a in group]
    results = call(
        adam_kernel,
        None,
        [SMEM_SPEC] + [VMEM_SPEC] * 32,
        [VMEM_SPEC] * 30,
        [shaped((1, 1), F32)] * 3 + [shaped(a.shape, F32) for a in flat_params],
        [pltpu.VMEM((SMALL_ROWS, D), F32)],
        10**6,
        10**6,
        "adam",
    )(place, grad_rest, grad_others, swapped, near, far, *flat_params)
    news = list(results[3:])
    for group in (0, 2, 5, 8):
        for member in range(3 * group, 3 * group + 3):
            news[member] = flat(news[member])
    return tuple(a.reshape(()) for a in results[0:3]) + tuple(news)


def solution(mesh):
    placed = (
        P("wide", None, None),
        P("wide", None),
        P("wide"),
        P("wide", None),
        P("wide", None),
        P("wide", None),
        P(None, "wide"),
        P(None, "wide"),
        P(None, "wide"),
        P(None, None, "wide", "narrow"),
        P(None, None, "wide", "narrow"),
        P(None, None, "wide", "narrow"),
        P(None, "narrow", "wide"),
        P(None, "narrow", "wide"),
        P(None, "narrow", "wide"),
        P(None, "wide", "narrow"),
        P(None, "wide", "narrow"),
        P(None, "wide", "narrow"),
        P(None, "narrow"),
        P(None, "narrow"),
        P(None, "narrow"),
        P(None, "narrow", "wide"),
        P(None, "narrow", "wide"),
        P(None, "narrow", "wide"),
        P(),
        P(),
        P(),
        P("wide", "narrow"),
        P("wide", "narrow"),
        P("wide", "narrow"),
        P("wide", None),
        P("wide", None),
        P("wide", None),
    )
    return jax.shard_map(
        per_device,
        mesh=mesh,
        in_specs=placed,
        out_specs=(P(), P(), P()) + placed[6:],
        check_vma=False,
    )
```

```python
import functools

import jax
import jax.numpy as jnp
from jax import lax
from jax.experimental import pallas as pl
from jax.experimental.pallas import tpu as pltpu
from jax.sharding import PartitionSpec as P

D = 256
HEADS = 4
HEAD_DIM = 64
FF = 1024
VOCAB = 512
ACTIONS = 18
GAMES = 26
OBS = 16
FRAMES = 20
STEP_NUMBER = 5
FRAME_TOKENS = 17
LENGTH = 340
ROWS = 896
NVEC = 14

EPS_NORM = 1e-05
BETA_ONE = 0.5
BETA_TWO = 0.5
RATE_TABLE = 0.5
RATE_MATRIX = 0.05
RATE_VECTOR = 0.2
DECAY_RATE = 0.01
EPS_ADAM = 1e-08
CLIP_AT = 0.1

SEQ = 352
KEYS = 384
QBLOCKS = ((0, 128, 128), (128, 128, 256), (256, 96, 384))

COL_QKV, COL_PROJ, COL_UP, COL_DOWN, COL_LAYER = 0, 768, 1024, 2048, 3072
HALF_ATTENTION = ((0, 128, 0), (128, 128, 256), (256, 128, 512), (384, 128, COL_PROJ))
HALF_LAYER = HALF_ATTENTION + ((512, 512, COL_UP), (1024, 512, COL_DOWN))
COL_TABLE, COL_SMALL, COL_FIRST = 3072, 3968, 4096
HALF_FIRST = HALF_LAYER + ((1536, 512, COL_TABLE),)
HALF_FIRST_COLS = 2048
COL_HEAD, COL_SECOND = 3072, 3584
HALF_SECOND = HALF_LAYER + ((1536, 256, COL_HEAD),)
HALF_SECOND_COLS = 1792
GRAD_UP, GRAD_DOWN = 0, 1024
HALF_GRAD_FF = ((0, 512, GRAD_UP), (512, 512, GRAD_DOWN))
GRAD_TABLE, GRAD_SMALL = 1024, 1920
HALF_GRAD_REST = HALF_ATTENTION + ((512, 512, GRAD_TABLE),)
HALF_GRAD_COLS = 1024
SMALL_ROWS, SMALL_BIAS, SMALL_SIDE = 32, 14, 22

F32, BF16 = jnp.float32, jnp.bfloat16
VMEM_BYTES = 60 * 1024 * 1024


def dot_nn(a, b):
    return lax.dot_general(a, b, (((1,), (0,)), ((), ())), preferred_element_type=F32)


def dot_nt(a, b):
    return lax.dot_general(a, b, (((1,), (1,)), ((), ())), preferred_element_type=F32)


def dot_tn(a, b):
    return lax.dot_general(a, b, (((0,), (0,)), ((), ())), preferred_element_type=F32)


def tiles(rows, size):
    return [slice(first, first + size) for first in range(0, rows, size)]


def normalise(x):
    centred = x - jnp.mean(x, axis=1, keepdims=True)
    scale = lax.rsqrt(jnp.mean(centred * centred, axis=1, keepdims=True) + EPS_NORM)
    return centred * scale, scale


def normalise_back(grad, xhat, scale, gain):
    inner = grad * gain
    mean_one = jnp.mean(inner, axis=1, keepdims=True)
    mean_two = jnp.mean(inner * xhat, axis=1, keepdims=True)
    return scale * (inner - mean_one - xhat * mean_two)


def column_sum(a):
    return jnp.sum(a, axis=0, keepdims=True)


def fold(a):
    return jnp.sum(a.reshape(a.shape[0] // 8, 8, a.shape[1]), axis=0)


def plus(total, a):
    return a if total is None else total + a


def split_heads(source_ref, column, row, count, target_ref, target_row):
    for h in range(HEADS):
        lanes = slice(h * HEAD_DIM, (h + 1) * HEAD_DIM)
        target_ref[target_row + h * count : target_row + (h + 1) * count, lanes] = source_ref[
            row : row + count, column + h * HEAD_DIM : column + (h + 1) * HEAD_DIM
        ]


def assemble(pieces_mine, pieces_other, place_ref, w_ref, halves):
    me, core = place_ref[0], place_ref[1]
    is_first = core == 0
    for p in range(4):
        for z in range(4):
            row = pl.multiple_of((me ^ (4 * z + p)) * 16, 16)
            for src, width, dest in halves:
                mine = pieces_mine[p][z, :, src : src + width]
                other = pieces_other[p][z, :, src : src + width]
                if dest == COL_QKV:
                    mine, other = mine * 0.125, other * 0.125
                w_ref[pl.ds(row, 16), dest : dest + width] = jnp.where(is_first, mine, other)
                w_ref[pl.ds(row, 16), dest + width : dest + 2 * width] = jnp.where(
                    is_first, other, mine
                )


def disperse(g_ref, place_ref, keep_ref, send_ref, halves, scaled=True):
    me, core = place_ref[0], place_ref[1]
    is_first = core == 0
    for p in range(4):
        for z in range(4):
            row = pl.multiple_of((me ^ (4 * z + p)) * 16, 16)
            for src, width, dest in halves:
                low = g_ref[pl.ds(row, 16), dest : dest + width]
                high = g_ref[pl.ds(row, 16), dest + width : dest + 2 * width]
                if scaled and dest == COL_QKV:
                    low, high = low * 0.125, high * 0.125
                keep_ref[p, z, :, src : src + width] = jnp.where(is_first, low, high)
                send_ref[p, z, :, src : src + width] = jnp.where(is_first, high, low).astype(BF16)


def make_hits(meta_ref, hits_ref):
    for rows in tiles(SEQ, 32):
        lane = lax.broadcasted_iota(jnp.int32, (32, ROWS), 1)
        place = lax.broadcasted_iota(jnp.int32, (32, 1), 0) + (VOCAB + ACTIONS + GAMES + rows.start)
        meta = meta_ref[rows]
        hit = (lane == meta[:, 0:1]) | (lane == meta[:, 1:2]) | (lane == place)
        hits_ref[rows] = jnp.where(hit, 1.0, 0.0).astype(BF16)


def lower_norm(x_ref, gain, offset, out_ref):
    for rows in tiles(SEQ, 32):
        out_ref[rows] = (normalise(x_ref[rows])[0] * gain + offset).astype(BF16)


def layer_forward(x_ref, w_ref, vec, bias, kept, work):
    qkv_ref, p_ref, o_ref, m_ref, h_ref, gp_ref, a_ref, c_ref = kept
    qs_ref, kv_ref, score_refs, u_ref, y_ref = work
    lower_norm(x_ref, vec[0:1], vec[1:2], a_ref)
    for j in range(3):
        cols = slice(256 * j, 256 * j + 256)
        qkv_ref[0:SEQ, cols] = dot_nn(a_ref[...], w_ref[:, cols]).astype(BF16)
    qkv_ref[SEQ:KEYS] = jnp.zeros((KEYS - SEQ, 768), BF16)
    split_heads(qkv_ref, 512, 0, KEYS, kv_ref, 0)
    for (first, count, seen), s_ref in zip(QBLOCKS, score_refs):
        base = HEADS * first
        split_heads(qkv_ref, 0, first, count, qs_ref, base)
        s_ref[...] = dot_nt(
            qs_ref[base : base + HEADS * count], qkv_ref[0:seen, 256:512]
        )
        for rows in tiles(HEADS * count, 32):
            row = lax.broadcasted_iota(jnp.int32, (32, 128), 0) + rows.start % count
            causal = row >= lax.broadcasted_iota(jnp.int32, (32, 128), 1)
            scores = jnp.where(causal, s_ref[rows, seen - 128 :], -1e30)
            if seen > 128:
                scores = jnp.concatenate([s_ref[rows, : seen - 128], scores], axis=1)
            expanded = jnp.exp(scores - jnp.max(scores, axis=1, keepdims=True))
            probs = expanded * (1.0 / jnp.sum(expanded, axis=1, keepdims=True))
            p_ref[base + rows.start : base + rows.stop, 0:seen] = probs.astype(BF16)
        out = dot_nn(
            jnp.concatenate(
                [p_ref[base + h * count : base + (h + 1) * count, 0:seen] for h in range(HEADS)],
                axis=1,
            ),
            jnp.concatenate([kv_ref[h * KEYS : h * KEYS + seen] for h in range(HEADS)], axis=0),
        )
        o_ref[first : first + count] = out.astype(BF16)
    y_ref[...] = dot_nt(o_ref[...], w_ref[:, COL_PROJ : COL_PROJ + 256])
    for rows in tiles(SEQ, 32):
        middle = x_ref[rows] + (y_ref[rows] + vec[2:3])
        m_ref[rows] = middle
        c_ref[rows] = (normalise(middle)[0] * vec[3:4] + vec[4:5]).astype(BF16)
    for chunk in range(4):
        cols = slice(256 * chunk, 256 * chunk + 256)
        u_ref[chunk] = dot_nn(c_ref[...], w_ref[:, COL_UP + cols.start : COL_UP + cols.stop])
        for rows in tiles(SEQ, 32):
            up = u_ref[chunk, rows] + bias[:, cols]
            square = up * up
            bent = jnp.tanh(up * (0.7978845608028654 + 0.0356774081363 * square))
            half = 0.5 + 0.5 * bent
            hidden = up * half
            slope = 0.7978845608028654 + 0.1070322244089 * square
            gp_ref[rows, cols] = (half + hidden * (1.0 - bent) * slope).astype(BF16)
            h_ref[rows, cols] = hidden.astype(BF16)
    y_ref[...] = dot_nt(h_ref[...], w_ref[:, COL_DOWN : COL_DOWN + FF])


def add_gradient(g_ref, column, left_ref, right_ref, left_turned):
    left_turned[...] = jnp.transpose(left_ref[...])
    for first in range(0, right_ref.shape[1], 256):
        cols = slice(first, min(first + 256, right_ref.shape[1]))
        g_ref[:, column + cols.start : column + cols.stop] += dot_nn(
            left_turned[...], right_ref[0:SEQ, cols]
        )


def ff_backward(grad_ref, grad16_ref, w_ref, vec, kept, g_ref, g_up, g_down, v_ref, v_row, bias_row, work, mid_ref, mid16_ref):
    m_ref, h_ref, gp_ref, c_ref = kept
    u_ref, y_ref, du_ref, turned_ref = work
    for chunk in range(4):
        cols = slice(256 * chunk, 256 * chunk + 256)
        u_ref[chunk] = dot_nn(
            grad16_ref[...], w_ref[:, COL_DOWN + cols.start : COL_DOWN + cols.stop]
        )
        total = None
        for rows in tiles(SEQ, 32):
            grad_up = u_ref[chunk, rows] * gp_ref[rows, cols].astype(F32)
            total = plus(total, fold(grad_up))
            du_ref[rows, cols] = grad_up.astype(BF16)
        v_ref[bias_row + chunk] += total
    add_gradient(g_ref, g_down, grad16_ref, h_ref, turned_ref.at[0])
    add_gradient(g_ref, g_up, c_ref, du_ref, turned_ref.at[1])
    y_ref[...] = dot_nt(du_ref[...], w_ref[:, COL_UP : COL_UP + FF])
    totals = [None] * 3
    for rows in tiles(SEQ, 32):
        xhat, scale = normalise(m_ref[rows])
        grad = y_ref[rows]
        mid = grad_ref[rows] + normalise_back(grad, xhat, scale, vec[3:4])
        mid_ref[rows] = mid
        if mid16_ref is not None:
            mid16_ref[rows] = mid.astype(BF16)
        for i, a in enumerate((mid, grad * xhat, grad)):
            totals[i] = plus(totals[i], fold(a))
    for i in range(3):
        v_ref[v_row + 2 + i] += totals[i]


def attention_backward(mid_ref, mid16_ref, w_ref, vec, kept, g_ref, v_ref, v_row, work, out_ref, out16_ref):
    x_ref, qkv_ref, p_ref, o_ref, a_ref = kept
    qs_ref, kv_ref, dos_ref, ds_ref, dkv_ref, dqkv_ref, score_refs, y_ref, turned_ref = work
    add_gradient(g_ref, COL_PROJ, mid16_ref, o_ref, turned_ref.at[0])
    dqkv_ref[:, 0:256] = dot_nn(mid16_ref[...], w_ref[:, COL_PROJ : COL_PROJ + 256]).astype(BF16)
    split_heads(qkv_ref, 256, 0, KEYS, kv_ref, 0)
    dkv_ref[...] = jnp.zeros(dkv_ref.shape, F32)
    for first, count, seen in QBLOCKS:
        split_heads(dqkv_ref, 0, first, count, dos_ref, HEADS * first)
    for (first, count, seen), s_ref in zip(QBLOCKS, score_refs):
        base = HEADS * first
        block = slice(base, base + HEADS * count)
        s_ref[...] = dot_nt(dos_ref[block], qkv_ref[0:seen, 512:768])
        for rows in tiles(HEADS * count, 32):
            here = slice(base + rows.start, base + rows.stop)
            probs, grad = p_ref[here, 0:seen].astype(F32), s_ref[rows]
            inner = jnp.sum(probs * grad, axis=1, keepdims=True)
            ds_ref[here, 0:seen] = (probs * (grad - inner)).astype(BF16)
        grad_query = dot_nn(
            jnp.concatenate(
                [ds_ref[base + h * count : base + (h + 1) * count, 0:seen] for h in range(HEADS)],
                axis=1,
            ),
            jnp.concatenate([kv_ref[h * KEYS : h * KEYS + seen] for h in range(HEADS)], axis=0),
        )
        dqkv_ref[first : first + count, 0:256] = grad_query.astype(BF16)
        dkv_ref[0:seen, 0:256] += dot_tn(ds_ref[block, 0:seen], qs_ref[block])
        dkv_ref[0:seen, 256:512] += dot_tn(p_ref[block, 0:seen], dos_ref[block])
    for rows in tiles(SEQ, 32):
        dqkv_ref[rows, 256:768] = dkv_ref[rows].astype(BF16)
    add_gradient(g_ref, COL_QKV, a_ref, dqkv_ref, turned_ref.at[1])
    y_ref[...] = dot_nt(dqkv_ref[...], w_ref[:, COL_QKV : COL_QKV + 768])
    totals = [None] * 2
    for rows in tiles(SEQ, 32):
        xhat, scale = normalise(x_ref[rows])
        grad = y_ref[rows]
        out = mid_ref[rows] + normalise_back(grad, xhat, scale, vec[0:1])
        if out_ref is not None:
            out_ref[rows] = out
        if out16_ref is not None:
            out16_ref[rows] = out.astype(BF16)
        for i, a in enumerate((grad * xhat, grad)):
            totals[i] = plus(totals[i], fold(a))
    for i in range(2):
        v_ref[v_row + i] += totals[i]


def own_bias(place_ref, mine, other):
    is_first = place_ref[1] == 0
    return jnp.concatenate(
        [jnp.where(is_first, mine, other), jnp.where(is_first, other, mine)], axis=1
    )


def prepare_kernel(place_ref, games_ref, tokens, actions, valid, rewards, ends, after, out, x_ref):
    count = out.shape[0]
    frames = tokens.shape[2]
    base = place_ref[1] * count
    row = lax.broadcasted_iota(jnp.int32, (SEQ, frames), 0)
    start = lax.broadcasted_iota(jnp.int32, (SEQ, frames), 1) * FRAME_TOKENS
    here = jnp.where((row >= start) & (row < start + FRAME_TOKENS), 1.0, 0.0).astype(BF16)
    coming = jnp.where((row >= start - FRAME_TOKENS) & (row < start), 1.0, 0.0).astype(BF16)
    passed = jnp.sum(jnp.where(row >= start + FRAME_TOKENS, 1, 0), axis=1, keepdims=True)
    place = lax.broadcasted_iota(jnp.int32, (SEQ, 1), 0)
    spot = place - passed * FRAME_TOKENS
    lane = lax.broadcasted_iota(jnp.int32, (SEQ, 24), 1)
    wide_lane = lax.broadcasted_iota(jnp.int32, (SEQ, 128), 1)
    inside = place < LENGTH
    x_ref[...] = jnp.zeros(x_ref.shape, jnp.int32)
    for s in range(count):
        x_ref[0:OBS] = tokens[base + s]
        x_ref[16:17] = actions[pl.ds(base + s, 1)] + VOCAB
        x_ref[17:18] = valid[pl.ds(base + s, 1)]
        x_ref[18:19] = rewards[pl.ds(base + s, 1)]
        x_ref[19:20] = ends[pl.ds(base + s, 1)] + 3
        high = (x_ref[...] >> 4).astype(F32).astype(BF16)
        low = (x_ref[...] & 15).astype(F32).astype(BF16)
        now = dot_nt(here, high) * 16.0 + dot_nt(here, low)
        soon = dot_nt(coming, high) * 16.0 + dot_nt(coming, low)

        def pick(condition, a):
            return jnp.sum(jnp.where(condition, a, 0.0), axis=1, keepdims=True).astype(jnp.int32)

        ids = jnp.where(inside, pick(lane == spot, now), -1)
        game = jnp.where(inside, games_ref[base + s] + (VOCAB + ACTIONS), -1)
        target = pick((lane == spot + 1) & (spot < 15), now)
        target = target + pick((lane == 0) & (spot == 16), soon)
        weight = pick((lane == 17) & (spot < 15), now) + pick((lane == 17) & (spot == 16), soon)
        side = pick((lane == 17) & (spot == 16), now)
        reward, end = pick(lane == 18, now), pick(lane == 19, now)
        result = jnp.zeros((SEQ, 128), jnp.int32)
        for c, column in enumerate((ids, game, target, weight, side, reward, end)):
            result = jnp.where(wide_lane == c, column, result)
        out[s] = result


def first_forward_kernel(*refs):
    place_ref, meta_ref, vec_ref, bias_ref, bias_other = refs[0:5]
    mine, other = refs[5:9], refs[9:13]
    w_out, side_out, next_ref, hits_ref, x_ref = refs[13:18]
    kept = [ref.at[0] for ref in refs[18:26]]
    w_ref, qs_ref, kv_ref, s0, s1, s2, u_ref, y_ref = refs[26:34]

    @pl.when(pl.program_id(0) == 0)
    def _():
        assemble(mine, other, place_ref, w_ref, HALF_FIRST)
        w_out[...] = w_ref[...]
        side_out[...] = w_ref[:, COL_SMALL:]
        qs_ref[...] = jnp.zeros(qs_ref.shape, BF16)
        kv_ref[...] = jnp.zeros(kv_ref.shape, BF16)

    make_hits(meta_ref.at[0], hits_ref.at[0])
    x_ref[0] = dot_nt(hits_ref[0], w_ref[:, COL_TABLE : COL_TABLE + ROWS])
    bias = own_bias(place_ref, bias_ref[0:1], bias_other[0:1])
    vec = vec_ref[0:6]
    layer_forward(x_ref.at[0], w_ref, vec, bias, kept, (qs_ref, kv_ref, (s0, s1, s2), u_ref, y_ref))
    m_ref = kept[3]
    for rows in tiles(SEQ, 32):
        next_ref[0, rows] = m_ref[rows] + (y_ref[rows] + vec[5:6])


def codebook_losses(logits, meta):
    weight = meta[:, 3:4].astype(F32)
    peak = jnp.max(logits, axis=1, keepdims=True)
    expanded = jnp.exp(logits - peak)
    total = jnp.sum(expanded, axis=1, keepdims=True)
    hit = lax.broadcasted_iota(jnp.int32, logits.shape, 1) == meta[:, 2:3]
    picked = jnp.sum(jnp.where(hit, logits, 0.0), axis=1, keepdims=True)
    loss = weight * (peak + jnp.log(total) - picked)
    return loss, expanded * (weight / total) - jnp.where(hit, weight, 0.0)


def side_losses(side, meta):
    lane = lax.broadcasted_iota(jnp.int32, side.shape, 1)
    is_reward, is_end = lane < 3, (lane == 3) | (lane == 4)
    is_side = lane < 5
    weight = meta[:, 4:5].astype(F32)
    reward_peak = jnp.max(jnp.where(is_reward, side, -1e30), axis=1, keepdims=True)
    end_peak = jnp.max(jnp.where(is_end, side, -1e30), axis=1, keepdims=True)
    shifted = jnp.where(is_side, side - jnp.where(is_reward, reward_peak, end_peak), 0.0)
    expanded = jnp.where(is_side, jnp.exp(shifted), 0.0)
    reward_total = jnp.sum(jnp.where(is_reward, expanded, 0.0), axis=1, keepdims=True)
    end_total = jnp.sum(jnp.where(is_end, expanded, 0.0), axis=1, keepdims=True)
    hit = (lane == meta[:, 5:6]) | (lane == meta[:, 6:7])
    picked = jnp.sum(jnp.where(hit, side, 0.0), axis=1, keepdims=True)
    terms = reward_peak + jnp.log(reward_total) + end_peak + jnp.log(end_total) - picked
    grad = expanded * jnp.where(is_reward, weight / reward_total, weight / end_total)
    return weight * terms, grad - jnp.where(hit, weight, 0.0), weight


def middle_kernel(*refs):
    place_ref, meta_ref, vec_ref, bias_ref, bias_other, side_ref, in_ref = refs[0:7]
    mine, other = refs[7:11], refs[11:15]
    grad_ref, keep_ref, send_ref, v_out, scalar_ref = refs[15:20]
    w_ref, g_ref, v_ref = refs[20:23]
    kept = refs[23:31]
    qkv_ref, p_ref, o_ref, m_ref, h_ref, gp_ref, a_ref, c_ref = kept
    qs_ref, kv_ref, s0, s1, s2, u_ref, y_ref = refs[31:38]
    du_ref, turned_ref, dos_ref, ds_ref, dkv_ref, dqkv_ref = refs[38:44]
    last_ref, final_ref, logit_ref, dlogit_ref, up_ref, up16_ref, mid_ref, mid16_ref = refs[44:52]
    scores = (s0, s1, s2)
    step = pl.program_id(0)

    @pl.when(step == 0)
    def _():
        assemble(mine, other, place_ref, w_ref, HALF_SECOND)
        w_ref[:, COL_SECOND:] = side_ref[...]
        g_ref[...] = jnp.zeros(g_ref.shape, F32)
        v_ref[...] = jnp.zeros(v_ref.shape, F32)
        scalar_ref[...] = jnp.zeros(scalar_ref.shape, F32)
        for ref in (qs_ref, kv_ref, dos_ref):
            ref[...] = jnp.zeros(ref.shape, BF16)

    x_ref = in_ref.at[0]
    vec = vec_ref[6:12]
    bias = own_bias(place_ref, bias_ref[1:2], bias_other[1:2])
    layer_forward(x_ref, w_ref, vec, bias, kept, (qs_ref, kv_ref, scores, u_ref, y_ref))

    gain, offset = vec_ref[12:13], vec_ref[13:14]
    for rows in tiles(SEQ, 32):
        last = m_ref[rows] + (y_ref[rows] + vec[5:6])
        last_ref[rows] = last
        final_ref[rows] = (normalise(last)[0] * gain + offset).astype(BF16)
    cols_head = slice(COL_HEAD, COL_HEAD + VOCAB + 128)
    logit_ref[...] = dot_nn(final_ref[...], w_ref[:, cols_head])
    loss, valid = None, None
    for rows in tiles(SEQ, 32):
        meta = meta_ref[0, rows]
        token_loss, grad = codebook_losses(logit_ref[rows, :VOCAB], meta)
        dlogit_ref[rows, :VOCAB] = grad.astype(BF16)
        side_loss, grad, weight = side_losses(logit_ref[rows, VOCAB:], meta)
        dlogit_ref[rows, VOCAB:] = grad.astype(BF16)
        loss, valid = plus(loss, token_loss + side_loss), plus(valid, weight)
    scalar_lane = lax.broadcasted_iota(jnp.int32, (8, 128), 1)
    scalar_row = lax.broadcasted_iota(jnp.int32, (8, 128), 0) == 0
    scalar_ref[...] += jnp.where(scalar_row & (scalar_lane == 0), column_sum(loss), 0.0)
    scalar_ref[...] += jnp.where(scalar_row & (scalar_lane == 1), column_sum(valid), 0.0)
    add_gradient(g_ref, COL_HEAD, final_ref, dlogit_ref, turned_ref.at[0])
    y_ref[...] = dot_nt(dlogit_ref[...], w_ref[:, cols_head])
    totals = [None] * 3
    for rows in tiles(SEQ, 32):
        xhat, scale = normalise(last_ref[rows])
        grad = y_ref[rows]
        up = normalise_back(grad, xhat, scale, gain)
        up_ref[rows] = up
        up16_ref[rows] = up.astype(BF16)
        for i, a in enumerate((up, grad * xhat, grad)):
            totals[i] = plus(totals[i], fold(a))
    for i in range(3):
        v_ref[11 + i] += totals[i]
    ff_backward(
        up_ref,
        up16_ref,
        w_ref,
        vec,
        (m_ref, h_ref, gp_ref, c_ref),
        g_ref,
        COL_UP,
        COL_DOWN,
        v_ref,
        6,
        SMALL_BIAS + 4,
        (u_ref, y_ref, du_ref, turned_ref),
        mid_ref,
        mid16_ref,
    )
    attention_backward(
        mid_ref,
        mid16_ref,
        w_ref,
        vec,
        (x_ref, qkv_ref, p_ref, o_ref, a_ref),
        g_ref,
        v_ref,
        6,
        (qs_ref, kv_ref, dos_ref, ds_ref, dkv_ref, dqkv_ref, scores, y_ref, turned_ref),
        grad_ref.at[0],
        None,
    )

    @pl.when(step == pl.num_programs(0) - 1)
    def _():
        disperse(g_ref, place_ref, keep_ref, send_ref, HALF_SECOND)
        side = jnp.transpose(g_ref[:, COL_SECOND:])
        for i in range(5):
            v_ref[SMALL_SIDE + i, 0:1] = side[i : i + 1]
        v_out[...] = v_ref[...]


def ff_backward_kernel(*refs):
    place_ref, vec_ref, w_ref, grad_ref, v_in = refs[0:5]
    kept = [ref.at[0] for ref in refs[5:9]]
    mid_ref, keep_ref, send_ref, v_out = refs[9:13]
    g_ref, v_ref, grad16_ref, u_ref, y_ref, du_ref, turned_ref = refs[13:20]
    step = pl.program_id(0)

    @pl.when(step == 0)
    def _():
        g_ref[...] = jnp.zeros(g_ref.shape, F32)
        v_ref[...] = v_in[...]

    total = None
    for rows in tiles(SEQ, 32):
        grad = grad_ref[0, rows]
        grad16_ref[rows] = grad.astype(BF16)
        total = plus(total, fold(grad))
    v_ref[5] += total
    ff_backward(
        grad_ref.at[0],
        grad16_ref,
        w_ref,
        vec_ref[0:6],
        kept,
        g_ref,
        GRAD_UP,
        GRAD_DOWN,
        v_ref,
        0,
        SMALL_BIAS,
        (u_ref, y_ref, du_ref, turned_ref),
        mid_ref.at[0],
        None,
    )

    @pl.when(step == pl.num_programs(0) - 1)
    def _():
        disperse(g_ref, place_ref, keep_ref, send_ref, HALF_GRAD_FF, False)
        v_out[...] = v_ref[...]


def attention_backward_kernel(*refs):
    place_ref, vec_ref, w_ref, mid_ref, hits_ref, v_in = refs[0:6]
    kept = [ref.at[0] for ref in refs[6:11]]
    keep_ref, send_ref, v_out = refs[12:15]
    g_ref, v_ref, mid16_ref, out16_ref = refs[15:19]
    qs_ref, kv_ref, s0, s1, s2, y_ref = refs[19:25]
    turned_ref, dos_ref, ds_ref, dkv_ref, dqkv_ref = refs[25:30]
    qkv_ref = kept[1]
    step = pl.program_id(0)

    @pl.when(step == 0)
    def _():
        g_ref[...] = jnp.zeros(g_ref.shape, F32)
        v_ref[...] = v_in[...]
        for ref in (qs_ref, kv_ref, dos_ref):
            ref[...] = jnp.zeros(ref.shape, BF16)

    for first, count, _ in QBLOCKS:
        split_heads(qkv_ref, 0, first, count, qs_ref, HEADS * first)
    for rows in tiles(SEQ, 32):
        mid16_ref[rows] = mid_ref[0, rows].astype(BF16)
    attention_backward(
        mid_ref.at[0],
        mid16_ref,
        w_ref,
        vec_ref[0:6],
        kept,
        g_ref,
        v_ref,
        0,
        (qs_ref, kv_ref, dos_ref, ds_ref, dkv_ref, dqkv_ref, (s0, s1, s2), y_ref, turned_ref),
        None,
        out16_ref,
    )
    add_gradient(g_ref, GRAD_TABLE, out16_ref, hits_ref.at[0], turned_ref.at[0])

    @pl.when(step == pl.num_programs(0) - 1)
    def _():
        small = jnp.sum(v_ref[...], axis=1)
        v_out[...] = small
        for block in range(16):
            quarter = small[8 * (block // 4) : 8 * (block // 4) + 8]
            g_ref[16 * block : 16 * block + 8, GRAD_SMALL:] = quarter[:, 0:128]
            g_ref[16 * block + 8 : 16 * block + 16, GRAD_SMALL:] = quarter[:, 128:256]
        disperse(g_ref, place_ref, keep_ref, send_ref, HALF_GRAD_REST)


def pack_layer(attn, proj, up, down, layer, out):
    for j in range(3):
        out[:, 128 * j : 128 * j + 128] = attn[layer, j].astype(BF16)
    out[:, 384:512] = proj[layer].astype(BF16)
    out[:, 512:1024] = up[layer].astype(BF16)
    out[:, 1024:1536] = down[layer].astype(BF16)


def pack_kernel(place_ref, table, attn, proj, up, down, head, side, first, second, pad_ref):
    pack_layer(attn, proj, up, down, 0, first)
    pack_layer(attn, proj, up, down, 1, second)
    second[:, 1536:1792] = head[...].astype(BF16)
    rows = side.shape[1]
    eye = (
        lax.broadcasted_iota(jnp.int32, (rows, rows), 0)
        == lax.broadcasted_iota(jnp.int32, (rows, rows), 1)
    )
    eye = jnp.where(eye, 1.0, 0.0).astype(BF16)
    pad_ref[...] = jnp.zeros(pad_ref.shape, F32)
    pad_ref[:, 0:5] = dot_nt(eye, side[...].astype(BF16))
    high = jnp.concatenate([table[:, 512:896], pad_ref[...]], axis=1)
    first[:, 1536:2048] = jnp.where(place_ref[1] == 0, table[:, 0:512], high).astype(BF16)


def finish_kernel(*refs):
    count = (len(refs) - 6) // 2
    place_ref = refs[0]
    scalar_ref = refs[2 * count + 1]
    out_rest, out_other, out_table, out_small = refs[2 * count + 2 :]
    square = jnp.zeros((1, 1), F32)
    for pieces, out in ((refs[1 : count + 1], out_rest), (refs[count + 1 : 2 * count + 1], out_other)):
        total = pieces[0][...]
        for piece in pieces[1:]:
            total = total + piece[...].astype(F32)
        out[...] = total
        square = square + column_sum(jnp.sum(total * total, axis=1, keepdims=True))
    small = out_rest[:, 896:1024]
    extra = column_sum(jnp.sum(small * small, axis=1, keepdims=True))
    square = square - jnp.where(place_ref[1] == 0, 0.0, extra)
    out_table[...] = out_rest[:, 512:1024]
    rows = small.shape[0]
    out_small[0:rows] = small
    lane = lax.broadcasted_iota(jnp.int32, (8, 128), 1)
    top = lax.broadcasted_iota(jnp.int32, (8, 128), 0) == 0
    out_small[rows : rows + 8] = scalar_ref[...] + jnp.where(top & (lane == 2), square, 0.0)


def adam_rule(weight, moment, second, gradient, step_rate, decay_rate):
    moment_new = BETA_ONE * moment + (1.0 - BETA_ONE) * gradient
    second_new = BETA_TWO * second + (1.0 - BETA_TWO) * gradient * gradient
    moment_hat = moment_new / (1.0 - BETA_ONE**STEP_NUMBER)
    second_hat = second_new / (1.0 - BETA_TWO**STEP_NUMBER)
    weight_new = weight - step_rate * (
        moment_hat / (jnp.sqrt(second_hat) + EPS_ADAM) + decay_rate * weight
    )
    return (weight_new, moment_new, second_new)


def adam_kernel(*refs):
    place_ref, rest, others, swapped = refs[0:4]
    quarters = refs[4:8]
    params = [refs[8 + 3 * i : 11 + 3 * i] for i in range(9)]
    loss_ref, valid_ref, norm_ref = refs[35:38]
    outs = [refs[38 + 3 * i : 41 + 3 * i] for i in range(9)]
    small_ref = refs[65]
    me, wide = place_ref[0], place_ref[2]
    is_first = place_ref[1] == 0
    rows = rest.shape[0]
    for k in range(4):
        row = pl.multiple_of(((me >> 2) ^ k) * 8, 8)
        small_ref[pl.ds(row, 8), 0:128] = quarters[k][0:8]
        small_ref[pl.ds(row, 8), 128:256] = quarters[k][8:16]
    tops = [quarter[16:17] for quarter in quarters]
    scalars = (tops[0] + tops[1]) + (tops[2] + tops[3])
    small = small_ref[...]
    loss, valid, square = scalars[:, 0:1], scalars[:, 1:2], scalars[:, 2:3]
    square = square + column_sum(jnp.sum(small * small, axis=1, keepdims=True))
    inverse = 1.0 / valid
    norm = jnp.sqrt(square) * inverse
    loss_ref[...], valid_ref[...], norm_ref[...] = loss, valid, norm
    factor = jnp.minimum(1.0, CLIP_AT / (norm + 1e-06)) * inverse
    table, attn, proj, up, bias, down, vectors, head, side = range(9)

    def update(which, index, gradient, step_rate, decay_rate):
        news = adam_rule(
            *(ref[index] for ref in params[which]), factor * gradient, step_rate, decay_rate
        )
        for ref, new in zip(outs[which], news):
            ref[index] = new

    layers = ((rest, others, 1792), (others, others, 512))
    for layer, (attention, feed, at) in enumerate(layers):
        for j in range(3):
            update(attn, (layer, j), attention[:, 128 * j : 128 * j + 128], RATE_MATRIX, DECAY_RATE)
        update(proj, (layer,), attention[:, 384:512], RATE_MATRIX, DECAY_RATE)
        update(up, (layer,), feed[:, at : at + 512], RATE_MATRIX, DECAY_RATE)
        update(down, (layer,), feed[:, at + 512 : at + 1024], RATE_MATRIX, DECAY_RATE)
        for i in range(2):
            low = SMALL_BIAS + 4 * layer + i
            row = jnp.where(is_first, small[low : low + 1], small[low + 2 : low + 3])
            index = (slice(layer, layer + 1), slice(256 * i, 256 * i + 256))
            update(bias, index, row, RATE_VECTOR, 0.0)
    whole = (slice(None), slice(None))
    update(head, whole, others[:, 1536:1792], RATE_MATRIX, DECAY_RATE)
    mine, theirs = rest[:, 512:1024], swapped[:, 0:512]
    low, high = jnp.where(is_first, mine, theirs), jnp.where(is_first, theirs, mine)
    update(table, (slice(None), slice(0, 512)), low, RATE_TABLE, DECAY_RATE)
    update(table, (slice(None), slice(512, 896)), high[:, 0:384], RATE_TABLE, DECAY_RATE)
    update(vectors, whole, small[0:NVEC], RATE_VECTOR, 0.0)
    turned = pltpu.roll(small[SMALL_SIDE : SMALL_SIDE + 8], lax.rem(D - wide * rows, D), 1)
    update(side, whole, turned[0:5, 0:rows], RATE_MATRIX, DECAY_RATE)


def swap(a, axis, distance):
    size = lax.axis_size(axis)
    return lax.ppermute(a, axis, [(i, i ^ distance) for i in range(size)])


def swap_column(piece, n_high):
    return [piece] + [swap(piece, "wide", 4 * k) for k in range(1, n_high)]


def gather_plane(column):
    return [column] + [swap(column, "wide", p) for p in range(1, 4)]


def gather_cores(mine):
    return [swap(a, "narrow", 1) for a in mine]


def in_blocks(parts, wide):
    n_high, rows, cols = parts[0].shape
    if rows == 16:
        return parts
    whole = jnp.stack(parts, axis=1).reshape(4 * n_high, rows, cols)
    whole = whole[wide ^ jnp.arange(4 * n_high)].reshape(4, 4, 16, cols)
    return [whole[:, p] for p in range(4)]


def in_pieces(blocks, wide, n_high):
    cols = blocks.shape[-1]
    if n_high == 4:
        return blocks
    rows = 64 // n_high
    whole = blocks.transpose(1, 0, 2, 3).reshape(4 * n_high, rows, cols)
    whole = whole[wide ^ jnp.arange(4 * n_high)]
    return whole.reshape(n_high, 4, rows, cols).transpose(1, 0, 2, 3)


def add_cores(keep, send, wide, n_high):
    keep, send = in_pieces(keep, wide, n_high), in_pieces(send, wide, n_high)
    received = swap(send, "narrow", 1)
    return [keep[p] + received[p].astype(F32) for p in range(4)]


def swap_plane(sums):
    return [swap(sums[p].astype(BF16), "wide", p) for p in range(1, 4)]


def add_plane(own, received):
    for a in received:
        own = own + a.astype(F32)
    return own


def column_pieces(own):
    return [own[0]] + [swap(own[k].astype(BF16), "wide", 4 * k) for k in range(1, own.shape[0])]


def full_spec(a):
    return pl.BlockSpec(a.shape, lambda *_: (0,) * len(a.shape))


def row_spec(shape):
    return pl.BlockSpec((1,) + shape, lambda i: (i,) + (0,) * len(shape))


def shaped(shape, dtype):
    return jax.ShapeDtypeStruct(shape, dtype)


VMEM_SPEC = pl.BlockSpec(memory_space=pltpu.VMEM)
ANY_SPEC = pl.BlockSpec(memory_space=pl.ANY)
SMEM_SPEC = pl.BlockSpec(memory_space=pltpu.SMEM)


def call(kernel, grid, in_specs, out_specs, out_shape, scratch, flops, bytes_accessed, name):
    extra = {"grid": grid} if grid else {}
    return pl.pallas_call(
        kernel,
        in_specs=in_specs,
        out_specs=out_specs,
        out_shape=out_shape,
        scratch_shapes=scratch,
        compiler_params=pltpu.CompilerParams(vmem_limit_bytes=VMEM_BYTES),
        cost_estimate=pl.CostEstimate(
            flops=flops, bytes_accessed=bytes_accessed, transcendentals=0
        ),
        name=name,
        **extra,
    )


KEPT = (
    ((KEYS, 768), BF16),
    ((HEADS * SEQ, KEYS), BF16),
    ((SEQ, D), BF16),
    ((SEQ, D), F32),
    ((SEQ, FF), BF16),
    ((SEQ, FF), BF16),
    ((SEQ, D), BF16),
    ((SEQ, D), BF16),
)
FORWARD_WORK = [
    pltpu.VMEM((HEADS * SEQ, D), BF16),
    pltpu.VMEM((HEADS * KEYS, D), BF16),
    pltpu.VMEM((HEADS * 128, 128), F32),
    pltpu.VMEM((HEADS * 128, 256), F32),
    pltpu.VMEM((HEADS * 96, 384), F32),
    pltpu.VMEM((4, SEQ, 256), F32),
    pltpu.VMEM((SEQ, D), F32),
]
FF_WORK = pltpu.VMEM((SEQ, FF), BF16)
TURNED_WORK = pltpu.VMEM((2, D, SEQ), BF16)
ATTENTION_WORK = [
    pltpu.VMEM((HEADS * SEQ, D), BF16),
    pltpu.VMEM((HEADS * SEQ, KEYS), BF16),
    pltpu.VMEM((KEYS, 512), F32),
    pltpu.VMEM((SEQ, 768), BF16),
]


def per_device(
    tokens,
    actions,
    game_ids,
    valid_steps,
    rewards,
    end_flags,
    embed_table,
    table_first,
    table_second,
    attn_weight,
    attn_first,
    attn_second,
    proj_weight,
    proj_first,
    proj_second,
    up_weight,
    up_first,
    up_second,
    up_bias,
    bias_first,
    bias_second,
    down_weight,
    down_first,
    down_second,
    vectors,
    vectors_first,
    vectors_second,
    head_weight,
    head_first,
    head_second,
    side_weight,
    side_first,
    side_second,
):
    n_high = lax.axis_size("wide") // 4
    wide, core = lax.axis_index("wide"), lax.axis_index("narrow")
    rows = side_weight.shape[0]
    fast = rows == 16
    place = jnp.stack([wide if fast else jnp.zeros_like(wide), core, wide]).astype(jnp.int32)

    def flat(a):
        return jnp.swapaxes(a, -1, -2)

    params = (
        (flat(embed_table), flat(table_first), flat(table_second)),
        (attn_weight, attn_first, attn_second),
        (flat(proj_weight), flat(proj_first), flat(proj_second)),
        (up_weight, up_first, up_second),
        (up_bias, bias_first, bias_second),
        (flat(down_weight), flat(down_first), flat(down_second)),
        (vectors, vectors_first, vectors_second),
        (head_weight, head_first, head_second),
        (flat(side_weight), flat(side_first), flat(side_second)),
    )
    table, attn, proj, up, _, down, _, head, side = (group[0] for group in params)

    piece_first, piece_second = call(
        pack_kernel,
        None,
        [SMEM_SPEC] + [VMEM_SPEC] * 7,
        [VMEM_SPEC] * 2,
        [shaped((rows, HALF_FIRST_COLS), BF16), shaped((rows, HALF_SECOND_COLS), BF16)],
        [pltpu.VMEM((rows, 128), F32)],
        10**6,
        10**6,
        "pack",
    )(place, table, attn, proj, up, down, head, side)
    first_column = swap_column(piece_first, n_high)

    count = tokens.shape[0] // lax.axis_size("narrow")
    meta = call(
        prepare_kernel,
        None,
        [SMEM_SPEC] * 2 + [VMEM_SPEC] * 5 + [ANY_SPEC],
        VMEM_SPEC,
        shaped((count, SEQ, 128), jnp.int32),
        [pltpu.VMEM((24, FRAMES), jnp.int32)],
        10**6,
        10**6,
        "prepare",
    )(place, game_ids, flat(tokens), actions, valid_steps, rewards, end_flags, piece_first)
    first_column, meta = lax.optimization_barrier((first_column, meta))
    first_mine = gather_plane(jnp.stack(first_column))
    piece_second, beside = lax.optimization_barrier((piece_second, first_mine[1]))
    first_mine = [first_mine[0], beside] + first_mine[2:]
    first_other = gather_cores(first_mine)
    second_column = jnp.stack(swap_column(piece_second, n_high))
    second_mine = gather_plane(second_column)
    first_parts = in_blocks(first_mine, wide) + in_blocks(first_other, wide)
    other_bias = swap(up_bias, "narrow", 1)

    kept_specs = [row_spec(shape) for shape, _ in KEPT]
    kept_shapes = [shaped((count,) + shape, dtype) for shape, dtype in KEPT]
    row_f32 = shaped((count, SEQ, D), F32)
    meta_spec = row_spec((SEQ, 128))
    vec_specs = [full_spec(vectors), full_spec(up_bias), full_spec(up_bias)]
    w_spec = pl.BlockSpec((D, COL_FIRST), lambda i: (0, 0))
    side_spec = pl.BlockSpec((D, 128), lambda i: (0, 0))
    hits_spec = row_spec((SEQ, ROWS))
    results = call(
        first_forward_kernel,
        (count,),
        [SMEM_SPEC, meta_spec] + vec_specs + [full_spec(a) for a in first_parts],
        [w_spec, side_spec, row_spec((SEQ, D)), hits_spec, row_spec((SEQ, D))] + kept_specs,
        [shaped((D, COL_FIRST), BF16), shaped((D, 128), BF16), row_f32]
        + [shaped((count, SEQ, ROWS), BF16), row_f32]
        + kept_shapes,
        [pltpu.VMEM((D, COL_FIRST), BF16)] + FORWARD_WORK,
        4 * 10**9,
        20 * 10**6,
        "first_forward",
    )(place, meta, vectors, up_bias, other_bias, *first_parts)
    w_first, side_copy, stream, hits, stream_first = results[0:5]
    kept = results[5:]
    kept_qkv, kept_p, kept_o, kept_m, kept_h, kept_gp, kept_a, kept_c = kept
    received, side_copy = lax.optimization_barrier((second_mine[1:], side_copy))
    second_mine = second_mine[0:1] + received
    second_other = gather_cores(second_mine)
    second_parts = in_blocks(second_mine, wide) + in_blocks(second_other, wide)

    def blocks(cols):
        return pl.BlockSpec((4, 4, 16, cols), lambda i: (0, 0, 0, 0))

    def block_shapes(cols):
        return [shaped((4, 4, 16, cols), F32), shaped((4, 4, 16, cols), BF16)]

    small_spec = pl.BlockSpec((SMALL_ROWS, 8, D), lambda i: (0, 0, 0))
    small_shape = shaped((SMALL_ROWS, 8, D), F32)
    small_scratch = pltpu.VMEM((SMALL_ROWS, 8, D), F32)
    scalar_spec = pl.BlockSpec((8, 128), lambda i: (0, 0))
    grad_stream, keep_second, send_second, small_grads, scalars = call(
        middle_kernel,
        (count,),
        [SMEM_SPEC, meta_spec]
        + vec_specs
        + [side_spec, row_spec((SEQ, D))]
        + [full_spec(a) for a in second_parts],
        [row_spec((SEQ, D))] + [blocks(HALF_SECOND_COLS)] * 2 + [small_spec, scalar_spec],
        [row_f32] + block_shapes(HALF_SECOND_COLS) + [small_shape, shaped((8, 128), F32)],
        [
            pltpu.VMEM((D, COL_SECOND + 128), BF16),
            pltpu.VMEM((D, COL_SECOND + 128), F32),
            small_scratch,
        ]
        + [pltpu.VMEM(shape, dtype) for shape, dtype in KEPT]
        + FORWARD_WORK
        + [FF_WORK, TURNED_WORK]
        + ATTENTION_WORK
        + [
            pltpu.VMEM((SEQ, D), F32),
            pltpu.VMEM((SEQ, D), BF16),
            pltpu.VMEM((SEQ, VOCAB + 128), F32),
            pltpu.VMEM((SEQ, VOCAB + 128), BF16),
            pltpu.VMEM((SEQ, D), F32),
            pltpu.VMEM((SEQ, D), BF16),
            pltpu.VMEM((SEQ, D), F32),
            pltpu.VMEM((SEQ, D), BF16),
        ],
        15 * 10**9,
        20 * 10**6,
        "middle",
    )(place, meta, vectors, up_bias, other_bias, side_copy, stream, *second_parts)
    second_sums = add_cores(keep_second, send_second, wide, n_high)

    kept_ff = (kept_m, kept_h, kept_gp, kept_c)
    grad_mid, keep_ff, send_ff, small_grads = call(
        ff_backward_kernel,
        (count,),
        [SMEM_SPEC, full_spec(vectors), w_spec, row_spec((SEQ, D)), small_spec]
        + [row_spec(a.shape[1:]) for a in kept_ff],
        [row_spec((SEQ, D))] + [blocks(HALF_GRAD_COLS)] * 2 + [small_spec],
        [row_f32] + block_shapes(HALF_GRAD_COLS) + [small_shape],
        [
            pltpu.VMEM((D, 2048), F32),
            small_scratch,
            pltpu.VMEM((SEQ, D), BF16),
            pltpu.VMEM((4, SEQ, 256), F32),
            pltpu.VMEM((SEQ, D), F32),
            FF_WORK,
            TURNED_WORK,
        ],
        4 * 10**9,
        10 * 10**6,
        "ff_backward",
    )(place, vectors, w_first, grad_stream, small_grads, *kept_ff)
    ff_sums = add_cores(keep_ff, send_ff, wide, n_high)
    other_sums = [jnp.concatenate(pair, axis=-1) for pair in zip(second_sums, ff_sums)]
    others_received = swap_plane(other_sums)

    kept_attention = (stream_first, kept_qkv, kept_p, kept_o, kept_a)
    keep_rest, send_rest, small_grads = call(
        attention_backward_kernel,
        (count,),
        [SMEM_SPEC, full_spec(vectors), w_spec, row_spec((SEQ, D)), hits_spec, small_spec]
        + [row_spec(a.shape[1:]) for a in kept_attention]
        + [ANY_SPEC],
        [blocks(HALF_GRAD_COLS)] * 2 + [pl.BlockSpec((SMALL_ROWS, D), lambda i: (0, 0))],
        block_shapes(HALF_GRAD_COLS) + [shaped((SMALL_ROWS, D), F32)],
        [
            pltpu.VMEM((D, 2048), F32),
            small_scratch,
            pltpu.VMEM((SEQ, D), BF16),
            pltpu.VMEM((SEQ, D), BF16),
        ]
        + FORWARD_WORK[0:5]
        + [pltpu.VMEM((SEQ, D), F32), TURNED_WORK]
        + ATTENTION_WORK,
        6 * 10**9,
        20 * 10**6,
        "attention_backward",
    )(place, vectors, w_first, grad_mid, hits, small_grads, *kept_attention, other_sums[0])
    others_received, keep_rest = lax.optimization_barrier((others_received, keep_rest))
    rest_sums = add_cores(keep_rest, send_rest, wide, n_high)
    rest_received = swap_plane(rest_sums)
    other_pieces = column_pieces(add_plane(other_sums[0], others_received))
    rest_pieces = column_pieces(add_plane(rest_sums[0], rest_received))

    grad_rest, grad_others, table_part, small = call(
        finish_kernel,
        None,
        [SMEM_SPEC] + [VMEM_SPEC] * (2 * n_high + 1),
        [VMEM_SPEC] * 4,
        [
            shaped((rows, HALF_GRAD_COLS), F32),
            shaped((rows, HALF_GRAD_COLS + HALF_SECOND_COLS), F32),
            shaped((rows, 512), F32),
            shaped((rows + 8, 128), F32),
        ],
        [],
        10**6,
        10**6,
        "finish",
    )(place, *rest_pieces, *other_pieces, scalars)

    if fast:
        is_small = (jnp.arange(rows + 8) < rows)[:, None]
        beside = swap(small, "narrow", 1)
        small = jnp.where(is_small, jnp.where(core == 1, small, beside), small + beside)
        plane = [small] + [swap(small, "wide", p) for p in range(1, 4)]
        chosen = jnp.where(
            wide & 2 == 0,
            jnp.where(wide & 1 == 0, plane[0], plane[1]),
            jnp.where(wide & 1 == 0, plane[2], plane[3]),
        )
        small = jnp.where(is_small, chosen, (plane[0] + plane[1]) + (plane[2] + plane[3]))
        quarters = [small] + [swap(small, "wide", 4 * k) for k in range(1, 4)]
    else:
        sums = lax.psum(small[rows:], ("wide", "narrow"))
        total = lax.psum(small_grads, ("wide", "narrow"))
        total = total.reshape(4, 8, 2, 128).transpose(0, 2, 1, 3).reshape(4, 16, 128)
        ends = [sums] + [jnp.zeros_like(sums)] * 3
        quarters = [jnp.concatenate(pair) for pair in zip(total, ends)]
    swapped = swap(table_part, "narrow", 1)

    flat_params = [a for group in params for a in group]
    results = call(
        adam_kernel,
        None,
        [SMEM_SPEC] + [VMEM_SPEC] * 34,
        [VMEM_SPEC] * 30,
        [shaped((1, 1), F32)] * 3 + [shaped(a.shape, F32) for a in flat_params],
        [pltpu.VMEM((SMALL_ROWS, D), F32)],
        10**6,
        10**6,
        "adam",
    )(place, grad_rest, grad_others, swapped, *quarters, *flat_params)
    news = list(results[3:])
    for group in (0, 2, 5, 8):
        for member in range(3 * group, 3 * group + 3):
            news[member] = flat(news[member])
    return tuple(a.reshape(()) for a in results[0:3]) + tuple(news)


def solution(mesh):
    placed = (
        P("wide", None, None),
        P("wide", None),
        P("wide"),
        P("wide", None),
        P("wide", None),
        P("wide", None),
        P(None, "wide"),
        P(None, "wide"),
        P(None, "wide"),
        P(None, None, "wide", "narrow"),
        P(None, None, "wide", "narrow"),
        P(None, None, "wide", "narrow"),
        P(None, "narrow", "wide"),
        P(None, "narrow", "wide"),
        P(None, "narrow", "wide"),
        P(None, "wide", "narrow"),
        P(None, "wide", "narrow"),
        P(None, "wide", "narrow"),
        P(None, "narrow"),
        P(None, "narrow"),
        P(None, "narrow"),
        P(None, "narrow", "wide"),
        P(None, "narrow", "wide"),
        P(None, "narrow", "wide"),
        P(),
        P(),
        P(),
        P("wide", "narrow"),
        P("wide", "narrow"),
        P("wide", "narrow"),
        P("wide", None),
        P("wide", None),
        P("wide", None),
    )
    return jax.shard_map(
        per_device,
        mesh=mesh,
        in_specs=placed,
        out_specs=(P(), P(), P()) + placed[6:],
        check_vma=False,
    )
```

```python
import functools

import jax
import jax.numpy as jnp
from jax import lax
from jax.experimental import pallas as pl
from jax.experimental.pallas import tpu as pltpu
from jax.sharding import PartitionSpec as P

D = 256
HEADS = 4
HEAD_DIM = 64
FF = 1024
VOCAB = 512
ACTIONS = 18
GAMES = 26
OBS = 16
FRAMES = 20
STEP_NUMBER = 5
FRAME_TOKENS = 17
LENGTH = 340
ROWS = 896
NVEC = 14

EPS_NORM = 1e-05
BETA_ONE = 0.5
BETA_TWO = 0.5
RATE_TABLE = 0.5
RATE_MATRIX = 0.05
RATE_VECTOR = 0.2
DECAY_RATE = 0.01
EPS_ADAM = 1e-08
CLIP_AT = 0.1

SEQ = 352
KEYS = 384
STEP_SEQS = 2
STEP = STEP_SEQS * SEQ
TILE = 64
QBLOCKS = ((0, 128, 128), (128, 128, 256), (256, 96, 384))

COL_QKV, COL_PROJ, COL_UP, COL_DOWN, COL_LAYER = 0, 768, 1024, 2048, 3072
HALF_ATTENTION = ((0, 128, 0), (128, 128, 256), (256, 128, 512), (384, 128, COL_PROJ))
HALF_LAYER = HALF_ATTENTION + ((512, 512, COL_UP), (1024, 512, COL_DOWN))
COL_TABLE, COL_SMALL, COL_FIRST = 3072, 3968, 4096
HALF_FIRST = HALF_LAYER + ((1536, 512, COL_TABLE),)
HALF_FIRST_COLS = 2048
COL_HEAD, COL_SECOND = 3072, 3584
HALF_SECOND = HALF_LAYER + ((1536, 256, COL_HEAD),)
HALF_SECOND_COLS = 1792
GRAD_UP, GRAD_DOWN = 0, 1024
HALF_GRAD_FF = ((0, 512, GRAD_UP), (512, 512, GRAD_DOWN))
GRAD_TABLE, GRAD_SMALL = 1024, 1920
HALF_GRAD_REST = HALF_ATTENTION + ((512, 512, GRAD_TABLE),)
HALF_GRAD_COLS = 1024
SMALL_ROWS, SMALL_BIAS, SMALL_SIDE = 32, 14, 22

F32, BF16 = jnp.float32, jnp.bfloat16
VMEM_BYTES = 60 * 1024 * 1024


def dot_nn(a, b):
    return lax.dot_general(a, b, (((1,), (0,)), ((), ())), preferred_element_type=F32)


def dot_nt(a, b):
    return lax.dot_general(a, b, (((1,), (1,)), ((), ())), preferred_element_type=F32)


def dot_tn(a, b):
    return lax.dot_general(a, b, (((0,), (0,)), ((), ())), preferred_element_type=F32)


def tiles(rows, size):
    return [slice(first, first + size) for first in range(0, rows, size)]


def normalise(x):
    centred = x - jnp.mean(x, axis=1, keepdims=True)
    scale = lax.rsqrt(jnp.mean(centred * centred, axis=1, keepdims=True) + EPS_NORM)
    return centred * scale, scale


def normalise_back(grad, xhat, scale, gain):
    inner = grad * gain
    mean_one = jnp.mean(inner, axis=1, keepdims=True)
    mean_two = jnp.mean(inner * xhat, axis=1, keepdims=True)
    return scale * (inner - mean_one - xhat * mean_two)


def column_sum(a):
    return jnp.sum(a, axis=0, keepdims=True)


def fold(a):
    return jnp.sum(a.reshape(a.shape[0] // 8, 8, a.shape[1]), axis=0)


def plus(total, a):
    return a if total is None else total + a


def split_heads(source_ref, column, row, count, target_ref, target_row):
    for h in range(HEADS):
        lanes = slice(h * HEAD_DIM, (h + 1) * HEAD_DIM)
        target_ref[target_row + h * count : target_row + (h + 1) * count, lanes] = source_ref[
            row : row + count, column + h * HEAD_DIM : column + (h + 1) * HEAD_DIM
        ]


def assemble(pieces_mine, pieces_other, place_ref, w_ref, halves):
    me, core = place_ref[0], place_ref[1]
    is_first = core == 0
    for p in range(4):
        for z in range(4):
            row = pl.multiple_of((me ^ (4 * z + p)) * 16, 16)
            for src, width, dest in halves:
                mine = pieces_mine[p][z, :, src : src + width]
                other = pieces_other[p][z, :, src : src + width]
                if dest == COL_QKV:
                    mine, other = mine * 0.125, other * 0.125
                w_ref[pl.ds(row, 16), dest : dest + width] = jnp.where(is_first, mine, other)
                w_ref[pl.ds(row, 16), dest + width : dest + 2 * width] = jnp.where(
                    is_first, other, mine
                )


def disperse(g_ref, place_ref, keep_ref, send_ref, halves, scaled=True):
    me, core = place_ref[0], place_ref[1]
    is_first = core == 0
    for p in range(4):
        for z in range(4):
            row = pl.multiple_of((me ^ (4 * z + p)) * 16, 16)
            for src, width, dest in halves:
                low = g_ref[pl.ds(row, 16), dest : dest + width]
                high = g_ref[pl.ds(row, 16), dest + width : dest + 2 * width]
                if scaled and dest == COL_QKV:
                    low, high = low * 0.125, high * 0.125
                keep_ref[p, z, :, src : src + width] = jnp.where(is_first, low, high)
                send_ref[p, z, :, src : src + width] = jnp.where(is_first, high, low).astype(BF16)


def make_hits(meta_ref, hits_ref):
    for s in range(STEP_SEQS):
        for first in range(0, SEQ, 32):
            rows = slice(s * SEQ + first, s * SEQ + first + 32)
            lane = lax.broadcasted_iota(jnp.int32, (32, ROWS), 1)
            place = lax.broadcasted_iota(jnp.int32, (32, 1), 0) + (VOCAB + ACTIONS + GAMES + first)
            meta = meta_ref[rows]
            hit = (lane == meta[:, 0:1]) | (lane == meta[:, 1:2]) | (lane == place)
            hits_ref[rows] = jnp.where(hit, 1.0, 0.0).astype(BF16)


def lower_norm(x_ref, gain, offset, out_ref):
    for rows in tiles(STEP, TILE):
        out_ref[rows] = (normalise(x_ref[rows])[0] * gain + offset).astype(BF16)


def split_queries(source_ref, stride, target_ref):
    for s in range(STEP_SEQS):
        for first, count, _ in QBLOCKS:
            split_heads(
                source_ref, 0, s * stride + first, count, target_ref, HEADS * (s * SEQ + first)
            )


def layer_forward(x_ref, w_ref, vec, bias, kept, work):
    qkv_ref, p_ref, o_ref, m_ref, h_ref, gp_ref, a_ref, c_ref = kept
    qs_ref, kv_ref, score_refs, u_ref, y_ref = work
    lower_norm(x_ref, vec[0:1], vec[1:2], a_ref)
    qkv = dot_nn(a_ref[...], w_ref[:, 0:768]).astype(BF16)
    for s in range(STEP_SEQS):
        qkv_ref[s * KEYS : s * KEYS + SEQ] = qkv[s * SEQ : (s + 1) * SEQ]
        qkv_ref[s * KEYS + SEQ : (s + 1) * KEYS] = jnp.zeros((KEYS - SEQ, 768), BF16)
    split_queries(qkv_ref, KEYS, qs_ref)
    for s in range(STEP_SEQS):
        key = s * KEYS
        split_heads(qkv_ref, 512, key, KEYS, kv_ref.at[s], 0)
        for (first, count, seen), s_ref in zip(QBLOCKS, score_refs):
            base = HEADS * (s * SEQ + first)
            s_ref[s] = dot_nt(
                qs_ref[base : base + HEADS * count], qkv_ref[key : key + seen, 256:512]
            )
            row = lax.broadcasted_iota(jnp.int32, (count, 128), 0)
            causal = row >= lax.broadcasted_iota(jnp.int32, (count, 128), 1)
            for rows in tiles(HEADS * count, count):
                scores = jnp.where(causal, s_ref[s, rows, seen - 128 :], -1e30)
                if seen > 128:
                    scores = jnp.concatenate([s_ref[s, rows, : seen - 128], scores], axis=1)
                expanded = jnp.exp(scores - jnp.max(scores, axis=1, keepdims=True))
                probs = expanded * (1.0 / jnp.sum(expanded, axis=1, keepdims=True))
                p_ref[base + rows.start : base + rows.stop, 0:seen] = probs.astype(BF16)
            out = dot_nn(
                jnp.concatenate(
                    [p_ref[base + h * count : base + (h + 1) * count, 0:seen] for h in range(HEADS)],
                    axis=1,
                ),
                jnp.concatenate(
                    [kv_ref[s, h * KEYS : h * KEYS + seen] for h in range(HEADS)], axis=0
                ),
            )
            o_ref[s * SEQ + first : s * SEQ + first + count] = out.astype(BF16)
    y_ref[...] = dot_nt(o_ref[...], w_ref[:, COL_PROJ : COL_PROJ + 256])
    for rows in tiles(STEP, TILE):
        middle = x_ref[rows] + (y_ref[rows] + vec[2:3])
        m_ref[rows] = middle
        c_ref[rows] = (normalise(middle)[0] * vec[3:4] + vec[4:5]).astype(BF16)
    u_ref[...] = dot_nn(c_ref[...], w_ref[:, COL_UP : COL_UP + FF])
    for rows in tiles(STEP, TILE):
        for chunk in range(4):
            cols = slice(256 * chunk, 256 * chunk + 256)
            up = u_ref[rows, cols] + bias[:, cols]
            square = up * up
            bent = jnp.tanh(up * (0.7978845608028654 + 0.0356774081363 * square))
            half = 0.5 + 0.5 * bent
            hidden = up * half
            slope = 0.7978845608028654 + 0.1070322244089 * square
            gp_ref[rows, cols] = (half + hidden * (1.0 - bent) * slope).astype(BF16)
            h_ref[rows, cols] = hidden.astype(BF16)
    y_ref[...] = dot_nt(h_ref[...], w_ref[:, COL_DOWN : COL_DOWN + FF])


def add_gradient(g_ref, column, left_ref, right_ref):
    g_ref[:, column : column + right_ref.shape[1]] += dot_tn(left_ref[...], right_ref[...])


def ff_backward(grad_ref, grad16_ref, w_ref, vec, kept, g_ref, g_up, g_down, v_ref, v_row, bias_row, work, mid_ref, mid16_ref):
    m_ref, h_ref, gp_ref, c_ref = kept
    u_ref, y_ref, du_ref = work
    u_ref[...] = dot_nn(grad16_ref[...], w_ref[:, COL_DOWN : COL_DOWN + FF])
    for chunk in range(4):
        cols = slice(256 * chunk, 256 * chunk + 256)
        total = None
        for rows in tiles(STEP, TILE):
            grad_up = u_ref[rows, cols] * gp_ref[rows, cols].astype(F32)
            total = plus(total, fold(grad_up))
            du_ref[rows, cols] = grad_up.astype(BF16)
        v_ref[bias_row + chunk] += total
    add_gradient(g_ref, g_down, grad16_ref, h_ref)
    add_gradient(g_ref, g_up, c_ref, du_ref)
    y_ref[...] = dot_nt(du_ref[...], w_ref[:, COL_UP : COL_UP + FF])
    totals = [None] * 3
    for rows in tiles(STEP, TILE):
        xhat, scale = normalise(m_ref[rows])
        grad = y_ref[rows]
        mid = grad_ref[rows] + normalise_back(grad, xhat, scale, vec[3:4])
        mid_ref[rows] = mid
        if mid16_ref is not None:
            mid16_ref[rows] = mid.astype(BF16)
        for i, a in enumerate((mid, grad * xhat, grad)):
            totals[i] = plus(totals[i], fold(a))
    for i in range(3):
        v_ref[v_row + 2 + i] += totals[i]


def attention_backward(mid_ref, mid16_ref, w_ref, vec, kept, g_ref, v_ref, v_row, work, out_ref, out16_ref):
    x_ref, qkv_ref, p_ref, o_ref, a_ref = kept
    qs_ref, kv_ref, dos_ref, ds_ref, dkv_ref, dqkv_ref, score_refs, y_ref = work
    add_gradient(g_ref, COL_PROJ, mid16_ref, o_ref)
    dqkv_ref[:, 0:256] = dot_nn(mid16_ref[...], w_ref[:, COL_PROJ : COL_PROJ + 256]).astype(BF16)
    dkv_ref[...] = jnp.zeros(dkv_ref.shape, F32)
    split_queries(dqkv_ref, SEQ, dos_ref)
    for s in range(STEP_SEQS):
        key = s * KEYS
        split_heads(qkv_ref, 256, key, KEYS, kv_ref.at[s], 0)
        for (first, count, seen), s_ref in zip(QBLOCKS, score_refs):
            base = HEADS * (s * SEQ + first)
            block = slice(base, base + HEADS * count)
            s_ref[s] = dot_nt(dos_ref[block], qkv_ref[key : key + seen, 512:768])
            for rows in tiles(HEADS * count, count):
                here = slice(base + rows.start, base + rows.stop)
                probs, grad = p_ref[here, 0:seen].astype(F32), s_ref[s, rows]
                inner = jnp.sum(probs * grad, axis=1, keepdims=True)
                ds_ref[here, 0:seen] = (probs * (grad - inner)).astype(BF16)
            grad_query = dot_nn(
                jnp.concatenate(
                    [ds_ref[base + h * count : base + (h + 1) * count, 0:seen] for h in range(HEADS)],
                    axis=1,
                ),
                jnp.concatenate(
                    [kv_ref[s, h * KEYS : h * KEYS + seen] for h in range(HEADS)], axis=0
                ),
            )
            at = s * SEQ + first
            dqkv_ref[at : at + count, 0:256] = grad_query.astype(BF16)
            dkv_ref[key : key + seen, 0:256] += dot_tn(ds_ref[block, 0:seen], qs_ref[block])
            dkv_ref[key : key + seen, 256:512] += dot_tn(p_ref[block, 0:seen], dos_ref[block])
        for rows in tiles(SEQ, 32):
            dqkv_ref[s * SEQ + rows.start : s * SEQ + rows.stop, 256:768] = dkv_ref[
                key + rows.start : key + rows.stop
            ].astype(BF16)
    add_gradient(g_ref, COL_QKV, a_ref, dqkv_ref)
    y_ref[...] = dot_nt(dqkv_ref[...], w_ref[:, COL_QKV : COL_QKV + 768])
    totals = [None] * 2
    for rows in tiles(STEP, TILE):
        xhat, scale = normalise(x_ref[rows])
        grad = y_ref[rows]
        out = mid_ref[rows] + normalise_back(grad, xhat, scale, vec[0:1])
        if out_ref is not None:
            out_ref[rows] = out
        if out16_ref is not None:
            out16_ref[rows] = out.astype(BF16)
        for i, a in enumerate((grad * xhat, grad)):
            totals[i] = plus(totals[i], fold(a))
    for i in range(2):
        v_ref[v_row + i] += totals[i]


def own_bias(place_ref, mine, other):
    is_first = place_ref[1] == 0
    return jnp.concatenate(
        [jnp.where(is_first, mine, other), jnp.where(is_first, other, mine)], axis=1
    )


def prepare_kernel(place_ref, games_ref, tokens, actions, valid, rewards, ends, after, out, x_ref):
    count = out.shape[0]
    frames = tokens.shape[2]
    base = place_ref[1] * count
    row = lax.broadcasted_iota(jnp.int32, (SEQ, frames), 0)
    start = lax.broadcasted_iota(jnp.int32, (SEQ, frames), 1) * FRAME_TOKENS
    here = jnp.where((row >= start) & (row < start + FRAME_TOKENS), 1.0, 0.0).astype(BF16)
    coming = jnp.where((row >= start - FRAME_TOKENS) & (row < start), 1.0, 0.0).astype(BF16)
    passed = jnp.sum(jnp.where(row >= start + FRAME_TOKENS, 1, 0), axis=1, keepdims=True)
    place = lax.broadcasted_iota(jnp.int32, (SEQ, 1), 0)
    spot = place - passed * FRAME_TOKENS
    lane = lax.broadcasted_iota(jnp.int32, (SEQ, 24), 1)
    wide_lane = lax.broadcasted_iota(jnp.int32, (SEQ, 128), 1)
    inside = place < LENGTH
    x_ref[...] = jnp.zeros(x_ref.shape, jnp.int32)
    for s in range(count):
        x_ref[0:OBS] = tokens[base + s]
        x_ref[16:17] = actions[pl.ds(base + s, 1)] + VOCAB
        x_ref[17:18] = valid[pl.ds(base + s, 1)]
        x_ref[18:19] = rewards[pl.ds(base + s, 1)]
        x_ref[19:20] = ends[pl.ds(base + s, 1)] + 3
        high = (x_ref[...] >> 4).astype(F32).astype(BF16)
        low = (x_ref[...] & 15).astype(F32).astype(BF16)
        now = dot_nt(here, high) * 16.0 + dot_nt(here, low)
        soon = dot_nt(coming, high) * 16.0 + dot_nt(coming, low)

        def pick(condition, a):
            return jnp.sum(jnp.where(condition, a, 0.0), axis=1, keepdims=True).astype(jnp.int32)

        ids = jnp.where(inside, pick(lane == spot, now), -1)
        game = jnp.where(inside, games_ref[base + s] + (VOCAB + ACTIONS), -1)
        target = pick((lane == spot + 1) & (spot < 15), now)
        target = target + pick((lane == 0) & (spot == 16), soon)
        weight = pick((lane == 17) & (spot < 15), now) + pick((lane == 17) & (spot == 16), soon)
        side = pick((lane == 17) & (spot == 16), now)
        reward, end = pick(lane == 18, now), pick(lane == 19, now)
        result = jnp.zeros((SEQ, 128), jnp.int32)
        for c, column in enumerate((ids, game, target, weight, side, reward, end)):
            result = jnp.where(wide_lane == c, column, result)
        out[s] = result


def first_forward_kernel(*refs):
    place_ref, meta_ref, vec_ref, bias_ref, bias_other = refs[0:5]
    mine, other = refs[5:9], refs[9:13]
    w_out, side_out, next_ref, hits_ref, x_ref = refs[13:18]
    kept = [ref.at[0] for ref in refs[18:26]]
    w_ref, qs_ref, kv_ref, s0, s1, s2, u_ref, y_ref = refs[26:34]

    @pl.when(pl.program_id(0) == 0)
    def _():
        assemble(mine, other, place_ref, w_ref, HALF_FIRST)
        w_out[...] = w_ref[...]
        side_out[...] = w_ref[:, COL_SMALL:]
        qs_ref[...] = jnp.zeros(qs_ref.shape, BF16)
        kv_ref[...] = jnp.zeros(kv_ref.shape, BF16)

    make_hits(meta_ref.at[0], hits_ref.at[0])
    x_ref[0] = dot_nt(hits_ref[0], w_ref[:, COL_TABLE : COL_TABLE + ROWS])
    bias = own_bias(place_ref, bias_ref[0:1], bias_other[0:1])
    vec = vec_ref[0:6]
    layer_forward(x_ref.at[0], w_ref, vec, bias, kept, (qs_ref, kv_ref, (s0, s1, s2), u_ref, y_ref))
    m_ref = kept[3]
    for rows in tiles(STEP, TILE):
        next_ref[0, rows] = m_ref[rows] + (y_ref[rows] + vec[5:6])


def codebook_losses(logits, meta):
    weight = meta[:, 3:4].astype(F32)
    peak = jnp.max(logits, axis=1, keepdims=True)
    expanded = jnp.exp(logits - peak)
    total = jnp.sum(expanded, axis=1, keepdims=True)
    hit = lax.broadcasted_iota(jnp.int32, logits.shape, 1) == meta[:, 2:3]
    picked = jnp.sum(jnp.where(hit, logits, 0.0), axis=1, keepdims=True)
    loss = weight * (peak + jnp.log(total) - picked)
    return loss, expanded * (weight / total) - jnp.where(hit, weight, 0.0)


def side_losses(side, meta):
    lane = lax.broadcasted_iota(jnp.int32, side.shape, 1)
    is_reward, is_end = lane < 3, (lane == 3) | (lane == 4)
    is_side = lane < 5
    weight = meta[:, 4:5].astype(F32)
    reward_peak = jnp.max(jnp.where(is_reward, side, -1e30), axis=1, keepdims=True)
    end_peak = jnp.max(jnp.where(is_end, side, -1e30), axis=1, keepdims=True)
    shifted = jnp.where(is_side, side - jnp.where(is_reward, reward_peak, end_peak), 0.0)
    expanded = jnp.where(is_side, jnp.exp(shifted), 0.0)
    reward_total = jnp.sum(jnp.where(is_reward, expanded, 0.0), axis=1, keepdims=True)
    end_total = jnp.sum(jnp.where(is_end, expanded, 0.0), axis=1, keepdims=True)
    hit = (lane == meta[:, 5:6]) | (lane == meta[:, 6:7])
    picked = jnp.sum(jnp.where(hit, side, 0.0), axis=1, keepdims=True)
    terms = reward_peak + jnp.log(reward_total) + end_peak + jnp.log(end_total) - picked
    grad = expanded * jnp.where(is_reward, weight / reward_total, weight / end_total)
    return weight * terms, grad - jnp.where(hit, weight, 0.0), weight


def middle_kernel(*refs):
    place_ref, meta_ref, vec_ref, bias_ref, bias_other, side_ref, in_ref = refs[0:7]
    mine, other = refs[7:11], refs[11:15]
    grad_ref, keep_ref, send_ref, v_out, scalar_ref = refs[15:20]
    w_ref, g_ref, v_ref = refs[20:23]
    kept = refs[23:31]
    qkv_ref, p_ref, o_ref, m_ref, h_ref, gp_ref, a_ref, c_ref = kept
    qs_ref, kv_ref, s0, s1, s2, u_ref, y_ref = refs[31:38]
    du_ref, dos_ref, ds_ref, dkv_ref, dqkv_ref = refs[38:43]
    last_ref, final_ref, logit_ref, dlogit_ref, up_ref, up16_ref, mid_ref, mid16_ref = refs[43:51]
    scores = (s0, s1, s2)
    step = pl.program_id(0)

    @pl.when(step == 0)
    def _():
        assemble(mine, other, place_ref, w_ref, HALF_SECOND)
        w_ref[:, COL_SECOND:] = side_ref[...]
        g_ref[...] = jnp.zeros(g_ref.shape, F32)
        v_ref[...] = jnp.zeros(v_ref.shape, F32)
        scalar_ref[...] = jnp.zeros(scalar_ref.shape, F32)
        for ref in (qs_ref, kv_ref, dos_ref):
            ref[...] = jnp.zeros(ref.shape, BF16)

    x_ref = in_ref.at[0]
    vec = vec_ref[6:12]
    bias = own_bias(place_ref, bias_ref[1:2], bias_other[1:2])
    layer_forward(x_ref, w_ref, vec, bias, kept, (qs_ref, kv_ref, scores, u_ref, y_ref))

    gain, offset = vec_ref[12:13], vec_ref[13:14]
    for rows in tiles(STEP, TILE):
        last = m_ref[rows] + (y_ref[rows] + vec[5:6])
        last_ref[rows] = last
        final_ref[rows] = (normalise(last)[0] * gain + offset).astype(BF16)
    cols_head = slice(COL_HEAD, COL_HEAD + VOCAB + 128)
    logit_ref[...] = dot_nn(final_ref[...], w_ref[:, cols_head])
    loss, valid = None, None
    for rows in tiles(STEP, TILE):
        meta = meta_ref[0, rows]
        token_loss, grad = codebook_losses(logit_ref[rows, :VOCAB], meta)
        dlogit_ref[rows, :VOCAB] = grad.astype(BF16)
        side_loss, grad, weight = side_losses(logit_ref[rows, VOCAB:], meta)
        dlogit_ref[rows, VOCAB:] = grad.astype(BF16)
        loss, valid = plus(loss, token_loss + side_loss), plus(valid, weight)
    scalar_lane = lax.broadcasted_iota(jnp.int32, (8, 128), 1)
    scalar_row = lax.broadcasted_iota(jnp.int32, (8, 128), 0) == 0
    scalar_ref[...] += jnp.where(scalar_row & (scalar_lane == 0), column_sum(loss), 0.0)
    scalar_ref[...] += jnp.where(scalar_row & (scalar_lane == 1), column_sum(valid), 0.0)
    add_gradient(g_ref, COL_HEAD, final_ref, dlogit_ref)
    y_ref[...] = dot_nt(dlogit_ref[...], w_ref[:, cols_head])
    totals = [None] * 3
    for rows in tiles(STEP, TILE):
        xhat, scale = normalise(last_ref[rows])
        grad = y_ref[rows]
        up = normalise_back(grad, xhat, scale, gain)
        up_ref[rows] = up
        up16_ref[rows] = up.astype(BF16)
        for i, a in enumerate((up, grad * xhat, grad)):
            totals[i] = plus(totals[i], fold(a))
    for i in range(3):
        v_ref[11 + i] += totals[i]
    ff_backward(
        up_ref,
        up16_ref,
        w_ref,
        vec,
        (m_ref, h_ref, gp_ref, c_ref),
        g_ref,
        COL_UP,
        COL_DOWN,
        v_ref,
        6,
        SMALL_BIAS + 4,
        (u_ref, y_ref, du_ref),
        mid_ref,
        mid16_ref,
    )
    attention_backward(
        mid_ref,
        mid16_ref,
        w_ref,
        vec,
        (x_ref, qkv_ref, p_ref, o_ref, a_ref),
        g_ref,
        v_ref,
        6,
        (qs_ref, kv_ref, dos_ref, ds_ref, dkv_ref, dqkv_ref, scores, y_ref),
        grad_ref.at[0],
        None,
    )

    @pl.when(step == pl.num_programs(0) - 1)
    def _():
        disperse(g_ref, place_ref, keep_ref, send_ref, HALF_SECOND)
        side = jnp.transpose(g_ref[:, COL_SECOND:])
        for i in range(5):
            v_ref[SMALL_SIDE + i, 0:1] = side[i : i + 1]
        v_out[...] = v_ref[...]


def ff_backward_kernel(*refs):
    place_ref, vec_ref, w_ref, grad_ref, v_in = refs[0:5]
    kept = [ref.at[0] for ref in refs[5:9]]
    mid_ref, keep_ref, send_ref, v_out = refs[9:13]
    g_ref, v_ref, grad16_ref, u_ref, y_ref, du_ref = refs[13:19]
    step = pl.program_id(0)

    @pl.when(step == 0)
    def _():
        g_ref[...] = jnp.zeros(g_ref.shape, F32)
        v_ref[...] = v_in[...]

    total = None
    for rows in tiles(STEP, TILE):
        grad = grad_ref[0, rows]
        grad16_ref[rows] = grad.astype(BF16)
        total = plus(total, fold(grad))
    v_ref[5] += total
    ff_backward(
        grad_ref.at[0],
        grad16_ref,
        w_ref,
        vec_ref[0:6],
        kept,
        g_ref,
        GRAD_UP,
        GRAD_DOWN,
        v_ref,
        0,
        SMALL_BIAS,
        (u_ref, y_ref, du_ref),
        mid_ref.at[0],
        None,
    )

    @pl.when(step == pl.num_programs(0) - 1)
    def _():
        disperse(g_ref, place_ref, keep_ref, send_ref, HALF_GRAD_FF, False)
        v_out[...] = v_ref[...]


def attention_backward_kernel(*refs):
    place_ref, vec_ref, w_ref, mid_ref, hits_ref, v_in = refs[0:6]
    kept = [ref.at[0] for ref in refs[6:11]]
    keep_ref, send_ref, v_out = refs[12:15]
    g_ref, v_ref, mid16_ref, out16_ref = refs[15:19]
    qs_ref, kv_ref, s0, s1, s2, y_ref = refs[19:25]
    dos_ref, ds_ref, dkv_ref, dqkv_ref = refs[25:29]
    qkv_ref = kept[1]
    step = pl.program_id(0)

    @pl.when(step == 0)
    def _():
        g_ref[...] = jnp.zeros(g_ref.shape, F32)
        v_ref[...] = v_in[...]
        for ref in (qs_ref, kv_ref, dos_ref):
            ref[...] = jnp.zeros(ref.shape, BF16)

    split_queries(qkv_ref, KEYS, qs_ref)
    for rows in tiles(STEP, TILE):
        mid16_ref[rows] = mid_ref[0, rows].astype(BF16)
    attention_backward(
        mid_ref.at[0],
        mid16_ref,
        w_ref,
        vec_ref[0:6],
        kept,
        g_ref,
        v_ref,
        0,
        (qs_ref, kv_ref, dos_ref, ds_ref, dkv_ref, dqkv_ref, (s0, s1, s2), y_ref),
        None,
        out16_ref,
    )
    add_gradient(g_ref, GRAD_TABLE, out16_ref, hits_ref.at[0])

    @pl.when(step == pl.num_programs(0) - 1)
    def _():
        small = jnp.sum(v_ref[...], axis=1)
        v_out[...] = small
        for block in range(16):
            quarter = small[8 * (block // 4) : 8 * (block // 4) + 8]
            g_ref[16 * block : 16 * block + 8, GRAD_SMALL:] = quarter[:, 0:128]
            g_ref[16 * block + 8 : 16 * block + 16, GRAD_SMALL:] = quarter[:, 128:256]
        disperse(g_ref, place_ref, keep_ref, send_ref, HALF_GRAD_REST)


def pack_layer(attn, proj, up, down, layer, out, at):
    for j in range(3):
        out[:, at + 128 * j : at + 128 * j + 128] = attn[layer, j].astype(BF16)
    out[:, at + 384 : at + 512] = proj[layer].astype(BF16)
    out[:, at + 512 : at + 1024] = up[layer].astype(BF16)
    out[:, at + 1024 : at + 1536] = down[layer].astype(BF16)


def pack_kernel(place_ref, table, attn, proj, up, down, head, side, out, pad_ref):
    pack_layer(attn, proj, up, down, 0, out, 0)
    pack_layer(attn, proj, up, down, 1, out, HALF_FIRST_COLS)
    out[:, HALF_FIRST_COLS + 1536 :] = head[...].astype(BF16)
    rows = side.shape[1]
    eye = (
        lax.broadcasted_iota(jnp.int32, (rows, rows), 0)
        == lax.broadcasted_iota(jnp.int32, (rows, rows), 1)
    )
    eye = jnp.where(eye, 1.0, 0.0).astype(BF16)
    pad_ref[...] = jnp.zeros(pad_ref.shape, F32)
    pad_ref[:, 0:5] = dot_nt(eye, side[...].astype(BF16))
    high = jnp.concatenate([table[:, 512:896], pad_ref[...]], axis=1)
    out[:, 1536:2048] = jnp.where(place_ref[1] == 0, table[:, 0:512], high).astype(BF16)


def finish_kernel(*refs):
    count = (len(refs) - 6) // 2
    place_ref = refs[0]
    scalar_ref = refs[2 * count + 1]
    out_rest, out_other, out_table, out_small = refs[2 * count + 2 :]
    square = jnp.zeros((1, 1), F32)
    for pieces, out in ((refs[1 : count + 1], out_rest), (refs[count + 1 : 2 * count + 1], out_other)):
        total = pieces[0][...]
        for piece in pieces[1:]:
            total = total + piece[...].astype(F32)
        out[...] = total
        square = square + column_sum(jnp.sum(total * total, axis=1, keepdims=True))
    small = out_rest[:, 896:1024]
    extra = column_sum(jnp.sum(small * small, axis=1, keepdims=True))
    square = square - jnp.where(place_ref[1] == 0, 0.0, extra)
    out_table[...] = out_rest[:, 512:1024]
    rows = small.shape[0]
    out_small[0:rows] = small
    lane = lax.broadcasted_iota(jnp.int32, (8, 128), 1)
    top = lax.broadcasted_iota(jnp.int32, (8, 128), 0) == 0
    out_small[rows : rows + 8] = scalar_ref[...] + jnp.where(top & (lane == 2), square, 0.0)


def adam_rule(weight, moment, second, gradient, step_rate, decay_rate):
    moment_new = BETA_ONE * moment + (1.0 - BETA_ONE) * gradient
    second_new = BETA_TWO * second + (1.0 - BETA_TWO) * gradient * gradient
    moment_hat = moment_new / (1.0 - BETA_ONE**STEP_NUMBER)
    second_hat = second_new / (1.0 - BETA_TWO**STEP_NUMBER)
    weight_new = weight - step_rate * (
        moment_hat / (jnp.sqrt(second_hat) + EPS_ADAM) + decay_rate * weight
    )
    return (weight_new, moment_new, second_new)


def adam_kernel(*refs):
    place_ref, rest, others, swapped = refs[0:4]
    quarters = refs[4:8]
    params = [refs[8 + 3 * i : 11 + 3 * i] for i in range(9)]
    loss_ref, valid_ref, norm_ref = refs[35:38]
    outs = [refs[38 + 3 * i : 41 + 3 * i] for i in range(9)]
    small_ref = refs[65]
    me, wide = place_ref[0], place_ref[2]
    is_first = place_ref[1] == 0
    rows = rest.shape[0]
    for k in range(4):
        row = pl.multiple_of(((me >> 2) ^ k) * 8, 8)
        small_ref[pl.ds(row, 8), 0:128] = quarters[k][0:8]
        small_ref[pl.ds(row, 8), 128:256] = quarters[k][8:16]
    tops = [quarter[16:17] for quarter in quarters]
    scalars = (tops[0] + tops[1]) + (tops[2] + tops[3])
    small = small_ref[...]
    loss, valid, square = scalars[:, 0:1], scalars[:, 1:2], scalars[:, 2:3]
    square = square + column_sum(jnp.sum(small * small, axis=1, keepdims=True))
    inverse = 1.0 / valid
    norm = jnp.sqrt(square) * inverse
    loss_ref[...], valid_ref[...], norm_ref[...] = loss, valid, norm
    factor = jnp.minimum(1.0, CLIP_AT / (norm + 1e-06)) * inverse
    table, attn, proj, up, bias, down, vectors, head, side = range(9)

    def update(which, index, gradient, step_rate, decay_rate):
        news = adam_rule(
            *(ref[index] for ref in params[which]), factor * gradient, step_rate, decay_rate
        )
        for ref, new in zip(outs[which], news):
            ref[index] = new

    layers = ((rest, others, 1792), (others, others, 512))
    for layer, (attention, feed, at) in enumerate(layers):
        for j in range(3):
            update(attn, (layer, j), attention[:, 128 * j : 128 * j + 128], RATE_MATRIX, DECAY_RATE)
        update(proj, (layer,), attention[:, 384:512], RATE_MATRIX, DECAY_RATE)
        update(up, (layer,), feed[:, at : at + 512], RATE_MATRIX, DECAY_RATE)
        update(down, (layer,), feed[:, at + 512 : at + 1024], RATE_MATRIX, DECAY_RATE)
        for i in range(2):
            low = SMALL_BIAS + 4 * layer + i
            row = jnp.where(is_first, small[low : low + 1], small[low + 2 : low + 3])
            index = (slice(layer, layer + 1), slice(256 * i, 256 * i + 256))
            update(bias, index, row, RATE_VECTOR, 0.0)
    whole = (slice(None), slice(None))
    update(head, whole, others[:, 1536:1792], RATE_MATRIX, DECAY_RATE)
    mine, theirs = rest[:, 512:1024], swapped[:, 0:512]
    low, high = jnp.where(is_first, mine, theirs), jnp.where(is_first, theirs, mine)
    update(table, (slice(None), slice(0, 512)), low, RATE_TABLE, DECAY_RATE)
    update(table, (slice(None), slice(512, 896)), high[:, 0:384], RATE_TABLE, DECAY_RATE)
    update(vectors, whole, small[0:NVEC], RATE_VECTOR, 0.0)
    turned = pltpu.roll(small[SMALL_SIDE : SMALL_SIDE + 8], lax.rem(D - wide * rows, D), 1)
    update(side, whole, turned[0:5, 0:rows], RATE_MATRIX, DECAY_RATE)


def swap(a, axis, distance):
    size = lax.axis_size(axis)
    return lax.ppermute(a, axis, [(i, i ^ distance) for i in range(size)])


def swap_column(piece, n_high):
    return [piece] + [swap(piece, "wide", 4 * k) for k in range(1, n_high)]


def gather_plane(column):
    return [column] + [swap(column, "wide", p) for p in range(1, 4)]


def gather_cores(mine):
    return [swap(a, "narrow", 1) for a in mine]


def in_blocks(parts, wide):
    n_high, rows, cols = parts[0].shape
    if rows == 16:
        return parts
    whole = jnp.stack(parts, axis=1).reshape(4 * n_high, rows, cols)
    whole = whole[wide ^ jnp.arange(4 * n_high)].reshape(4, 4, 16, cols)
    return [whole[:, p] for p in range(4)]


def in_pieces(blocks, wide, n_high):
    cols = blocks.shape[-1]
    if n_high == 4:
        return blocks
    rows = 64 // n_high
    whole = blocks.transpose(1, 0, 2, 3).reshape(4 * n_high, rows, cols)
    whole = whole[wide ^ jnp.arange(4 * n_high)]
    return whole.reshape(n_high, 4, rows, cols).transpose(1, 0, 2, 3)


def add_cores(keep, send, wide, n_high):
    keep, send = in_pieces(keep, wide, n_high), in_pieces(send, wide, n_high)
    received = swap(send, "narrow", 1)
    return [keep[p] + received[p].astype(F32) for p in range(4)]


def swap_plane(sums):
    return [swap(sums[p].astype(BF16), "wide", p) for p in range(1, 4)]


def add_plane(own, received):
    for a in received:
        own = own + a.astype(F32)
    return own


def column_pieces(own):
    return [own[0]] + [swap(own[k].astype(BF16), "wide", 4 * k) for k in range(1, own.shape[0])]


def full_spec(a):
    return pl.BlockSpec(a.shape, lambda *_: (0,) * len(a.shape))


def row_spec(shape):
    return pl.BlockSpec((1,) + shape, lambda i: (i,) + (0,) * len(shape))


def shaped(shape, dtype):
    return jax.ShapeDtypeStruct(shape, dtype)


VMEM_SPEC = pl.BlockSpec(memory_space=pltpu.VMEM)
ANY_SPEC = pl.BlockSpec(memory_space=pl.ANY)
SMEM_SPEC = pl.BlockSpec(memory_space=pltpu.SMEM)


def call(kernel, grid, in_specs, out_specs, out_shape, scratch, flops, bytes_accessed, name):
    extra = {"grid": grid} if grid else {}
    return pl.pallas_call(
        kernel,
        in_specs=in_specs,
        out_specs=out_specs,
        out_shape=out_shape,
        scratch_shapes=scratch,
        compiler_params=pltpu.CompilerParams(vmem_limit_bytes=VMEM_BYTES),
        cost_estimate=pl.CostEstimate(
            flops=flops, bytes_accessed=bytes_accessed, transcendentals=0
        ),
        name=name,
        **extra,
    )


KEPT = (
    ((STEP_SEQS * KEYS, 768), BF16),
    ((HEADS * STEP, KEYS), BF16),
    ((STEP, D), BF16),
    ((STEP, D), F32),
    ((STEP, FF), BF16),
    ((STEP, FF), BF16),
    ((STEP, D), BF16),
    ((STEP, D), BF16),
)
FORWARD_WORK = [
    pltpu.VMEM((HEADS * STEP, D), BF16),
    pltpu.VMEM((STEP_SEQS, HEADS * KEYS, D), BF16),
    pltpu.VMEM((STEP_SEQS, HEADS * 128, 128), F32),
    pltpu.VMEM((STEP_SEQS, HEADS * 128, 256), F32),
    pltpu.VMEM((STEP_SEQS, HEADS * 96, 384), F32),
    pltpu.VMEM((STEP, FF), F32),
    pltpu.VMEM((STEP, D), F32),
]
FF_WORK = pltpu.VMEM((STEP, FF), BF16)
ATTENTION_WORK = [
    pltpu.VMEM((HEADS * STEP, D), BF16),
    pltpu.VMEM((HEADS * STEP, KEYS), BF16),
    pltpu.VMEM((STEP_SEQS * KEYS, 512), F32),
    pltpu.VMEM((STEP, 768), BF16),
]


def per_device(
    tokens,
    actions,
    game_ids,
    valid_steps,
    rewards,
    end_flags,
    embed_table,
    table_first,
    table_second,
    attn_weight,
    attn_first,
    attn_second,
    proj_weight,
    proj_first,
    proj_second,
    up_weight,
    up_first,
    up_second,
    up_bias,
    bias_first,
    bias_second,
    down_weight,
    down_first,
    down_second,
    vectors,
    vectors_first,
    vectors_second,
    head_weight,
    head_first,
    head_second,
    side_weight,
    side_first,
    side_second,
):
    n_high = lax.axis_size("wide") // 4
    wide, core = lax.axis_index("wide"), lax.axis_index("narrow")
    rows = side_weight.shape[0]
    fast = rows == 16
    place = jnp.stack([wide if fast else jnp.zeros_like(wide), core, wide]).astype(jnp.int32)

    def flat(a):
        return jnp.swapaxes(a, -1, -2)

    params = (
        (flat(embed_table), flat(table_first), flat(table_second)),
        (attn_weight, attn_first, attn_second),
        (flat(proj_weight), flat(proj_first), flat(proj_second)),
        (up_weight, up_first, up_second),
        (up_bias, bias_first, bias_second),
        (flat(down_weight), flat(down_first), flat(down_second)),
        (vectors, vectors_first, vectors_second),
        (head_weight, head_first, head_second),
        (flat(side_weight), flat(side_first), flat(side_second)),
    )
    table, attn, proj, up, _, down, _, head, side = (group[0] for group in params)

    piece = call(
        pack_kernel,
        None,
        [SMEM_SPEC] + [VMEM_SPEC] * 7,
        VMEM_SPEC,
        shaped((rows, HALF_FIRST_COLS + HALF_SECOND_COLS), BF16),
        [pltpu.VMEM((rows, 128), F32)],
        10**6,
        10**6,
        "pack",
    )(place, table, attn, proj, up, down, head, side)
    column = swap_column(piece, n_high)

    count = tokens.shape[0] // lax.axis_size("narrow")
    meta = call(
        prepare_kernel,
        None,
        [SMEM_SPEC] * 2 + [VMEM_SPEC] * 5 + [ANY_SPEC],
        VMEM_SPEC,
        shaped((count, SEQ, 128), jnp.int32),
        [pltpu.VMEM((24, FRAMES), jnp.int32)],
        10**6,
        10**6,
        "prepare",
    )(place, game_ids, flat(tokens), actions, valid_steps, rewards, end_flags, piece)
    column, meta = lax.optimization_barrier((column, meta))
    first_mine = gather_plane(jnp.stack([a[:, :HALF_FIRST_COLS] for a in column]))
    second_column = jnp.stack([a[:, HALF_FIRST_COLS:] for a in column])
    second_column, last = lax.optimization_barrier((second_column, first_mine[3]))
    first_mine = first_mine[0:3] + [last]
    first_other = gather_cores(first_mine)
    second_mine = gather_plane(second_column)
    first_parts = in_blocks(first_mine, wide) + in_blocks(first_other, wide)
    other_bias = swap(up_bias, "narrow", 1)

    steps = count // STEP_SEQS
    meta = meta.reshape(steps, STEP, 128)
    kept_specs = [row_spec(shape) for shape, _ in KEPT]
    kept_shapes = [shaped((steps,) + shape, dtype) for shape, dtype in KEPT]
    row_f32 = shaped((steps, STEP, D), F32)
    meta_spec = row_spec((STEP, 128))
    vec_specs = [full_spec(vectors), full_spec(up_bias), full_spec(up_bias)]
    w_spec = pl.BlockSpec((D, COL_FIRST), lambda i: (0, 0))
    side_spec = pl.BlockSpec((D, 128), lambda i: (0, 0))
    hits_spec = row_spec((STEP, ROWS))
    results = call(
        first_forward_kernel,
        (steps,),
        [SMEM_SPEC, meta_spec] + vec_specs + [full_spec(a) for a in first_parts],
        [w_spec, side_spec, row_spec((STEP, D)), hits_spec, row_spec((STEP, D))] + kept_specs,
        [shaped((D, COL_FIRST), BF16), shaped((D, 128), BF16), row_f32]
        + [shaped((steps, STEP, ROWS), BF16), row_f32]
        + kept_shapes,
        [pltpu.VMEM((D, COL_FIRST), BF16)] + FORWARD_WORK,
        4 * 10**9,
        20 * 10**6,
        "first_forward",
    )(place, meta, vectors, up_bias, other_bias, *first_parts)
    w_first, side_copy, stream, hits, stream_first = results[0:5]
    kept = results[5:]
    kept_qkv, kept_p, kept_o, kept_m, kept_h, kept_gp, kept_a, kept_c = kept
    received, side_copy = lax.optimization_barrier((second_mine[1:], side_copy))
    second_mine = second_mine[0:1] + received
    second_other = gather_cores(second_mine)
    second_parts = in_blocks(second_mine, wide) + in_blocks(second_other, wide)

    def blocks(cols):
        return pl.BlockSpec((4, 4, 16, cols), lambda i: (0, 0, 0, 0))

    def block_shapes(cols):
        return [shaped((4, 4, 16, cols), F32), shaped((4, 4, 16, cols), BF16)]

    small_spec = pl.BlockSpec((SMALL_ROWS, 8, D), lambda i: (0, 0, 0))
    small_shape = shaped((SMALL_ROWS, 8, D), F32)
    small_scratch = pltpu.VMEM((SMALL_ROWS, 8, D), F32)
    scalar_spec = pl.BlockSpec((8, 128), lambda i: (0, 0))
    grad_stream, keep_second, send_second, small_grads, scalars = call(
        middle_kernel,
        (steps,),
        [SMEM_SPEC, meta_spec]
        + vec_specs
        + [side_spec, row_spec((STEP, D))]
        + [full_spec(a) for a in second_parts],
        [row_spec((STEP, D))] + [blocks(HALF_SECOND_COLS)] * 2 + [small_spec, scalar_spec],
        [row_f32] + block_shapes(HALF_SECOND_COLS) + [small_shape, shaped((8, 128), F32)],
        [
            pltpu.VMEM((D, COL_SECOND + 128), BF16),
            pltpu.VMEM((D, COL_SECOND + 128), F32),
            small_scratch,
        ]
        + [pltpu.VMEM(shape, dtype) for shape, dtype in KEPT]
        + FORWARD_WORK
        + [FF_WORK]
        + ATTENTION_WORK
        + [
            pltpu.VMEM((STEP, D), F32),
            pltpu.VMEM((STEP, D), BF16),
            pltpu.VMEM((STEP, VOCAB + 128), F32),
            pltpu.VMEM((STEP, VOCAB + 128), BF16),
            pltpu.VMEM((STEP, D), F32),
            pltpu.VMEM((STEP, D), BF16),
            pltpu.VMEM((STEP, D), F32),
            pltpu.VMEM((STEP, D), BF16),
        ],
        15 * 10**9,
        20 * 10**6,
        "middle",
    )(place, meta, vectors, up_bias, other_bias, side_copy, stream, *second_parts)
    second_sums = add_cores(keep_second, send_second, wide, n_high)

    kept_ff = (kept_m, kept_h, kept_gp, kept_c)
    grad_mid, keep_ff, send_ff, small_grads = call(
        ff_backward_kernel,
        (steps,),
        [SMEM_SPEC, full_spec(vectors), w_spec, row_spec((STEP, D)), small_spec]
        + [row_spec(a.shape[1:]) for a in kept_ff],
        [row_spec((STEP, D))] + [blocks(HALF_GRAD_COLS)] * 2 + [small_spec],
        [row_f32] + block_shapes(HALF_GRAD_COLS) + [small_shape],
        [
            pltpu.VMEM((D, 2048), F32),
            small_scratch,
            pltpu.VMEM((STEP, D), BF16),
            pltpu.VMEM((STEP, FF), F32),
            pltpu.VMEM((STEP, D), F32),
            FF_WORK,
        ],
        4 * 10**9,
        10 * 10**6,
        "ff_backward",
    )(place, vectors, w_first, grad_stream, small_grads, *kept_ff)
    ff_sums = add_cores(keep_ff, send_ff, wide, n_high)
    other_sums = [jnp.concatenate(pair, axis=-1) for pair in zip(second_sums, ff_sums)]
    others_received = swap_plane(other_sums)

    kept_attention = (stream_first, kept_qkv, kept_p, kept_o, kept_a)
    keep_rest, send_rest, small_grads = call(
        attention_backward_kernel,
        (steps,),
        [SMEM_SPEC, full_spec(vectors), w_spec, row_spec((STEP, D)), hits_spec, small_spec]
        + [row_spec(a.shape[1:]) for a in kept_attention]
        + [ANY_SPEC],
        [blocks(HALF_GRAD_COLS)] * 2 + [pl.BlockSpec((SMALL_ROWS, D), lambda i: (0, 0))],
        block_shapes(HALF_GRAD_COLS) + [shaped((SMALL_ROWS, D), F32)],
        [
            pltpu.VMEM((D, 2048), F32),
            small_scratch,
            pltpu.VMEM((STEP, D), BF16),
            pltpu.VMEM((STEP, D), BF16),
        ]
        + FORWARD_WORK[0:5]
        + [pltpu.VMEM((STEP, D), F32)]
        + ATTENTION_WORK,
        6 * 10**9,
        20 * 10**6,
        "attention_backward",
    )(place, vectors, w_first, grad_mid, hits, small_grads, *kept_attention, other_sums[0])
    others_received, keep_rest = lax.optimization_barrier((others_received, keep_rest))
    rest_sums = add_cores(keep_rest, send_rest, wide, n_high)
    rest_received = swap_plane(rest_sums)
    other_pieces = column_pieces(add_plane(other_sums[0], others_received))
    rest_pieces = column_pieces(add_plane(rest_sums[0], rest_received))

    grad_rest, grad_others, table_part, small = call(
        finish_kernel,
        None,
        [SMEM_SPEC] + [VMEM_SPEC] * (2 * n_high + 1),
        [VMEM_SPEC] * 4,
        [
            shaped((rows, HALF_GRAD_COLS), F32),
            shaped((rows, HALF_GRAD_COLS + HALF_SECOND_COLS), F32),
            shaped((rows, 512), F32),
            shaped((rows + 8, 128), F32),
        ],
        [],
        10**6,
        10**6,
        "finish",
    )(place, *rest_pieces, *other_pieces, scalars)

    if fast:
        is_small = (jnp.arange(rows + 8) < rows)[:, None]
        beside = swap(small, "narrow", 1)
        small = jnp.where(is_small, jnp.where(core == 1, small, beside), small + beside)
        plane = [small] + [swap(small, "wide", p) for p in range(1, 4)]
        chosen = jnp.where(
            wide & 2 == 0,
            jnp.where(wide & 1 == 0, plane[0], plane[1]),
            jnp.where(wide & 1 == 0, plane[2], plane[3]),
        )
        small = jnp.where(is_small, chosen, (plane[0] + plane[1]) + (plane[2] + plane[3]))
        quarters = [small] + [swap(small, "wide", 4 * k) for k in range(1, 4)]
    else:
        sums = lax.psum(small[rows:], ("wide", "narrow"))
        total = lax.psum(small_grads, ("wide", "narrow"))
        total = total.reshape(4, 8, 2, 128).transpose(0, 2, 1, 3).reshape(4, 16, 128)
        ends = [sums] + [jnp.zeros_like(sums)] * 3
        quarters = [jnp.concatenate(pair) for pair in zip(total, ends)]
    swapped = swap(table_part, "narrow", 1)

    flat_params = [a for group in params for a in group]
    results = call(
        adam_kernel,
        None,
        [SMEM_SPEC] + [VMEM_SPEC] * 34,
        [VMEM_SPEC] * 30,
        [shaped((1, 1), F32)] * 3 + [shaped(a.shape, F32) for a in flat_params],
        [pltpu.VMEM((SMALL_ROWS, D), F32)],
        10**6,
        10**6,
        "adam",
    )(place, grad_rest, grad_others, swapped, *quarters, *flat_params)
    news = list(results[3:])
    for group in (0, 2, 5, 8):
        for member in range(3 * group, 3 * group + 3):
            news[member] = flat(news[member])
    return tuple(a.reshape(()) for a in results[0:3]) + tuple(news)


def solution(mesh):
    placed = (
        P("wide", None, None),
        P("wide", None),
        P("wide"),
        P("wide", None),
        P("wide", None),
        P("wide", None),
        P(None, "wide"),
        P(None, "wide"),
        P(None, "wide"),
        P(None, None, "wide", "narrow"),
        P(None, None, "wide", "narrow"),
        P(None, None, "wide", "narrow"),
        P(None, "narrow", "wide"),
        P(None, "narrow", "wide"),
        P(None, "narrow", "wide"),
        P(None, "wide", "narrow"),
        P(None, "wide", "narrow"),
        P(None, "wide", "narrow"),
        P(None, "narrow"),
        P(None, "narrow"),
        P(None, "narrow"),
        P(None, "narrow", "wide"),
        P(None, "narrow", "wide"),
        P(None, "narrow", "wide"),
        P(),
        P(),
        P(),
        P("wide", "narrow"),
        P("wide", "narrow"),
        P("wide", "narrow"),
        P("wide", None),
        P("wide", None),
        P("wide", None),
    )
    return jax.shard_map(
        per_device,
        mesh=mesh,
        in_specs=placed,
        out_specs=(P(), P(), P()) + placed[6:],
        check_vma=False,
    )
```

```python
import functools

import jax
import jax.numpy as jnp
from jax import lax
from jax.experimental import pallas as pl
from jax.experimental.pallas import tpu as pltpu
from jax.sharding import PartitionSpec as P

D = 256
HEADS = 4
HEAD_DIM = 64
FF = 1024
VOCAB = 512
ACTIONS = 18
GAMES = 26
OBS = 16
FRAMES = 20
STEP_NUMBER = 5
FRAME_TOKENS = 17
LENGTH = 340
ROWS = 896
NVEC = 14

EPS_NORM = 1e-05
BETA_ONE = 0.5
BETA_TWO = 0.5
RATE_TABLE = 0.5
RATE_MATRIX = 0.05
RATE_VECTOR = 0.2
DECAY_RATE = 0.01
EPS_ADAM = 1e-08
CLIP_AT = 0.1

SEQ = 352
KEYS = 384
STEP_SEQS = 2
STEP = STEP_SEQS * SEQ
TILE = 64
QBLOCKS = ((0, 128, 128), (128, 128, 256), (256, 96, 384))

COL_QKV, COL_PROJ, COL_UP, COL_DOWN, COL_LAYER = 0, 768, 1024, 2048, 3072
HALF_ATTENTION = ((0, 128, 0), (128, 128, 256), (256, 128, 512), (384, 128, COL_PROJ))
HALF_LAYER = HALF_ATTENTION + ((512, 512, COL_UP), (1024, 512, COL_DOWN))
COL_TABLE, COL_SMALL, COL_FIRST = 3072, 3968, 4096
HALF_FIRST = HALF_LAYER + ((1536, 512, COL_TABLE),)
HALF_FIRST_COLS = 2048
COL_HEAD, COL_SECOND = 3072, 3584
HALF_SECOND = HALF_LAYER + ((1536, 256, COL_HEAD),)
HALF_SECOND_COLS = 1792
GRAD_UP, GRAD_DOWN = 0, 1024
HALF_GRAD_FF = ((0, 512, GRAD_UP), (512, 512, GRAD_DOWN))
GRAD_TABLE, GRAD_SMALL = 1024, 1920
HALF_GRAD_REST = HALF_ATTENTION + ((512, 512, GRAD_TABLE),)
HALF_GRAD_COLS = 1024
SMALL_ROWS, SMALL_BIAS, SMALL_SIDE = 32, 14, 22

F32, BF16 = jnp.float32, jnp.bfloat16
VMEM_BYTES = 60 * 1024 * 1024


def dot_nn(a, b):
    return lax.dot_general(a, b, (((1,), (0,)), ((), ())), preferred_element_type=F32)


def dot_nt(a, b):
    return lax.dot_general(a, b, (((1,), (1,)), ((), ())), preferred_element_type=F32)


def dot_tn(a, b):
    return lax.dot_general(a, b, (((0,), (0,)), ((), ())), preferred_element_type=F32)


def over(count, size, body):
    def step(i, _):
        body(pl.ds(pl.multiple_of(i * size, size), size))
        return 0

    lax.fori_loop(0, count // size, step, 0)


def over_adding(count, size, body, sums):
    def step(i, totals):
        parts = body(pl.ds(pl.multiple_of(i * size, size), size))
        return tuple(total + fold(part) for total, part in zip(totals, parts))

    return lax.fori_loop(0, count // size, step, (jnp.zeros((8, D), F32),) * sums)


def normalise(x):
    centred = x - jnp.mean(x, axis=1, keepdims=True)
    scale = lax.rsqrt(jnp.mean(centred * centred, axis=1, keepdims=True) + EPS_NORM)
    return centred * scale, scale


def normalise_back(grad, xhat, scale, gain):
    inner = grad * gain
    mean_one = jnp.mean(inner, axis=1, keepdims=True)
    mean_two = jnp.mean(inner * xhat, axis=1, keepdims=True)
    return scale * (inner - mean_one - xhat * mean_two)


def column_sum(a):
    return jnp.sum(a, axis=0, keepdims=True)


def fold(a):
    return jnp.sum(a.reshape(a.shape[0] // 8, 8, a.shape[1]), axis=0)


def assemble(pieces_mine, pieces_other, place_ref, w_ref, halves):
    me, core = place_ref[0], place_ref[1]
    is_first = core == 0
    for p in range(4):

        def block(z, _, p=p):
            row = pl.multiple_of((me ^ (4 * z + p)) * 16, 16)
            for src, width, dest in halves:
                mine = pieces_mine[p][z, :, src : src + width]
                other = pieces_other[p][z, :, src : src + width]
                if dest == COL_QKV:
                    mine, other = mine * 0.125, other * 0.125
                w_ref[pl.ds(row, 16), dest : dest + width] = jnp.where(is_first, mine, other)
                w_ref[pl.ds(row, 16), dest + width : dest + 2 * width] = jnp.where(
                    is_first, other, mine
                )
            return 0

        lax.fori_loop(0, 4, block, 0)


def disperse(g_ref, place_ref, keep_ref, send_ref, halves, scaled=True):
    me, core = place_ref[0], place_ref[1]
    is_first = core == 0

    def block(i, _):
        p, z = i >> 2, i & 3
        row = pl.multiple_of((me ^ (4 * z + p)) * 16, 16)
        for src, width, dest in halves:
            low = g_ref[pl.ds(row, 16), dest : dest + width]
            high = g_ref[pl.ds(row, 16), dest + width : dest + 2 * width]
            if scaled and dest == COL_QKV:
                low, high = low * 0.125, high * 0.125
            keep_ref[p, z, :, src : src + width] = jnp.where(is_first, low, high)
            send_ref[p, z, :, src : src + width] = jnp.where(is_first, high, low).astype(BF16)
        return 0

    lax.fori_loop(0, 16, block, 0)


def make_hits(meta_ref, hits_ref):
    def tile(i, _):
        rows = pl.ds(pl.multiple_of(i * 32, 32), 32)
        first = lax.rem(i, SEQ // 32) * 32 + (VOCAB + ACTIONS + GAMES)
        lane = lax.broadcasted_iota(jnp.int32, (32, ROWS), 1)
        place = lax.broadcasted_iota(jnp.int32, (32, 1), 0) + first
        meta = meta_ref[rows]
        hit = (lane == meta[:, 0:1]) | (lane == meta[:, 1:2]) | (lane == place)
        hits_ref[rows] = jnp.where(hit, 1.0, 0.0).astype(BF16)
        return 0

    lax.fori_loop(0, STEP // 32, tile, 0)


def lower_norm(x_ref, gain, offset, out_ref):
    def tile(rows):
        out_ref[rows] = (normalise(x_ref[rows])[0] * gain + offset).astype(BF16)

    over(STEP, TILE, tile)


def split_queries(source_ref, source_row, target_ref, target_row):
    for first, count, _ in QBLOCKS:
        for h in range(HEADS):
            lanes = slice(h * HEAD_DIM, (h + 1) * HEAD_DIM)
            target = pl.ds(target_row + HEADS * first + h * count, count)
            target_ref[target, lanes] = source_ref[pl.ds(source_row + first, count), lanes]


def split_keys(source_ref, source_row, column, target_ref):
    for h in range(HEADS):
        lanes = slice(h * HEAD_DIM, (h + 1) * HEAD_DIM)
        source = slice(column + h * HEAD_DIM, column + (h + 1) * HEAD_DIM)
        target_ref[h * KEYS : (h + 1) * KEYS, lanes] = source_ref[pl.ds(source_row, KEYS), source]


def over_sequences(body):
    def step(s, _):
        body(
            pl.multiple_of(s * SEQ, 32),
            pl.multiple_of(s * KEYS, 128),
            pl.multiple_of(s * (HEADS * SEQ), 128),
        )
        return 0

    lax.fori_loop(0, STEP_SEQS, step, 0)


def sum_heads(p_ref, base, count, seen, kv_ref):
    return dot_nn(
        jnp.concatenate(
            [p_ref[pl.ds(base + h * count, count), 0:seen] for h in range(HEADS)], axis=1
        ),
        jnp.concatenate([kv_ref[h * KEYS : h * KEYS + seen] for h in range(HEADS)], axis=0),
    )


def layer_forward(x_ref, w_ref, vec, bias_ref, kept, work):
    qkv_ref, p_ref, o_ref, m_ref, h_ref, gp_ref, a_ref, c_ref = kept
    qs_ref, kv_ref, score_refs, u_ref, y_ref = work
    lower_norm(x_ref, vec[0:1], vec[1:2], a_ref)

    def project(cols):
        qkv = dot_nn(a_ref[...], w_ref[:, cols]).astype(BF16)
        for s in range(STEP_SEQS):
            qkv_ref[s * KEYS : s * KEYS + SEQ, cols] = qkv[s * SEQ : (s + 1) * SEQ]

    over(768, 256, project)
    for s in range(STEP_SEQS):
        qkv_ref[s * KEYS + SEQ : (s + 1) * KEYS] = jnp.zeros((KEYS - SEQ, 768), BF16)

    def attend(row, key, base):
        split_queries(qkv_ref, key, qs_ref, base)
        split_keys(qkv_ref, key, 512, kv_ref)
        for (first, count, seen), s_ref in zip(QBLOCKS, score_refs):
            block = base + HEADS * first
            s_ref[...] = dot_nt(
                qs_ref[pl.ds(block, HEADS * count)], qkv_ref[pl.ds(key, seen), 256:512]
            )

            def soften(h, _):
                rows = pl.ds(pl.multiple_of(h * count, 32), count)
                line = lax.broadcasted_iota(jnp.int32, (count, 128), 0)
                causal = line >= lax.broadcasted_iota(jnp.int32, (count, 128), 1)
                scores = jnp.where(causal, s_ref[rows, seen - 128 :], -1e30)
                if seen > 128:
                    scores = jnp.concatenate([s_ref[rows, : seen - 128], scores], axis=1)
                expanded = jnp.exp(scores - jnp.max(scores, axis=1, keepdims=True))
                probs = expanded * (1.0 / jnp.sum(expanded, axis=1, keepdims=True))
                p_ref[pl.ds(block + rows.start, count), 0:seen] = probs.astype(BF16)
                return 0

            lax.fori_loop(0, HEADS, soften, 0)
            out = sum_heads(p_ref, block, count, seen, kv_ref)
            o_ref[pl.ds(row + first, count)] = out.astype(BF16)

    over_sequences(attend)
    y_ref[...] = dot_nt(o_ref[...], w_ref[:, COL_PROJ : COL_PROJ + 256])

    def middle_tile(rows):
        middle = x_ref[rows] + (y_ref[rows] + vec[2:3])
        m_ref[rows] = middle
        c_ref[rows] = (normalise(middle)[0] * vec[3:4] + vec[4:5]).astype(BF16)

    over(STEP, TILE, middle_tile)

    def up_columns(cols):
        w_cols = pl.ds(pl.multiple_of(COL_UP + cols.start, 256), 256)
        u_ref[:, cols] = dot_nn(c_ref[...], w_ref[:, w_cols])

    over(FF, 256, up_columns)

    def gelu_tile(rows):
        for chunk in range(4):
            cols = slice(256 * chunk, 256 * chunk + 256)
            up = u_ref[rows, cols] + bias_ref[:, cols]
            square = up * up
            bent = jnp.tanh(up * (0.7978845608028654 + 0.0356774081363 * square))
            half = 0.5 + 0.5 * bent
            hidden = up * half
            slope = 0.7978845608028654 + 0.1070322244089 * square
            gp_ref[rows, cols] = (half + hidden * (1.0 - bent) * slope).astype(BF16)
            h_ref[rows, cols] = hidden.astype(BF16)

    over(STEP, 32, gelu_tile)
    y_ref[...] = dot_nt(h_ref[...], w_ref[:, COL_DOWN : COL_DOWN + FF])


def add_gradient(g_ref, column, left_ref, right_ref):
    g_ref[:, column : column + right_ref.shape[1]] += dot_tn(left_ref[...], right_ref[...])


def ff_backward(grad_ref, grad16_ref, w_ref, vec, kept, g_ref, g_up, g_down, v_ref, v_row, bias_row, work, mid_ref, mid16_ref):
    m_ref, h_ref, gp_ref, c_ref = kept
    u_ref, y_ref, du_ref = work

    def columns(i, _):
        cols = pl.ds(pl.multiple_of(i * 256, 256), 256)
        w_cols = pl.ds(pl.multiple_of(COL_DOWN + i * 256, 256), 256)
        u_ref[:, cols] = dot_nn(grad16_ref[...], w_ref[:, w_cols])

        def tile(rows):
            grad_up = u_ref[rows, cols] * gp_ref[rows, cols].astype(F32)
            du_ref[rows, cols] = grad_up.astype(BF16)
            return (grad_up,)

        v_ref[bias_row + i] += over_adding(STEP, TILE, tile, 1)[0]
        return 0

    lax.fori_loop(0, 4, columns, 0)
    add_gradient(g_ref, g_down, grad16_ref, h_ref)
    add_gradient(g_ref, g_up, c_ref, du_ref)
    y_ref[...] = dot_nt(du_ref[...], w_ref[:, COL_UP : COL_UP + FF])

    def tile(rows):
        xhat, scale = normalise(m_ref[rows])
        grad = y_ref[rows]
        mid = grad_ref[rows] + normalise_back(grad, xhat, scale, vec[3:4])
        mid_ref[rows] = mid
        if mid16_ref is not None:
            mid16_ref[rows] = mid.astype(BF16)
        return mid, grad * xhat, grad

    for i, total in enumerate(over_adding(STEP, TILE, tile, 3)):
        v_ref[v_row + 2 + i] += total


def attention_backward(mid_ref, mid16_ref, w_ref, vec, kept, g_ref, v_ref, v_row, work, out_ref, out16_ref):
    x_ref, qkv_ref, p_ref, o_ref, a_ref = kept
    qs_ref, kv_ref, dos_ref, ds_ref, dkv_ref, dqkv_ref, score_refs, y_ref = work
    add_gradient(g_ref, COL_PROJ, mid16_ref, o_ref)
    dqkv_ref[:, 0:256] = dot_nn(mid16_ref[...], w_ref[:, COL_PROJ : COL_PROJ + 256]).astype(BF16)

    def attend(row, key, base):
        split_queries(dqkv_ref, row, dos_ref, base)
        split_keys(qkv_ref, key, 256, kv_ref)
        dkv_ref[...] = jnp.zeros(dkv_ref.shape, F32)
        for (first, count, seen), s_ref in zip(QBLOCKS, score_refs):
            block = base + HEADS * first
            whole = pl.ds(block, HEADS * count)
            s_ref[...] = dot_nt(dos_ref[whole], qkv_ref[pl.ds(key, seen), 512:768])

            def scores_back(h, _):
                rows = pl.ds(pl.multiple_of(h * count, 32), count)
                here = pl.ds(block + rows.start, count)
                probs, grad = p_ref[here, 0:seen].astype(F32), s_ref[rows]
                inner = jnp.sum(probs * grad, axis=1, keepdims=True)
                ds_ref[here, 0:seen] = (probs * (grad - inner)).astype(BF16)
                return 0

            lax.fori_loop(0, HEADS, scores_back, 0)
            grad_query = sum_heads(ds_ref, block, count, seen, kv_ref)
            dqkv_ref[pl.ds(row + first, count), 0:256] = grad_query.astype(BF16)
            dkv_ref[0:seen, 0:256] += dot_tn(ds_ref[whole, 0:seen], qs_ref[whole])
            dkv_ref[0:seen, 256:512] += dot_tn(p_ref[whole, 0:seen], dos_ref[whole])

        def store(rows):
            dqkv_ref[pl.ds(row + rows.start, 32), 256:768] = dkv_ref[rows].astype(BF16)

        over(SEQ, 32, store)

    over_sequences(attend)
    add_gradient(g_ref, COL_QKV, a_ref, dqkv_ref)
    y_ref[...] = dot_nt(dqkv_ref[...], w_ref[:, COL_QKV : COL_QKV + 768])

    def tile(rows):
        xhat, scale = normalise(x_ref[rows])
        grad = y_ref[rows]
        out = mid_ref[rows] + normalise_back(grad, xhat, scale, vec[0:1])
        if out_ref is not None:
            out_ref[rows] = out
        if out16_ref is not None:
            out16_ref[rows] = out.astype(BF16)
        return grad * xhat, grad

    for i, total in enumerate(over_adding(STEP, TILE, tile, 2)):
        v_ref[v_row + i] += total


def set_bias(place_ref, mine, other, bias_ref):
    is_first = place_ref[1] == 0
    bias_ref[:, 0:512] = jnp.where(is_first, mine, other)
    bias_ref[:, 512:1024] = jnp.where(is_first, other, mine)


def prepare_kernel(place_ref, games_ref, tokens, actions, valid, rewards, ends, after, out, x_ref):
    count = out.shape[0]
    frames = tokens.shape[2]
    base = place_ref[1] * count
    row = lax.broadcasted_iota(jnp.int32, (SEQ, frames), 0)
    start = lax.broadcasted_iota(jnp.int32, (SEQ, frames), 1) * FRAME_TOKENS
    here = jnp.where((row >= start) & (row < start + FRAME_TOKENS), 1.0, 0.0).astype(BF16)
    coming = jnp.where((row >= start - FRAME_TOKENS) & (row < start), 1.0, 0.0).astype(BF16)
    passed = jnp.sum(jnp.where(row >= start + FRAME_TOKENS, 1, 0), axis=1, keepdims=True)
    place = lax.broadcasted_iota(jnp.int32, (SEQ, 1), 0)
    spot = place - passed * FRAME_TOKENS
    lane = lax.broadcasted_iota(jnp.int32, (SEQ, 24), 1)
    wide_lane = lax.broadcasted_iota(jnp.int32, (SEQ, 128), 1)
    inside = place < LENGTH
    x_ref[...] = jnp.zeros(x_ref.shape, jnp.int32)
    for s in range(count):
        x_ref[0:OBS] = tokens[base + s]
        x_ref[16:17] = actions[pl.ds(base + s, 1)] + VOCAB
        x_ref[17:18] = valid[pl.ds(base + s, 1)]
        x_ref[18:19] = rewards[pl.ds(base + s, 1)]
        x_ref[19:20] = ends[pl.ds(base + s, 1)] + 3
        high = (x_ref[...] >> 4).astype(F32).astype(BF16)
        low = (x_ref[...] & 15).astype(F32).astype(BF16)
        now = dot_nt(here, high) * 16.0 + dot_nt(here, low)
        soon = dot_nt(coming, high) * 16.0 + dot_nt(coming, low)

        def pick(condition, a):
            return jnp.sum(jnp.where(condition, a, 0.0), axis=1, keepdims=True).astype(jnp.int32)

        ids = jnp.where(inside, pick(lane == spot, now), -1)
        game = jnp.where(inside, games_ref[base + s] + (VOCAB + ACTIONS), -1)
        target = pick((lane == spot + 1) & (spot < 15), now)
        target = target + pick((lane == 0) & (spot == 16), soon)
        weight = pick((lane == 17) & (spot < 15), now) + pick((lane == 17) & (spot == 16), soon)
        side = pick((lane == 17) & (spot == 16), now)
        reward, end = pick(lane == 18, now), pick(lane == 19, now)
        result = jnp.zeros((SEQ, 128), jnp.int32)
        for c, column in enumerate((ids, game, target, weight, side, reward, end)):
            result = jnp.where(wide_lane == c, column, result)
        out[s] = result


def first_forward_kernel(*refs):
    place_ref, meta_ref, vec_ref, bias_ref, bias_other = refs[0:5]
    mine, other = refs[5:9], refs[9:13]
    w_out, side_out, next_ref, hits_ref, x_ref = refs[13:18]
    kept = [ref.at[0] for ref in refs[18:26]]
    w_ref, bias_row, qs_ref, kv_ref, s0, s1, s2, u_ref, y_ref = refs[26:35]

    @pl.when(pl.program_id(0) == 0)
    def _():
        assemble(mine, other, place_ref, w_ref, HALF_FIRST)
        w_out[...] = w_ref[...]
        side_out[...] = w_ref[:, COL_SMALL:]
        set_bias(place_ref, bias_ref[0:1], bias_other[0:1], bias_row)
        qs_ref[...] = jnp.zeros(qs_ref.shape, BF16)
        kv_ref[...] = jnp.zeros(kv_ref.shape, BF16)

    make_hits(meta_ref.at[0], hits_ref.at[0])
    x_ref[0] = dot_nt(hits_ref[0], w_ref[:, COL_TABLE : COL_TABLE + ROWS])
    vec = vec_ref[0:6]
    layer_forward(x_ref.at[0], w_ref, vec, bias_row, kept, (qs_ref, kv_ref, (s0, s1, s2), u_ref, y_ref))
    m_ref = kept[3]

    def tile(rows):
        next_ref[0, rows] = m_ref[rows] + (y_ref[rows] + vec[5:6])

    over(STEP, TILE, tile)


def codebook_losses(logits, meta):
    weight = meta[:, 3:4].astype(F32)
    peak = jnp.max(logits, axis=1, keepdims=True)
    expanded = jnp.exp(logits - peak)
    total = jnp.sum(expanded, axis=1, keepdims=True)
    hit = lax.broadcasted_iota(jnp.int32, logits.shape, 1) == meta[:, 2:3]
    picked = jnp.sum(jnp.where(hit, logits, 0.0), axis=1, keepdims=True)
    loss = weight * (peak + jnp.log(total) - picked)
    return loss, expanded * (weight / total) - jnp.where(hit, weight, 0.0)


def side_losses(side, meta):
    lane = lax.broadcasted_iota(jnp.int32, side.shape, 1)
    is_reward, is_end = lane < 3, (lane == 3) | (lane == 4)
    is_side = lane < 5
    weight = meta[:, 4:5].astype(F32)
    reward_peak = jnp.max(jnp.where(is_reward, side, -1e30), axis=1, keepdims=True)
    end_peak = jnp.max(jnp.where(is_end, side, -1e30), axis=1, keepdims=True)
    shifted = jnp.where(is_side, side - jnp.where(is_reward, reward_peak, end_peak), 0.0)
    expanded = jnp.where(is_side, jnp.exp(shifted), 0.0)
    reward_total = jnp.sum(jnp.where(is_reward, expanded, 0.0), axis=1, keepdims=True)
    end_total = jnp.sum(jnp.where(is_end, expanded, 0.0), axis=1, keepdims=True)
    hit = (lane == meta[:, 5:6]) | (lane == meta[:, 6:7])
    picked = jnp.sum(jnp.where(hit, side, 0.0), axis=1, keepdims=True)
    terms = reward_peak + jnp.log(reward_total) + end_peak + jnp.log(end_total) - picked
    grad = expanded * jnp.where(is_reward, weight / reward_total, weight / end_total)
    return weight * terms, grad - jnp.where(hit, weight, 0.0), weight


def middle_kernel(*refs):
    place_ref, meta_ref, vec_ref, bias_ref, bias_other, side_ref, in_ref = refs[0:7]
    mine, other = refs[7:11], refs[11:15]
    grad_ref, keep_ref, send_ref, v_out, scalar_ref = refs[15:20]
    w_ref, g_ref, v_ref, bias_row = refs[20:24]
    kept = refs[24:32]
    qkv_ref, p_ref, o_ref, m_ref, h_ref, gp_ref, a_ref, c_ref = kept
    qs_ref, kv_ref, s0, s1, s2, u_ref, y_ref = refs[32:39]
    du_ref, dos_ref, ds_ref, dkv_ref, dqkv_ref = refs[39:44]
    last_ref, final_ref, logit_ref, dlogit_ref, up_ref, up16_ref, mid_ref, mid16_ref = refs[44:52]
    scores = (s0, s1, s2)
    step = pl.program_id(0)

    @pl.when(step == 0)
    def _():
        assemble(mine, other, place_ref, w_ref, HALF_SECOND)
        w_ref[:, COL_SECOND:] = side_ref[...]
        set_bias(place_ref, bias_ref[1:2], bias_other[1:2], bias_row)
        g_ref[...] = jnp.zeros(g_ref.shape, F32)
        v_ref[...] = jnp.zeros(v_ref.shape, F32)
        scalar_ref[...] = jnp.zeros(scalar_ref.shape, F32)
        for ref in (qs_ref, kv_ref, dos_ref):
            ref[...] = jnp.zeros(ref.shape, BF16)

    x_ref = in_ref.at[0]
    vec = vec_ref[6:12]
    layer_forward(x_ref, w_ref, vec, bias_row, kept, (qs_ref, kv_ref, scores, u_ref, y_ref))

    gain, offset = vec_ref[12:13], vec_ref[13:14]

    def last_tile(rows):
        last = m_ref[rows] + (y_ref[rows] + vec[5:6])
        last_ref[rows] = last
        final_ref[rows] = (normalise(last)[0] * gain + offset).astype(BF16)

    over(STEP, TILE, last_tile)

    def head_columns(cols):
        w_cols = pl.ds(pl.multiple_of(COL_HEAD + cols.start, 128), 128)
        logit_ref[:, cols] = dot_nn(final_ref[...], w_ref[:, w_cols])

    over(VOCAB + 128, 128, head_columns)

    def loss_tile(i, carry):
        loss, valid = carry
        rows = pl.ds(pl.multiple_of(i * 32, 32), 32)
        meta = meta_ref[0, rows]
        token_loss, grad = codebook_losses(logit_ref[rows, :VOCAB], meta)
        dlogit_ref[rows, :VOCAB] = grad.astype(BF16)
        side_loss, grad, weight = side_losses(logit_ref[rows, VOCAB:], meta)
        dlogit_ref[rows, VOCAB:] = grad.astype(BF16)
        return loss + token_loss + side_loss, valid + weight

    nothing = jnp.zeros((32, 1), F32)
    loss, valid = lax.fori_loop(0, STEP // 32, loss_tile, (nothing, nothing))
    scalar_lane = lax.broadcasted_iota(jnp.int32, (8, 128), 1)
    scalar_row = lax.broadcasted_iota(jnp.int32, (8, 128), 0) == 0
    scalar_ref[...] += jnp.where(scalar_row & (scalar_lane == 0), column_sum(loss), 0.0)
    scalar_ref[...] += jnp.where(scalar_row & (scalar_lane == 1), column_sum(valid), 0.0)
    add_gradient(g_ref, COL_HEAD, final_ref, dlogit_ref)
    y_ref[...] = dot_nt(dlogit_ref[...], w_ref[:, COL_HEAD : COL_HEAD + VOCAB + 128])

    def up_tile(rows):
        xhat, scale = normalise(last_ref[rows])
        grad = y_ref[rows]
        up = normalise_back(grad, xhat, scale, gain)
        up_ref[rows] = up
        up16_ref[rows] = up.astype(BF16)
        return up, grad * xhat, grad

    for i, total in enumerate(over_adding(STEP, TILE, up_tile, 3)):
        v_ref[11 + i] += total
    ff_backward(
        up_ref,
        up16_ref,
        w_ref,
        vec,
        (m_ref, h_ref, gp_ref, c_ref),
        g_ref,
        COL_UP,
        COL_DOWN,
        v_ref,
        6,
        SMALL_BIAS + 4,
        (u_ref, y_ref, du_ref),
        mid_ref,
        mid16_ref,
    )
    attention_backward(
        mid_ref,
        mid16_ref,
        w_ref,
        vec,
        (x_ref, qkv_ref, p_ref, o_ref, a_ref),
        g_ref,
        v_ref,
        6,
        (qs_ref, kv_ref, dos_ref, ds_ref, dkv_ref, dqkv_ref, scores, y_ref),
        grad_ref.at[0],
        None,
    )

    @pl.when(step == pl.num_programs(0) - 1)
    def _():
        disperse(g_ref, place_ref, keep_ref, send_ref, HALF_SECOND)
        side = jnp.transpose(g_ref[:, COL_SECOND:])
        for i in range(5):
            v_ref[SMALL_SIDE + i, 0:1] = side[i : i + 1]
        v_out[...] = v_ref[...]


def ff_backward_kernel(*refs):
    place_ref, vec_ref, w_ref, grad_ref, v_in = refs[0:5]
    kept = [ref.at[0] for ref in refs[5:9]]
    mid_ref, keep_ref, send_ref, v_out = refs[9:13]
    g_ref, v_ref, grad16_ref, u_ref, y_ref, du_ref = refs[13:19]
    step = pl.program_id(0)

    @pl.when(step == 0)
    def _():
        g_ref[...] = jnp.zeros(g_ref.shape, F32)
        v_ref[...] = v_in[...]

    def tile(rows):
        grad = grad_ref[0, rows]
        grad16_ref[rows] = grad.astype(BF16)
        return (grad,)

    v_ref[5] += over_adding(STEP, TILE, tile, 1)[0]
    ff_backward(
        grad_ref.at[0],
        grad16_ref,
        w_ref,
        vec_ref[0:6],
        kept,
        g_ref,
        GRAD_UP,
        GRAD_DOWN,
        v_ref,
        0,
        SMALL_BIAS,
        (u_ref, y_ref, du_ref),
        mid_ref.at[0],
        None,
    )

    @pl.when(step == pl.num_programs(0) - 1)
    def _():
        disperse(g_ref, place_ref, keep_ref, send_ref, HALF_GRAD_FF, False)
        v_out[...] = v_ref[...]


def attention_backward_kernel(*refs):
    place_ref, vec_ref, w_ref, mid_ref, hits_ref, v_in = refs[0:6]
    kept = [ref.at[0] for ref in refs[6:11]]
    keep_ref, send_ref, v_out = refs[12:15]
    g_ref, v_ref, mid16_ref, out16_ref = refs[15:19]
    qs_ref, kv_ref, s0, s1, s2, y_ref = refs[19:25]
    dos_ref, ds_ref, dkv_ref, dqkv_ref = refs[25:29]
    qkv_ref = kept[1]
    step = pl.program_id(0)

    @pl.when(step == 0)
    def _():
        g_ref[...] = jnp.zeros(g_ref.shape, F32)
        v_ref[...] = v_in[...]
        for ref in (qs_ref, kv_ref, dos_ref):
            ref[...] = jnp.zeros(ref.shape, BF16)

    over_sequences(lambda row, key, base: split_queries(qkv_ref, key, qs_ref, base))

    def tile(rows):
        mid16_ref[rows] = mid_ref[0, rows].astype(BF16)

    over(STEP, TILE, tile)
    attention_backward(
        mid_ref.at[0],
        mid16_ref,
        w_ref,
        vec_ref[0:6],
        kept,
        g_ref,
        v_ref,
        0,
        (qs_ref, kv_ref, dos_ref, ds_ref, dkv_ref, dqkv_ref, (s0, s1, s2), y_ref),
        None,
        out16_ref,
    )
    add_gradient(g_ref, GRAD_TABLE, out16_ref, hits_ref.at[0])

    @pl.when(step == pl.num_programs(0) - 1)
    def _():
        small = jnp.sum(v_ref[...], axis=1)
        v_out[...] = small
        for block in range(16):
            quarter = small[8 * (block // 4) : 8 * (block // 4) + 8]
            g_ref[16 * block : 16 * block + 8, GRAD_SMALL:] = quarter[:, 0:128]
            g_ref[16 * block + 8 : 16 * block + 16, GRAD_SMALL:] = quarter[:, 128:256]
        disperse(g_ref, place_ref, keep_ref, send_ref, HALF_GRAD_REST)


def pack_layer(attn, proj, up, down, layer, out, at):
    for j in range(3):
        out[:, at + 128 * j : at + 128 * j + 128] = attn[layer, j].astype(BF16)
    out[:, at + 384 : at + 512] = proj[layer].astype(BF16)
    out[:, at + 512 : at + 1024] = up[layer].astype(BF16)
    out[:, at + 1024 : at + 1536] = down[layer].astype(BF16)


def pack_kernel(place_ref, table, attn, proj, up, down, head, side, out, pad_ref):
    pack_layer(attn, proj, up, down, 0, out, 0)
    pack_layer(attn, proj, up, down, 1, out, HALF_FIRST_COLS)
    out[:, HALF_FIRST_COLS + 1536 :] = head[...].astype(BF16)
    rows = side.shape[1]
    eye = (
        lax.broadcasted_iota(jnp.int32, (rows, rows), 0)
        == lax.broadcasted_iota(jnp.int32, (rows, rows), 1)
    )
    eye = jnp.where(eye, 1.0, 0.0).astype(BF16)
    pad_ref[...] = jnp.zeros(pad_ref.shape, F32)
    pad_ref[:, 0:5] = dot_nt(eye, side[...].astype(BF16))
    high = jnp.concatenate([table[:, 512:896], pad_ref[...]], axis=1)
    out[:, 1536:2048] = jnp.where(place_ref[1] == 0, table[:, 0:512], high).astype(BF16)


def finish_kernel(*refs):
    count = (len(refs) - 6) // 2
    place_ref = refs[0]
    scalar_ref = refs[2 * count + 1]
    out_rest, out_other, out_table, out_small = refs[2 * count + 2 :]
    square = jnp.zeros((1, 1), F32)
    for pieces, out in ((refs[1 : count + 1], out_rest), (refs[count + 1 : 2 * count + 1], out_other)):
        total = pieces[0][...]
        for piece in pieces[1:]:
            total = total + piece[...].astype(F32)
        out[...] = total
        square = square + column_sum(jnp.sum(total * total, axis=1, keepdims=True))
    small = out_rest[:, 896:1024]
    extra = column_sum(jnp.sum(small * small, axis=1, keepdims=True))
    square = square - jnp.where(place_ref[1] == 0, 0.0, extra)
    out_table[...] = out_rest[:, 512:1024]
    rows = small.shape[0]
    out_small[0:rows] = small
    lane = lax.broadcasted_iota(jnp.int32, (8, 128), 1)
    top = lax.broadcasted_iota(jnp.int32, (8, 128), 0) == 0
    out_small[rows : rows + 8] = scalar_ref[...] + jnp.where(top & (lane == 2), square, 0.0)


def adam_rule(weight, moment, second, gradient, step_rate, decay_rate):
    moment_new = BETA_ONE * moment + (1.0 - BETA_ONE) * gradient
    second_new = BETA_TWO * second + (1.0 - BETA_TWO) * gradient * gradient
    moment_hat = moment_new / (1.0 - BETA_ONE**STEP_NUMBER)
    second_hat = second_new / (1.0 - BETA_TWO**STEP_NUMBER)
    weight_new = weight - step_rate * (
        moment_hat / (jnp.sqrt(second_hat) + EPS_ADAM) + decay_rate * weight
    )
    return (weight_new, moment_new, second_new)


def adam_kernel(*refs):
    place_ref, rest, others, swapped = refs[0:4]
    quarters = refs[4:8]
    params = [refs[8 + 3 * i : 11 + 3 * i] for i in range(9)]
    loss_ref, valid_ref, norm_ref = refs[35:38]
    outs = [refs[38 + 3 * i : 41 + 3 * i] for i in range(9)]
    small_ref = refs[65]
    me, wide = place_ref[0], place_ref[2]
    is_first = place_ref[1] == 0
    rows = rest.shape[0]
    for k in range(4):
        row = pl.multiple_of(((me >> 2) ^ k) * 8, 8)
        small_ref[pl.ds(row, 8), 0:128] = quarters[k][0:8]
        small_ref[pl.ds(row, 8), 128:256] = quarters[k][8:16]
    tops = [quarter[16:17] for quarter in quarters]
    scalars = (tops[0] + tops[1]) + (tops[2] + tops[3])
    small = small_ref[...]
    loss, valid, square = scalars[:, 0:1], scalars[:, 1:2], scalars[:, 2:3]
    square = square + column_sum(jnp.sum(small * small, axis=1, keepdims=True))
    inverse = 1.0 / valid
    norm = jnp.sqrt(square) * inverse
    loss_ref[...], valid_ref[...], norm_ref[...] = loss, valid, norm
    factor = jnp.minimum(1.0, CLIP_AT / (norm + 1e-06)) * inverse
    table, attn, proj, up, bias, down, vectors, head, side = range(9)

    def update(which, index, gradient, step_rate, decay_rate):
        news = adam_rule(
            *(ref[index] for ref in params[which]), factor * gradient, step_rate, decay_rate
        )
        for ref, new in zip(outs[which], news):
            ref[index] = new

    layers = ((rest, others, 1792), (others, others, 512))
    for layer, (attention, feed, at) in enumerate(layers):
        for j in range(3):
            update(attn, (layer, j), attention[:, 128 * j : 128 * j + 128], RATE_MATRIX, DECAY_RATE)
        update(proj, (layer,), attention[:, 384:512], RATE_MATRIX, DECAY_RATE)
        update(up, (layer,), feed[:, at : at + 512], RATE_MATRIX, DECAY_RATE)
        update(down, (layer,), feed[:, at + 512 : at + 1024], RATE_MATRIX, DECAY_RATE)
        for i in range(2):
            low = SMALL_BIAS + 4 * layer + i
            row = jnp.where(is_first, small[low : low + 1], small[low + 2 : low + 3])
            index = (slice(layer, layer + 1), slice(256 * i, 256 * i + 256))
            update(bias, index, row, RATE_VECTOR, 0.0)
    whole = (slice(None), slice(None))
    update(head, whole, others[:, 1536:1792], RATE_MATRIX, DECAY_RATE)
    mine, theirs = rest[:, 512:1024], swapped[:, 0:512]
    low, high = jnp.where(is_first, mine, theirs), jnp.where(is_first, theirs, mine)
    update(table, (slice(None), slice(0, 512)), low, RATE_TABLE, DECAY_RATE)
    update(table, (slice(None), slice(512, 896)), high[:, 0:384], RATE_TABLE, DECAY_RATE)
    update(vectors, whole, small[0:NVEC], RATE_VECTOR, 0.0)
    turned = pltpu.roll(small[SMALL_SIDE : SMALL_SIDE + 8], lax.rem(D - wide * rows, D), 1)
    update(side, whole, turned[0:5, 0:rows], RATE_MATRIX, DECAY_RATE)


def swap(a, axis, distance):
    size = lax.axis_size(axis)
    return lax.ppermute(a, axis, [(i, i ^ distance) for i in range(size)])


def swap_column(piece, n_high):
    return [piece] + [swap(piece, "wide", 4 * k) for k in range(1, n_high)]


def gather_plane(column):
    return [column] + [swap(column, "wide", p) for p in range(1, 4)]


def gather_cores(mine):
    return [swap(a, "narrow", 1) for a in mine]


def in_blocks(parts, wide):
    n_high, rows, cols = parts[0].shape
    if rows == 16:
        return parts
    whole = jnp.stack(parts, axis=1).reshape(4 * n_high, rows, cols)
    whole = whole[wide ^ jnp.arange(4 * n_high)].reshape(4, 4, 16, cols)
    return [whole[:, p] for p in range(4)]


def in_pieces(blocks, wide, n_high):
    cols = blocks.shape[-1]
    if n_high == 4:
        return blocks
    rows = 64 // n_high
    whole = blocks.transpose(1, 0, 2, 3).reshape(4 * n_high, rows, cols)
    whole = whole[wide ^ jnp.arange(4 * n_high)]
    return whole.reshape(n_high, 4, rows, cols).transpose(1, 0, 2, 3)


def add_cores(keep, send, wide, n_high):
    keep, send = in_pieces(keep, wide, n_high), in_pieces(send, wide, n_high)
    received = swap(send, "narrow", 1)
    return [keep[p] + received[p].astype(F32) for p in range(4)]


def swap_plane(sums):
    return [swap(sums[p].astype(BF16), "wide", p) for p in range(1, 4)]


def add_plane(own, received):
    for a in received:
        own = own + a.astype(F32)
    return own


def column_pieces(own):
    return [own[0]] + [swap(own[k].astype(BF16), "wide", 4 * k) for k in range(1, own.shape[0])]


def full_spec(a):
    return pl.BlockSpec(a.shape, lambda *_: (0,) * len(a.shape))


def row_spec(shape):
    return pl.BlockSpec((1,) + shape, lambda i: (i,) + (0,) * len(shape))


def shaped(shape, dtype):
    return jax.ShapeDtypeStruct(shape, dtype)


VMEM_SPEC = pl.BlockSpec(memory_space=pltpu.VMEM)
ANY_SPEC = pl.BlockSpec(memory_space=pl.ANY)
SMEM_SPEC = pl.BlockSpec(memory_space=pltpu.SMEM)


def call(kernel, grid, in_specs, out_specs, out_shape, scratch, flops, bytes_accessed, name):
    extra = {"grid": grid} if grid else {}
    return pl.pallas_call(
        kernel,
        in_specs=in_specs,
        out_specs=out_specs,
        out_shape=out_shape,
        scratch_shapes=scratch,
        compiler_params=pltpu.CompilerParams(vmem_limit_bytes=VMEM_BYTES),
        cost_estimate=pl.CostEstimate(
            flops=flops, bytes_accessed=bytes_accessed, transcendentals=0
        ),
        name=name,
        **extra,
    )


KEPT = (
    ((STEP_SEQS * KEYS, 768), BF16),
    ((HEADS * STEP, KEYS), BF16),
    ((STEP, D), BF16),
    ((STEP, D), F32),
    ((STEP, FF), BF16),
    ((STEP, FF), BF16),
    ((STEP, D), BF16),
    ((STEP, D), BF16),
)
FORWARD_WORK = [
    pltpu.VMEM((HEADS * STEP, D), BF16),
    pltpu.VMEM((HEADS * KEYS, D), BF16),
    pltpu.VMEM((HEADS * 128, 128), F32),
    pltpu.VMEM((HEADS * 128, 256), F32),
    pltpu.VMEM((HEADS * 96, 384), F32),
    pltpu.VMEM((STEP, FF), F32),
    pltpu.VMEM((STEP, D), F32),
]
FF_WORK = pltpu.VMEM((STEP, FF), BF16)
BIAS_WORK = pltpu.VMEM((1, FF), F32)
ATTENTION_WORK = [
    pltpu.VMEM((HEADS * STEP, D), BF16),
    pltpu.VMEM((HEADS * STEP, KEYS), BF16),
    pltpu.VMEM((KEYS, 512), F32),
    pltpu.VMEM((STEP, 768), BF16),
]


def per_device(
    tokens,
    actions,
    game_ids,
    valid_steps,
    rewards,
    end_flags,
    embed_table,
    table_first,
    table_second,
    attn_weight,
    attn_first,
    attn_second,
    proj_weight,
    proj_first,
    proj_second,
    up_weight,
    up_first,
    up_second,
    up_bias,
    bias_first,
    bias_second,
    down_weight,
    down_first,
    down_second,
    vectors,
    vectors_first,
    vectors_second,
    head_weight,
    head_first,
    head_second,
    side_weight,
    side_first,
    side_second,
):
    n_high = lax.axis_size("wide") // 4
    wide, core = lax.axis_index("wide"), lax.axis_index("narrow")
    rows = side_weight.shape[0]
    fast = rows == 16
    place = jnp.stack([wide if fast else jnp.zeros_like(wide), core, wide]).astype(jnp.int32)

    def flat(a):
        return jnp.swapaxes(a, -1, -2)

    params = (
        (flat(embed_table), flat(table_first), flat(table_second)),
        (attn_weight, attn_first, attn_second),
        (flat(proj_weight), flat(proj_first), flat(proj_second)),
        (up_weight, up_first, up_second),
        (up_bias, bias_first, bias_second),
        (flat(down_weight), flat(down_first), flat(down_second)),
        (vectors, vectors_first, vectors_second),
        (head_weight, head_first, head_second),
        (flat(side_weight), flat(side_first), flat(side_second)),
    )
    table, attn, proj, up, _, down, _, head, side = (group[0] for group in params)

    piece = call(
        pack_kernel,
        None,
        [SMEM_SPEC] + [VMEM_SPEC] * 7,
        VMEM_SPEC,
        shaped((rows, HALF_FIRST_COLS + HALF_SECOND_COLS), BF16),
        [pltpu.VMEM((rows, 128), F32)],
        10**6,
        10**6,
        "pack",
    )(place, table, attn, proj, up, down, head, side)
    column = swap_column(piece, n_high)

    count = tokens.shape[0] // lax.axis_size("narrow")
    meta = call(
        prepare_kernel,
        None,
        [SMEM_SPEC] * 2 + [VMEM_SPEC] * 5 + [ANY_SPEC],
        VMEM_SPEC,
        shaped((count, SEQ, 128), jnp.int32),
        [pltpu.VMEM((24, FRAMES), jnp.int32)],
        10**6,
        10**6,
        "prepare",
    )(place, game_ids, flat(tokens), actions, valid_steps, rewards, end_flags, piece)
    column, meta = lax.optimization_barrier((column, meta))
    first_mine = gather_plane(jnp.stack([a[:, :HALF_FIRST_COLS] for a in column]))
    second_column = jnp.stack([a[:, HALF_FIRST_COLS:] for a in column])
    second_column, last = lax.optimization_barrier((second_column, first_mine[3]))
    first_mine = first_mine[0:3] + [last]
    first_other = gather_cores(first_mine)
    second_mine = gather_plane(second_column)
    first_parts = in_blocks(first_mine, wide) + in_blocks(first_other, wide)
    other_bias = swap(up_bias, "narrow", 1)

    steps = count // STEP_SEQS
    meta = meta.reshape(steps, STEP, 128)
    kept_specs = [row_spec(shape) for shape, _ in KEPT]
    kept_shapes = [shaped((steps,) + shape, dtype) for shape, dtype in KEPT]
    row_f32 = shaped((steps, STEP, D), F32)
    meta_spec = row_spec((STEP, 128))
    vec_specs = [full_spec(vectors), full_spec(up_bias), full_spec(up_bias)]
    w_spec = pl.BlockSpec((D, COL_FIRST), lambda i: (0, 0))
    side_spec = pl.BlockSpec((D, 128), lambda i: (0, 0))
    hits_spec = row_spec((STEP, ROWS))
    results = call(
        first_forward_kernel,
        (steps,),
        [SMEM_SPEC, meta_spec] + vec_specs + [full_spec(a) for a in first_parts],
        [w_spec, side_spec, row_spec((STEP, D)), hits_spec, row_spec((STEP, D))] + kept_specs,
        [shaped((D, COL_FIRST), BF16), shaped((D, 128), BF16), row_f32]
        + [shaped((steps, STEP, ROWS), BF16), row_f32]
        + kept_shapes,
        [pltpu.VMEM((D, COL_FIRST), BF16), BIAS_WORK] + FORWARD_WORK,
        4 * 10**9,
        20 * 10**6,
        "first_forward",
    )(place, meta, vectors, up_bias, other_bias, *first_parts)
    w_first, side_copy, stream, hits, stream_first = results[0:5]
    kept = results[5:]
    kept_qkv, kept_p, kept_o, kept_m, kept_h, kept_gp, kept_a, kept_c = kept
    received, side_copy = lax.optimization_barrier((second_mine[1:], side_copy))
    second_mine = second_mine[0:1] + received
    second_other = gather_cores(second_mine)
    second_parts = in_blocks(second_mine, wide) + in_blocks(second_other, wide)

    def blocks(cols):
        return pl.BlockSpec((4, 4, 16, cols), lambda i: (0, 0, 0, 0))

    def block_shapes(cols):
        return [shaped((4, 4, 16, cols), F32), shaped((4, 4, 16, cols), BF16)]

    small_spec = pl.BlockSpec((SMALL_ROWS, 8, D), lambda i: (0, 0, 0))
    small_shape = shaped((SMALL_ROWS, 8, D), F32)
    small_scratch = pltpu.VMEM((SMALL_ROWS, 8, D), F32)
    scalar_spec = pl.BlockSpec((8, 128), lambda i: (0, 0))
    grad_stream, keep_second, send_second, small_grads, scalars = call(
        middle_kernel,
        (steps,),
        [SMEM_SPEC, meta_spec]
        + vec_specs
        + [side_spec, row_spec((STEP, D))]
        + [full_spec(a) for a in second_parts],
        [row_spec((STEP, D))] + [blocks(HALF_SECOND_COLS)] * 2 + [small_spec, scalar_spec],
        [row_f32] + block_shapes(HALF_SECOND_COLS) + [small_shape, shaped((8, 128), F32)],
        [
            pltpu.VMEM((D, COL_SECOND + 128), BF16),
            pltpu.VMEM((D, COL_SECOND + 128), F32),
            small_scratch,
            BIAS_WORK,
        ]
        + [pltpu.VMEM(shape, dtype) for shape, dtype in KEPT]
        + FORWARD_WORK
        + [FF_WORK]
        + ATTENTION_WORK
        + [
            pltpu.VMEM((STEP, D), F32),
            pltpu.VMEM((STEP, D), BF16),
            pltpu.VMEM((STEP, VOCAB + 128), F32),
            pltpu.VMEM((STEP, VOCAB + 128), BF16),
            pltpu.VMEM((STEP, D), F32),
            pltpu.VMEM((STEP, D), BF16),
            pltpu.VMEM((STEP, D), F32),
            pltpu.VMEM((STEP, D), BF16),
        ],
        15 * 10**9,
        20 * 10**6,
        "middle",
    )(place, meta, vectors, up_bias, other_bias, side_copy, stream, *second_parts)
    second_sums = add_cores(keep_second, send_second, wide, n_high)

    kept_ff = (kept_m, kept_h, kept_gp, kept_c)
    grad_mid, keep_ff, send_ff, small_grads = call(
        ff_backward_kernel,
        (steps,),
        [SMEM_SPEC, full_spec(vectors), w_spec, row_spec((STEP, D)), small_spec]
        + [row_spec(a.shape[1:]) for a in kept_ff],
        [row_spec((STEP, D))] + [blocks(HALF_GRAD_COLS)] * 2 + [small_spec],
        [row_f32] + block_shapes(HALF_GRAD_COLS) + [small_shape],
        [
            pltpu.VMEM((D, 2048), F32),
            small_scratch,
            pltpu.VMEM((STEP, D), BF16),
            pltpu.VMEM((STEP, FF), F32),
            pltpu.VMEM((STEP, D), F32),
            FF_WORK,
        ],
        4 * 10**9,
        10 * 10**6,
        "ff_backward",
    )(place, vectors, w_first, grad_stream, small_grads, *kept_ff)
    ff_sums = add_cores(keep_ff, send_ff, wide, n_high)
    other_sums = [jnp.concatenate(pair, axis=-1) for pair in zip(second_sums, ff_sums)]
    others_received = swap_plane(other_sums)

    kept_attention = (stream_first, kept_qkv, kept_p, kept_o, kept_a)
    keep_rest, send_rest, small_grads = call(
        attention_backward_kernel,
        (steps,),
        [SMEM_SPEC, full_spec(vectors), w_spec, row_spec((STEP, D)), hits_spec, small_spec]
        + [row_spec(a.shape[1:]) for a in kept_attention]
        + [ANY_SPEC],
        [blocks(HALF_GRAD_COLS)] * 2 + [pl.BlockSpec((SMALL_ROWS, D), lambda i: (0, 0))],
        block_shapes(HALF_GRAD_COLS) + [shaped((SMALL_ROWS, D), F32)],
        [
            pltpu.VMEM((D, 2048), F32),
            small_scratch,
            pltpu.VMEM((STEP, D), BF16),
            pltpu.VMEM((STEP, D), BF16),
        ]
        + FORWARD_WORK[0:5]
        + [pltpu.VMEM((STEP, D), F32)]
        + ATTENTION_WORK,
        6 * 10**9,
        20 * 10**6,
        "attention_backward",
    )(place, vectors, w_first, grad_mid, hits, small_grads, *kept_attention, other_sums[0])
    others_received, keep_rest = lax.optimization_barrier((others_received, keep_rest))
    rest_sums = add_cores(keep_rest, send_rest, wide, n_high)
    rest_received = swap_plane(rest_sums)
    other_pieces = column_pieces(add_plane(other_sums[0], others_received))
    rest_pieces = column_pieces(add_plane(rest_sums[0], rest_received))

    grad_rest, grad_others, table_part, small = call(
        finish_kernel,
        None,
        [SMEM_SPEC] + [VMEM_SPEC] * (2 * n_high + 1),
        [VMEM_SPEC] * 4,
        [
            shaped((rows, HALF_GRAD_COLS), F32),
            shaped((rows, HALF_GRAD_COLS + HALF_SECOND_COLS), F32),
            shaped((rows, 512), F32),
            shaped((rows + 8, 128), F32),
        ],
        [],
        10**6,
        10**6,
        "finish",
    )(place, *rest_pieces, *other_pieces, scalars)

    if fast:
        is_small = (jnp.arange(rows + 8) < rows)[:, None]
        beside = swap(small, "narrow", 1)
        small = jnp.where(is_small, jnp.where(core == 1, small, beside), small + beside)
        plane = [small] + [swap(small, "wide", p) for p in range(1, 4)]
        chosen = jnp.where(
            wide & 2 == 0,
            jnp.where(wide & 1 == 0, plane[0], plane[1]),
            jnp.where(wide & 1 == 0, plane[2], plane[3]),
        )
        small = jnp.where(is_small, chosen, (plane[0] + plane[1]) + (plane[2] + plane[3]))
        quarters = [small] + [swap(small, "wide", 4 * k) for k in range(1, 4)]
    else:
        sums = lax.psum(small[rows:], ("wide", "narrow"))
        total = lax.psum(small_grads, ("wide", "narrow"))
        total = total.reshape(4, 8, 2, 128).transpose(0, 2, 1, 3).reshape(4, 16, 128)
        ends = [sums] + [jnp.zeros_like(sums)] * 3
        quarters = [jnp.concatenate(pair) for pair in zip(total, ends)]
    swapped = swap(table_part, "narrow", 1)

    flat_params = [a for group in params for a in group]
    results = call(
        adam_kernel,
        None,
        [SMEM_SPEC] + [VMEM_SPEC] * 34,
        [VMEM_SPEC] * 30,
        [shaped((1, 1), F32)] * 3 + [shaped(a.shape, F32) for a in flat_params],
        [pltpu.VMEM((SMALL_ROWS, D), F32)],
        10**6,
        10**6,
        "adam",
    )(place, grad_rest, grad_others, swapped, *quarters, *flat_params)
    news = list(results[3:])
    for group in (0, 2, 5, 8):
        for member in range(3 * group, 3 * group + 3):
            news[member] = flat(news[member])
    return tuple(a.reshape(()) for a in results[0:3]) + tuple(news)


def solution(mesh):
    placed = (
        P("wide", None, None),
        P("wide", None),
        P("wide"),
        P("wide", None),
        P("wide", None),
        P("wide", None),
        P(None, "wide"),
        P(None, "wide"),
        P(None, "wide"),
        P(None, None, "wide", "narrow"),
        P(None, None, "wide", "narrow"),
        P(None, None, "wide", "narrow"),
        P(None, "narrow", "wide"),
        P(None, "narrow", "wide"),
        P(None, "narrow", "wide"),
        P(None, "wide", "narrow"),
        P(None, "wide", "narrow"),
        P(None, "wide", "narrow"),
        P(None, "narrow"),
        P(None, "narrow"),
        P(None, "narrow"),
        P(None, "narrow", "wide"),
        P(None, "narrow", "wide"),
        P(None, "narrow", "wide"),
        P(),
        P(),
        P(),
        P("wide", "narrow"),
        P("wide", "narrow"),
        P("wide", "narrow"),
        P("wide", None),
        P("wide", None),
        P("wide", None),
    )
    return jax.shard_map(
        per_device,
        mesh=mesh,
        in_specs=placed,
        out_specs=(P(), P(), P()) + placed[6:],
        check_vma=False,
    )
```

```python
import functools

import jax
import jax.numpy as jnp
from jax import lax
from jax.experimental import pallas as pl
from jax.experimental.pallas import tpu as pltpu
from jax.sharding import PartitionSpec as P

D = 256
HEADS = 4
HEAD_DIM = 64
FF = 1024
VOCAB = 512
ACTIONS = 18
GAMES = 26
OBS = 16
FRAMES = 20
STEP_NUMBER = 5
FRAME_TOKENS = 17
LENGTH = 340
ROWS = 896
NVEC = 14

EPS_NORM = 1e-05
BETA_ONE = 0.5
BETA_TWO = 0.5
RATE_TABLE = 0.5
RATE_MATRIX = 0.05
RATE_VECTOR = 0.2
DECAY_RATE = 0.01
EPS_ADAM = 1e-08
CLIP_AT = 0.1

SEQ = 352
KEYS = 384
BLOCK, BLOCKS = 128, 3
TILE = 32
SIDE_ROWS = 32
QUERIES = HEADS * BLOCK
VALUE_ROWS = 80

COL_QKV, COL_PROJ, COL_UP, COL_DOWN, COL_LAYER = 0, 768, 1024, 2048, 3072
HALF_ATTENTION = ((0, 128, 0), (128, 128, 256), (256, 128, 512), (384, 128, COL_PROJ))
HALF_LAYER = HALF_ATTENTION + ((512, 512, COL_UP), (1024, 512, COL_DOWN))
COL_TABLE, COL_SMALL, COL_FIRST = 3072, 3968, 4096
HALF_FIRST = HALF_LAYER + ((1536, 512, COL_TABLE),)
HALF_FIRST_COLS = 2048
COL_HEAD, COL_SECOND = 3072, 3584
HALF_SECOND = HALF_LAYER + ((1536, 256, COL_HEAD),)
HALF_SECOND_COLS = 1792
GRAD_UP, GRAD_DOWN = 0, 1024
HALF_GRAD_FF = ((0, 512, GRAD_UP), (512, 512, GRAD_DOWN))
GRAD_TABLE, GRAD_SMALL = 1024, 1920
HALF_GRAD_REST = HALF_ATTENTION + ((512, 512, GRAD_TABLE),)
HALF_GRAD_COLS = 1024
SMALL_ROWS, SMALL_BIAS, SMALL_SIDE = 32, 14, 22

F32, BF16 = jnp.float32, jnp.bfloat16
VMEM_BYTES = 60 * 1024 * 1024


def dot_nn(a, b):
    return lax.dot_general(a, b, (((1,), (0,)), ((), ())), preferred_element_type=F32)


def dot_nt(a, b):
    return lax.dot_general(a, b, (((1,), (1,)), ((), ())), preferred_element_type=F32)


def dot_tn(a, b):
    return lax.dot_general(a, b, (((0,), (0,)), ((), ())), preferred_element_type=F32)


def tiles(rows, size):
    return [slice(first, first + size) for first in range(0, rows, size)]


def normalise(x):
    centred = x - jnp.mean(x, axis=1, keepdims=True)
    scale = lax.rsqrt(jnp.mean(centred * centred, axis=1, keepdims=True) + EPS_NORM)
    return centred * scale, scale


def normalise_back(grad, xhat, scale, gain):
    inner = grad * gain
    mean_one = jnp.mean(inner, axis=1, keepdims=True)
    mean_two = jnp.mean(inner * xhat, axis=1, keepdims=True)
    return scale * (inner - mean_one - xhat * mean_two)


def column_sum(a):
    return jnp.sum(a, axis=0, keepdims=True)


def fold(a):
    return jnp.sum(a.reshape(a.shape[0] // 8, 8, a.shape[1]), axis=0)


def plus(total, a):
    return a if total is None else total + a


def block_lanes(i, h=None):
    if h is None:
        return slice(QUERIES * i, QUERIES * (i + 1))
    return slice(QUERIES * i + BLOCK * h, QUERIES * i + BLOCK * (h + 1))


def head_rows(h):
    return slice(HEAD_DIM * h, HEAD_DIM * (h + 1))


def spread_heads(source, target_ref):
    for h in range(HEADS):
        for i in range(BLOCKS):
            target_ref[head_rows(h), block_lanes(i, h)] = source[
                head_rows(h), BLOCK * i : BLOCK * (i + 1)
            ]


def causal_mask():
    key = lax.broadcasted_iota(jnp.int32, (BLOCK, QUERIES), 0)
    query = lax.broadcasted_iota(jnp.int32, (BLOCK, QUERIES), 1) & (BLOCK - 1)
    return jnp.where(key <= query, 0.0, -1e30)


def assemble(pieces_mine, pieces_other, place_ref, w_ref, halves):
    me, core = place_ref[0], place_ref[1]
    is_first = core == 0
    for p in range(4):

        def block(z, _, p=p):
            row = pl.multiple_of((me ^ (4 * z + p)) * 16, 16)
            for src, width, dest in halves:
                mine = pieces_mine[p][z, :, src : src + width]
                other = pieces_other[p][z, :, src : src + width]
                if dest == COL_QKV:
                    mine, other = mine * 0.125, other * 0.125
                w_ref[pl.ds(row, 16), dest : dest + width] = jnp.where(is_first, mine, other)
                w_ref[pl.ds(row, 16), dest + width : dest + 2 * width] = jnp.where(
                    is_first, other, mine
                )
            return 0

        lax.fori_loop(0, 4, block, 0)


def disperse(g_ref, place_ref, keep_ref, send_ref, halves, scaled=True):
    is_first = place_ref[1] == 0

    def block(i, _):
        p, z = i >> 2, i & 3
        row = pl.multiple_of((4 * z + p) * 16, 16)
        for src, width, dest in halves:
            low = g_ref[pl.ds(row, 16), dest : dest + width]
            high = g_ref[pl.ds(row, 16), dest + width : dest + 2 * width]
            if scaled and dest == COL_QKV:
                low, high = low * 0.125, high * 0.125
            keep_ref[p, z, :, src : src + width] = jnp.where(is_first, low, high)
            send_ref[p, z, :, src : src + width] = jnp.where(is_first, high, low).astype(BF16)
        return 0

    lax.fori_loop(0, 16, block, 0)


def make_hits(meta_ref, hits_ref):
    for rows in tiles(SEQ, TILE):
        lane = lax.broadcasted_iota(jnp.int32, (TILE, ROWS), 1)
        place = lax.broadcasted_iota(jnp.int32, (TILE, 1), 0) + (VOCAB + ACTIONS + GAMES + rows.start)
        meta = meta_ref[rows]
        hit = (lane == meta[:, 0:1]) | (lane == meta[:, 1:2]) | (lane == place)
        hits_ref[rows] = jnp.where(hit, 1.0, 0.0).astype(BF16)


def gelu_and_slope(up):
    up = up.astype(BF16)
    square = up * up
    half = jax.nn.sigmoid(up * (BF16(1.5957691216057308) + BF16(0.0713548162726) * square))
    hidden = up * half
    slope = BF16(1.5957691216057308) + BF16(0.2140644488178) * square
    return hidden, half + hidden * (BF16(1.0) - half) * slope


def layer_forward(x_ref, w_ref, vec, bias, kept, work):
    qt_ref, kv_ref, pt_ref, r_ref, ot_ref, o_ref, m_ref, h_ref, gp_ref, a_ref, c_ref = kept
    qst_ref, vt_ref, mask_ref, wqt_ref, u_ref, y_ref = work
    for rows in tiles(SEQ, TILE):
        a_ref[rows] = (normalise(x_ref[rows])[0] * vec[0:1] + vec[1:2]).astype(BF16)
    a_ref[SEQ:KEYS] = jnp.zeros((KEYS - SEQ, D), BF16)
    kv_ref[0:SEQ] = dot_nn(a_ref[0:SEQ], w_ref[:, 256:768]).astype(BF16)
    kv_ref[SEQ:KEYS] = jnp.zeros((KEYS - SEQ, 512), BF16)
    qt_ref[...] = dot_nt(wqt_ref[...], a_ref[...]).astype(BF16)
    spread_heads(qt_ref, qst_ref)
    turned = jnp.transpose(kv_ref[:, 256:512])
    for h in range(HEADS):
        vt_ref[VALUE_ROWS * h : VALUE_ROWS * h + HEAD_DIM] = turned[head_rows(h)]
    for i in range(BLOCKS):
        seen, first = BLOCK * (i + 1), BLOCK * i
        lanes = block_lanes(i)
        scores = dot_nn(kv_ref[0:seen, 0:256], qst_ref[:, lanes])
        last = scores[first:] + mask_ref[...]
        peak = jnp.max(last, axis=0, keepdims=True)
        if i:
            peak = jnp.maximum(peak, jnp.max(scores[0:first], axis=0, keepdims=True))
            pt_ref[0:first, lanes] = jnp.exp(scores[0:first] - peak).astype(BF16)
        pt_ref[first:seen, lanes] = jnp.exp(last - peak).astype(BF16)
        for h in range(HEADS):
            values = vt_ref[VALUE_ROWS * h : VALUE_ROWS * (h + 1), 0:seen]
            out = dot_nn(values, pt_ref[0:seen, block_lanes(i, h)])
            inverse = 1.0 / out[HEAD_DIM : HEAD_DIM + 1]
            r_ref[h : h + 1, first:seen] = inverse
            ot_ref[head_rows(h), first:seen] = (out[0:HEAD_DIM] * inverse).astype(BF16)
    o_ref[...] = jnp.transpose(ot_ref[...])[0:SEQ]
    y_ref[...] = dot_nt(o_ref[...], w_ref[:, COL_PROJ : COL_PROJ + 256])
    for rows in tiles(SEQ, TILE):
        middle = x_ref[rows] + (y_ref[rows] + vec[2:3])
        m_ref[rows] = middle
        c_ref[rows] = (normalise(middle)[0] * vec[3:4] + vec[4:5]).astype(BF16)
    u_ref[...] = dot_nn(c_ref[...], w_ref[:, COL_UP : COL_UP + FF])
    for rows in tiles(SEQ, TILE):
        for first in range(0, FF, 256):
            cols = slice(first, first + 256)
            h_ref[rows, cols], gp_ref[rows, cols] = gelu_and_slope(u_ref[rows, cols] + bias[:, cols])
    y_ref[...] = dot_nt(h_ref[...], w_ref[:, COL_DOWN : COL_DOWN + FF])


def add_gradient(g_ref, column, left, right):
    g_ref[:, column : column + right.shape[1]] += dot_tn(left, right)


def ff_backward(grad_ref, grad16_ref, w_ref, vec, kept, g_ref, g_up, g_down, v_ref, v_row, bias_row, work, mid_ref, mid16_ref):
    m_ref, h_ref, gp_ref, c_ref = kept
    du_ref, ones_ref, u_ref, y_ref = work
    u_ref[...] = dot_nn(grad16_ref[...], w_ref[:, COL_DOWN : COL_DOWN + FF])
    for rows in tiles(SEQ, TILE):
        du_ref[rows] = u_ref[rows].astype(BF16) * gp_ref[rows]
    add_gradient(g_ref, g_down, grad16_ref[...], h_ref[...])
    add_gradient(g_ref, g_up, c_ref[...], du_ref[...])
    bias_grad = dot_nn(ones_ref[...], du_ref[...])
    for chunk in range(4):
        v_ref[bias_row + chunk, 0:1] += bias_grad[0:1, 256 * chunk : 256 * chunk + 256]
    y_ref[...] = dot_nt(du_ref[...], w_ref[:, COL_UP : COL_UP + FF])
    totals = [None] * 3
    for rows in tiles(SEQ, TILE):
        xhat, scale = normalise(m_ref[rows])
        grad = y_ref[rows]
        mid = grad_ref[rows] + normalise_back(grad, xhat, scale, vec[3:4])
        mid_ref[rows] = mid
        if mid16_ref is not None:
            mid16_ref[rows] = mid.astype(BF16)
        for i, a in enumerate((mid, grad * xhat, grad)):
            totals[i] = plus(totals[i], fold(a))
    for i in range(3):
        v_ref[v_row + 2 + i] += totals[i]


def attention_backward(mid_ref, mid16_ref, w_ref, vec, kept, g_ref, v_ref, v_row, work, out_ref):
    x_ref, qt_ref, kv_ref, pt_ref, r_ref, ot_ref, o_ref, a_ref = kept
    dost_ref, qst_ref, kt_ref, dst_ref, dqt_ref, dkv_ref, dqkv_ref, proj_ref, y_ref = work
    add_gradient(g_ref, COL_PROJ, mid16_ref[0:SEQ], o_ref[...])
    grad_o = dot_nt(proj_ref[...], mid16_ref[...]).astype(BF16).astype(F32)
    kt_ref[...] = jnp.transpose(kv_ref[:, 0:256])
    deltas = []
    for h in range(HEADS):
        scaled = grad_o[head_rows(h)] * r_ref[h : h + 1]
        deltas.append(column_sum(scaled * ot_ref[head_rows(h)].astype(F32)))
        scaled = scaled.astype(BF16)
        for i in range(BLOCKS):
            dost_ref[head_rows(h), block_lanes(i, h)] = scaled[:, BLOCK * i : BLOCK * (i + 1)]
    for i in range(BLOCKS):
        seen, first = BLOCK * (i + 1), BLOCK * i
        lanes = block_lanes(i)
        delta = jnp.concatenate([a[:, first:seen] for a in deltas], axis=1)
        grad = dot_nn(kv_ref[0:seen, 256:512], dost_ref[:, lanes])
        dst_ref[0:seen, lanes] = pt_ref[0:seen, lanes] * (grad - delta).astype(BF16)
        for h in range(HEADS):
            out = dot_nn(kt_ref[head_rows(h), 0:seen], dst_ref[0:seen, block_lanes(i, h)])
            dqt_ref[head_rows(h), first:seen] = out.astype(BF16)
        for at, left, right in ((0, dst_ref, qst_ref), (256, pt_ref, dost_ref)):
            out = dot_nt(left[0:seen, lanes], right[:, lanes])
            if i:
                dkv_ref[0:first, at : at + 256] += out[0:first]
            dkv_ref[first:seen, at : at + 256] = out[first:]
    dqkv_ref[:, 0:256] = jnp.transpose(dqt_ref[...])[0:SEQ]
    dqkv_ref[:, 256:768] = dkv_ref[0:SEQ].astype(BF16)
    add_gradient(g_ref, COL_QKV, a_ref[0:SEQ], dqkv_ref[...])
    y_ref[...] = dot_nt(dqkv_ref[...], w_ref[:, COL_QKV : COL_QKV + 768])
    totals = [None] * 2
    for rows in tiles(SEQ, TILE):
        xhat, scale = normalise(x_ref[rows])
        grad = y_ref[rows]
        out = mid_ref[rows] + normalise_back(grad, xhat, scale, vec[0:1])
        out_ref[rows] = out.astype(out_ref.dtype)
        for i, a in enumerate((grad * xhat, grad)):
            totals[i] = plus(totals[i], fold(a))
    for i in range(2):
        v_ref[v_row + i] += totals[i]


def own_bias(place_ref, mine, other):
    is_first = place_ref[1] == 0
    return jnp.concatenate(
        [jnp.where(is_first, mine, other), jnp.where(is_first, other, mine)], axis=1
    )


def prepare_kernel(
    place_ref, games_ref, tokens, actions, valid, rewards, ends, after, out, out_side, x_ref
):
    count = out.shape[0]
    frames = tokens.shape[2]
    base = place_ref[1] * count
    row = lax.broadcasted_iota(jnp.int32, (SEQ, frames), 0)
    start = lax.broadcasted_iota(jnp.int32, (SEQ, frames), 1) * FRAME_TOKENS
    here = jnp.where((row >= start) & (row < start + FRAME_TOKENS), 1.0, 0.0).astype(BF16)
    coming = jnp.where((row >= start - FRAME_TOKENS) & (row < start), 1.0, 0.0).astype(BF16)
    passed = jnp.sum(jnp.where(row >= start + FRAME_TOKENS, 1, 0), axis=1, keepdims=True)
    place = lax.broadcasted_iota(jnp.int32, (SEQ, 1), 0)
    spot = place - passed * FRAME_TOKENS
    lane = lax.broadcasted_iota(jnp.int32, (SEQ, 24), 1)
    wide_lane = lax.broadcasted_iota(jnp.int32, (SEQ, 128), 1)
    inside = place < LENGTH
    one_frame = (
        lax.broadcasted_iota(jnp.int32, (SIDE_ROWS, frames), 0)
        == lax.broadcasted_iota(jnp.int32, (SIDE_ROWS, frames), 1)
    )
    one_frame = jnp.where(one_frame, 1.0, 0.0).astype(BF16)
    side_lane = lax.broadcasted_iota(jnp.int32, (SIDE_ROWS, 128), 1)
    x_ref[...] = jnp.zeros(x_ref.shape, jnp.int32)
    for s in range(count):
        x_ref[0:OBS] = tokens[base + s]
        x_ref[16:17] = actions[pl.ds(base + s, 1)] + VOCAB
        x_ref[17:18] = valid[pl.ds(base + s, 1)]
        x_ref[18:19] = rewards[pl.ds(base + s, 1)]
        x_ref[19:20] = ends[pl.ds(base + s, 1)] + 3
        high = (x_ref[...] >> 4).astype(F32).astype(BF16)
        low = (x_ref[...] & 15).astype(F32).astype(BF16)
        now = dot_nt(here, high) * 16.0 + dot_nt(here, low)
        soon = dot_nt(coming, high) * 16.0 + dot_nt(coming, low)

        def pick(condition, a):
            return jnp.sum(jnp.where(condition, a, 0.0), axis=1, keepdims=True).astype(jnp.int32)

        ids = jnp.where(inside, pick(lane == spot, now), -1)
        game = jnp.where(inside, games_ref[base + s] + (VOCAB + ACTIONS), -1)
        target = pick((lane == spot + 1) & (spot < 15), now)
        target = target + pick((lane == 0) & (spot == 16), soon)
        weight = pick((lane == 17) & (spot < 15), now) + pick((lane == 17) & (spot == 16), soon)
        result = jnp.zeros((SEQ, 128), jnp.int32)
        for c, column in enumerate((ids, game, target, weight)):
            result = jnp.where(wide_lane == c, column, result)
        out[s] = result
        by_frame = dot_nt(one_frame, high) * 16.0 + dot_nt(one_frame, low)
        result = jnp.zeros((SIDE_ROWS, 128), jnp.int32)
        for c in range(3):
            column = by_frame[:, 17 + c : 18 + c].astype(jnp.int32)
            result = jnp.where(side_lane == c, column, result)
        out_side[s] = result


def start_forward(work, w_ref):
    qst_ref, vt_ref, mask_ref, wqt_ref, u_ref, y_ref = work
    qst_ref[...] = jnp.zeros(qst_ref.shape, BF16)
    vt_ref[...] = jnp.ones(vt_ref.shape, BF16)
    mask_ref[...] = causal_mask()
    wqt_ref[...] = jnp.transpose(w_ref[:, 0:256])


def first_forward_kernel(*refs):
    place_ref, meta_ref, vec_ref, bias_ref, bias_other = refs[0:5]
    mine, other = refs[5:9], refs[9:13]
    w_out, side_out, next_ref, hits_ref, x_ref = refs[13:18]
    kept = [ref.at[0] for ref in refs[18:29]]
    w_ref = refs[29]
    work = refs[30:36]

    @pl.when(pl.program_id(0) == 0)
    def _():
        assemble(mine, other, place_ref, w_ref, HALF_FIRST)
        w_out[...] = w_ref[...]
        side_out[...] = w_ref[:, COL_SMALL:]
        start_forward(work, w_ref)

    make_hits(meta_ref.at[0], hits_ref.at[0])
    x_ref[0] = dot_nt(hits_ref[0], w_ref[:, COL_TABLE : COL_TABLE + ROWS])
    bias = own_bias(place_ref, bias_ref[0:1], bias_other[0:1])
    vec = vec_ref[0:6]
    layer_forward(x_ref.at[0], w_ref, vec, bias, kept, work)
    for rows in tiles(SEQ, TILE):
        next_ref[0, rows] = kept[6][rows] + (work[5][rows] + vec[5:6])


def codebook_losses(logits, meta):
    weight = meta[:, 3:4].astype(F32)
    peak = jnp.max(logits, axis=1, keepdims=True)
    expanded = jnp.exp(logits - peak)
    total = jnp.sum(expanded, axis=1, keepdims=True)
    hit = lax.broadcasted_iota(jnp.int32, logits.shape, 1) == meta[:, 2:3]
    hit = jnp.where(hit, weight, 0.0)
    return weight * (peak + jnp.log(total)), hit, expanded * (weight / total) - hit


def side_losses(side, meta):
    lane = lax.broadcasted_iota(jnp.int32, side.shape, 1)
    is_reward, is_end = lane < 3, (lane == 3) | (lane == 4)
    is_side = lane < 5
    weight = meta[:, 0:1].astype(F32)
    reward_peak = jnp.max(jnp.where(is_reward, side, -1e30), axis=1, keepdims=True)
    end_peak = jnp.max(jnp.where(is_end, side, -1e30), axis=1, keepdims=True)
    shifted = jnp.where(is_side, side - jnp.where(is_reward, reward_peak, end_peak), 0.0)
    expanded = jnp.where(is_side, jnp.exp(shifted), 0.0)
    reward_total = jnp.sum(jnp.where(is_reward, expanded, 0.0), axis=1, keepdims=True)
    end_total = jnp.sum(jnp.where(is_end, expanded, 0.0), axis=1, keepdims=True)
    hit = (lane == meta[:, 1:2]) | (lane == meta[:, 2:3])
    picked = jnp.sum(jnp.where(hit, side, 0.0), axis=1, keepdims=True)
    terms = reward_peak + jnp.log(reward_total) + end_peak + jnp.log(end_total) - picked
    grad = expanded * jnp.where(is_reward, weight / reward_total, weight / end_total)
    return weight * terms, grad - jnp.where(hit, weight, 0.0), weight


def frame_ends(shape, frame_axis):
    frame = lax.broadcasted_iota(jnp.int32, shape, frame_axis)
    row = lax.broadcasted_iota(jnp.int32, shape, 1 - frame_axis)
    hit = (row == frame * FRAME_TOKENS + OBS) & (frame < FRAMES)
    return jnp.where(hit, 1.0, 0.0).astype(BF16)


def middle_kernel(*refs):
    place_ref, meta_ref, frame_ref, vec_ref, bias_ref, bias_other, side_ref, in_ref = refs[0:8]
    mine, other = refs[8:12], refs[12:16]
    grad_ref, keep_ref, send_ref, v_out, scalar_ref = refs[16:21]
    refs = refs[1:]
    w_ref, g_ref, v_ref = refs[20:23]
    kept = refs[23:34]
    qt_ref, kv_ref, pt_ref, r_ref, ot_ref, o_ref, m_ref, h_ref, gp_ref, a_ref, c_ref = kept
    forward_work = refs[34:40]
    u_ref, y_ref = forward_work[4:6]
    backward_work = refs[40:47]
    proj_ref = refs[47]
    du_ref, ones_ref, up_ref, up16_ref, mid_ref, mid16_ref = refs[48:54]
    last_ref, final_ref, logit_ref, dlogit_ref, pick_ref, put_ref = refs[54:60]
    dost_ref = backward_work[0]
    step = pl.program_id(0)

    @pl.when(step == 0)
    def _():
        assemble(mine, other, place_ref, w_ref, HALF_SECOND)
        w_ref[:, COL_SECOND:] = side_ref[...]
        g_ref[...] = jnp.zeros(g_ref.shape, F32)
        v_ref[...] = jnp.zeros(v_ref.shape, F32)
        scalar_ref[...] = jnp.zeros(scalar_ref.shape, F32)
        start_forward(forward_work, w_ref)
        dost_ref[...] = jnp.zeros(dost_ref.shape, BF16)
        proj_ref[...] = jnp.transpose(w_ref[:, COL_PROJ : COL_PROJ + 256])
        ones_ref[...] = jnp.ones(ones_ref.shape, BF16)
        mid16_ref[SEQ:KEYS] = jnp.zeros((KEYS - SEQ, D), BF16)
        pick_ref[...] = frame_ends((SIDE_ROWS, SEQ), 0)
        put_ref[...] = frame_ends((SEQ, SIDE_ROWS), 1)

    x_ref = in_ref.at[0]
    vec = vec_ref[6:12]
    bias = own_bias(place_ref, bias_ref[1:2], bias_other[1:2])
    layer_forward(x_ref, w_ref, vec, bias, kept, forward_work)

    gain, offset = vec_ref[12:13], vec_ref[13:14]
    for rows in tiles(SEQ, TILE):
        last = m_ref[rows] + (y_ref[rows] + vec[5:6])
        last_ref[rows] = last
        final_ref[rows] = (normalise(last)[0] * gain + offset).astype(BF16)
    cols_head = slice(COL_HEAD, COL_HEAD + VOCAB + 128)
    logit_ref[...] = dot_nn(final_ref[...], w_ref[:, COL_HEAD : COL_HEAD + VOCAB])
    logs, picked = None, None
    for rows in tiles(SEQ, TILE):
        logits = logit_ref[rows]
        log, hit, grad = codebook_losses(logits, meta_ref[0, rows])
        dlogit_ref[rows, :VOCAB] = grad.astype(BF16)
        logs, picked = plus(logs, log), plus(picked, fold(hit * logits))
    acting = dot_nn(pick_ref[...], final_ref[...]).astype(BF16)
    side = dot_nn(acting, w_ref[:, COL_HEAD + VOCAB : COL_HEAD + VOCAB + 128])
    side_loss, grad, weight = side_losses(side, frame_ref[0])
    dlogit_ref[:, VOCAB:] = dot_nn(put_ref[...], grad.astype(BF16)).astype(BF16)
    loss = column_sum(logs) + column_sum(side_loss)
    loss = loss - jnp.sum(column_sum(picked), axis=1, keepdims=True)
    valid = column_sum(weight)
    scalar_lane = lax.broadcasted_iota(jnp.int32, (8, 128), 1)
    scalar_row = lax.broadcasted_iota(jnp.int32, (8, 128), 0) == 0
    scalar_ref[...] += jnp.where(
        scalar_row,
        jnp.where(scalar_lane == 0, loss, jnp.where(scalar_lane == 1, valid, 0.0)),
        0.0,
    )
    add_gradient(g_ref, COL_HEAD, final_ref[...], dlogit_ref[...])
    y_ref[...] = dot_nt(dlogit_ref[...], w_ref[:, cols_head])
    totals = [None] * 3
    for rows in tiles(SEQ, TILE):
        xhat, scale = normalise(last_ref[rows])
        grad = y_ref[rows]
        up = normalise_back(grad, xhat, scale, gain)
        up_ref[rows] = up
        up16_ref[rows] = up.astype(BF16)
        for i, a in enumerate((up, grad * xhat, grad)):
            totals[i] = plus(totals[i], fold(a))
    for i in range(3):
        v_ref[11 + i] += totals[i]
    ff_backward(
        up_ref,
        up16_ref,
        w_ref,
        vec,
        (m_ref, h_ref, gp_ref, c_ref),
        g_ref,
        COL_UP,
        COL_DOWN,
        v_ref,
        6,
        SMALL_BIAS + 4,
        (du_ref, ones_ref, u_ref, y_ref),
        mid_ref,
        mid16_ref,
    )
    attention_backward(
        mid_ref,
        mid16_ref,
        w_ref,
        vec,
        (x_ref, qt_ref, kv_ref, pt_ref, r_ref, ot_ref, o_ref, a_ref),
        g_ref,
        v_ref,
        6,
        (dost_ref, forward_work[0]) + tuple(backward_work[2:]) + (proj_ref, y_ref),
        grad_ref.at[0],
    )

    @pl.when(step == pl.num_programs(0) - 1)
    def _():
        disperse(g_ref, place_ref, keep_ref, send_ref, HALF_SECOND)
        side = jnp.transpose(g_ref[:, COL_SECOND:])
        for i in range(5):
            v_ref[SMALL_SIDE + i, 0:1] = side[i : i + 1]
        v_out[...] = v_ref[...]


def ff_backward_kernel(*refs):
    place_ref, vec_ref, w_ref, grad_ref, v_in = refs[0:5]
    kept = [ref.at[0] for ref in refs[5:9]]
    mid_ref, keep_ref, send_ref, v_out = refs[9:13]
    g_ref, v_ref, grad16_ref = refs[13:16]
    work = refs[16:20]
    ones_ref = work[1]
    step = pl.program_id(0)

    @pl.when(step == 0)
    def _():
        g_ref[...] = jnp.zeros(g_ref.shape, F32)
        v_ref[...] = v_in[...]
        ones_ref[...] = jnp.ones(ones_ref.shape, BF16)

    total = None
    for rows in tiles(SEQ, TILE):
        grad = grad_ref[0, rows]
        grad16_ref[rows] = grad.astype(BF16)
        total = plus(total, fold(grad))
    v_ref[5] += total
    ff_backward(
        grad_ref.at[0],
        grad16_ref,
        w_ref,
        vec_ref[0:6],
        kept,
        g_ref,
        GRAD_UP,
        GRAD_DOWN,
        v_ref,
        0,
        SMALL_BIAS,
        work,
        mid_ref.at[0],
        None,
    )

    @pl.when(step == pl.num_programs(0) - 1)
    def _():
        disperse(g_ref, place_ref, keep_ref, send_ref, HALF_GRAD_FF, False)
        v_out[...] = v_ref[...]


def attention_backward_kernel(*refs):
    place_ref, vec_ref, w_ref, mid_ref, hits_ref, v_in = refs[0:6]
    kept = [ref.at[0] for ref in refs[6:14]]
    keep_ref, send_ref, v_out = refs[15:18]
    g_ref, v_ref, mid16_ref, out16_ref = refs[18:22]
    work = refs[22:31]
    dost_ref, qst_ref, proj_ref = work[0], work[1], work[7]
    step = pl.program_id(0)

    @pl.when(step == 0)
    def _():
        g_ref[...] = jnp.zeros(g_ref.shape, F32)
        v_ref[...] = v_in[...]
        dost_ref[...] = jnp.zeros(dost_ref.shape, BF16)
        qst_ref[...] = jnp.zeros(qst_ref.shape, BF16)
        proj_ref[...] = jnp.transpose(w_ref[:, COL_PROJ : COL_PROJ + 256])
        mid16_ref[SEQ:KEYS] = jnp.zeros((KEYS - SEQ, D), BF16)

    spread_heads(kept[1], qst_ref)
    for rows in tiles(SEQ, TILE):
        mid16_ref[rows] = mid_ref[0, rows].astype(BF16)
    attention_backward(
        mid_ref.at[0], mid16_ref, w_ref, vec_ref[0:6], kept, g_ref, v_ref, 0, work, out16_ref
    )
    add_gradient(g_ref, GRAD_TABLE, out16_ref[...], hits_ref[0])

    @pl.when(step == pl.num_programs(0) - 1)
    def _():
        small = jnp.sum(v_ref[...], axis=1)
        v_out[...] = small
        for block in range(16):
            quarter = small[8 * (block // 4) : 8 * (block // 4) + 8]
            g_ref[16 * block : 16 * block + 8, GRAD_SMALL:] = quarter[:, 0:128]
            g_ref[16 * block + 8 : 16 * block + 16, GRAD_SMALL:] = quarter[:, 128:256]
        disperse(g_ref, place_ref, keep_ref, send_ref, HALF_GRAD_REST)


def pack_layer(attn, proj, up, down, layer, out, at):
    for j in range(3):
        out[:, at + 128 * j : at + 128 * j + 128] = attn[layer, j].astype(BF16)
    out[:, at + 384 : at + 512] = proj[layer].astype(BF16)
    out[:, at + 512 : at + 1024] = up[layer].astype(BF16)
    out[:, at + 1024 : at + 1536] = down[layer].astype(BF16)


def pack_kernel(place_ref, table, attn, proj, up, down, head, side, out, pad_ref):
    pack_layer(attn, proj, up, down, 0, out, 0)
    pack_layer(attn, proj, up, down, 1, out, HALF_FIRST_COLS)
    out[:, HALF_FIRST_COLS + 1536 :] = head[...].astype(BF16)
    rows = side.shape[1]
    eye = (
        lax.broadcasted_iota(jnp.int32, (rows, rows), 0)
        == lax.broadcasted_iota(jnp.int32, (rows, rows), 1)
    )
    eye = jnp.where(eye, 1.0, 0.0).astype(BF16)
    pad_ref[...] = jnp.zeros(pad_ref.shape, F32)
    pad_ref[:, 0:5] = dot_nt(eye, side[...].astype(BF16))
    high = jnp.concatenate([table[:, 512:896], pad_ref[...]], axis=1)
    out[:, 1536:2048] = jnp.where(place_ref[1] == 0, table[:, 0:512], high).astype(BF16)


def finish_kernel(place_ref, rest, others, scalar_ref, out_rest, out_other, out_table, out_small):
    square = jnp.zeros((1, 1), F32)
    for pieces, out in ((rest, out_rest), (others, out_other)):
        total = pieces[0].astype(F32)
        for i in range(1, pieces.shape[0]):
            total = total + pieces[i].astype(F32)
        out[...] = total
        square = square + column_sum(jnp.sum(total * total, axis=1, keepdims=True))
    small = out_rest[:, 896:1024]
    extra = column_sum(jnp.sum(small * small, axis=1, keepdims=True))
    square = square - jnp.where(place_ref[1] == 0, 0.0, extra)
    out_table[...] = out_rest[:, 512:1024]
    rows = small.shape[0]
    out_small[0:rows] = small
    lane = lax.broadcasted_iota(jnp.int32, (8, 128), 1)
    top = lax.broadcasted_iota(jnp.int32, (8, 128), 0) == 0
    out_small[rows : rows + 8] = scalar_ref[...] + jnp.where(top & (lane == 2), square, 0.0)


def adam_rule(weight, moment, second, gradient, step_rate, decay_rate):
    moment_new = BETA_ONE * moment + (1.0 - BETA_ONE) * gradient
    second_new = BETA_TWO * second + (1.0 - BETA_TWO) * gradient * gradient
    moment_hat = moment_new / (1.0 - BETA_ONE**STEP_NUMBER)
    second_hat = second_new / (1.0 - BETA_TWO**STEP_NUMBER)
    weight_new = weight - step_rate * (
        moment_hat / (jnp.sqrt(second_hat) + EPS_ADAM) + decay_rate * weight
    )
    return (weight_new, moment_new, second_new)


def adam_kernel(fast, place_ref, rest, others, swapped, gathered, *refs):
    rows = rest.shape[0]
    quarters = [gathered.at[4 * z] for z in range(4)] if fast else [refs[0].at[z] for z in range(4)]
    refs = refs if fast else refs[1:]
    params = [refs[3 * i : 3 * i + 3] for i in range(9)]
    loss_ref, valid_ref, norm_ref = refs[27:30]
    outs = [refs[30 + 3 * i : 33 + 3 * i] for i in range(9)]
    small_ref = refs[57]
    wide = place_ref[2]
    is_first = place_ref[1] == 0
    for z in range(4):
        small_ref[8 * z : 8 * z + 8, 0:128] = quarters[z][0:8]
        small_ref[8 * z : 8 * z + 8, 128:256] = quarters[z][8:16]
    scalars = gathered[0, rows : rows + 1]
    for i in range(1, gathered.shape[0]):
        scalars = scalars + gathered[i, rows : rows + 1]
    small = small_ref[...]
    loss, valid, square = scalars[:, 0:1], scalars[:, 1:2], scalars[:, 2:3]
    square = square + column_sum(jnp.sum(small * small, axis=1, keepdims=True))
    inverse = 1.0 / valid
    norm = jnp.sqrt(square) * inverse
    loss_ref[...], valid_ref[...], norm_ref[...] = loss, valid, norm
    factor = jnp.minimum(1.0, CLIP_AT / (norm + 1e-06)) * inverse
    table, attn, proj, up, bias, down, vectors, head, side = range(9)

    def update(which, index, gradient, step_rate, decay_rate):
        news = adam_rule(
            *(ref[index] for ref in params[which]), factor * gradient, step_rate, decay_rate
        )
        for ref, new in zip(outs[which], news):
            ref[index] = new

    layers = ((rest, others, 1792), (others, others, 512))
    for layer, (attention, feed, at) in enumerate(layers):
        for j in range(3):
            update(attn, (layer, j), attention[:, 128 * j : 128 * j + 128], RATE_MATRIX, DECAY_RATE)
        update(proj, (layer,), attention[:, 384:512], RATE_MATRIX, DECAY_RATE)
        update(up, (layer,), feed[:, at : at + 512], RATE_MATRIX, DECAY_RATE)
        update(down, (layer,), feed[:, at + 512 : at + 1024], RATE_MATRIX, DECAY_RATE)
        for i in range(2):
            low = SMALL_BIAS + 4 * layer + i
            row = jnp.where(is_first, small[low : low + 1], small[low + 2 : low + 3])
            index = (slice(layer, layer + 1), slice(256 * i, 256 * i + 256))
            update(bias, index, row, RATE_VECTOR, 0.0)
    whole = (slice(None), slice(None))
    update(head, whole, others[:, 1536:1792], RATE_MATRIX, DECAY_RATE)
    mine, theirs = rest[:, 512:1024], swapped[:, 0:512]
    low, high = jnp.where(is_first, mine, theirs), jnp.where(is_first, theirs, mine)
    update(table, (slice(None), slice(0, 512)), low, RATE_TABLE, DECAY_RATE)
    update(table, (slice(None), slice(512, 896)), high[:, 0:384], RATE_TABLE, DECAY_RATE)
    update(vectors, whole, small[0:NVEC], RATE_VECTOR, 0.0)
    turned = pltpu.roll(small[SMALL_SIDE : SMALL_SIDE + 8], lax.rem(D - wide * rows, D), 1)
    update(side, whole, turned[0:5, 0:rows], RATE_MATRIX, DECAY_RATE)


def swap(a, axis, distance):
    size = lax.axis_size(axis)
    return lax.ppermute(a, axis, [(i, i ^ distance) for i in range(size)])


def swap_column(piece, n_high):
    return [piece] + [swap(piece, "wide", 4 * k) for k in range(1, n_high)]


def gather_plane(column):
    return [column] + [swap(column, "wide", p) for p in range(1, 4)]


def gather_cores(mine):
    return [swap(a, "narrow", 1) for a in mine]


def in_blocks(parts, wide):
    n_high, rows, cols = parts[0].shape
    if rows == 16:
        return parts
    whole = jnp.stack(parts, axis=1).reshape(4 * n_high, rows, cols)
    whole = whole[wide ^ jnp.arange(4 * n_high)].reshape(4, 4, 16, cols)
    return [whole[:, p] for p in range(4)]


def in_pieces(blocks, n_high):
    if n_high == 4:
        return blocks
    cols = blocks.shape[-1]
    whole = blocks.transpose(1, 0, 2, 3).reshape(n_high, 4, 64 // n_high, cols)
    return whole.transpose(1, 0, 2, 3)


def add_cores(keep, send, n_high):
    keep, send = in_pieces(keep, n_high), in_pieces(send, n_high)
    return keep + swap(send, "narrow", 1).astype(F32)


def exchange(a, groups):
    return lax.all_to_all(a, "wide", 0, 0, axis_index_groups=groups)


def plane_groups(n_high):
    return [[4 * h + p for p in range(4)] for h in range(n_high)]


def column_groups(n_high):
    return [[4 * h + p for h in range(n_high)] for p in range(4)]


def full_spec(a):
    return pl.BlockSpec(a.shape, lambda *_: (0,) * len(a.shape))


def row_spec(shape):
    return pl.BlockSpec((1,) + shape, lambda i: (i,) + (0,) * len(shape))


def shaped(shape, dtype):
    return jax.ShapeDtypeStruct(shape, dtype)


VMEM_SPEC = pl.BlockSpec(memory_space=pltpu.VMEM)
ANY_SPEC = pl.BlockSpec(memory_space=pl.ANY)
SMEM_SPEC = pl.BlockSpec(memory_space=pltpu.SMEM)


def call(kernel, grid, in_specs, out_specs, out_shape, scratch, flops, bytes_accessed, name):
    extra = {"grid": grid} if grid else {}
    return pl.pallas_call(
        kernel,
        in_specs=in_specs,
        out_specs=out_specs,
        out_shape=out_shape,
        scratch_shapes=scratch,
        compiler_params=pltpu.CompilerParams(vmem_limit_bytes=VMEM_BYTES),
        cost_estimate=pl.CostEstimate(
            flops=flops, bytes_accessed=bytes_accessed, transcendentals=0
        ),
        name=name,
        **extra,
    )


KEPT = (
    ((D, KEYS), BF16),
    ((KEYS, 512), BF16),
    ((KEYS, BLOCKS * QUERIES), BF16),
    ((8, KEYS), F32),
    ((D, KEYS), BF16),
    ((SEQ, D), BF16),
    ((SEQ, D), F32),
    ((SEQ, FF), BF16),
    ((SEQ, FF), BF16),
    ((KEYS, D), BF16),
    ((SEQ, D), BF16),
)
FORWARD_WORK = [
    pltpu.VMEM((D, BLOCKS * QUERIES), BF16),
    pltpu.VMEM((HEADS * VALUE_ROWS, KEYS), BF16),
    pltpu.VMEM((BLOCK, QUERIES), F32),
    pltpu.VMEM((D, D), BF16),
    pltpu.VMEM((SEQ, FF), F32),
    pltpu.VMEM((SEQ, D), F32),
]
BACKWARD_WORK = [
    pltpu.VMEM((D, BLOCKS * QUERIES), BF16),
    pltpu.VMEM((D, BLOCKS * QUERIES), BF16),
    pltpu.VMEM((D, KEYS), BF16),
    pltpu.VMEM((KEYS, BLOCKS * QUERIES), BF16),
    pltpu.VMEM((D, KEYS), BF16),
    pltpu.VMEM((KEYS, 512), F32),
    pltpu.VMEM((SEQ, 768), BF16),
]
PROJ_WORK = pltpu.VMEM((D, D), BF16)
ONES_WORK = pltpu.VMEM((16, SEQ), BF16)


def per_device(
    tokens,
    actions,
    game_ids,
    valid_steps,
    rewards,
    end_flags,
    embed_table,
    table_first,
    table_second,
    attn_weight,
    attn_first,
    attn_second,
    proj_weight,
    proj_first,
    proj_second,
    up_weight,
    up_first,
    up_second,
    up_bias,
    bias_first,
    bias_second,
    down_weight,
    down_first,
    down_second,
    vectors,
    vectors_first,
    vectors_second,
    head_weight,
    head_first,
    head_second,
    side_weight,
    side_first,
    side_second,
):
    n_high = lax.axis_size("wide") // 4
    wide, core = lax.axis_index("wide"), lax.axis_index("narrow")
    rows = side_weight.shape[0]
    fast = rows == 16
    place = jnp.stack([wide if fast else jnp.zeros_like(wide), core, wide]).astype(jnp.int32)

    def flat(a):
        return jnp.swapaxes(a, -1, -2)

    params = (
        (flat(embed_table), flat(table_first), flat(table_second)),
        (attn_weight, attn_first, attn_second),
        (flat(proj_weight), flat(proj_first), flat(proj_second)),
        (up_weight, up_first, up_second),
        (up_bias, bias_first, bias_second),
        (flat(down_weight), flat(down_first), flat(down_second)),
        (vectors, vectors_first, vectors_second),
        (head_weight, head_first, head_second),
        (flat(side_weight), flat(side_first), flat(side_second)),
    )
    table, attn, proj, up, _, down, _, head, side = (group[0] for group in params)

    piece = call(
        pack_kernel,
        None,
        [SMEM_SPEC] + [VMEM_SPEC] * 7,
        VMEM_SPEC,
        shaped((rows, HALF_FIRST_COLS + HALF_SECOND_COLS), BF16),
        [pltpu.VMEM((rows, 128), F32)],
        10**6,
        10**6,
        "pack",
    )(place, table, attn, proj, up, down, head, side)
    column = swap_column(piece, n_high)

    count = tokens.shape[0] // lax.axis_size("narrow")
    meta, frame_meta = call(
        prepare_kernel,
        None,
        [SMEM_SPEC] * 2 + [VMEM_SPEC] * 5 + [ANY_SPEC],
        [VMEM_SPEC] * 2,
        [shaped((count, SEQ, 128), jnp.int32), shaped((count, SIDE_ROWS, 128), jnp.int32)],
        [pltpu.VMEM((24, FRAMES), jnp.int32)],
        10**6,
        10**6,
        "prepare",
    )(place, game_ids, flat(tokens), actions, valid_steps, rewards, end_flags, piece)
    column, meta = lax.optimization_barrier((column, meta))
    first_mine = gather_plane(jnp.stack([a[:, :HALF_FIRST_COLS] for a in column]))
    second_column = jnp.stack([a[:, HALF_FIRST_COLS:] for a in column])
    second_column, last = lax.optimization_barrier((second_column, first_mine[3]))
    first_mine = first_mine[0:3] + [last]
    first_other = gather_cores(first_mine)
    second_mine = gather_plane(second_column)
    first_parts = in_blocks(first_mine, wide) + in_blocks(first_other, wide)
    other_bias = swap(up_bias, "narrow", 1)

    kept_specs = [row_spec(shape) for shape, _ in KEPT]
    kept_shapes = [shaped((count,) + shape, dtype) for shape, dtype in KEPT]
    row_f32 = shaped((count, SEQ, D), F32)
    meta_spec = row_spec((SEQ, 128))
    vec_specs = [full_spec(vectors), full_spec(up_bias), full_spec(up_bias)]
    w_spec = pl.BlockSpec((D, COL_FIRST), lambda i: (0, 0))
    side_spec = pl.BlockSpec((D, 128), lambda i: (0, 0))
    hits_spec = row_spec((SEQ, ROWS))
    results = call(
        first_forward_kernel,
        (count,),
        [SMEM_SPEC, meta_spec] + vec_specs + [full_spec(a) for a in first_parts],
        [w_spec, side_spec, row_spec((SEQ, D)), hits_spec, row_spec((SEQ, D))] + kept_specs,
        [shaped((D, COL_FIRST), BF16), shaped((D, 128), BF16), row_f32]
        + [shaped((count, SEQ, ROWS), BF16), row_f32]
        + kept_shapes,
        [pltpu.VMEM((D, COL_FIRST), BF16)] + FORWARD_WORK,
        4 * 10**9,
        20 * 10**6,
        "first_forward",
    )(place, meta, vectors, up_bias, other_bias, *first_parts)
    w_first, side_copy, stream, hits, stream_first = results[0:5]
    kept = results[5:]
    received, side_copy = lax.optimization_barrier((second_mine[1:], side_copy))
    second_mine = second_mine[0:1] + received
    second_other = gather_cores(second_mine)
    second_parts = in_blocks(second_mine, wide) + in_blocks(second_other, wide)

    def blocks(cols):
        return pl.BlockSpec((4, 4, 16, cols), lambda i: (0, 0, 0, 0))

    def block_shapes(cols):
        return [shaped((4, 4, 16, cols), F32), shaped((4, 4, 16, cols), BF16)]

    small_spec = pl.BlockSpec((SMALL_ROWS, 8, D), lambda i: (0, 0, 0))
    small_shape = shaped((SMALL_ROWS, 8, D), F32)
    small_scratch = pltpu.VMEM((SMALL_ROWS, 8, D), F32)
    scalar_spec = pl.BlockSpec((8, 128), lambda i: (0, 0))
    grad_stream, keep_second, send_second, small_grads, scalars = call(
        middle_kernel,
        (count,),
        [SMEM_SPEC, meta_spec, row_spec((SIDE_ROWS, 128))]
        + vec_specs
        + [side_spec, row_spec((SEQ, D))]
        + [full_spec(a) for a in second_parts],
        [row_spec((SEQ, D))] + [blocks(HALF_SECOND_COLS)] * 2 + [small_spec, scalar_spec],
        [row_f32] + block_shapes(HALF_SECOND_COLS) + [small_shape, shaped((8, 128), F32)],
        [
            pltpu.VMEM((D, COL_SECOND + 128), BF16),
            pltpu.VMEM((D, COL_SECOND + 128), F32),
            small_scratch,
        ]
        + [pltpu.VMEM(shape, dtype) for shape, dtype in KEPT]
        + FORWARD_WORK
        + BACKWARD_WORK
        + [
            PROJ_WORK,
            pltpu.VMEM((SEQ, FF), BF16),
            ONES_WORK,
            pltpu.VMEM((SEQ, D), F32),
            pltpu.VMEM((SEQ, D), BF16),
            pltpu.VMEM((SEQ, D), F32),
            pltpu.VMEM((KEYS, D), BF16),
            pltpu.VMEM((SEQ, D), F32),
            pltpu.VMEM((SEQ, D), BF16),
            pltpu.VMEM((SEQ, VOCAB), F32),
            pltpu.VMEM((SEQ, VOCAB + 128), BF16),
            pltpu.VMEM((SIDE_ROWS, SEQ), BF16),
            pltpu.VMEM((SEQ, SIDE_ROWS), BF16),
        ],
        15 * 10**9,
        20 * 10**6,
        "middle",
    )(place, meta, frame_meta, vectors, up_bias, other_bias, side_copy, stream, *second_parts)
    second_sums = add_cores(keep_second, send_second, n_high)

    kept_ff = (kept[6], kept[7], kept[8], kept[10])
    grad_mid, keep_ff, send_ff, small_grads = call(
        ff_backward_kernel,
        (count,),
        [SMEM_SPEC, full_spec(vectors), w_spec, row_spec((SEQ, D)), small_spec]
        + [row_spec(a.shape[1:]) for a in kept_ff],
        [row_spec((SEQ, D))] + [blocks(HALF_GRAD_COLS)] * 2 + [small_spec],
        [row_f32] + block_shapes(HALF_GRAD_COLS) + [small_shape],
        [
            pltpu.VMEM((D, 2048), F32),
            small_scratch,
            pltpu.VMEM((SEQ, D), BF16),
            pltpu.VMEM((SEQ, FF), BF16),
            ONES_WORK,
            pltpu.VMEM((SEQ, FF), F32),
            pltpu.VMEM((SEQ, D), F32),
        ],
        4 * 10**9,
        10 * 10**6,
        "ff_backward",
    )(place, vectors, w_first, grad_stream, small_grads, *kept_ff)
    ff_sums = add_cores(keep_ff, send_ff, n_high)
    other_sums = jnp.concatenate([second_sums.astype(BF16), ff_sums.astype(BF16)], axis=-1)
    others = exchange(other_sums, plane_groups(n_high))

    kept_attention = (stream_first,) + tuple(kept[0:6]) + (kept[9],)
    keep_rest, send_rest, small_grads = call(
        attention_backward_kernel,
        (count,),
        [SMEM_SPEC, full_spec(vectors), w_spec, row_spec((SEQ, D)), hits_spec, small_spec]
        + [row_spec(a.shape[1:]) for a in kept_attention]
        + [ANY_SPEC],
        [blocks(HALF_GRAD_COLS)] * 2 + [pl.BlockSpec((SMALL_ROWS, D), lambda i: (0, 0))],
        block_shapes(HALF_GRAD_COLS) + [shaped((SMALL_ROWS, D), F32)],
        [pltpu.VMEM((D, 2048), F32), small_scratch]
        + [pltpu.VMEM((KEYS, D), BF16), pltpu.VMEM((SEQ, D), BF16)]
        + BACKWARD_WORK
        + [PROJ_WORK, pltpu.VMEM((SEQ, D), F32)],
        6 * 10**9,
        20 * 10**6,
        "attention_backward",
    )(place, vectors, w_first, grad_mid, hits, small_grads, *kept_attention, other_sums)
    others, keep_rest = lax.optimization_barrier((others, keep_rest))
    rest_sums = add_cores(keep_rest, send_rest, n_high).astype(BF16)
    rest = exchange(rest_sums, plane_groups(n_high))

    def along_column(parts):
        parts = [parts[p].astype(F32) for p in range(4)]
        total = (parts[0] + parts[1]) + (parts[2] + parts[3])
        return exchange(total.astype(BF16), column_groups(n_high))

    others, rest = along_column(others), along_column(rest)

    grad_rest, grad_others, table_part, small = call(
        finish_kernel,
        None,
        [SMEM_SPEC] + [VMEM_SPEC] * 3,
        [VMEM_SPEC] * 4,
        [
            shaped((rows, HALF_GRAD_COLS), F32),
            shaped((rows, HALF_GRAD_COLS + HALF_SECOND_COLS), F32),
            shaped((rows, 512), F32),
            shaped((rows + 8, 128), F32),
        ],
        [],
        10**6,
        10**6,
        "finish",
    )(place, rest, others, scalars)

    beside = swap(small, "narrow", 1)
    is_small = (jnp.arange(rows + 8) < rows)[:, None]
    small = jnp.where(is_small, jnp.where(core == 1, small, beside), small + beside)
    gathered = exchange(jnp.broadcast_to(small, (4 * n_high,) + small.shape), None)
    quarters = []
    if not fast:
        total = lax.psum(small_grads, ("wide", "narrow"))
        quarters = [total.reshape(4, 8, 2, 128).transpose(0, 2, 1, 3).reshape(4, 16, 128)]
    swapped = swap(table_part, "narrow", 1)

    flat_params = [a for group in params for a in group]
    results = call(
        functools.partial(adam_kernel, fast),
        None,
        [SMEM_SPEC] + [VMEM_SPEC] * (31 + len(quarters)),
        [VMEM_SPEC] * 30,
        [shaped((1, 1), F32)] * 3 + [shaped(a.shape, F32) for a in flat_params],
        [pltpu.VMEM((SMALL_ROWS, D), F32)],
        10**6,
        10**6,
        "adam",
    )(place, grad_rest, grad_others, swapped, gathered, *quarters, *flat_params)
    news = list(results[3:])
    for group in (0, 2, 5, 8):
        for member in range(3 * group, 3 * group + 3):
            news[member] = flat(news[member])
    return tuple(a.reshape(()) for a in results[0:3]) + tuple(news)


def solution(mesh):
    placed = (
        P("wide", None, None),
        P("wide", None),
        P("wide"),
        P("wide", None),
        P("wide", None),
        P("wide", None),
        P(None, "wide"),
        P(None, "wide"),
        P(None, "wide"),
        P(None, None, "wide", "narrow"),
        P(None, None, "wide", "narrow"),
        P(None, None, "wide", "narrow"),
        P(None, "narrow", "wide"),
        P(None, "narrow", "wide"),
        P(None, "narrow", "wide"),
        P(None, "wide", "narrow"),
        P(None, "wide", "narrow"),
        P(None, "wide", "narrow"),
        P(None, "narrow"),
        P(None, "narrow"),
        P(None, "narrow"),
        P(None, "narrow", "wide"),
        P(None, "narrow", "wide"),
        P(None, "narrow", "wide"),
        P(),
        P(),
        P(),
        P("wide", "narrow"),
        P("wide", "narrow"),
        P("wide", "narrow"),
        P("wide", None),
        P("wide", None),
        P("wide", None),
    )
    return jax.shard_map(
        per_device,
        mesh=mesh,
        in_specs=placed,
        out_specs=(P(), P(), P()) + placed[6:],
        check_vma=False,
    )
```

```python
import functools

import jax
import jax.numpy as jnp
from jax import lax
from jax.experimental import pallas as pl
from jax.experimental.pallas import tpu as pltpu
from jax.sharding import PartitionSpec as P

D = 256
HEADS = 4
HEAD_DIM = 64
FF = 1024
VOCAB = 512
ACTIONS = 18
GAMES = 26
OBS = 16
FRAMES = 20
STEP_NUMBER = 5
FRAME_TOKENS = 17
LENGTH = 340
ROWS = 896
NVEC = 14

EPS_NORM = 1e-05
BETA_ONE = 0.5
BETA_TWO = 0.5
RATE_TABLE = 0.5
RATE_MATRIX = 0.05
RATE_VECTOR = 0.2
DECAY_RATE = 0.01
EPS_ADAM = 1e-08
CLIP_AT = 0.1

SEQ = 352
KEYS = 384
BLOCK, BLOCKS = 128, 3
TILE = 32
SIDE_ROWS = 32
QUERIES = HEADS * BLOCK
VALUE_ROWS = 80

COL_QKV, COL_PROJ, COL_UP, COL_DOWN, COL_LAYER = 0, 768, 1024, 2048, 3072
HALF_ATTENTION = ((0, 128, 0), (128, 128, 256), (256, 128, 512), (384, 128, COL_PROJ))
HALF_LAYER = HALF_ATTENTION + ((512, 512, COL_UP), (1024, 512, COL_DOWN))
COL_TABLE, COL_SMALL, COL_FIRST = 3072, 3968, 4096
HALF_FIRST = HALF_LAYER + ((1536, 512, COL_TABLE),)
HALF_FIRST_COLS = 2048
COL_HEAD, COL_SECOND = 3072, 3584
HALF_SECOND = HALF_LAYER + ((1536, 256, COL_HEAD),)
HALF_SECOND_COLS = 1792
GRAD_UP, GRAD_DOWN = 0, 1024
HALF_GRAD_FF = ((0, 512, GRAD_UP), (512, 512, GRAD_DOWN))
GRAD_TABLE, GRAD_SMALL = 1024, 1920
HALF_GRAD_REST = HALF_ATTENTION + ((512, 512, GRAD_TABLE),)
HALF_GRAD_COLS = 1024
SMALL_ROWS, SMALL_BIAS, SMALL_SIDE = 32, 14, 22

F32, BF16 = jnp.float32, jnp.bfloat16
MIB = 1024 * 1024


def dot_nn(a, b):
    return lax.dot_general(a, b, (((1,), (0,)), ((), ())), preferred_element_type=F32)


def dot_nt(a, b):
    return lax.dot_general(a, b, (((1,), (1,)), ((), ())), preferred_element_type=F32)


def dot_tn(a, b):
    return lax.dot_general(a, b, (((0,), (0,)), ((), ())), preferred_element_type=F32)


def tiles(rows, size):
    return [slice(first, first + size) for first in range(0, rows, size)]


def normalise(x):
    centred = x - jnp.mean(x, axis=1, keepdims=True)
    scale = lax.rsqrt(jnp.mean(centred * centred, axis=1, keepdims=True) + EPS_NORM)
    return centred * scale, scale


def normalise_back(grad, xhat, scale, gain):
    inner = grad * gain
    mean_one = jnp.mean(inner, axis=1, keepdims=True)
    mean_two = jnp.mean(inner * xhat, axis=1, keepdims=True)
    return scale * (inner - mean_one - xhat * mean_two)


def column_sum(a):
    return jnp.sum(a, axis=0, keepdims=True)


def fold(a):
    return jnp.sum(a.reshape(a.shape[0] // 8, 8, a.shape[1]), axis=0)


def plus(total, a):
    return a if total is None else total + a


def block_lanes(i, h=None):
    if h is None:
        return slice(QUERIES * i, QUERIES * (i + 1))
    return slice(QUERIES * i + BLOCK * h, QUERIES * i + BLOCK * (h + 1))


def head_rows(h):
    return slice(HEAD_DIM * h, HEAD_DIM * (h + 1))


def spread_heads(source, target_ref):
    for h in range(HEADS):
        for i in range(BLOCKS):
            target_ref[head_rows(h), block_lanes(i, h)] = source[
                head_rows(h), BLOCK * i : BLOCK * (i + 1)
            ]


def causal_mask():
    key = lax.broadcasted_iota(jnp.int32, (BLOCK, QUERIES), 0)
    query = lax.broadcasted_iota(jnp.int32, (BLOCK, QUERIES), 1) & (BLOCK - 1)
    return jnp.where(key <= query, 0.0, -1e30)


def assemble(pieces_mine, pieces_other, place_ref, w_ref, halves):
    me, core = place_ref[0], place_ref[1]
    is_first = core == 0
    for p in range(4):

        def block(z, _, p=p):
            row = pl.multiple_of((me ^ (4 * z + p)) * 16, 16)
            for src, width, dest in halves:
                mine = pieces_mine[p][z, :, src : src + width]
                other = pieces_other[p][z, :, src : src + width]
                if dest == COL_QKV:
                    mine, other = mine * 0.125, other * 0.125
                w_ref[pl.ds(row, 16), dest : dest + width] = jnp.where(is_first, mine, other)
                w_ref[pl.ds(row, 16), dest + width : dest + 2 * width] = jnp.where(
                    is_first, other, mine
                )
            return 0

        lax.fori_loop(0, 4, block, 0)


def disperse(g_ref, place_ref, keep_ref, send_ref, halves, scaled=True):
    me, core = place_ref[0], place_ref[1]
    is_first = core == 0

    def block(i, _):
        p, z = i >> 2, i & 3
        row = pl.multiple_of((me ^ (4 * z + p)) * 16, 16)
        for src, width, dest in halves:
            low = g_ref[pl.ds(row, 16), dest : dest + width]
            high = g_ref[pl.ds(row, 16), dest + width : dest + 2 * width]
            if scaled and dest == COL_QKV:
                low, high = low * 0.125, high * 0.125
            keep_ref[p, z, :, src : src + width] = jnp.where(is_first, low, high).astype(BF16)
            send_ref[p, z, :, src : src + width] = jnp.where(is_first, high, low).astype(BF16)
        return 0

    lax.fori_loop(0, 16, block, 0)


def make_hits(meta_ref, hits_ref):
    for rows in tiles(SEQ, TILE):
        lane = lax.broadcasted_iota(jnp.int32, (TILE, ROWS), 1)
        place = lax.broadcasted_iota(jnp.int32, (TILE, 1), 0) + (VOCAB + ACTIONS + GAMES + rows.start)
        meta = meta_ref[rows]
        hit = (lane == meta[:, 0:1]) | (lane == meta[:, 1:2]) | (lane == place)
        hits_ref[rows] = jnp.where(hit, 1.0, 0.0).astype(BF16)


def gelu_and_slope(up):
    up = up.astype(BF16)
    square = up * up
    half = jax.nn.sigmoid(up * (BF16(1.5957691216057308) + BF16(0.0713548162726) * square))
    hidden = up * half
    slope = BF16(1.5957691216057308) + BF16(0.2140644488178) * square
    return hidden, half + hidden * (BF16(1.0) - half) * slope


def layer_forward(x_ref, w_ref, vec, bias, kept, work):
    qt_ref, kv_ref, p0, p1, p2, r_ref, ot_ref, o_ref, m_ref, h_ref, gp_ref, a_ref, c_ref = kept
    qst_ref, vt_ref, mask_ref, wqt_ref, u_ref, y_ref = work
    for rows in tiles(SEQ, TILE):
        a_ref[rows] = (normalise(x_ref[rows])[0] * vec[0:1] + vec[1:2]).astype(BF16)
    a_ref[SEQ:KEYS] = jnp.zeros((KEYS - SEQ, D), BF16)
    kv_ref[0:SEQ] = dot_nn(a_ref[0:SEQ], w_ref[:, 256:768]).astype(BF16)
    kv_ref[SEQ:KEYS] = jnp.zeros((KEYS - SEQ, 512), BF16)
    qt_ref[...] = dot_nt(wqt_ref[...], a_ref[...]).astype(BF16)
    spread_heads(qt_ref, qst_ref)
    turned = jnp.transpose(kv_ref[:, 256:512])
    for h in range(HEADS):
        vt_ref[VALUE_ROWS * h : VALUE_ROWS * h + HEAD_DIM] = turned[head_rows(h)]
    for i, pt_ref in enumerate((p0, p1, p2)):
        seen, first = BLOCK * (i + 1), BLOCK * i
        scores = dot_nn(kv_ref[0:seen, 0:256], qst_ref[:, block_lanes(i)])
        last = scores[first:] + mask_ref[...]
        peak = jnp.max(last, axis=0, keepdims=True)
        if i:
            peak = jnp.maximum(peak, jnp.max(scores[0:first], axis=0, keepdims=True))
            pt_ref[0:first] = jnp.exp(scores[0:first] - peak).astype(BF16)
        pt_ref[first:seen] = jnp.exp(last - peak).astype(BF16)
        for h in range(HEADS):
            values = vt_ref[VALUE_ROWS * h : VALUE_ROWS * (h + 1), 0:seen]
            out = dot_nn(values, pt_ref[:, BLOCK * h : BLOCK * (h + 1)])
            inverse = 1.0 / out[HEAD_DIM : HEAD_DIM + 1]
            r_ref[h : h + 1, first:seen] = inverse
            ot_ref[head_rows(h), first:seen] = (out[0:HEAD_DIM] * inverse).astype(BF16)
    o_ref[...] = jnp.transpose(ot_ref[...])[0:SEQ]
    y_ref[...] = dot_nt(o_ref[...], w_ref[:, COL_PROJ : COL_PROJ + 256])
    for rows in tiles(SEQ, TILE):
        middle = x_ref[rows] + (y_ref[rows] + vec[2:3])
        m_ref[rows] = middle
        c_ref[rows] = (normalise(middle)[0] * vec[3:4] + vec[4:5]).astype(BF16)
    u_ref[...] = dot_nn(c_ref[...], w_ref[:, COL_UP : COL_UP + FF])
    for rows in tiles(SEQ, TILE):
        for first in range(0, FF, 256):
            cols = slice(first, first + 256)
            h_ref[rows, cols], gp_ref[rows, cols] = gelu_and_slope(u_ref[rows, cols] + bias[:, cols])
    y_ref[...] = dot_nt(h_ref[...], w_ref[:, COL_DOWN : COL_DOWN + FF])


def add_gradient(g_ref, column, left, right):
    g_ref[:, column : column + right.shape[1]] += dot_tn(left, right)


def ff_backward(grad_ref, grad16_ref, w_ref, w_up, w_down, vec, kept, g_ref, g_up, g_down, v_ref, v_row, bias_row, work, mid_ref, mid16_ref):
    m_ref, h_ref, gp_ref, c_ref = kept
    du_ref, ones_ref, u_ref, y_ref = work
    u_ref[...] = dot_nn(grad16_ref[...], w_ref[:, w_down : w_down + FF])
    for rows in tiles(SEQ, TILE):
        du_ref[rows] = u_ref[rows].astype(BF16) * gp_ref[rows]
    add_gradient(g_ref, g_down, grad16_ref[...], h_ref[...])
    add_gradient(g_ref, g_up, c_ref[...], du_ref[...])
    bias_grad = dot_nn(ones_ref[...], du_ref[...])
    for chunk in range(4):
        v_ref[bias_row + chunk, 0:1] += bias_grad[0:1, 256 * chunk : 256 * chunk + 256]
    y_ref[...] = dot_nt(du_ref[...], w_ref[:, w_up : w_up + FF])
    totals = [None] * 3
    for rows in tiles(SEQ, TILE):
        xhat, scale = normalise(m_ref[rows])
        grad = y_ref[rows]
        mid = grad_ref[rows] + normalise_back(grad, xhat, scale, vec[3:4])
        mid_ref[rows] = mid
        if mid16_ref is not None:
            mid16_ref[rows] = mid.astype(BF16)
        for i, a in enumerate((mid, grad * xhat, grad)):
            totals[i] = plus(totals[i], fold(a))
    for i in range(3):
        v_ref[v_row + 2 + i] += totals[i]


def attention_backward(mid_ref, mid16_ref, w_ref, vec, kept, g_ref, v_ref, v_row, work, out_ref):
    x_ref, qt_ref, kv_ref, p0, p1, p2, r_ref, ot_ref, o_ref, a_ref = kept
    dost_ref, qst_ref, kt_ref, dst_ref, dqt_ref, dkv_ref, dqkv_ref, proj_ref, y_ref = work
    add_gradient(g_ref, COL_PROJ, mid16_ref[0:SEQ], o_ref[...])
    grad_o = dot_nt(proj_ref[...], mid16_ref[...]).astype(BF16).astype(F32)
    kt_ref[...] = jnp.transpose(kv_ref[:, 0:256])
    deltas = []
    for h in range(HEADS):
        scaled = grad_o[head_rows(h)] * r_ref[h : h + 1]
        deltas.append(column_sum(scaled * ot_ref[head_rows(h)].astype(F32)))
        scaled = scaled.astype(BF16)
        for i in range(BLOCKS):
            dost_ref[head_rows(h), block_lanes(i, h)] = scaled[:, BLOCK * i : BLOCK * (i + 1)]
    for i, pt_ref in enumerate((p0, p1, p2)):
        seen, first = BLOCK * (i + 1), BLOCK * i
        lanes = block_lanes(i)
        delta = jnp.concatenate([a[:, first:seen] for a in deltas], axis=1)
        grad = dot_nn(kv_ref[0:seen, 256:512], dost_ref[:, lanes])
        dst_ref[0:seen, lanes] = pt_ref[...] * (grad - delta).astype(BF16)
        for h in range(HEADS):
            out = dot_nn(kt_ref[head_rows(h), 0:seen], dst_ref[0:seen, block_lanes(i, h)])
            dqt_ref[head_rows(h), first:seen] = out.astype(BF16)
        for at, left, right in (
            (0, dst_ref[0:seen, lanes], qst_ref),
            (256, pt_ref[...], dost_ref),
        ):
            out = dot_nt(left, right[:, lanes])
            if i:
                dkv_ref[0:first, at : at + 256] += out[0:first]
            dkv_ref[first:seen, at : at + 256] = out[first:]
    dqkv_ref[:, 0:256] = jnp.transpose(dqt_ref[...])[0:SEQ]
    dqkv_ref[:, 256:768] = dkv_ref[0:SEQ].astype(BF16)
    add_gradient(g_ref, COL_QKV, a_ref[0:SEQ], dqkv_ref[...])
    y_ref[...] = dot_nt(dqkv_ref[...], w_ref[:, COL_QKV : COL_QKV + 768])
    totals = [None] * 2
    for rows in tiles(SEQ, TILE):
        xhat, scale = normalise(x_ref[rows])
        grad = y_ref[rows]
        out = mid_ref[rows] + normalise_back(grad, xhat, scale, vec[0:1])
        out_ref[rows] = out.astype(out_ref.dtype)
        for i, a in enumerate((grad * xhat, grad)):
            totals[i] = plus(totals[i], fold(a))
    for i in range(2):
        v_ref[v_row + i] += totals[i]


def own_bias(place_ref, mine, other):
    is_first = place_ref[1] == 0
    return jnp.concatenate(
        [jnp.where(is_first, mine, other), jnp.where(is_first, other, mine)], axis=1
    )


def prepare_kernel(
    place_ref, games_ref, tokens, actions, valid, rewards, ends, after, out, out_side, x_ref
):
    count = out.shape[0]
    frames = tokens.shape[2]
    base = place_ref[1] * count
    row = lax.broadcasted_iota(jnp.int32, (SEQ, frames), 0)
    start = lax.broadcasted_iota(jnp.int32, (SEQ, frames), 1) * FRAME_TOKENS
    here = jnp.where((row >= start) & (row < start + FRAME_TOKENS), 1.0, 0.0).astype(BF16)
    coming = jnp.where((row >= start - FRAME_TOKENS) & (row < start), 1.0, 0.0).astype(BF16)
    passed = jnp.sum(jnp.where(row >= start + FRAME_TOKENS, 1, 0), axis=1, keepdims=True)
    place = lax.broadcasted_iota(jnp.int32, (SEQ, 1), 0)
    spot = place - passed * FRAME_TOKENS
    lane = lax.broadcasted_iota(jnp.int32, (SEQ, 24), 1)
    wide_lane = lax.broadcasted_iota(jnp.int32, (SEQ, 128), 1)
    inside = place < LENGTH
    one_frame = (
        lax.broadcasted_iota(jnp.int32, (SIDE_ROWS, frames), 0)
        == lax.broadcasted_iota(jnp.int32, (SIDE_ROWS, frames), 1)
    )
    one_frame = jnp.where(one_frame, 1.0, 0.0).astype(BF16)
    side_lane = lax.broadcasted_iota(jnp.int32, (SIDE_ROWS, 128), 1)
    x_ref[...] = jnp.zeros(x_ref.shape, jnp.int32)
    for s in range(count):
        x_ref[0:OBS] = tokens[base + s]
        x_ref[16:17] = actions[pl.ds(base + s, 1)] + VOCAB
        x_ref[17:18] = valid[pl.ds(base + s, 1)]
        x_ref[18:19] = rewards[pl.ds(base + s, 1)]
        x_ref[19:20] = ends[pl.ds(base + s, 1)] + 3
        high = (x_ref[...] >> 4).astype(F32).astype(BF16)
        low = (x_ref[...] & 15).astype(F32).astype(BF16)
        now = dot_nt(here, high) * 16.0 + dot_nt(here, low)
        soon = dot_nt(coming, high) * 16.0 + dot_nt(coming, low)

        def pick(condition, a):
            return jnp.sum(jnp.where(condition, a, 0.0), axis=1, keepdims=True).astype(jnp.int32)

        ids = jnp.where(inside, pick(lane == spot, now), -1)
        game = jnp.where(inside, games_ref[base + s] + (VOCAB + ACTIONS), -1)
        target = pick((lane == spot + 1) & (spot < 15), now)
        target = target + pick((lane == 0) & (spot == 16), soon)
        weight = pick((lane == 17) & (spot < 15), now) + pick((lane == 17) & (spot == 16), soon)
        result = jnp.zeros((SEQ, 128), jnp.int32)
        for c, column in enumerate((ids, game, target, weight)):
            result = jnp.where(wide_lane == c, column, result)
        out[s] = result
        by_frame = dot_nt(one_frame, high) * 16.0 + dot_nt(one_frame, low)
        result = jnp.zeros((SIDE_ROWS, 128), jnp.int32)
        for c in range(3):
            column = by_frame[:, 17 + c : 18 + c].astype(jnp.int32)
            result = jnp.where(side_lane == c, column, result)
        out_side[s] = result


def start_forward(work, w_ref):
    qst_ref, vt_ref, mask_ref, wqt_ref, u_ref, y_ref = work
    qst_ref[...] = jnp.zeros(qst_ref.shape, BF16)
    vt_ref[...] = jnp.ones(vt_ref.shape, BF16)
    mask_ref[...] = causal_mask()
    wqt_ref[...] = jnp.transpose(w_ref[:, 0:256])


def first_forward_kernel(*refs):
    place_ref, meta_ref, vec_ref, bias_ref, bias_other = refs[0:5]
    mine, other = refs[5:9], refs[9:13]
    w_attention, w_ff, side_out, next_ref, hits_ref, x_ref = refs[13:19]
    kept = [ref.at[0] for ref in refs[19:32]]
    w_ref = refs[32]
    work = refs[33:39]

    @pl.when(pl.program_id(0) == 0)
    def _():
        assemble(mine, other, place_ref, w_ref, HALF_FIRST)
        w_attention[...] = w_ref[:, 0:COL_UP]
        w_ff[...] = w_ref[:, COL_UP:COL_TABLE]
        side_out[...] = w_ref[:, COL_SMALL:]
        start_forward(work, w_ref)

    make_hits(meta_ref.at[0], hits_ref.at[0])
    x_ref[0] = dot_nt(hits_ref[0], w_ref[:, COL_TABLE : COL_TABLE + ROWS])
    bias = own_bias(place_ref, bias_ref[0:1], bias_other[0:1])
    vec = vec_ref[0:6]
    layer_forward(x_ref.at[0], w_ref, vec, bias, kept, work)
    for rows in tiles(SEQ, TILE):
        next_ref[0, rows] = kept[8][rows] + (work[5][rows] + vec[5:6])


def codebook_losses(logits, meta):
    weight = meta[:, 3:4].astype(F32)
    peak = jnp.max(logits, axis=1, keepdims=True)
    expanded = jnp.exp(logits - peak)
    total = jnp.sum(expanded, axis=1, keepdims=True)
    hit = lax.broadcasted_iota(jnp.int32, logits.shape, 1) == meta[:, 2:3]
    hit = jnp.where(hit, weight, 0.0)
    return weight * (peak + jnp.log(total)), hit, expanded * (weight / total) - hit


def side_losses(side, meta):
    lane = lax.broadcasted_iota(jnp.int32, side.shape, 1)
    is_reward, is_end = lane < 3, (lane == 3) | (lane == 4)
    is_side = lane < 5
    weight = meta[:, 0:1].astype(F32)
    reward_peak = jnp.max(jnp.where(is_reward, side, -1e30), axis=1, keepdims=True)
    end_peak = jnp.max(jnp.where(is_end, side, -1e30), axis=1, keepdims=True)
    shifted = jnp.where(is_side, side - jnp.where(is_reward, reward_peak, end_peak), 0.0)
    expanded = jnp.where(is_side, jnp.exp(shifted), 0.0)
    reward_total = jnp.sum(jnp.where(is_reward, expanded, 0.0), axis=1, keepdims=True)
    end_total = jnp.sum(jnp.where(is_end, expanded, 0.0), axis=1, keepdims=True)
    hit = (lane == meta[:, 1:2]) | (lane == meta[:, 2:3])
    picked = jnp.sum(jnp.where(hit, side, 0.0), axis=1, keepdims=True)
    terms = reward_peak + jnp.log(reward_total) + end_peak + jnp.log(end_total) - picked
    grad = expanded * jnp.where(is_reward, weight / reward_total, weight / end_total)
    return weight * terms, grad - jnp.where(hit, weight, 0.0), weight


def frame_ends(shape, frame_axis):
    frame = lax.broadcasted_iota(jnp.int32, shape, frame_axis)
    row = lax.broadcasted_iota(jnp.int32, shape, 1 - frame_axis)
    hit = (row == frame * FRAME_TOKENS + OBS) & (frame < FRAMES)
    return jnp.where(hit, 1.0, 0.0).astype(BF16)


def middle_kernel(*refs):
    place_ref, meta_ref, frame_ref, vec_ref, bias_ref, bias_other, side_ref, in_ref = refs[0:8]
    mine, other = refs[8:12], refs[12:16]
    grad_ref, keep_ref, send_ref, v_out, scalar_ref = refs[16:21]
    refs = refs[1:]
    w_ref, g_ref, v_ref = refs[20:23]
    kept = refs[23:36]
    m_ref, h_ref, gp_ref, a_ref, c_ref = kept[8:13]
    forward_work = refs[36:42]
    u_ref, y_ref = forward_work[4:6]
    backward_work = refs[42:49]
    proj_ref = refs[49]
    du_ref, ones_ref, up_ref, up16_ref, mid_ref, mid16_ref = refs[50:56]
    last_ref, final_ref, logit_ref, dlogit_ref, pick_ref, put_ref = refs[56:62]
    dost_ref = backward_work[0]
    step = pl.program_id(0)

    @pl.when(step == 0)
    def _():
        assemble(mine, other, place_ref, w_ref, HALF_SECOND)
        w_ref[:, COL_SECOND:] = side_ref[...]
        g_ref[...] = jnp.zeros(g_ref.shape, F32)
        v_ref[...] = jnp.zeros(v_ref.shape, F32)
        scalar_ref[...] = jnp.zeros(scalar_ref.shape, F32)
        start_forward(forward_work, w_ref)
        dost_ref[...] = jnp.zeros(dost_ref.shape, BF16)
        proj_ref[...] = jnp.transpose(w_ref[:, COL_PROJ : COL_PROJ + 256])
        ones_ref[...] = jnp.ones(ones_ref.shape, BF16)
        mid16_ref[SEQ:KEYS] = jnp.zeros((KEYS - SEQ, D), BF16)
        pick_ref[...] = frame_ends((SIDE_ROWS, SEQ), 0)
        put_ref[...] = frame_ends((SEQ, SIDE_ROWS), 1)

    x_ref = in_ref.at[0]
    vec = vec_ref[6:12]
    bias = own_bias(place_ref, bias_ref[1:2], bias_other[1:2])
    layer_forward(x_ref, w_ref, vec, bias, kept, forward_work)

    gain, offset = vec_ref[12:13], vec_ref[13:14]
    for rows in tiles(SEQ, TILE):
        last = m_ref[rows] + (y_ref[rows] + vec[5:6])
        last_ref[rows] = last
        final_ref[rows] = (normalise(last)[0] * gain + offset).astype(BF16)
    cols_head = slice(COL_HEAD, COL_HEAD + VOCAB + 128)
    logit_ref[...] = dot_nn(final_ref[...], w_ref[:, COL_HEAD : COL_HEAD + VOCAB])
    logs, picked = None, None
    for rows in tiles(SEQ, TILE):
        logits = logit_ref[rows]
        log, hit, grad = codebook_losses(logits, meta_ref[0, rows])
        dlogit_ref[rows, :VOCAB] = grad.astype(BF16)
        logs, picked = plus(logs, log), plus(picked, fold(hit * logits))
    acting = dot_nn(pick_ref[...], final_ref[...]).astype(BF16)
    side = dot_nn(acting, w_ref[:, COL_HEAD + VOCAB : COL_HEAD + VOCAB + 128])
    side_loss, grad, weight = side_losses(side, frame_ref[0])
    dlogit_ref[:, VOCAB:] = dot_nn(put_ref[...], grad.astype(BF16)).astype(BF16)
    loss = column_sum(logs) + column_sum(side_loss)
    loss = loss - jnp.sum(column_sum(picked), axis=1, keepdims=True)
    valid = column_sum(weight)
    scalar_lane = lax.broadcasted_iota(jnp.int32, (8, 128), 1)
    scalar_row = lax.broadcasted_iota(jnp.int32, (8, 128), 0) == 0
    scalar_ref[...] += jnp.where(
        scalar_row,
        jnp.where(scalar_lane == 0, loss, jnp.where(scalar_lane == 1, valid, 0.0)),
        0.0,
    )
    add_gradient(g_ref, COL_HEAD, final_ref[...], dlogit_ref[...])
    y_ref[...] = dot_nt(dlogit_ref[...], w_ref[:, cols_head])
    totals = [None] * 3
    for rows in tiles(SEQ, TILE):
        xhat, scale = normalise(last_ref[rows])
        grad = y_ref[rows]
        up = normalise_back(grad, xhat, scale, gain)
        up_ref[rows] = up
        up16_ref[rows] = up.astype(BF16)
        for i, a in enumerate((up, grad * xhat, grad)):
            totals[i] = plus(totals[i], fold(a))
    for i in range(3):
        v_ref[11 + i] += totals[i]
    ff_backward(
        up_ref,
        up16_ref,
        w_ref,
        COL_UP,
        COL_DOWN,
        vec,
        (m_ref, h_ref, gp_ref, c_ref),
        g_ref,
        COL_UP,
        COL_DOWN,
        v_ref,
        6,
        SMALL_BIAS + 4,
        (du_ref, ones_ref, u_ref, y_ref),
        mid_ref,
        mid16_ref,
    )
    attention_backward(
        mid_ref,
        mid16_ref,
        w_ref,
        vec,
        (x_ref,) + tuple(kept[0:8]) + (a_ref,),
        g_ref,
        v_ref,
        6,
        (dost_ref, forward_work[0]) + tuple(backward_work[2:]) + (proj_ref, y_ref),
        grad_ref.at[0],
    )

    @pl.when(step == pl.num_programs(0) - 1)
    def _():
        disperse(g_ref, place_ref, keep_ref, send_ref, HALF_SECOND)
        side = jnp.transpose(g_ref[:, COL_SECOND:])
        for i in range(5):
            v_ref[SMALL_SIDE + i, 0:1] = side[i : i + 1]
        v_out[...] = v_ref[...]


def ff_backward_kernel(*refs):
    place_ref, vec_ref, w_ref, grad_ref, v_in = refs[0:5]
    kept = [ref.at[0] for ref in refs[5:9]]
    mid_ref, keep_ref, send_ref, v_out = refs[9:13]
    g_ref, v_ref, grad16_ref = refs[13:16]
    work = refs[16:20]
    ones_ref = work[1]
    step = pl.program_id(0)

    @pl.when(step == 0)
    def _():
        g_ref[...] = jnp.zeros(g_ref.shape, F32)
        v_ref[...] = v_in[...]
        ones_ref[...] = jnp.ones(ones_ref.shape, BF16)

    total = None
    for rows in tiles(SEQ, TILE):
        grad = grad_ref[0, rows]
        grad16_ref[rows] = grad.astype(BF16)
        total = plus(total, fold(grad))
    v_ref[5] += total
    ff_backward(
        grad_ref.at[0],
        grad16_ref,
        w_ref,
        GRAD_UP,
        GRAD_DOWN,
        vec_ref[0:6],
        kept,
        g_ref,
        GRAD_UP,
        GRAD_DOWN,
        v_ref,
        0,
        SMALL_BIAS,
        work,
        mid_ref.at[0],
        None,
    )

    @pl.when(step == pl.num_programs(0) - 1)
    def _():
        disperse(g_ref, place_ref, keep_ref, send_ref, HALF_GRAD_FF, False)
        v_out[...] = v_ref[...]


def attention_backward_kernel(*refs):
    place_ref, vec_ref, w_ref, mid_ref, hits_ref, v_in = refs[0:6]
    kept = [ref.at[0] for ref in refs[6:16]]
    keep_ref, send_ref, v_out = refs[17:20]
    g_ref, v_ref, mid16_ref, out16_ref = refs[20:24]
    work = refs[24:33]
    dost_ref, qst_ref, proj_ref = work[0], work[1], work[7]
    step = pl.program_id(0)

    @pl.when(step == 0)
    def _():
        g_ref[...] = jnp.zeros(g_ref.shape, F32)
        v_ref[...] = v_in[...]
        dost_ref[...] = jnp.zeros(dost_ref.shape, BF16)
        qst_ref[...] = jnp.zeros(qst_ref.shape, BF16)
        proj_ref[...] = jnp.transpose(w_ref[:, COL_PROJ : COL_PROJ + 256])
        mid16_ref[SEQ:KEYS] = jnp.zeros((KEYS - SEQ, D), BF16)

    spread_heads(kept[1], qst_ref)
    for rows in tiles(SEQ, TILE):
        mid16_ref[rows] = mid_ref[0, rows].astype(BF16)
    attention_backward(
        mid_ref.at[0], mid16_ref, w_ref, vec_ref[0:6], kept, g_ref, v_ref, 0, work, out16_ref
    )
    add_gradient(g_ref, GRAD_TABLE, out16_ref[...], hits_ref[0])

    @pl.when(step == pl.num_programs(0) - 1)
    def _():
        small = jnp.sum(v_ref[...], axis=1)
        v_out[...] = small
        for block in range(16):
            quarter = small[8 * (block // 4) : 8 * (block // 4) + 8]
            g_ref[16 * block : 16 * block + 8, GRAD_SMALL:] = quarter[:, 0:128]
            g_ref[16 * block + 8 : 16 * block + 16, GRAD_SMALL:] = quarter[:, 128:256]
        disperse(g_ref, place_ref, keep_ref, send_ref, HALF_GRAD_REST)


def pack_layer(attn, proj, up, down, layer, out):
    for j in range(3):
        out[:, 128 * j : 128 * j + 128] = attn[layer, j].astype(BF16)
    out[:, 384:512] = proj[layer].astype(BF16)
    out[:, 512:1024] = up[layer].astype(BF16)
    out[:, 1024:1536] = down[layer].astype(BF16)


def pack_kernel(place_ref, table, attn, proj, up, down, head, side, first, second, pad_ref):
    pack_layer(attn, proj, up, down, 0, first)
    pack_layer(attn, proj, up, down, 1, second)
    second[:, 1536:1792] = head[...].astype(BF16)
    rows = side.shape[1]
    eye = (
        lax.broadcasted_iota(jnp.int32, (rows, rows), 0)
        == lax.broadcasted_iota(jnp.int32, (rows, rows), 1)
    )
    eye = jnp.where(eye, 1.0, 0.0).astype(BF16)
    pad_ref[...] = jnp.zeros(pad_ref.shape, F32)
    pad_ref[:, 0:5] = dot_nt(eye, side[...].astype(BF16))
    high = jnp.concatenate([table[:, 512:896], pad_ref[...]], axis=1)
    first[:, 1536:2048] = jnp.where(place_ref[1] == 0, table[:, 0:512], high).astype(BF16)


def finish_kernel(*refs):
    count = (len(refs) - 6) // 2
    place_ref = refs[0]
    scalar_ref = refs[2 * count + 1]
    out_rest, out_other, out_table, out_small = refs[2 * count + 2 :]
    square = jnp.zeros((1, 1), F32)
    for pieces, out in ((refs[1 : count + 1], out_rest), (refs[count + 1 : 2 * count + 1], out_other)):
        total = pieces[0][...]
        for piece in pieces[1:]:
            total = total + piece[...].astype(F32)
        out[...] = total
        square = square + column_sum(jnp.sum(total * total, axis=1, keepdims=True))
    small = out_rest[:, 896:1024]
    extra = column_sum(jnp.sum(small * small, axis=1, keepdims=True))
    square = square - jnp.where(place_ref[1] == 0, 0.0, extra)
    out_table[...] = out_rest[:, 512:1024]
    rows = small.shape[0]
    out_small[0:rows] = small
    lane = lax.broadcasted_iota(jnp.int32, (8, 128), 1)
    top = lax.broadcasted_iota(jnp.int32, (8, 128), 0) == 0
    out_small[rows : rows + 8] = scalar_ref[...] + jnp.where(top & (lane == 2), square, 0.0)


def adam_rule(weight, moment, second, gradient, step_rate, decay_rate):
    moment_new = BETA_ONE * moment + (1.0 - BETA_ONE) * gradient
    second_new = BETA_TWO * second + (1.0 - BETA_TWO) * gradient * gradient
    moment_hat = moment_new / (1.0 - BETA_ONE**STEP_NUMBER)
    second_hat = second_new / (1.0 - BETA_TWO**STEP_NUMBER)
    weight_new = weight - step_rate * (
        moment_hat / (jnp.sqrt(second_hat) + EPS_ADAM) + decay_rate * weight
    )
    return (weight_new, moment_new, second_new)


def adam_kernel(fast, place_ref, rest, others, swapped, gathered, *refs):
    rows = rest.shape[0]
    quarters = [gathered.at[4 * z] for z in range(4)] if fast else [refs[0].at[z] for z in range(4)]
    refs = refs if fast else refs[1:]
    params = [refs[3 * i : 3 * i + 3] for i in range(9)]
    loss_ref, valid_ref, norm_ref = refs[27:30]
    outs = [refs[30 + 3 * i : 33 + 3 * i] for i in range(9)]
    small_ref = refs[57]
    wide = place_ref[2]
    is_first = place_ref[1] == 0
    for z in range(4):
        small_ref[8 * z : 8 * z + 8, 0:128] = quarters[z][0:8]
        small_ref[8 * z : 8 * z + 8, 128:256] = quarters[z][8:16]
    scalars = gathered[0, rows : rows + 1]
    for i in range(1, gathered.shape[0]):
        scalars = scalars + gathered[i, rows : rows + 1]
    small = small_ref[...]
    loss, valid, square = scalars[:, 0:1], scalars[:, 1:2], scalars[:, 2:3]
    square = square + column_sum(jnp.sum(small * small, axis=1, keepdims=True))
    inverse = 1.0 / valid
    norm = jnp.sqrt(square) * inverse
    loss_ref[...], valid_ref[...], norm_ref[...] = loss, valid, norm
    factor = jnp.minimum(1.0, CLIP_AT / (norm + 1e-06)) * inverse
    table, attn, proj, up, bias, down, vectors, head, side = range(9)

    def update(which, index, gradient, step_rate, decay_rate):
        news = adam_rule(
            *(ref[index] for ref in params[which]), factor * gradient, step_rate, decay_rate
        )
        for ref, new in zip(outs[which], news):
            ref[index] = new

    layers = ((rest, others, 1792), (others, others, 512))
    for layer, (attention, feed, at) in enumerate(layers):
        for j in range(3):
            update(attn, (layer, j), attention[:, 128 * j : 128 * j + 128], RATE_MATRIX, DECAY_RATE)
        update(proj, (layer,), attention[:, 384:512], RATE_MATRIX, DECAY_RATE)
        update(up, (layer,), feed[:, at : at + 512], RATE_MATRIX, DECAY_RATE)
        update(down, (layer,), feed[:, at + 512 : at + 1024], RATE_MATRIX, DECAY_RATE)
        for i in range(2):
            low = SMALL_BIAS + 4 * layer + i
            row = jnp.where(is_first, small[low : low + 1], small[low + 2 : low + 3])
            index = (slice(layer, layer + 1), slice(256 * i, 256 * i + 256))
            update(bias, index, row, RATE_VECTOR, 0.0)
    whole = (slice(None), slice(None))
    update(head, whole, others[:, 1536:1792], RATE_MATRIX, DECAY_RATE)
    mine, theirs = rest[:, 512:1024], swapped[:, 0:512]
    low, high = jnp.where(is_first, mine, theirs), jnp.where(is_first, theirs, mine)
    update(table, (slice(None), slice(0, 512)), low, RATE_TABLE, DECAY_RATE)
    update(table, (slice(None), slice(512, 896)), high[:, 0:384], RATE_TABLE, DECAY_RATE)
    update(vectors, whole, small[0:NVEC], RATE_VECTOR, 0.0)
    turned = pltpu.roll(small[SMALL_SIDE : SMALL_SIDE + 8], lax.rem(D - wide * rows, D), 1)
    update(side, whole, turned[0:5, 0:rows], RATE_MATRIX, DECAY_RATE)


def swap(a, axis, distance):
    size = lax.axis_size(axis)
    return lax.ppermute(a, axis, [(i, i ^ distance) for i in range(size)])


def swap_column(piece, n_high):
    return [piece] + [swap(piece, "wide", 4 * k) for k in range(1, n_high)]


def gather_plane(column):
    return [column] + [swap(column, "wide", p) for p in range(1, 4)]


def gather_cores(mine):
    return [swap(a, "narrow", 1) for a in mine]


def in_blocks(parts, wide):
    n_high, rows, cols = parts[0].shape
    if rows == 16:
        return parts
    whole = jnp.stack(parts, axis=1).reshape(4 * n_high, rows, cols)
    whole = whole[wide ^ jnp.arange(4 * n_high)].reshape(4, 4, 16, cols)
    return [whole[:, p] for p in range(4)]


def in_pieces(blocks, wide, n_high):
    cols = blocks.shape[-1]
    if n_high == 4:
        return blocks
    rows = 64 // n_high
    whole = blocks.transpose(1, 0, 2, 3).reshape(4 * n_high, rows, cols)
    whole = whole[wide ^ jnp.arange(4 * n_high)]
    return whole.reshape(n_high, 4, rows, cols).transpose(1, 0, 2, 3)


def add_cores(keep, send, wide, n_high):
    keep, send = in_pieces(keep, wide, n_high), in_pieces(send, wide, n_high)
    received = swap(send, "narrow", 1)
    return [keep[p].astype(F32) + received[p].astype(F32) for p in range(4)]


def swap_plane(sums):
    return [swap(sums[p].astype(BF16), "wide", p) for p in range(1, 4)]


def add_plane(own, received):
    for a in received:
        own = own + a.astype(F32)
    return own


def column_pieces(own):
    return [own[0]] + [swap(own[k].astype(BF16), "wide", 4 * k) for k in range(1, own.shape[0])]


def resident(arrays):
    return [pltpu.with_memory_space_constraint(a, pltpu.VMEM) for a in arrays]


def full_spec(a):
    return pl.BlockSpec(a.shape, lambda *_: (0,) * len(a.shape))


def row_spec(shape):
    return pl.BlockSpec((1,) + shape, lambda i: (i,) + (0,) * len(shape))


def shaped(shape, dtype):
    return jax.ShapeDtypeStruct(shape, dtype)


VMEM_SPEC = pl.BlockSpec(memory_space=pltpu.VMEM)
ANY_SPEC = pl.BlockSpec(memory_space=pl.ANY)
SMEM_SPEC = pl.BlockSpec(memory_space=pltpu.SMEM)


VMEM_MIB = {
    "pack": 58,
    "prepare": 58,
    "first_forward": 36,
    "middle": 34,
    "ff_backward": 30,
    "attention_backward": 30,
    "finish": 58,
    "adam": 58,
}


def call(kernel, grid, in_specs, out_specs, out_shape, scratch, flops, bytes_accessed, name):
    extra = {"grid": grid} if grid else {}
    return pl.pallas_call(
        kernel,
        in_specs=in_specs,
        out_specs=out_specs,
        out_shape=out_shape,
        scratch_shapes=scratch,
        compiler_params=pltpu.CompilerParams(vmem_limit_bytes=VMEM_MIB[name] * MIB),
        cost_estimate=pl.CostEstimate(
            flops=flops, bytes_accessed=bytes_accessed, transcendentals=0
        ),
        name=name,
        **extra,
    )


KEPT = (
    ((D, KEYS), BF16),
    ((KEYS, 512), BF16),
    ((BLOCK, QUERIES), BF16),
    ((2 * BLOCK, QUERIES), BF16),
    ((3 * BLOCK, QUERIES), BF16),
    ((8, KEYS), F32),
    ((D, KEYS), BF16),
    ((SEQ, D), BF16),
    ((SEQ, D), F32),
    ((SEQ, FF), BF16),
    ((SEQ, FF), BF16),
    ((KEYS, D), BF16),
    ((SEQ, D), BF16),
)
FORWARD_WORK = [
    pltpu.VMEM((D, BLOCKS * QUERIES), BF16),
    pltpu.VMEM((HEADS * VALUE_ROWS, KEYS), BF16),
    pltpu.VMEM((BLOCK, QUERIES), F32),
    pltpu.VMEM((D, D), BF16),
    pltpu.VMEM((SEQ, FF), F32),
    pltpu.VMEM((SEQ, D), F32),
]
BACKWARD_WORK = [
    pltpu.VMEM((D, BLOCKS * QUERIES), BF16),
    pltpu.VMEM((D, BLOCKS * QUERIES), BF16),
    pltpu.VMEM((D, KEYS), BF16),
    pltpu.VMEM((KEYS, BLOCKS * QUERIES), BF16),
    pltpu.VMEM((D, KEYS), BF16),
    pltpu.VMEM((KEYS, 512), F32),
    pltpu.VMEM((SEQ, 768), BF16),
]
PROJ_WORK = pltpu.VMEM((D, D), BF16)
ONES_WORK = pltpu.VMEM((16, SEQ), BF16)


def per_device(
    tokens,
    actions,
    game_ids,
    valid_steps,
    rewards,
    end_flags,
    embed_table,
    table_first,
    table_second,
    attn_weight,
    attn_first,
    attn_second,
    proj_weight,
    proj_first,
    proj_second,
    up_weight,
    up_first,
    up_second,
    up_bias,
    bias_first,
    bias_second,
    down_weight,
    down_first,
    down_second,
    vectors,
    vectors_first,
    vectors_second,
    head_weight,
    head_first,
    head_second,
    side_weight,
    side_first,
    side_second,
):
    n_high = lax.axis_size("wide") // 4
    wide, core = lax.axis_index("wide"), lax.axis_index("narrow")
    rows = side_weight.shape[0]
    fast = rows == 16
    place = jnp.stack([wide if fast else jnp.zeros_like(wide), core, wide]).astype(jnp.int32)

    def flat(a):
        return jnp.swapaxes(a, -1, -2)

    params = (
        (flat(embed_table), flat(table_first), flat(table_second)),
        (attn_weight, attn_first, attn_second),
        (flat(proj_weight), flat(proj_first), flat(proj_second)),
        (up_weight, up_first, up_second),
        (up_bias, bias_first, bias_second),
        (flat(down_weight), flat(down_first), flat(down_second)),
        (vectors, vectors_first, vectors_second),
        (head_weight, head_first, head_second),
        (flat(side_weight), flat(side_first), flat(side_second)),
    )
    table, attn, proj, up, _, down, _, head, side = (group[0] for group in params)

    piece_first, piece_second = call(
        pack_kernel,
        None,
        [SMEM_SPEC] + [VMEM_SPEC] * 7,
        [VMEM_SPEC] * 2,
        [shaped((rows, HALF_FIRST_COLS), BF16), shaped((rows, HALF_SECOND_COLS), BF16)],
        [pltpu.VMEM((rows, 128), F32)],
        10**6,
        10**6,
        "pack",
    )(place, table, attn, proj, up, down, head, side)
    other_bias = swap(up_bias, "narrow", 1)
    column = swap_column(piece_first, n_high)

    count = tokens.shape[0] // lax.axis_size("narrow")
    meta, frame_meta = call(
        prepare_kernel,
        None,
        [SMEM_SPEC] * 2 + [VMEM_SPEC] * 5 + [ANY_SPEC],
        [VMEM_SPEC] * 2,
        [shaped((count, SEQ, 128), jnp.int32), shaped((count, SIDE_ROWS, 128), jnp.int32)],
        [pltpu.VMEM((24, FRAMES), jnp.int32)],
        10**6,
        10**6,
        "prepare",
    )(place, game_ids, flat(tokens), actions, valid_steps, rewards, end_flags, piece_first)
    column, meta, other_bias = lax.optimization_barrier((column, meta, other_bias))
    first_column = jnp.stack(column)
    beside, above = swap(first_column, "wide", 1), swap(first_column, "wide", 2)
    beside, first_column, piece_second = lax.optimization_barrier(
        (beside, first_column, piece_second)
    )
    across = swap(first_column, "wide", 3)
    second_column = jnp.stack(swap_column(piece_second, n_high))
    second_column, across = lax.optimization_barrier((second_column, across))
    first_mine = [first_column, beside, above, across]
    first_other = gather_cores(first_mine)
    second_mine = gather_plane(second_column)
    first_parts = in_blocks(first_mine, wide) + in_blocks(first_other, wide)

    kept_specs = [row_spec(shape) for shape, _ in KEPT]
    kept_shapes = [shaped((count,) + shape, dtype) for shape, dtype in KEPT]
    row_f32 = shaped((count, SEQ, D), F32)
    meta_spec = row_spec((SEQ, 128))
    vec_specs = [full_spec(vectors), full_spec(up_bias), full_spec(up_bias)]
    w_attention_spec = pl.BlockSpec((D, 1024), lambda i: (0, 0))
    w_ff_spec = pl.BlockSpec((D, 2048), lambda i: (0, 0))
    side_spec = pl.BlockSpec((D, 128), lambda i: (0, 0))
    hits_spec = row_spec((SEQ, ROWS))
    results = call(
        first_forward_kernel,
        (count,),
        [SMEM_SPEC, meta_spec] + vec_specs + [VMEM_SPEC] * 8,
        [w_attention_spec, w_ff_spec, side_spec, row_spec((SEQ, D)), hits_spec, row_spec((SEQ, D))]
        + kept_specs,
        [shaped((D, 1024), BF16), shaped((D, 2048), BF16), shaped((D, 128), BF16), row_f32]
        + [shaped((count, SEQ, ROWS), BF16), row_f32]
        + kept_shapes,
        [pltpu.VMEM((D, COL_FIRST), BF16)] + FORWARD_WORK,
        4 * 10**9,
        20 * 10**6,
        "first_forward",
    )(place, meta, vectors, up_bias, other_bias, *resident(first_parts))
    w_attention, w_ff, side_copy, stream, hits, stream_first = results[0:6]
    kept = results[6:]
    received, side_copy = lax.optimization_barrier((second_mine[1:], side_copy))
    second_mine = second_mine[0:1] + received
    second_other = gather_cores(second_mine)
    second_parts = in_blocks(second_mine, wide) + in_blocks(second_other, wide)

    def blocks(cols):
        return pl.BlockSpec((4, 4, 16, cols), lambda i: (0, 0, 0, 0))

    def block_shapes(cols):
        return [shaped((4, 4, 16, cols), BF16)] * 2

    small_spec = pl.BlockSpec((SMALL_ROWS, 8, D), lambda i: (0, 0, 0))
    small_shape = shaped((SMALL_ROWS, 8, D), F32)
    small_scratch = pltpu.VMEM((SMALL_ROWS, 8, D), F32)
    scalar_spec = pl.BlockSpec((8, 128), lambda i: (0, 0))
    grad_stream, keep_second, send_second, small_grads, scalars = call(
        middle_kernel,
        (count,),
        [SMEM_SPEC, meta_spec, row_spec((SIDE_ROWS, 128))]
        + vec_specs
        + [side_spec, row_spec((SEQ, D))]
        + [VMEM_SPEC] * 8,
        [row_spec((SEQ, D))] + [blocks(HALF_SECOND_COLS)] * 2 + [small_spec, scalar_spec],
        [row_f32] + block_shapes(HALF_SECOND_COLS) + [small_shape, shaped((8, 128), F32)],
        [
            pltpu.VMEM((D, COL_SECOND + 128), BF16),
            pltpu.VMEM((D, COL_SECOND + 128), F32),
            small_scratch,
        ]
        + [pltpu.VMEM(shape, dtype) for shape, dtype in KEPT]
        + FORWARD_WORK
        + BACKWARD_WORK
        + [
            PROJ_WORK,
            pltpu.VMEM((SEQ, FF), BF16),
            ONES_WORK,
            pltpu.VMEM((SEQ, D), F32),
            pltpu.VMEM((SEQ, D), BF16),
            pltpu.VMEM((SEQ, D), F32),
            pltpu.VMEM((KEYS, D), BF16),
            pltpu.VMEM((SEQ, D), F32),
            pltpu.VMEM((SEQ, D), BF16),
            pltpu.VMEM((SEQ, VOCAB), F32),
            pltpu.VMEM((SEQ, VOCAB + 128), BF16),
            pltpu.VMEM((SIDE_ROWS, SEQ), BF16),
            pltpu.VMEM((SEQ, SIDE_ROWS), BF16),
        ],
        15 * 10**9,
        20 * 10**6,
        "middle",
    )(place, meta, frame_meta, vectors, up_bias, other_bias, side_copy, stream, *resident(second_parts))
    second_sums = add_cores(keep_second, send_second, wide, n_high)

    kept_ff = (kept[8], kept[9], kept[10], kept[12])
    grad_mid, keep_ff, send_ff, small_grads = call(
        ff_backward_kernel,
        (count,),
        [SMEM_SPEC, full_spec(vectors), w_ff_spec, row_spec((SEQ, D)), small_spec]
        + [row_spec(a.shape[1:]) for a in kept_ff],
        [row_spec((SEQ, D))] + [blocks(HALF_GRAD_COLS)] * 2 + [small_spec],
        [row_f32] + block_shapes(HALF_GRAD_COLS) + [small_shape],
        [
            pltpu.VMEM((D, 2048), F32),
            small_scratch,
            pltpu.VMEM((SEQ, D), BF16),
            pltpu.VMEM((SEQ, FF), BF16),
            ONES_WORK,
            pltpu.VMEM((SEQ, FF), F32),
            pltpu.VMEM((SEQ, D), F32),
        ],
        4 * 10**9,
        10 * 10**6,
        "ff_backward",
    )(place, vectors, w_ff, grad_stream, small_grads, *kept_ff)
    ff_sums = add_cores(keep_ff, send_ff, wide, n_high)
    other_sums = [jnp.concatenate(pair, axis=-1) for pair in zip(second_sums, ff_sums)]
    others_received = swap_plane(other_sums)
    kept_attention = (stream_first,) + tuple(kept[0:8]) + (kept[11],)
    keep_rest, send_rest, small_grads = call(
        attention_backward_kernel,
        (count,),
        [SMEM_SPEC, full_spec(vectors), w_attention_spec, row_spec((SEQ, D)), hits_spec, small_spec]
        + [row_spec(a.shape[1:]) for a in kept_attention]
        + [ANY_SPEC],
        [blocks(HALF_GRAD_COLS)] * 2 + [pl.BlockSpec((SMALL_ROWS, D), lambda i: (0, 0))],
        block_shapes(HALF_GRAD_COLS) + [shaped((SMALL_ROWS, D), F32)],
        [pltpu.VMEM((D, 2048), F32), small_scratch]
        + [pltpu.VMEM((KEYS, D), BF16), pltpu.VMEM((SEQ, D), BF16)]
        + BACKWARD_WORK
        + [PROJ_WORK, pltpu.VMEM((SEQ, D), F32)],
        6 * 10**9,
        20 * 10**6,
        "attention_backward",
    )(place, vectors, w_attention, grad_mid, hits, small_grads, *kept_attention, other_sums[0])
    others_received, keep_rest = lax.optimization_barrier((others_received, keep_rest))
    rest_sums = add_cores(keep_rest, send_rest, wide, n_high)
    rest_received = swap_plane(rest_sums)
    other_pieces = column_pieces(add_plane(other_sums[0], others_received))
    rest_pieces = column_pieces(add_plane(rest_sums[0], rest_received))

    grad_rest, grad_others, table_part, small = call(
        finish_kernel,
        None,
        [SMEM_SPEC] + [VMEM_SPEC] * (2 * n_high + 1),
        [VMEM_SPEC] * 4,
        [
            shaped((rows, HALF_GRAD_COLS), F32),
            shaped((rows, HALF_GRAD_COLS + HALF_SECOND_COLS), F32),
            shaped((rows, 512), F32),
            shaped((rows + 8, 128), F32),
        ],
        [],
        10**6,
        10**6,
        "finish",
    )(place, *resident(rest_pieces + other_pieces), scalars)

    beside = swap(small, "narrow", 1)
    is_small = (jnp.arange(rows + 8) < rows)[:, None]
    small = jnp.where(is_small, jnp.where(core == 1, small, beside), small + beside)
    small = jnp.broadcast_to(small, (4 * n_high,) + small.shape)
    gathered = lax.all_to_all(small, "wide", 0, 0)
    quarters = []
    if not fast:
        total = lax.psum(small_grads, ("wide", "narrow"))
        quarters = [total.reshape(4, 8, 2, 128).transpose(0, 2, 1, 3).reshape(4, 16, 128)]
    swapped = swap(table_part, "narrow", 1)

    flat_params = [a for group in params for a in group]
    results = call(
        functools.partial(adam_kernel, fast),
        None,
        [SMEM_SPEC] + [VMEM_SPEC] * (31 + len(quarters)),
        [VMEM_SPEC] * 30,
        [shaped((1, 1), F32)] * 3 + [shaped(a.shape, F32) for a in flat_params],
        [pltpu.VMEM((SMALL_ROWS, D), F32)],
        10**6,
        10**6,
        "adam",
    )(place, grad_rest, grad_others, *resident([swapped, gathered]), *quarters, *flat_params)
    news = list(results[3:])
    for group in (0, 2, 5, 8):
        for member in range(3 * group, 3 * group + 3):
            news[member] = flat(news[member])
    return tuple(a.reshape(()) for a in results[0:3]) + tuple(news)


def solution(mesh):
    placed = (
        P("wide", None, None),
        P("wide", None),
        P("wide"),
        P("wide", None),
        P("wide", None),
        P("wide", None),
        P(None, "wide"),
        P(None, "wide"),
        P(None, "wide"),
        P(None, None, "wide", "narrow"),
        P(None, None, "wide", "narrow"),
        P(None, None, "wide", "narrow"),
        P(None, "narrow", "wide"),
        P(None, "narrow", "wide"),
        P(None, "narrow", "wide"),
        P(None, "wide", "narrow"),
        P(None, "wide", "narrow"),
        P(None, "wide", "narrow"),
        P(None, "narrow"),
        P(None, "narrow"),
        P(None, "narrow"),
        P(None, "narrow", "wide"),
        P(None, "narrow", "wide"),
        P(None, "narrow", "wide"),
        P(),
        P(),
        P(),
        P("wide", "narrow"),
        P("wide", "narrow"),
        P("wide", "narrow"),
        P("wide", None),
        P("wide", None),
        P("wide", None),
    )
    return jax.shard_map(
        per_device,
        mesh=mesh,
        in_specs=placed,
        out_specs=(P(), P(), P()) + placed[6:],
        check_vma=False,
    )
```

```python
import functools

import jax
import jax.numpy as jnp
from jax import lax
from jax.experimental import pallas as pl
from jax.experimental.pallas import tpu as pltpu
from jax.sharding import PartitionSpec as P

D = 256
HEADS = 4
HEAD_DIM = 64
FF = 1024
VOCAB = 512
ACTIONS = 18
GAMES = 26
OBS = 16
FRAMES = 20
STEP_NUMBER = 5
FRAME_TOKENS = 17
LENGTH = 340
ROWS = 896
NVEC = 14

EPS_NORM = 1e-05
BETA_ONE = 0.5
BETA_TWO = 0.5
RATE_TABLE = 0.5
RATE_MATRIX = 0.05
RATE_VECTOR = 0.2
DECAY_RATE = 0.01
EPS_ADAM = 1e-08
CLIP_AT = 0.1

SEQ = 352
KEYS = 384
BLOCK, BLOCKS = 128, 3
TILE = 32
SIDE_ROWS = 32
QUERIES = HEADS * BLOCK
VALUE_ROWS = 80

COL_QKV, COL_PROJ, COL_UP, COL_DOWN, COL_LAYER = 0, 768, 1024, 2048, 3072
HALF_ATTENTION = ((0, 128, 0), (128, 128, 256), (256, 128, 512), (384, 128, COL_PROJ))
HALF_LAYER = HALF_ATTENTION + ((512, 512, COL_UP), (1024, 512, COL_DOWN))
COL_TABLE, COL_SMALL, COL_FIRST = 3072, 3968, 4096
HALF_FIRST = HALF_LAYER + ((1536, 512, COL_TABLE),)
HALF_FIRST_COLS = 2048
COL_HEAD, COL_SECOND = 3072, 3584
HALF_SECOND = HALF_LAYER + ((1536, 256, COL_HEAD),)
HALF_SECOND_COLS = 1792
GRAD_UP, GRAD_DOWN = 0, 1024
HALF_GRAD_FF = ((0, 512, GRAD_UP), (512, 512, GRAD_DOWN))
GRAD_TABLE, GRAD_SMALL = 1024, 1920
HALF_GRAD_REST = HALF_ATTENTION + ((512, 512, GRAD_TABLE),)
HALF_GRAD_COLS = 1024
SMALL_ROWS, SMALL_BIAS, SMALL_SIDE = 32, 14, 22

F32, BF16 = jnp.float32, jnp.bfloat16
MIB = 1024 * 1024


def dot_nn(a, b):
    return lax.dot_general(a, b, (((1,), (0,)), ((), ())), preferred_element_type=F32)


def dot_nt(a, b):
    return lax.dot_general(a, b, (((1,), (1,)), ((), ())), preferred_element_type=F32)


def dot_tn(a, b):
    return lax.dot_general(a, b, (((0,), (0,)), ((), ())), preferred_element_type=F32)


def places(fast):
    wide, core = lax.axis_index("wide"), lax.axis_index("narrow")
    return (wide if fast else 0), core, wide


def tiles(rows, size):
    return [slice(first, first + size) for first in range(0, rows, size)]


def normalise(x):
    centred = x - jnp.mean(x, axis=1, keepdims=True)
    scale = lax.rsqrt(jnp.mean(centred * centred, axis=1, keepdims=True) + EPS_NORM)
    return centred * scale, scale


def normalise_back(grad, xhat, scale, gain):
    inner = grad * gain
    mean_one = jnp.mean(inner, axis=1, keepdims=True)
    mean_two = jnp.mean(inner * xhat, axis=1, keepdims=True)
    return scale * (inner - mean_one - xhat * mean_two)


def column_sum(a):
    return jnp.sum(a, axis=0, keepdims=True)


def fold(a):
    return jnp.sum(a.reshape(a.shape[0] // 8, 8, a.shape[1]), axis=0)


def plus(total, a):
    return a if total is None else total + a


def block_lanes(i, h=None):
    if h is None:
        return slice(QUERIES * i, QUERIES * (i + 1))
    return slice(QUERIES * i + BLOCK * h, QUERIES * i + BLOCK * (h + 1))


def head_rows(h):
    return slice(HEAD_DIM * h, HEAD_DIM * (h + 1))


def spread_heads(source, target_ref):
    for h in range(HEADS):
        for i in range(BLOCKS):
            target_ref[head_rows(h), block_lanes(i, h)] = source[
                head_rows(h), BLOCK * i : BLOCK * (i + 1)
            ]


def causal_mask():
    key = lax.broadcasted_iota(jnp.int32, (BLOCK, QUERIES), 0)
    query = lax.broadcasted_iota(jnp.int32, (BLOCK, QUERIES), 1) & (BLOCK - 1)
    return jnp.where(key <= query, 0.0, -1e30)


def assemble(pieces_mine, pieces_other, place, w_ref, halves):
    me, core, _ = place
    is_first = core == 0
    for p in range(4):

        def block(z, _, p=p):
            row = pl.multiple_of((me ^ (4 * z + p)) * 16, 16)
            for src, width, dest in halves:
                mine = pieces_mine[p][z, :, src : src + width]
                other = pieces_other[p][z, :, src : src + width]
                if dest == COL_QKV:
                    mine, other = mine * 0.125, other * 0.125
                w_ref[pl.ds(row, 16), dest : dest + width] = jnp.where(is_first, mine, other)
                w_ref[pl.ds(row, 16), dest + width : dest + 2 * width] = jnp.where(
                    is_first, other, mine
                )
            return 0

        lax.fori_loop(0, 4, block, 0)


def disperse(g_ref, place, keep_ref, send_ref, halves, scaled=True):
    me, core, _ = place
    is_first = core == 0

    def block(i, _):
        p, z = i >> 2, i & 3
        row = pl.multiple_of((me ^ (4 * z + p)) * 16, 16)
        for src, width, dest in halves:
            low = g_ref[pl.ds(row, 16), dest : dest + width]
            high = g_ref[pl.ds(row, 16), dest + width : dest + 2 * width]
            if scaled and dest == COL_QKV:
                low, high = low * 0.125, high * 0.125
            keep_ref[p, z, :, src : src + width] = jnp.where(is_first, low, high).astype(BF16)
            send_ref[p, z, :, src : src + width] = jnp.where(is_first, high, low).astype(BF16)
        return 0

    lax.fori_loop(0, 16, block, 0)


def make_hits(meta_ref, hits_ref):
    for rows in tiles(SEQ, TILE):
        lane = lax.broadcasted_iota(jnp.int32, (TILE, ROWS), 1)
        place = lax.broadcasted_iota(jnp.int32, (TILE, 1), 0) + (VOCAB + ACTIONS + GAMES + rows.start)
        meta = meta_ref[rows]
        hit = (lane == meta[:, 0:1]) | (lane == meta[:, 1:2]) | (lane == place)
        hits_ref[rows] = jnp.where(hit, 1.0, 0.0).astype(BF16)


def gelu_and_slope(up):
    up = up.astype(BF16)
    square = up * up
    half = jax.nn.sigmoid(up * (BF16(1.5957691216057308) + BF16(0.0713548162726) * square))
    hidden = up * half
    slope = BF16(1.5957691216057308) + BF16(0.2140644488178) * square
    return hidden, half + hidden * (BF16(1.0) - half) * slope


def layer_forward(x_ref, w_ref, vec, bias, kept, work):
    qt_ref, kv_ref, p0, p1, p2, r_ref, ot_ref, o_ref, m_ref, h_ref, gp_ref, a_ref, c_ref = kept
    qst_ref, vt_ref, mask_ref, wqt_ref, u_ref, y_ref = work
    for rows in tiles(SEQ, TILE):
        a_ref[rows] = (normalise(x_ref[rows])[0] * vec[0:1] + vec[1:2]).astype(BF16)
    a_ref[SEQ:KEYS] = jnp.zeros((KEYS - SEQ, D), BF16)
    kv_ref[0:SEQ] = dot_nn(a_ref[0:SEQ], w_ref[:, 256:768]).astype(BF16)
    kv_ref[SEQ:KEYS] = jnp.zeros((KEYS - SEQ, 512), BF16)
    qt_ref[...] = dot_nt(wqt_ref[...], a_ref[...]).astype(BF16)
    spread_heads(qt_ref, qst_ref)
    turned = jnp.transpose(kv_ref[:, 256:512])
    for h in range(HEADS):
        vt_ref[VALUE_ROWS * h : VALUE_ROWS * h + HEAD_DIM] = turned[head_rows(h)]
    for i, pt_ref in enumerate((p0, p1, p2)):
        seen, first = BLOCK * (i + 1), BLOCK * i
        scores = dot_nn(kv_ref[0:seen, 0:256], qst_ref[:, block_lanes(i)])
        last = scores[first:] + mask_ref[...]
        peak = jnp.max(last, axis=0, keepdims=True)
        if i:
            peak = jnp.maximum(peak, jnp.max(scores[0:first], axis=0, keepdims=True))
            pt_ref[0:first] = jnp.exp(scores[0:first] - peak).astype(BF16)
        pt_ref[first:seen] = jnp.exp(last - peak).astype(BF16)
        for h in range(HEADS):
            values = vt_ref[VALUE_ROWS * h : VALUE_ROWS * (h + 1), 0:seen]
            out = dot_nn(values, pt_ref[:, BLOCK * h : BLOCK * (h + 1)])
            inverse = 1.0 / out[HEAD_DIM : HEAD_DIM + 1]
            r_ref[h : h + 1, first:seen] = inverse
            ot_ref[head_rows(h), first:seen] = (out[0:HEAD_DIM] * inverse).astype(BF16)
    o_ref[...] = jnp.transpose(ot_ref[...])[0:SEQ]
    y_ref[...] = dot_nt(o_ref[...], w_ref[:, COL_PROJ : COL_PROJ + 256])
    for rows in tiles(SEQ, TILE):
        middle = x_ref[rows] + (y_ref[rows] + vec[2:3])
        m_ref[rows] = middle
        c_ref[rows] = (normalise(middle)[0] * vec[3:4] + vec[4:5]).astype(BF16)
    u_ref[...] = dot_nn(c_ref[...], w_ref[:, COL_UP : COL_UP + FF])
    for rows in tiles(SEQ, TILE):
        for first in range(0, FF, 256):
            cols = slice(first, first + 256)
            h_ref[rows, cols], gp_ref[rows, cols] = gelu_and_slope(u_ref[rows, cols] + bias[:, cols])
    y_ref[...] = dot_nt(h_ref[...], w_ref[:, COL_DOWN : COL_DOWN + FF])


def add_gradient(g_ref, column, left, right):
    g_ref[:, column : column + right.shape[1]] += dot_tn(left, right)


def ff_backward(grad_ref, grad16_ref, w_ref, w_up, w_down, vec, kept, g_ref, g_up, g_down, v_ref, v_row, bias_row, work, mid_ref, mid16_ref):
    m_ref, h_ref, gp_ref, c_ref = kept
    du_ref, ones_ref, u_ref, y_ref = work
    u_ref[...] = dot_nn(grad16_ref[...], w_ref[:, w_down : w_down + FF])
    for rows in tiles(SEQ, TILE):
        du_ref[rows] = u_ref[rows].astype(BF16) * gp_ref[rows]
    add_gradient(g_ref, g_down, grad16_ref[...], h_ref[...])
    add_gradient(g_ref, g_up, c_ref[...], du_ref[...])
    bias_grad = dot_nn(ones_ref[...], du_ref[...])
    for chunk in range(4):
        v_ref[bias_row + chunk, 0:1] += bias_grad[0:1, 256 * chunk : 256 * chunk + 256]
    y_ref[...] = dot_nt(du_ref[...], w_ref[:, w_up : w_up + FF])
    totals = [None] * 3
    for rows in tiles(SEQ, TILE):
        xhat, scale = normalise(m_ref[rows])
        grad = y_ref[rows]
        mid = grad_ref[rows] + normalise_back(grad, xhat, scale, vec[3:4])
        mid_ref[rows] = mid
        if mid16_ref is not None:
            mid16_ref[rows] = mid.astype(BF16)
        for i, a in enumerate((mid, grad * xhat, grad)):
            totals[i] = plus(totals[i], fold(a))
    for i in range(3):
        v_ref[v_row + 2 + i] += totals[i]


def attention_backward(mid_ref, mid16_ref, w_ref, vec, kept, g_ref, v_ref, v_row, work, out_ref):
    x_ref, qt_ref, kv_ref, p0, p1, p2, r_ref, ot_ref, o_ref, a_ref = kept
    dost_ref, qst_ref, kt_ref, dst_ref, dqt_ref, dkv_ref, dqkv_ref, proj_ref, y_ref = work
    add_gradient(g_ref, COL_PROJ, mid16_ref[0:SEQ], o_ref[...])
    grad_o = dot_nt(proj_ref[...], mid16_ref[...]).astype(BF16).astype(F32)
    kt_ref[...] = jnp.transpose(kv_ref[:, 0:256])
    deltas = []
    for h in range(HEADS):
        scaled = grad_o[head_rows(h)] * r_ref[h : h + 1]
        deltas.append(column_sum(scaled * ot_ref[head_rows(h)].astype(F32)))
        scaled = scaled.astype(BF16)
        for i in range(BLOCKS):
            dost_ref[head_rows(h), block_lanes(i, h)] = scaled[:, BLOCK * i : BLOCK * (i + 1)]
    for i, pt_ref in enumerate((p0, p1, p2)):
        seen, first = BLOCK * (i + 1), BLOCK * i
        lanes = block_lanes(i)
        delta = jnp.concatenate([a[:, first:seen] for a in deltas], axis=1)
        grad = dot_nn(kv_ref[0:seen, 256:512], dost_ref[:, lanes])
        dst_ref[0:seen, lanes] = pt_ref[...] * (grad - delta).astype(BF16)
        for h in range(HEADS):
            out = dot_nn(kt_ref[head_rows(h), 0:seen], dst_ref[0:seen, block_lanes(i, h)])
            dqt_ref[head_rows(h), first:seen] = out.astype(BF16)
        for at, left, right in (
            (0, dst_ref[0:seen, lanes], qst_ref),
            (256, pt_ref[...], dost_ref),
        ):
            out = dot_nt(left, right[:, lanes])
            if i:
                dkv_ref[0:first, at : at + 256] += out[0:first]
            dkv_ref[first:seen, at : at + 256] = out[first:]
    dqkv_ref[:, 0:256] = jnp.transpose(dqt_ref[...])[0:SEQ]
    dqkv_ref[:, 256:768] = dkv_ref[0:SEQ].astype(BF16)
    add_gradient(g_ref, COL_QKV, a_ref[0:SEQ], dqkv_ref[...])
    y_ref[...] = dot_nt(dqkv_ref[...], w_ref[:, COL_QKV : COL_QKV + 768])
    totals = [None] * 2
    for rows in tiles(SEQ, TILE):
        xhat, scale = normalise(x_ref[rows])
        grad = y_ref[rows]
        out = mid_ref[rows] + normalise_back(grad, xhat, scale, vec[0:1])
        out_ref[rows] = out.astype(out_ref.dtype)
        for i, a in enumerate((grad * xhat, grad)):
            totals[i] = plus(totals[i], fold(a))
    for i in range(2):
        v_ref[v_row + i] += totals[i]


def own_bias(place, mine, other):
    is_first = place[1] == 0
    return jnp.concatenate(
        [jnp.where(is_first, mine, other), jnp.where(is_first, other, mine)], axis=1
    )


def prepare_kernel(
    fast, games_ref, tokens, actions, valid, rewards, ends, out, out_side, x_ref
):
    count = out.shape[0]
    frames = tokens.shape[2]
    base = places(fast)[1] * count
    row = lax.broadcasted_iota(jnp.int32, (SEQ, frames), 0)
    start = lax.broadcasted_iota(jnp.int32, (SEQ, frames), 1) * FRAME_TOKENS
    here = jnp.where((row >= start) & (row < start + FRAME_TOKENS), 1.0, 0.0).astype(BF16)
    coming = jnp.where((row >= start - FRAME_TOKENS) & (row < start), 1.0, 0.0).astype(BF16)
    passed = jnp.sum(jnp.where(row >= start + FRAME_TOKENS, 1, 0), axis=1, keepdims=True)
    place = lax.broadcasted_iota(jnp.int32, (SEQ, 1), 0)
    spot = place - passed * FRAME_TOKENS
    lane = lax.broadcasted_iota(jnp.int32, (SEQ, 24), 1)
    wide_lane = lax.broadcasted_iota(jnp.int32, (SEQ, 128), 1)
    inside = place < LENGTH
    one_frame = (
        lax.broadcasted_iota(jnp.int32, (SIDE_ROWS, frames), 0)
        == lax.broadcasted_iota(jnp.int32, (SIDE_ROWS, frames), 1)
    )
    one_frame = jnp.where(one_frame, 1.0, 0.0).astype(BF16)
    side_lane = lax.broadcasted_iota(jnp.int32, (SIDE_ROWS, 128), 1)
    x_ref[...] = jnp.zeros(x_ref.shape, jnp.int32)
    for s in range(count):
        x_ref[0:OBS] = tokens[base + s]
        x_ref[16:17] = actions[pl.ds(base + s, 1)] + VOCAB
        x_ref[17:18] = valid[pl.ds(base + s, 1)]
        x_ref[18:19] = rewards[pl.ds(base + s, 1)]
        x_ref[19:20] = ends[pl.ds(base + s, 1)] + 3
        high = (x_ref[...] >> 4).astype(F32).astype(BF16)
        low = (x_ref[...] & 15).astype(F32).astype(BF16)
        now = dot_nt(here, high) * 16.0 + dot_nt(here, low)
        soon = dot_nt(coming, high) * 16.0 + dot_nt(coming, low)

        def pick(condition, a):
            return jnp.sum(jnp.where(condition, a, 0.0), axis=1, keepdims=True).astype(jnp.int32)

        ids = jnp.where(inside, pick(lane == spot, now), -1)
        game = jnp.where(inside, games_ref[base + s] + (VOCAB + ACTIONS), -1)
        target = pick((lane == spot + 1) & (spot < 15), now)
        target = target + pick((lane == 0) & (spot == 16), soon)
        weight = pick((lane == 17) & (spot < 15), now) + pick((lane == 17) & (spot == 16), soon)
        result = jnp.zeros((SEQ, 128), jnp.int32)
        for c, column in enumerate((ids, game, target, weight)):
            result = jnp.where(wide_lane == c, column, result)
        out[s] = result
        by_frame = dot_nt(one_frame, high) * 16.0 + dot_nt(one_frame, low)
        result = jnp.zeros((SIDE_ROWS, 128), jnp.int32)
        for c in range(3):
            column = by_frame[:, 17 + c : 18 + c].astype(jnp.int32)
            result = jnp.where(side_lane == c, column, result)
        out_side[s] = result


def start_forward(work, w_ref):
    qst_ref, vt_ref, mask_ref, wqt_ref, u_ref, y_ref = work
    qst_ref[...] = jnp.zeros(qst_ref.shape, BF16)
    vt_ref[...] = jnp.ones(vt_ref.shape, BF16)
    mask_ref[...] = causal_mask()
    wqt_ref[...] = jnp.transpose(w_ref[:, 0:256])


def first_forward_kernel(fast, *refs):
    refs = (places(fast),) + refs
    place, meta_ref, vec_ref, bias_ref, bias_other = refs[0:5]
    mine, other = refs[5:9], refs[9:13]
    w_attention, w_ff, side_out, next_ref, hits_ref, x_ref = refs[13:19]
    kept = [ref.at[0] for ref in refs[19:32]]
    w_ref = refs[32]
    work = refs[33:39]

    @pl.when(pl.program_id(0) == 0)
    def _():
        assemble(mine, other, place, w_ref, HALF_FIRST)
        w_attention[...] = w_ref[:, 0:COL_UP]
        w_ff[...] = w_ref[:, COL_UP:COL_TABLE]
        side_out[...] = w_ref[:, COL_SMALL:]
        start_forward(work, w_ref)

    make_hits(meta_ref.at[0], hits_ref.at[0])
    x_ref[0] = dot_nt(hits_ref[0], w_ref[:, COL_TABLE : COL_TABLE + ROWS])
    bias = own_bias(place, bias_ref[0:1], bias_other[0:1])
    vec = vec_ref[0:6]
    layer_forward(x_ref.at[0], w_ref, vec, bias, kept, work)
    for rows in tiles(SEQ, TILE):
        next_ref[0, rows] = kept[8][rows] + (work[5][rows] + vec[5:6])


def codebook_losses(logits, meta):
    weight = meta[:, 3:4].astype(F32)
    peak = jnp.max(logits, axis=1, keepdims=True)
    expanded = jnp.exp(logits - peak)
    total = jnp.sum(expanded, axis=1, keepdims=True)
    hit = lax.broadcasted_iota(jnp.int32, logits.shape, 1) == meta[:, 2:3]
    hit = jnp.where(hit, weight, 0.0)
    return weight * (peak + jnp.log(total)), hit, expanded * (weight / total) - hit


def side_losses(side, meta):
    lane = lax.broadcasted_iota(jnp.int32, side.shape, 1)
    is_reward, is_end = lane < 3, (lane == 3) | (lane == 4)
    is_side = lane < 5
    weight = meta[:, 0:1].astype(F32)
    reward_peak = jnp.max(jnp.where(is_reward, side, -1e30), axis=1, keepdims=True)
    end_peak = jnp.max(jnp.where(is_end, side, -1e30), axis=1, keepdims=True)
    shifted = jnp.where(is_side, side - jnp.where(is_reward, reward_peak, end_peak), 0.0)
    expanded = jnp.where(is_side, jnp.exp(shifted), 0.0)
    reward_total = jnp.sum(jnp.where(is_reward, expanded, 0.0), axis=1, keepdims=True)
    end_total = jnp.sum(jnp.where(is_end, expanded, 0.0), axis=1, keepdims=True)
    hit = (lane == meta[:, 1:2]) | (lane == meta[:, 2:3])
    picked = jnp.sum(jnp.where(hit, side, 0.0), axis=1, keepdims=True)
    terms = reward_peak + jnp.log(reward_total) + end_peak + jnp.log(end_total) - picked
    grad = expanded * jnp.where(is_reward, weight / reward_total, weight / end_total)
    return weight * terms, grad - jnp.where(hit, weight, 0.0), weight


def frame_ends(shape, frame_axis):
    frame = lax.broadcasted_iota(jnp.int32, shape, frame_axis)
    row = lax.broadcasted_iota(jnp.int32, shape, 1 - frame_axis)
    hit = (row == frame * FRAME_TOKENS + OBS) & (frame < FRAMES)
    return jnp.where(hit, 1.0, 0.0).astype(BF16)


def middle_kernel(fast, *refs):
    refs = (places(fast),) + refs
    place, meta_ref, frame_ref, vec_ref, bias_ref, bias_other, side_ref, in_ref = refs[0:8]
    mine, other = refs[8:12], refs[12:16]
    grad_ref, keep_ref, send_ref, v_out, scalar_ref = refs[16:21]
    refs = refs[1:]
    w_ref, g_ref, v_ref = refs[20:23]
    kept = refs[23:36]
    m_ref, h_ref, gp_ref, a_ref, c_ref = kept[8:13]
    forward_work = refs[36:42]
    u_ref, y_ref = forward_work[4:6]
    backward_work = refs[42:48]
    proj_ref = refs[48]
    du_ref, ones_ref, up_ref, up16_ref, mid_ref, mid16_ref = refs[49:55]
    last_ref, final_ref, logit_ref, dlogit_ref, pick_ref, put_ref = refs[55:61]
    dost_ref = backward_work[0]
    step = pl.program_id(0)

    @pl.when(step == 0)
    def _():
        assemble(mine, other, place, w_ref, HALF_SECOND)
        w_ref[:, COL_SECOND:] = side_ref[...]
        g_ref[...] = jnp.zeros(g_ref.shape, F32)
        v_ref[...] = jnp.zeros(v_ref.shape, F32)
        scalar_ref[...] = jnp.zeros(scalar_ref.shape, F32)
        start_forward(forward_work, w_ref)
        dost_ref[...] = jnp.zeros(dost_ref.shape, BF16)
        proj_ref[...] = jnp.transpose(w_ref[:, COL_PROJ : COL_PROJ + 256])
        ones_ref[...] = jnp.ones(ones_ref.shape, BF16)
        mid16_ref[SEQ:KEYS] = jnp.zeros((KEYS - SEQ, D), BF16)
        pick_ref[...] = frame_ends((SIDE_ROWS, SEQ), 0)
        put_ref[...] = frame_ends((SEQ, SIDE_ROWS), 1)

    x_ref = in_ref.at[0]
    vec = vec_ref[6:12]
    bias = own_bias(place, bias_ref[1:2], bias_other[1:2])
    layer_forward(x_ref, w_ref, vec, bias, kept, forward_work)

    gain, offset = vec_ref[12:13], vec_ref[13:14]
    for rows in tiles(SEQ, TILE):
        last = m_ref[rows] + (y_ref[rows] + vec[5:6])
        last_ref[rows] = last
        final_ref[rows] = (normalise(last)[0] * gain + offset).astype(BF16)
    cols_head = slice(COL_HEAD, COL_HEAD + VOCAB + 128)
    logit_ref[...] = dot_nn(final_ref[...], w_ref[:, COL_HEAD : COL_HEAD + VOCAB])
    logs, picked = None, None
    for rows in tiles(SEQ, TILE):
        logits = logit_ref[rows]
        log, hit, grad = codebook_losses(logits, meta_ref[0, rows])
        dlogit_ref[rows, :VOCAB] = grad.astype(BF16)
        logs, picked = plus(logs, log), plus(picked, fold(hit * logits))
    acting = dot_nn(pick_ref[...], final_ref[...]).astype(BF16)
    side = dot_nn(acting, w_ref[:, COL_HEAD + VOCAB : COL_HEAD + VOCAB + 128])
    side_loss, grad, weight = side_losses(side, frame_ref[0])
    dlogit_ref[:, VOCAB:] = dot_nn(put_ref[...], grad.astype(BF16)).astype(BF16)
    loss = column_sum(logs) + column_sum(side_loss)
    loss = loss - jnp.sum(column_sum(picked), axis=1, keepdims=True)
    valid = column_sum(weight)
    scalar_lane = lax.broadcasted_iota(jnp.int32, (8, 128), 1)
    scalar_row = lax.broadcasted_iota(jnp.int32, (8, 128), 0) == 0
    scalar_ref[...] += jnp.where(
        scalar_row,
        jnp.where(scalar_lane == 0, loss, jnp.where(scalar_lane == 1, valid, 0.0)),
        0.0,
    )
    add_gradient(g_ref, COL_HEAD, final_ref[...], dlogit_ref[...])
    y_ref[...] = dot_nt(dlogit_ref[...], w_ref[:, cols_head])
    totals = [None] * 3
    for rows in tiles(SEQ, TILE):
        xhat, scale = normalise(last_ref[rows])
        grad = y_ref[rows]
        up = normalise_back(grad, xhat, scale, gain)
        up_ref[rows] = up
        up16_ref[rows] = up.astype(BF16)
        for i, a in enumerate((up, grad * xhat, grad)):
            totals[i] = plus(totals[i], fold(a))
    for i in range(3):
        v_ref[11 + i] += totals[i]
    ff_backward(
        up_ref,
        up16_ref,
        w_ref,
        COL_UP,
        COL_DOWN,
        vec,
        (m_ref, h_ref, gp_ref, c_ref),
        g_ref,
        COL_UP,
        COL_DOWN,
        v_ref,
        6,
        SMALL_BIAS + 4,
        (du_ref, ones_ref, u_ref, y_ref),
        mid_ref,
        mid16_ref,
    )
    attention_backward(
        mid_ref,
        mid16_ref,
        w_ref,
        vec,
        (x_ref,) + tuple(kept[0:8]) + (a_ref,),
        g_ref,
        v_ref,
        6,
        (dost_ref, forward_work[0]) + tuple(backward_work[1:]) + (proj_ref, y_ref),
        grad_ref.at[0],
    )

    @pl.when(step == pl.num_programs(0) - 1)
    def _():
        disperse(g_ref, place, keep_ref, send_ref, HALF_SECOND)
        side = jnp.transpose(g_ref[:, COL_SECOND:])
        for i in range(5):
            v_ref[SMALL_SIDE + i, 0:1] = side[i : i + 1]
        v_out[...] = v_ref[...]


def ff_backward_kernel(fast, *refs):
    refs = (places(fast),) + refs
    place, vec_ref, w_ref, grad_ref, v_in = refs[0:5]
    kept = [ref.at[0] for ref in refs[5:9]]
    mid_ref, keep_ref, send_ref, v_out = refs[9:13]
    g_ref, v_ref, grad16_ref = refs[13:16]
    work = refs[16:20]
    ones_ref = work[1]
    step = pl.program_id(0)

    @pl.when(step == 0)
    def _():
        g_ref[...] = jnp.zeros(g_ref.shape, F32)
        v_ref[...] = v_in[...]
        ones_ref[...] = jnp.ones(ones_ref.shape, BF16)

    total = None
    for rows in tiles(SEQ, TILE):
        grad = grad_ref[0, rows]
        grad16_ref[rows] = grad.astype(BF16)
        total = plus(total, fold(grad))
    v_ref[5] += total
    ff_backward(
        grad_ref.at[0],
        grad16_ref,
        w_ref,
        GRAD_UP,
        GRAD_DOWN,
        vec_ref[0:6],
        kept,
        g_ref,
        GRAD_UP,
        GRAD_DOWN,
        v_ref,
        0,
        SMALL_BIAS,
        work,
        mid_ref.at[0],
        None,
    )

    @pl.when(step == pl.num_programs(0) - 1)
    def _():
        disperse(g_ref, place, keep_ref, send_ref, HALF_GRAD_FF, False)
        v_out[...] = v_ref[...]


def attention_backward_kernel(fast, *refs):
    refs = (places(fast),) + refs
    place, vec_ref, w_ref, mid_ref, hits_ref, v_in = refs[0:6]
    kept = [ref.at[0] for ref in refs[6:16]]
    keep_ref, send_ref, v_out = refs[17:20]
    g_ref, v_ref, mid16_ref, out16_ref = refs[20:24]
    work = refs[24:33]
    dost_ref, qst_ref, proj_ref = work[0], work[1], work[7]
    step = pl.program_id(0)

    @pl.when(step == 0)
    def _():
        g_ref[...] = jnp.zeros(g_ref.shape, F32)
        v_ref[...] = v_in[...]
        dost_ref[...] = jnp.zeros(dost_ref.shape, BF16)
        qst_ref[...] = jnp.zeros(qst_ref.shape, BF16)
        proj_ref[...] = jnp.transpose(w_ref[:, COL_PROJ : COL_PROJ + 256])
        mid16_ref[SEQ:KEYS] = jnp.zeros((KEYS - SEQ, D), BF16)

    spread_heads(kept[1], qst_ref)
    for rows in tiles(SEQ, TILE):
        mid16_ref[rows] = mid_ref[0, rows].astype(BF16)
    attention_backward(
        mid_ref.at[0], mid16_ref, w_ref, vec_ref[0:6], kept, g_ref, v_ref, 0, work, out16_ref
    )
    add_gradient(g_ref, GRAD_TABLE, out16_ref[...], hits_ref[0])

    @pl.when(step == pl.num_programs(0) - 1)
    def _():
        small = jnp.sum(v_ref[...], axis=1)
        v_out[...] = small
        for block in range(16):
            quarter = small[8 * (block // 4) : 8 * (block // 4) + 8]
            g_ref[16 * block : 16 * block + 8, GRAD_SMALL:] = quarter[:, 0:128]
            g_ref[16 * block + 8 : 16 * block + 16, GRAD_SMALL:] = quarter[:, 128:256]
        disperse(g_ref, place, keep_ref, send_ref, HALF_GRAD_REST)


def pack_layer(attn, proj, up, down, layer, out):
    for j in range(3):
        out[:, 128 * j : 128 * j + 128] = attn[layer, j].astype(BF16)
    out[:, 384:512] = proj[layer].astype(BF16)
    out[:, 512:1024] = up[layer].astype(BF16)
    out[:, 1024:1536] = down[layer].astype(BF16)


def pack_kernel(fast, table, attn, proj, up, down, head, side, first, second, pad_ref):
    pack_layer(attn, proj, up, down, 0, first)
    pack_layer(attn, proj, up, down, 1, second)
    second[:, 1536:1792] = head[...].astype(BF16)
    rows = side.shape[1]
    eye = (
        lax.broadcasted_iota(jnp.int32, (rows, rows), 0)
        == lax.broadcasted_iota(jnp.int32, (rows, rows), 1)
    )
    eye = jnp.where(eye, 1.0, 0.0).astype(BF16)
    pad_ref[...] = jnp.zeros(pad_ref.shape, F32)
    pad_ref[:, 0:5] = dot_nt(eye, side[...].astype(BF16))
    high = jnp.concatenate([table[:, 512:896], pad_ref[...]], axis=1)
    first[:, 1536:2048] = jnp.where(places(fast)[1] == 0, table[:, 0:512], high).astype(BF16)


def finish_kernel(fast, *refs):
    count = (len(refs) - 5) // 2
    scalar_ref = refs[2 * count]
    out_rest, out_other, out_table, out_small = refs[2 * count + 1 :]
    square = jnp.zeros((1, 1), F32)
    for pieces, out in ((refs[0:count], out_rest), (refs[count : 2 * count], out_other)):
        total = pieces[0][...]
        for piece in pieces[1:]:
            total = total + piece[...].astype(F32)
        out[...] = total
        square = square + column_sum(jnp.sum(total * total, axis=1, keepdims=True))
    small = out_rest[:, 896:1024]
    extra = column_sum(jnp.sum(small * small, axis=1, keepdims=True))
    square = square - jnp.where(places(fast)[1] == 0, 0.0, extra)
    out_table[...] = out_rest[:, 512:1024]
    rows = small.shape[0]
    lane = lax.broadcasted_iota(jnp.int32, (8, 128), 1)
    top = lax.broadcasted_iota(jnp.int32, (8, 128), 0) == 0
    scalars = scalar_ref[...] + jnp.where(top & (lane == 2), square, 0.0)
    for i in range(out_small.shape[0]):
        out_small[i, 0:rows] = small
        out_small[i, rows : rows + 8] = scalars


def adam_rule(weight, moment, second, gradient, step_rate, decay_rate):
    moment_new = BETA_ONE * moment + (1.0 - BETA_ONE) * gradient
    second_new = BETA_TWO * second + (1.0 - BETA_TWO) * gradient * gradient
    moment_hat = moment_new / (1.0 - BETA_ONE**STEP_NUMBER)
    second_hat = second_new / (1.0 - BETA_TWO**STEP_NUMBER)
    weight_new = weight - step_rate * (
        moment_hat / (jnp.sqrt(second_hat) + EPS_ADAM) + decay_rate * weight
    )
    return (weight_new, moment_new, second_new)


def adam_kernel(fast, rest, others, swapped, gathered, beside, *refs):
    rows = rest.shape[0]
    _, core, wide = places(fast)
    is_first = core == 0
    if fast:
        quarters = [jnp.where(is_first, beside[4 * z], gathered[4 * z]) for z in range(4)]
    else:
        quarters = [refs[0][z] for z in range(4)]
        refs = refs[1:]
    params = [refs[3 * i : 3 * i + 3] for i in range(9)]
    loss_ref, valid_ref, norm_ref = refs[27:30]
    outs = [refs[30 + 3 * i : 33 + 3 * i] for i in range(9)]
    small_ref = refs[57]
    for z in range(4):
        small_ref[8 * z : 8 * z + 8, 0:128] = quarters[z][0:8]
        small_ref[8 * z : 8 * z + 8, 128:256] = quarters[z][8:16]
    sums = []
    for source in (gathered, beside):
        total = source[0, rows : rows + 1]
        for i in range(1, source.shape[0]):
            total = total + source[i, rows : rows + 1]
        sums.append(total)
    scalars = sums[0] + sums[1]
    small = small_ref[...]
    loss, valid, square = scalars[:, 0:1], scalars[:, 1:2], scalars[:, 2:3]
    square = square + column_sum(jnp.sum(small * small, axis=1, keepdims=True))
    inverse = 1.0 / valid
    norm = jnp.sqrt(square) * inverse
    loss_ref[...], valid_ref[...], norm_ref[...] = loss, valid, norm
    factor = jnp.minimum(1.0, CLIP_AT / (norm + 1e-06)) * inverse
    table, attn, proj, up, bias, down, vectors, head, side = range(9)

    def update(which, index, gradient, step_rate, decay_rate):
        news = adam_rule(
            *(ref[index] for ref in params[which]), factor * gradient, step_rate, decay_rate
        )
        for ref, new in zip(outs[which], news):
            ref[index] = new

    layers = ((rest, others, 1792), (others, others, 512))
    for layer, (attention, feed, at) in enumerate(layers):
        for j in range(3):
            update(attn, (layer, j), attention[:, 128 * j : 128 * j + 128], RATE_MATRIX, DECAY_RATE)
        update(proj, (layer,), attention[:, 384:512], RATE_MATRIX, DECAY_RATE)
        update(up, (layer,), feed[:, at : at + 512], RATE_MATRIX, DECAY_RATE)
        update(down, (layer,), feed[:, at + 512 : at + 1024], RATE_MATRIX, DECAY_RATE)
        for i in range(2):
            low = SMALL_BIAS + 4 * layer + i
            row = jnp.where(is_first, small[low : low + 1], small[low + 2 : low + 3])
            index = (slice(layer, layer + 1), slice(256 * i, 256 * i + 256))
            update(bias, index, row, RATE_VECTOR, 0.0)
    whole = (slice(None), slice(None))
    update(head, whole, others[:, 1536:1792], RATE_MATRIX, DECAY_RATE)
    mine, theirs = rest[:, 512:1024], swapped[:, 0:512]
    low, high = jnp.where(is_first, mine, theirs), jnp.where(is_first, theirs, mine)
    update(table, (slice(None), slice(0, 512)), low, RATE_TABLE, DECAY_RATE)
    update(table, (slice(None), slice(512, 896)), high[:, 0:384], RATE_TABLE, DECAY_RATE)
    update(vectors, whole, small[0:NVEC], RATE_VECTOR, 0.0)
    turned = pltpu.roll(small[SMALL_SIDE : SMALL_SIDE + 8], lax.rem(D - wide * rows, D), 1)
    update(side, whole, turned[0:5, 0:rows], RATE_MATRIX, DECAY_RATE)


def swap(a, axis, distance):
    size = lax.axis_size(axis)
    return lax.ppermute(a, axis, [(i, i ^ distance) for i in range(size)])


def swap_column(piece, n_high):
    return [piece] + [swap(piece, "wide", 4 * k) for k in range(1, n_high)]


def gather_plane(column):
    return [column] + [swap(column, "wide", p) for p in range(1, 4)]


def gather_cores(mine):
    return [swap(a, "narrow", 1) for a in mine]


def in_blocks(parts, wide):
    n_high, rows, cols = parts[0].shape
    if rows == 16:
        return parts
    whole = jnp.stack(parts, axis=1).reshape(4 * n_high, rows, cols)
    whole = whole[wide ^ jnp.arange(4 * n_high)].reshape(4, 4, 16, cols)
    return [whole[:, p] for p in range(4)]


def in_pieces(blocks, wide, n_high):
    cols = blocks.shape[-1]
    if n_high == 4:
        return blocks
    rows = 64 // n_high
    whole = blocks.transpose(1, 0, 2, 3).reshape(4 * n_high, rows, cols)
    whole = whole[wide ^ jnp.arange(4 * n_high)]
    return whole.reshape(n_high, 4, rows, cols).transpose(1, 0, 2, 3)


def add_cores(keep, send, wide, n_high):
    keep, send = in_pieces(keep, wide, n_high), in_pieces(send, wide, n_high)
    received = swap(send, "narrow", 1)
    return [keep[p].astype(F32) + received[p].astype(F32) for p in range(4)]


def swap_plane(sums):
    return [swap(sums[p].astype(BF16), "wide", p) for p in range(1, 4)]


def add_plane(own, received):
    for a in received:
        own = own + a.astype(F32)
    return own


def column_pieces(own):
    return [own[0]] + [swap(own[k].astype(BF16), "wide", 4 * k) for k in range(1, own.shape[0])]


def resident(arrays):
    return [pltpu.with_memory_space_constraint(a, pltpu.VMEM) for a in arrays]


def in_hbm(arrays):
    return [pltpu.with_memory_space_constraint(a, pltpu.HBM) for a in arrays]


def full_spec(a):
    return pl.BlockSpec(a.shape, lambda *_: (0,) * len(a.shape))


def row_spec(shape):
    return pl.BlockSpec((1,) + shape, lambda i: (i,) + (0,) * len(shape))


def shaped(shape, dtype):
    return jax.ShapeDtypeStruct(shape, dtype)


VMEM_SPEC = pl.BlockSpec(memory_space=pltpu.VMEM)
ANY_SPEC = pl.BlockSpec(memory_space=pl.ANY)
SMEM_SPEC = pl.BlockSpec(memory_space=pltpu.SMEM)


VMEM_MIB = {
    "pack": 58,
    "prepare": 58,
    "first_forward": 24,
    "middle": 27,
    "ff_backward": 17,
    "attention_backward": 20,
    "finish": 58,
    "adam": 58,
}


def call(kernel, grid, in_specs, out_specs, out_shape, scratch, flops, bytes_accessed, name):
    extra = {"grid": grid} if grid else {}
    return pl.pallas_call(
        kernel,
        in_specs=in_specs,
        out_specs=out_specs,
        out_shape=out_shape,
        scratch_shapes=scratch,
        compiler_params=pltpu.CompilerParams(vmem_limit_bytes=VMEM_MIB[name] * MIB),
        cost_estimate=pl.CostEstimate(
            flops=flops, bytes_accessed=bytes_accessed, transcendentals=0
        ),
        name=name,
        **extra,
    )


KEPT = (
    ((D, KEYS), BF16),
    ((KEYS, 512), BF16),
    ((BLOCK, QUERIES), BF16),
    ((2 * BLOCK, QUERIES), BF16),
    ((3 * BLOCK, QUERIES), BF16),
    ((8, KEYS), F32),
    ((D, KEYS), BF16),
    ((SEQ, D), BF16),
    ((SEQ, D), F32),
    ((SEQ, FF), BF16),
    ((SEQ, FF), BF16),
    ((KEYS, D), BF16),
    ((SEQ, D), BF16),
)
FORWARD_WORK = [
    pltpu.VMEM((D, BLOCKS * QUERIES), BF16),
    pltpu.VMEM((HEADS * VALUE_ROWS, KEYS), BF16),
    pltpu.VMEM((BLOCK, QUERIES), F32),
    pltpu.VMEM((D, D), BF16),
    pltpu.VMEM((SEQ, FF), F32),
    pltpu.VMEM((SEQ, D), F32),
]
BACKWARD_WORK = [
    pltpu.VMEM((D, BLOCKS * QUERIES), BF16),
    pltpu.VMEM((D, BLOCKS * QUERIES), BF16),
    pltpu.VMEM((D, KEYS), BF16),
    pltpu.VMEM((KEYS, BLOCKS * QUERIES), BF16),
    pltpu.VMEM((D, KEYS), BF16),
    pltpu.VMEM((KEYS, 512), F32),
    pltpu.VMEM((SEQ, 768), BF16),
]
PROJ_WORK = pltpu.VMEM((D, D), BF16)
ONES_WORK = pltpu.VMEM((16, SEQ), BF16)


def per_device(
    tokens,
    actions,
    game_ids,
    valid_steps,
    rewards,
    end_flags,
    embed_table,
    table_first,
    table_second,
    attn_weight,
    attn_first,
    attn_second,
    proj_weight,
    proj_first,
    proj_second,
    up_weight,
    up_first,
    up_second,
    up_bias,
    bias_first,
    bias_second,
    down_weight,
    down_first,
    down_second,
    vectors,
    vectors_first,
    vectors_second,
    head_weight,
    head_first,
    head_second,
    side_weight,
    side_first,
    side_second,
):
    n_high = lax.axis_size("wide") // 4
    wide = lax.axis_index("wide")
    rows = side_weight.shape[0]
    fast = rows == 16

    def flat(a):
        return jnp.swapaxes(a, -1, -2)

    params = (
        (flat(embed_table), flat(table_first), flat(table_second)),
        (attn_weight, attn_first, attn_second),
        (flat(proj_weight), flat(proj_first), flat(proj_second)),
        (up_weight, up_first, up_second),
        (up_bias, bias_first, bias_second),
        (flat(down_weight), flat(down_first), flat(down_second)),
        (vectors, vectors_first, vectors_second),
        (head_weight, head_first, head_second),
        (flat(side_weight), flat(side_first), flat(side_second)),
    )
    table, attn, proj, up, _, down, _, head, side = (group[0] for group in params)

    piece_first, piece_second = call(
        functools.partial(pack_kernel, fast),
        None,
        [VMEM_SPEC] * 7,
        [VMEM_SPEC] * 2,
        [shaped((rows, HALF_FIRST_COLS), BF16), shaped((rows, HALF_SECOND_COLS), BF16)],
        [pltpu.VMEM((rows, 128), F32)],
        10**6,
        10**6,
        "pack",
    )(table, attn, proj, up, down, head, side)
    other_bias = swap(up_bias, "narrow", 1)
    column = swap_column(piece_first, n_high)

    column, other_bias = lax.optimization_barrier((column, other_bias))
    first_column = jnp.stack(column)
    beside, above = swap(first_column, "wide", 1), swap(first_column, "wide", 2)

    count = tokens.shape[0] // lax.axis_size("narrow")
    ids, first_column = lax.optimization_barrier((flat(tokens), first_column))
    meta, frame_meta = call(
        functools.partial(prepare_kernel, fast),
        None,
        [SMEM_SPEC] + [VMEM_SPEC] * 5,
        [VMEM_SPEC] * 2,
        [shaped((count, SEQ, 128), jnp.int32), shaped((count, SIDE_ROWS, 128), jnp.int32)],
        [pltpu.VMEM((24, FRAMES), jnp.int32)],
        10**6,
        10**6,
        "prepare",
    )(game_ids, ids, actions, valid_steps, rewards, end_flags)
    beside, first_column, meta = lax.optimization_barrier((beside, first_column, meta))
    above, piece_second = lax.optimization_barrier((above, piece_second))
    across = swap(first_column, "wide", 3)
    second_column = jnp.stack(swap_column(piece_second, n_high))
    second_column, across = lax.optimization_barrier((second_column, across))
    first_mine = [first_column, beside, above, across]
    first_other = gather_cores(first_mine)
    second_mine = gather_plane(second_column)
    first_parts = in_blocks(first_mine, wide) + in_blocks(first_other, wide)

    kept_specs = [row_spec(shape) for shape, _ in KEPT]
    kept_shapes = [shaped((count,) + shape, dtype) for shape, dtype in KEPT]
    row_f32 = shaped((count, SEQ, D), F32)
    meta_spec = row_spec((SEQ, 128))
    vec_specs = [full_spec(vectors), full_spec(up_bias), full_spec(up_bias)]
    w_attention_spec = pl.BlockSpec((D, 1024), lambda i: (0, 0))
    w_ff_spec = pl.BlockSpec((D, 2048), lambda i: (0, 0))
    side_spec = pl.BlockSpec((D, 128), lambda i: (0, 0))
    hits_spec = row_spec((SEQ, ROWS))
    results = call(
        functools.partial(first_forward_kernel, fast),
        (count,),
        [meta_spec] + vec_specs + [VMEM_SPEC] * 8,
        [w_attention_spec, w_ff_spec, side_spec, row_spec((SEQ, D)), hits_spec, row_spec((SEQ, D))]
        + kept_specs,
        [shaped((D, 1024), BF16), shaped((D, 2048), BF16), shaped((D, 128), BF16), row_f32]
        + [shaped((count, SEQ, ROWS), BF16), row_f32]
        + kept_shapes,
        [pltpu.VMEM((D, COL_FIRST), BF16)] + FORWARD_WORK,
        4 * 10**9,
        20 * 10**6,
        "first_forward",
    )(*in_hbm([meta, vectors, up_bias, other_bias]), *resident(first_parts))
    w_attention, w_ff, side_copy, stream, hits, stream_first = results[0:6]
    kept = results[6:]
    received, side_copy = lax.optimization_barrier((second_mine[1:], side_copy))
    second_mine = second_mine[0:1] + received
    second_other = gather_cores(second_mine)
    second_parts = in_blocks(second_mine, wide) + in_blocks(second_other, wide)

    def blocks(cols):
        return pl.BlockSpec((4, 4, 16, cols), lambda i: (0, 0, 0, 0))

    def block_shapes(cols):
        return [shaped((4, 4, 16, cols), BF16)] * 2

    small_spec = pl.BlockSpec((SMALL_ROWS, 8, D), lambda i: (0, 0, 0))
    small_shape = shaped((SMALL_ROWS, 8, D), F32)
    small_scratch = pltpu.VMEM((SMALL_ROWS, 8, D), F32)
    scalar_spec = pl.BlockSpec((8, 128), lambda i: (0, 0))
    grad_stream, keep_second, send_second, small_grads, scalars = call(
        functools.partial(middle_kernel, fast),
        (count,),
        [meta_spec, row_spec((SIDE_ROWS, 128))]
        + vec_specs
        + [side_spec, row_spec((SEQ, D))]
        + [VMEM_SPEC] * 8,
        [row_spec((SEQ, D))] + [blocks(HALF_SECOND_COLS)] * 2 + [small_spec, scalar_spec],
        [row_f32] + block_shapes(HALF_SECOND_COLS) + [small_shape, shaped((8, 128), F32)],
        [
            pltpu.VMEM((D, COL_SECOND + 128), BF16),
            pltpu.VMEM((D, COL_SECOND + 128), F32),
            small_scratch,
        ]
        + [pltpu.VMEM(shape, dtype) for shape, dtype in KEPT]
        + FORWARD_WORK
        + BACKWARD_WORK[0:1]
        + BACKWARD_WORK[2:]
        + [
            PROJ_WORK,
            pltpu.VMEM((SEQ, FF), BF16),
            ONES_WORK,
            pltpu.VMEM((SEQ, D), F32),
            pltpu.VMEM((SEQ, D), BF16),
            pltpu.VMEM((SEQ, D), F32),
            pltpu.VMEM((KEYS, D), BF16),
            pltpu.VMEM((SEQ, D), F32),
            pltpu.VMEM((SEQ, D), BF16),
            pltpu.VMEM((SEQ, VOCAB), F32),
            pltpu.VMEM((SEQ, VOCAB + 128), BF16),
            pltpu.VMEM((SIDE_ROWS, SEQ), BF16),
            pltpu.VMEM((SEQ, SIDE_ROWS), BF16),
        ],
        15 * 10**9,
        20 * 10**6,
        "middle",
    )(
        *in_hbm([meta, frame_meta, vectors, up_bias, other_bias]),
        side_copy,
        stream,
        *resident(second_parts),
    )
    second_sums = add_cores(keep_second, send_second, wide, n_high)

    kept_ff = (kept[8], kept[9], kept[10], kept[12])
    grad_mid, keep_ff, send_ff, small_grads = call(
        functools.partial(ff_backward_kernel, fast),
        (count,),
        [full_spec(vectors), w_ff_spec, row_spec((SEQ, D)), small_spec]
        + [row_spec(a.shape[1:]) for a in kept_ff],
        [row_spec((SEQ, D))] + [blocks(HALF_GRAD_COLS)] * 2 + [small_spec],
        [row_f32] + block_shapes(HALF_GRAD_COLS) + [small_shape],
        [
            pltpu.VMEM((D, 2048), F32),
            small_scratch,
            pltpu.VMEM((SEQ, D), BF16),
            pltpu.VMEM((SEQ, FF), BF16),
            ONES_WORK,
            pltpu.VMEM((SEQ, FF), F32),
            pltpu.VMEM((SEQ, D), F32),
        ],
        4 * 10**9,
        10 * 10**6,
        "ff_backward",
    )(*in_hbm([vectors]), w_ff, grad_stream, small_grads, *kept_ff)
    ff_sums = add_cores(keep_ff, send_ff, wide, n_high)
    other_sums = [jnp.concatenate(pair, axis=-1) for pair in zip(second_sums, ff_sums)]
    others_received = swap_plane(other_sums)
    kept_attention = (stream_first,) + tuple(kept[0:8]) + (kept[11],)
    keep_rest, send_rest, small_grads = call(
        functools.partial(attention_backward_kernel, fast),
        (count,),
        [full_spec(vectors), w_attention_spec, row_spec((SEQ, D)), hits_spec, small_spec]
        + [row_spec(a.shape[1:]) for a in kept_attention]
        + [ANY_SPEC],
        [blocks(HALF_GRAD_COLS)] * 2 + [pl.BlockSpec((SMALL_ROWS, D), lambda i: (0, 0))],
        block_shapes(HALF_GRAD_COLS) + [shaped((SMALL_ROWS, D), F32)],
        [pltpu.VMEM((D, 2048), F32), small_scratch]
        + [pltpu.VMEM((KEYS, D), BF16), pltpu.VMEM((SEQ, D), BF16)]
        + BACKWARD_WORK
        + [PROJ_WORK, pltpu.VMEM((SEQ, D), F32)],
        6 * 10**9,
        20 * 10**6,
        "attention_backward",
    )(*in_hbm([vectors]), w_attention, grad_mid, hits, small_grads, *kept_attention, other_sums[0])
    others_received, keep_rest = lax.optimization_barrier((others_received, keep_rest))
    rest_sums = add_cores(keep_rest, send_rest, wide, n_high)
    rest_received = swap_plane(rest_sums)
    other_pieces = column_pieces(add_plane(other_sums[0], others_received))
    rest_pieces = column_pieces(add_plane(rest_sums[0], rest_received))

    grad_rest, grad_others, table_part, small = call(
        functools.partial(finish_kernel, fast),
        None,
        [VMEM_SPEC] * (2 * n_high + 1),
        [VMEM_SPEC] * 4,
        [
            shaped((rows, HALF_GRAD_COLS), F32),
            shaped((rows, HALF_GRAD_COLS + HALF_SECOND_COLS), F32),
            shaped((rows, 512), F32),
            shaped((4 * n_high, rows + 8, 128), F32),
        ],
        [],
        10**6,
        10**6,
        "finish",
    )(*resident(rest_pieces + other_pieces), scalars)

    gathered = lax.all_to_all(small, "wide", 0, 0)
    beside = swap(gathered, "narrow", 1)
    quarters = []
    if not fast:
        total = lax.psum(small_grads, ("wide", "narrow"))
        quarters = [total.reshape(4, 8, 2, 128).transpose(0, 2, 1, 3).reshape(4, 16, 128)]
    swapped = swap(table_part, "narrow", 1)

    flat_params = [a for group in params for a in group]
    results = call(
        functools.partial(adam_kernel, fast),
        None,
        [VMEM_SPEC] * (32 + len(quarters)),
        [VMEM_SPEC] * 30,
        [shaped((1, 1), F32)] * 3 + [shaped(a.shape, F32) for a in flat_params],
        [pltpu.VMEM((SMALL_ROWS, D), F32)],
        10**6,
        10**6,
        "adam",
    )(grad_rest, grad_others, *resident([swapped, gathered, beside]), *quarters, *flat_params)
    news = list(results[3:])
    for group in (0, 2, 5, 8):
        for member in range(3 * group, 3 * group + 3):
            news[member] = flat(news[member])
    return tuple(a.reshape(()) for a in results[0:3]) + tuple(news)


def solution(mesh):
    placed = (
        P("wide", None, None),
        P("wide", None),
        P("wide"),
        P("wide", None),
        P("wide", None),
        P("wide", None),
        P(None, "wide"),
        P(None, "wide"),
        P(None, "wide"),
        P(None, None, "wide", "narrow"),
        P(None, None, "wide", "narrow"),
        P(None, None, "wide", "narrow"),
        P(None, "narrow", "wide"),
        P(None, "narrow", "wide"),
        P(None, "narrow", "wide"),
        P(None, "wide", "narrow"),
        P(None, "wide", "narrow"),
        P(None, "wide", "narrow"),
        P(None, "narrow"),
        P(None, "narrow"),
        P(None, "narrow"),
        P(None, "narrow", "wide"),
        P(None, "narrow", "wide"),
        P(None, "narrow", "wide"),
        P(),
        P(),
        P(),
        P("wide", "narrow"),
        P("wide", "narrow"),
        P("wide", "narrow"),
        P("wide", None),
        P("wide", None),
        P("wide", None),
    )
    return jax.shard_map(
        per_device,
        mesh=mesh,
        in_specs=placed,
        out_specs=(P(), P(), P()) + placed[6:],
        check_vma=False,
    )
```

```python
import functools

import jax
import jax.numpy as jnp
from jax import lax
from jax.experimental import pallas as pl
from jax.experimental.pallas import tpu as pltpu
from jax.sharding import PartitionSpec as P

D = 256
HEADS = 4
HEAD_DIM = 64
FF = 1024
VOCAB = 512
ACTIONS = 18
GAMES = 26
OBS = 16
FRAMES = 20
STEP_NUMBER = 5
FRAME_TOKENS = 17
LENGTH = 340
ROWS = 896
NVEC = 14

EPS_NORM = 1e-05
BETA_ONE = 0.5
BETA_TWO = 0.5
RATE_TABLE = 0.5
RATE_MATRIX = 0.05
RATE_VECTOR = 0.2
DECAY_RATE = 0.01
EPS_ADAM = 1e-08
CLIP_AT = 0.1

SEQ = 352
KEYS = 384
BLOCK, BLOCKS = 128, 3
TILE = 32
SIDE_ROWS = 32
QUERIES = HEADS * BLOCK
VALUE_ROWS = 80

COL_QKV, COL_PROJ, COL_UP, COL_DOWN, COL_LAYER = 0, 768, 1024, 2048, 3072
HALF_ATTENTION = ((0, 128, 0), (128, 128, 256), (256, 128, 512), (384, 128, COL_PROJ))
HALF_LAYER = HALF_ATTENTION + ((512, 512, COL_UP), (1024, 512, COL_DOWN))
COL_TABLE, COL_SMALL, COL_FIRST = 3072, 3968, 4096
HALF_FIRST = HALF_LAYER + ((1536, 512, COL_TABLE),)
HALF_FIRST_COLS = 2048
COL_HEAD, COL_SECOND = 3072, 3584
HALF_SECOND = HALF_LAYER + ((1536, 256, COL_HEAD),)
HALF_SECOND_COLS = 1792
GRAD_UP, GRAD_DOWN = 0, 1024
HALF_GRAD_FF = ((0, 512, GRAD_UP), (512, 512, GRAD_DOWN))
GRAD_TABLE, GRAD_SMALL = 1024, 1920
HALF_GRAD_REST = HALF_ATTENTION + ((512, 512, GRAD_TABLE),)
HALF_GRAD_COLS = 1024
SMALL_ROWS, SMALL_BIAS, SMALL_SIDE = 32, 14, 22

F32, BF16 = jnp.float32, jnp.bfloat16
MIB = 1024 * 1024


def dot_nn(a, b):
    return lax.dot_general(a, b, (((1,), (0,)), ((), ())), preferred_element_type=F32)


def dot_nt(a, b):
    return lax.dot_general(a, b, (((1,), (1,)), ((), ())), preferred_element_type=F32)


def dot_tn(a, b):
    return lax.dot_general(a, b, (((0,), (0,)), ((), ())), preferred_element_type=F32)


def places(fast):
    wide, core = lax.axis_index("wide"), lax.axis_index("narrow")
    return (wide if fast else 0), core, wide


def tiles(rows, size):
    return [slice(first, first + size) for first in range(0, rows, size)]


def normalise(x):
    centred = x - jnp.mean(x, axis=1, keepdims=True)
    scale = lax.rsqrt(jnp.mean(centred * centred, axis=1, keepdims=True) + EPS_NORM)
    return centred * scale, scale


def normalise_back(grad, xhat, scale, gain):
    inner = grad * gain
    mean_one = jnp.mean(inner, axis=1, keepdims=True)
    mean_two = jnp.mean(inner * xhat, axis=1, keepdims=True)
    return scale * (inner - mean_one - xhat * mean_two)


def column_sum(a):
    return jnp.sum(a, axis=0, keepdims=True)


def fold(a):
    return jnp.sum(a.reshape(a.shape[0] // 8, 8, a.shape[1]), axis=0)


def plus(total, a):
    return a if total is None else total + a


def block_lanes(i, h=None):
    if h is None:
        return slice(QUERIES * i, QUERIES * (i + 1))
    return slice(QUERIES * i + BLOCK * h, QUERIES * i + BLOCK * (h + 1))


def head_rows(h):
    return slice(HEAD_DIM * h, HEAD_DIM * (h + 1))


def spread_heads(source, target_ref):
    for h in range(HEADS):
        for i in range(BLOCKS):
            target_ref[head_rows(h), block_lanes(i, h)] = source[
                head_rows(h), BLOCK * i : BLOCK * (i + 1)
            ]


def causal_mask():
    key = lax.broadcasted_iota(jnp.int32, (BLOCK, QUERIES), 0)
    query = lax.broadcasted_iota(jnp.int32, (BLOCK, QUERIES), 1) & (BLOCK - 1)
    return jnp.where(key <= query, 0.0, -1e30)


def assemble(pieces_mine, pieces_other, place, w_ref, halves):
    me, core, _ = place
    is_first = core == 0
    for p in range(4):

        def block(z, _, p=p):
            row = pl.multiple_of((me ^ (4 * z + p)) * 16, 16)
            for src, width, dest in halves:
                mine = pieces_mine[p][z, :, src : src + width]
                other = pieces_other[p][z, :, src : src + width]
                if dest == COL_QKV:
                    mine, other = mine * 0.125, other * 0.125
                w_ref[pl.ds(row, 16), dest : dest + width] = jnp.where(is_first, mine, other)
                w_ref[pl.ds(row, 16), dest + width : dest + 2 * width] = jnp.where(
                    is_first, other, mine
                )
            return 0

        lax.fori_loop(0, 4, block, 0)


def disperse(g_ref, place, keep_ref, send_ref, halves, scaled=True):
    me, core, _ = place
    is_first = core == 0

    def block(i, _):
        p, z = i >> 2, i & 3
        row = pl.multiple_of((me ^ (4 * z + p)) * 16, 16)
        for src, width, dest in halves:
            low = g_ref[pl.ds(row, 16), dest : dest + width]
            high = g_ref[pl.ds(row, 16), dest + width : dest + 2 * width]
            if scaled and dest == COL_QKV:
                low, high = low * 0.125, high * 0.125
            keep_ref[p, z, :, src : src + width] = jnp.where(is_first, low, high).astype(BF16)
            send_ref[p, z, :, src : src + width] = jnp.where(is_first, high, low).astype(BF16)
        return 0

    lax.fori_loop(0, 16, block, 0)


def make_hits(meta_ref, hits_ref):
    for rows in tiles(SEQ, TILE):
        lane = lax.broadcasted_iota(jnp.int32, (TILE, ROWS), 1)
        place = lax.broadcasted_iota(jnp.int32, (TILE, 1), 0) + (VOCAB + ACTIONS + GAMES + rows.start)
        meta = meta_ref[rows]
        hit = (lane == meta[:, 0:1]) | (lane == meta[:, 1:2]) | (lane == place)
        hits_ref[rows] = jnp.where(hit, 1.0, 0.0).astype(BF16)


def gelu_and_slope(up):
    up = up.astype(BF16)
    square = up * up
    half = jax.nn.sigmoid(up * (BF16(1.5957691216057308) + BF16(0.0713548162726) * square))
    hidden = up * half
    slope = BF16(1.5957691216057308) + BF16(0.2140644488178) * square
    return hidden, half + hidden * (BF16(1.0) - half) * slope


def layer_forward(x_ref, w_ref, vec, bias, kept, work):
    qt_ref, kv_ref, p0, p1, p2, r_ref, ot_ref, o_ref, m_ref, h_ref, gp_ref, a_ref, c_ref = kept
    qst_ref, vt_ref, mask_ref, wqt_ref, long_ref, u_ref, y_ref = work
    for rows in tiles(SEQ, TILE):
        normed16 = (normalise(x_ref[rows])[0] * vec[0:1] + vec[1:2]).astype(BF16)
        a_ref[rows], long_ref[rows] = normed16, normed16
    kv_ref[0:SEQ] = dot_nn(long_ref[0:SEQ], w_ref[:, 256:768]).astype(BF16)
    kv_ref[SEQ:KEYS] = jnp.zeros((KEYS - SEQ, 512), BF16)
    qt_ref[...] = dot_nt(wqt_ref[...], long_ref[...]).astype(BF16)
    spread_heads(qt_ref, qst_ref)
    turned = jnp.transpose(kv_ref[:, 256:512])
    for h in range(HEADS):
        vt_ref[VALUE_ROWS * h : VALUE_ROWS * h + HEAD_DIM] = turned[head_rows(h)]
    for i, pt_ref in enumerate((p0, p1, p2)):
        seen, first = BLOCK * (i + 1), BLOCK * i
        scores = dot_nn(kv_ref[0:seen, 0:256], qst_ref[:, block_lanes(i)])
        last = scores[first:] + mask_ref[...]
        peak = jnp.max(last, axis=0, keepdims=True)
        if i:
            peak = jnp.maximum(peak, jnp.max(scores[0:first], axis=0, keepdims=True))
            pt_ref[0:first] = jnp.exp(scores[0:first] - peak).astype(BF16)
        pt_ref[first:seen] = jnp.exp(last - peak).astype(BF16)
        for h in range(HEADS):
            values = vt_ref[VALUE_ROWS * h : VALUE_ROWS * (h + 1), 0:seen]
            out = dot_nn(values, pt_ref[:, BLOCK * h : BLOCK * (h + 1)])
            inverse = 1.0 / out[HEAD_DIM : HEAD_DIM + 1]
            r_ref[h : h + 1, first:seen] = inverse
            ot_ref[head_rows(h), first:seen] = (out[0:HEAD_DIM] * inverse).astype(BF16)
    o_ref[...] = jnp.transpose(ot_ref[...])[0:SEQ]
    y_ref[...] = dot_nt(o_ref[...], w_ref[:, COL_PROJ : COL_PROJ + 256])
    for rows in tiles(SEQ, TILE):
        middle = x_ref[rows] + (y_ref[rows] + vec[2:3])
        m_ref[rows] = middle
        c_ref[rows] = (normalise(middle)[0] * vec[3:4] + vec[4:5]).astype(BF16)
    u_ref[...] = dot_nn(c_ref[...], w_ref[:, COL_UP : COL_UP + FF])
    for rows in tiles(SEQ, TILE):
        for first in range(0, FF, 256):
            cols = slice(first, first + 256)
            h_ref[rows, cols], gp_ref[rows, cols] = gelu_and_slope(u_ref[rows, cols] + bias[:, cols])
    y_ref[...] = dot_nt(h_ref[...], w_ref[:, COL_DOWN : COL_DOWN + FF])


def add_gradient(g_ref, column, left, right):
    g_ref[:, column : column + right.shape[1]] += dot_tn(left, right)


def ff_backward(grad_ref, grad16_ref, w_ref, w_up, w_down, vec, kept, v_ref, v_row, bias_row, work, mid_ref, mid16_refs):
    m_ref, gp_ref = kept
    du_ref, ones_ref, u_ref, y_ref = work
    u_ref[...] = dot_nn(grad16_ref[...], w_ref[:, w_down : w_down + FF])
    for rows in tiles(SEQ, TILE):
        du_ref[rows] = u_ref[rows].astype(BF16) * gp_ref[rows]
    bias_grad = dot_nn(ones_ref[...], du_ref[...])
    for chunk in range(4):
        v_ref[bias_row + chunk, 0:1] += bias_grad[0:1, 256 * chunk : 256 * chunk + 256]
    y_ref[...] = dot_nt(du_ref[...], w_ref[:, w_up : w_up + FF])
    totals = [None] * 3
    for rows in tiles(SEQ, TILE):
        xhat, scale = normalise(m_ref[rows])
        grad = y_ref[rows]
        mid = grad_ref[rows] + normalise_back(grad, xhat, scale, vec[3:4])
        mid_ref[rows] = mid
        for mid16_ref in mid16_refs:
            mid16_ref[rows] = mid.astype(BF16)
        for i, a in enumerate((mid, grad * xhat, grad)):
            totals[i] = plus(totals[i], fold(a))
    for i in range(3):
        v_ref[v_row + 2 + i] += totals[i]


def attention_backward(mid_ref, mid16_ref, w_ref, vec, kept, v_ref, v_row, work, out_ref):
    x_ref, qt_ref, kv_ref, p0, p1, p2, r_ref, ot_ref = kept
    dost_ref, qst_ref, kt_ref, dst_ref, dqt_ref, dkv_ref, dqkv_ref, proj_ref, y_ref = work
    grad_o = dot_nt(proj_ref[...], mid16_ref[...]).astype(BF16).astype(F32)
    kt_ref[...] = jnp.transpose(kv_ref[:, 0:256])
    deltas = []
    for h in range(HEADS):
        scaled = grad_o[head_rows(h)] * r_ref[h : h + 1]
        deltas.append(column_sum(scaled * ot_ref[head_rows(h)].astype(F32)))
        scaled = scaled.astype(BF16)
        for i in range(BLOCKS):
            dost_ref[head_rows(h), block_lanes(i, h)] = scaled[:, BLOCK * i : BLOCK * (i + 1)]
    for i, pt_ref in enumerate((p0, p1, p2)):
        seen, first = BLOCK * (i + 1), BLOCK * i
        lanes = block_lanes(i)
        delta = jnp.concatenate([a[:, first:seen] for a in deltas], axis=1)
        grad = dot_nn(kv_ref[0:seen, 256:512], dost_ref[:, lanes])
        dst_ref[0:seen, lanes] = pt_ref[...] * (grad - delta).astype(BF16)
        for h in range(HEADS):
            out = dot_nn(kt_ref[head_rows(h), 0:seen], dst_ref[0:seen, block_lanes(i, h)])
            dqt_ref[head_rows(h), first:seen] = out.astype(BF16)
        for at, left, right in (
            (0, dst_ref[0:seen, lanes], qst_ref),
            (256, pt_ref[...], dost_ref),
        ):
            out = dot_nt(left, right[:, lanes])
            if i:
                dkv_ref[0:first, at : at + 256] += out[0:first]
            dkv_ref[first:seen, at : at + 256] = out[first:]
    dqkv_ref[:, 0:256] = jnp.transpose(dqt_ref[...])[0:SEQ]
    dqkv_ref[:, 256:768] = dkv_ref[0:SEQ].astype(BF16)
    y_ref[...] = dot_nt(dqkv_ref[...], w_ref[:, COL_QKV : COL_QKV + 768])
    totals = [None] * 2
    for rows in tiles(SEQ, TILE):
        xhat, scale = normalise(x_ref[rows])
        grad = y_ref[rows]
        out = mid_ref[rows] + normalise_back(grad, xhat, scale, vec[0:1])
        out_ref[rows] = out.astype(out_ref.dtype)
        for i, a in enumerate((grad * xhat, grad)):
            totals[i] = plus(totals[i], fold(a))
    for i in range(2):
        v_ref[v_row + i] += totals[i]


def own_bias(place, mine, other):
    is_first = place[1] == 0
    return jnp.concatenate(
        [jnp.where(is_first, mine, other), jnp.where(is_first, other, mine)], axis=1
    )


def prepare_kernel(
    fast, games_ref, tokens, actions, valid, rewards, ends, out, out_side, x_ref
):
    count = out.shape[0]
    frames = tokens.shape[2]
    base = places(fast)[1] * count
    row = lax.broadcasted_iota(jnp.int32, (SEQ, frames), 0)
    start = lax.broadcasted_iota(jnp.int32, (SEQ, frames), 1) * FRAME_TOKENS
    here = jnp.where((row >= start) & (row < start + FRAME_TOKENS), 1.0, 0.0).astype(BF16)
    coming = jnp.where((row >= start - FRAME_TOKENS) & (row < start), 1.0, 0.0).astype(BF16)
    passed = jnp.sum(jnp.where(row >= start + FRAME_TOKENS, 1, 0), axis=1, keepdims=True)
    place = lax.broadcasted_iota(jnp.int32, (SEQ, 1), 0)
    spot = place - passed * FRAME_TOKENS
    lane = lax.broadcasted_iota(jnp.int32, (SEQ, 24), 1)
    wide_lane = lax.broadcasted_iota(jnp.int32, (SEQ, 128), 1)
    inside = place < LENGTH
    one_frame = (
        lax.broadcasted_iota(jnp.int32, (SIDE_ROWS, frames), 0)
        == lax.broadcasted_iota(jnp.int32, (SIDE_ROWS, frames), 1)
    )
    one_frame = jnp.where(one_frame, 1.0, 0.0).astype(BF16)
    side_lane = lax.broadcasted_iota(jnp.int32, (SIDE_ROWS, 128), 1)
    x_ref[...] = jnp.zeros(x_ref.shape, jnp.int32)
    for s in range(count):
        x_ref[0:OBS] = tokens[base + s]
        x_ref[16:17] = actions[pl.ds(base + s, 1)] + VOCAB
        x_ref[17:18] = valid[pl.ds(base + s, 1)]
        x_ref[18:19] = rewards[pl.ds(base + s, 1)]
        x_ref[19:20] = ends[pl.ds(base + s, 1)] + 3
        high = (x_ref[...] >> 4).astype(F32).astype(BF16)
        low = (x_ref[...] & 15).astype(F32).astype(BF16)
        now = dot_nt(here, high) * 16.0 + dot_nt(here, low)
        soon = dot_nt(coming, high) * 16.0 + dot_nt(coming, low)

        def pick(condition, a):
            return jnp.sum(jnp.where(condition, a, 0.0), axis=1, keepdims=True).astype(jnp.int32)

        ids = jnp.where(inside, pick(lane == spot, now), -1)
        game = jnp.where(inside, games_ref[base + s] + (VOCAB + ACTIONS), -1)
        target = pick((lane == spot + 1) & (spot < 15), now)
        target = target + pick((lane == 0) & (spot == 16), soon)
        weight = pick((lane == 17) & (spot < 15), now) + pick((lane == 17) & (spot == 16), soon)
        result = jnp.zeros((SEQ, 128), jnp.int32)
        for c, column in enumerate((ids, game, target, weight)):
            result = jnp.where(wide_lane == c, column, result)
        out[s] = result
        by_frame = dot_nt(one_frame, high) * 16.0 + dot_nt(one_frame, low)
        result = jnp.zeros((SIDE_ROWS, 128), jnp.int32)
        for c in range(3):
            column = by_frame[:, 17 + c : 18 + c].astype(jnp.int32)
            result = jnp.where(side_lane == c, column, result)
        out_side[s] = result


def start_forward(work, w_ref):
    qst_ref, vt_ref, mask_ref, wqt_ref, long_ref, u_ref, y_ref = work
    long_ref[SEQ:KEYS] = jnp.zeros((KEYS - SEQ, D), BF16)
    qst_ref[...] = jnp.zeros(qst_ref.shape, BF16)
    vt_ref[...] = jnp.ones(vt_ref.shape, BF16)
    mask_ref[...] = causal_mask()
    wqt_ref[...] = jnp.transpose(w_ref[:, 0:256])


def first_forward_kernel(fast, *refs):
    refs = (places(fast),) + refs
    place, meta_ref, vec_ref, bias_ref, bias_other = refs[0:5]
    mine, other = refs[5:9], refs[9:13]
    w_attention, w_ff, side_out, next_ref, hits_ref, x_ref = refs[13:19]
    kept = [ref.at[0] for ref in refs[19:32]]
    w_ref = refs[32]
    work = refs[33:40]

    @pl.when(pl.program_id(0) == 0)
    def _():
        assemble(mine, other, place, w_ref, HALF_FIRST)
        w_attention[...] = w_ref[:, 0:COL_UP]
        w_ff[...] = w_ref[:, COL_UP:COL_TABLE]
        side_out[...] = w_ref[:, COL_SMALL:]
        start_forward(work, w_ref)

    make_hits(meta_ref.at[0], hits_ref.at[0])
    x_ref[0] = dot_nt(hits_ref[0], w_ref[:, COL_TABLE : COL_TABLE + ROWS])
    bias = own_bias(place, bias_ref[0:1], bias_other[0:1])
    vec = vec_ref[0:6]
    layer_forward(x_ref.at[0], w_ref, vec, bias, kept, work)
    for rows in tiles(SEQ, TILE):
        next_ref[0, rows] = kept[8][rows] + (work[6][rows] + vec[5:6])


def codebook_losses(logits, meta):
    weight = meta[:, 3:4].astype(F32)
    peak = jnp.max(logits, axis=1, keepdims=True)
    expanded = jnp.exp(logits - peak)
    total = jnp.sum(expanded, axis=1, keepdims=True)
    hit = lax.broadcasted_iota(jnp.int32, logits.shape, 1) == meta[:, 2:3]
    hit = jnp.where(hit, weight, 0.0)
    return weight * (peak + jnp.log(total)), hit, expanded * (weight / total) - hit


def side_losses(side, meta):
    lane = lax.broadcasted_iota(jnp.int32, side.shape, 1)
    is_reward, is_end = lane < 3, (lane == 3) | (lane == 4)
    is_side = lane < 5
    weight = meta[:, 0:1].astype(F32)
    reward_peak = jnp.max(jnp.where(is_reward, side, -1e30), axis=1, keepdims=True)
    end_peak = jnp.max(jnp.where(is_end, side, -1e30), axis=1, keepdims=True)
    shifted = jnp.where(is_side, side - jnp.where(is_reward, reward_peak, end_peak), 0.0)
    expanded = jnp.where(is_side, jnp.exp(shifted), 0.0)
    reward_total = jnp.sum(jnp.where(is_reward, expanded, 0.0), axis=1, keepdims=True)
    end_total = jnp.sum(jnp.where(is_end, expanded, 0.0), axis=1, keepdims=True)
    hit = (lane == meta[:, 1:2]) | (lane == meta[:, 2:3])
    picked = jnp.sum(jnp.where(hit, side, 0.0), axis=1, keepdims=True)
    terms = reward_peak + jnp.log(reward_total) + end_peak + jnp.log(end_total) - picked
    grad = expanded * jnp.where(is_reward, weight / reward_total, weight / end_total)
    return weight * terms, grad - jnp.where(hit, weight, 0.0), weight


def frame_ends(shape, frame_axis):
    frame = lax.broadcasted_iota(jnp.int32, shape, frame_axis)
    row = lax.broadcasted_iota(jnp.int32, shape, 1 - frame_axis)
    hit = (row == frame * FRAME_TOKENS + OBS) & (frame < FRAMES)
    return jnp.where(hit, 1.0, 0.0).astype(BF16)


def middle_kernel(fast, *refs):
    refs = (places(fast),) + refs
    place, meta_ref, frame_ref, vec_ref, bias_ref, bias_other, side_ref, in_ref = refs[0:8]
    mine, other = refs[8:12], refs[12:16]
    grad_ref, keep_ref, send_ref, v_out, scalar_ref = refs[16:21]
    refs = refs[1:]
    w_ref, g_ref, v_ref = refs[20:23]
    kept = list(refs[23:36])
    forward_work = refs[36:43]
    u_ref, y_ref = forward_work[5:7]
    backward_work = list(refs[43:49])
    proj_ref = refs[49]
    du_all, ones_ref, up_ref, up16_all, mid_ref, mid16_ref = refs[50:56]
    last_ref, final_all, logit_ref, dlogit_all, pick_ref, put_ref, mid16_all = refs[56:63]
    o_all, h_all, a_all, c_all, dqkv_all = kept[7], kept[9], kept[11], kept[12], backward_work[5]
    dost_ref = backward_work[0]
    step = pl.program_id(0)

    @pl.when(step == 0)
    def _():
        assemble(mine, other, place, w_ref, HALF_SECOND)
        w_ref[:, COL_SECOND:] = side_ref[...]
        g_ref[...] = jnp.zeros(g_ref.shape, F32)
        v_ref[...] = jnp.zeros(v_ref.shape, F32)
        scalar_ref[...] = jnp.zeros(scalar_ref.shape, F32)
        start_forward(forward_work, w_ref)
        dost_ref[...] = jnp.zeros(dost_ref.shape, BF16)
        proj_ref[...] = jnp.transpose(w_ref[:, COL_PROJ : COL_PROJ + 256])
        ones_ref[...] = jnp.ones(ones_ref.shape, BF16)
        mid16_ref[SEQ:KEYS] = jnp.zeros((KEYS - SEQ, D), BF16)
        pick_ref[...] = frame_ends((SIDE_ROWS, SEQ), 0)
        put_ref[...] = frame_ends((SEQ, SIDE_ROWS), 1)

    here = pl.ds(pl.multiple_of((step & 1) * SEQ, 32), SEQ)
    for i in (7, 9, 11, 12):
        kept[i] = kept[i].at[here]
    m_ref, h_ref, gp_ref = kept[8:11]
    backward_work[5] = dqkv_all.at[here]
    du_ref, up16_ref, pair16_ref = du_all.at[here], up16_all.at[here], mid16_all.at[here]
    final_ref, dlogit_ref = final_all.at[here], dlogit_all.at[here]
    x_ref = in_ref.at[0]
    vec = vec_ref[6:12]
    bias = own_bias(place, bias_ref[1:2], bias_other[1:2])
    layer_forward(x_ref, w_ref, vec, bias, kept, forward_work)

    gain, offset = vec_ref[12:13], vec_ref[13:14]
    for rows in tiles(SEQ, TILE):
        last = m_ref[rows] + (y_ref[rows] + vec[5:6])
        last_ref[rows] = last
        final_ref[rows] = (normalise(last)[0] * gain + offset).astype(BF16)
    cols_head = slice(COL_HEAD, COL_HEAD + VOCAB + 128)
    logit_ref[...] = dot_nn(final_ref[...], w_ref[:, COL_HEAD : COL_HEAD + VOCAB])
    logs, picked = None, None
    for rows in tiles(SEQ, TILE):
        logits = logit_ref[rows]
        log, hit, grad = codebook_losses(logits, meta_ref[0, rows])
        dlogit_ref[rows, :VOCAB] = grad.astype(BF16)
        logs, picked = plus(logs, log), plus(picked, fold(hit * logits))
    acting = dot_nn(pick_ref[...], final_ref[...]).astype(BF16)
    side = dot_nn(acting, w_ref[:, COL_HEAD + VOCAB : COL_HEAD + VOCAB + 128])
    side_loss, grad, weight = side_losses(side, frame_ref[0])
    dlogit_ref[:, VOCAB:] = dot_nn(put_ref[...], grad.astype(BF16)).astype(BF16)
    loss = column_sum(logs) + column_sum(side_loss)
    loss = loss - jnp.sum(column_sum(picked), axis=1, keepdims=True)
    valid = column_sum(weight)
    scalar_lane = lax.broadcasted_iota(jnp.int32, (8, 128), 1)
    scalar_row = lax.broadcasted_iota(jnp.int32, (8, 128), 0) == 0
    scalar_ref[...] += jnp.where(
        scalar_row,
        jnp.where(scalar_lane == 0, loss, jnp.where(scalar_lane == 1, valid, 0.0)),
        0.0,
    )
    y_ref[...] = dot_nt(dlogit_ref[...], w_ref[:, cols_head])
    totals = [None] * 3
    for rows in tiles(SEQ, TILE):
        xhat, scale = normalise(last_ref[rows])
        grad = y_ref[rows]
        up = normalise_back(grad, xhat, scale, gain)
        up_ref[rows] = up
        up16_ref[rows] = up.astype(BF16)
        for i, a in enumerate((up, grad * xhat, grad)):
            totals[i] = plus(totals[i], fold(a))
    for i in range(3):
        v_ref[11 + i] += totals[i]
    ff_backward(
        up_ref,
        up16_ref,
        w_ref,
        COL_UP,
        COL_DOWN,
        vec,
        (m_ref, gp_ref),
        v_ref,
        6,
        SMALL_BIAS + 4,
        (du_ref, ones_ref, u_ref, y_ref),
        mid_ref,
        (mid16_ref, pair16_ref),
    )
    attention_backward(
        mid_ref,
        mid16_ref,
        w_ref,
        vec,
        (x_ref,) + tuple(kept[0:7]),
        v_ref,
        6,
        (dost_ref, forward_work[0]) + tuple(backward_work[1:]) + (proj_ref, y_ref),
        grad_ref.at[0],
    )

    @pl.when(step & 1 == 1)
    def _():
        add_gradient(g_ref, COL_QKV, a_all[...], dqkv_all[...])
        add_gradient(g_ref, COL_PROJ, mid16_all[...], o_all[...])
        add_gradient(g_ref, COL_UP, c_all[...], du_all[...])
        add_gradient(g_ref, COL_DOWN, up16_all[...], h_all[...])
        add_gradient(g_ref, COL_HEAD, final_all[...], dlogit_all[...])

    @pl.when(step == pl.num_programs(0) - 1)
    def _():
        disperse(g_ref, place, keep_ref, send_ref, HALF_SECOND)
        side = jnp.transpose(g_ref[:, COL_SECOND:])
        for i in range(5):
            v_ref[SMALL_SIDE + i, 0:1] = side[i : i + 1]
        v_out[...] = v_ref[...]


def ff_backward_kernel(fast, *refs):
    vec_ref, w_ref, grad_ref, v_in, m_ref, gp_ref, h_all, c_all = refs[0:8]
    mid_ref, keep_ref, send_ref, v_out = refs[8:12]
    g_ref, v_ref, grad16_all, du_all, ones_ref, u_ref, y_ref = refs[12:19]
    step = pl.program_id(0)

    @pl.when(step == 0)
    def _():
        v_ref[...] = v_in[...]
        ones_ref[...] = jnp.ones(ones_ref.shape, BF16)

    here = pl.ds(pl.multiple_of(step * SEQ, 32), SEQ)
    grad16_ref = grad16_all.at[here]
    total = None
    for rows in tiles(SEQ, TILE):
        grad = grad_ref[0, rows]
        grad16_ref[rows] = grad.astype(BF16)
        total = plus(total, fold(grad))
    v_ref[5] += total
    ff_backward(
        grad_ref.at[0],
        grad16_ref,
        w_ref,
        GRAD_UP,
        GRAD_DOWN,
        vec_ref[0:6],
        (m_ref.at[0], gp_ref.at[0]),
        v_ref,
        0,
        SMALL_BIAS,
        (du_all.at[here], ones_ref, u_ref, y_ref),
        mid_ref.at[0],
        (),
    )

    @pl.when(step == pl.num_programs(0) - 1)
    def _():
        g_ref[:, GRAD_UP : GRAD_UP + FF] = dot_tn(c_all[...], du_all[...])
        g_ref[:, GRAD_DOWN : GRAD_DOWN + FF] = dot_tn(grad16_all[...], h_all[...])
        disperse(g_ref, places(fast), keep_ref, send_ref, HALF_GRAD_FF, False)
        v_out[...] = v_ref[...]


def attention_backward_kernel(fast, *refs):
    vec_ref, w_ref, mid_ref, v_in = refs[0:4]
    kept = [ref.at[0] for ref in refs[4:12]]
    o_all, a_all, hits_all = refs[12:15]
    keep_ref, send_ref, v_out = refs[16:19]
    g_ref, v_ref, mid16_ref, mid16_all, out16_all, dqkv_all = refs[19:25]
    work = list(refs[25:33])
    dost_ref, qst_ref, proj_ref = work[0], work[1], work[6]
    step = pl.program_id(0)

    @pl.when(step == 0)
    def _():
        v_ref[...] = v_in[...]
        dost_ref[...] = jnp.zeros(dost_ref.shape, BF16)
        qst_ref[...] = jnp.zeros(qst_ref.shape, BF16)
        proj_ref[...] = jnp.transpose(w_ref[:, COL_PROJ : COL_PROJ + 256])
        mid16_ref[SEQ:KEYS] = jnp.zeros((KEYS - SEQ, D), BF16)

    here = pl.ds(pl.multiple_of(step * SEQ, 32), SEQ)
    all16_ref = mid16_all.at[here]
    spread_heads(kept[1], qst_ref)
    for rows in tiles(SEQ, TILE):
        mid16 = mid_ref[0, rows].astype(BF16)
        mid16_ref[rows], all16_ref[rows] = mid16, mid16
    work.insert(6, dqkv_all.at[here])
    attention_backward(
        mid_ref.at[0],
        mid16_ref,
        w_ref,
        vec_ref[0:6],
        kept,
        v_ref,
        0,
        work,
        out16_all.at[here],
    )

    @pl.when(step == pl.num_programs(0) - 1)
    def _():
        g_ref[:, COL_QKV : COL_QKV + 768] = dot_tn(a_all[...], dqkv_all[...])
        g_ref[:, COL_PROJ : COL_PROJ + 256] = dot_tn(mid16_all[...], o_all[...])
        g_ref[:, GRAD_TABLE : GRAD_TABLE + ROWS] = dot_tn(out16_all[...], hits_all[...])
        small = jnp.sum(v_ref[...], axis=1)
        v_out[...] = small
        for block in range(16):
            quarter = small[8 * (block // 4) : 8 * (block // 4) + 8]
            g_ref[16 * block : 16 * block + 8, GRAD_SMALL:] = quarter[:, 0:128]
            g_ref[16 * block + 8 : 16 * block + 16, GRAD_SMALL:] = quarter[:, 128:256]
        disperse(g_ref, places(fast), keep_ref, send_ref, HALF_GRAD_REST)


def pack_layer(attn, proj, up, down, layer, out):
    for j in range(3):
        out[:, 128 * j : 128 * j + 128] = attn[layer, j].astype(BF16)
    out[:, 384:512] = proj[layer].astype(BF16)
    out[:, 512:1024] = up[layer].astype(BF16)
    out[:, 1024:1536] = down[layer].astype(BF16)


def pack_kernel(fast, table, attn, proj, up, down, head, side, first, second, pad_ref):
    pack_layer(attn, proj, up, down, 0, first)
    pack_layer(attn, proj, up, down, 1, second)
    second[:, 1536:1792] = head[...].astype(BF16)
    rows = side.shape[1]
    eye = (
        lax.broadcasted_iota(jnp.int32, (rows, rows), 0)
        == lax.broadcasted_iota(jnp.int32, (rows, rows), 1)
    )
    eye = jnp.where(eye, 1.0, 0.0).astype(BF16)
    pad_ref[...] = jnp.zeros(pad_ref.shape, F32)
    pad_ref[:, 0:5] = dot_nt(eye, side[...].astype(BF16))
    high = jnp.concatenate([table[:, 512:896], pad_ref[...]], axis=1)
    first[:, 1536:2048] = jnp.where(places(fast)[1] == 0, table[:, 0:512], high).astype(BF16)


def finish_kernel(fast, *refs):
    count = (len(refs) - 5) // 2
    scalar_ref = refs[2 * count]
    out_rest, out_other, out_table, out_small = refs[2 * count + 1 :]
    square = jnp.zeros((1, 1), F32)
    for pieces, out in ((refs[0:count], out_rest), (refs[count : 2 * count], out_other)):
        total = pieces[0][...]
        for piece in pieces[1:]:
            total = total + piece[...].astype(F32)
        out[...] = total
        square = square + column_sum(jnp.sum(total * total, axis=1, keepdims=True))
    small = out_rest[:, 896:1024]
    extra = column_sum(jnp.sum(small * small, axis=1, keepdims=True))
    square = square - jnp.where(places(fast)[1] == 0, 0.0, extra)
    out_table[...] = out_rest[:, 512:1024]
    rows = small.shape[0]
    lane = lax.broadcasted_iota(jnp.int32, (8, 128), 1)
    top = lax.broadcasted_iota(jnp.int32, (8, 128), 0) == 0
    scalars = scalar_ref[...] + jnp.where(top & (lane == 2), square, 0.0)
    for i in range(out_small.shape[0]):
        out_small[i, 0:rows] = small
        out_small[i, rows : rows + 8] = scalars


def adam_rule(weight, moment, second, gradient, step_rate, decay_rate):
    moment_new = BETA_ONE * moment + (1.0 - BETA_ONE) * gradient
    second_new = BETA_TWO * second + (1.0 - BETA_TWO) * gradient * gradient
    moment_hat = moment_new / (1.0 - BETA_ONE**STEP_NUMBER)
    second_hat = second_new / (1.0 - BETA_TWO**STEP_NUMBER)
    weight_new = weight - step_rate * (
        moment_hat / (jnp.sqrt(second_hat) + EPS_ADAM) + decay_rate * weight
    )
    return (weight_new, moment_new, second_new)


def adam_kernel(fast, rest, others, swapped, gathered, beside, *refs):
    rows = rest.shape[0]
    _, core, wide = places(fast)
    is_first = core == 0
    if fast:
        quarters = [jnp.where(is_first, beside[4 * z], gathered[4 * z]) for z in range(4)]
    else:
        quarters = [refs[0][z] for z in range(4)]
        refs = refs[1:]
    params = [refs[3 * i : 3 * i + 3] for i in range(9)]
    loss_ref, valid_ref, norm_ref = refs[27:30]
    outs = [refs[30 + 3 * i : 33 + 3 * i] for i in range(9)]
    small_ref = refs[57]
    for z in range(4):
        small_ref[8 * z : 8 * z + 8, 0:128] = quarters[z][0:8]
        small_ref[8 * z : 8 * z + 8, 128:256] = quarters[z][8:16]
    sums = []
    for source in (gathered, beside):
        total = source[0, rows : rows + 1]
        for i in range(1, source.shape[0]):
            total = total + source[i, rows : rows + 1]
        sums.append(total)
    scalars = sums[0] + sums[1]
    small = small_ref[...]
    loss, valid, square = scalars[:, 0:1], scalars[:, 1:2], scalars[:, 2:3]
    square = square + column_sum(jnp.sum(small * small, axis=1, keepdims=True))
    inverse = 1.0 / valid
    norm = jnp.sqrt(square) * inverse
    loss_ref[...], valid_ref[...], norm_ref[...] = loss, valid, norm
    factor = jnp.minimum(1.0, CLIP_AT / (norm + 1e-06)) * inverse
    table, attn, proj, up, bias, down, vectors, head, side = range(9)

    def update(which, index, gradient, step_rate, decay_rate):
        news = adam_rule(
            *(ref[index] for ref in params[which]), factor * gradient, step_rate, decay_rate
        )
        for ref, new in zip(outs[which], news):
            ref[index] = new

    layers = ((rest, others, 1792), (others, others, 512))
    for layer, (attention, feed, at) in enumerate(layers):
        for j in range(3):
            update(attn, (layer, j), attention[:, 128 * j : 128 * j + 128], RATE_MATRIX, DECAY_RATE)
        update(proj, (layer,), attention[:, 384:512], RATE_MATRIX, DECAY_RATE)
        update(up, (layer,), feed[:, at : at + 512], RATE_MATRIX, DECAY_RATE)
        update(down, (layer,), feed[:, at + 512 : at + 1024], RATE_MATRIX, DECAY_RATE)
        for i in range(2):
            low = SMALL_BIAS + 4 * layer + i
            row = jnp.where(is_first, small[low : low + 1], small[low + 2 : low + 3])
            index = (slice(layer, layer + 1), slice(256 * i, 256 * i + 256))
            update(bias, index, row, RATE_VECTOR, 0.0)
    whole = (slice(None), slice(None))
    update(head, whole, others[:, 1536:1792], RATE_MATRIX, DECAY_RATE)
    mine, theirs = rest[:, 512:1024], swapped[:, 0:512]
    low, high = jnp.where(is_first, mine, theirs), jnp.where(is_first, theirs, mine)
    update(table, (slice(None), slice(0, 512)), low, RATE_TABLE, DECAY_RATE)
    update(table, (slice(None), slice(512, 896)), high[:, 0:384], RATE_TABLE, DECAY_RATE)
    update(vectors, whole, small[0:NVEC], RATE_VECTOR, 0.0)
    turned = pltpu.roll(small[SMALL_SIDE : SMALL_SIDE + 8], lax.rem(D - wide * rows, D), 1)
    update(side, whole, turned[0:5, 0:rows], RATE_MATRIX, DECAY_RATE)


def swap(a, axis, distance):
    size = lax.axis_size(axis)
    return lax.ppermute(a, axis, [(i, i ^ distance) for i in range(size)])


def swap_column(piece, n_high):
    return [piece] + [swap(piece, "wide", 4 * k) for k in range(1, n_high)]


def gather_plane(column):
    return [column] + [swap(column, "wide", p) for p in range(1, 4)]


def gather_cores(mine):
    return [swap(a, "narrow", 1) for a in mine]


def in_blocks(parts, wide):
    n_high, rows, cols = parts[0].shape
    if rows == 16:
        return parts
    whole = jnp.stack(parts, axis=1).reshape(4 * n_high, rows, cols)
    whole = whole[wide ^ jnp.arange(4 * n_high)].reshape(4, 4, 16, cols)
    return [whole[:, p] for p in range(4)]


def in_pieces(blocks, wide, n_high):
    cols = blocks.shape[-1]
    if n_high == 4:
        return blocks
    rows = 64 // n_high
    whole = blocks.transpose(1, 0, 2, 3).reshape(4 * n_high, rows, cols)
    whole = whole[wide ^ jnp.arange(4 * n_high)]
    return whole.reshape(n_high, 4, rows, cols).transpose(1, 0, 2, 3)


def add_cores(keep, send, wide, n_high):
    keep, send = in_pieces(keep, wide, n_high), in_pieces(send, wide, n_high)
    received = swap(send, "narrow", 1)
    return [keep[p].astype(F32) + received[p].astype(F32) for p in range(4)]


def swap_plane(sums):
    return [swap(sums[p].astype(BF16), "wide", p) for p in range(1, 4)]


def add_plane(own, received):
    for a in received:
        own = own + a.astype(F32)
    return own


def column_pieces(own):
    return [own[0]] + [swap(own[k].astype(BF16), "wide", 4 * k) for k in range(1, own.shape[0])]


def resident(arrays):
    return [pltpu.with_memory_space_constraint(a, pltpu.VMEM) for a in arrays]


def in_hbm(arrays):
    return [pltpu.with_memory_space_constraint(a, pltpu.HBM) for a in arrays]


def full_spec(a):
    return pl.BlockSpec(a.shape, lambda *_: (0,) * len(a.shape))


def row_spec(shape):
    return pl.BlockSpec((1,) + shape, lambda i: (i,) + (0,) * len(shape))


def shaped(shape, dtype):
    return jax.ShapeDtypeStruct(shape, dtype)


VMEM_SPEC = pl.BlockSpec(memory_space=pltpu.VMEM)
ANY_SPEC = pl.BlockSpec(memory_space=pl.ANY)
SMEM_SPEC = pl.BlockSpec(memory_space=pltpu.SMEM)


VMEM_MIB = {
    "pack": 58,
    "prepare": 58,
    "first_forward": 24,
    "middle": 31,
    "ff_backward": 24,
    "attention_backward": 26,
    "finish": 58,
    "adam": 58,
}


def call(kernel, grid, in_specs, out_specs, out_shape, scratch, flops, bytes_accessed, name):
    extra = {"grid": grid} if grid else {}
    return pl.pallas_call(
        kernel,
        in_specs=in_specs,
        out_specs=out_specs,
        out_shape=out_shape,
        scratch_shapes=scratch,
        compiler_params=pltpu.CompilerParams(vmem_limit_bytes=VMEM_MIB[name] * MIB),
        cost_estimate=pl.CostEstimate(
            flops=flops, bytes_accessed=bytes_accessed, transcendentals=0
        ),
        name=name,
        **extra,
    )


KEPT = (
    ((D, KEYS), BF16),
    ((KEYS, 512), BF16),
    ((BLOCK, QUERIES), BF16),
    ((2 * BLOCK, QUERIES), BF16),
    ((3 * BLOCK, QUERIES), BF16),
    ((8, KEYS), F32),
    ((D, KEYS), BF16),
    ((SEQ, D), BF16),
    ((SEQ, D), F32),
    ((SEQ, FF), BF16),
    ((SEQ, FF), BF16),
    ((SEQ, D), BF16),
    ((SEQ, D), BF16),
)
FORWARD_WORK = [
    pltpu.VMEM((D, BLOCKS * QUERIES), BF16),
    pltpu.VMEM((HEADS * VALUE_ROWS, KEYS), BF16),
    pltpu.VMEM((BLOCK, QUERIES), F32),
    pltpu.VMEM((D, D), BF16),
    pltpu.VMEM((KEYS, D), BF16),
    pltpu.VMEM((SEQ, FF), F32),
    pltpu.VMEM((SEQ, D), F32),
]
BACKWARD_WORK = [
    pltpu.VMEM((D, BLOCKS * QUERIES), BF16),
    pltpu.VMEM((D, BLOCKS * QUERIES), BF16),
    pltpu.VMEM((D, KEYS), BF16),
    pltpu.VMEM((KEYS, BLOCKS * QUERIES), BF16),
    pltpu.VMEM((D, KEYS), BF16),
    pltpu.VMEM((KEYS, 512), F32),
    pltpu.VMEM((SEQ, 768), BF16),
]
PROJ_WORK = pltpu.VMEM((D, D), BF16)
ONES_WORK = pltpu.VMEM((16, SEQ), BF16)


def per_device(
    tokens,
    actions,
    game_ids,
    valid_steps,
    rewards,
    end_flags,
    embed_table,
    table_first,
    table_second,
    attn_weight,
    attn_first,
    attn_second,
    proj_weight,
    proj_first,
    proj_second,
    up_weight,
    up_first,
    up_second,
    up_bias,
    bias_first,
    bias_second,
    down_weight,
    down_first,
    down_second,
    vectors,
    vectors_first,
    vectors_second,
    head_weight,
    head_first,
    head_second,
    side_weight,
    side_first,
    side_second,
):
    n_high = lax.axis_size("wide") // 4
    wide = lax.axis_index("wide")
    rows = side_weight.shape[0]
    fast = rows == 16

    def flat(a):
        return jnp.swapaxes(a, -1, -2)

    params = (
        (flat(embed_table), flat(table_first), flat(table_second)),
        (attn_weight, attn_first, attn_second),
        (flat(proj_weight), flat(proj_first), flat(proj_second)),
        (up_weight, up_first, up_second),
        (up_bias, bias_first, bias_second),
        (flat(down_weight), flat(down_first), flat(down_second)),
        (vectors, vectors_first, vectors_second),
        (head_weight, head_first, head_second),
        (flat(side_weight), flat(side_first), flat(side_second)),
    )
    table, attn, proj, up, _, down, _, head, side = (group[0] for group in params)

    piece_first, piece_second = call(
        functools.partial(pack_kernel, fast),
        None,
        [VMEM_SPEC] * 7,
        [VMEM_SPEC] * 2,
        [shaped((rows, HALF_FIRST_COLS), BF16), shaped((rows, HALF_SECOND_COLS), BF16)],
        [pltpu.VMEM((rows, 128), F32)],
        10**6,
        10**6,
        "pack",
    )(table, attn, proj, up, down, head, side)
    other_bias = swap(up_bias, "narrow", 1)
    column = swap_column(piece_first, n_high)

    count = tokens.shape[0] // lax.axis_size("narrow")
    meta, frame_meta = call(
        functools.partial(prepare_kernel, fast),
        None,
        [SMEM_SPEC] + [VMEM_SPEC] * 5,
        [VMEM_SPEC] * 2,
        [shaped((count, SEQ, 128), jnp.int32), shaped((count, SIDE_ROWS, 128), jnp.int32)],
        [pltpu.VMEM((24, FRAMES), jnp.int32)],
        10**6,
        10**6,
        "prepare",
    )(game_ids, flat(tokens), actions, valid_steps, rewards, end_flags)
    column, other_bias, meta = lax.optimization_barrier((column, other_bias, meta))
    first_column = jnp.stack(column)
    first_mine = gather_plane(first_column)
    own, piece_second = lax.optimization_barrier((swap(first_column, "narrow", 1), piece_second))
    second_column = jnp.stack(swap_column(piece_second, n_high))
    second_column, across = lax.optimization_barrier((second_column, first_mine[3]))
    first_mine = first_mine[0:3] + [across]
    first_other = [own] + gather_cores(first_mine[1:])
    second_mine = gather_plane(second_column)
    first_parts = in_blocks(first_mine, wide) + in_blocks(first_other, wide)

    kept_specs = [row_spec(shape) for shape, _ in KEPT]
    kept_shapes = [shaped((count,) + shape, dtype) for shape, dtype in KEPT]
    row_f32 = shaped((count, SEQ, D), F32)
    meta_spec = row_spec((SEQ, 128))
    vec_specs = [full_spec(vectors), full_spec(up_bias), full_spec(up_bias)]
    w_attention_spec = pl.BlockSpec((D, 1024), lambda i: (0, 0))
    w_ff_spec = pl.BlockSpec((D, 2048), lambda i: (0, 0))
    side_spec = pl.BlockSpec((D, 128), lambda i: (0, 0))
    hits_spec = row_spec((SEQ, ROWS))
    results = call(
        functools.partial(first_forward_kernel, fast),
        (count,),
        [meta_spec] + vec_specs + [VMEM_SPEC] * 8,
        [w_attention_spec, w_ff_spec, side_spec, row_spec((SEQ, D)), hits_spec, row_spec((SEQ, D))]
        + kept_specs,
        [shaped((D, 1024), BF16), shaped((D, 2048), BF16), shaped((D, 128), BF16), row_f32]
        + [shaped((count, SEQ, ROWS), BF16), row_f32]
        + kept_shapes,
        [pltpu.VMEM((D, COL_FIRST), BF16)] + FORWARD_WORK,
        4 * 10**9,
        20 * 10**6,
        "first_forward",
    )(*in_hbm([meta, vectors, up_bias, other_bias]), *resident(first_parts))
    w_attention, w_ff, side_copy, stream, hits, stream_first = results[0:6]
    kept = results[6:]
    received, side_copy = lax.optimization_barrier((second_mine[1:], side_copy))
    second_mine = second_mine[0:1] + received
    second_other = gather_cores(second_mine)
    second_parts = in_blocks(second_mine, wide) + in_blocks(second_other, wide)

    def blocks(cols):
        return pl.BlockSpec((4, 4, 16, cols), lambda i: (0, 0, 0, 0))

    def block_shapes(cols):
        return [shaped((4, 4, 16, cols), BF16)] * 2

    small_spec = pl.BlockSpec((SMALL_ROWS, 8, D), lambda i: (0, 0, 0))
    small_shape = shaped((SMALL_ROWS, 8, D), F32)
    small_scratch = pltpu.VMEM((SMALL_ROWS, 8, D), F32)
    scalar_spec = pl.BlockSpec((8, 128), lambda i: (0, 0))
    grad_stream, keep_second, send_second, small_grads, scalars = call(
        functools.partial(middle_kernel, fast),
        (count,),
        [meta_spec, row_spec((SIDE_ROWS, 128))]
        + vec_specs
        + [side_spec, row_spec((SEQ, D))]
        + [VMEM_SPEC] * 8,
        [row_spec((SEQ, D))] + [blocks(HALF_SECOND_COLS)] * 2 + [small_spec, scalar_spec],
        [row_f32] + block_shapes(HALF_SECOND_COLS) + [small_shape, shaped((8, 128), F32)],
        [
            pltpu.VMEM((D, COL_SECOND + 128), BF16),
            pltpu.VMEM((D, COL_SECOND + 128), F32),
            small_scratch,
        ]
        + [pltpu.VMEM(shape, dtype) for shape, dtype in KEPT[0:7]]
        + [pltpu.VMEM((2 * SEQ, D), BF16), pltpu.VMEM(*KEPT[8])]
        + [pltpu.VMEM((2 * SEQ, FF), BF16), pltpu.VMEM(*KEPT[10])]
        + [pltpu.VMEM((2 * SEQ, D), BF16)] * 2
        + FORWARD_WORK
        + BACKWARD_WORK[0:1]
        + BACKWARD_WORK[2:6]
        + [pltpu.VMEM((2 * SEQ, 768), BF16)]
        + [
            PROJ_WORK,
            pltpu.VMEM((2 * SEQ, FF), BF16),
            ONES_WORK,
            pltpu.VMEM((SEQ, D), F32),
            pltpu.VMEM((2 * SEQ, D), BF16),
            pltpu.VMEM((SEQ, D), F32),
            pltpu.VMEM((KEYS, D), BF16),
            pltpu.VMEM((SEQ, D), F32),
            pltpu.VMEM((2 * SEQ, D), BF16),
            pltpu.VMEM((SEQ, VOCAB), F32),
            pltpu.VMEM((2 * SEQ, VOCAB + 128), BF16),
            pltpu.VMEM((SIDE_ROWS, SEQ), BF16),
            pltpu.VMEM((SEQ, SIDE_ROWS), BF16),
            pltpu.VMEM((2 * SEQ, D), BF16),
        ],
        15 * 10**9,
        20 * 10**6,
        "middle",
    )(
        *in_hbm([meta, frame_meta, vectors, up_bias, other_bias]),
        side_copy,
        stream,
        *resident(second_parts),
    )
    second_sums = add_cores(keep_second, send_second, wide, n_high)

    def joined(a):
        return a.reshape((count * a.shape[1],) + a.shape[2:])

    joined_ff = [joined(kept[9]), joined(kept[12])]
    grad_mid, keep_ff, send_ff, small_grads = call(
        functools.partial(ff_backward_kernel, fast),
        (count,),
        [full_spec(vectors), w_ff_spec, row_spec((SEQ, D)), small_spec]
        + [row_spec(a.shape[1:]) for a in (kept[8], kept[10])]
        + [VMEM_SPEC] * 2,
        [row_spec((SEQ, D))] + [blocks(HALF_GRAD_COLS)] * 2 + [small_spec],
        [row_f32] + block_shapes(HALF_GRAD_COLS) + [small_shape],
        [
            pltpu.VMEM((D, 2048), F32),
            small_scratch,
            pltpu.VMEM((count * SEQ, D), BF16),
            pltpu.VMEM((count * SEQ, FF), BF16),
            ONES_WORK,
            pltpu.VMEM((SEQ, FF), F32),
            pltpu.VMEM((SEQ, D), F32),
        ],
        4 * 10**9,
        10 * 10**6,
        "ff_backward",
    )(*in_hbm([vectors]), w_ff, grad_stream, small_grads, kept[8], kept[10], *joined_ff)
    ff_sums = add_cores(keep_ff, send_ff, wide, n_high)
    other_sums = [jnp.concatenate(pair, axis=-1) for pair in zip(second_sums, ff_sums)]
    others_received = swap_plane(other_sums)
    kept_attention = (stream_first,) + tuple(kept[0:7])
    joined_attention = [joined(kept[7]), joined(kept[11]), joined(hits)]
    keep_rest, send_rest, small_grads = call(
        functools.partial(attention_backward_kernel, fast),
        (count,),
        [full_spec(vectors), w_attention_spec, row_spec((SEQ, D)), small_spec]
        + [row_spec(a.shape[1:]) for a in kept_attention]
        + [VMEM_SPEC] * 3
        + [ANY_SPEC],
        [blocks(HALF_GRAD_COLS)] * 2 + [pl.BlockSpec((SMALL_ROWS, D), lambda i: (0, 0))],
        block_shapes(HALF_GRAD_COLS) + [shaped((SMALL_ROWS, D), F32)],
        [pltpu.VMEM((D, 2048), F32), small_scratch, pltpu.VMEM((KEYS, D), BF16)]
        + [pltpu.VMEM((count * SEQ, D), BF16)] * 2
        + [pltpu.VMEM((count * SEQ, 768), BF16)]
        + BACKWARD_WORK[0:6]
        + [PROJ_WORK, pltpu.VMEM((SEQ, D), F32)],
        6 * 10**9,
        20 * 10**6,
        "attention_backward",
    )(
        *in_hbm([vectors]),
        w_attention,
        grad_mid,
        small_grads,
        *kept_attention,
        *joined_attention,
        other_sums[0],
    )
    others_received, keep_rest = lax.optimization_barrier((others_received, keep_rest))
    rest_sums = add_cores(keep_rest, send_rest, wide, n_high)
    rest_received = swap_plane(rest_sums)
    other_pieces = column_pieces(add_plane(other_sums[0], others_received))
    rest_pieces = column_pieces(add_plane(rest_sums[0], rest_received))

    grad_rest, grad_others, table_part, small = call(
        functools.partial(finish_kernel, fast),
        None,
        [VMEM_SPEC] * (2 * n_high + 1),
        [VMEM_SPEC] * 4,
        [
            shaped((rows, HALF_GRAD_COLS), F32),
            shaped((rows, HALF_GRAD_COLS + HALF_SECOND_COLS), F32),
            shaped((rows, 512), F32),
            shaped((4 * n_high, rows + 8, 128), F32),
        ],
        [],
        10**6,
        10**6,
        "finish",
    )(*resident(rest_pieces + other_pieces), scalars)

    gathered = lax.all_to_all(small, "wide", 0, 0)
    beside = swap(gathered, "narrow", 1)
    quarters = []
    if not fast:
        total = lax.psum(small_grads, ("wide", "narrow"))
        quarters = [total.reshape(4, 8, 2, 128).transpose(0, 2, 1, 3).reshape(4, 16, 128)]
    swapped = swap(table_part, "narrow", 1)

    flat_params = [a for group in params for a in group]
    results = call(
        functools.partial(adam_kernel, fast),
        None,
        [VMEM_SPEC] * (32 + len(quarters)),
        [VMEM_SPEC] * 30,
        [shaped((1, 1), F32)] * 3 + [shaped(a.shape, F32) for a in flat_params],
        [pltpu.VMEM((SMALL_ROWS, D), F32)],
        10**6,
        10**6,
        "adam",
    )(grad_rest, grad_others, *resident([swapped, gathered, beside]), *quarters, *flat_params)
    news = list(results[3:])
    for group in (0, 2, 5, 8):
        for member in range(3 * group, 3 * group + 3):
            news[member] = flat(news[member])
    return tuple(a.reshape(()) for a in results[0:3]) + tuple(news)


def solution(mesh):
    placed = (
        P("wide", None, None),
        P("wide", None),
        P("wide"),
        P("wide", None),
        P("wide", None),
        P("wide", None),
        P(None, "wide"),
        P(None, "wide"),
        P(None, "wide"),
        P(None, None, "wide", "narrow"),
        P(None, None, "wide", "narrow"),
        P(None, None, "wide", "narrow"),
        P(None, "narrow", "wide"),
        P(None, "narrow", "wide"),
        P(None, "narrow", "wide"),
        P(None, "wide", "narrow"),
        P(None, "wide", "narrow"),
        P(None, "wide", "narrow"),
        P(None, "narrow"),
        P(None, "narrow"),
        P(None, "narrow"),
        P(None, "narrow", "wide"),
        P(None, "narrow", "wide"),
        P(None, "narrow", "wide"),
        P(),
        P(),
        P(),
        P("wide", "narrow"),
        P("wide", "narrow"),
        P("wide", "narrow"),
        P("wide", None),
        P("wide", None),
        P("wide", None),
    )
    return jax.shard_map(
        per_device,
        mesh=mesh,
        in_specs=placed,
        out_specs=(P(), P(), P()) + placed[6:],
        check_vma=False,
    )
```

```python
import functools

import jax
import jax.numpy as jnp
from jax import lax
from jax.experimental import pallas as pl
from jax.experimental.pallas import tpu as pltpu
from jax.sharding import PartitionSpec as P

D = 256
HEADS = 4
HEAD_DIM = 64
FF = 1024
VOCAB = 512
ACTIONS = 18
GAMES = 26
OBS = 16
FRAMES = 20
STEP_NUMBER = 5
FRAME_TOKENS = 17
LENGTH = 340
ROWS = 896
NVEC = 14

EPS_NORM = 1e-05
BETA_ONE = 0.5
BETA_TWO = 0.5
RATE_TABLE = 0.5
RATE_MATRIX = 0.05
RATE_VECTOR = 0.2
DECAY_RATE = 0.01
EPS_ADAM = 1e-08
CLIP_AT = 0.1

SEQ = 352
KEYS = 384
BLOCK, BLOCKS = 128, 3
TILE = 32
SIDE_ROWS = 32
QUERIES = HEADS * BLOCK
VALUE_ROWS = 80

COL_QKV, COL_PROJ, COL_UP, COL_DOWN, COL_LAYER = 0, 768, 1024, 2048, 3072
HALF_ATTENTION = ((0, 128, 0), (128, 128, 256), (256, 128, 512), (384, 128, COL_PROJ))
HALF_LAYER = HALF_ATTENTION + ((512, 512, COL_UP), (1024, 512, COL_DOWN))
COL_TABLE, COL_SMALL, COL_FIRST = 3072, 3968, 4096
HALF_FIRST = HALF_LAYER + ((1536, 512, COL_TABLE),)
HALF_FIRST_COLS = 2048
COL_HEAD, COL_SECOND = 3072, 3584
HALF_SECOND = HALF_LAYER + ((1536, 256, COL_HEAD),)
HALF_SECOND_COLS = 1792
GRAD_UP, GRAD_DOWN = 0, 1024
HALF_GRAD_FF = ((0, 512, GRAD_UP), (512, 512, GRAD_DOWN))
GRAD_TABLE, GRAD_SMALL = 1024, 1920
HALF_GRAD_REST = HALF_ATTENTION + ((512, 512, GRAD_TABLE),)
HALF_GRAD_COLS = 1024
SMALL_ROWS, SMALL_BIAS, SMALL_SIDE = 32, 14, 22

F32, BF16 = jnp.float32, jnp.bfloat16
MIB = 1024 * 1024


def dot_nn(a, b):
    return lax.dot_general(a, b, (((1,), (0,)), ((), ())), preferred_element_type=F32)


def dot_nt(a, b):
    return lax.dot_general(a, b, (((1,), (1,)), ((), ())), preferred_element_type=F32)


def dot_tn(a, b):
    return lax.dot_general(a, b, (((0,), (0,)), ((), ())), preferred_element_type=F32)


def places(fast):
    wide, core = lax.axis_index("wide"), lax.axis_index("narrow")
    return (wide if fast else 0), core, wide


def tiles(rows, size):
    return [slice(first, first + size) for first in range(0, rows, size)]


def normalise(x):
    centred = x - jnp.mean(x, axis=1, keepdims=True)
    scale = lax.rsqrt(jnp.mean(centred * centred, axis=1, keepdims=True) + EPS_NORM)
    return centred * scale, scale


def keep_norm(rows, xhat, scale, kept):
    kept[0][rows] = xhat.astype(BF16)
    kept[1][rows] = jnp.broadcast_to(scale, (TILE, 128))


def kept_norm(rows, kept):
    scale = kept[1][rows]
    return kept[0][rows].astype(F32), jnp.concatenate([scale, scale], axis=1)


def normalise_back(grad, xhat, scale, gain):
    inner = grad * gain
    mean_one = jnp.mean(inner, axis=1, keepdims=True)
    mean_two = jnp.mean(inner * xhat, axis=1, keepdims=True)
    return scale * (inner - mean_one - xhat * mean_two)


def column_sum(a):
    return jnp.sum(a, axis=0, keepdims=True)


def fold(a):
    return jnp.sum(a.reshape(a.shape[0] // 8, 8, a.shape[1]), axis=0)


def plus(total, a):
    return a if total is None else total + a


def block_lanes(i, h=None):
    if h is None:
        return slice(QUERIES * i, QUERIES * (i + 1))
    return slice(QUERIES * i + BLOCK * h, QUERIES * i + BLOCK * (h + 1))


def head_rows(h):
    return slice(HEAD_DIM * h, HEAD_DIM * (h + 1))


def spread_heads(source, target_ref):
    for h in range(HEADS):
        for i in range(BLOCKS):
            target_ref[head_rows(h), block_lanes(i, h)] = source[
                head_rows(h), BLOCK * i : BLOCK * (i + 1)
            ]


def causal_mask():
    key = lax.broadcasted_iota(jnp.int32, (BLOCK, QUERIES), 0)
    query = lax.broadcasted_iota(jnp.int32, (BLOCK, QUERIES), 1) & (BLOCK - 1)
    return jnp.where(key <= query, 0.0, -1e30)


def assemble(pieces_mine, pieces_other, place, w_ref, halves):
    me, core, _ = place
    is_first = core == 0
    for p in range(4):

        def block(z, _, p=p):
            row = pl.multiple_of((me ^ (4 * z + p)) * 16, 16)
            for src, width, dest in halves:
                mine = pieces_mine[p][z, :, src : src + width]
                other = pieces_other[p][z, :, src : src + width]
                if dest == COL_QKV:
                    mine, other = mine * 0.125, other * 0.125
                w_ref[pl.ds(row, 16), dest : dest + width] = jnp.where(is_first, mine, other)
                w_ref[pl.ds(row, 16), dest + width : dest + 2 * width] = jnp.where(
                    is_first, other, mine
                )
            return 0

        lax.fori_loop(0, 4, block, 0)


def disperse(g_ref, place, keep_ref, send_ref, halves, scaled=True, by_distance=True):
    me, core, _ = place
    is_first = core == 0

    def block(i, _):
        p, z = i >> 2, i & 3
        spot = 4 * z + p
        owner = me ^ spot if by_distance else spot ^ (me & ~3)
        row = pl.multiple_of(owner * 16, 16)
        for src, width, dest in halves:
            low = g_ref[pl.ds(row, 16), dest : dest + width]
            high = g_ref[pl.ds(row, 16), dest + width : dest + 2 * width]
            if scaled and dest == COL_QKV:
                low, high = low * 0.125, high * 0.125
            keep_ref[p, z, :, src : src + width] = jnp.where(is_first, low, high).astype(BF16)
            send_ref[p, z, :, src : src + width] = jnp.where(is_first, high, low).astype(BF16)
        return 0

    lax.fori_loop(0, 16, block, 0)


def make_hits(meta_ref, hits_ref):
    for rows in tiles(SEQ, TILE):
        lane = lax.broadcasted_iota(jnp.int32, (TILE, ROWS), 1)
        place = lax.broadcasted_iota(jnp.int32, (TILE, 1), 0) + (VOCAB + ACTIONS + GAMES + rows.start)
        meta = meta_ref[rows]
        hit = (lane == meta[:, 0:1]) | (lane == meta[:, 1:2]) | (lane == place)
        hits_ref[rows] = jnp.where(hit, 1.0, 0.0).astype(BF16)


def gelu_and_slope(up):
    up = up.astype(BF16)
    square = up * up
    half = jax.nn.sigmoid(up * (BF16(1.5957691216057308) + BF16(0.0713548162726) * square))
    hidden = up * half
    slope = BF16(1.5957691216057308) + BF16(0.2140644488178) * square
    return hidden, half + hidden * (BF16(1.0) - half) * slope


def layer_forward(x_ref, w_ref, vec, bias, kept, work):
    qt_ref, kv_ref, p0, p1, p2, r_ref, ot_ref, o_ref = kept[0:8]
    h_ref, gp_ref, a_ref, c_ref = kept[9:13]
    qst_ref, vt_ref, mask_ref, wqt_ref, long_ref, u_ref, y_ref, m_ref = work
    for rows in tiles(SEQ, TILE):
        xhat, scale = normalise(x_ref[rows])
        keep_norm(rows, xhat, scale, kept[14:16])
        normed16 = (xhat * vec[0:1] + vec[1:2]).astype(BF16)
        a_ref[rows], long_ref[rows] = normed16, normed16
    kv_ref[0:SEQ] = dot_nn(long_ref[0:SEQ], w_ref[:, 256:768]).astype(BF16)
    kv_ref[SEQ:KEYS] = jnp.zeros((KEYS - SEQ, 512), BF16)
    qt_ref[...] = dot_nt(wqt_ref[...], long_ref[...]).astype(BF16)
    spread_heads(qt_ref, qst_ref)
    turned = jnp.transpose(kv_ref[:, 256:512])
    for h in range(HEADS):
        vt_ref[VALUE_ROWS * h : VALUE_ROWS * h + HEAD_DIM] = turned[head_rows(h)]
    for i, pt_ref in enumerate((p0, p1, p2)):
        seen, first = BLOCK * (i + 1), BLOCK * i
        scores = dot_nn(kv_ref[0:seen, 0:256], qst_ref[:, block_lanes(i)])
        last = scores[first:] + mask_ref[...]
        peak = jnp.max(last, axis=0, keepdims=True)
        if i:
            peak = jnp.maximum(peak, jnp.max(scores[0:first], axis=0, keepdims=True))
            pt_ref[0:first] = jnp.exp(scores[0:first] - peak).astype(BF16)
        pt_ref[first:seen] = jnp.exp(last - peak).astype(BF16)
        for h in range(HEADS):
            values = vt_ref[VALUE_ROWS * h : VALUE_ROWS * (h + 1), 0:seen]
            out = dot_nn(values, pt_ref[:, BLOCK * h : BLOCK * (h + 1)])
            inverse = 1.0 / out[HEAD_DIM : HEAD_DIM + 1]
            r_ref[h : h + 1, first:seen] = inverse
            ot_ref[head_rows(h), first:seen] = (out[0:HEAD_DIM] * inverse).astype(BF16)
    o_ref[...] = jnp.transpose(ot_ref[...])[0:SEQ]
    y_ref[...] = dot_nt(o_ref[...], w_ref[:, COL_PROJ : COL_PROJ + 256])
    for rows in tiles(SEQ, TILE):
        middle = x_ref[rows] + (y_ref[rows] + vec[2:3])
        m_ref[rows] = middle
        xhat, scale = normalise(middle)
        keep_norm(rows, xhat, scale, (kept[8], kept[13]))
        c_ref[rows] = (xhat * vec[3:4] + vec[4:5]).astype(BF16)
    u_ref[...] = dot_nn(c_ref[...], w_ref[:, COL_UP : COL_UP + FF])
    for rows in tiles(SEQ, TILE):
        for first in range(0, FF, 256):
            cols = slice(first, first + 256)
            h_ref[rows, cols], gp_ref[rows, cols] = gelu_and_slope(u_ref[rows, cols] + bias[:, cols])
    y_ref[...] = dot_nt(h_ref[...], w_ref[:, COL_DOWN : COL_DOWN + FF])


def add_gradient(g_ref, column, left, right):
    g_ref[:, column : column + right.shape[1]] += dot_tn(left, right)


def ff_backward(grad_ref, grad16_ref, w_ref, w_up, w_down, vec, kept, v_ref, v_row, bias_row, work, mid_ref, mid16_refs):
    norm_kept, gp_ref = kept
    du_ref, ones_ref, u_ref, y_ref = work
    u_ref[...] = dot_nn(grad16_ref[...], w_ref[:, w_down : w_down + FF])
    for rows in tiles(SEQ, TILE):
        du_ref[rows] = u_ref[rows].astype(BF16) * gp_ref[rows]
    bias_grad = dot_nn(ones_ref[...], du_ref[...])
    for chunk in range(4):
        v_ref[bias_row + chunk, 0:1] += bias_grad[0:1, 256 * chunk : 256 * chunk + 256]
    y_ref[...] = dot_nt(du_ref[...], w_ref[:, w_up : w_up + FF])
    totals = [None] * 3
    for rows in tiles(SEQ, TILE):
        xhat, scale = kept_norm(rows, norm_kept)
        grad = y_ref[rows]
        mid = grad_ref[rows] + normalise_back(grad, xhat, scale, vec[3:4])
        mid_ref[rows] = mid
        for mid16_ref in mid16_refs:
            mid16_ref[rows] = mid.astype(BF16)
        for i, a in enumerate((mid, grad * xhat, grad)):
            totals[i] = plus(totals[i], fold(a))
    for i in range(3):
        v_ref[v_row + 2 + i] += totals[i]


def attention_backward(mid_ref, mid16_ref, w_ref, vec, kept, v_ref, v_row, work, out_ref):
    norm_kept, (qt_ref, kv_ref, p0, p1, p2, r_ref, ot_ref) = kept
    dost_ref, qst_ref, kt_ref, dst_ref, dqt_ref, dkv_ref, dqkv_ref, proj_ref, y_ref = work
    grad_o = dot_nt(proj_ref[...], mid16_ref[...]).astype(BF16).astype(F32)
    kt_ref[...] = jnp.transpose(kv_ref[:, 0:256])
    deltas = []
    for h in range(HEADS):
        scaled = grad_o[head_rows(h)] * r_ref[h : h + 1]
        deltas.append(column_sum(scaled * ot_ref[head_rows(h)].astype(F32)))
        scaled = scaled.astype(BF16)
        for i in range(BLOCKS):
            dost_ref[head_rows(h), block_lanes(i, h)] = scaled[:, BLOCK * i : BLOCK * (i + 1)]
    for i, pt_ref in enumerate((p0, p1, p2)):
        seen, first = BLOCK * (i + 1), BLOCK * i
        lanes = block_lanes(i)
        delta = jnp.concatenate([a[:, first:seen] for a in deltas], axis=1)
        grad = dot_nn(kv_ref[0:seen, 256:512], dost_ref[:, lanes])
        dst_ref[0:seen, lanes] = pt_ref[...] * (grad - delta).astype(BF16)
        for h in range(HEADS):
            out = dot_nn(kt_ref[head_rows(h), 0:seen], dst_ref[0:seen, block_lanes(i, h)])
            dqt_ref[head_rows(h), first:seen] = out.astype(BF16)
        for at, left, right in (
            (0, dst_ref[0:seen, lanes], qst_ref),
            (256, pt_ref[...], dost_ref),
        ):
            out = dot_nt(left, right[:, lanes])
            if i:
                dkv_ref[0:first, at : at + 256] += out[0:first]
            dkv_ref[first:seen, at : at + 256] = out[first:]
    dqkv_ref[:, 0:256] = jnp.transpose(dqt_ref[...])[0:SEQ]
    dqkv_ref[:, 256:768] = dkv_ref[0:SEQ].astype(BF16)
    y_ref[...] = dot_nt(dqkv_ref[...], w_ref[:, COL_QKV : COL_QKV + 768])
    totals = [None] * 2
    for rows in tiles(SEQ, TILE):
        xhat, scale = kept_norm(rows, norm_kept)
        grad = y_ref[rows]
        out = mid_ref[rows] + normalise_back(grad, xhat, scale, vec[0:1])
        out_ref[rows] = out.astype(out_ref.dtype)
        for i, a in enumerate((grad * xhat, grad)):
            totals[i] = plus(totals[i], fold(a))
    for i in range(2):
        v_ref[v_row + i] += totals[i]


def own_bias(place, mine, other):
    is_first = place[1] == 0
    return jnp.concatenate(
        [jnp.where(is_first, mine, other), jnp.where(is_first, other, mine)], axis=1
    )


def prepare_kernel(
    fast, games_ref, tokens, actions, valid, rewards, ends, out, out_side, x_ref
):
    count = out.shape[0]
    frames = tokens.shape[2]
    base = places(fast)[1] * count
    row = lax.broadcasted_iota(jnp.int32, (SEQ, frames), 0)
    start = lax.broadcasted_iota(jnp.int32, (SEQ, frames), 1) * FRAME_TOKENS
    here = jnp.where((row >= start) & (row < start + FRAME_TOKENS), 1.0, 0.0).astype(BF16)
    coming = jnp.where((row >= start - FRAME_TOKENS) & (row < start), 1.0, 0.0).astype(BF16)
    passed = jnp.sum(jnp.where(row >= start + FRAME_TOKENS, 1, 0), axis=1, keepdims=True)
    place = lax.broadcasted_iota(jnp.int32, (SEQ, 1), 0)
    spot = place - passed * FRAME_TOKENS
    lane = lax.broadcasted_iota(jnp.int32, (SEQ, 24), 1)
    wide_lane = lax.broadcasted_iota(jnp.int32, (SEQ, 128), 1)
    inside = place < LENGTH
    one_frame = (
        lax.broadcasted_iota(jnp.int32, (SIDE_ROWS, frames), 0)
        == lax.broadcasted_iota(jnp.int32, (SIDE_ROWS, frames), 1)
    )
    one_frame = jnp.where(one_frame, 1.0, 0.0).astype(BF16)
    side_lane = lax.broadcasted_iota(jnp.int32, (SIDE_ROWS, 128), 1)
    x_ref[...] = jnp.zeros(x_ref.shape, jnp.int32)
    for s in range(count):
        x_ref[0:OBS] = tokens[base + s]
        x_ref[16:17] = actions[pl.ds(base + s, 1)] + VOCAB
        x_ref[17:18] = valid[pl.ds(base + s, 1)]
        x_ref[18:19] = rewards[pl.ds(base + s, 1)]
        x_ref[19:20] = ends[pl.ds(base + s, 1)] + 3
        high = (x_ref[...] >> 4).astype(F32).astype(BF16)
        low = (x_ref[...] & 15).astype(F32).astype(BF16)
        now = dot_nt(here, high) * 16.0 + dot_nt(here, low)
        soon = dot_nt(coming, high) * 16.0 + dot_nt(coming, low)

        def pick(condition, a):
            return jnp.sum(jnp.where(condition, a, 0.0), axis=1, keepdims=True).astype(jnp.int32)

        ids = jnp.where(inside, pick(lane == spot, now), -1)
        game = jnp.where(inside, games_ref[base + s] + (VOCAB + ACTIONS), -1)
        target = pick((lane == spot + 1) & (spot < 15), now)
        target = target + pick((lane == 0) & (spot == 16), soon)
        weight = pick((lane == 17) & (spot < 15), now) + pick((lane == 17) & (spot == 16), soon)
        result = jnp.zeros((SEQ, 128), jnp.int32)
        for c, column in enumerate((ids, game, target, weight)):
            result = jnp.where(wide_lane == c, column, result)
        out[s] = result
        by_frame = dot_nt(one_frame, high) * 16.0 + dot_nt(one_frame, low)
        result = jnp.zeros((SIDE_ROWS, 128), jnp.int32)
        for c in range(3):
            column = by_frame[:, 17 + c : 18 + c].astype(jnp.int32)
            result = jnp.where(side_lane == c, column, result)
        out_side[s] = result


def start_forward(work, w_ref):
    qst_ref, vt_ref, mask_ref, wqt_ref, long_ref = work[0:5]
    long_ref[SEQ:KEYS] = jnp.zeros((KEYS - SEQ, D), BF16)
    qst_ref[...] = jnp.zeros(qst_ref.shape, BF16)
    vt_ref[...] = jnp.ones(vt_ref.shape, BF16)
    mask_ref[...] = causal_mask()
    wqt_ref[...] = jnp.transpose(w_ref[:, 0:256])


def first_forward_kernel(fast, *refs):
    refs = (places(fast),) + refs
    place, meta_ref, vec_ref, bias_ref, bias_other = refs[0:5]
    mine, other = refs[5:9], refs[9:13]
    w_attention, w_ff, side_out, next_ref, hits_ref = refs[13:18]
    kept = [ref.at[0] for ref in refs[18:34]]
    w_ref, x_ref = refs[34:36]
    work = refs[36:44]
    y_ref, m_ref = work[6:8]

    @pl.when(pl.program_id(0) == 0)
    def _():
        assemble(mine, other, place, w_ref, HALF_FIRST)
        w_attention[...] = w_ref[:, 0:COL_UP]
        w_ff[...] = w_ref[:, COL_UP:COL_TABLE]
        side_out[...] = w_ref[:, COL_SMALL:]
        start_forward(work, w_ref)

    make_hits(meta_ref.at[0], hits_ref.at[0])
    x_ref[...] = dot_nt(hits_ref[0], w_ref[:, COL_TABLE : COL_TABLE + ROWS])
    bias = own_bias(place, bias_ref[0:1], bias_other[0:1])
    vec = vec_ref[0:6]
    layer_forward(x_ref, w_ref, vec, bias, kept, work)
    for rows in tiles(SEQ, TILE):
        next_ref[0, rows] = m_ref[rows] + (y_ref[rows] + vec[5:6])


def codebook_losses(logits, meta):
    weight = meta[:, 3:4].astype(F32)
    peak = jnp.max(logits, axis=1, keepdims=True)
    expanded = jnp.exp(logits - peak)
    total = jnp.sum(expanded, axis=1, keepdims=True)
    hit = lax.broadcasted_iota(jnp.int32, logits.shape, 1) == meta[:, 2:3]
    hit = jnp.where(hit, weight, 0.0)
    return weight * (peak + jnp.log(total)), hit, expanded * (weight / total) - hit


def side_losses(side, meta):
    lane = lax.broadcasted_iota(jnp.int32, side.shape, 1)
    is_reward, is_end = lane < 3, (lane == 3) | (lane == 4)
    is_side = lane < 5
    weight = meta[:, 0:1].astype(F32)
    reward_peak = jnp.max(jnp.where(is_reward, side, -1e30), axis=1, keepdims=True)
    end_peak = jnp.max(jnp.where(is_end, side, -1e30), axis=1, keepdims=True)
    shifted = jnp.where(is_side, side - jnp.where(is_reward, reward_peak, end_peak), 0.0)
    expanded = jnp.where(is_side, jnp.exp(shifted), 0.0)
    reward_total = jnp.sum(jnp.where(is_reward, expanded, 0.0), axis=1, keepdims=True)
    end_total = jnp.sum(jnp.where(is_end, expanded, 0.0), axis=1, keepdims=True)
    hit = (lane == meta[:, 1:2]) | (lane == meta[:, 2:3])
    picked = jnp.sum(jnp.where(hit, side, 0.0), axis=1, keepdims=True)
    terms = reward_peak + jnp.log(reward_total) + end_peak + jnp.log(end_total) - picked
    grad = expanded * jnp.where(is_reward, weight / reward_total, weight / end_total)
    return weight * terms, grad - jnp.where(hit, weight, 0.0), weight


def frame_ends(shape, frame_axis):
    frame = lax.broadcasted_iota(jnp.int32, shape, frame_axis)
    row = lax.broadcasted_iota(jnp.int32, shape, 1 - frame_axis)
    hit = (row == frame * FRAME_TOKENS + OBS) & (frame < FRAMES)
    return jnp.where(hit, 1.0, 0.0).astype(BF16)


def middle_kernel(fast, *refs):
    refs = (places(fast),) + refs
    place, meta_ref, frame_ref, vec_ref, bias_ref, bias_other, side_ref, in_ref = refs[0:8]
    mine, other = refs[8:12], refs[12:16]
    grad_ref, keep_ref, send_ref, v_out, scalar_ref = refs[16:21]
    refs = refs[1:]
    w_ref, g_ref, v_ref = refs[20:23]
    kept = list(refs[23:39])
    forward_work = refs[39:47]
    u_ref, y_ref, m_ref = forward_work[5:8]
    backward_work = list(refs[47:53])
    proj_ref = refs[53]
    du_all, ones_ref, up_ref, up16_all, mid_ref, mid16_ref = refs[54:60]
    last_kept = refs[60:62]
    final_all, logit_ref, dlogit_all, pick_ref, put_ref, mid16_all = refs[62:68]
    o_all, h_all, a_all, c_all, dqkv_all = kept[7], kept[9], kept[11], kept[12], backward_work[5]
    dost_ref = backward_work[0]
    step = pl.program_id(0)

    @pl.when(step == 0)
    def _():
        assemble(mine, other, place, w_ref, HALF_SECOND)
        w_ref[:, COL_SECOND:] = side_ref[...]
        g_ref[...] = jnp.zeros(g_ref.shape, F32)
        v_ref[...] = jnp.zeros(v_ref.shape, F32)
        scalar_ref[...] = jnp.zeros(scalar_ref.shape, F32)
        start_forward(forward_work, w_ref)
        dost_ref[...] = jnp.zeros(dost_ref.shape, BF16)
        proj_ref[...] = jnp.transpose(w_ref[:, COL_PROJ : COL_PROJ + 256])
        ones_ref[...] = jnp.ones(ones_ref.shape, BF16)
        mid16_ref[SEQ:KEYS] = jnp.zeros((KEYS - SEQ, D), BF16)
        pick_ref[...] = frame_ends((SIDE_ROWS, SEQ), 0)
        put_ref[...] = frame_ends((SEQ, SIDE_ROWS), 1)

    here = pl.ds(pl.multiple_of((step & 1) * SEQ, 32), SEQ)
    for i in (7, 9, 11, 12):
        kept[i] = kept[i].at[here]
    gp_ref = kept[10]
    backward_work[5] = dqkv_all.at[here]
    du_ref, up16_ref, pair16_ref = du_all.at[here], up16_all.at[here], mid16_all.at[here]
    final_ref, dlogit_ref = final_all.at[here], dlogit_all.at[here]
    x_ref = in_ref.at[0]
    vec = vec_ref[6:12]
    bias = own_bias(place, bias_ref[1:2], bias_other[1:2])
    layer_forward(x_ref, w_ref, vec, bias, kept, forward_work)

    gain, offset = vec_ref[12:13], vec_ref[13:14]
    for rows in tiles(SEQ, TILE):
        last = m_ref[rows] + (y_ref[rows] + vec[5:6])
        xhat, scale = normalise(last)
        keep_norm(rows, xhat, scale, last_kept)
        final_ref[rows] = (xhat * gain + offset).astype(BF16)
    cols_head = slice(COL_HEAD, COL_HEAD + VOCAB + 128)
    logit_ref[...] = dot_nn(final_ref[...], w_ref[:, COL_HEAD : COL_HEAD + VOCAB])
    logs, picked = None, None
    for rows in tiles(SEQ, TILE):
        logits = logit_ref[rows]
        log, hit, grad = codebook_losses(logits, meta_ref[0, rows])
        dlogit_ref[rows, :VOCAB] = grad.astype(BF16)
        logs, picked = plus(logs, log), plus(picked, fold(hit * logits))
    acting = dot_nn(pick_ref[...], final_ref[...]).astype(BF16)
    side = dot_nn(acting, w_ref[:, COL_HEAD + VOCAB : COL_HEAD + VOCAB + 128])
    side_loss, grad, weight = side_losses(side, frame_ref[0])
    dlogit_ref[:, VOCAB:] = dot_nn(put_ref[...], grad.astype(BF16)).astype(BF16)
    loss = column_sum(logs) + column_sum(side_loss)
    loss = loss - jnp.sum(column_sum(picked), axis=1, keepdims=True)
    valid = column_sum(weight)
    scalar_lane = lax.broadcasted_iota(jnp.int32, (8, 128), 1)
    scalar_row = lax.broadcasted_iota(jnp.int32, (8, 128), 0) == 0
    scalar_ref[...] += jnp.where(
        scalar_row,
        jnp.where(scalar_lane == 0, loss, jnp.where(scalar_lane == 1, valid, 0.0)),
        0.0,
    )
    y_ref[...] = dot_nt(dlogit_ref[...], w_ref[:, cols_head])
    totals = [None] * 3
    for rows in tiles(SEQ, TILE):
        xhat, scale = kept_norm(rows, last_kept)
        grad = y_ref[rows]
        up = normalise_back(grad, xhat, scale, gain)
        up_ref[rows] = up
        up16_ref[rows] = up.astype(BF16)
        for i, a in enumerate((up, grad * xhat, grad)):
            totals[i] = plus(totals[i], fold(a))
    for i in range(3):
        v_ref[11 + i] += totals[i]
    ff_backward(
        up_ref,
        up16_ref,
        w_ref,
        COL_UP,
        COL_DOWN,
        vec,
        ((kept[8], kept[13]), gp_ref),
        v_ref,
        6,
        SMALL_BIAS + 4,
        (du_ref, ones_ref, u_ref, y_ref),
        mid_ref,
        (mid16_ref, pair16_ref),
    )
    attention_backward(
        mid_ref,
        mid16_ref,
        w_ref,
        vec,
        (kept[14:16], kept[0:7]),
        v_ref,
        6,
        (dost_ref, forward_work[0]) + tuple(backward_work[1:]) + (proj_ref, y_ref),
        grad_ref.at[0],
    )

    @pl.when(step & 1 == 1)
    def _():
        add_gradient(g_ref, COL_QKV, a_all[...], dqkv_all[...])
        add_gradient(g_ref, COL_PROJ, mid16_all[...], o_all[...])
        add_gradient(g_ref, COL_UP, c_all[...], du_all[...])
        add_gradient(g_ref, COL_DOWN, up16_all[...], h_all[...])
        add_gradient(g_ref, COL_HEAD, final_all[...], dlogit_all[...])

    @pl.when(step == pl.num_programs(0) - 1)
    def _():
        disperse(g_ref, place, keep_ref, send_ref, HALF_SECOND, True, False)
        side = jnp.transpose(g_ref[:, COL_SECOND:])
        for i in range(5):
            v_ref[SMALL_SIDE + i, 0:1] = side[i : i + 1]
        v_out[...] = v_ref[...]


def ff_backward_kernel(fast, *refs):
    vec_ref, w_ref, grad_ref, v_in = refs[0:4]
    xhat_ref, scale_ref, h_ref, gp_ref, c_ref = [ref.at[0] for ref in refs[4:9]]
    mid_ref, keep_ref, send_ref, v_out = refs[9:13]
    g_ref, v_ref, grad16_ref, du_ref, ones_ref, u_ref, y_ref = refs[13:20]
    step = pl.program_id(0)

    @pl.when(step == 0)
    def _():
        g_ref[...] = jnp.zeros(g_ref.shape, F32)
        v_ref[...] = v_in[...]
        ones_ref[...] = jnp.ones(ones_ref.shape, BF16)

    total = None
    for rows in tiles(SEQ, TILE):
        grad = grad_ref[0, rows]
        grad16_ref[rows] = grad.astype(BF16)
        total = plus(total, fold(grad))
    v_ref[5] += total
    ff_backward(
        grad_ref.at[0],
        grad16_ref,
        w_ref,
        GRAD_UP,
        GRAD_DOWN,
        vec_ref[0:6],
        ((xhat_ref, scale_ref), gp_ref),
        v_ref,
        0,
        SMALL_BIAS,
        (du_ref, ones_ref, u_ref, y_ref),
        mid_ref.at[0],
        (),
    )
    add_gradient(g_ref, GRAD_DOWN, grad16_ref[...], h_ref[...])
    add_gradient(g_ref, GRAD_UP, c_ref[...], du_ref[...])

    @pl.when(step == pl.num_programs(0) - 1)
    def _():
        disperse(g_ref, places(fast), keep_ref, send_ref, HALF_GRAD_FF, False, False)
        v_out[...] = v_ref[...]


def attention_backward_kernel(fast, *refs):
    vec_ref, w_ref, mid_ref, v_in, scalar_in = refs[0:5]
    kept = [ref.at[0] for ref in refs[5:14]]
    o_all, a_all, hits_all = refs[14:17]
    keep_ref, send_ref, v_out, scalar_out = refs[18:22]
    g_ref, v_ref, mid16_ref, mid16_all, out16_all, dqkv_all = refs[22:28]
    work = list(refs[28:36])
    dost_ref, qst_ref, proj_ref = work[0], work[1], work[6]
    step = pl.program_id(0)

    @pl.when(step == 0)
    def _():
        v_ref[...] = v_in[...]
        scalar_out[...] = scalar_in[...]
        dost_ref[...] = jnp.zeros(dost_ref.shape, BF16)
        qst_ref[...] = jnp.zeros(qst_ref.shape, BF16)
        proj_ref[...] = jnp.transpose(w_ref[:, COL_PROJ : COL_PROJ + 256])
        mid16_ref[SEQ:KEYS] = jnp.zeros((KEYS - SEQ, D), BF16)

    here = pl.ds(pl.multiple_of(step * SEQ, 32), SEQ)
    all16_ref = mid16_all.at[here]
    spread_heads(kept[2], qst_ref)
    for rows in tiles(SEQ, TILE):
        mid16 = mid_ref[0, rows].astype(BF16)
        mid16_ref[rows], all16_ref[rows] = mid16, mid16
    work.insert(6, dqkv_all.at[here])
    attention_backward(
        mid_ref.at[0],
        mid16_ref,
        w_ref,
        vec_ref[0:6],
        (kept[0:2], kept[2:9]),
        v_ref,
        0,
        work,
        out16_all.at[here],
    )

    @pl.when(step == pl.num_programs(0) - 1)
    def _():
        g_ref[:, COL_QKV : COL_QKV + 768] = dot_tn(a_all[...], dqkv_all[...])
        g_ref[:, COL_PROJ : COL_PROJ + 256] = dot_tn(mid16_all[...], o_all[...])
        g_ref[:, GRAD_TABLE : GRAD_TABLE + ROWS] = dot_tn(out16_all[...], hits_all[...])
        small = jnp.sum(v_ref[...], axis=1)
        v_out[...] = small
        for block in range(16):
            quarter = small[8 * (block // 4) : 8 * (block // 4) + 8]
            g_ref[16 * block : 16 * block + 8, GRAD_SMALL:] = quarter[:, 0:128]
            g_ref[16 * block + 8 : 16 * block + 16, GRAD_SMALL:] = quarter[:, 128:256]
        disperse(g_ref, places(fast), keep_ref, send_ref, HALF_GRAD_REST)


def pack_layer(attn, proj, up, down, layer, out):
    for j in range(3):
        out[:, 128 * j : 128 * j + 128] = attn[layer, j].astype(BF16)
    out[:, 384:512] = proj[layer].astype(BF16)
    out[:, 512:1024] = up[layer].astype(BF16)
    out[:, 1024:1536] = down[layer].astype(BF16)


def pack_kernel(fast, table, attn, proj, up, down, head, side, first, second, pad_ref):
    pack_layer(attn, proj, up, down, 0, first)
    pack_layer(attn, proj, up, down, 1, second)
    second[:, 1536:1792] = head[...].astype(BF16)
    rows = side.shape[1]
    eye = (
        lax.broadcasted_iota(jnp.int32, (rows, rows), 0)
        == lax.broadcasted_iota(jnp.int32, (rows, rows), 1)
    )
    eye = jnp.where(eye, 1.0, 0.0).astype(BF16)
    pad_ref[...] = jnp.zeros(pad_ref.shape, F32)
    pad_ref[:, 0:5] = dot_nt(eye, side[...].astype(BF16))
    high = jnp.concatenate([table[:, 512:896], pad_ref[...]], axis=1)
    first[:, 1536:2048] = jnp.where(places(fast)[1] == 0, table[:, 0:512], high).astype(BF16)


def finish_kernel(fast, *refs):
    count = (len(refs) - 5) // 2
    scalar_ref = refs[2 * count]
    out_rest, out_other, out_table, out_small = refs[2 * count + 1 :]
    square = jnp.zeros((1, 1), F32)
    for pieces, out in ((refs[0:count], out_rest), (refs[count : 2 * count], out_other)):
        total = pieces[0][...]
        for piece in pieces[1:]:
            total = total + piece[...].astype(F32)
        out[...] = total
        square = square + column_sum(jnp.sum(total * total, axis=1, keepdims=True))
    small = out_rest[:, 896:1024]
    extra = column_sum(jnp.sum(small * small, axis=1, keepdims=True))
    square = square - jnp.where(places(fast)[1] == 0, 0.0, extra)
    out_table[...] = out_rest[:, 512:1024]
    rows = small.shape[0]
    lane = lax.broadcasted_iota(jnp.int32, (8, 128), 1)
    top = lax.broadcasted_iota(jnp.int32, (8, 128), 0) == 0
    scalars = scalar_ref[...] + jnp.where(top & (lane == 2), square, 0.0)
    for i in range(out_small.shape[0]):
        out_small[i, 0:rows] = small
        out_small[i, rows : rows + 8] = scalars


def adam_rule(weight, moment, second, gradient, step_rate, decay_rate):
    moment_new = BETA_ONE * moment + (1.0 - BETA_ONE) * gradient
    second_new = BETA_TWO * second + (1.0 - BETA_TWO) * gradient * gradient
    moment_hat = moment_new / (1.0 - BETA_ONE**STEP_NUMBER)
    second_hat = second_new / (1.0 - BETA_TWO**STEP_NUMBER)
    weight_new = weight - step_rate * (
        moment_hat / (jnp.sqrt(second_hat) + EPS_ADAM) + decay_rate * weight
    )
    return (weight_new, moment_new, second_new)


def adam_kernel(fast, rest, others, swapped, gathered, beside, *refs):
    rows = rest.shape[0]
    _, core, wide = places(fast)
    is_first = core == 0
    if fast:
        quarters = [jnp.where(is_first, beside[4 * z], gathered[4 * z]) for z in range(4)]
    else:
        quarters = [refs[0][z] for z in range(4)]
        refs = refs[1:]
    params = [refs[3 * i : 3 * i + 3] for i in range(9)]
    loss_ref, valid_ref, norm_ref = refs[27:30]
    outs = [refs[30 + 3 * i : 33 + 3 * i] for i in range(9)]
    small_ref = refs[57]
    for z in range(4):
        small_ref[8 * z : 8 * z + 8, 0:128] = quarters[z][0:8]
        small_ref[8 * z : 8 * z + 8, 128:256] = quarters[z][8:16]
    sums = []
    for source in (gathered, beside):
        total = source[0, rows : rows + 1]
        for i in range(1, source.shape[0]):
            total = total + source[i, rows : rows + 1]
        sums.append(total)
    scalars = sums[0] + sums[1]
    small = small_ref[...]
    loss, valid, square = scalars[:, 0:1], scalars[:, 1:2], scalars[:, 2:3]
    square = square + column_sum(jnp.sum(small * small, axis=1, keepdims=True))
    inverse = 1.0 / valid
    norm = jnp.sqrt(square) * inverse
    loss_ref[...], valid_ref[...], norm_ref[...] = loss, valid, norm
    factor = jnp.minimum(1.0, CLIP_AT / (norm + 1e-06)) * inverse
    table, attn, proj, up, bias, down, vectors, head, side = range(9)

    def update(which, index, gradient, step_rate, decay_rate):
        news = adam_rule(
            *(ref[index] for ref in params[which]), factor * gradient, step_rate, decay_rate
        )
        for ref, new in zip(outs[which], news):
            ref[index] = new

    layers = ((rest, others, 1792), (others, others, 512))
    for layer, (attention, feed, at) in enumerate(layers):
        for j in range(3):
            update(attn, (layer, j), attention[:, 128 * j : 128 * j + 128], RATE_MATRIX, DECAY_RATE)
        update(proj, (layer,), attention[:, 384:512], RATE_MATRIX, DECAY_RATE)
        update(up, (layer,), feed[:, at : at + 512], RATE_MATRIX, DECAY_RATE)
        update(down, (layer,), feed[:, at + 512 : at + 1024], RATE_MATRIX, DECAY_RATE)
        for i in range(2):
            low = SMALL_BIAS + 4 * layer + i
            row = jnp.where(is_first, small[low : low + 1], small[low + 2 : low + 3])
            index = (slice(layer, layer + 1), slice(256 * i, 256 * i + 256))
            update(bias, index, row, RATE_VECTOR, 0.0)
    whole = (slice(None), slice(None))
    update(head, whole, others[:, 1536:1792], RATE_MATRIX, DECAY_RATE)
    mine, theirs = rest[:, 512:1024], swapped[:, 0:512]
    low, high = jnp.where(is_first, mine, theirs), jnp.where(is_first, theirs, mine)
    update(table, (slice(None), slice(0, 512)), low, RATE_TABLE, DECAY_RATE)
    update(table, (slice(None), slice(512, 896)), high[:, 0:384], RATE_TABLE, DECAY_RATE)
    update(vectors, whole, small[0:NVEC], RATE_VECTOR, 0.0)
    turned = pltpu.roll(small[SMALL_SIDE : SMALL_SIDE + 8], lax.rem(D - wide * rows, D), 1)
    update(side, whole, turned[0:5, 0:rows], RATE_MATRIX, DECAY_RATE)


def swap(a, axis, distance):
    size = lax.axis_size(axis)
    return lax.ppermute(a, axis, [(i, i ^ distance) for i in range(size)])


def swap_column(piece, n_high):
    return [piece] + [swap(piece, "wide", 4 * k) for k in range(1, n_high)]


def gather_plane(column):
    return [column] + [swap(column, "wide", p) for p in range(1, 4)]


def gather_cores(mine):
    return [swap(a, "narrow", 1) for a in mine]


def in_blocks(parts, wide):
    n_high, rows, cols = parts[0].shape
    if rows == 16:
        return parts
    whole = jnp.stack(parts, axis=1).reshape(4 * n_high, rows, cols)
    whole = whole[wide ^ jnp.arange(4 * n_high)].reshape(4, 4, 16, cols)
    return [whole[:, p] for p in range(4)]


def in_pieces(blocks, wide, n_high, by_distance):
    cols = blocks.shape[-1]
    if n_high == 4:
        return blocks
    rows = 64 // n_high
    whole = blocks.transpose(1, 0, 2, 3).reshape(4 * n_high, rows, cols)
    order = jnp.arange(4 * n_high)
    whole = whole[wide ^ order if by_distance else order ^ (wide & ~3)]
    return whole.reshape(n_high, 4, rows, cols).transpose(1, 0, 2, 3)


def add_cores(keep, send, wide, n_high, by_distance):
    keep = in_pieces(keep, wide, n_high, by_distance)
    send = in_pieces(send, wide, n_high, by_distance)
    received = swap(send, "narrow", 1)
    return [keep[p].astype(F32) + received[p].astype(F32) for p in range(4)]


def swap_plane(sums):
    return [swap(sums[p].astype(BF16), "wide", p) for p in range(1, 4)]


def add_plane(own, received):
    for a in received:
        own = own + a.astype(F32)
    return own


def column_pieces(own):
    return [own[0]] + [swap(own[k].astype(BF16), "wide", 4 * k) for k in range(1, own.shape[0])]


def resident(arrays):
    return [pltpu.with_memory_space_constraint(a, pltpu.VMEM) for a in arrays]


def in_hbm(arrays):
    return [pltpu.with_memory_space_constraint(a, pltpu.HBM) for a in arrays]


def full_spec(a):
    return pl.BlockSpec(a.shape, lambda *_: (0,) * len(a.shape))


def row_spec(shape):
    return pl.BlockSpec((1,) + shape, lambda i: (i,) + (0,) * len(shape))


def shaped(shape, dtype):
    return jax.ShapeDtypeStruct(shape, dtype)


VMEM_SPEC = pl.BlockSpec(memory_space=pltpu.VMEM)
ANY_SPEC = pl.BlockSpec(memory_space=pl.ANY)
SMEM_SPEC = pl.BlockSpec(memory_space=pltpu.SMEM)


VMEM_MIB = {
    "pack": 58,
    "prepare": 58,
    "first_forward": 26,
    "middle": 32,
    "ff_backward": 20,
    "attention_backward": 26,
    "finish": 58,
    "adam": 58,
}


def call(kernel, grid, in_specs, out_specs, out_shape, scratch, flops, bytes_accessed, name):
    extra = {"grid": grid} if grid else {}
    return pl.pallas_call(
        kernel,
        in_specs=in_specs,
        out_specs=out_specs,
        out_shape=out_shape,
        scratch_shapes=scratch,
        compiler_params=pltpu.CompilerParams(vmem_limit_bytes=VMEM_MIB[name] * MIB),
        cost_estimate=pl.CostEstimate(
            flops=flops, bytes_accessed=bytes_accessed, transcendentals=0
        ),
        name=name,
        **extra,
    )


KEPT = (
    ((D, KEYS), BF16),
    ((KEYS, 512), BF16),
    ((BLOCK, QUERIES), BF16),
    ((2 * BLOCK, QUERIES), BF16),
    ((3 * BLOCK, QUERIES), BF16),
    ((8, KEYS), F32),
    ((D, KEYS), BF16),
    ((SEQ, D), BF16),
    ((SEQ, D), BF16),
    ((SEQ, FF), BF16),
    ((SEQ, FF), BF16),
    ((SEQ, D), BF16),
    ((SEQ, D), BF16),
    ((SEQ, 128), F32),
    ((SEQ, D), BF16),
    ((SEQ, 128), F32),
)
FORWARD_WORK = [
    pltpu.VMEM((D, BLOCKS * QUERIES), BF16),
    pltpu.VMEM((HEADS * VALUE_ROWS, KEYS), BF16),
    pltpu.VMEM((BLOCK, QUERIES), F32),
    pltpu.VMEM((D, D), BF16),
    pltpu.VMEM((KEYS, D), BF16),
    pltpu.VMEM((SEQ, FF), F32),
    pltpu.VMEM((SEQ, D), F32),
    pltpu.VMEM((SEQ, D), F32),
]
BACKWARD_WORK = [
    pltpu.VMEM((D, BLOCKS * QUERIES), BF16),
    pltpu.VMEM((D, BLOCKS * QUERIES), BF16),
    pltpu.VMEM((D, KEYS), BF16),
    pltpu.VMEM((KEYS, BLOCKS * QUERIES), BF16),
    pltpu.VMEM((D, KEYS), BF16),
    pltpu.VMEM((KEYS, 512), F32),
    pltpu.VMEM((SEQ, 768), BF16),
]
PROJ_WORK = pltpu.VMEM((D, D), BF16)
ONES_WORK = pltpu.VMEM((16, SEQ), BF16)


def per_device(
    tokens,
    actions,
    game_ids,
    valid_steps,
    rewards,
    end_flags,
    embed_table,
    table_first,
    table_second,
    attn_weight,
    attn_first,
    attn_second,
    proj_weight,
    proj_first,
    proj_second,
    up_weight,
    up_first,
    up_second,
    up_bias,
    bias_first,
    bias_second,
    down_weight,
    down_first,
    down_second,
    vectors,
    vectors_first,
    vectors_second,
    head_weight,
    head_first,
    head_second,
    side_weight,
    side_first,
    side_second,
):
    n_high = lax.axis_size("wide") // 4
    wide = lax.axis_index("wide")
    rows = side_weight.shape[0]
    fast = rows == 16

    def flat(a):
        return jnp.swapaxes(a, -1, -2)

    params = (
        (flat(embed_table), flat(table_first), flat(table_second)),
        (attn_weight, attn_first, attn_second),
        (flat(proj_weight), flat(proj_first), flat(proj_second)),
        (up_weight, up_first, up_second),
        (up_bias, bias_first, bias_second),
        (flat(down_weight), flat(down_first), flat(down_second)),
        (vectors, vectors_first, vectors_second),
        (head_weight, head_first, head_second),
        (flat(side_weight), flat(side_first), flat(side_second)),
    )
    table, attn, proj, up, _, down, _, head, side = (group[0] for group in params)

    piece_first, piece_second = call(
        functools.partial(pack_kernel, fast),
        None,
        [VMEM_SPEC] * 7,
        [VMEM_SPEC] * 2,
        [shaped((rows, HALF_FIRST_COLS), BF16), shaped((rows, HALF_SECOND_COLS), BF16)],
        [pltpu.VMEM((rows, 128), F32)],
        10**6,
        10**6,
        "pack",
    )(table, attn, proj, up, down, head, side)
    other_bias = swap(up_bias, "narrow", 1)
    column = swap_column(piece_first, n_high)

    count = tokens.shape[0] // lax.axis_size("narrow")
    meta, frame_meta = call(
        functools.partial(prepare_kernel, fast),
        None,
        [SMEM_SPEC] + [VMEM_SPEC] * 5,
        [VMEM_SPEC] * 2,
        [shaped((count, SEQ, 128), jnp.int32), shaped((count, SIDE_ROWS, 128), jnp.int32)],
        [pltpu.VMEM((24, FRAMES), jnp.int32)],
        10**6,
        10**6,
        "prepare",
    )(game_ids, flat(tokens), actions, valid_steps, rewards, end_flags)
    column, other_bias, meta = lax.optimization_barrier((column, other_bias, meta))
    first_column = jnp.stack(column)
    first_mine = gather_plane(first_column)
    own, piece_second = lax.optimization_barrier((swap(first_column, "narrow", 1), piece_second))
    second_column = jnp.stack(swap_column(piece_second, n_high))
    second_column, across = lax.optimization_barrier((second_column, first_mine[3]))
    first_mine = first_mine[0:3] + [across]
    first_other = [own] + gather_cores(first_mine[1:])
    second_mine = gather_plane(second_column)
    first_parts = in_blocks(first_mine, wide) + in_blocks(first_other, wide)

    kept_specs = [row_spec(shape) for shape, _ in KEPT]
    kept_shapes = [shaped((count,) + shape, dtype) for shape, dtype in KEPT]
    row_f32 = shaped((count, SEQ, D), F32)
    meta_spec = row_spec((SEQ, 128))
    vec_specs = [full_spec(vectors), full_spec(up_bias), full_spec(up_bias)]
    w_attention_spec = pl.BlockSpec((D, 1024), lambda i: (0, 0))
    w_ff_spec = pl.BlockSpec((D, 2048), lambda i: (0, 0))
    side_spec = pl.BlockSpec((D, 128), lambda i: (0, 0))
    hits_spec = row_spec((SEQ, ROWS))
    results = call(
        functools.partial(first_forward_kernel, fast),
        (count,),
        [meta_spec] + vec_specs + [VMEM_SPEC] * 8,
        [w_attention_spec, w_ff_spec, side_spec, row_spec((SEQ, D)), hits_spec] + kept_specs,
        [shaped((D, 1024), BF16), shaped((D, 2048), BF16), shaped((D, 128), BF16), row_f32]
        + [shaped((count, SEQ, ROWS), BF16)]
        + kept_shapes,
        [pltpu.VMEM((D, COL_FIRST), BF16), pltpu.VMEM((SEQ, D), F32)] + FORWARD_WORK,
        4 * 10**9,
        20 * 10**6,
        "first_forward",
    )(*in_hbm([meta, vectors, up_bias, other_bias]), *resident(first_parts))
    w_attention, w_ff, side_copy, stream, hits = results[0:5]
    kept = results[5:]
    received, side_copy = lax.optimization_barrier((second_mine[1:], side_copy))
    second_mine = second_mine[0:1] + received
    second_other = gather_cores(second_mine)
    second_parts = in_blocks(second_mine, wide) + in_blocks(second_other, wide)

    def blocks(cols):
        return pl.BlockSpec((4, 4, 16, cols), lambda i: (0, 0, 0, 0))

    def block_shapes(cols):
        return [shaped((4, 4, 16, cols), BF16)] * 2

    small_spec = pl.BlockSpec((SMALL_ROWS, 8, D), lambda i: (0, 0, 0))
    small_shape = shaped((SMALL_ROWS, 8, D), F32)
    small_scratch = pltpu.VMEM((SMALL_ROWS, 8, D), F32)
    scalar_spec = pl.BlockSpec((8, 128), lambda i: (0, 0))
    grad_stream, keep_second, send_second, small_grads, scalars = call(
        functools.partial(middle_kernel, fast),
        (count,),
        [meta_spec, row_spec((SIDE_ROWS, 128))]
        + vec_specs
        + [side_spec, row_spec((SEQ, D))]
        + [VMEM_SPEC] * 8,
        [row_spec((SEQ, D))] + [blocks(HALF_SECOND_COLS)] * 2 + [small_spec, scalar_spec],
        [row_f32] + block_shapes(HALF_SECOND_COLS) + [small_shape, shaped((8, 128), F32)],
        [
            pltpu.VMEM((D, COL_SECOND + 128), BF16),
            pltpu.VMEM((D, COL_SECOND + 128), F32),
            small_scratch,
        ]
        + [pltpu.VMEM(shape, dtype) for shape, dtype in KEPT[0:7]]
        + [pltpu.VMEM((2 * SEQ, D), BF16), pltpu.VMEM(*KEPT[8])]
        + [pltpu.VMEM((2 * SEQ, FF), BF16), pltpu.VMEM(*KEPT[10])]
        + [pltpu.VMEM((2 * SEQ, D), BF16)] * 2
        + [pltpu.VMEM(*a) for a in KEPT[13:16]]
        + FORWARD_WORK
        + BACKWARD_WORK[0:1]
        + BACKWARD_WORK[2:6]
        + [pltpu.VMEM((2 * SEQ, 768), BF16)]
        + [
            PROJ_WORK,
            pltpu.VMEM((2 * SEQ, FF), BF16),
            ONES_WORK,
            pltpu.VMEM((SEQ, D), F32),
            pltpu.VMEM((2 * SEQ, D), BF16),
            pltpu.VMEM((SEQ, D), F32),
            pltpu.VMEM((KEYS, D), BF16),
            pltpu.VMEM((SEQ, D), BF16),
            pltpu.VMEM((SEQ, 128), F32),
            pltpu.VMEM((2 * SEQ, D), BF16),
            pltpu.VMEM((SEQ, VOCAB), F32),
            pltpu.VMEM((2 * SEQ, VOCAB + 128), BF16),
            pltpu.VMEM((SIDE_ROWS, SEQ), BF16),
            pltpu.VMEM((SEQ, SIDE_ROWS), BF16),
            pltpu.VMEM((2 * SEQ, D), BF16),
        ],
        15 * 10**9,
        20 * 10**6,
        "middle",
    )(
        *in_hbm([meta, frame_meta, vectors, up_bias, other_bias]),
        side_copy,
        stream,
        *resident(second_parts),
    )
    second_sums = add_cores(keep_second, send_second, wide, n_high, False)

    def joined(a):
        return a.reshape((count * a.shape[1],) + a.shape[2:])

    kept_ff = (kept[8], kept[13], kept[9], kept[10], kept[12])
    grad_mid, keep_ff, send_ff, small_grads = call(
        functools.partial(ff_backward_kernel, fast),
        (count,),
        [full_spec(vectors), w_ff_spec, row_spec((SEQ, D)), small_spec]
        + [row_spec(a.shape[1:]) for a in kept_ff],
        [row_spec((SEQ, D))] + [blocks(HALF_GRAD_COLS)] * 2 + [small_spec],
        [row_f32] + block_shapes(HALF_GRAD_COLS) + [small_shape],
        [
            pltpu.VMEM((D, 2048), F32),
            small_scratch,
            pltpu.VMEM((SEQ, D), BF16),
            pltpu.VMEM((SEQ, FF), BF16),
            ONES_WORK,
            pltpu.VMEM((SEQ, FF), F32),
            pltpu.VMEM((SEQ, D), F32),
        ],
        4 * 10**9,
        10 * 10**6,
        "ff_backward",
    )(*in_hbm([vectors]), w_ff, grad_stream, small_grads, *kept_ff)
    ff_sums = add_cores(keep_ff, send_ff, wide, n_high, False)
    other_sums = jnp.concatenate(
        [
            jnp.stack([a.astype(BF16) for a in second_sums]),
            jnp.stack([a.astype(BF16) for a in ff_sums]),
        ],
        axis=-1,
    )
    plane = [[4 * h + p for p in range(4)] for h in range(n_high)]
    others = lax.all_to_all(other_sums, "wide", 0, 0, axis_index_groups=plane)

    kept_attention = (kept[14], kept[15]) + tuple(kept[0:7])
    joined_attention = [joined(kept[7]), joined(kept[11]), joined(hits)]
    keep_rest, send_rest, small_grads, scalars = call(
        functools.partial(attention_backward_kernel, fast),
        (count,),
        [full_spec(vectors), w_attention_spec, row_spec((SEQ, D)), small_spec, scalar_spec]
        + [row_spec(a.shape[1:]) for a in kept_attention]
        + [VMEM_SPEC] * 3
        + [ANY_SPEC],
        [blocks(HALF_GRAD_COLS)] * 2
        + [pl.BlockSpec((SMALL_ROWS, D), lambda i: (0, 0)), scalar_spec],
        block_shapes(HALF_GRAD_COLS) + [shaped((SMALL_ROWS, D), F32), shaped((8, 128), F32)],
        [pltpu.VMEM((D, 2048), F32), small_scratch, pltpu.VMEM((KEYS, D), BF16)]
        + [pltpu.VMEM((count * SEQ, D), BF16)] * 2
        + [pltpu.VMEM((count * SEQ, 768), BF16)]
        + BACKWARD_WORK[0:6]
        + [PROJ_WORK, pltpu.VMEM((SEQ, D), F32)],
        6 * 10**9,
        20 * 10**6,
        "attention_backward",
    )(
        *in_hbm([vectors]),
        w_attention,
        grad_mid,
        small_grads,
        scalars,
        *kept_attention,
        *joined_attention,
        other_sums,
    )
    others, scalars = lax.optimization_barrier((others, scalars))
    rest_sums = add_cores(keep_rest, send_rest, wide, n_high, True)
    rest_received = swap_plane(rest_sums)
    others, rest_sums[0] = lax.optimization_barrier((others, rest_sums[0]))
    others = [others[p].astype(F32) for p in range(4)]
    other_pieces = column_pieces((others[0] + others[1]) + (others[2] + others[3]))
    rest_pieces = column_pieces(add_plane(rest_sums[0], rest_received))

    grad_rest, grad_others, table_part, small = call(
        functools.partial(finish_kernel, fast),
        None,
        [VMEM_SPEC] * (2 * n_high + 1),
        [VMEM_SPEC] * 4,
        [
            shaped((rows, HALF_GRAD_COLS), F32),
            shaped((rows, HALF_GRAD_COLS + HALF_SECOND_COLS), F32),
            shaped((rows, 512), F32),
            shaped((4 * n_high, rows + 8, 128), F32),
        ],
        [],
        10**6,
        10**6,
        "finish",
    )(*resident(rest_pieces + other_pieces), scalars)

    gathered = lax.all_to_all(small, "wide", 0, 0)
    beside = swap(gathered, "narrow", 1)
    quarters = []
    if not fast:
        total = lax.psum(small_grads, ("wide", "narrow"))
        quarters = [total.reshape(4, 8, 2, 128).transpose(0, 2, 1, 3).reshape(4, 16, 128)]
    swapped = swap(table_part, "narrow", 1)

    flat_params = [a for group in params for a in group]
    results = call(
        functools.partial(adam_kernel, fast),
        None,
        [VMEM_SPEC] * (32 + len(quarters)),
        [VMEM_SPEC] * 30,
        [shaped((1, 1), F32)] * 3 + [shaped(a.shape, F32) for a in flat_params],
        [pltpu.VMEM((SMALL_ROWS, D), F32)],
        10**6,
        10**6,
        "adam",
    )(grad_rest, grad_others, *resident([swapped, gathered, beside]), *quarters, *flat_params)
    news = list(results[3:])
    for group in (0, 2, 5, 8):
        for member in range(3 * group, 3 * group + 3):
            news[member] = flat(news[member])
    return tuple(a.reshape(()) for a in results[0:3]) + tuple(news)


def solution(mesh):
    placed = (
        P("wide", None, None),
        P("wide", None),
        P("wide"),
        P("wide", None),
        P("wide", None),
        P("wide", None),
        P(None, "wide"),
        P(None, "wide"),
        P(None, "wide"),
        P(None, None, "wide", "narrow"),
        P(None, None, "wide", "narrow"),
        P(None, None, "wide", "narrow"),
        P(None, "narrow", "wide"),
        P(None, "narrow", "wide"),
        P(None, "narrow", "wide"),
        P(None, "wide", "narrow"),
        P(None, "wide", "narrow"),
        P(None, "wide", "narrow"),
        P(None, "narrow"),
        P(None, "narrow"),
        P(None, "narrow"),
        P(None, "narrow", "wide"),
        P(None, "narrow", "wide"),
        P(None, "narrow", "wide"),
        P(),
        P(),
        P(),
        P("wide", "narrow"),
        P("wide", "narrow"),
        P("wide", "narrow"),
        P("wide", None),
        P("wide", None),
        P("wide", None),
    )
    return jax.shard_map(
        per_device,
        mesh=mesh,
        in_specs=placed,
        out_specs=(P(), P(), P()) + placed[6:],
        check_vma=False,
    )
```

```python
import functools

import jax
import jax.numpy as jnp
from jax import lax
from jax.experimental import pallas as pl
from jax.experimental.pallas import tpu as pltpu
from jax.sharding import PartitionSpec as P

D = 256
HEADS = 4
HEAD_DIM = 64
FF = 1024
VOCAB = 512
ACTIONS = 18
GAMES = 26
OBS = 16
FRAMES = 20
STEP_NUMBER = 5
FRAME_TOKENS = 17
LENGTH = 340
ROWS = 896
NVEC = 14

EPS_NORM = 1e-05
BETA_ONE = 0.5
BETA_TWO = 0.5
RATE_TABLE = 0.5
RATE_MATRIX = 0.05
RATE_VECTOR = 0.2
DECAY_RATE = 0.01
EPS_ADAM = 1e-08
CLIP_AT = 0.1

SEQ = 352
KEYS = 384
BLOCK, BLOCKS = 128, 3
TILE = 32
SIDE_ROWS = 32
QUERIES = HEADS * BLOCK
VALUE_ROWS = 80

COL_QKV, COL_PROJ, COL_UP, COL_DOWN, COL_LAYER = 0, 768, 1024, 2048, 3072
HALF_ATTENTION = ((0, 128, 0), (128, 128, 256), (256, 128, 512), (384, 128, COL_PROJ))
HALF_LAYER = HALF_ATTENTION + ((512, 512, COL_UP), (1024, 512, COL_DOWN))
COL_TABLE, COL_SMALL, COL_FIRST = 3072, 3968, 4096
HALF_FIRST = HALF_LAYER + ((1536, 512, COL_TABLE),)
HALF_FIRST_COLS = 2048
COL_HEAD, COL_SECOND = 3072, 3584
HALF_SECOND = HALF_LAYER + ((1536, 256, COL_HEAD),)
HALF_SECOND_COLS = 1792
GRAD_UP, GRAD_DOWN = 0, 1024
HALF_GRAD_FF = ((0, 512, GRAD_UP), (512, 512, GRAD_DOWN))
GRAD_TABLE, GRAD_SMALL = 1024, 1920
HALF_GRAD_REST = HALF_ATTENTION + ((512, 512, GRAD_TABLE),)
HALF_GRAD_COLS = 1024
SMALL_ROWS, SMALL_BIAS, SMALL_SIDE = 32, 14, 22

F32, BF16 = jnp.float32, jnp.bfloat16
MIB = 1024 * 1024


def dot_nn(a, b):
    return lax.dot_general(a, b, (((1,), (0,)), ((), ())), preferred_element_type=F32)


def dot_nt(a, b):
    return lax.dot_general(a, b, (((1,), (1,)), ((), ())), preferred_element_type=F32)


def dot_tn(a, b):
    return lax.dot_general(a, b, (((0,), (0,)), ((), ())), preferred_element_type=F32)


def places(fast):
    wide, core = lax.axis_index("wide"), lax.axis_index("narrow")
    return (wide if fast else 0), core, wide


def tiles(rows, size):
    return [slice(first, first + size) for first in range(0, rows, size)]


def normalise(x):
    centred = x - jnp.mean(x, axis=1, keepdims=True)
    scale = lax.rsqrt(jnp.mean(centred * centred, axis=1, keepdims=True) + EPS_NORM)
    return centred * scale, scale


def keep_norm(rows, xhat, scale, kept):
    kept[0][rows] = xhat.astype(BF16)
    kept[1][rows] = jnp.broadcast_to(scale, (TILE, 128))


def kept_norm(rows, kept):
    scale = kept[1][rows]
    return kept[0][rows].astype(F32), jnp.concatenate([scale, scale], axis=1)


def normalise_back(grad, xhat, scale, gain):
    inner = grad * gain
    mean_one = jnp.mean(inner, axis=1, keepdims=True)
    mean_two = jnp.mean(inner * xhat, axis=1, keepdims=True)
    return scale * (inner - mean_one - xhat * mean_two)


def column_sum(a):
    return jnp.sum(a, axis=0, keepdims=True)


def fold(a):
    return jnp.sum(a.reshape(a.shape[0] // 8, 8, a.shape[1]), axis=0)


def plus(total, a):
    return a if total is None else total + a


def block_lanes(i, h=None):
    if h is None:
        return slice(QUERIES * i, QUERIES * (i + 1))
    return slice(QUERIES * i + BLOCK * h, QUERIES * i + BLOCK * (h + 1))


def head_rows(h):
    return slice(HEAD_DIM * h, HEAD_DIM * (h + 1))


def spread_heads(source, target_ref):
    for h in range(HEADS):
        for i in range(BLOCKS):
            target_ref[head_rows(h), block_lanes(i, h)] = source[
                head_rows(h), BLOCK * i : BLOCK * (i + 1)
            ]


def causal_mask():
    key = lax.broadcasted_iota(jnp.int32, (BLOCK, QUERIES), 0)
    query = lax.broadcasted_iota(jnp.int32, (BLOCK, QUERIES), 1) & (BLOCK - 1)
    return jnp.where(key <= query, 0.0, -1e30)


def assemble(pieces_mine, pieces_other, place, w_ref, halves):
    me, core, _ = place
    is_first = core == 0
    for p in range(4):

        def block(z, _, p=p):
            row = pl.multiple_of((me ^ (4 * z + p)) * 16, 16)
            for src, width, dest in halves:
                mine = pieces_mine[p][z, :, src : src + width]
                other = pieces_other[p][z, :, src : src + width]
                if dest == COL_QKV:
                    mine, other = mine * 0.125, other * 0.125
                w_ref[pl.ds(row, 16), dest : dest + width] = jnp.where(is_first, mine, other)
                w_ref[pl.ds(row, 16), dest + width : dest + 2 * width] = jnp.where(
                    is_first, other, mine
                )
            return 0

        lax.fori_loop(0, 4, block, 0)


def disperse(g_ref, place, keep_ref, send_ref, halves, scaled=True):
    me, core, _ = place
    is_first = core == 0

    def block(i, _):
        p, z = i >> 2, i & 3
        row = pl.multiple_of((me ^ (4 * z + p)) * 16, 16)
        for src, width, dest in halves:
            low = g_ref[pl.ds(row, 16), dest : dest + width]
            high = g_ref[pl.ds(row, 16), dest + width : dest + 2 * width]
            if scaled and dest == COL_QKV:
                low, high = low * 0.125, high * 0.125
            keep_ref[p, z, :, src : src + width] = jnp.where(is_first, low, high).astype(BF16)
            send_ref[p, z, :, src : src + width] = jnp.where(is_first, high, low).astype(BF16)
        return 0

    lax.fori_loop(0, 16, block, 0)


def make_hits(meta_ref, hits_ref):
    for rows in tiles(SEQ, TILE):
        lane = lax.broadcasted_iota(jnp.int32, (TILE, ROWS), 1)
        place = lax.broadcasted_iota(jnp.int32, (TILE, 1), 0) + (VOCAB + ACTIONS + GAMES + rows.start)
        meta = meta_ref[rows]
        hit = (lane == meta[:, 0:1]) | (lane == meta[:, 1:2]) | (lane == place)
        hits_ref[rows] = jnp.where(hit, 1.0, 0.0).astype(BF16)


def gelu_and_slope(up):
    up = up.astype(BF16)
    square = up * up
    half = jax.nn.sigmoid(up * (BF16(1.5957691216057308) + BF16(0.0713548162726) * square))
    hidden = up * half
    slope = BF16(1.5957691216057308) + BF16(0.2140644488178) * square
    return hidden, half + hidden * (BF16(1.0) - half) * slope


def layer_forward(x_ref, w_ref, vec, bias, kept, work):
    qt_ref, kv_ref, p0, p1, p2, r_ref, ot_ref, o_ref = kept[0:8]
    h_ref, gp_ref, a_ref, c_ref = kept[9:13]
    qst_ref, vt_ref, mask_ref, wqt_ref, long_ref, u_ref, y_ref, m_ref = work
    for rows in tiles(SEQ, TILE):
        xhat, scale = normalise(x_ref[rows])
        keep_norm(rows, xhat, scale, kept[14:16])
        normed16 = (xhat * vec[0:1] + vec[1:2]).astype(BF16)
        a_ref[rows], long_ref[rows] = normed16, normed16
    kv_ref[0:SEQ] = dot_nn(long_ref[0:SEQ], w_ref[:, 256:768]).astype(BF16)
    kv_ref[SEQ:KEYS] = jnp.zeros((KEYS - SEQ, 512), BF16)
    qt_ref[...] = dot_nt(wqt_ref[...], long_ref[...]).astype(BF16)
    spread_heads(qt_ref, qst_ref)
    turned = jnp.transpose(kv_ref[:, 256:512])
    for h in range(HEADS):
        vt_ref[VALUE_ROWS * h : VALUE_ROWS * h + HEAD_DIM] = turned[head_rows(h)]
    for i, pt_ref in enumerate((p0, p1, p2)):
        seen, first = BLOCK * (i + 1), BLOCK * i
        scores = dot_nn(kv_ref[0:seen, 0:256], qst_ref[:, block_lanes(i)])
        last = scores[first:] + mask_ref[...]
        peak = jnp.max(last, axis=0, keepdims=True)
        if i:
            peak = jnp.maximum(peak, jnp.max(scores[0:first], axis=0, keepdims=True))
            pt_ref[0:first] = jnp.exp(scores[0:first] - peak).astype(BF16)
        pt_ref[first:seen] = jnp.exp(last - peak).astype(BF16)
        for h in range(HEADS):
            values = vt_ref[VALUE_ROWS * h : VALUE_ROWS * (h + 1), 0:seen]
            out = dot_nn(values, pt_ref[:, BLOCK * h : BLOCK * (h + 1)])
            inverse = 1.0 / out[HEAD_DIM : HEAD_DIM + 1]
            r_ref[h : h + 1, first:seen] = inverse
            ot_ref[head_rows(h), first:seen] = (out[0:HEAD_DIM] * inverse).astype(BF16)
    o_ref[...] = jnp.transpose(ot_ref[...])[0:SEQ]
    y_ref[...] = dot_nt(o_ref[...], w_ref[:, COL_PROJ : COL_PROJ + 256])
    for rows in tiles(SEQ, TILE):
        middle = x_ref[rows] + (y_ref[rows] + vec[2:3])
        m_ref[rows] = middle
        xhat, scale = normalise(middle)
        keep_norm(rows, xhat, scale, (kept[8], kept[13]))
        c_ref[rows] = (xhat * vec[3:4] + vec[4:5]).astype(BF16)
    u_ref[...] = dot_nn(c_ref[...], w_ref[:, COL_UP : COL_UP + FF])
    for rows in tiles(SEQ, TILE):
        for first in range(0, FF, 256):
            cols = slice(first, first + 256)
            h_ref[rows, cols], gp_ref[rows, cols] = gelu_and_slope(u_ref[rows, cols] + bias[:, cols])
    y_ref[...] = dot_nt(h_ref[...], w_ref[:, COL_DOWN : COL_DOWN + FF])


def add_gradient(g_ref, column, left, right):
    g_ref[:, column : column + right.shape[1]] += dot_tn(left, right)


def ff_backward(grad_ref, grad16_ref, w_ref, w_up, w_down, vec, kept, v_ref, v_row, bias_row, work, mid_ref, mid16_refs):
    norm_kept, gp_ref = kept
    du_ref, ones_ref, u_ref, y_ref = work
    u_ref[...] = dot_nn(grad16_ref[...], w_ref[:, w_down : w_down + FF])
    for rows in tiles(SEQ, TILE):
        du_ref[rows] = u_ref[rows].astype(BF16) * gp_ref[rows]
    bias_grad = dot_nn(ones_ref[...], du_ref[...])
    for chunk in range(4):
        v_ref[bias_row + chunk, 0:1] += bias_grad[0:1, 256 * chunk : 256 * chunk + 256]
    y_ref[...] = dot_nt(du_ref[...], w_ref[:, w_up : w_up + FF])
    totals = [None] * 3
    for rows in tiles(SEQ, TILE):
        xhat, scale = kept_norm(rows, norm_kept)
        grad = y_ref[rows]
        mid = grad_ref[rows] + normalise_back(grad, xhat, scale, vec[3:4])
        mid_ref[rows] = mid
        for mid16_ref in mid16_refs:
            mid16_ref[rows] = mid.astype(BF16)
        for i, a in enumerate((mid, grad * xhat, grad)):
            totals[i] = plus(totals[i], fold(a))
    for i in range(3):
        v_ref[v_row + 2 + i] += totals[i]


def attention_backward(mid_ref, mid16_ref, w_ref, vec, kept, v_ref, v_row, work, out_ref):
    norm_kept, (qt_ref, kv_ref, p0, p1, p2, r_ref, ot_ref) = kept
    dost_ref, qst_ref, kt_ref, dst_ref, dqt_ref, dkv_ref, dqkv_ref, proj_ref, y_ref = work
    grad_o = dot_nt(proj_ref[...], mid16_ref[...]).astype(BF16).astype(F32)
    kt_ref[...] = jnp.transpose(kv_ref[:, 0:256])
    deltas = []
    for h in range(HEADS):
        scaled = grad_o[head_rows(h)] * r_ref[h : h + 1]
        deltas.append(column_sum(scaled * ot_ref[head_rows(h)].astype(F32)))
        scaled = scaled.astype(BF16)
        for i in range(BLOCKS):
            dost_ref[head_rows(h), block_lanes(i, h)] = scaled[:, BLOCK * i : BLOCK * (i + 1)]
    for i, pt_ref in enumerate((p0, p1, p2)):
        seen, first = BLOCK * (i + 1), BLOCK * i
        lanes = block_lanes(i)
        delta = jnp.concatenate([a[:, first:seen] for a in deltas], axis=1)
        grad = dot_nn(kv_ref[0:seen, 256:512], dost_ref[:, lanes])
        dst_ref[0:seen, lanes] = pt_ref[...] * (grad - delta).astype(BF16)
        for h in range(HEADS):
            out = dot_nn(kt_ref[head_rows(h), 0:seen], dst_ref[0:seen, block_lanes(i, h)])
            dqt_ref[head_rows(h), first:seen] = out.astype(BF16)
        for at, left, right in (
            (0, dst_ref[0:seen, lanes], qst_ref),
            (256, pt_ref[...], dost_ref),
        ):
            out = dot_nt(left, right[:, lanes])
            if i:
                dkv_ref[0:first, at : at + 256] += out[0:first]
            dkv_ref[first:seen, at : at + 256] = out[first:]
    dqkv_ref[:, 0:256] = jnp.transpose(dqt_ref[...])[0:SEQ]
    dqkv_ref[:, 256:768] = dkv_ref[0:SEQ].astype(BF16)
    y_ref[...] = dot_nt(dqkv_ref[...], w_ref[:, COL_QKV : COL_QKV + 768])
    totals = [None] * 2
    for rows in tiles(SEQ, TILE):
        xhat, scale = kept_norm(rows, norm_kept)
        grad = y_ref[rows]
        out = mid_ref[rows] + normalise_back(grad, xhat, scale, vec[0:1])
        out_ref[rows] = out.astype(out_ref.dtype)
        for i, a in enumerate((grad * xhat, grad)):
            totals[i] = plus(totals[i], fold(a))
    for i in range(2):
        v_ref[v_row + i] += totals[i]


def own_bias(place, mine, other):
    is_first = place[1] == 0
    return jnp.concatenate(
        [jnp.where(is_first, mine, other), jnp.where(is_first, other, mine)], axis=1
    )


def prepare_kernel(
    fast, games_ref, tokens, actions, valid, rewards, ends, out, out_side, x_ref
):
    count = out.shape[0]
    frames = tokens.shape[2]
    base = places(fast)[1] * count
    row = lax.broadcasted_iota(jnp.int32, (SEQ, frames), 0)
    start = lax.broadcasted_iota(jnp.int32, (SEQ, frames), 1) * FRAME_TOKENS
    here = jnp.where((row >= start) & (row < start + FRAME_TOKENS), 1.0, 0.0).astype(BF16)
    coming = jnp.where((row >= start - FRAME_TOKENS) & (row < start), 1.0, 0.0).astype(BF16)
    passed = jnp.sum(jnp.where(row >= start + FRAME_TOKENS, 1, 0), axis=1, keepdims=True)
    place = lax.broadcasted_iota(jnp.int32, (SEQ, 1), 0)
    spot = place - passed * FRAME_TOKENS
    lane = lax.broadcasted_iota(jnp.int32, (SEQ, 24), 1)
    wide_lane = lax.broadcasted_iota(jnp.int32, (SEQ, 128), 1)
    inside = place < LENGTH
    one_frame = (
        lax.broadcasted_iota(jnp.int32, (SIDE_ROWS, frames), 0)
        == lax.broadcasted_iota(jnp.int32, (SIDE_ROWS, frames), 1)
    )
    one_frame = jnp.where(one_frame, 1.0, 0.0).astype(BF16)
    side_lane = lax.broadcasted_iota(jnp.int32, (SIDE_ROWS, 128), 1)
    x_ref[...] = jnp.zeros(x_ref.shape, jnp.int32)
    for s in range(count):
        x_ref[0:OBS] = tokens[base + s]
        x_ref[16:17] = actions[pl.ds(base + s, 1)] + VOCAB
        x_ref[17:18] = valid[pl.ds(base + s, 1)]
        x_ref[18:19] = rewards[pl.ds(base + s, 1)]
        x_ref[19:20] = ends[pl.ds(base + s, 1)] + 3
        high = (x_ref[...] >> 4).astype(F32).astype(BF16)
        low = (x_ref[...] & 15).astype(F32).astype(BF16)
        now = dot_nt(here, high) * 16.0 + dot_nt(here, low)
        soon = dot_nt(coming, high) * 16.0 + dot_nt(coming, low)

        def pick(condition, a):
            return jnp.sum(jnp.where(condition, a, 0.0), axis=1, keepdims=True).astype(jnp.int32)

        ids = jnp.where(inside, pick(lane == spot, now), -1)
        game = jnp.where(inside, games_ref[base + s] + (VOCAB + ACTIONS), -1)
        target = pick((lane == spot + 1) & (spot < 15), now)
        target = target + pick((lane == 0) & (spot == 16), soon)
        weight = pick((lane == 17) & (spot < 15), now) + pick((lane == 17) & (spot == 16), soon)
        result = jnp.zeros((SEQ, 128), jnp.int32)
        for c, column in enumerate((ids, game, target, weight)):
            result = jnp.where(wide_lane == c, column, result)
        out[s] = result
        by_frame = dot_nt(one_frame, high) * 16.0 + dot_nt(one_frame, low)
        result = jnp.zeros((SIDE_ROWS, 128), jnp.int32)
        for c in range(3):
            column = by_frame[:, 17 + c : 18 + c].astype(jnp.int32)
            result = jnp.where(side_lane == c, column, result)
        out_side[s] = result


def start_forward(work, w_ref):
    qst_ref, vt_ref, mask_ref, wqt_ref, long_ref = work[0:5]
    long_ref[SEQ:KEYS] = jnp.zeros((KEYS - SEQ, D), BF16)
    qst_ref[...] = jnp.zeros(qst_ref.shape, BF16)
    vt_ref[...] = jnp.ones(vt_ref.shape, BF16)
    mask_ref[...] = causal_mask()
    wqt_ref[...] = jnp.transpose(w_ref[:, 0:256])


def first_forward_kernel(fast, *refs):
    refs = (places(fast),) + refs
    place, meta_ref, vec_ref, bias_ref, bias_other = refs[0:5]
    mine, other = refs[5:9], refs[9:13]
    w_attention, w_ff, side_out, next_ref, hits_ref = refs[13:18]
    kept = [ref.at[0] for ref in refs[18:34]]
    w_ref, x_ref = refs[34:36]
    work = refs[36:44]
    y_ref, m_ref = work[6:8]

    @pl.when(pl.program_id(0) == 0)
    def _():
        assemble(mine, other, place, w_ref, HALF_FIRST)
        w_attention[...] = w_ref[:, 0:COL_UP]
        w_ff[...] = w_ref[:, COL_UP:COL_TABLE]
        side_out[...] = w_ref[:, COL_SMALL:]
        start_forward(work, w_ref)

    make_hits(meta_ref.at[0], hits_ref.at[0])
    x_ref[...] = dot_nt(hits_ref[0], w_ref[:, COL_TABLE : COL_TABLE + ROWS])
    bias = own_bias(place, bias_ref[0:1], bias_other[0:1])
    vec = vec_ref[0:6]
    layer_forward(x_ref, w_ref, vec, bias, kept, work)
    for rows in tiles(SEQ, TILE):
        next_ref[0, rows] = m_ref[rows] + (y_ref[rows] + vec[5:6])


def codebook_losses(logits, meta):
    weight = meta[:, 3:4].astype(F32)
    peak = jnp.max(logits, axis=1, keepdims=True)
    expanded = jnp.exp(logits - peak)
    total = jnp.sum(expanded, axis=1, keepdims=True)
    hit = lax.broadcasted_iota(jnp.int32, logits.shape, 1) == meta[:, 2:3]
    hit = jnp.where(hit, weight, 0.0)
    return weight * (peak + jnp.log(total)), hit, expanded * (weight / total) - hit


def side_losses(side, meta):
    lane = lax.broadcasted_iota(jnp.int32, side.shape, 1)
    is_reward, is_end = lane < 3, (lane == 3) | (lane == 4)
    is_side = lane < 5
    weight = meta[:, 0:1].astype(F32)
    reward_peak = jnp.max(jnp.where(is_reward, side, -1e30), axis=1, keepdims=True)
    end_peak = jnp.max(jnp.where(is_end, side, -1e30), axis=1, keepdims=True)
    shifted = jnp.where(is_side, side - jnp.where(is_reward, reward_peak, end_peak), 0.0)
    expanded = jnp.where(is_side, jnp.exp(shifted), 0.0)
    reward_total = jnp.sum(jnp.where(is_reward, expanded, 0.0), axis=1, keepdims=True)
    end_total = jnp.sum(jnp.where(is_end, expanded, 0.0), axis=1, keepdims=True)
    hit = (lane == meta[:, 1:2]) | (lane == meta[:, 2:3])
    picked = jnp.sum(jnp.where(hit, side, 0.0), axis=1, keepdims=True)
    terms = reward_peak + jnp.log(reward_total) + end_peak + jnp.log(end_total) - picked
    grad = expanded * jnp.where(is_reward, weight / reward_total, weight / end_total)
    return weight * terms, grad - jnp.where(hit, weight, 0.0), weight


def frame_ends(shape, frame_axis):
    frame = lax.broadcasted_iota(jnp.int32, shape, frame_axis)
    row = lax.broadcasted_iota(jnp.int32, shape, 1 - frame_axis)
    hit = (row == frame * FRAME_TOKENS + OBS) & (frame < FRAMES)
    return jnp.where(hit, 1.0, 0.0).astype(BF16)


def middle_kernel(fast, *refs):
    refs = (places(fast),) + refs
    place, meta_ref, frame_ref, vec_ref, bias_ref, bias_other, side_ref, in_ref = refs[0:8]
    mine, other = refs[8:12], refs[12:16]
    grad_ref, keep_ref, send_ref, v_out, scalar_ref = refs[16:21]
    refs = refs[1:]
    w_ref, g_ref, v_ref = refs[20:23]
    kept = list(refs[23:39])
    forward_work = refs[39:47]
    u_ref, y_ref, m_ref = forward_work[5:8]
    backward_work = list(refs[47:53])
    proj_ref = refs[53]
    du_all, ones_ref, up_ref, up16_all, mid_ref, mid16_ref = refs[54:60]
    last_kept = refs[60:62]
    final_all, logit_ref, dlogit_all, pick_ref, put_ref, mid16_all = refs[62:68]
    o_all, h_all, a_all, c_all, dqkv_all = kept[7], kept[9], kept[11], kept[12], backward_work[5]
    dost_ref = backward_work[0]
    step = pl.program_id(0)

    @pl.when(step == 0)
    def _():
        assemble(mine, other, place, w_ref, HALF_SECOND)
        w_ref[:, COL_SECOND:] = side_ref[...]
        g_ref[...] = jnp.zeros(g_ref.shape, F32)
        v_ref[...] = jnp.zeros(v_ref.shape, F32)
        scalar_ref[...] = jnp.zeros(scalar_ref.shape, F32)
        start_forward(forward_work, w_ref)
        dost_ref[...] = jnp.zeros(dost_ref.shape, BF16)
        proj_ref[...] = jnp.transpose(w_ref[:, COL_PROJ : COL_PROJ + 256])
        ones_ref[...] = jnp.ones(ones_ref.shape, BF16)
        mid16_ref[SEQ:KEYS] = jnp.zeros((KEYS - SEQ, D), BF16)
        pick_ref[...] = frame_ends((SIDE_ROWS, SEQ), 0)
        put_ref[...] = frame_ends((SEQ, SIDE_ROWS), 1)

    here = pl.ds(pl.multiple_of((step & 1) * SEQ, 32), SEQ)
    for i in (7, 9, 11, 12):
        kept[i] = kept[i].at[here]
    gp_ref = kept[10]
    backward_work[5] = dqkv_all.at[here]
    du_ref, up16_ref, pair16_ref = du_all.at[here], up16_all.at[here], mid16_all.at[here]
    final_ref, dlogit_ref = final_all.at[here], dlogit_all.at[here]
    x_ref = in_ref.at[0]
    vec = vec_ref[6:12]
    bias = own_bias(place, bias_ref[1:2], bias_other[1:2])
    layer_forward(x_ref, w_ref, vec, bias, kept, forward_work)

    gain, offset = vec_ref[12:13], vec_ref[13:14]
    for rows in tiles(SEQ, TILE):
        last = m_ref[rows] + (y_ref[rows] + vec[5:6])
        xhat, scale = normalise(last)
        keep_norm(rows, xhat, scale, last_kept)
        final_ref[rows] = (xhat * gain + offset).astype(BF16)
    cols_head = slice(COL_HEAD, COL_HEAD + VOCAB + 128)
    logit_ref[...] = dot_nn(final_ref[...], w_ref[:, COL_HEAD : COL_HEAD + VOCAB])
    logs, picked = None, None
    for rows in tiles(SEQ, TILE):
        logits = logit_ref[rows]
        log, hit, grad = codebook_losses(logits, meta_ref[0, rows])
        dlogit_ref[rows, :VOCAB] = grad.astype(BF16)
        logs, picked = plus(logs, log), plus(picked, fold(hit * logits))
    acting = dot_nn(pick_ref[...], final_ref[...]).astype(BF16)
    side = dot_nn(acting, w_ref[:, COL_HEAD + VOCAB : COL_HEAD + VOCAB + 128])
    side_loss, grad, weight = side_losses(side, frame_ref[0])
    dlogit_ref[:, VOCAB:] = dot_nn(put_ref[...], grad.astype(BF16)).astype(BF16)
    loss = column_sum(logs) + column_sum(side_loss)
    loss = loss - jnp.sum(column_sum(picked), axis=1, keepdims=True)
    valid = column_sum(weight)
    scalar_lane = lax.broadcasted_iota(jnp.int32, (8, 128), 1)
    scalar_row = lax.broadcasted_iota(jnp.int32, (8, 128), 0) == 0
    scalar_ref[...] += jnp.where(
        scalar_row,
        jnp.where(scalar_lane == 0, loss, jnp.where(scalar_lane == 1, valid, 0.0)),
        0.0,
    )
    y_ref[...] = dot_nt(dlogit_ref[...], w_ref[:, cols_head])
    totals = [None] * 3
    for rows in tiles(SEQ, TILE):
        xhat, scale = kept_norm(rows, last_kept)
        grad = y_ref[rows]
        up = normalise_back(grad, xhat, scale, gain)
        up_ref[rows] = up
        up16_ref[rows] = up.astype(BF16)
        for i, a in enumerate((up, grad * xhat, grad)):
            totals[i] = plus(totals[i], fold(a))
    for i in range(3):
        v_ref[11 + i] += totals[i]
    ff_backward(
        up_ref,
        up16_ref,
        w_ref,
        COL_UP,
        COL_DOWN,
        vec,
        ((kept[8], kept[13]), gp_ref),
        v_ref,
        6,
        SMALL_BIAS + 4,
        (du_ref, ones_ref, u_ref, y_ref),
        mid_ref,
        (mid16_ref, pair16_ref),
    )
    attention_backward(
        mid_ref,
        mid16_ref,
        w_ref,
        vec,
        (kept[14:16], kept[0:7]),
        v_ref,
        6,
        (dost_ref, forward_work[0]) + tuple(backward_work[1:]) + (proj_ref, y_ref),
        grad_ref.at[0],
    )

    @pl.when(step & 1 == 1)
    def _():
        add_gradient(g_ref, COL_QKV, a_all[...], dqkv_all[...])
        add_gradient(g_ref, COL_PROJ, mid16_all[...], o_all[...])
        add_gradient(g_ref, COL_UP, c_all[...], du_all[...])
        add_gradient(g_ref, COL_DOWN, up16_all[...], h_all[...])
        add_gradient(g_ref, COL_HEAD, final_all[...], dlogit_all[...])

    @pl.when(step == pl.num_programs(0) - 1)
    def _():
        disperse(g_ref, place, keep_ref, send_ref, HALF_SECOND)
        side = jnp.transpose(g_ref[:, COL_SECOND:])
        for i in range(5):
            v_ref[SMALL_SIDE + i, 0:1] = side[i : i + 1]
        v_out[...] = v_ref[...]


def ff_backward_kernel(fast, *refs):
    vec_ref, w_ref, grad_ref, v_in = refs[0:4]
    xhat_ref, scale_ref, h_ref, gp_ref, c_ref = [ref.at[0] for ref in refs[4:9]]
    mid_ref, keep_ref, send_ref, v_out = refs[9:13]
    g_ref, v_ref, grad16_ref, du_ref, ones_ref, u_ref, y_ref = refs[13:20]
    step = pl.program_id(0)

    @pl.when(step == 0)
    def _():
        g_ref[...] = jnp.zeros(g_ref.shape, F32)
        v_ref[...] = v_in[...]
        ones_ref[...] = jnp.ones(ones_ref.shape, BF16)

    total = None
    for rows in tiles(SEQ, TILE):
        grad = grad_ref[0, rows]
        grad16_ref[rows] = grad.astype(BF16)
        total = plus(total, fold(grad))
    v_ref[5] += total
    ff_backward(
        grad_ref.at[0],
        grad16_ref,
        w_ref,
        GRAD_UP,
        GRAD_DOWN,
        vec_ref[0:6],
        ((xhat_ref, scale_ref), gp_ref),
        v_ref,
        0,
        SMALL_BIAS,
        (du_ref, ones_ref, u_ref, y_ref),
        mid_ref.at[0],
        (),
    )
    add_gradient(g_ref, GRAD_DOWN, grad16_ref[...], h_ref[...])
    add_gradient(g_ref, GRAD_UP, c_ref[...], du_ref[...])

    @pl.when(step == pl.num_programs(0) - 1)
    def _():
        disperse(g_ref, places(fast), keep_ref, send_ref, HALF_GRAD_FF, False)
        v_out[...] = v_ref[...]


def attention_backward_kernel(fast, *refs):
    vec_ref, w_ref, mid_ref, v_in = refs[0:4]
    kept = [ref.at[0] for ref in refs[4:13]]
    o_all, a_all, hits_all = refs[13:16]
    keep_ref, send_ref, v_out = refs[17:20]
    g_ref, v_ref, mid16_ref, mid16_all, out16_all, dqkv_all = refs[20:26]
    work = list(refs[26:34])
    dost_ref, qst_ref, proj_ref = work[0], work[1], work[6]
    step = pl.program_id(0)

    @pl.when(step == 0)
    def _():
        v_ref[...] = v_in[...]
        dost_ref[...] = jnp.zeros(dost_ref.shape, BF16)
        qst_ref[...] = jnp.zeros(qst_ref.shape, BF16)
        proj_ref[...] = jnp.transpose(w_ref[:, COL_PROJ : COL_PROJ + 256])
        mid16_ref[SEQ:KEYS] = jnp.zeros((KEYS - SEQ, D), BF16)

    here = pl.ds(pl.multiple_of(step * SEQ, 32), SEQ)
    all16_ref = mid16_all.at[here]
    spread_heads(kept[2], qst_ref)
    for rows in tiles(SEQ, TILE):
        mid16 = mid_ref[0, rows].astype(BF16)
        mid16_ref[rows], all16_ref[rows] = mid16, mid16
    work.insert(6, dqkv_all.at[here])
    attention_backward(
        mid_ref.at[0],
        mid16_ref,
        w_ref,
        vec_ref[0:6],
        (kept[0:2], kept[2:9]),
        v_ref,
        0,
        work,
        out16_all.at[here],
    )

    @pl.when(step == pl.num_programs(0) - 1)
    def _():
        g_ref[:, COL_QKV : COL_QKV + 768] = dot_tn(a_all[...], dqkv_all[...])
        g_ref[:, COL_PROJ : COL_PROJ + 256] = dot_tn(mid16_all[...], o_all[...])
        g_ref[:, GRAD_TABLE : GRAD_TABLE + ROWS] = dot_tn(out16_all[...], hits_all[...])
        small = jnp.sum(v_ref[...], axis=1)
        v_out[...] = small
        for block in range(16):
            quarter = small[8 * (block // 4) : 8 * (block // 4) + 8]
            g_ref[16 * block : 16 * block + 8, GRAD_SMALL:] = quarter[:, 0:128]
            g_ref[16 * block + 8 : 16 * block + 16, GRAD_SMALL:] = quarter[:, 128:256]
        disperse(g_ref, places(fast), keep_ref, send_ref, HALF_GRAD_REST)


def pack_layer(attn, proj, up, down, layer, out):
    for j in range(3):
        out[:, 128 * j : 128 * j + 128] = attn[layer, j].astype(BF16)
    out[:, 384:512] = proj[layer].astype(BF16)
    out[:, 512:1024] = up[layer].astype(BF16)
    out[:, 1024:1536] = down[layer].astype(BF16)


def pack_kernel(fast, table, attn, proj, up, down, head, side, first, second, pad_ref):
    pack_layer(attn, proj, up, down, 0, first)
    pack_layer(attn, proj, up, down, 1, second)
    second[:, 1536:1792] = head[...].astype(BF16)
    rows = side.shape[1]
    eye = (
        lax.broadcasted_iota(jnp.int32, (rows, rows), 0)
        == lax.broadcasted_iota(jnp.int32, (rows, rows), 1)
    )
    eye = jnp.where(eye, 1.0, 0.0).astype(BF16)
    pad_ref[...] = jnp.zeros(pad_ref.shape, F32)
    pad_ref[:, 0:5] = dot_nt(eye, side[...].astype(BF16))
    high = jnp.concatenate([table[:, 512:896], pad_ref[...]], axis=1)
    first[:, 1536:2048] = jnp.where(places(fast)[1] == 0, table[:, 0:512], high).astype(BF16)


def finish_kernel(fast, *refs):
    count = (len(refs) - 5) // 2
    scalar_ref = refs[2 * count]
    out_rest, out_other, out_table, out_small = refs[2 * count + 1 :]
    square = jnp.zeros((1, 1), F32)
    for pieces, out in ((refs[0:count], out_rest), (refs[count : 2 * count], out_other)):
        total = pieces[0][...]
        for piece in pieces[1:]:
            total = total + piece[...].astype(F32)
        out[...] = total
        square = square + column_sum(jnp.sum(total * total, axis=1, keepdims=True))
    small = out_rest[:, 896:1024]
    extra = column_sum(jnp.sum(small * small, axis=1, keepdims=True))
    square = square - jnp.where(places(fast)[1] == 0, 0.0, extra)
    out_table[...] = out_rest[:, 512:1024]
    lane = lax.broadcasted_iota(jnp.int32, (8, 128), 1)
    row = lax.broadcasted_iota(jnp.int32, (8, 128), 0)
    message = scalar_ref[...] + jnp.where((row == 0) & (lane == 2), square, 0.0)
    if fast:
        spot = places(fast)[2] & 3
        part = jnp.where(spot & 1 == 0, small[0:4], small[4:8])
        part = jnp.where(spot & 2 == 0, part, jnp.where(spot & 1 == 0, small[8:12], small[12:16]))
        message = jnp.concatenate([part, message[0:4]], axis=0)
    for i in range(out_small.shape[0]):
        out_small[i] = message


def adam_rule(weight, moment, second, gradient, step_rate, decay_rate):
    moment_new = BETA_ONE * moment + (1.0 - BETA_ONE) * gradient
    second_new = BETA_TWO * second + (1.0 - BETA_TWO) * gradient * gradient
    moment_hat = moment_new / (1.0 - BETA_ONE**STEP_NUMBER)
    second_hat = second_new / (1.0 - BETA_TWO**STEP_NUMBER)
    weight_new = weight - step_rate * (
        moment_hat / (jnp.sqrt(second_hat) + EPS_ADAM) + decay_rate * weight
    )
    return (weight_new, moment_new, second_new)


def adam_kernel(fast, rest, others, swapped, gathered, beside, *refs):
    rows = rest.shape[0]
    _, core, wide = places(fast)
    is_first = core == 0
    if fast:
        small_parts = jnp.where(is_first, beside[...], gathered[...])
        quarters = [
            jnp.concatenate([small_parts[4 * z + p, 0:4] for p in range(4)], axis=0)
            for z in range(4)
        ]
    else:
        quarters = [refs[0][z] for z in range(4)]
        refs = refs[1:]
    params = [refs[3 * i : 3 * i + 3] for i in range(9)]
    loss_ref, valid_ref, norm_ref = refs[27:30]
    outs = [refs[30 + 3 * i : 33 + 3 * i] for i in range(9)]
    small_ref = refs[57]
    for z in range(4):
        small_ref[8 * z : 8 * z + 8, 0:128] = quarters[z][0:8]
        small_ref[8 * z : 8 * z + 8, 128:256] = quarters[z][8:16]
    sums = []
    for source in (gathered, beside):
        line = 4 if fast else 0
        total = source[0, line : line + 1]
        for i in range(1, source.shape[0]):
            total = total + source[i, line : line + 1]
        sums.append(total)
    scalars = sums[0] + sums[1]
    small = small_ref[...]
    loss, valid, square = scalars[:, 0:1], scalars[:, 1:2], scalars[:, 2:3]
    square = square + column_sum(jnp.sum(small * small, axis=1, keepdims=True))
    inverse = 1.0 / valid
    norm = jnp.sqrt(square) * inverse
    loss_ref[...], valid_ref[...], norm_ref[...] = loss, valid, norm
    factor = jnp.minimum(1.0, CLIP_AT / (norm + 1e-06)) * inverse
    table, attn, proj, up, bias, down, vectors, head, side = range(9)

    def update(which, index, gradient, step_rate, decay_rate):
        news = adam_rule(
            *(ref[index] for ref in params[which]), factor * gradient, step_rate, decay_rate
        )
        for ref, new in zip(outs[which], news):
            ref[index] = new

    layers = ((rest, others, 1792), (others, others, 512))
    for layer, (attention, feed, at) in enumerate(layers):
        for j in range(3):
            update(attn, (layer, j), attention[:, 128 * j : 128 * j + 128], RATE_MATRIX, DECAY_RATE)
        update(proj, (layer,), attention[:, 384:512], RATE_MATRIX, DECAY_RATE)
        update(up, (layer,), feed[:, at : at + 512], RATE_MATRIX, DECAY_RATE)
        update(down, (layer,), feed[:, at + 512 : at + 1024], RATE_MATRIX, DECAY_RATE)
        for i in range(2):
            low = SMALL_BIAS + 4 * layer + i
            row = jnp.where(is_first, small[low : low + 1], small[low + 2 : low + 3])
            index = (slice(layer, layer + 1), slice(256 * i, 256 * i + 256))
            update(bias, index, row, RATE_VECTOR, 0.0)
    whole = (slice(None), slice(None))
    update(head, whole, others[:, 1536:1792], RATE_MATRIX, DECAY_RATE)
    mine, theirs = rest[:, 512:1024], swapped[:, 0:512]
    low, high = jnp.where(is_first, mine, theirs), jnp.where(is_first, theirs, mine)
    update(table, (slice(None), slice(0, 512)), low, RATE_TABLE, DECAY_RATE)
    update(table, (slice(None), slice(512, 896)), high[:, 0:384], RATE_TABLE, DECAY_RATE)
    update(vectors, whole, small[0:NVEC], RATE_VECTOR, 0.0)
    turned = pltpu.roll(small[SMALL_SIDE : SMALL_SIDE + 8], lax.rem(D - wide * rows, D), 1)
    update(side, whole, turned[0:5, 0:rows], RATE_MATRIX, DECAY_RATE)


def swap(a, axis, distance):
    size = lax.axis_size(axis)
    return lax.ppermute(a, axis, [(i, i ^ distance) for i in range(size)])


def swap_column(piece, n_high):
    return [piece] + [swap(piece, "wide", 4 * k) for k in range(1, n_high)]


def gather_plane(column):
    return [column] + [swap(column, "wide", p) for p in range(1, 4)]


def gather_cores(mine):
    return [swap(a, "narrow", 1) for a in mine]


def in_blocks(parts, wide):
    n_high, rows, cols = parts[0].shape
    if rows == 16:
        return parts
    whole = jnp.stack(parts, axis=1).reshape(4 * n_high, rows, cols)
    whole = whole[wide ^ jnp.arange(4 * n_high)].reshape(4, 4, 16, cols)
    return [whole[:, p] for p in range(4)]


def in_pieces(blocks, wide, n_high):
    cols = blocks.shape[-1]
    if n_high == 4:
        return blocks
    rows = 64 // n_high
    whole = blocks.transpose(1, 0, 2, 3).reshape(4 * n_high, rows, cols)
    whole = whole[wide ^ jnp.arange(4 * n_high)]
    return whole.reshape(n_high, 4, rows, cols).transpose(1, 0, 2, 3)


def add_cores(keep, send, wide, n_high):
    keep, send = in_pieces(keep, wide, n_high), in_pieces(send, wide, n_high)
    received = swap(send, "narrow", 1)
    return [keep[p].astype(F32) + received[p].astype(F32) for p in range(4)]


def swap_plane(sums):
    return [swap(sums[p].astype(BF16), "wide", p) for p in range(1, 4)]


def add_plane(own, received):
    for a in received:
        own = own + a.astype(F32)
    return own


def column_pieces(own):
    return [own[0]] + [swap(own[k].astype(BF16), "wide", 4 * k) for k in range(1, own.shape[0])]


def resident(arrays):
    return [pltpu.with_memory_space_constraint(a, pltpu.VMEM) for a in arrays]


def in_hbm(arrays):
    return [pltpu.with_memory_space_constraint(a, pltpu.HBM) for a in arrays]


def full_spec(a):
    return pl.BlockSpec(a.shape, lambda *_: (0,) * len(a.shape))


def row_spec(shape):
    return pl.BlockSpec((1,) + shape, lambda i: (i,) + (0,) * len(shape))


def shaped(shape, dtype):
    return jax.ShapeDtypeStruct(shape, dtype)


VMEM_SPEC = pl.BlockSpec(memory_space=pltpu.VMEM)
ANY_SPEC = pl.BlockSpec(memory_space=pl.ANY)
SMEM_SPEC = pl.BlockSpec(memory_space=pltpu.SMEM)


VMEM_MIB = {
    "pack": 58,
    "prepare": 58,
    "first_forward": 22,
    "middle": 28,
    "ff_backward": 15,
    "attention_backward": 22,
    "finish": 58,
    "adam": 58,
}


def call(kernel, grid, in_specs, out_specs, out_shape, scratch, flops, bytes_accessed, name):
    extra = {"grid": grid} if grid else {}
    return pl.pallas_call(
        kernel,
        in_specs=in_specs,
        out_specs=out_specs,
        out_shape=out_shape,
        scratch_shapes=scratch,
        compiler_params=pltpu.CompilerParams(vmem_limit_bytes=VMEM_MIB[name] * MIB),
        cost_estimate=pl.CostEstimate(
            flops=flops, bytes_accessed=bytes_accessed, transcendentals=0
        ),
        name=name,
        **extra,
    )


KEPT = (
    ((D, KEYS), BF16),
    ((KEYS, 512), BF16),
    ((BLOCK, QUERIES), BF16),
    ((2 * BLOCK, QUERIES), BF16),
    ((3 * BLOCK, QUERIES), BF16),
    ((8, KEYS), F32),
    ((D, KEYS), BF16),
    ((SEQ, D), BF16),
    ((SEQ, D), BF16),
    ((SEQ, FF), BF16),
    ((SEQ, FF), BF16),
    ((SEQ, D), BF16),
    ((SEQ, D), BF16),
    ((SEQ, 128), F32),
    ((SEQ, D), BF16),
    ((SEQ, 128), F32),
)
FORWARD_WORK = [
    pltpu.VMEM((D, BLOCKS * QUERIES), BF16),
    pltpu.VMEM((HEADS * VALUE_ROWS, KEYS), BF16),
    pltpu.VMEM((BLOCK, QUERIES), F32),
    pltpu.VMEM((D, D), BF16),
    pltpu.VMEM((KEYS, D), BF16),
    pltpu.VMEM((SEQ, FF), F32),
    pltpu.VMEM((SEQ, D), F32),
    pltpu.VMEM((SEQ, D), F32),
]
BACKWARD_WORK = [
    pltpu.VMEM((D, BLOCKS * QUERIES), BF16),
    pltpu.VMEM((D, BLOCKS * QUERIES), BF16),
    pltpu.VMEM((D, KEYS), BF16),
    pltpu.VMEM((KEYS, BLOCKS * QUERIES), BF16),
    pltpu.VMEM((D, KEYS), BF16),
    pltpu.VMEM((KEYS, 512), F32),
    pltpu.VMEM((SEQ, 768), BF16),
]
PROJ_WORK = pltpu.VMEM((D, D), BF16)
ONES_WORK = pltpu.VMEM((16, SEQ), BF16)


def per_device(
    tokens,
    actions,
    game_ids,
    valid_steps,
    rewards,
    end_flags,
    embed_table,
    table_first,
    table_second,
    attn_weight,
    attn_first,
    attn_second,
    proj_weight,
    proj_first,
    proj_second,
    up_weight,
    up_first,
    up_second,
    up_bias,
    bias_first,
    bias_second,
    down_weight,
    down_first,
    down_second,
    vectors,
    vectors_first,
    vectors_second,
    head_weight,
    head_first,
    head_second,
    side_weight,
    side_first,
    side_second,
):
    n_high = lax.axis_size("wide") // 4
    wide = lax.axis_index("wide")
    rows = side_weight.shape[0]
    fast = rows == 16

    def flat(a):
        return jnp.swapaxes(a, -1, -2)

    params = (
        (flat(embed_table), flat(table_first), flat(table_second)),
        (attn_weight, attn_first, attn_second),
        (flat(proj_weight), flat(proj_first), flat(proj_second)),
        (up_weight, up_first, up_second),
        (up_bias, bias_first, bias_second),
        (flat(down_weight), flat(down_first), flat(down_second)),
        (vectors, vectors_first, vectors_second),
        (head_weight, head_first, head_second),
        (flat(side_weight), flat(side_first), flat(side_second)),
    )
    table, attn, proj, up, _, down, _, head, side = (group[0] for group in params)

    piece_first, piece_second = call(
        functools.partial(pack_kernel, fast),
        None,
        [VMEM_SPEC] * 7,
        [VMEM_SPEC] * 2,
        [shaped((rows, HALF_FIRST_COLS), BF16), shaped((rows, HALF_SECOND_COLS), BF16)],
        [pltpu.VMEM((rows, 128), F32)],
        10**6,
        10**6,
        "pack",
    )(table, attn, proj, up, down, head, side)
    other_bias = swap(up_bias, "narrow", 1)
    column = swap_column(piece_first, n_high)

    count = tokens.shape[0] // lax.axis_size("narrow")
    meta, frame_meta = call(
        functools.partial(prepare_kernel, fast),
        None,
        [SMEM_SPEC] + [VMEM_SPEC] * 5,
        [VMEM_SPEC] * 2,
        [shaped((count, SEQ, 128), jnp.int32), shaped((count, SIDE_ROWS, 128), jnp.int32)],
        [pltpu.VMEM((24, FRAMES), jnp.int32)],
        10**6,
        10**6,
        "prepare",
    )(game_ids, flat(tokens), actions, valid_steps, rewards, end_flags)
    column, other_bias, meta = lax.optimization_barrier((column, other_bias, meta))
    first_column = jnp.stack(column)
    first_mine = gather_plane(first_column)
    own, piece_second = lax.optimization_barrier((swap(first_column, "narrow", 1), piece_second))
    second_column = jnp.stack(swap_column(piece_second, n_high))
    second_column, across = lax.optimization_barrier((second_column, first_mine[3]))
    first_mine = first_mine[0:3] + [across]
    first_other = [own] + gather_cores(first_mine[1:])
    second_mine = gather_plane(second_column)
    first_parts = in_blocks(first_mine, wide) + in_blocks(first_other, wide)

    kept_specs = [row_spec(shape) for shape, _ in KEPT]
    kept_shapes = [shaped((count,) + shape, dtype) for shape, dtype in KEPT]
    row_f32 = shaped((count, SEQ, D), F32)
    meta_spec = row_spec((SEQ, 128))
    vec_specs = [full_spec(vectors), full_spec(up_bias), full_spec(up_bias)]
    w_attention_spec = pl.BlockSpec((D, 1024), lambda i: (0, 0))
    w_ff_spec = pl.BlockSpec((D, 2048), lambda i: (0, 0))
    side_spec = pl.BlockSpec((D, 128), lambda i: (0, 0))
    hits_spec = row_spec((SEQ, ROWS))
    results = call(
        functools.partial(first_forward_kernel, fast),
        (count,),
        [meta_spec] + vec_specs + [VMEM_SPEC] * 8,
        [w_attention_spec, w_ff_spec, side_spec, row_spec((SEQ, D)), hits_spec] + kept_specs,
        [shaped((D, 1024), BF16), shaped((D, 2048), BF16), shaped((D, 128), BF16), row_f32]
        + [shaped((count, SEQ, ROWS), BF16)]
        + kept_shapes,
        [pltpu.VMEM((D, COL_FIRST), BF16), pltpu.VMEM((SEQ, D), F32)] + FORWARD_WORK,
        4 * 10**9,
        20 * 10**6,
        "first_forward",
    )(*in_hbm([meta, vectors, up_bias, other_bias]), *resident(first_parts))
    w_attention, w_ff, side_copy, stream, hits = results[0:5]
    kept = results[5:]
    received, side_copy = lax.optimization_barrier((second_mine[1:], side_copy))
    second_mine = second_mine[0:1] + received
    second_other = gather_cores(second_mine)
    second_parts = in_blocks(second_mine, wide) + in_blocks(second_other, wide)

    def blocks(cols):
        return pl.BlockSpec((4, 4, 16, cols), lambda i: (0, 0, 0, 0))

    def block_shapes(cols):
        return [shaped((4, 4, 16, cols), BF16)] * 2

    small_spec = pl.BlockSpec((SMALL_ROWS, 8, D), lambda i: (0, 0, 0))
    small_shape = shaped((SMALL_ROWS, 8, D), F32)
    small_scratch = pltpu.VMEM((SMALL_ROWS, 8, D), F32)
    scalar_spec = pl.BlockSpec((8, 128), lambda i: (0, 0))
    grad_stream, keep_second, send_second, small_grads, scalars = call(
        functools.partial(middle_kernel, fast),
        (count,),
        [meta_spec, row_spec((SIDE_ROWS, 128))]
        + vec_specs
        + [side_spec, row_spec((SEQ, D))]
        + [VMEM_SPEC] * 8,
        [row_spec((SEQ, D))] + [blocks(HALF_SECOND_COLS)] * 2 + [small_spec, scalar_spec],
        [row_f32] + block_shapes(HALF_SECOND_COLS) + [small_shape, shaped((8, 128), F32)],
        [
            pltpu.VMEM((D, COL_SECOND + 128), BF16),
            pltpu.VMEM((D, COL_SECOND + 128), F32),
            small_scratch,
        ]
        + [pltpu.VMEM(shape, dtype) for shape, dtype in KEPT[0:7]]
        + [pltpu.VMEM((2 * SEQ, D), BF16), pltpu.VMEM(*KEPT[8])]
        + [pltpu.VMEM((2 * SEQ, FF), BF16), pltpu.VMEM(*KEPT[10])]
        + [pltpu.VMEM((2 * SEQ, D), BF16)] * 2
        + [pltpu.VMEM(*a) for a in KEPT[13:16]]
        + FORWARD_WORK
        + BACKWARD_WORK[0:1]
        + BACKWARD_WORK[2:6]
        + [pltpu.VMEM((2 * SEQ, 768), BF16)]
        + [
            PROJ_WORK,
            pltpu.VMEM((2 * SEQ, FF), BF16),
            ONES_WORK,
            pltpu.VMEM((SEQ, D), F32),
            pltpu.VMEM((2 * SEQ, D), BF16),
            pltpu.VMEM((SEQ, D), F32),
            pltpu.VMEM((KEYS, D), BF16),
            pltpu.VMEM((SEQ, D), BF16),
            pltpu.VMEM((SEQ, 128), F32),
            pltpu.VMEM((2 * SEQ, D), BF16),
            pltpu.VMEM((SEQ, VOCAB), F32),
            pltpu.VMEM((2 * SEQ, VOCAB + 128), BF16),
            pltpu.VMEM((SIDE_ROWS, SEQ), BF16),
            pltpu.VMEM((SEQ, SIDE_ROWS), BF16),
            pltpu.VMEM((2 * SEQ, D), BF16),
        ],
        15 * 10**9,
        20 * 10**6,
        "middle",
    )(
        *in_hbm([meta, frame_meta, vectors, up_bias, other_bias]),
        side_copy,
        stream,
        *resident(second_parts),
    )
    second_sums = add_cores(keep_second, send_second, wide, n_high)

    def joined(a):
        return a.reshape((count * a.shape[1],) + a.shape[2:])

    kept_ff = (kept[8], kept[13], kept[9], kept[10], kept[12])
    grad_mid, keep_ff, send_ff, small_grads = call(
        functools.partial(ff_backward_kernel, fast),
        (count,),
        [full_spec(vectors), w_ff_spec, row_spec((SEQ, D)), small_spec]
        + [row_spec(a.shape[1:]) for a in kept_ff],
        [row_spec((SEQ, D))] + [blocks(HALF_GRAD_COLS)] * 2 + [small_spec],
        [row_f32] + block_shapes(HALF_GRAD_COLS) + [small_shape],
        [
            pltpu.VMEM((D, 2048), F32),
            small_scratch,
            pltpu.VMEM((SEQ, D), BF16),
            pltpu.VMEM((SEQ, FF), BF16),
            ONES_WORK,
            pltpu.VMEM((SEQ, FF), F32),
            pltpu.VMEM((SEQ, D), F32),
        ],
        4 * 10**9,
        10 * 10**6,
        "ff_backward",
    )(*in_hbm([vectors]), w_ff, grad_stream, small_grads, *kept_ff)
    ff_sums = add_cores(keep_ff, send_ff, wide, n_high)
    other_sums = [jnp.concatenate(pair, axis=-1) for pair in zip(second_sums, ff_sums)]
    others_received = swap_plane(other_sums)
    kept_attention = (kept[14], kept[15]) + tuple(kept[0:7])
    joined_attention = [joined(kept[7]), joined(kept[11]), joined(hits)]
    keep_rest, send_rest, small_grads = call(
        functools.partial(attention_backward_kernel, fast),
        (count,),
        [full_spec(vectors), w_attention_spec, row_spec((SEQ, D)), small_spec]
        + [row_spec(a.shape[1:]) for a in kept_attention]
        + [VMEM_SPEC] * 3
        + [ANY_SPEC],
        [blocks(HALF_GRAD_COLS)] * 2 + [pl.BlockSpec((SMALL_ROWS, D), lambda i: (0, 0))],
        block_shapes(HALF_GRAD_COLS) + [shaped((SMALL_ROWS, D), F32)],
        [pltpu.VMEM((D, 2048), F32), small_scratch, pltpu.VMEM((KEYS, D), BF16)]
        + [pltpu.VMEM((count * SEQ, D), BF16)] * 2
        + [pltpu.VMEM((count * SEQ, 768), BF16)]
        + BACKWARD_WORK[0:6]
        + [PROJ_WORK, pltpu.VMEM((SEQ, D), F32)],
        6 * 10**9,
        20 * 10**6,
        "attention_backward",
    )(
        *in_hbm([vectors]),
        w_attention,
        grad_mid,
        small_grads,
        *kept_attention,
        *joined_attention,
        other_sums[0],
    )
    others_received, keep_rest = lax.optimization_barrier((others_received, keep_rest))
    rest_sums = add_cores(keep_rest, send_rest, wide, n_high)
    rest_received = swap_plane(rest_sums)
    other_pieces = column_pieces(add_plane(other_sums[0], others_received))
    rest_pieces = column_pieces(add_plane(rest_sums[0], rest_received))

    grad_rest, grad_others, table_part, small = call(
        functools.partial(finish_kernel, fast),
        None,
        [VMEM_SPEC] * (2 * n_high + 1),
        [VMEM_SPEC] * 4,
        [
            shaped((rows, HALF_GRAD_COLS), F32),
            shaped((rows, HALF_GRAD_COLS + HALF_SECOND_COLS), F32),
            shaped((rows, 512), F32),
            shaped((4 * n_high, 8, 128), F32),
        ],
        [],
        10**6,
        10**6,
        "finish",
    )(*resident(rest_pieces + other_pieces), scalars)

    gathered = lax.all_to_all(small, "wide", 0, 0)
    beside = swap(gathered, "narrow", 1)
    quarters = []
    if not fast:
        total = lax.psum(small_grads, ("wide", "narrow"))
        quarters = [total.reshape(4, 8, 2, 128).transpose(0, 2, 1, 3).reshape(4, 16, 128)]
    swapped = swap(table_part, "narrow", 1)

    flat_params = [a for group in params for a in group]
    results = call(
        functools.partial(adam_kernel, fast),
        None,
        [VMEM_SPEC] * (32 + len(quarters)),
        [VMEM_SPEC] * 30,
        [shaped((1, 1), F32)] * 3 + [shaped(a.shape, F32) for a in flat_params],
        [pltpu.VMEM((SMALL_ROWS, D), F32)],
        10**6,
        10**6,
        "adam",
    )(grad_rest, grad_others, *resident([swapped, gathered, beside]), *quarters, *flat_params)
    news = list(results[3:])
    for group in (0, 2, 5, 8):
        for member in range(3 * group, 3 * group + 3):
            news[member] = flat(news[member])
    return tuple(a.reshape(()) for a in results[0:3]) + tuple(news)


def solution(mesh):
    placed = (
        P("wide", None, None),
        P("wide", None),
        P("wide"),
        P("wide", None),
        P("wide", None),
        P("wide", None),
        P(None, "wide"),
        P(None, "wide"),
        P(None, "wide"),
        P(None, None, "wide", "narrow"),
        P(None, None, "wide", "narrow"),
        P(None, None, "wide", "narrow"),
        P(None, "narrow", "wide"),
        P(None, "narrow", "wide"),
        P(None, "narrow", "wide"),
        P(None, "wide", "narrow"),
        P(None, "wide", "narrow"),
        P(None, "wide", "narrow"),
        P(None, "narrow"),
        P(None, "narrow"),
        P(None, "narrow"),
        P(None, "narrow", "wide"),
        P(None, "narrow", "wide"),
        P(None, "narrow", "wide"),
        P(),
        P(),
        P(),
        P("wide", "narrow"),
        P("wide", "narrow"),
        P("wide", "narrow"),
        P("wide", None),
        P("wide", None),
        P("wide", None),
    )
    return jax.shard_map(
        per_device,
        mesh=mesh,
        in_specs=placed,
        out_specs=(P(), P(), P()) + placed[6:],
        check_vma=False,
    )
```

```python
import functools

import jax
import jax.numpy as jnp
from jax import lax
from jax.experimental import pallas as pl
from jax.experimental.pallas import tpu as pltpu
from jax.sharding import PartitionSpec as P

D = 256
HEADS = 4
HEAD_DIM = 64
FF = 1024
VOCAB = 512
ACTIONS = 18
GAMES = 26
OBS = 16
FRAMES = 20
STEP_NUMBER = 5
FRAME_TOKENS = 17
LENGTH = 340
ROWS = 896
NVEC = 14

EPS_NORM = 1e-05
BETA_ONE = 0.5
BETA_TWO = 0.5
RATE_TABLE = 0.5
RATE_MATRIX = 0.05
RATE_VECTOR = 0.2
DECAY_RATE = 0.01
EPS_ADAM = 1e-08
CLIP_AT = 0.1

SEQ = 352
KEYS = 384
BLOCK, BLOCKS = 128, 3
TILE = 32
SIDE_ROWS = 32
QUERIES = HEADS * BLOCK
VALUE_ROWS = 80

COL_QKV, COL_PROJ, COL_UP, COL_DOWN, COL_LAYER = 0, 768, 1024, 2048, 3072
HALF_ATTENTION = ((0, 128, 0), (128, 128, 256), (256, 128, 512), (384, 128, COL_PROJ))
HALF_LAYER = HALF_ATTENTION + ((512, 512, COL_UP), (1024, 512, COL_DOWN))
COL_TABLE, COL_SMALL, COL_FIRST = 3072, 3968, 4096
HALF_FIRST = HALF_LAYER + ((1536, 512, COL_TABLE),)
HALF_FIRST_COLS = 2048
COL_HEAD, COL_SECOND = 3072, 3584
HALF_SECOND = HALF_LAYER + ((1536, 256, COL_HEAD),)
HALF_SECOND_COLS = 1792
GRAD_UP, GRAD_DOWN = 0, 1024
HALF_GRAD_FF = ((0, 512, GRAD_UP), (512, 512, GRAD_DOWN))
GRAD_TABLE, GRAD_SMALL = 1024, 1920
HALF_GRAD_REST = HALF_ATTENTION + ((512, 512, GRAD_TABLE),)
HALF_GRAD_COLS = 1024
SMALL_ROWS, SMALL_BIAS, SMALL_SIDE = 32, 14, 22

F32, BF16 = jnp.float32, jnp.bfloat16
MIB = 1024 * 1024


def dot_nn(a, b):
    return lax.dot_general(a, b, (((1,), (0,)), ((), ())), preferred_element_type=F32)


def dot_nt(a, b):
    return lax.dot_general(a, b, (((1,), (1,)), ((), ())), preferred_element_type=F32)


def dot_tn(a, b):
    return lax.dot_general(a, b, (((0,), (0,)), ((), ())), preferred_element_type=F32)


def places(fast):
    wide, core = lax.axis_index("wide"), lax.axis_index("narrow")
    return (wide if fast else 0), core, wide


def tiles(rows, size):
    return [slice(first, first + size) for first in range(0, rows, size)]


def normalise(x):
    centred = x - jnp.mean(x, axis=1, keepdims=True)
    scale = lax.rsqrt(jnp.mean(centred * centred, axis=1, keepdims=True) + EPS_NORM)
    return centred * scale, scale


def keep_norm(rows, xhat, scale, kept):
    kept[0][rows] = xhat.astype(BF16)
    kept[1][rows] = jnp.broadcast_to(scale, (TILE, 128))


def kept_norm(rows, kept):
    scale = kept[1][rows]
    return kept[0][rows].astype(F32), jnp.concatenate([scale, scale], axis=1)


def normalise_back(grad, xhat, scale, gain):
    inner = grad * gain
    mean_one = jnp.mean(inner, axis=1, keepdims=True)
    mean_two = jnp.mean(inner * xhat, axis=1, keepdims=True)
    return scale * (inner - mean_one - xhat * mean_two)


def column_sum(a):
    return jnp.sum(a, axis=0, keepdims=True)


def fold(a):
    return jnp.sum(a.reshape(a.shape[0] // 8, 8, a.shape[1]), axis=0)


def plus(total, a):
    return a if total is None else total + a


def block_lanes(i, h=None):
    if h is None:
        return slice(QUERIES * i, QUERIES * (i + 1))
    return slice(QUERIES * i + BLOCK * h, QUERIES * i + BLOCK * (h + 1))


def head_rows(h):
    return slice(HEAD_DIM * h, HEAD_DIM * (h + 1))


def spread_heads(source, target_ref):
    for h in range(HEADS):
        for i in range(BLOCKS):
            target_ref[head_rows(h), block_lanes(i, h)] = source[
                head_rows(h), BLOCK * i : BLOCK * (i + 1)
            ]


def causal_mask():
    key = lax.broadcasted_iota(jnp.int32, (BLOCK, QUERIES), 0)
    query = lax.broadcasted_iota(jnp.int32, (BLOCK, QUERIES), 1) & (BLOCK - 1)
    return jnp.where(key <= query, 0.0, -1e30)


def assemble(pieces_mine, pieces_other, place, w_ref, halves):
    me, core, _ = place
    is_first = core == 0
    for p in range(4):

        def block(z, _, p=p):
            row = pl.multiple_of((me ^ (4 * z + p)) * 16, 16)
            for src, width, dest in halves:
                mine = pieces_mine[p][z, :, src : src + width]
                other = pieces_other[p][z, :, src : src + width]
                if dest == COL_QKV:
                    mine, other = mine * 0.125, other * 0.125
                w_ref[pl.ds(row, 16), dest : dest + width] = jnp.where(is_first, mine, other)
                w_ref[pl.ds(row, 16), dest + width : dest + 2 * width] = jnp.where(
                    is_first, other, mine
                )
            return 0

        lax.fori_loop(0, 4, block, 0)


def disperse(g_ref, place, keep_ref, send_ref, halves, scaled=True):
    me, core, _ = place
    is_first = core == 0

    def block(i, _):
        p, z = i >> 2, i & 3
        row = pl.multiple_of((me ^ (4 * z + p)) * 16, 16)
        for src, width, dest in halves:
            low = g_ref[pl.ds(row, 16), dest : dest + width]
            high = g_ref[pl.ds(row, 16), dest + width : dest + 2 * width]
            if scaled and dest == COL_QKV:
                low, high = low * 0.125, high * 0.125
            keep_ref[p, z, :, src : src + width] = jnp.where(is_first, low, high).astype(BF16)
            send_ref[p, z, :, src : src + width] = jnp.where(is_first, high, low).astype(BF16)
        return 0

    lax.fori_loop(0, 16, block, 0)


def make_hits(ids, game, hits_ref):
    lane = lax.broadcasted_iota(jnp.int32, (TILE, ROWS), 1)
    for rows in tiles(SEQ, TILE):
        place = lax.broadcasted_iota(jnp.int32, (TILE, 1), 0) + (VOCAB + ACTIONS + GAMES + rows.start)
        hit = (lane == ids[rows]) | (lane == game[rows]) | (lane == place)
        hits_ref[rows] = jnp.where(hit, 1.0, 0.0).astype(BF16)


def gelu_and_slope(up):
    up = up.astype(BF16)
    square = up * up
    half = jax.nn.sigmoid(up * (BF16(1.5957691216057308) + BF16(0.0713548162726) * square))
    hidden = up * half
    slope = BF16(1.5957691216057308) + BF16(0.2140644488178) * square
    return hidden, half + hidden * (BF16(1.0) - half) * slope


def layer_forward(x_ref, w_ref, vec, bias, kept, work):
    qt_ref, kv_ref, p0, p1, p2, r_ref, ot_ref, o_ref = kept[0:8]
    h_ref, gp_ref, a_ref, c_ref = kept[9:13]
    qst_ref, vt_ref, mask_ref, wqt_ref, long_ref, u_ref, y_ref, m_ref = work
    for rows in tiles(SEQ, TILE):
        xhat, scale = normalise(x_ref[rows])
        keep_norm(rows, xhat, scale, kept[14:16])
        normed16 = (xhat * vec[0:1] + vec[1:2]).astype(BF16)
        a_ref[rows], long_ref[rows] = normed16, normed16
    kv_ref[0:SEQ] = dot_nn(long_ref[0:SEQ], w_ref[:, 256:768]).astype(BF16)
    kv_ref[SEQ:KEYS] = jnp.zeros((KEYS - SEQ, 512), BF16)
    qt_ref[...] = dot_nt(wqt_ref[...], long_ref[...]).astype(BF16)
    spread_heads(qt_ref, qst_ref)
    turned = jnp.transpose(kv_ref[:, 256:512])
    for h in range(HEADS):
        vt_ref[VALUE_ROWS * h : VALUE_ROWS * h + HEAD_DIM] = turned[head_rows(h)]
    for i, pt_ref in enumerate((p0, p1, p2)):
        seen, first = BLOCK * (i + 1), BLOCK * i
        scores = dot_nn(kv_ref[0:seen, 0:256], qst_ref[:, block_lanes(i)])
        last = scores[first:] + mask_ref[...]
        peak = jnp.max(last, axis=0, keepdims=True)
        if i:
            peak = jnp.maximum(peak, jnp.max(scores[0:first], axis=0, keepdims=True))
            pt_ref[0:first] = jnp.exp(scores[0:first] - peak).astype(BF16)
        pt_ref[first:seen] = jnp.exp(last - peak).astype(BF16)
        for h in range(HEADS):
            values = vt_ref[VALUE_ROWS * h : VALUE_ROWS * (h + 1), 0:seen]
            out = dot_nn(values, pt_ref[:, BLOCK * h : BLOCK * (h + 1)])
            inverse = 1.0 / out[HEAD_DIM : HEAD_DIM + 1]
            r_ref[h : h + 1, first:seen] = inverse
            ot_ref[head_rows(h), first:seen] = (out[0:HEAD_DIM] * inverse).astype(BF16)
    o_ref[...] = jnp.transpose(ot_ref[...])[0:SEQ]
    y_ref[...] = dot_nt(o_ref[...], w_ref[:, COL_PROJ : COL_PROJ + 256])
    for rows in tiles(SEQ, TILE):
        middle = x_ref[rows] + (y_ref[rows] + vec[2:3])
        m_ref[rows] = middle
        xhat, scale = normalise(middle)
        keep_norm(rows, xhat, scale, (kept[8], kept[13]))
        c_ref[rows] = (xhat * vec[3:4] + vec[4:5]).astype(BF16)
    u_ref[...] = dot_nn(c_ref[...], w_ref[:, COL_UP : COL_UP + FF])
    for rows in tiles(SEQ, TILE):
        for first in range(0, FF, 256):
            cols = slice(first, first + 256)
            h_ref[rows, cols], gp_ref[rows, cols] = gelu_and_slope(u_ref[rows, cols] + bias[:, cols])
    y_ref[...] = dot_nt(h_ref[...], w_ref[:, COL_DOWN : COL_DOWN + FF])


def add_gradient(g_ref, column, left, right):
    g_ref[:, column : column + right.shape[1]] += dot_tn(left, right)


def ff_backward(grad_ref, grad16_ref, w_ref, w_up, w_down, vec, kept, v_ref, v_row, bias_row, work, mid_ref, mid16_refs):
    norm_kept, gp_ref = kept
    du_ref, ones_ref, u_ref, y_ref = work
    u_ref[...] = dot_nn(grad16_ref[...], w_ref[:, w_down : w_down + FF])
    for rows in tiles(SEQ, TILE):
        du_ref[rows] = u_ref[rows].astype(BF16) * gp_ref[rows]
    bias_grad = dot_nn(ones_ref[...], du_ref[...])
    for chunk in range(4):
        v_ref[bias_row + chunk, 0:1] += bias_grad[0:1, 256 * chunk : 256 * chunk + 256]
    y_ref[...] = dot_nt(du_ref[...], w_ref[:, w_up : w_up + FF])
    totals = [None] * 3
    for rows in tiles(SEQ, TILE):
        xhat, scale = kept_norm(rows, norm_kept)
        grad = y_ref[rows]
        mid = grad_ref[rows] + normalise_back(grad, xhat, scale, vec[3:4])
        mid_ref[rows] = mid
        for mid16_ref in mid16_refs:
            mid16_ref[rows] = mid.astype(BF16)
        for i, a in enumerate((mid, grad * xhat, grad)):
            totals[i] = plus(totals[i], fold(a))
    for i in range(3):
        v_ref[v_row + 2 + i] += totals[i]


def attention_backward(mid_ref, mid16_ref, w_ref, vec, kept, v_ref, v_row, work, out_ref):
    norm_kept, (qt_ref, kv_ref, p0, p1, p2, r_ref, ot_ref) = kept
    dost_ref, qst_ref, kt_ref, dst_ref, dqt_ref, dkv_ref, dqkv_ref, proj_ref, y_ref = work
    grad_o = dot_nt(proj_ref[...], mid16_ref[...])
    kt_ref[...] = jnp.transpose(kv_ref[:, 0:256])
    deltas = []
    for h in range(HEADS):
        scaled = grad_o[head_rows(h)] * r_ref[h : h + 1]
        deltas.append(column_sum(scaled * ot_ref[head_rows(h)].astype(F32)))
        scaled = scaled.astype(BF16)
        for i in range(BLOCKS):
            dost_ref[head_rows(h), block_lanes(i, h)] = scaled[:, BLOCK * i : BLOCK * (i + 1)]
    for i, pt_ref in enumerate((p0, p1, p2)):
        seen, first = BLOCK * (i + 1), BLOCK * i
        lanes = block_lanes(i)
        delta = jnp.concatenate([a[:, first:seen] for a in deltas], axis=1)
        grad = dot_nn(kv_ref[0:seen, 256:512], dost_ref[:, lanes])
        dst_ref[0:seen, lanes] = pt_ref[...] * (grad - delta).astype(BF16)
        for h in range(HEADS):
            out = dot_nn(kt_ref[head_rows(h), 0:seen], dst_ref[0:seen, block_lanes(i, h)])
            dqt_ref[head_rows(h), first:seen] = out.astype(BF16)
        for at, left, right in (
            (0, dst_ref[0:seen, lanes], qst_ref),
            (256, pt_ref[...], dost_ref),
        ):
            out = dot_nt(left, right[:, lanes])
            if i:
                dkv_ref[0:first, at : at + 256] += out[0:first]
            dkv_ref[first:seen, at : at + 256] = out[first:]
    dqkv_ref[:, 0:256] = jnp.transpose(dqt_ref[...])[0:SEQ]
    dqkv_ref[:, 256:768] = dkv_ref[0:SEQ].astype(BF16)
    y_ref[...] = dot_nt(dqkv_ref[...], w_ref[:, COL_QKV : COL_QKV + 768])
    totals = [None] * 2
    for rows in tiles(SEQ, TILE):
        xhat, scale = kept_norm(rows, norm_kept)
        grad = y_ref[rows]
        out = mid_ref[rows] + normalise_back(grad, xhat, scale, vec[0:1])
        out_ref[rows] = out.astype(out_ref.dtype)
        for i, a in enumerate((grad * xhat, grad)):
            totals[i] = plus(totals[i], fold(a))
    for i in range(2):
        v_ref[v_row + i] += totals[i]


def own_bias(place, mine, other):
    is_first = place[1] == 0
    return jnp.concatenate(
        [jnp.where(is_first, mine, other), jnp.where(is_first, other, mine)], axis=1
    )


def prepare_kernel(
    fast, games_ref, tokens, actions, valid, rewards, ends, out, out_side, out_hits, x_ref
):
    count = out.shape[0]
    frames = tokens.shape[2]
    base = places(fast)[1] * count
    row = lax.broadcasted_iota(jnp.int32, (SEQ, frames), 0)
    start = lax.broadcasted_iota(jnp.int32, (SEQ, frames), 1) * FRAME_TOKENS
    here = jnp.where((row >= start) & (row < start + FRAME_TOKENS), 1.0, 0.0).astype(BF16)
    coming = jnp.where((row >= start - FRAME_TOKENS) & (row < start), 1.0, 0.0).astype(BF16)
    passed = jnp.sum(jnp.where(row >= start + FRAME_TOKENS, 1, 0), axis=1, keepdims=True)
    place = lax.broadcasted_iota(jnp.int32, (SEQ, 1), 0)
    spot = place - passed * FRAME_TOKENS
    lane = lax.broadcasted_iota(jnp.int32, (SEQ, 24), 1)
    wide_lane = lax.broadcasted_iota(jnp.int32, (SEQ, 128), 1)
    inside = place < LENGTH
    one_frame = (
        lax.broadcasted_iota(jnp.int32, (SIDE_ROWS, frames), 0)
        == lax.broadcasted_iota(jnp.int32, (SIDE_ROWS, frames), 1)
    )
    one_frame = jnp.where(one_frame, 1.0, 0.0).astype(BF16)
    side_lane = lax.broadcasted_iota(jnp.int32, (SIDE_ROWS, 128), 1)
    x_ref[...] = jnp.zeros(x_ref.shape, jnp.int32)
    for s in range(count):
        x_ref[0:OBS] = tokens[base + s]
        x_ref[16:17] = actions[pl.ds(base + s, 1)] + VOCAB
        x_ref[17:18] = valid[pl.ds(base + s, 1)]
        x_ref[18:19] = rewards[pl.ds(base + s, 1)]
        x_ref[19:20] = ends[pl.ds(base + s, 1)] + 3
        high = (x_ref[...] >> 4).astype(F32).astype(BF16)
        low = (x_ref[...] & 15).astype(F32).astype(BF16)
        now = dot_nt(here, high) * 16.0 + dot_nt(here, low)
        soon = dot_nt(coming, high) * 16.0 + dot_nt(coming, low)

        at_end = spot == 16
        packed = jnp.where(lane == spot, now, 0.0)
        target = jnp.where((lane == spot + 1) & (spot < 15), now, 0.0)
        target = target + jnp.where((lane == 0) & at_end, soon, 0.0)
        weight = jnp.where((lane == 17) & (spot < 15), now, 0.0)
        weight = weight + jnp.where((lane == 17) & at_end, soon, 0.0)
        packed = packed + 1024.0 * target + 1048576.0 * weight
        packed = jnp.sum(packed, axis=1, keepdims=True).astype(jnp.int32)
        ids = jnp.where(inside, packed & 1023, -1)
        game = jnp.where(inside, games_ref[base + s] + (VOCAB + ACTIONS), -1)
        target, weight = (packed >> 10) & 1023, packed >> 20
        out[s] = jnp.where(wide_lane == 2, target, jnp.where(wide_lane == 3, weight, 0))
        make_hits(ids, game, out_hits.at[s])
        by_frame = dot_nt(one_frame, high) * 16.0 + dot_nt(one_frame, low)
        result = jnp.zeros((SIDE_ROWS, 128), jnp.int32)
        for c in range(3):
            column = by_frame[:, 17 + c : 18 + c].astype(jnp.int32)
            result = jnp.where(side_lane == c, column, result)
        out_side[s] = result


def start_forward(work, w_ref):
    qst_ref, vt_ref, mask_ref, wqt_ref, long_ref = work[0:5]
    long_ref[SEQ:KEYS] = jnp.zeros((KEYS - SEQ, D), BF16)
    qst_ref[...] = jnp.zeros(qst_ref.shape, BF16)
    vt_ref[...] = jnp.ones(vt_ref.shape, BF16)
    mask_ref[...] = causal_mask()
    wqt_ref[...] = jnp.transpose(w_ref[:, 0:256])


def first_forward_kernel(fast, *refs):
    refs = (places(fast),) + refs
    place, hits_ref, vec_ref, bias_ref, bias_other = refs[0:5]
    mine, other = refs[5:9], refs[9:13]
    w_attention, w_ff, side_out, next_ref = refs[13:17]
    kept = [ref.at[0] for ref in refs[17:33]]
    w_ref, x_ref = refs[33:35]
    work = refs[35:43]
    y_ref, m_ref = work[6:8]

    @pl.when(pl.program_id(0) == 0)
    def _():
        assemble(mine, other, place, w_ref, HALF_FIRST)
        w_attention[...] = w_ref[:, 0:COL_UP]
        w_ff[...] = w_ref[:, COL_UP:COL_TABLE]
        side_out[...] = w_ref[:, COL_SMALL:]
        start_forward(work, w_ref)

    x_ref[...] = dot_nt(hits_ref[0], w_ref[:, COL_TABLE : COL_TABLE + ROWS])
    bias = own_bias(place, bias_ref[0:1], bias_other[0:1])
    vec = vec_ref[0:6]
    layer_forward(x_ref, w_ref, vec, bias, kept, work)
    for rows in tiles(SEQ, TILE):
        next_ref[0, rows] = m_ref[rows] + (y_ref[rows] + vec[5:6])


def codebook_losses(logits, meta):
    weight = meta[:, 3:4].astype(F32)
    peak = jnp.max(logits, axis=1, keepdims=True)
    expanded = jnp.exp(logits - peak)
    total = jnp.sum(expanded, axis=1, keepdims=True)
    hit = lax.broadcasted_iota(jnp.int32, logits.shape, 1) == meta[:, 2:3]
    hit = jnp.where(hit, weight, 0.0)
    return weight * (peak + jnp.log(total)), hit, expanded * (weight / total) - hit


def side_losses(side, meta):
    lane = lax.broadcasted_iota(jnp.int32, side.shape, 1)
    is_reward, is_end = lane < 3, (lane == 3) | (lane == 4)
    is_side = lane < 5
    weight = meta[:, 0:1].astype(F32)
    reward_peak = jnp.max(jnp.where(is_reward, side, -1e30), axis=1, keepdims=True)
    end_peak = jnp.max(jnp.where(is_end, side, -1e30), axis=1, keepdims=True)
    shifted = jnp.where(is_side, side - jnp.where(is_reward, reward_peak, end_peak), 0.0)
    expanded = jnp.where(is_side, jnp.exp(shifted), 0.0)
    reward_total = jnp.sum(jnp.where(is_reward, expanded, 0.0), axis=1, keepdims=True)
    end_total = jnp.sum(jnp.where(is_end, expanded, 0.0), axis=1, keepdims=True)
    hit = (lane == meta[:, 1:2]) | (lane == meta[:, 2:3])
    picked = jnp.sum(jnp.where(hit, side, 0.0), axis=1, keepdims=True)
    terms = reward_peak + jnp.log(reward_total) + end_peak + jnp.log(end_total) - picked
    grad = expanded * jnp.where(is_reward, weight / reward_total, weight / end_total)
    return weight * terms, grad - jnp.where(hit, weight, 0.0), weight


def frame_ends(shape, frame_axis):
    frame = lax.broadcasted_iota(jnp.int32, shape, frame_axis)
    row = lax.broadcasted_iota(jnp.int32, shape, 1 - frame_axis)
    hit = (row == frame * FRAME_TOKENS + OBS) & (frame < FRAMES)
    return jnp.where(hit, 1.0, 0.0).astype(BF16)


def middle_kernel(fast, *refs):
    refs = (places(fast),) + refs
    place, meta_ref, frame_ref, vec_ref, bias_ref, bias_other, side_ref, in_ref = refs[0:8]
    mine, other = refs[8:12], refs[12:16]
    grad_ref, keep_ref, send_ref, v_out, scalar_ref = refs[16:21]
    refs = refs[1:]
    w_ref, g_ref, v_ref = refs[20:23]
    kept = list(refs[23:39])
    forward_work = refs[39:47]
    u_ref, y_ref, m_ref = forward_work[5:8]
    backward_work = list(refs[47:53])
    proj_ref = refs[53]
    du_all, ones_ref, up_ref, up16_all, mid_ref, mid16_ref = refs[54:60]
    last_kept = refs[60:62]
    final_all, logit_ref, dlogit_all, pick_ref, put_ref, mid16_all = refs[62:68]
    o_all, h_all, a_all, c_all, dqkv_all = kept[7], kept[9], kept[11], kept[12], backward_work[5]
    dost_ref = backward_work[0]
    step = pl.program_id(0)

    @pl.when(step == 0)
    def _():
        assemble(mine, other, place, w_ref, HALF_SECOND)
        w_ref[:, COL_SECOND:] = side_ref[...]
        g_ref[...] = jnp.zeros(g_ref.shape, F32)
        v_ref[...] = jnp.zeros(v_ref.shape, F32)
        scalar_ref[...] = jnp.zeros(scalar_ref.shape, F32)
        start_forward(forward_work, w_ref)
        dost_ref[...] = jnp.zeros(dost_ref.shape, BF16)
        proj_ref[...] = jnp.transpose(w_ref[:, COL_PROJ : COL_PROJ + 256])
        ones_ref[...] = jnp.ones(ones_ref.shape, BF16)
        mid16_ref[SEQ:KEYS] = jnp.zeros((KEYS - SEQ, D), BF16)
        pick_ref[...] = frame_ends((SIDE_ROWS, SEQ), 0)
        put_ref[...] = frame_ends((SEQ, SIDE_ROWS), 1)

    here = pl.ds(pl.multiple_of((step & 1) * SEQ, 32), SEQ)
    for i in (7, 9, 11, 12):
        kept[i] = kept[i].at[here]
    gp_ref = kept[10]
    backward_work[5] = dqkv_all.at[here]
    du_ref, up16_ref, pair16_ref = du_all.at[here], up16_all.at[here], mid16_all.at[here]
    final_ref, dlogit_ref = final_all.at[here], dlogit_all.at[here]
    x_ref = in_ref.at[0]
    vec = vec_ref[6:12]
    bias = own_bias(place, bias_ref[1:2], bias_other[1:2])
    layer_forward(x_ref, w_ref, vec, bias, kept, forward_work)

    gain, offset = vec_ref[12:13], vec_ref[13:14]
    for rows in tiles(SEQ, TILE):
        last = m_ref[rows] + (y_ref[rows] + vec[5:6])
        xhat, scale = normalise(last)
        keep_norm(rows, xhat, scale, last_kept)
        final_ref[rows] = (xhat * gain + offset).astype(BF16)
    cols_head = slice(COL_HEAD, COL_HEAD + VOCAB + 128)
    logit_ref[...] = dot_nn(final_ref[...], w_ref[:, COL_HEAD : COL_HEAD + VOCAB])
    logs, picked = None, None
    for rows in tiles(SEQ, TILE):
        logits = logit_ref[rows]
        log, hit, grad = codebook_losses(logits, meta_ref[0, rows])
        dlogit_ref[rows, :VOCAB] = grad.astype(BF16)
        logs, picked = plus(logs, log), plus(picked, fold(hit * logits))
    acting = dot_nn(pick_ref[...], final_ref[...]).astype(BF16)
    side = dot_nn(acting, w_ref[:, COL_HEAD + VOCAB : COL_HEAD + VOCAB + 128])
    side_loss, grad, weight = side_losses(side, frame_ref[0])
    dlogit_ref[:, VOCAB:] = dot_nn(put_ref[...], grad.astype(BF16)).astype(BF16)
    loss = column_sum(logs) + column_sum(side_loss)
    loss = loss - jnp.sum(column_sum(picked), axis=1, keepdims=True)
    valid = column_sum(weight)
    scalar_lane = lax.broadcasted_iota(jnp.int32, (8, 128), 1)
    scalar_row = lax.broadcasted_iota(jnp.int32, (8, 128), 0) == 0
    scalar_ref[...] += jnp.where(
        scalar_row,
        jnp.where(scalar_lane == 0, loss, jnp.where(scalar_lane == 1, valid, 0.0)),
        0.0,
    )
    y_ref[...] = dot_nt(dlogit_ref[...], w_ref[:, cols_head])
    totals = [None] * 3
    for rows in tiles(SEQ, TILE):
        xhat, scale = kept_norm(rows, last_kept)
        grad = y_ref[rows]
        up = normalise_back(grad, xhat, scale, gain)
        up_ref[rows] = up
        up16_ref[rows] = up.astype(BF16)
        for i, a in enumerate((up, grad * xhat, grad)):
            totals[i] = plus(totals[i], fold(a))
    for i in range(3):
        v_ref[11 + i] += totals[i]
    ff_backward(
        up_ref,
        up16_ref,
        w_ref,
        COL_UP,
        COL_DOWN,
        vec,
        ((kept[8], kept[13]), gp_ref),
        v_ref,
        6,
        SMALL_BIAS + 4,
        (du_ref, ones_ref, u_ref, y_ref),
        mid_ref,
        (mid16_ref, pair16_ref),
    )
    attention_backward(
        mid_ref,
        mid16_ref,
        w_ref,
        vec,
        (kept[14:16], kept[0:7]),
        v_ref,
        6,
        (dost_ref, forward_work[0]) + tuple(backward_work[1:]) + (proj_ref, y_ref),
        grad_ref.at[0],
    )

    @pl.when(step & 1 == 1)
    def _():
        add_gradient(g_ref, COL_QKV, a_all[...], dqkv_all[...])
        add_gradient(g_ref, COL_PROJ, mid16_all[...], o_all[...])
        add_gradient(g_ref, COL_UP, c_all[...], du_all[...])
        add_gradient(g_ref, COL_DOWN, up16_all[...], h_all[...])
        add_gradient(g_ref, COL_HEAD, final_all[...], dlogit_all[...])

    @pl.when(step == pl.num_programs(0) - 1)
    def _():
        disperse(g_ref, place, keep_ref, send_ref, HALF_SECOND)
        side = jnp.transpose(g_ref[:, COL_SECOND:])
        for i in range(5):
            v_ref[SMALL_SIDE + i, 0:1] = side[i : i + 1]
        v_out[...] = v_ref[...]


def ff_backward_kernel(fast, *refs):
    vec_ref, w_ref, grad_ref, v_in = refs[0:4]
    xhat_ref, scale_ref, h_ref, gp_ref, c_ref = [ref.at[0] for ref in refs[4:9]]
    mid_ref, keep_ref, send_ref, v_out = refs[9:13]
    g_ref, v_ref, grad16_ref, du_ref, ones_ref, u_ref, y_ref = refs[13:20]
    step = pl.program_id(0)

    @pl.when(step == 0)
    def _():
        g_ref[...] = jnp.zeros(g_ref.shape, F32)
        v_ref[...] = v_in[...]
        ones_ref[...] = jnp.ones(ones_ref.shape, BF16)

    total = None
    for rows in tiles(SEQ, TILE):
        grad = grad_ref[0, rows]
        grad16_ref[rows] = grad.astype(BF16)
        total = plus(total, fold(grad))
    v_ref[5] += total
    ff_backward(
        grad_ref.at[0],
        grad16_ref,
        w_ref,
        GRAD_UP,
        GRAD_DOWN,
        vec_ref[0:6],
        ((xhat_ref, scale_ref), gp_ref),
        v_ref,
        0,
        SMALL_BIAS,
        (du_ref, ones_ref, u_ref, y_ref),
        mid_ref.at[0],
        (),
    )
    add_gradient(g_ref, GRAD_DOWN, grad16_ref[...], h_ref[...])
    add_gradient(g_ref, GRAD_UP, c_ref[...], du_ref[...])

    @pl.when(step == pl.num_programs(0) - 1)
    def _():
        disperse(g_ref, places(fast), keep_ref, send_ref, HALF_GRAD_FF, False)
        v_out[...] = v_ref[...]


def attention_backward_kernel(fast, *refs):
    vec_ref, w_ref, mid_ref, v_in = refs[0:4]
    kept = [ref.at[0] for ref in refs[4:13]]
    o_all, a_all, hits_all = refs[13:16]
    keep_ref, send_ref, v_out = refs[17:20]
    g_ref, v_ref, mid16_ref, mid16_all, out16_all, dqkv_all = refs[20:26]
    work = list(refs[26:34])
    dost_ref, qst_ref, proj_ref = work[0], work[1], work[6]
    step = pl.program_id(0)

    @pl.when(step == 0)
    def _():
        v_ref[...] = v_in[...]
        dost_ref[...] = jnp.zeros(dost_ref.shape, BF16)
        qst_ref[...] = jnp.zeros(qst_ref.shape, BF16)
        proj_ref[...] = jnp.transpose(w_ref[:, COL_PROJ : COL_PROJ + 256])
        mid16_ref[SEQ:KEYS] = jnp.zeros((KEYS - SEQ, D), BF16)

    here = pl.ds(pl.multiple_of(step * SEQ, 32), SEQ)
    all16_ref = mid16_all.at[here]
    spread_heads(kept[2], qst_ref)
    for rows in tiles(SEQ, TILE):
        mid16 = mid_ref[0, rows].astype(BF16)
        mid16_ref[rows], all16_ref[rows] = mid16, mid16
    work.insert(6, dqkv_all.at[here])
    attention_backward(
        mid_ref.at[0],
        mid16_ref,
        w_ref,
        vec_ref[0:6],
        (kept[0:2], kept[2:9]),
        v_ref,
        0,
        work,
        out16_all.at[here],
    )

    @pl.when(step == pl.num_programs(0) - 1)
    def _():
        g_ref[:, COL_QKV : COL_QKV + 768] = dot_tn(a_all[...], dqkv_all[...])
        g_ref[:, COL_PROJ : COL_PROJ + 256] = dot_tn(mid16_all[...], o_all[...])
        g_ref[:, GRAD_TABLE : GRAD_TABLE + ROWS] = dot_tn(out16_all[...], hits_all[...])
        small = jnp.sum(v_ref[...], axis=1)
        v_out[...] = small
        for block in range(16):
            quarter = small[8 * (block // 4) : 8 * (block // 4) + 8]
            g_ref[16 * block : 16 * block + 8, GRAD_SMALL:] = quarter[:, 0:128]
            g_ref[16 * block + 8 : 16 * block + 16, GRAD_SMALL:] = quarter[:, 128:256]
        disperse(g_ref, places(fast), keep_ref, send_ref, HALF_GRAD_REST)


def pack_layer(attn, proj, up, down, layer, out):
    for j in range(3):
        out[:, 128 * j : 128 * j + 128] = attn[layer, j].astype(BF16)
    out[:, 384:512] = proj[layer].astype(BF16)
    out[:, 512:1024] = up[layer].astype(BF16)
    out[:, 1024:1536] = down[layer].astype(BF16)


def pack_kernel(fast, table, attn, proj, up, down, head, side, first, second, pad_ref):
    pack_layer(attn, proj, up, down, 0, first)
    pack_layer(attn, proj, up, down, 1, second)
    second[:, 1536:1792] = head[...].astype(BF16)
    rows = side.shape[1]
    eye = (
        lax.broadcasted_iota(jnp.int32, (rows, rows), 0)
        == lax.broadcasted_iota(jnp.int32, (rows, rows), 1)
    )
    eye = jnp.where(eye, 1.0, 0.0).astype(BF16)
    pad_ref[...] = jnp.zeros(pad_ref.shape, F32)
    pad_ref[:, 0:5] = dot_nt(eye, side[...].astype(BF16))
    high = jnp.concatenate([table[:, 512:896], pad_ref[...]], axis=1)
    first[:, 1536:2048] = jnp.where(places(fast)[1] == 0, table[:, 0:512], high).astype(BF16)


def finish_kernel(fast, *refs):
    count = (len(refs) - 5) // 2
    scalar_ref = refs[2 * count]
    out_rest, out_other, out_table, out_small = refs[2 * count + 1 :]
    square = jnp.zeros((1, 1), F32)
    for pieces, out in ((refs[0:count], out_rest), (refs[count : 2 * count], out_other)):
        total = pieces[0][...]
        for piece in pieces[1:]:
            total = total + piece[...].astype(F32)
        out[...] = total
        square = square + column_sum(jnp.sum(total * total, axis=1, keepdims=True))
    small = out_rest[:, 896:1024]
    extra = column_sum(jnp.sum(small * small, axis=1, keepdims=True))
    square = square - jnp.where(places(fast)[1] == 0, 0.0, extra)
    out_table[...] = out_rest[:, 512:1024]
    lane = lax.broadcasted_iota(jnp.int32, (8, 128), 1)
    row = lax.broadcasted_iota(jnp.int32, (8, 128), 0)
    message = scalar_ref[...] + jnp.where((row == 0) & (lane == 2), square, 0.0)
    if fast:
        spot = places(fast)[2] & 3
        part = jnp.where(spot & 1 == 0, small[0:4], small[4:8])
        part = jnp.where(spot & 2 == 0, part, jnp.where(spot & 1 == 0, small[8:12], small[12:16]))
        message = jnp.concatenate([part, message[0:4]], axis=0)
    for i in range(out_small.shape[0]):
        out_small[i] = message


def adam_rule(weight, moment, second, gradient, step_rate, decay_rate):
    moment_new = BETA_ONE * moment + (1.0 - BETA_ONE) * gradient
    second_new = BETA_TWO * second + (1.0 - BETA_TWO) * gradient * gradient
    moment_hat = moment_new / (1.0 - BETA_ONE**STEP_NUMBER)
    second_hat = second_new / (1.0 - BETA_TWO**STEP_NUMBER)
    weight_new = weight - step_rate * (
        moment_hat / (jnp.sqrt(second_hat) + EPS_ADAM) + decay_rate * weight
    )
    return (weight_new, moment_new, second_new)


def adam_kernel(fast, rest, others, swapped, gathered, beside, *refs):
    rows = rest.shape[0]
    _, core, wide = places(fast)
    is_first = core == 0
    if fast:
        small_parts = jnp.where(is_first, beside[...], gathered[...])
        quarters = [
            jnp.concatenate([small_parts[4 * z + p, 0:4] for p in range(4)], axis=0)
            for z in range(4)
        ]
    else:
        quarters = [refs[0][z] for z in range(4)]
        refs = refs[1:]
    params = [refs[3 * i : 3 * i + 3] for i in range(9)]
    loss_ref, valid_ref, norm_ref = refs[27:30]
    outs = [refs[30 + 3 * i : 33 + 3 * i] for i in range(9)]
    small_ref = refs[57]
    for z in range(4):
        small_ref[8 * z : 8 * z + 8, 0:128] = quarters[z][0:8]
        small_ref[8 * z : 8 * z + 8, 128:256] = quarters[z][8:16]
    sums = []
    for source in (gathered, beside):
        line = 4 if fast else 0
        total = source[0, line : line + 1]
        for i in range(1, source.shape[0]):
            total = total + source[i, line : line + 1]
        sums.append(total)
    scalars = sums[0] + sums[1]
    small = small_ref[...]
    loss, valid, square = scalars[:, 0:1], scalars[:, 1:2], scalars[:, 2:3]
    square = square + column_sum(jnp.sum(small * small, axis=1, keepdims=True))
    inverse = 1.0 / valid
    norm = jnp.sqrt(square) * inverse
    loss_ref[...], valid_ref[...], norm_ref[...] = loss, valid, norm
    factor = jnp.minimum(1.0, CLIP_AT / (norm + 1e-06)) * inverse
    table, attn, proj, up, bias, down, vectors, head, side = range(9)

    def update(which, index, gradient, step_rate, decay_rate):
        news = adam_rule(
            *(ref[index] for ref in params[which]), factor * gradient, step_rate, decay_rate
        )
        for ref, new in zip(outs[which], news):
            ref[index] = new

    layers = ((rest, others, 1792), (others, others, 512))
    for layer, (attention, feed, at) in enumerate(layers):
        for j in range(3):
            update(attn, (layer, j), attention[:, 128 * j : 128 * j + 128], RATE_MATRIX, DECAY_RATE)
        update(proj, (layer,), attention[:, 384:512], RATE_MATRIX, DECAY_RATE)
        update(up, (layer,), feed[:, at : at + 512], RATE_MATRIX, DECAY_RATE)
        update(down, (layer,), feed[:, at + 512 : at + 1024], RATE_MATRIX, DECAY_RATE)
        for i in range(2):
            low = SMALL_BIAS + 4 * layer + i
            row = jnp.where(is_first, small[low : low + 1], small[low + 2 : low + 3])
            index = (slice(layer, layer + 1), slice(256 * i, 256 * i + 256))
            update(bias, index, row, RATE_VECTOR, 0.0)
    whole = (slice(None), slice(None))
    update(head, whole, others[:, 1536:1792], RATE_MATRIX, DECAY_RATE)
    mine, theirs = rest[:, 512:1024], swapped[:, 0:512]
    low, high = jnp.where(is_first, mine, theirs), jnp.where(is_first, theirs, mine)
    update(table, (slice(None), slice(0, 512)), low, RATE_TABLE, DECAY_RATE)
    update(table, (slice(None), slice(512, 896)), high[:, 0:384], RATE_TABLE, DECAY_RATE)
    update(vectors, whole, small[0:NVEC], RATE_VECTOR, 0.0)
    turned = pltpu.roll(small[SMALL_SIDE : SMALL_SIDE + 8], lax.rem(D - wide * rows, D), 1)
    update(side, whole, turned[0:5, 0:rows], RATE_MATRIX, DECAY_RATE)


def swap(a, axis, distance):
    size = lax.axis_size(axis)
    return lax.ppermute(a, axis, [(i, i ^ distance) for i in range(size)])


def swap_column(piece, n_high):
    return [piece] + [swap(piece, "wide", 4 * k) for k in range(1, n_high)]


def gather_plane(column):
    return [column] + [swap(column, "wide", p) for p in range(1, 4)]


def gather_cores(mine):
    return [swap(a, "narrow", 1) for a in mine]


def in_blocks(parts, wide):
    n_high, rows, cols = parts[0].shape
    if rows == 16:
        return parts
    whole = jnp.stack(parts, axis=1).reshape(4 * n_high, rows, cols)
    whole = whole[wide ^ jnp.arange(4 * n_high)].reshape(4, 4, 16, cols)
    return [whole[:, p] for p in range(4)]


def in_pieces(blocks, wide, n_high):
    cols = blocks.shape[-1]
    if n_high == 4:
        return blocks
    rows = 64 // n_high
    whole = blocks.transpose(1, 0, 2, 3).reshape(4 * n_high, rows, cols)
    whole = whole[wide ^ jnp.arange(4 * n_high)]
    return whole.reshape(n_high, 4, rows, cols).transpose(1, 0, 2, 3)


def add_cores(keep, send, wide, n_high):
    keep, send = in_pieces(keep, wide, n_high), in_pieces(send, wide, n_high)
    received = swap(send, "narrow", 1)
    return [keep[p].astype(F32) + received[p].astype(F32) for p in range(4)]


def swap_plane(sums):
    return [swap(sums[p].astype(BF16), "wide", p) for p in range(1, 4)]


def add_plane(own, received):
    for a in received:
        own = own + a.astype(F32)
    return own


def column_pieces(own):
    return [own[0]] + [swap(own[k].astype(BF16), "wide", 4 * k) for k in range(1, own.shape[0])]


def resident(arrays):
    return [pltpu.with_memory_space_constraint(a, pltpu.VMEM) for a in arrays]


def in_hbm(arrays):
    return [pltpu.with_memory_space_constraint(a, pltpu.HBM) for a in arrays]


def full_spec(a):
    return pl.BlockSpec(a.shape, lambda *_: (0,) * len(a.shape))


def row_spec(shape):
    return pl.BlockSpec((1,) + shape, lambda i: (i,) + (0,) * len(shape))


def shaped(shape, dtype):
    return jax.ShapeDtypeStruct(shape, dtype)


VMEM_SPEC = pl.BlockSpec(memory_space=pltpu.VMEM)
ANY_SPEC = pl.BlockSpec(memory_space=pl.ANY)
SMEM_SPEC = pl.BlockSpec(memory_space=pltpu.SMEM)


VMEM_MIB = {
    "pack": 58,
    "prepare": 24,
    "first_forward": 22,
    "middle": 28,
    "ff_backward": 15,
    "attention_backward": 22,
    "finish": 58,
    "adam": 58,
}


def call(kernel, grid, in_specs, out_specs, out_shape, scratch, flops, bytes_accessed, name):
    extra = {"grid": grid} if grid else {}
    return pl.pallas_call(
        kernel,
        in_specs=in_specs,
        out_specs=out_specs,
        out_shape=out_shape,
        scratch_shapes=scratch,
        compiler_params=pltpu.CompilerParams(vmem_limit_bytes=VMEM_MIB[name] * MIB),
        cost_estimate=pl.CostEstimate(
            flops=flops, bytes_accessed=bytes_accessed, transcendentals=0
        ),
        name=name,
        **extra,
    )


KEPT = (
    ((D, KEYS), BF16),
    ((KEYS, 512), BF16),
    ((BLOCK, QUERIES), BF16),
    ((2 * BLOCK, QUERIES), BF16),
    ((3 * BLOCK, QUERIES), BF16),
    ((8, KEYS), F32),
    ((D, KEYS), BF16),
    ((SEQ, D), BF16),
    ((SEQ, D), BF16),
    ((SEQ, FF), BF16),
    ((SEQ, FF), BF16),
    ((SEQ, D), BF16),
    ((SEQ, D), BF16),
    ((SEQ, 128), F32),
    ((SEQ, D), BF16),
    ((SEQ, 128), F32),
)
FORWARD_WORK = [
    pltpu.VMEM((D, BLOCKS * QUERIES), BF16),
    pltpu.VMEM((HEADS * VALUE_ROWS, KEYS), BF16),
    pltpu.VMEM((BLOCK, QUERIES), F32),
    pltpu.VMEM((D, D), BF16),
    pltpu.VMEM((KEYS, D), BF16),
    pltpu.VMEM((SEQ, FF), F32),
    pltpu.VMEM((SEQ, D), F32),
    pltpu.VMEM((SEQ, D), F32),
]
BACKWARD_WORK = [
    pltpu.VMEM((D, BLOCKS * QUERIES), BF16),
    pltpu.VMEM((D, BLOCKS * QUERIES), BF16),
    pltpu.VMEM((D, KEYS), BF16),
    pltpu.VMEM((KEYS, BLOCKS * QUERIES), BF16),
    pltpu.VMEM((D, KEYS), BF16),
    pltpu.VMEM((KEYS, 512), F32),
    pltpu.VMEM((SEQ, 768), BF16),
]
PROJ_WORK = pltpu.VMEM((D, D), BF16)
ONES_WORK = pltpu.VMEM((16, SEQ), BF16)


def per_device(
    tokens,
    actions,
    game_ids,
    valid_steps,
    rewards,
    end_flags,
    embed_table,
    table_first,
    table_second,
    attn_weight,
    attn_first,
    attn_second,
    proj_weight,
    proj_first,
    proj_second,
    up_weight,
    up_first,
    up_second,
    up_bias,
    bias_first,
    bias_second,
    down_weight,
    down_first,
    down_second,
    vectors,
    vectors_first,
    vectors_second,
    head_weight,
    head_first,
    head_second,
    side_weight,
    side_first,
    side_second,
):
    n_high = lax.axis_size("wide") // 4
    wide = lax.axis_index("wide")
    rows = side_weight.shape[0]
    fast = rows == 16

    def flat(a):
        return jnp.swapaxes(a, -1, -2)

    params = (
        (flat(embed_table), flat(table_first), flat(table_second)),
        (attn_weight, attn_first, attn_second),
        (flat(proj_weight), flat(proj_first), flat(proj_second)),
        (up_weight, up_first, up_second),
        (up_bias, bias_first, bias_second),
        (flat(down_weight), flat(down_first), flat(down_second)),
        (vectors, vectors_first, vectors_second),
        (head_weight, head_first, head_second),
        (flat(side_weight), flat(side_first), flat(side_second)),
    )
    table, attn, proj, up, _, down, _, head, side = (group[0] for group in params)

    piece_first, piece_second = call(
        functools.partial(pack_kernel, fast),
        None,
        [VMEM_SPEC] * 7,
        [VMEM_SPEC] * 2,
        [shaped((rows, HALF_FIRST_COLS), BF16), shaped((rows, HALF_SECOND_COLS), BF16)],
        [pltpu.VMEM((rows, 128), F32)],
        10**6,
        10**6,
        "pack",
    )(table, attn, proj, up, down, head, side)
    other_bias = swap(up_bias, "narrow", 1)
    column = swap_column(piece_first, n_high)

    count = tokens.shape[0] // lax.axis_size("narrow")
    meta, frame_meta, hits = call(
        functools.partial(prepare_kernel, fast),
        None,
        [SMEM_SPEC] + [VMEM_SPEC] * 5,
        [VMEM_SPEC] * 3,
        [
            shaped((count, SEQ, 128), jnp.int32),
            shaped((count, SIDE_ROWS, 128), jnp.int32),
            shaped((count, SEQ, ROWS), BF16),
        ],
        [pltpu.VMEM((24, FRAMES), jnp.int32)],
        10**6,
        10**6,
        "prepare",
    )(*in_hbm([game_ids, flat(tokens), actions, valid_steps, rewards, end_flags]))
    column, other_bias, hits = lax.optimization_barrier((column, other_bias, hits))
    first_column = jnp.stack(column)
    first_mine = gather_plane(first_column)
    own, piece_second = lax.optimization_barrier((swap(first_column, "narrow", 1), piece_second))
    first_other = [own] + gather_cores(first_mine[1:])
    second_column = jnp.stack(swap_column(piece_second, n_high))
    second_column, across = lax.optimization_barrier((second_column, first_other[3]))
    first_other = first_other[0:3] + [across]
    second_mine = gather_plane(second_column)
    first_parts = in_blocks(first_mine, wide) + in_blocks(first_other, wide)

    kept_specs = [row_spec(shape) for shape, _ in KEPT]
    kept_shapes = [shaped((count,) + shape, dtype) for shape, dtype in KEPT]
    row_f32 = shaped((count, SEQ, D), F32)
    meta_spec = row_spec((SEQ, 128))
    vec_specs = [full_spec(vectors), full_spec(up_bias), full_spec(up_bias)]
    w_attention_spec = pl.BlockSpec((D, 1024), lambda i: (0, 0))
    w_ff_spec = pl.BlockSpec((D, 2048), lambda i: (0, 0))
    side_spec = pl.BlockSpec((D, 128), lambda i: (0, 0))
    hits_spec = row_spec((SEQ, ROWS))
    results = call(
        functools.partial(first_forward_kernel, fast),
        (count,),
        [hits_spec] + vec_specs + [VMEM_SPEC] * 8,
        [w_attention_spec, w_ff_spec, side_spec, row_spec((SEQ, D))] + kept_specs,
        [shaped((D, 1024), BF16), shaped((D, 2048), BF16), shaped((D, 128), BF16), row_f32]
        + kept_shapes,
        [pltpu.VMEM((D, COL_FIRST), BF16), pltpu.VMEM((SEQ, D), F32)] + FORWARD_WORK,
        4 * 10**9,
        20 * 10**6,
        "first_forward",
    )(hits, *in_hbm([vectors, up_bias, other_bias]), *resident(first_parts))
    w_attention, w_ff, side_copy, stream = results[0:4]
    kept = results[4:]
    received, side_copy = lax.optimization_barrier((second_mine[1:], side_copy))
    second_mine = second_mine[0:1] + received
    second_other = gather_cores(second_mine)
    second_parts = in_blocks(second_mine, wide) + in_blocks(second_other, wide)

    def blocks(cols):
        return pl.BlockSpec((4, 4, 16, cols), lambda i: (0, 0, 0, 0))

    def block_shapes(cols):
        return [shaped((4, 4, 16, cols), BF16)] * 2

    small_spec = pl.BlockSpec((SMALL_ROWS, 8, D), lambda i: (0, 0, 0))
    small_shape = shaped((SMALL_ROWS, 8, D), F32)
    small_scratch = pltpu.VMEM((SMALL_ROWS, 8, D), F32)
    scalar_spec = pl.BlockSpec((8, 128), lambda i: (0, 0))
    grad_stream, keep_second, send_second, small_grads, scalars = call(
        functools.partial(middle_kernel, fast),
        (count,),
        [meta_spec, row_spec((SIDE_ROWS, 128))]
        + vec_specs
        + [side_spec, row_spec((SEQ, D))]
        + [VMEM_SPEC] * 8,
        [row_spec((SEQ, D))] + [blocks(HALF_SECOND_COLS)] * 2 + [small_spec, scalar_spec],
        [row_f32] + block_shapes(HALF_SECOND_COLS) + [small_shape, shaped((8, 128), F32)],
        [
            pltpu.VMEM((D, COL_SECOND + 128), BF16),
            pltpu.VMEM((D, COL_SECOND + 128), F32),
            small_scratch,
        ]
        + [pltpu.VMEM(shape, dtype) for shape, dtype in KEPT[0:7]]
        + [pltpu.VMEM((2 * SEQ, D), BF16), pltpu.VMEM(*KEPT[8])]
        + [pltpu.VMEM((2 * SEQ, FF), BF16), pltpu.VMEM(*KEPT[10])]
        + [pltpu.VMEM((2 * SEQ, D), BF16)] * 2
        + [pltpu.VMEM(*a) for a in KEPT[13:16]]
        + FORWARD_WORK
        + BACKWARD_WORK[0:1]
        + BACKWARD_WORK[2:6]
        + [pltpu.VMEM((2 * SEQ, 768), BF16)]
        + [
            PROJ_WORK,
            pltpu.VMEM((2 * SEQ, FF), BF16),
            ONES_WORK,
            pltpu.VMEM((SEQ, D), F32),
            pltpu.VMEM((2 * SEQ, D), BF16),
            pltpu.VMEM((SEQ, D), F32),
            pltpu.VMEM((KEYS, D), BF16),
            pltpu.VMEM((SEQ, D), BF16),
            pltpu.VMEM((SEQ, 128), F32),
            pltpu.VMEM((2 * SEQ, D), BF16),
            pltpu.VMEM((SEQ, VOCAB), F32),
            pltpu.VMEM((2 * SEQ, VOCAB + 128), BF16),
            pltpu.VMEM((SIDE_ROWS, SEQ), BF16),
            pltpu.VMEM((SEQ, SIDE_ROWS), BF16),
            pltpu.VMEM((2 * SEQ, D), BF16),
        ],
        15 * 10**9,
        20 * 10**6,
        "middle",
    )(
        *in_hbm([meta, frame_meta, vectors, up_bias, other_bias]),
        side_copy,
        stream,
        *resident(second_parts),
    )
    second_sums = add_cores(keep_second, send_second, wide, n_high)

    def joined(a):
        return a.reshape((count * a.shape[1],) + a.shape[2:])

    kept_ff = (kept[8], kept[13], kept[9], kept[10], kept[12])
    grad_mid, keep_ff, send_ff, small_grads = call(
        functools.partial(ff_backward_kernel, fast),
        (count,),
        [full_spec(vectors), w_ff_spec, row_spec((SEQ, D)), small_spec]
        + [row_spec(a.shape[1:]) for a in kept_ff],
        [row_spec((SEQ, D))] + [blocks(HALF_GRAD_COLS)] * 2 + [small_spec],
        [row_f32] + block_shapes(HALF_GRAD_COLS) + [small_shape],
        [
            pltpu.VMEM((D, 2048), F32),
            small_scratch,
            pltpu.VMEM((SEQ, D), BF16),
            pltpu.VMEM((SEQ, FF), BF16),
            ONES_WORK,
            pltpu.VMEM((SEQ, FF), F32),
            pltpu.VMEM((SEQ, D), F32),
        ],
        4 * 10**9,
        10 * 10**6,
        "ff_backward",
    )(*in_hbm([vectors]), w_ff, grad_stream, small_grads, *kept_ff)
    ff_sums = add_cores(keep_ff, send_ff, wide, n_high)
    other_sums = [jnp.concatenate(pair, axis=-1) for pair in zip(second_sums, ff_sums)]
    others_received = swap_plane(other_sums)
    kept_attention = (kept[14], kept[15]) + tuple(kept[0:7])
    joined_attention = [joined(kept[7]), joined(kept[11]), joined(hits)]
    keep_rest, send_rest, small_grads = call(
        functools.partial(attention_backward_kernel, fast),
        (count,),
        [full_spec(vectors), w_attention_spec, row_spec((SEQ, D)), small_spec]
        + [row_spec(a.shape[1:]) for a in kept_attention]
        + [VMEM_SPEC] * 3
        + [ANY_SPEC],
        [blocks(HALF_GRAD_COLS)] * 2 + [pl.BlockSpec((SMALL_ROWS, D), lambda i: (0, 0))],
        block_shapes(HALF_GRAD_COLS) + [shaped((SMALL_ROWS, D), F32)],
        [pltpu.VMEM((D, 2048), F32), small_scratch, pltpu.VMEM((KEYS, D), BF16)]
        + [pltpu.VMEM((count * SEQ, D), BF16)] * 2
        + [pltpu.VMEM((count * SEQ, 768), BF16)]
        + BACKWARD_WORK[0:6]
        + [PROJ_WORK, pltpu.VMEM((SEQ, D), F32)],
        6 * 10**9,
        20 * 10**6,
        "attention_backward",
    )(
        *in_hbm([vectors]),
        w_attention,
        grad_mid,
        small_grads,
        *kept_attention,
        *joined_attention,
        other_sums[0],
    )
    others_received, keep_rest = lax.optimization_barrier((others_received, keep_rest))
    rest_sums = add_cores(keep_rest, send_rest, wide, n_high)
    rest_received = swap_plane(rest_sums)
    other_pieces = column_pieces(add_plane(other_sums[0], others_received))
    rest_pieces = column_pieces(add_plane(rest_sums[0], rest_received))

    grad_rest, grad_others, table_part, small = call(
        functools.partial(finish_kernel, fast),
        None,
        [VMEM_SPEC] * (2 * n_high + 1),
        [VMEM_SPEC] * 4,
        [
            shaped((rows, HALF_GRAD_COLS), F32),
            shaped((rows, HALF_GRAD_COLS + HALF_SECOND_COLS), F32),
            shaped((rows, 512), F32),
            shaped((4 * n_high, 8, 128), F32),
        ],
        [],
        10**6,
        10**6,
        "finish",
    )(*resident(rest_pieces + other_pieces), scalars)

    gathered = lax.all_to_all(small, "wide", 0, 0)
    beside = swap(gathered, "narrow", 1)
    quarters = []
    if not fast:
        total = lax.psum(small_grads, ("wide", "narrow"))
        quarters = [total.reshape(4, 8, 2, 128).transpose(0, 2, 1, 3).reshape(4, 16, 128)]
    swapped = swap(table_part, "narrow", 1)

    flat_params = [a for group in params for a in group]
    results = call(
        functools.partial(adam_kernel, fast),
        None,
        [VMEM_SPEC] * (32 + len(quarters)),
        [VMEM_SPEC] * 30,
        [shaped((1, 1), F32)] * 3 + [shaped(a.shape, F32) for a in flat_params],
        [pltpu.VMEM((SMALL_ROWS, D), F32)],
        10**6,
        10**6,
        "adam",
    )(grad_rest, grad_others, *resident([swapped, gathered, beside]), *quarters, *flat_params)
    news = list(results[3:])
    for group in (0, 2, 5, 8):
        for member in range(3 * group, 3 * group + 3):
            news[member] = flat(news[member])
    return tuple(a.reshape(()) for a in results[0:3]) + tuple(news)


def solution(mesh):
    placed = (
        P("wide", None, None),
        P("wide", None),
        P("wide"),
        P("wide", None),
        P("wide", None),
        P("wide", None),
        P(None, "wide"),
        P(None, "wide"),
        P(None, "wide"),
        P(None, None, "wide", "narrow"),
        P(None, None, "wide", "narrow"),
        P(None, None, "wide", "narrow"),
        P(None, "narrow", "wide"),
        P(None, "narrow", "wide"),
        P(None, "narrow", "wide"),
        P(None, "wide", "narrow"),
        P(None, "wide", "narrow"),
        P(None, "wide", "narrow"),
        P(None, "narrow"),
        P(None, "narrow"),
        P(None, "narrow"),
        P(None, "narrow", "wide"),
        P(None, "narrow", "wide"),
        P(None, "narrow", "wide"),
        P(),
        P(),
        P(),
        P("wide", "narrow"),
        P("wide", "narrow"),
        P("wide", "narrow"),
        P("wide", None),
        P("wide", None),
        P("wide", None),
    )
    return jax.shard_map(
        per_device,
        mesh=mesh,
        in_specs=placed,
        out_specs=(P(), P(), P()) + placed[6:],
        check_vma=False,
    )
```

```python
import functools

import jax
import jax.numpy as jnp
from jax import lax
from jax.experimental import pallas as pl
from jax.experimental.pallas import tpu as pltpu
from jax.sharding import PartitionSpec as P

D = 256
HEADS = 4
HEAD_DIM = 64
FF = 1024
VOCAB = 512
ACTIONS = 18
GAMES = 26
OBS = 16
FRAMES = 20
STEP_NUMBER = 5
FRAME_TOKENS = 17
LENGTH = 340
ROWS = 896
NVEC = 14

EPS_NORM = 1e-05
BETA_ONE = 0.5
BETA_TWO = 0.5
RATE_TABLE = 0.5
RATE_MATRIX = 0.05
RATE_VECTOR = 0.2
DECAY_RATE = 0.01
EPS_ADAM = 1e-08
CLIP_AT = 0.1

SEQ = 352
KEYS = 384
BLOCK, BLOCKS = 128, 3
TILE = 32
SIDE_ROWS = 32
QUERIES = HEADS * BLOCK
VALUE_ROWS = 80

COL_QKV, COL_PROJ, COL_UP, COL_DOWN, COL_LAYER = 0, 768, 1024, 2048, 3072
HALF_ATTENTION = ((0, 128, 0), (128, 128, 256), (256, 128, 512), (384, 128, COL_PROJ))
HALF_LAYER = HALF_ATTENTION + ((512, 512, COL_UP), (1024, 512, COL_DOWN))
COL_TABLE, COL_SMALL, COL_FIRST = 3072, 3968, 4096
HALF_FIRST = HALF_LAYER + ((1536, 512, COL_TABLE),)
HALF_FIRST_COLS = 2048
COL_HEAD, COL_SECOND = 3072, 3584
HALF_SECOND = HALF_LAYER + ((1536, 256, COL_HEAD),)
HALF_SECOND_COLS = 1792
GRAD_UP, GRAD_DOWN = 0, 1024
HALF_GRAD_FF = ((0, 512, GRAD_UP), (512, 512, GRAD_DOWN))
GRAD_TABLE, GRAD_SMALL = 1024, 1920
HALF_GRAD_REST = HALF_ATTENTION + ((512, 512, GRAD_TABLE),)
HALF_GRAD_COLS = 1024
SMALL_ROWS, SMALL_BIAS, SMALL_SIDE = 32, 14, 22

F32, BF16 = jnp.float32, jnp.bfloat16
MIB = 1024 * 1024


def dot_nn(a, b):
    return lax.dot_general(a, b, (((1,), (0,)), ((), ())), preferred_element_type=F32)


def dot_nt(a, b):
    return lax.dot_general(a, b, (((1,), (1,)), ((), ())), preferred_element_type=F32)


def dot_tn(a, b):
    return lax.dot_general(a, b, (((0,), (0,)), ((), ())), preferred_element_type=F32)


def places(fast):
    wide, core = lax.axis_index("wide"), lax.axis_index("narrow")
    return (wide if fast else 0), core, wide


def tiles(rows, size):
    return [slice(first, first + size) for first in range(0, rows, size)]


def normalise(x):
    centred = x - jnp.mean(x, axis=1, keepdims=True)
    scale = lax.rsqrt(jnp.mean(centred * centred, axis=1, keepdims=True) + EPS_NORM)
    return centred * scale, scale


def keep_norm(rows, xhat, scale, kept):
    kept[0][rows] = xhat.astype(BF16)
    kept[1][rows] = jnp.broadcast_to(scale, (TILE, 128))


def kept_norm(rows, kept):
    scale = kept[1][rows]
    return kept[0][rows].astype(F32), jnp.concatenate([scale, scale], axis=1)


def normalise_back(grad, xhat, scale, gain):
    inner = grad * gain
    mean_one = jnp.mean(inner, axis=1, keepdims=True)
    mean_two = jnp.mean(inner * xhat, axis=1, keepdims=True)
    return scale * (inner - mean_one - xhat * mean_two)


def column_sum(a):
    return jnp.sum(a, axis=0, keepdims=True)


def fold(a):
    return jnp.sum(a.reshape(a.shape[0] // 8, 8, a.shape[1]), axis=0)


def plus(total, a):
    return a if total is None else total + a


def block_lanes(i, h=None):
    if h is None:
        return slice(QUERIES * i, QUERIES * (i + 1))
    return slice(QUERIES * i + BLOCK * h, QUERIES * i + BLOCK * (h + 1))


def head_rows(h):
    return slice(HEAD_DIM * h, HEAD_DIM * (h + 1))


def spread_heads(source, target_ref):
    for h in range(HEADS):
        for i in range(BLOCKS):
            target_ref[head_rows(h), block_lanes(i, h)] = source[
                head_rows(h), BLOCK * i : BLOCK * (i + 1)
            ]


def causal_mask():
    key = lax.broadcasted_iota(jnp.int32, (BLOCK, QUERIES), 0)
    query = lax.broadcasted_iota(jnp.int32, (BLOCK, QUERIES), 1) & (BLOCK - 1)
    return jnp.where(key <= query, 0.0, -1e30)


def assemble(pieces_mine, pieces_other, place, w_ref, halves):
    me, core, _ = place
    is_first = core == 0
    for p in range(4):

        def block(z, _, p=p):
            row = pl.multiple_of((me ^ (4 * z + p)) * 16, 16)
            for src, width, dest in halves:
                mine = pieces_mine[p][z, :, src : src + width]
                other = pieces_other[p][z, :, src : src + width]
                if dest == COL_QKV:
                    mine, other = mine * 0.125, other * 0.125
                w_ref[pl.ds(row, 16), dest : dest + width] = jnp.where(is_first, mine, other)
                w_ref[pl.ds(row, 16), dest + width : dest + 2 * width] = jnp.where(
                    is_first, other, mine
                )
            return 0

        lax.fori_loop(0, 4, block, 0)


def disperse(g_ref, place, keep_ref, send_ref, halves, scaled=True):
    me, core, _ = place
    is_first = core == 0

    def block(i, _):
        p, z = i >> 2, i & 3
        row = pl.multiple_of((me ^ (4 * z + p)) * 16, 16)
        for src, width, dest in halves:
            low = g_ref[pl.ds(row, 16), dest : dest + width]
            high = g_ref[pl.ds(row, 16), dest + width : dest + 2 * width]
            if scaled and dest == COL_QKV:
                low, high = low * 0.125, high * 0.125
            keep_ref[p, z, :, src : src + width] = jnp.where(is_first, low, high).astype(BF16)
            send_ref[p, z, :, src : src + width] = jnp.where(is_first, high, low).astype(BF16)
        return 0

    lax.fori_loop(0, 16, block, 0)


def make_hits(ids, game, hits_ref):
    lane = lax.broadcasted_iota(jnp.int32, (TILE, ROWS), 1)
    for rows in tiles(SEQ, TILE):
        place = lax.broadcasted_iota(jnp.int32, (TILE, 1), 0) + (VOCAB + ACTIONS + GAMES + rows.start)
        hit = (lane == ids[rows]) | (lane == game[rows]) | (lane == place)
        hits_ref[rows] = jnp.where(hit, 1.0, 0.0).astype(BF16)


def gelu_and_slope(up):
    up = up.astype(BF16)
    square = up * up
    half = jax.nn.sigmoid(up * (BF16(1.5957691216057308) + BF16(0.0713548162726) * square))
    hidden = up * half
    slope = BF16(1.5957691216057308) + BF16(0.2140644488178) * square
    return hidden, half + hidden * (BF16(1.0) - half) * slope


def layer_forward(x_ref, w_ref, vec, bias, kept, work):
    qt_ref, kv_ref, p0, p1, p2, r_ref, ot_ref, o_ref = kept[0:8]
    h_ref, gp_ref, a_ref, c_ref = kept[9:13]
    qst_ref, vt_ref, mask_ref, wqt_ref, long_ref, u_ref, y_ref, m_ref = work
    for rows in tiles(SEQ, TILE):
        xhat, scale = normalise(x_ref[rows])
        keep_norm(rows, xhat, scale, kept[14:16])
        normed16 = (xhat * vec[0:1] + vec[1:2]).astype(BF16)
        a_ref[rows], long_ref[rows] = normed16, normed16
    kv_ref[0:SEQ] = dot_nn(long_ref[0:SEQ], w_ref[:, 256:768]).astype(BF16)
    kv_ref[SEQ:KEYS] = jnp.zeros((KEYS - SEQ, 512), BF16)
    qt_ref[...] = dot_nt(wqt_ref[...], long_ref[...]).astype(BF16)
    spread_heads(qt_ref, qst_ref)
    turned = jnp.transpose(kv_ref[:, 256:512])
    for h in range(HEADS):
        vt_ref[VALUE_ROWS * h : VALUE_ROWS * h + HEAD_DIM] = turned[head_rows(h)]
    for i, pt_ref in enumerate((p0, p1, p2)):
        seen, first = BLOCK * (i + 1), BLOCK * i
        scores = dot_nn(kv_ref[0:seen, 0:256], qst_ref[:, block_lanes(i)])
        last = scores[first:] + mask_ref[...]
        peak = jnp.max(last, axis=0, keepdims=True)
        if i:
            peak = jnp.maximum(peak, jnp.max(scores[0:first], axis=0, keepdims=True))
            pt_ref[0:first] = jnp.exp(scores[0:first] - peak).astype(BF16)
        pt_ref[first:seen] = jnp.exp(last - peak).astype(BF16)
        for h in range(HEADS):
            values = vt_ref[VALUE_ROWS * h : VALUE_ROWS * (h + 1), 0:seen]
            out = dot_nn(values, pt_ref[:, BLOCK * h : BLOCK * (h + 1)])
            inverse = 1.0 / out[HEAD_DIM : HEAD_DIM + 1]
            r_ref[h : h + 1, first:seen] = inverse
            ot_ref[head_rows(h), first:seen] = (out[0:HEAD_DIM] * inverse).astype(BF16)
    o_ref[...] = jnp.transpose(ot_ref[...])[0:SEQ]
    y_ref[...] = dot_nt(o_ref[...], w_ref[:, COL_PROJ : COL_PROJ + 256])
    for rows in tiles(SEQ, TILE):
        middle = x_ref[rows] + (y_ref[rows] + vec[2:3])
        m_ref[rows] = middle
        xhat, scale = normalise(middle)
        keep_norm(rows, xhat, scale, (kept[8], kept[13]))
        c_ref[rows] = (xhat * vec[3:4] + vec[4:5]).astype(BF16)
    u_ref[...] = dot_nn(c_ref[...], w_ref[:, COL_UP : COL_UP + FF])
    for rows in tiles(SEQ, TILE):
        for first in range(0, FF, 256):
            cols = slice(first, first + 256)
            h_ref[rows, cols], gp_ref[rows, cols] = gelu_and_slope(u_ref[rows, cols] + bias[:, cols])
    y_ref[...] = dot_nt(h_ref[...], w_ref[:, COL_DOWN : COL_DOWN + FF])


def add_gradient(g_ref, column, left, right):
    g_ref[:, column : column + right.shape[1]] += dot_tn(left, right)


def ff_backward(grad_ref, grad16_ref, w_ref, w_up, w_down, vec, kept, v_ref, v_row, bias_row, work, mid_ref, mid16_refs):
    norm_kept, gp_ref = kept
    du_ref, ones_ref, u_ref, y_ref = work
    u_ref[...] = dot_nn(grad16_ref[...], w_ref[:, w_down : w_down + FF])
    for rows in tiles(SEQ, TILE):
        du_ref[rows] = u_ref[rows].astype(BF16) * gp_ref[rows]
    bias_grad = dot_nn(ones_ref[...], du_ref[...])
    for chunk in range(4):
        v_ref[bias_row + chunk, 0:1] += bias_grad[0:1, 256 * chunk : 256 * chunk + 256]
    y_ref[...] = dot_nt(du_ref[...], w_ref[:, w_up : w_up + FF])
    totals = [None] * 3
    for rows in tiles(SEQ, TILE):
        xhat, scale = kept_norm(rows, norm_kept)
        grad = y_ref[rows]
        mid = grad_ref[rows] + normalise_back(grad, xhat, scale, vec[3:4])
        mid_ref[rows] = mid
        for mid16_ref in mid16_refs:
            mid16_ref[rows] = mid.astype(BF16)
        for i, a in enumerate((mid, grad * xhat, grad)):
            totals[i] = plus(totals[i], fold(a))
    for i in range(3):
        v_ref[v_row + 2 + i] += totals[i]


def attention_backward(mid_ref, mid16_ref, w_ref, vec, kept, v_ref, v_row, work, out_ref):
    norm_kept, (qt_ref, kv_ref, p0, p1, p2, r_ref, ot_ref) = kept
    dost_ref, qst_ref, kt_ref, dst_ref, dqt_ref, dkv_ref, dqkv_ref, proj_ref, y_ref = work
    grad_o = dot_nt(proj_ref[...], mid16_ref[...])
    kt_ref[...] = jnp.transpose(kv_ref[:, 0:256])
    deltas = []
    for h in range(HEADS):
        scaled = grad_o[head_rows(h)] * r_ref[h : h + 1]
        deltas.append(column_sum(scaled * ot_ref[head_rows(h)].astype(F32)))
        scaled = scaled.astype(BF16)
        for i in range(BLOCKS):
            dost_ref[head_rows(h), block_lanes(i, h)] = scaled[:, BLOCK * i : BLOCK * (i + 1)]
    for i, pt_ref in enumerate((p0, p1, p2)):
        seen, first = BLOCK * (i + 1), BLOCK * i
        lanes = block_lanes(i)
        delta = jnp.concatenate([a[:, first:seen] for a in deltas], axis=1)
        grad = dot_nn(kv_ref[0:seen, 256:512], dost_ref[:, lanes])
        dst_ref[0:seen, lanes] = pt_ref[...] * (grad - delta).astype(BF16)
        for h in range(HEADS):
            out = dot_nn(kt_ref[head_rows(h), 0:seen], dst_ref[0:seen, block_lanes(i, h)])
            dqt_ref[head_rows(h), first:seen] = out.astype(BF16)
        for at, left, right in (
            (0, dst_ref[0:seen, lanes], qst_ref),
            (256, pt_ref[...], dost_ref),
        ):
            out = dot_nt(left, right[:, lanes])
            if i:
                dkv_ref[0:first, at : at + 256] += out[0:first]
            dkv_ref[first:seen, at : at + 256] = out[first:]
    dqkv_ref[:, 0:256] = jnp.transpose(dqt_ref[...])[0:SEQ]
    dqkv_ref[:, 256:768] = dkv_ref[0:SEQ].astype(BF16)
    y_ref[...] = dot_nt(dqkv_ref[...], w_ref[:, COL_QKV : COL_QKV + 768])
    totals = [None] * 2
    for rows in tiles(SEQ, TILE):
        xhat, scale = kept_norm(rows, norm_kept)
        grad = y_ref[rows]
        out = mid_ref[rows] + normalise_back(grad, xhat, scale, vec[0:1])
        out_ref[rows] = out.astype(out_ref.dtype)
        for i, a in enumerate((grad * xhat, grad)):
            totals[i] = plus(totals[i], fold(a))
    for i in range(2):
        v_ref[v_row + i] += totals[i]


def own_bias(place, mine, other):
    is_first = place[1] == 0
    return jnp.concatenate(
        [jnp.where(is_first, mine, other), jnp.where(is_first, other, mine)], axis=1
    )


def prepare_kernel(
    fast, games_ref, tokens, actions, valid, rewards, ends, out, out_side, out_hits, x_ref
):
    count = out.shape[0]
    frames = tokens.shape[2]
    base = places(fast)[1] * count
    row = lax.broadcasted_iota(jnp.int32, (SEQ, frames), 0)
    start = lax.broadcasted_iota(jnp.int32, (SEQ, frames), 1) * FRAME_TOKENS
    here = jnp.where((row >= start) & (row < start + FRAME_TOKENS), 1.0, 0.0).astype(BF16)
    coming = jnp.where((row >= start - FRAME_TOKENS) & (row < start), 1.0, 0.0).astype(BF16)
    passed = jnp.sum(jnp.where(row >= start + FRAME_TOKENS, 1, 0), axis=1, keepdims=True)
    place = lax.broadcasted_iota(jnp.int32, (SEQ, 1), 0)
    spot = place - passed * FRAME_TOKENS
    lane = lax.broadcasted_iota(jnp.int32, (SEQ, 24), 1)
    wide_lane = lax.broadcasted_iota(jnp.int32, (SEQ, 128), 1)
    inside = place < LENGTH
    one_frame = (
        lax.broadcasted_iota(jnp.int32, (SIDE_ROWS, frames), 0)
        == lax.broadcasted_iota(jnp.int32, (SIDE_ROWS, frames), 1)
    )
    one_frame = jnp.where(one_frame, 1.0, 0.0).astype(BF16)
    side_lane = lax.broadcasted_iota(jnp.int32, (SIDE_ROWS, 128), 1)
    x_ref[...] = jnp.zeros(x_ref.shape, jnp.int32)
    for s in range(count):
        x_ref[0:OBS] = tokens[base + s]
        x_ref[16:17] = actions[pl.ds(base + s, 1)] + VOCAB
        x_ref[17:18] = valid[pl.ds(base + s, 1)]
        x_ref[18:19] = rewards[pl.ds(base + s, 1)]
        x_ref[19:20] = ends[pl.ds(base + s, 1)] + 3
        high = (x_ref[...] >> 4).astype(F32).astype(BF16)
        low = (x_ref[...] & 15).astype(F32).astype(BF16)
        now = dot_nt(here, high) * 16.0 + dot_nt(here, low)
        soon = dot_nt(coming, high) * 16.0 + dot_nt(coming, low)

        at_end = spot == 16
        packed = jnp.where(lane == spot, now, 0.0)
        target = jnp.where((lane == spot + 1) & (spot < 15), now, 0.0)
        target = target + jnp.where((lane == 0) & at_end, soon, 0.0)
        weight = jnp.where((lane == 17) & (spot < 15), now, 0.0)
        weight = weight + jnp.where((lane == 17) & at_end, soon, 0.0)
        packed = packed + 1024.0 * target + 1048576.0 * weight
        packed = jnp.sum(packed, axis=1, keepdims=True).astype(jnp.int32)
        ids = jnp.where(inside, packed & 1023, -1)
        game = jnp.where(inside, games_ref[base + s] + (VOCAB + ACTIONS), -1)
        target, weight = (packed >> 10) & 1023, packed >> 20
        out[s] = jnp.where(wide_lane == 2, target, jnp.where(wide_lane == 3, weight, 0))
        make_hits(ids, game, out_hits.at[s])
        by_frame = dot_nt(one_frame, high) * 16.0 + dot_nt(one_frame, low)
        result = jnp.zeros((SIDE_ROWS, 128), jnp.int32)
        for c in range(3):
            column = by_frame[:, 17 + c : 18 + c].astype(jnp.int32)
            result = jnp.where(side_lane == c, column, result)
        out_side[s] = result


def start_forward(work, w_ref):
    qst_ref, vt_ref, mask_ref, wqt_ref, long_ref = work[0:5]
    long_ref[SEQ:KEYS] = jnp.zeros((KEYS - SEQ, D), BF16)
    qst_ref[...] = jnp.zeros(qst_ref.shape, BF16)
    vt_ref[...] = jnp.ones(vt_ref.shape, BF16)
    mask_ref[...] = causal_mask()
    wqt_ref[...] = jnp.transpose(w_ref[:, 0:256])


def first_forward_kernel(fast, *refs):
    refs = (places(fast),) + refs
    place, hits_ref, vec_ref, bias_ref, bias_other = refs[0:5]
    mine, other = refs[5:9], refs[9:13]
    w_attention, w_ff, side_out, next_ref = refs[13:17]
    kept = [ref.at[0] for ref in refs[17:33]]
    w_ref, x_ref = refs[33:35]
    work = refs[35:43]
    y_ref, m_ref = work[6:8]

    @pl.when(pl.program_id(0) == 0)
    def _():
        assemble(mine, other, place, w_ref, HALF_FIRST)
        w_attention[...] = w_ref[:, 0:COL_UP]
        w_ff[...] = w_ref[:, COL_UP:COL_TABLE]
        side_out[...] = w_ref[:, COL_SMALL:]
        start_forward(work, w_ref)

    x_ref[...] = dot_nt(hits_ref[0], w_ref[:, COL_TABLE : COL_TABLE + ROWS])
    bias = own_bias(place, bias_ref[0:1], bias_other[0:1])
    vec = vec_ref[0:6]
    layer_forward(x_ref, w_ref, vec, bias, kept, work)
    for rows in tiles(SEQ, TILE):
        next_ref[0, rows] = m_ref[rows] + (y_ref[rows] + vec[5:6])


def codebook_losses(logits, meta):
    weight = meta[:, 3:4].astype(F32)
    peak = jnp.max(logits, axis=1, keepdims=True)
    expanded = jnp.exp(logits - peak)
    total = jnp.sum(expanded, axis=1, keepdims=True)
    hit = lax.broadcasted_iota(jnp.int32, logits.shape, 1) == meta[:, 2:3]
    hit = jnp.where(hit, weight, 0.0)
    return weight * (peak + jnp.log(total)), hit, expanded * (weight / total) - hit


def side_losses(side, meta):
    lane = lax.broadcasted_iota(jnp.int32, side.shape, 1)
    is_reward, is_end = lane < 3, (lane == 3) | (lane == 4)
    is_side = lane < 5
    weight = meta[:, 0:1].astype(F32)
    reward_peak = jnp.max(jnp.where(is_reward, side, -1e30), axis=1, keepdims=True)
    end_peak = jnp.max(jnp.where(is_end, side, -1e30), axis=1, keepdims=True)
    shifted = jnp.where(is_side, side - jnp.where(is_reward, reward_peak, end_peak), 0.0)
    expanded = jnp.where(is_side, jnp.exp(shifted), 0.0)
    reward_total = jnp.sum(jnp.where(is_reward, expanded, 0.0), axis=1, keepdims=True)
    end_total = jnp.sum(jnp.where(is_end, expanded, 0.0), axis=1, keepdims=True)
    hit = (lane == meta[:, 1:2]) | (lane == meta[:, 2:3])
    picked = jnp.sum(jnp.where(hit, side, 0.0), axis=1, keepdims=True)
    terms = reward_peak + jnp.log(reward_total) + end_peak + jnp.log(end_total) - picked
    grad = expanded * jnp.where(is_reward, weight / reward_total, weight / end_total)
    return weight * terms, grad - jnp.where(hit, weight, 0.0), weight


def frame_ends(shape, frame_axis):
    frame = lax.broadcasted_iota(jnp.int32, shape, frame_axis)
    row = lax.broadcasted_iota(jnp.int32, shape, 1 - frame_axis)
    hit = (row == frame * FRAME_TOKENS + OBS) & (frame < FRAMES)
    return jnp.where(hit, 1.0, 0.0).astype(BF16)


def middle_kernel(fast, *refs):
    refs = (places(fast),) + refs
    place, meta_ref, frame_ref, vec_ref, bias_ref, bias_other, side_ref, in_ref = refs[0:8]
    mine, other = refs[8:12], refs[12:16]
    grad_ref, keep_ref, send_ref, v_out, scalar_ref = refs[16:21]
    refs = refs[1:]
    w_ref, g_ref, v_ref = refs[20:23]
    kept = list(refs[23:39])
    forward_work = refs[39:47]
    u_ref, y_ref, m_ref = forward_work[5:8]
    backward_work = list(refs[47:53])
    proj_ref = refs[53]
    du_all, ones_ref, up_ref, up16_all, mid_ref, mid16_ref = refs[54:60]
    last_kept = refs[60:62]
    final_all, logit_ref, dlogit_all, pick_ref, put_ref, mid16_all = refs[62:68]
    o_all, h_all, a_all, c_all, dqkv_all = kept[7], kept[9], kept[11], kept[12], backward_work[5]
    dost_ref = backward_work[0]
    step = pl.program_id(0)

    @pl.when(step == 0)
    def _():
        assemble(mine, other, place, w_ref, HALF_SECOND)
        w_ref[:, COL_SECOND:] = side_ref[...]
        g_ref[...] = jnp.zeros(g_ref.shape, F32)
        v_ref[...] = jnp.zeros(v_ref.shape, F32)
        scalar_ref[...] = jnp.zeros(scalar_ref.shape, F32)
        start_forward(forward_work, w_ref)
        dost_ref[...] = jnp.zeros(dost_ref.shape, BF16)
        proj_ref[...] = jnp.transpose(w_ref[:, COL_PROJ : COL_PROJ + 256])
        ones_ref[...] = jnp.ones(ones_ref.shape, BF16)
        mid16_ref[SEQ:KEYS] = jnp.zeros((KEYS - SEQ, D), BF16)
        pick_ref[...] = frame_ends((SIDE_ROWS, SEQ), 0)
        put_ref[...] = frame_ends((SEQ, SIDE_ROWS), 1)

    here = pl.ds(pl.multiple_of((step & 1) * SEQ, 32), SEQ)
    for i in (7, 9, 11, 12):
        kept[i] = kept[i].at[here]
    gp_ref = kept[10]
    backward_work[5] = dqkv_all.at[here]
    du_ref, up16_ref, pair16_ref = du_all.at[here], up16_all.at[here], mid16_all.at[here]
    final_ref, dlogit_ref = final_all.at[here], dlogit_all.at[here]
    x_ref = in_ref.at[0]
    vec = vec_ref[6:12]
    bias = own_bias(place, bias_ref[1:2], bias_other[1:2])
    layer_forward(x_ref, w_ref, vec, bias, kept, forward_work)

    gain, offset = vec_ref[12:13], vec_ref[13:14]
    for rows in tiles(SEQ, TILE):
        last = m_ref[rows] + (y_ref[rows] + vec[5:6])
        xhat, scale = normalise(last)
        keep_norm(rows, xhat, scale, last_kept)
        final_ref[rows] = (xhat * gain + offset).astype(BF16)
    cols_head = slice(COL_HEAD, COL_HEAD + VOCAB + 128)
    logit_ref[...] = dot_nn(final_ref[...], w_ref[:, COL_HEAD : COL_HEAD + VOCAB])
    logs, picked = None, None
    for rows in tiles(SEQ, TILE):
        logits = logit_ref[rows]
        log, hit, grad = codebook_losses(logits, meta_ref[0, rows])
        dlogit_ref[rows, :VOCAB] = grad.astype(BF16)
        logs, picked = plus(logs, log), plus(picked, fold(hit * logits))
    acting = dot_nn(pick_ref[...], final_ref[...]).astype(BF16)
    side = dot_nn(acting, w_ref[:, COL_HEAD + VOCAB : COL_HEAD + VOCAB + 128])
    side_loss, grad, weight = side_losses(side, frame_ref[0])
    dlogit_ref[:, VOCAB:] = dot_nn(put_ref[...], grad.astype(BF16)).astype(BF16)
    loss = column_sum(logs) + column_sum(side_loss)
    loss = loss - jnp.sum(column_sum(picked), axis=1, keepdims=True)
    valid = column_sum(weight)
    scalar_lane = lax.broadcasted_iota(jnp.int32, (8, 128), 1)
    scalar_row = lax.broadcasted_iota(jnp.int32, (8, 128), 0) == 0
    scalar_ref[...] += jnp.where(
        scalar_row,
        jnp.where(scalar_lane == 0, loss, jnp.where(scalar_lane == 1, valid, 0.0)),
        0.0,
    )
    y_ref[...] = dot_nt(dlogit_ref[...], w_ref[:, cols_head])
    totals = [None] * 3
    for rows in tiles(SEQ, TILE):
        xhat, scale = kept_norm(rows, last_kept)
        grad = y_ref[rows]
        up = normalise_back(grad, xhat, scale, gain)
        up_ref[rows] = up
        up16_ref[rows] = up.astype(BF16)
        for i, a in enumerate((up, grad * xhat, grad)):
            totals[i] = plus(totals[i], fold(a))
    for i in range(3):
        v_ref[11 + i] += totals[i]
    ff_backward(
        up_ref,
        up16_ref,
        w_ref,
        COL_UP,
        COL_DOWN,
        vec,
        ((kept[8], kept[13]), gp_ref),
        v_ref,
        6,
        SMALL_BIAS + 4,
        (du_ref, ones_ref, u_ref, y_ref),
        mid_ref,
        (mid16_ref, pair16_ref),
    )
    attention_backward(
        mid_ref,
        mid16_ref,
        w_ref,
        vec,
        (kept[14:16], kept[0:7]),
        v_ref,
        6,
        (dost_ref, forward_work[0]) + tuple(backward_work[1:]) + (proj_ref, y_ref),
        grad_ref.at[0],
    )

    @pl.when(step & 1 == 1)
    def _():
        add_gradient(g_ref, COL_QKV, a_all[...], dqkv_all[...])
        add_gradient(g_ref, COL_PROJ, mid16_all[...], o_all[...])
        add_gradient(g_ref, COL_UP, c_all[...], du_all[...])
        add_gradient(g_ref, COL_DOWN, up16_all[...], h_all[...])
        add_gradient(g_ref, COL_HEAD, final_all[...], dlogit_all[...])

    @pl.when(step == pl.num_programs(0) - 1)
    def _():
        disperse(g_ref, place, keep_ref, send_ref, HALF_SECOND)
        side = jnp.transpose(g_ref[:, COL_SECOND:])
        for i in range(5):
            v_ref[SMALL_SIDE + i, 0:1] = side[i : i + 1]
        v_out[...] = v_ref[...]


def ff_backward_kernel(fast, *refs):
    vec_ref, w_ref, grad_ref, v_in = refs[0:4]
    xhat_ref, scale_ref, h_ref, gp_ref, c_ref = [ref.at[0] for ref in refs[4:9]]
    mid_ref, keep_ref, send_ref, v_out = refs[9:13]
    g_ref, v_ref, grad16_ref, du_ref, ones_ref, u_ref, y_ref = refs[13:20]
    step = pl.program_id(0)

    @pl.when(step == 0)
    def _():
        g_ref[...] = jnp.zeros(g_ref.shape, F32)
        v_ref[...] = v_in[...]
        ones_ref[...] = jnp.ones(ones_ref.shape, BF16)

    total = None
    for rows in tiles(SEQ, TILE):
        grad = grad_ref[0, rows]
        grad16_ref[rows] = grad.astype(BF16)
        total = plus(total, fold(grad))
    v_ref[5] += total
    ff_backward(
        grad_ref.at[0],
        grad16_ref,
        w_ref,
        GRAD_UP,
        GRAD_DOWN,
        vec_ref[0:6],
        ((xhat_ref, scale_ref), gp_ref),
        v_ref,
        0,
        SMALL_BIAS,
        (du_ref, ones_ref, u_ref, y_ref),
        mid_ref.at[0],
        (),
    )
    add_gradient(g_ref, GRAD_DOWN, grad16_ref[...], h_ref[...])
    add_gradient(g_ref, GRAD_UP, c_ref[...], du_ref[...])

    @pl.when(step == pl.num_programs(0) - 1)
    def _():
        disperse(g_ref, places(fast), keep_ref, send_ref, HALF_GRAD_FF, False)
        v_out[...] = v_ref[...]


def attention_backward_kernel(fast, *refs):
    vec_ref, w_ref, mid_ref, v_in = refs[0:4]
    kept = [ref.at[0] for ref in refs[4:13]]
    o_all, a_all, hits_all = refs[13:16]
    keep_ref, send_ref, v_out = refs[17:20]
    g_ref, v_ref, mid16_ref, mid16_all, out16_all, dqkv_all = refs[20:26]
    work = list(refs[26:34])
    dost_ref, qst_ref, proj_ref = work[0], work[1], work[6]
    step = pl.program_id(0)

    @pl.when(step == 0)
    def _():
        v_ref[...] = v_in[...]
        dost_ref[...] = jnp.zeros(dost_ref.shape, BF16)
        qst_ref[...] = jnp.zeros(qst_ref.shape, BF16)
        proj_ref[...] = jnp.transpose(w_ref[:, COL_PROJ : COL_PROJ + 256])
        mid16_ref[SEQ:KEYS] = jnp.zeros((KEYS - SEQ, D), BF16)

    here = pl.ds(pl.multiple_of(step * SEQ, 32), SEQ)
    all16_ref = mid16_all.at[here]
    spread_heads(kept[2], qst_ref)
    for rows in tiles(SEQ, TILE):
        mid16 = mid_ref[0, rows].astype(BF16)
        mid16_ref[rows], all16_ref[rows] = mid16, mid16
    work.insert(6, dqkv_all.at[here])
    attention_backward(
        mid_ref.at[0],
        mid16_ref,
        w_ref,
        vec_ref[0:6],
        (kept[0:2], kept[2:9]),
        v_ref,
        0,
        work,
        out16_all.at[here],
    )

    @pl.when(step == pl.num_programs(0) - 1)
    def _():
        g_ref[:, COL_QKV : COL_QKV + 768] = dot_tn(a_all[...], dqkv_all[...])
        g_ref[:, COL_PROJ : COL_PROJ + 256] = dot_tn(mid16_all[...], o_all[...])
        g_ref[:, GRAD_TABLE : GRAD_TABLE + ROWS] = dot_tn(out16_all[...], hits_all[...])
        small = jnp.sum(v_ref[...], axis=1)
        v_out[...] = small
        for block in range(16):
            quarter = small[8 * (block // 4) : 8 * (block // 4) + 8]
            g_ref[16 * block : 16 * block + 8, GRAD_SMALL:] = quarter[:, 0:128]
            g_ref[16 * block + 8 : 16 * block + 16, GRAD_SMALL:] = quarter[:, 128:256]
        disperse(g_ref, places(fast), keep_ref, send_ref, HALF_GRAD_REST)


def pack_layer(attn, proj, up, down, layer, out):
    for j in range(3):
        out[:, 128 * j : 128 * j + 128] = attn[layer, j].astype(BF16)
    out[:, 384:512] = proj[layer].astype(BF16)
    out[:, 512:1024] = up[layer].astype(BF16)
    out[:, 1024:1536] = down[layer].astype(BF16)


def pack_kernel(fast, table, attn, proj, up, down, head, side, first, second, pad_ref):
    pack_layer(attn, proj, up, down, 0, first)
    pack_layer(attn, proj, up, down, 1, second)
    second[:, 1536:1792] = head[...].astype(BF16)
    rows = side.shape[1]
    eye = (
        lax.broadcasted_iota(jnp.int32, (rows, rows), 0)
        == lax.broadcasted_iota(jnp.int32, (rows, rows), 1)
    )
    eye = jnp.where(eye, 1.0, 0.0).astype(BF16)
    pad_ref[...] = jnp.zeros(pad_ref.shape, F32)
    pad_ref[:, 0:5] = dot_nt(eye, side[...].astype(BF16))
    high = jnp.concatenate([table[:, 512:896], pad_ref[...]], axis=1)
    first[:, 1536:2048] = jnp.where(places(fast)[1] == 0, table[:, 0:512], high).astype(BF16)


def finish_kernel(fast, *refs):
    count = (len(refs) - 5) // 2
    scalar_ref = refs[2 * count]
    out_rest, out_other, out_table, out_small = refs[2 * count + 1 :]
    square = jnp.zeros((1, 1), F32)
    for pieces, out in ((refs[0:count], out_rest), (refs[count : 2 * count], out_other)):
        total = pieces[0][...]
        for piece in pieces[1:]:
            total = total + piece[...].astype(F32)
        out[...] = total
        square = square + column_sum(jnp.sum(total * total, axis=1, keepdims=True))
    small = out_rest[:, 896:1024]
    extra = column_sum(jnp.sum(small * small, axis=1, keepdims=True))
    square = square - jnp.where(places(fast)[1] == 0, 0.0, extra)
    out_table[...] = out_rest[:, 512:1024]
    lane = lax.broadcasted_iota(jnp.int32, (8, 128), 1)
    row = lax.broadcasted_iota(jnp.int32, (8, 128), 0)
    message = scalar_ref[...] + jnp.where((row == 0) & (lane == 2), square, 0.0)
    if fast:
        spot = places(fast)[2] & 3
        part = jnp.where(spot & 1 == 0, small[0:4], small[4:8])
        part = jnp.where(spot & 2 == 0, part, jnp.where(spot & 1 == 0, small[8:12], small[12:16]))
        message = jnp.concatenate([part, message[0:4]], axis=0)
    for i in range(out_small.shape[0]):
        out_small[i] = message


def adam_rule(weight, moment, second, gradient, step_rate, decay_rate):
    moment_new = BETA_ONE * moment + (1.0 - BETA_ONE) * gradient
    second_new = BETA_TWO * second + (1.0 - BETA_TWO) * gradient * gradient
    moment_hat = moment_new / (1.0 - BETA_ONE**STEP_NUMBER)
    second_hat = second_new / (1.0 - BETA_TWO**STEP_NUMBER)
    weight_new = weight - step_rate * (
        moment_hat / (jnp.sqrt(second_hat) + EPS_ADAM) + decay_rate * weight
    )
    return (weight_new, moment_new, second_new)


def adam_kernel(fast, rest, others, swapped, gathered, beside, *refs):
    rows = rest.shape[0]
    _, core, wide = places(fast)
    is_first = core == 0
    if fast:
        small_parts = jnp.where(is_first, beside[...], gathered[...])
        quarters = [
            jnp.concatenate([small_parts[4 * z + p, 0:4] for p in range(4)], axis=0)
            for z in range(4)
        ]
    else:
        quarters = [refs[0][z] for z in range(4)]
        refs = refs[1:]
    params = [refs[3 * i : 3 * i + 3] for i in range(9)]
    loss_ref, valid_ref, norm_ref = refs[27:30]
    outs = [refs[30 + 3 * i : 33 + 3 * i] for i in range(9)]
    small_ref = refs[57]
    for z in range(4):
        small_ref[8 * z : 8 * z + 8, 0:128] = quarters[z][0:8]
        small_ref[8 * z : 8 * z + 8, 128:256] = quarters[z][8:16]
    sums = []
    for source in (gathered, beside):
        line = 4 if fast else 0
        total = source[0, line : line + 1]
        for i in range(1, source.shape[0]):
            total = total + source[i, line : line + 1]
        sums.append(total)
    scalars = sums[0] + sums[1]
    small = small_ref[...]
    loss, valid, square = scalars[:, 0:1], scalars[:, 1:2], scalars[:, 2:3]
    square = square + column_sum(jnp.sum(small * small, axis=1, keepdims=True))
    inverse = 1.0 / valid
    norm = jnp.sqrt(square) * inverse
    loss_ref[...], valid_ref[...], norm_ref[...] = loss, valid, norm
    factor = jnp.minimum(1.0, CLIP_AT / (norm + 1e-06)) * inverse
    table, attn, proj, up, bias, down, vectors, head, side = range(9)

    def update(which, index, gradient, step_rate, decay_rate):
        news = adam_rule(
            *(ref[index] for ref in params[which]), factor * gradient, step_rate, decay_rate
        )
        for ref, new in zip(outs[which], news):
            ref[index] = new

    layers = ((rest, others, 1792), (others, others, 512))
    for layer, (attention, feed, at) in enumerate(layers):
        for j in range(3):
            update(attn, (layer, j), attention[:, 128 * j : 128 * j + 128], RATE_MATRIX, DECAY_RATE)
        update(proj, (layer,), attention[:, 384:512], RATE_MATRIX, DECAY_RATE)
        update(up, (layer,), feed[:, at : at + 512], RATE_MATRIX, DECAY_RATE)
        update(down, (layer,), feed[:, at + 512 : at + 1024], RATE_MATRIX, DECAY_RATE)
        for i in range(2):
            low = SMALL_BIAS + 4 * layer + i
            row = jnp.where(is_first, small[low : low + 1], small[low + 2 : low + 3])
            index = (slice(layer, layer + 1), slice(256 * i, 256 * i + 256))
            update(bias, index, row, RATE_VECTOR, 0.0)
    whole = (slice(None), slice(None))
    update(head, whole, others[:, 1536:1792], RATE_MATRIX, DECAY_RATE)
    mine, theirs = rest[:, 512:1024], swapped[:, 0:512]
    low, high = jnp.where(is_first, mine, theirs), jnp.where(is_first, theirs, mine)
    update(table, (slice(None), slice(0, 512)), low, RATE_TABLE, DECAY_RATE)
    update(table, (slice(None), slice(512, 896)), high[:, 0:384], RATE_TABLE, DECAY_RATE)
    update(vectors, whole, small[0:NVEC], RATE_VECTOR, 0.0)
    turned = pltpu.roll(small[SMALL_SIDE : SMALL_SIDE + 8], lax.rem(D - wide * rows, D), 1)
    update(side, whole, turned[0:5, 0:rows], RATE_MATRIX, DECAY_RATE)


def swap(a, axis, distance):
    size = lax.axis_size(axis)
    return lax.ppermute(a, axis, [(i, i ^ distance) for i in range(size)])


def swap_column(piece, n_high):
    return [piece] + [swap(piece, "wide", 4 * k) for k in range(1, n_high)]


def gather_plane(column):
    return [column] + [swap(column, "wide", p) for p in range(1, 4)]


def gather_cores(mine):
    return [swap(a, "narrow", 1) for a in mine]


def in_blocks(parts, wide):
    n_high, rows, cols = parts[0].shape
    if rows == 16:
        return parts
    whole = jnp.stack(parts, axis=1).reshape(4 * n_high, rows, cols)
    whole = whole[wide ^ jnp.arange(4 * n_high)].reshape(4, 4, 16, cols)
    return [whole[:, p] for p in range(4)]


def in_pieces(blocks, wide, n_high):
    cols = blocks.shape[-1]
    if n_high == 4:
        return blocks
    rows = 64 // n_high
    whole = blocks.transpose(1, 0, 2, 3).reshape(4 * n_high, rows, cols)
    whole = whole[wide ^ jnp.arange(4 * n_high)]
    return whole.reshape(n_high, 4, rows, cols).transpose(1, 0, 2, 3)


def add_cores(keep, send, wide, n_high):
    keep, send = in_pieces(keep, wide, n_high), in_pieces(send, wide, n_high)
    received = swap(send, "narrow", 1)
    return [keep[p].astype(F32) + received[p].astype(F32) for p in range(4)]


def swap_plane(sums):
    return [swap(sums[p].astype(BF16), "wide", p) for p in range(1, 4)]


def add_plane(own, received):
    for a in received:
        own = own + a.astype(F32)
    return own


def column_pieces(own):
    return [own[0]] + [swap(own[k].astype(BF16), "wide", 4 * k) for k in range(1, own.shape[0])]


def resident(arrays):
    return [pltpu.with_memory_space_constraint(a, pltpu.VMEM) for a in arrays]


def in_hbm(arrays):
    return [pltpu.with_memory_space_constraint(a, pltpu.HBM) for a in arrays]


def full_spec(a):
    return pl.BlockSpec(a.shape, lambda *_: (0,) * len(a.shape))


def row_spec(shape):
    return pl.BlockSpec((1,) + shape, lambda i: (i,) + (0,) * len(shape))


def shaped(shape, dtype):
    return jax.ShapeDtypeStruct(shape, dtype)


VMEM_SPEC = pl.BlockSpec(memory_space=pltpu.VMEM)
ANY_SPEC = pl.BlockSpec(memory_space=pl.ANY)
SMEM_SPEC = pl.BlockSpec(memory_space=pltpu.SMEM)


VMEM_MIB = {
    "pack": 58,
    "prepare": 24,
    "first_forward": 22,
    "middle": 28,
    "ff_backward": 15,
    "attention_backward": 22,
    "finish": 58,
    "adam": 58,
}


def call(kernel, grid, in_specs, out_specs, out_shape, scratch, flops, bytes_accessed, name):
    extra = {"grid": grid} if grid else {}
    return pl.pallas_call(
        kernel,
        in_specs=in_specs,
        out_specs=out_specs,
        out_shape=out_shape,
        scratch_shapes=scratch,
        compiler_params=pltpu.CompilerParams(vmem_limit_bytes=VMEM_MIB[name] * MIB),
        cost_estimate=pl.CostEstimate(
            flops=flops, bytes_accessed=bytes_accessed, transcendentals=0
        ),
        name=name,
        **extra,
    )


KEPT = (
    ((D, KEYS), BF16),
    ((KEYS, 512), BF16),
    ((BLOCK, QUERIES), BF16),
    ((2 * BLOCK, QUERIES), BF16),
    ((3 * BLOCK, QUERIES), BF16),
    ((8, KEYS), F32),
    ((D, KEYS), BF16),
    ((SEQ, D), BF16),
    ((SEQ, D), BF16),
    ((SEQ, FF), BF16),
    ((SEQ, FF), BF16),
    ((SEQ, D), BF16),
    ((SEQ, D), BF16),
    ((SEQ, 128), F32),
    ((SEQ, D), BF16),
    ((SEQ, 128), F32),
)
FORWARD_WORK = [
    pltpu.VMEM((D, BLOCKS * QUERIES), BF16),
    pltpu.VMEM((HEADS * VALUE_ROWS, KEYS), BF16),
    pltpu.VMEM((BLOCK, QUERIES), F32),
    pltpu.VMEM((D, D), BF16),
    pltpu.VMEM((KEYS, D), BF16),
    pltpu.VMEM((SEQ, FF), F32),
    pltpu.VMEM((SEQ, D), F32),
    pltpu.VMEM((SEQ, D), F32),
]
BACKWARD_WORK = [
    pltpu.VMEM((D, BLOCKS * QUERIES), BF16),
    pltpu.VMEM((D, BLOCKS * QUERIES), BF16),
    pltpu.VMEM((D, KEYS), BF16),
    pltpu.VMEM((KEYS, BLOCKS * QUERIES), BF16),
    pltpu.VMEM((D, KEYS), BF16),
    pltpu.VMEM((KEYS, 512), F32),
    pltpu.VMEM((SEQ, 768), BF16),
]
PROJ_WORK = pltpu.VMEM((D, D), BF16)
ONES_WORK = pltpu.VMEM((16, SEQ), BF16)


def per_device(
    tokens,
    actions,
    game_ids,
    valid_steps,
    rewards,
    end_flags,
    embed_table,
    table_first,
    table_second,
    attn_weight,
    attn_first,
    attn_second,
    proj_weight,
    proj_first,
    proj_second,
    up_weight,
    up_first,
    up_second,
    up_bias,
    bias_first,
    bias_second,
    down_weight,
    down_first,
    down_second,
    vectors,
    vectors_first,
    vectors_second,
    head_weight,
    head_first,
    head_second,
    side_weight,
    side_first,
    side_second,
):
    n_high = lax.axis_size("wide") // 4
    wide = lax.axis_index("wide")
    rows = side_weight.shape[0]
    fast = rows == 16

    def flat(a):
        return jnp.swapaxes(a, -1, -2)

    params = (
        (flat(embed_table), flat(table_first), flat(table_second)),
        (attn_weight, attn_first, attn_second),
        (flat(proj_weight), flat(proj_first), flat(proj_second)),
        (up_weight, up_first, up_second),
        (up_bias, bias_first, bias_second),
        (flat(down_weight), flat(down_first), flat(down_second)),
        (vectors, vectors_first, vectors_second),
        (head_weight, head_first, head_second),
        (flat(side_weight), flat(side_first), flat(side_second)),
    )
    table, attn, proj, up, _, down, _, head, side = (group[0] for group in params)

    piece_first, piece_second = call(
        functools.partial(pack_kernel, fast),
        None,
        [VMEM_SPEC] * 7,
        [VMEM_SPEC] * 2,
        [shaped((rows, HALF_FIRST_COLS), BF16), shaped((rows, HALF_SECOND_COLS), BF16)],
        [pltpu.VMEM((rows, 128), F32)],
        10**6,
        10**6,
        "pack",
    )(table, attn, proj, up, down, head, side)
    other_bias = swap(up_bias, "narrow", 1)
    column = swap_column(piece_first, n_high)

    count = tokens.shape[0] // lax.axis_size("narrow")
    meta, frame_meta, hits = call(
        functools.partial(prepare_kernel, fast),
        None,
        [SMEM_SPEC] + [VMEM_SPEC] * 5,
        [VMEM_SPEC] * 3,
        [
            shaped((count, SEQ, 128), jnp.int32),
            shaped((count, SIDE_ROWS, 128), jnp.int32),
            shaped((count, SEQ, ROWS), BF16),
        ],
        [pltpu.VMEM((24, FRAMES), jnp.int32)],
        10**6,
        10**6,
        "prepare",
    )(*in_hbm([game_ids, flat(tokens), actions, valid_steps, rewards, end_flags]))
    column, other_bias, hits = lax.optimization_barrier((column, other_bias, hits))
    first_column = jnp.stack(column)
    first_mine = gather_plane(first_column)
    own, piece_second = lax.optimization_barrier((swap(first_column, "narrow", 1), piece_second))
    first_other = [own] + gather_cores(first_mine[1:])
    near = swap(piece_second, "wide", 4)
    near, far_piece = lax.optimization_barrier((near, piece_second))
    second_column = [piece_second, near, swap(piece_second, "wide", 8)]
    second_column += [swap(far_piece, "wide", 4 * k) for k in range(3, n_high)]
    second_column, across = lax.optimization_barrier(
        (jnp.stack(second_column), first_other[3])
    )
    first_other = first_other[0:3] + [across]
    second_mine = gather_plane(second_column)
    first_parts = in_blocks(first_mine, wide) + in_blocks(first_other, wide)

    kept_specs = [row_spec(shape) for shape, _ in KEPT]
    kept_shapes = [shaped((count,) + shape, dtype) for shape, dtype in KEPT]
    row_f32 = shaped((count, SEQ, D), F32)
    meta_spec = row_spec((SEQ, 128))
    vec_specs = [full_spec(vectors), full_spec(up_bias), full_spec(up_bias)]
    w_attention_spec = pl.BlockSpec((D, 1024), lambda i: (0, 0))
    w_ff_spec = pl.BlockSpec((D, 2048), lambda i: (0, 0))
    side_spec = pl.BlockSpec((D, 128), lambda i: (0, 0))
    hits_spec = row_spec((SEQ, ROWS))
    results = call(
        functools.partial(first_forward_kernel, fast),
        (count,),
        [hits_spec] + vec_specs + [VMEM_SPEC] * 8,
        [w_attention_spec, w_ff_spec, side_spec, row_spec((SEQ, D))] + kept_specs,
        [shaped((D, 1024), BF16), shaped((D, 2048), BF16), shaped((D, 128), BF16), row_f32]
        + kept_shapes,
        [pltpu.VMEM((D, COL_FIRST), BF16), pltpu.VMEM((SEQ, D), F32)] + FORWARD_WORK,
        4 * 10**9,
        20 * 10**6,
        "first_forward",
    )(hits, *in_hbm([vectors, up_bias, other_bias]), *resident(first_parts))
    w_attention, w_ff, side_copy, stream = results[0:4]
    kept = results[4:]
    received, side_copy = lax.optimization_barrier((second_mine[1:], side_copy))
    second_mine = second_mine[0:1] + received
    second_other = gather_cores(second_mine)
    second_parts = in_blocks(second_mine, wide) + in_blocks(second_other, wide)

    def blocks(cols):
        return pl.BlockSpec((4, 4, 16, cols), lambda i: (0, 0, 0, 0))

    def block_shapes(cols):
        return [shaped((4, 4, 16, cols), BF16)] * 2

    small_spec = pl.BlockSpec((SMALL_ROWS, 8, D), lambda i: (0, 0, 0))
    small_shape = shaped((SMALL_ROWS, 8, D), F32)
    small_scratch = pltpu.VMEM((SMALL_ROWS, 8, D), F32)
    scalar_spec = pl.BlockSpec((8, 128), lambda i: (0, 0))
    grad_stream, keep_second, send_second, small_grads, scalars = call(
        functools.partial(middle_kernel, fast),
        (count,),
        [meta_spec, row_spec((SIDE_ROWS, 128))]
        + vec_specs
        + [side_spec, row_spec((SEQ, D))]
        + [VMEM_SPEC] * 8,
        [row_spec((SEQ, D))] + [blocks(HALF_SECOND_COLS)] * 2 + [small_spec, scalar_spec],
        [row_f32] + block_shapes(HALF_SECOND_COLS) + [small_shape, shaped((8, 128), F32)],
        [
            pltpu.VMEM((D, COL_SECOND + 128), BF16),
            pltpu.VMEM((D, COL_SECOND + 128), F32),
            small_scratch,
        ]
        + [pltpu.VMEM(shape, dtype) for shape, dtype in KEPT[0:7]]
        + [pltpu.VMEM((2 * SEQ, D), BF16), pltpu.VMEM(*KEPT[8])]
        + [pltpu.VMEM((2 * SEQ, FF), BF16), pltpu.VMEM(*KEPT[10])]
        + [pltpu.VMEM((2 * SEQ, D), BF16)] * 2
        + [pltpu.VMEM(*a) for a in KEPT[13:16]]
        + FORWARD_WORK
        + BACKWARD_WORK[0:1]
        + BACKWARD_WORK[2:6]
        + [pltpu.VMEM((2 * SEQ, 768), BF16)]
        + [
            PROJ_WORK,
            pltpu.VMEM((2 * SEQ, FF), BF16),
            ONES_WORK,
            pltpu.VMEM((SEQ, D), F32),
            pltpu.VMEM((2 * SEQ, D), BF16),
            pltpu.VMEM((SEQ, D), F32),
            pltpu.VMEM((KEYS, D), BF16),
            pltpu.VMEM((SEQ, D), BF16),
            pltpu.VMEM((SEQ, 128), F32),
            pltpu.VMEM((2 * SEQ, D), BF16),
            pltpu.VMEM((SEQ, VOCAB), F32),
            pltpu.VMEM((2 * SEQ, VOCAB + 128), BF16),
            pltpu.VMEM((SIDE_ROWS, SEQ), BF16),
            pltpu.VMEM((SEQ, SIDE_ROWS), BF16),
            pltpu.VMEM((2 * SEQ, D), BF16),
        ],
        15 * 10**9,
        20 * 10**6,
        "middle",
    )(
        *in_hbm([meta, frame_meta, vectors, up_bias, other_bias]),
        side_copy,
        stream,
        *resident(second_parts),
    )
    second_sums = add_cores(keep_second, send_second, wide, n_high)

    def joined(a):
        return a.reshape((count * a.shape[1],) + a.shape[2:])

    kept_ff = (kept[8], kept[13], kept[9], kept[10], kept[12])
    grad_mid, keep_ff, send_ff, small_grads = call(
        functools.partial(ff_backward_kernel, fast),
        (count,),
        [full_spec(vectors), w_ff_spec, row_spec((SEQ, D)), small_spec]
        + [row_spec(a.shape[1:]) for a in kept_ff],
        [row_spec((SEQ, D))] + [blocks(HALF_GRAD_COLS)] * 2 + [small_spec],
        [row_f32] + block_shapes(HALF_GRAD_COLS) + [small_shape],
        [
            pltpu.VMEM((D, 2048), F32),
            small_scratch,
            pltpu.VMEM((SEQ, D), BF16),
            pltpu.VMEM((SEQ, FF), BF16),
            ONES_WORK,
            pltpu.VMEM((SEQ, FF), F32),
            pltpu.VMEM((SEQ, D), F32),
        ],
        4 * 10**9,
        10 * 10**6,
        "ff_backward",
    )(*in_hbm([vectors]), w_ff, grad_stream, small_grads, *kept_ff)
    ff_sums = add_cores(keep_ff, send_ff, wide, n_high)
    other_sums = [jnp.concatenate(pair, axis=-1) for pair in zip(second_sums, ff_sums)]
    others_received = swap_plane(other_sums)
    kept_attention = (kept[14], kept[15]) + tuple(kept[0:7])
    joined_attention = [joined(kept[7]), joined(kept[11]), joined(hits)]
    keep_rest, send_rest, small_grads = call(
        functools.partial(attention_backward_kernel, fast),
        (count,),
        [full_spec(vectors), w_attention_spec, row_spec((SEQ, D)), small_spec]
        + [row_spec(a.shape[1:]) for a in kept_attention]
        + [VMEM_SPEC] * 3
        + [ANY_SPEC],
        [blocks(HALF_GRAD_COLS)] * 2 + [pl.BlockSpec((SMALL_ROWS, D), lambda i: (0, 0))],
        block_shapes(HALF_GRAD_COLS) + [shaped((SMALL_ROWS, D), F32)],
        [pltpu.VMEM((D, 2048), F32), small_scratch, pltpu.VMEM((KEYS, D), BF16)]
        + [pltpu.VMEM((count * SEQ, D), BF16)] * 2
        + [pltpu.VMEM((count * SEQ, 768), BF16)]
        + BACKWARD_WORK[0:6]
        + [PROJ_WORK, pltpu.VMEM((SEQ, D), F32)],
        6 * 10**9,
        20 * 10**6,
        "attention_backward",
    )(
        *in_hbm([vectors]),
        w_attention,
        grad_mid,
        small_grads,
        *kept_attention,
        *joined_attention,
        other_sums[0],
    )
    others_received, keep_rest = lax.optimization_barrier((others_received, keep_rest))
    others = add_plane(other_sums[0], others_received)
    keep_rest = in_pieces(keep_rest, wide, n_high)
    received = swap(in_pieces(send_rest, wide, n_high), "narrow", 1)
    others, received = lax.optimization_barrier((others, received))
    rest_sums = [keep_rest[p].astype(F32) + received[p].astype(F32) for p in range(4)]
    rest_received = swap_plane(rest_sums)
    other_pieces = column_pieces(others)
    rest_pieces = column_pieces(add_plane(rest_sums[0], rest_received))

    grad_rest, grad_others, table_part, small = call(
        functools.partial(finish_kernel, fast),
        None,
        [VMEM_SPEC] * (2 * n_high + 1),
        [VMEM_SPEC] * 4,
        [
            shaped((rows, HALF_GRAD_COLS), F32),
            shaped((rows, HALF_GRAD_COLS + HALF_SECOND_COLS), F32),
            shaped((rows, 512), F32),
            shaped((4 * n_high, 8, 128), F32),
        ],
        [],
        10**6,
        10**6,
        "finish",
    )(*resident(rest_pieces + other_pieces), scalars)

    gathered = lax.all_to_all(small, "wide", 0, 0)
    beside = swap(gathered, "narrow", 1)
    quarters = []
    if not fast:
        total = lax.psum(small_grads, ("wide", "narrow"))
        quarters = [total.reshape(4, 8, 2, 128).transpose(0, 2, 1, 3).reshape(4, 16, 128)]
    swapped = swap(table_part, "narrow", 1)

    flat_params = [a for group in params for a in group]
    results = call(
        functools.partial(adam_kernel, fast),
        None,
        [VMEM_SPEC] * (32 + len(quarters)),
        [VMEM_SPEC] * 30,
        [shaped((1, 1), F32)] * 3 + [shaped(a.shape, F32) for a in flat_params],
        [pltpu.VMEM((SMALL_ROWS, D), F32)],
        10**6,
        10**6,
        "adam",
    )(grad_rest, grad_others, *resident([swapped, gathered, beside]), *quarters, *flat_params)
    news = list(results[3:])
    for group in (0, 2, 5, 8):
        for member in range(3 * group, 3 * group + 3):
            news[member] = flat(news[member])
    return tuple(a.reshape(()) for a in results[0:3]) + tuple(news)


def solution(mesh):
    placed = (
        P("wide", None, None),
        P("wide", None),
        P("wide"),
        P("wide", None),
        P("wide", None),
        P("wide", None),
        P(None, "wide"),
        P(None, "wide"),
        P(None, "wide"),
        P(None, None, "wide", "narrow"),
        P(None, None, "wide", "narrow"),
        P(None, None, "wide", "narrow"),
        P(None, "narrow", "wide"),
        P(None, "narrow", "wide"),
        P(None, "narrow", "wide"),
        P(None, "wide", "narrow"),
        P(None, "wide", "narrow"),
        P(None, "wide", "narrow"),
        P(None, "narrow"),
        P(None, "narrow"),
        P(None, "narrow"),
        P(None, "narrow", "wide"),
        P(None, "narrow", "wide"),
        P(None, "narrow", "wide"),
        P(),
        P(),
        P(),
        P("wide", "narrow"),
        P("wide", "narrow"),
        P("wide", "narrow"),
        P("wide", None),
        P("wide", None),
        P("wide", None),
    )
    return jax.shard_map(
        per_device,
        mesh=mesh,
        in_specs=placed,
        out_specs=(P(), P(), P()) + placed[6:],
        check_vma=False,
    )
```

```python
import functools

import jax
import jax.numpy as jnp
from jax import lax
from jax.experimental import pallas as pl
from jax.experimental.pallas import tpu as pltpu
from jax.sharding import PartitionSpec as P

D = 256
HEADS = 4
HEAD_DIM = 64
FF = 1024
VOCAB = 512
ACTIONS = 18
GAMES = 26
OBS = 16
FRAMES = 20
STEP_NUMBER = 5
FRAME_TOKENS = 17
LENGTH = 340
ROWS = 896
NVEC = 14

EPS_NORM = 1e-05
BETA_ONE = 0.5
BETA_TWO = 0.5
RATE_TABLE = 0.5
RATE_MATRIX = 0.05
RATE_VECTOR = 0.2
DECAY_RATE = 0.01
EPS_ADAM = 1e-08
CLIP_AT = 0.1

SEQ = 352
KEYS = 384
BLOCK, BLOCKS = 128, 3
TILE = 32
SIDE_ROWS = 32
QUERIES = HEADS * BLOCK
VALUE_ROWS = 80

COL_QKV, COL_PROJ, COL_UP, COL_DOWN, COL_LAYER = 0, 768, 1024, 2048, 3072
HALF_ATTENTION = ((0, 128, 0), (128, 128, 256), (256, 128, 512), (384, 128, COL_PROJ))
HALF_LAYER = HALF_ATTENTION + ((512, 512, COL_UP), (1024, 512, COL_DOWN))
COL_TABLE, COL_SMALL, COL_FIRST = 3072, 3968, 4096
HALF_FIRST = HALF_LAYER + ((1536, 512, COL_TABLE),)
HALF_FIRST_COLS = 2048
COL_HEAD, COL_SECOND = 3072, 3584
HALF_SECOND = HALF_LAYER + ((1536, 256, COL_HEAD),)
HALF_SECOND_COLS = 1792
GRAD_UP, GRAD_DOWN = 0, 1024
HALF_GRAD_FF = ((0, 512, GRAD_UP), (512, 512, GRAD_DOWN))
GRAD_TABLE, GRAD_SMALL = 1024, 1920
HALF_GRAD_REST = HALF_ATTENTION + ((512, 512, GRAD_TABLE),)
HALF_GRAD_COLS = 1024
SMALL_ROWS, SMALL_BIAS, SMALL_SIDE = 32, 14, 22

F32, BF16 = jnp.float32, jnp.bfloat16
MIB = 1024 * 1024


def dot_nn(a, b):
    return lax.dot_general(a, b, (((1,), (0,)), ((), ())), preferred_element_type=F32)


def dot_nt(a, b):
    return lax.dot_general(a, b, (((1,), (1,)), ((), ())), preferred_element_type=F32)


def dot_tn(a, b):
    return lax.dot_general(a, b, (((0,), (0,)), ((), ())), preferred_element_type=F32)


def places(fast):
    wide, core = lax.axis_index("wide"), lax.axis_index("narrow")
    return (wide if fast else 0), core, wide


def tiles(rows, size):
    return [slice(first, first + size) for first in range(0, rows, size)]


def normalise(x):
    centred = x - jnp.mean(x, axis=1, keepdims=True)
    scale = lax.rsqrt(jnp.mean(centred * centred, axis=1, keepdims=True) + EPS_NORM)
    return centred * scale, scale


def keep_norm(rows, xhat, scale, kept):
    kept[0][rows] = xhat.astype(BF16)
    kept[1][rows] = jnp.broadcast_to(scale, (TILE, 128))


def kept_norm(rows, kept):
    scale = kept[1][rows]
    return kept[0][rows].astype(F32), jnp.concatenate([scale, scale], axis=1)


def normalise_back(grad, xhat, scale, gain):
    inner = grad * gain
    mean_one = jnp.mean(inner, axis=1, keepdims=True)
    mean_two = jnp.mean(inner * xhat, axis=1, keepdims=True)
    return scale * (inner - mean_one - xhat * mean_two)


def column_sum(a):
    return jnp.sum(a, axis=0, keepdims=True)


def fold(a):
    return jnp.sum(a.reshape(a.shape[0] // 8, 8, a.shape[1]), axis=0)


def plus(total, a):
    return a if total is None else total + a


def block_lanes(i, h=None):
    if h is None:
        return slice(QUERIES * i, QUERIES * (i + 1))
    return slice(QUERIES * i + BLOCK * h, QUERIES * i + BLOCK * (h + 1))


def head_rows(h):
    return slice(HEAD_DIM * h, HEAD_DIM * (h + 1))


def spread_heads(source, target_ref):
    for h in range(HEADS):
        for i in range(BLOCKS):
            target_ref[head_rows(h), block_lanes(i, h)] = source[
                head_rows(h), BLOCK * i : BLOCK * (i + 1)
            ]


def causal_mask():
    key = lax.broadcasted_iota(jnp.int32, (BLOCK, QUERIES), 0)
    query = lax.broadcasted_iota(jnp.int32, (BLOCK, QUERIES), 1) & (BLOCK - 1)
    return jnp.where(key <= query, 0.0, -1e30)


def assemble(pieces_mine, pieces_other, place, w_ref, halves):
    me, core, _ = place
    is_first = core == 0
    for p in range(4):

        def block(z, _, p=p):
            row = pl.multiple_of((me ^ (4 * z + p)) * 16, 16)
            for src, width, dest in halves:
                mine = pieces_mine[p][z, :, src : src + width]
                other = pieces_other[p][z, :, src : src + width]
                if dest == COL_QKV:
                    mine, other = mine * 0.125, other * 0.125
                w_ref[pl.ds(row, 16), dest : dest + width] = jnp.where(is_first, mine, other)
                w_ref[pl.ds(row, 16), dest + width : dest + 2 * width] = jnp.where(
                    is_first, other, mine
                )
            return 0

        lax.fori_loop(0, 4, block, 0)


def disperse(g_ref, place, keep_ref, send_ref, halves, scaled=True):
    me, core, _ = place
    is_first = core == 0

    def block(i, _):
        p, z = i >> 2, i & 3
        row = pl.multiple_of((me ^ (4 * z + p)) * 16, 16)
        for src, width, dest in halves:
            low = g_ref[pl.ds(row, 16), dest : dest + width]
            high = g_ref[pl.ds(row, 16), dest + width : dest + 2 * width]
            if scaled and dest == COL_QKV:
                low, high = low * 0.125, high * 0.125
            keep_ref[p, z, :, src : src + width] = jnp.where(is_first, low, high).astype(BF16)
            send_ref[p, z, :, src : src + width] = jnp.where(is_first, high, low).astype(BF16)
        return 0

    lax.fori_loop(0, 16, block, 0)


def make_hits(ids, game, hits_ref):
    lane = lax.broadcasted_iota(jnp.int32, (TILE, ROWS), 1)
    for rows in tiles(SEQ, TILE):
        place = lax.broadcasted_iota(jnp.int32, (TILE, 1), 0) + (VOCAB + ACTIONS + GAMES + rows.start)
        hit = (lane == ids[rows]) | (lane == game[rows]) | (lane == place)
        hits_ref[rows] = jnp.where(hit, 1.0, 0.0).astype(BF16)


def gelu_and_slope(up):
    up = up.astype(BF16)
    square = up * up
    half = jax.nn.sigmoid(up * (BF16(1.5957691216057308) + BF16(0.0713548162726) * square))
    hidden = up * half
    slope = BF16(1.5957691216057308) + BF16(0.2140644488178) * square
    return hidden, half + hidden * (BF16(1.0) - half) * slope


def layer_forward(x_ref, w_ref, vec, bias, kept, work):
    qt_ref, kv_ref, p0, p1, p2, r_ref, ot_ref, o_ref = kept[0:8]
    h_ref, gp_ref, a_ref, c_ref = kept[9:13]
    qst_ref, vt_ref, mask_ref, wqt_ref, long_ref, u_ref, y_ref, m_ref = work
    for rows in tiles(SEQ, TILE):
        xhat, scale = normalise(x_ref[rows])
        keep_norm(rows, xhat, scale, kept[14:16])
        normed16 = (xhat * vec[0:1] + vec[1:2]).astype(BF16)
        a_ref[rows], long_ref[rows] = normed16, normed16
    kv_ref[0:SEQ] = dot_nn(long_ref[0:SEQ], w_ref[:, 256:768]).astype(BF16)
    kv_ref[SEQ:KEYS] = jnp.zeros((KEYS - SEQ, 512), BF16)
    qt_ref[...] = dot_nt(wqt_ref[...], long_ref[...]).astype(BF16)
    spread_heads(qt_ref, qst_ref)
    turned = jnp.transpose(kv_ref[:, 256:512])
    for h in range(HEADS):
        vt_ref[VALUE_ROWS * h : VALUE_ROWS * h + HEAD_DIM] = turned[head_rows(h)]
    for i, pt_ref in enumerate((p0, p1, p2)):
        seen, first = BLOCK * (i + 1), BLOCK * i
        scores = dot_nn(kv_ref[0:seen, 0:256], qst_ref[:, block_lanes(i)])
        last = scores[first:] + mask_ref[...]
        peak = jnp.max(last, axis=0, keepdims=True)
        if i:
            peak = jnp.maximum(peak, jnp.max(scores[0:first], axis=0, keepdims=True))
            pt_ref[0:first] = jnp.exp(scores[0:first] - peak).astype(BF16)
        pt_ref[first:seen] = jnp.exp(last - peak).astype(BF16)
        for h in range(HEADS):
            values = vt_ref[VALUE_ROWS * h : VALUE_ROWS * (h + 1), 0:seen]
            out = dot_nn(values, pt_ref[:, BLOCK * h : BLOCK * (h + 1)])
            inverse = 1.0 / out[HEAD_DIM : HEAD_DIM + 1]
            r_ref[h : h + 1, first:seen] = inverse
            ot_ref[head_rows(h), first:seen] = (out[0:HEAD_DIM] * inverse).astype(BF16)
    o_ref[...] = jnp.transpose(ot_ref[...])[0:SEQ]
    y_ref[...] = dot_nt(o_ref[...], w_ref[:, COL_PROJ : COL_PROJ + 256])
    for rows in tiles(SEQ, TILE):
        middle = x_ref[rows] + (y_ref[rows] + vec[2:3])
        m_ref[rows] = middle
        xhat, scale = normalise(middle)
        keep_norm(rows, xhat, scale, (kept[8], kept[13]))
        c_ref[rows] = (xhat * vec[3:4] + vec[4:5]).astype(BF16)
    u_ref[...] = dot_nn(c_ref[...], w_ref[:, COL_UP : COL_UP + FF])
    for rows in tiles(SEQ, TILE):
        for first in range(0, FF, 256):
            cols = slice(first, first + 256)
            h_ref[rows, cols], gp_ref[rows, cols] = gelu_and_slope(u_ref[rows, cols] + bias[:, cols])
    y_ref[...] = dot_nt(h_ref[...], w_ref[:, COL_DOWN : COL_DOWN + FF])


def add_gradient(g_ref, column, left, right):
    g_ref[:, column : column + right.shape[1]] += dot_tn(left, right)


def ff_backward(grad_ref, grad16_ref, w_ref, w_up, w_down, vec, kept, v_ref, v_row, bias_row, work, mid_ref, mid16_refs):
    norm_kept, gp_ref = kept
    du_ref, ones_ref, u_ref, y_ref = work
    u_ref[...] = dot_nn(grad16_ref[...], w_ref[:, w_down : w_down + FF])
    for rows in tiles(SEQ, TILE):
        du_ref[rows] = u_ref[rows].astype(BF16) * gp_ref[rows]
    bias_grad = dot_nn(ones_ref[...], du_ref[...])
    for chunk in range(4):
        v_ref[bias_row + chunk, 0:1] += bias_grad[0:1, 256 * chunk : 256 * chunk + 256]
    y_ref[...] = dot_nt(du_ref[...], w_ref[:, w_up : w_up + FF])
    totals = [None] * 3
    for rows in tiles(SEQ, TILE):
        xhat, scale = kept_norm(rows, norm_kept)
        grad = y_ref[rows]
        mid = grad_ref[rows] + normalise_back(grad, xhat, scale, vec[3:4])
        mid_ref[rows] = mid
        for mid16_ref in mid16_refs:
            mid16_ref[rows] = mid.astype(BF16)
        for i, a in enumerate((mid, grad * xhat, grad)):
            totals[i] = plus(totals[i], fold(a))
    for i in range(3):
        v_ref[v_row + 2 + i] += totals[i]


def attention_backward(mid_ref, mid16_ref, w_ref, vec, kept, v_ref, v_row, work, out_ref):
    norm_kept, (qt_ref, kv_ref, p0, p1, p2, r_ref, ot_ref) = kept
    dost_ref, qst_ref, kt_ref, dst_ref, dqt_ref, dkv_ref, dqkv_ref, proj_ref, y_ref = work
    grad_o = dot_nt(proj_ref[...], mid16_ref[...])
    kt_ref[...] = jnp.transpose(kv_ref[:, 0:256])
    deltas = []
    for h in range(HEADS):
        scaled = grad_o[head_rows(h)] * r_ref[h : h + 1]
        deltas.append(column_sum(scaled * ot_ref[head_rows(h)].astype(F32)))
        scaled = scaled.astype(BF16)
        for i in range(BLOCKS):
            dost_ref[head_rows(h), block_lanes(i, h)] = scaled[:, BLOCK * i : BLOCK * (i + 1)]
    for i, pt_ref in enumerate((p0, p1, p2)):
        seen, first = BLOCK * (i + 1), BLOCK * i
        lanes = block_lanes(i)
        delta = jnp.concatenate([a[:, first:seen] for a in deltas], axis=1)
        grad = dot_nn(kv_ref[0:seen, 256:512], dost_ref[:, lanes])
        dst_ref[0:seen, lanes] = pt_ref[...] * (grad - delta).astype(BF16)
        for h in range(HEADS):
            out = dot_nn(kt_ref[head_rows(h), 0:seen], dst_ref[0:seen, block_lanes(i, h)])
            dqt_ref[head_rows(h), first:seen] = out.astype(BF16)
        for at, left, right in (
            (0, dst_ref[0:seen, lanes], qst_ref),
            (256, pt_ref[...], dost_ref),
        ):
            out = dot_nt(left, right[:, lanes])
            if i:
                dkv_ref[0:first, at : at + 256] += out[0:first]
            dkv_ref[first:seen, at : at + 256] = out[first:]
    dqkv_ref[:, 0:256] = jnp.transpose(dqt_ref[...])[0:SEQ]
    dqkv_ref[:, 256:768] = dkv_ref[0:SEQ].astype(BF16)
    y_ref[...] = dot_nt(dqkv_ref[...], w_ref[:, COL_QKV : COL_QKV + 768])
    totals = [None] * 2
    for rows in tiles(SEQ, TILE):
        xhat, scale = kept_norm(rows, norm_kept)
        grad = y_ref[rows]
        out = mid_ref[rows] + normalise_back(grad, xhat, scale, vec[0:1])
        out_ref[rows] = out.astype(out_ref.dtype)
        for i, a in enumerate((grad * xhat, grad)):
            totals[i] = plus(totals[i], fold(a))
    for i in range(2):
        v_ref[v_row + i] += totals[i]


def own_bias(place, mine, other):
    is_first = place[1] == 0
    return jnp.concatenate(
        [jnp.where(is_first, mine, other), jnp.where(is_first, other, mine)], axis=1
    )


def prepare_kernel(
    fast, games_ref, tokens, actions, valid, rewards, ends, out, out_side, out_hits, x_ref
):
    count = out.shape[0]
    frames = tokens.shape[2]
    base = places(fast)[1] * count
    row = lax.broadcasted_iota(jnp.int32, (SEQ, frames), 0)
    start = lax.broadcasted_iota(jnp.int32, (SEQ, frames), 1) * FRAME_TOKENS
    here = jnp.where((row >= start) & (row < start + FRAME_TOKENS), 1.0, 0.0).astype(BF16)
    coming = jnp.where((row >= start - FRAME_TOKENS) & (row < start), 1.0, 0.0).astype(BF16)
    passed = jnp.sum(jnp.where(row >= start + FRAME_TOKENS, 1, 0), axis=1, keepdims=True)
    place = lax.broadcasted_iota(jnp.int32, (SEQ, 1), 0)
    spot = place - passed * FRAME_TOKENS
    lane = lax.broadcasted_iota(jnp.int32, (SEQ, 24), 1)
    wide_lane = lax.broadcasted_iota(jnp.int32, (SEQ, 128), 1)
    inside = place < LENGTH
    one_frame = (
        lax.broadcasted_iota(jnp.int32, (SIDE_ROWS, frames), 0)
        == lax.broadcasted_iota(jnp.int32, (SIDE_ROWS, frames), 1)
    )
    one_frame = jnp.where(one_frame, 1.0, 0.0).astype(BF16)
    side_lane = lax.broadcasted_iota(jnp.int32, (SIDE_ROWS, 128), 1)
    x_ref[...] = jnp.zeros(x_ref.shape, jnp.int32)
    for s in range(count):
        x_ref[0:OBS] = tokens[base + s]
        x_ref[16:17] = actions[pl.ds(base + s, 1)] + VOCAB
        x_ref[17:18] = valid[pl.ds(base + s, 1)]
        x_ref[18:19] = rewards[pl.ds(base + s, 1)]
        x_ref[19:20] = ends[pl.ds(base + s, 1)] + 3
        high = (x_ref[...] >> 4).astype(F32).astype(BF16)
        low = (x_ref[...] & 15).astype(F32).astype(BF16)
        now = dot_nt(here, high) * 16.0 + dot_nt(here, low)
        soon = dot_nt(coming, high) * 16.0 + dot_nt(coming, low)

        at_end = spot == 16
        packed = jnp.where(lane == spot, now, 0.0)
        target = jnp.where((lane == spot + 1) & (spot < 15), now, 0.0)
        target = target + jnp.where((lane == 0) & at_end, soon, 0.0)
        weight = jnp.where((lane == 17) & (spot < 15), now, 0.0)
        weight = weight + jnp.where((lane == 17) & at_end, soon, 0.0)
        packed = packed + 1024.0 * target + 1048576.0 * weight
        packed = jnp.sum(packed, axis=1, keepdims=True).astype(jnp.int32)
        ids = jnp.where(inside, packed & 1023, -1)
        game = jnp.where(inside, games_ref[base + s] + (VOCAB + ACTIONS), -1)
        target, weight = (packed >> 10) & 1023, packed >> 20
        out[s] = jnp.where(wide_lane == 2, target, jnp.where(wide_lane == 3, weight, 0))
        make_hits(ids, game, out_hits.at[s])
        by_frame = dot_nt(one_frame, high) * 16.0 + dot_nt(one_frame, low)
        result = jnp.zeros((SIDE_ROWS, 128), jnp.int32)
        for c in range(3):
            column = by_frame[:, 17 + c : 18 + c].astype(jnp.int32)
            result = jnp.where(side_lane == c, column, result)
        out_side[s] = result


def start_forward(work, w_ref):
    qst_ref, vt_ref, mask_ref, wqt_ref, long_ref = work[0:5]
    long_ref[SEQ:KEYS] = jnp.zeros((KEYS - SEQ, D), BF16)
    qst_ref[...] = jnp.zeros(qst_ref.shape, BF16)
    vt_ref[...] = jnp.ones(vt_ref.shape, BF16)
    mask_ref[...] = causal_mask()
    wqt_ref[...] = jnp.transpose(w_ref[:, 0:256])


def first_forward_kernel(fast, *refs):
    refs = (places(fast),) + refs
    place, hits_ref, vec_ref, bias_ref, bias_other = refs[0:5]
    mine, other = refs[5:9], refs[9:13]
    w_attention, w_ff, side_out, next_ref = refs[13:17]
    kept = [ref.at[0] for ref in refs[17:33]]
    w_ref, x_ref = refs[33:35]
    work = refs[35:43]
    y_ref, m_ref = work[6:8]

    @pl.when(pl.program_id(0) == 0)
    def _():
        assemble(mine, other, place, w_ref, HALF_FIRST)
        w_attention[...] = w_ref[:, 0:COL_UP]
        w_ff[...] = w_ref[:, COL_UP:COL_TABLE]
        side_out[...] = w_ref[:, COL_SMALL:]
        start_forward(work, w_ref)

    x_ref[...] = dot_nt(hits_ref[0], w_ref[:, COL_TABLE : COL_TABLE + ROWS])
    bias = own_bias(place, bias_ref[0:1], bias_other[0:1])
    vec = vec_ref[0:6]
    layer_forward(x_ref, w_ref, vec, bias, kept, work)
    for rows in tiles(SEQ, TILE):
        next_ref[0, rows] = m_ref[rows] + (y_ref[rows] + vec[5:6])


def codebook_losses(logits, meta):
    weight = meta[:, 3:4].astype(F32)
    peak = jnp.max(logits, axis=1, keepdims=True)
    expanded = jnp.exp(logits - peak)
    total = jnp.sum(expanded, axis=1, keepdims=True)
    hit = lax.broadcasted_iota(jnp.int32, logits.shape, 1) == meta[:, 2:3]
    hit = jnp.where(hit, weight, 0.0)
    return weight * (peak + jnp.log(total)), hit, expanded * (weight / total) - hit


def side_losses(side, meta):
    lane = lax.broadcasted_iota(jnp.int32, side.shape, 1)
    is_reward, is_end = lane < 3, (lane == 3) | (lane == 4)
    is_side = lane < 5
    weight = meta[:, 0:1].astype(F32)
    reward_peak = jnp.max(jnp.where(is_reward, side, -1e30), axis=1, keepdims=True)
    end_peak = jnp.max(jnp.where(is_end, side, -1e30), axis=1, keepdims=True)
    shifted = jnp.where(is_side, side - jnp.where(is_reward, reward_peak, end_peak), 0.0)
    expanded = jnp.where(is_side, jnp.exp(shifted), 0.0)
    reward_total = jnp.sum(jnp.where(is_reward, expanded, 0.0), axis=1, keepdims=True)
    end_total = jnp.sum(jnp.where(is_end, expanded, 0.0), axis=1, keepdims=True)
    hit = (lane == meta[:, 1:2]) | (lane == meta[:, 2:3])
    picked = jnp.sum(jnp.where(hit, side, 0.0), axis=1, keepdims=True)
    terms = reward_peak + jnp.log(reward_total) + end_peak + jnp.log(end_total) - picked
    grad = expanded * jnp.where(is_reward, weight / reward_total, weight / end_total)
    return weight * terms, grad - jnp.where(hit, weight, 0.0), weight


def frame_ends(shape, frame_axis):
    frame = lax.broadcasted_iota(jnp.int32, shape, frame_axis)
    row = lax.broadcasted_iota(jnp.int32, shape, 1 - frame_axis)
    hit = (row == frame * FRAME_TOKENS + OBS) & (frame < FRAMES)
    return jnp.where(hit, 1.0, 0.0).astype(BF16)


def middle_kernel(fast, *refs):
    refs = (places(fast),) + refs
    place, meta_ref, frame_ref, vec_ref, bias_ref, bias_other, side_ref, in_ref = refs[0:8]
    mine, other = refs[8:12], refs[12:16]
    grad_ref, keep_ref, send_ref, v_out, scalar_ref = refs[16:21]
    refs = refs[1:]
    w_ref, g_ref, v_ref = refs[20:23]
    kept = list(refs[23:39])
    forward_work = refs[39:47]
    u_ref, y_ref, m_ref = forward_work[5:8]
    backward_work = list(refs[47:53])
    proj_ref = refs[53]
    du_all, ones_ref, up_ref, up16_all, mid_ref, mid16_ref = refs[54:60]
    last_kept = refs[60:62]
    final_all, logit_ref, dlogit_all, pick_ref, put_ref, mid16_all = refs[62:68]
    o_all, h_all, a_all, c_all, dqkv_all = kept[7], kept[9], kept[11], kept[12], backward_work[5]
    dost_ref = backward_work[0]
    step = pl.program_id(0)

    @pl.when(step == 0)
    def _():
        assemble(mine, other, place, w_ref, HALF_SECOND)
        w_ref[:, COL_SECOND:] = side_ref[...]
        g_ref[...] = jnp.zeros(g_ref.shape, F32)
        v_ref[...] = jnp.zeros(v_ref.shape, F32)
        scalar_ref[...] = jnp.zeros(scalar_ref.shape, F32)
        start_forward(forward_work, w_ref)
        dost_ref[...] = jnp.zeros(dost_ref.shape, BF16)
        proj_ref[...] = jnp.transpose(w_ref[:, COL_PROJ : COL_PROJ + 256])
        ones_ref[...] = jnp.ones(ones_ref.shape, BF16)
        mid16_ref[SEQ:KEYS] = jnp.zeros((KEYS - SEQ, D), BF16)
        pick_ref[...] = frame_ends((SIDE_ROWS, SEQ), 0)
        put_ref[...] = frame_ends((SEQ, SIDE_ROWS), 1)

    here = pl.ds(pl.multiple_of((step & 1) * SEQ, 32), SEQ)
    for i in (7, 9, 11, 12):
        kept[i] = kept[i].at[here]
    gp_ref = kept[10]
    backward_work[5] = dqkv_all.at[here]
    du_ref, up16_ref, pair16_ref = du_all.at[here], up16_all.at[here], mid16_all.at[here]
    final_ref, dlogit_ref = final_all.at[here], dlogit_all.at[here]
    x_ref = in_ref.at[0]
    vec = vec_ref[6:12]
    bias = own_bias(place, bias_ref[1:2], bias_other[1:2])
    layer_forward(x_ref, w_ref, vec, bias, kept, forward_work)

    gain, offset = vec_ref[12:13], vec_ref[13:14]
    for rows in tiles(SEQ, TILE):
        last = m_ref[rows] + (y_ref[rows] + vec[5:6])
        xhat, scale = normalise(last)
        keep_norm(rows, xhat, scale, last_kept)
        final_ref[rows] = (xhat * gain + offset).astype(BF16)
    cols_head = slice(COL_HEAD, COL_HEAD + VOCAB + 128)
    logit_ref[...] = dot_nn(final_ref[...], w_ref[:, COL_HEAD : COL_HEAD + VOCAB])
    logs, picked = None, None
    for rows in tiles(SEQ, TILE):
        logits = logit_ref[rows]
        log, hit, grad = codebook_losses(logits, meta_ref[0, rows])
        dlogit_ref[rows, :VOCAB] = grad.astype(BF16)
        logs, picked = plus(logs, log), plus(picked, fold(hit * logits))
    acting = dot_nn(pick_ref[...], final_ref[...]).astype(BF16)
    side = dot_nn(acting, w_ref[:, COL_HEAD + VOCAB : COL_HEAD + VOCAB + 128])
    side_loss, grad, weight = side_losses(side, frame_ref[0])
    dlogit_ref[:, VOCAB:] = dot_nn(put_ref[...], grad.astype(BF16)).astype(BF16)
    loss = column_sum(logs) + column_sum(side_loss)
    loss = loss - jnp.sum(column_sum(picked), axis=1, keepdims=True)
    valid = column_sum(weight)
    scalar_lane = lax.broadcasted_iota(jnp.int32, (8, 128), 1)
    scalar_row = lax.broadcasted_iota(jnp.int32, (8, 128), 0) == 0
    scalar_ref[...] += jnp.where(
        scalar_row,
        jnp.where(scalar_lane == 0, loss, jnp.where(scalar_lane == 1, valid, 0.0)),
        0.0,
    )
    y_ref[...] = dot_nt(dlogit_ref[...], w_ref[:, cols_head])
    totals = [None] * 3
    for rows in tiles(SEQ, TILE):
        xhat, scale = kept_norm(rows, last_kept)
        grad = y_ref[rows]
        up = normalise_back(grad, xhat, scale, gain)
        up_ref[rows] = up
        up16_ref[rows] = up.astype(BF16)
        for i, a in enumerate((up, grad * xhat, grad)):
            totals[i] = plus(totals[i], fold(a))
    for i in range(3):
        v_ref[11 + i] += totals[i]
    ff_backward(
        up_ref,
        up16_ref,
        w_ref,
        COL_UP,
        COL_DOWN,
        vec,
        ((kept[8], kept[13]), gp_ref),
        v_ref,
        6,
        SMALL_BIAS + 4,
        (du_ref, ones_ref, u_ref, y_ref),
        mid_ref,
        (mid16_ref, pair16_ref),
    )
    attention_backward(
        mid_ref,
        mid16_ref,
        w_ref,
        vec,
        (kept[14:16], kept[0:7]),
        v_ref,
        6,
        (dost_ref, forward_work[0]) + tuple(backward_work[1:]) + (proj_ref, y_ref),
        grad_ref.at[0],
    )

    @pl.when(step & 1 == 1)
    def _():
        add_gradient(g_ref, COL_QKV, a_all[...], dqkv_all[...])
        add_gradient(g_ref, COL_PROJ, mid16_all[...], o_all[...])
        add_gradient(g_ref, COL_UP, c_all[...], du_all[...])
        add_gradient(g_ref, COL_DOWN, up16_all[...], h_all[...])
        add_gradient(g_ref, COL_HEAD, final_all[...], dlogit_all[...])

    @pl.when(step == pl.num_programs(0) - 1)
    def _():
        disperse(g_ref, place, keep_ref, send_ref, HALF_SECOND)
        side = jnp.transpose(g_ref[:, COL_SECOND:])
        for i in range(5):
            v_ref[SMALL_SIDE + i, 0:1] = side[i : i + 1]
        v_out[...] = v_ref[...]


def ff_backward_kernel(fast, *refs):
    vec_ref, w_ref, grad_ref, v_in = refs[0:4]
    xhat_ref, scale_ref, h_ref, gp_ref, c_ref = [ref.at[0] for ref in refs[4:9]]
    mid_ref, keep_ref, send_ref, v_out = refs[9:13]
    g_ref, v_ref, grad16_ref, du_ref, ones_ref, u_ref, y_ref = refs[13:20]
    step = pl.program_id(0)

    @pl.when(step == 0)
    def _():
        g_ref[...] = jnp.zeros(g_ref.shape, F32)
        v_ref[...] = v_in[...]
        ones_ref[...] = jnp.ones(ones_ref.shape, BF16)

    total = None
    for rows in tiles(SEQ, TILE):
        grad = grad_ref[0, rows]
        grad16_ref[rows] = grad.astype(BF16)
        total = plus(total, fold(grad))
    v_ref[5] += total
    ff_backward(
        grad_ref.at[0],
        grad16_ref,
        w_ref,
        GRAD_UP,
        GRAD_DOWN,
        vec_ref[0:6],
        ((xhat_ref, scale_ref), gp_ref),
        v_ref,
        0,
        SMALL_BIAS,
        (du_ref, ones_ref, u_ref, y_ref),
        mid_ref.at[0],
        (),
    )
    add_gradient(g_ref, GRAD_DOWN, grad16_ref[...], h_ref[...])
    add_gradient(g_ref, GRAD_UP, c_ref[...], du_ref[...])

    @pl.when(step == pl.num_programs(0) - 1)
    def _():
        disperse(g_ref, places(fast), keep_ref, send_ref, HALF_GRAD_FF, False)
        v_out[...] = v_ref[...]


def attention_backward_kernel(fast, *refs):
    vec_ref, w_ref, mid_ref, v_in = refs[0:4]
    kept = [ref.at[0] for ref in refs[4:13]]
    o_all, a_all, hits_all = refs[13:16]
    keep_ref, send_ref, v_out = refs[17:20]
    g_ref, v_ref, mid16_ref, mid16_all, out16_all, dqkv_all = refs[20:26]
    work = list(refs[26:34])
    dost_ref, qst_ref, proj_ref = work[0], work[1], work[6]
    step = pl.program_id(0)

    @pl.when(step == 0)
    def _():
        v_ref[...] = v_in[...]
        dost_ref[...] = jnp.zeros(dost_ref.shape, BF16)
        qst_ref[...] = jnp.zeros(qst_ref.shape, BF16)
        proj_ref[...] = jnp.transpose(w_ref[:, COL_PROJ : COL_PROJ + 256])
        mid16_ref[SEQ:KEYS] = jnp.zeros((KEYS - SEQ, D), BF16)

    here = pl.ds(pl.multiple_of(step * SEQ, 32), SEQ)
    all16_ref = mid16_all.at[here]
    spread_heads(kept[2], qst_ref)
    for rows in tiles(SEQ, TILE):
        mid16 = mid_ref[0, rows].astype(BF16)
        mid16_ref[rows], all16_ref[rows] = mid16, mid16
    work.insert(6, dqkv_all.at[here])
    attention_backward(
        mid_ref.at[0],
        mid16_ref,
        w_ref,
        vec_ref[0:6],
        (kept[0:2], kept[2:9]),
        v_ref,
        0,
        work,
        out16_all.at[here],
    )

    @pl.when(step == pl.num_programs(0) - 1)
    def _():
        g_ref[:, COL_QKV : COL_QKV + 768] = dot_tn(a_all[...], dqkv_all[...])
        g_ref[:, COL_PROJ : COL_PROJ + 256] = dot_tn(mid16_all[...], o_all[...])
        g_ref[:, GRAD_TABLE : GRAD_TABLE + ROWS] = dot_tn(out16_all[...], hits_all[...])
        small = jnp.sum(v_ref[...], axis=1)
        v_out[...] = small
        for block in range(16):
            quarter = small[8 * (block // 4) : 8 * (block // 4) + 8]
            g_ref[16 * block : 16 * block + 8, GRAD_SMALL:] = quarter[:, 0:128]
            g_ref[16 * block + 8 : 16 * block + 16, GRAD_SMALL:] = quarter[:, 128:256]
        disperse(g_ref, places(fast), keep_ref, send_ref, HALF_GRAD_REST)


def pack_layer(attn, proj, up, down, layer, out):
    for j in range(3):
        out[:, 128 * j : 128 * j + 128] = attn[layer, j].astype(BF16)
    out[:, 384:512] = proj[layer].astype(BF16)
    out[:, 512:1024] = up[layer].astype(BF16)
    out[:, 1024:1536] = down[layer].astype(BF16)


def pack_second_kernel(attn, proj, up, down, head, second):
    pack_layer(attn, proj, up, down, 0, second)
    second[:, 1536:1792] = head[...].astype(BF16)


def pack_kernel(fast, attn, proj, up, down, table, side, first, pad_ref):
    pack_layer(attn, proj, up, down, 0, first)
    rows = side.shape[1]
    eye = (
        lax.broadcasted_iota(jnp.int32, (rows, rows), 0)
        == lax.broadcasted_iota(jnp.int32, (rows, rows), 1)
    )
    eye = jnp.where(eye, 1.0, 0.0).astype(BF16)
    pad_ref[...] = jnp.zeros(pad_ref.shape, F32)
    pad_ref[:, 0:5] = dot_nt(eye, side[...].astype(BF16))
    high = jnp.concatenate([table[:, 512:896], pad_ref[...]], axis=1)
    first[:, 1536:2048] = jnp.where(places(fast)[1] == 0, table[:, 0:512], high).astype(BF16)


def finish_kernel(fast, *refs):
    count = (len(refs) - 5) // 2
    scalar_ref = refs[2 * count]
    out_rest, out_other, out_table, out_small = refs[2 * count + 1 :]
    square = jnp.zeros((1, 1), F32)
    for pieces, out in ((refs[0:count], out_rest), (refs[count : 2 * count], out_other)):
        total = pieces[0][...]
        for piece in pieces[1:]:
            total = total + piece[...].astype(F32)
        out[...] = total
        square = square + column_sum(jnp.sum(total * total, axis=1, keepdims=True))
    small = out_rest[:, 896:1024]
    extra = column_sum(jnp.sum(small * small, axis=1, keepdims=True))
    square = square - jnp.where(places(fast)[1] == 0, 0.0, extra)
    out_table[...] = out_rest[:, 512:1024]
    lane = lax.broadcasted_iota(jnp.int32, (8, 128), 1)
    row = lax.broadcasted_iota(jnp.int32, (8, 128), 0)
    message = scalar_ref[...] + jnp.where((row == 0) & (lane == 2), square, 0.0)
    if fast:
        spot = places(fast)[2] & 3
        part = jnp.where(spot & 1 == 0, small[0:4], small[4:8])
        part = jnp.where(spot & 2 == 0, part, jnp.where(spot & 1 == 0, small[8:12], small[12:16]))
        message = jnp.concatenate([part, message[0:4]], axis=0)
    for i in range(out_small.shape[0]):
        out_small[i] = message


def adam_rule(weight, moment, second, gradient, step_rate, decay_rate):
    moment_new = BETA_ONE * moment + (1.0 - BETA_ONE) * gradient
    second_new = BETA_TWO * second + (1.0 - BETA_TWO) * gradient * gradient
    moment_hat = moment_new / (1.0 - BETA_ONE**STEP_NUMBER)
    second_hat = second_new / (1.0 - BETA_TWO**STEP_NUMBER)
    weight_new = weight - step_rate * (
        moment_hat / (jnp.sqrt(second_hat) + EPS_ADAM) + decay_rate * weight
    )
    return (weight_new, moment_new, second_new)


def adam_kernel(fast, rest, others, swapped, gathered, beside, *refs):
    rows = rest.shape[0]
    _, core, wide = places(fast)
    is_first = core == 0
    if fast:
        small_parts = jnp.where(is_first, beside[...], gathered[...])
        quarters = [
            jnp.concatenate([small_parts[4 * z + p, 0:4] for p in range(4)], axis=0)
            for z in range(4)
        ]
    else:
        quarters = [refs[0][z] for z in range(4)]
        refs = refs[1:]
    params = [refs[3 * i : 3 * i + 3] for i in range(9)]
    loss_ref, valid_ref, norm_ref = refs[27:30]
    outs = [refs[30 + 3 * i : 33 + 3 * i] for i in range(9)]
    small_ref = refs[57]
    for z in range(4):
        small_ref[8 * z : 8 * z + 8, 0:128] = quarters[z][0:8]
        small_ref[8 * z : 8 * z + 8, 128:256] = quarters[z][8:16]
    sums = []
    for source in (gathered, beside):
        line = 4 if fast else 0
        total = source[0, line : line + 1]
        for i in range(1, source.shape[0]):
            total = total + source[i, line : line + 1]
        sums.append(total)
    scalars = sums[0] + sums[1]
    small = small_ref[...]
    loss, valid, square = scalars[:, 0:1], scalars[:, 1:2], scalars[:, 2:3]
    square = square + column_sum(jnp.sum(small * small, axis=1, keepdims=True))
    inverse = 1.0 / valid
    norm = jnp.sqrt(square) * inverse
    loss_ref[...], valid_ref[...], norm_ref[...] = loss, valid, norm
    factor = jnp.minimum(1.0, CLIP_AT / (norm + 1e-06)) * inverse
    table, attn, proj, up, bias, down, vectors, head, side = range(9)

    def update(which, index, gradient, step_rate, decay_rate):
        news = adam_rule(
            *(ref[index] for ref in params[which]), factor * gradient, step_rate, decay_rate
        )
        for ref, new in zip(outs[which], news):
            ref[index] = new

    layers = ((rest, others, 1792), (others, others, 512))
    for layer, (attention, feed, at) in enumerate(layers):
        for j in range(3):
            update(attn, (layer, j), attention[:, 128 * j : 128 * j + 128], RATE_MATRIX, DECAY_RATE)
        update(proj, (layer,), attention[:, 384:512], RATE_MATRIX, DECAY_RATE)
        update(up, (layer,), feed[:, at : at + 512], RATE_MATRIX, DECAY_RATE)
        update(down, (layer,), feed[:, at + 512 : at + 1024], RATE_MATRIX, DECAY_RATE)
        for i in range(2):
            low = SMALL_BIAS + 4 * layer + i
            row = jnp.where(is_first, small[low : low + 1], small[low + 2 : low + 3])
            index = (slice(layer, layer + 1), slice(256 * i, 256 * i + 256))
            update(bias, index, row, RATE_VECTOR, 0.0)
    whole = (slice(None), slice(None))
    update(head, whole, others[:, 1536:1792], RATE_MATRIX, DECAY_RATE)
    mine, theirs = rest[:, 512:1024], swapped[:, 0:512]
    low, high = jnp.where(is_first, mine, theirs), jnp.where(is_first, theirs, mine)
    update(table, (slice(None), slice(0, 512)), low, RATE_TABLE, DECAY_RATE)
    update(table, (slice(None), slice(512, 896)), high[:, 0:384], RATE_TABLE, DECAY_RATE)
    update(vectors, whole, small[0:NVEC], RATE_VECTOR, 0.0)
    turned = pltpu.roll(small[SMALL_SIDE : SMALL_SIDE + 8], lax.rem(D - wide * rows, D), 1)
    update(side, whole, turned[0:5, 0:rows], RATE_MATRIX, DECAY_RATE)


def swap(a, axis, distance):
    size = lax.axis_size(axis)
    return lax.ppermute(a, axis, [(i, i ^ distance) for i in range(size)])


def swap_column(piece, n_high):
    return [piece] + [swap(piece, "wide", 4 * k) for k in range(1, n_high)]


def gather_plane(column):
    return [column] + [swap(column, "wide", p) for p in range(1, 4)]


def gather_cores(mine):
    return [swap(a, "narrow", 1) for a in mine]


def in_blocks(parts, wide):
    n_high, rows, cols = parts[0].shape
    if rows == 16:
        return parts
    whole = jnp.stack(parts, axis=1).reshape(4 * n_high, rows, cols)
    whole = whole[wide ^ jnp.arange(4 * n_high)].reshape(4, 4, 16, cols)
    return [whole[:, p] for p in range(4)]


def in_pieces(blocks, wide, n_high):
    cols = blocks.shape[-1]
    if n_high == 4:
        return blocks
    rows = 64 // n_high
    whole = blocks.transpose(1, 0, 2, 3).reshape(4 * n_high, rows, cols)
    whole = whole[wide ^ jnp.arange(4 * n_high)]
    return whole.reshape(n_high, 4, rows, cols).transpose(1, 0, 2, 3)


def add_cores(keep, send, wide, n_high):
    keep, send = in_pieces(keep, wide, n_high), in_pieces(send, wide, n_high)
    received = swap(send, "narrow", 1)
    return [keep[p].astype(F32) + received[p].astype(F32) for p in range(4)]


def swap_plane(sums):
    return [swap(sums[p].astype(BF16), "wide", p) for p in range(1, 4)]


def add_plane(own, received):
    for a in received:
        own = own + a.astype(F32)
    return own


def column_pieces(own):
    return [own[0]] + [swap(own[k].astype(BF16), "wide", 4 * k) for k in range(1, own.shape[0])]


def resident(arrays):
    return [pltpu.with_memory_space_constraint(a, pltpu.VMEM) for a in arrays]


def in_hbm(arrays):
    return [pltpu.with_memory_space_constraint(a, pltpu.HBM) for a in arrays]


def full_spec(a):
    return pl.BlockSpec(a.shape, lambda *_: (0,) * len(a.shape))


def row_spec(shape):
    return pl.BlockSpec((1,) + shape, lambda i: (i,) + (0,) * len(shape))


def shaped(shape, dtype):
    return jax.ShapeDtypeStruct(shape, dtype)


VMEM_SPEC = pl.BlockSpec(memory_space=pltpu.VMEM)
ANY_SPEC = pl.BlockSpec(memory_space=pl.ANY)
SMEM_SPEC = pl.BlockSpec(memory_space=pltpu.SMEM)


VMEM_MIB = {
    "pack": 58,
    "pack_second": 58,
    "prepare": 24,
    "first_forward": 22,
    "middle": 28,
    "ff_backward": 15,
    "attention_backward": 22,
    "finish": 24,
    "adam": 20,
}


def call(kernel, grid, in_specs, out_specs, out_shape, scratch, flops, bytes_accessed, name):
    extra = {"grid": grid} if grid else {}
    return pl.pallas_call(
        kernel,
        in_specs=in_specs,
        out_specs=out_specs,
        out_shape=out_shape,
        scratch_shapes=scratch,
        compiler_params=pltpu.CompilerParams(vmem_limit_bytes=VMEM_MIB[name] * MIB),
        cost_estimate=pl.CostEstimate(
            flops=flops, bytes_accessed=bytes_accessed, transcendentals=0
        ),
        name=name,
        **extra,
    )


KEPT = (
    ((D, KEYS), BF16),
    ((KEYS, 512), BF16),
    ((BLOCK, QUERIES), BF16),
    ((2 * BLOCK, QUERIES), BF16),
    ((3 * BLOCK, QUERIES), BF16),
    ((8, KEYS), F32),
    ((D, KEYS), BF16),
    ((SEQ, D), BF16),
    ((SEQ, D), BF16),
    ((SEQ, FF), BF16),
    ((SEQ, FF), BF16),
    ((SEQ, D), BF16),
    ((SEQ, D), BF16),
    ((SEQ, 128), F32),
    ((SEQ, D), BF16),
    ((SEQ, 128), F32),
)
FORWARD_WORK = [
    pltpu.VMEM((D, BLOCKS * QUERIES), BF16),
    pltpu.VMEM((HEADS * VALUE_ROWS, KEYS), BF16),
    pltpu.VMEM((BLOCK, QUERIES), F32),
    pltpu.VMEM((D, D), BF16),
    pltpu.VMEM((KEYS, D), BF16),
    pltpu.VMEM((SEQ, FF), F32),
    pltpu.VMEM((SEQ, D), F32),
    pltpu.VMEM((SEQ, D), F32),
]
BACKWARD_WORK = [
    pltpu.VMEM((D, BLOCKS * QUERIES), BF16),
    pltpu.VMEM((D, BLOCKS * QUERIES), BF16),
    pltpu.VMEM((D, KEYS), BF16),
    pltpu.VMEM((KEYS, BLOCKS * QUERIES), BF16),
    pltpu.VMEM((D, KEYS), BF16),
    pltpu.VMEM((KEYS, 512), F32),
    pltpu.VMEM((SEQ, 768), BF16),
]
PROJ_WORK = pltpu.VMEM((D, D), BF16)
ONES_WORK = pltpu.VMEM((16, SEQ), BF16)


def per_device(
    tokens,
    actions,
    game_ids,
    valid_steps,
    rewards,
    end_flags,
    embed_table,
    table_first,
    table_second,
    attn_weight,
    attn_first,
    attn_second,
    proj_weight,
    proj_first,
    proj_second,
    up_weight,
    up_first,
    up_second,
    up_bias,
    bias_first,
    bias_second,
    down_weight,
    down_first,
    down_second,
    vectors,
    vectors_first,
    vectors_second,
    head_weight,
    head_first,
    head_second,
    side_weight,
    side_first,
    side_second,
):
    n_high = lax.axis_size("wide") // 4
    wide = lax.axis_index("wide")
    rows = side_weight.shape[0]
    fast = rows == 16

    def flat(a):
        return jnp.swapaxes(a, -1, -2)

    params = (
        (flat(embed_table), flat(table_first), flat(table_second)),
        (attn_weight, attn_first, attn_second),
        (flat(proj_weight), flat(proj_first), flat(proj_second)),
        (up_weight, up_first, up_second),
        (up_bias, bias_first, bias_second),
        (flat(down_weight), flat(down_first), flat(down_second)),
        (vectors, vectors_first, vectors_second),
        (head_weight, head_first, head_second),
        (flat(side_weight), flat(side_first), flat(side_second)),
    )
    table, attn, proj, up, _, down, _, head, side = (group[0] for group in params)

    def one_layer(layer):
        return [
            pl.BlockSpec((1,) + a.shape[1:], lambda i, n=len(a.shape): (layer,) + (0,) * (n - 1))
            for a in (attn, proj, up, down)
        ]

    piece_first = call(
        functools.partial(pack_kernel, fast),
        (1,),
        one_layer(0) + [VMEM_SPEC] * 2,
        VMEM_SPEC,
        shaped((rows, HALF_FIRST_COLS), BF16),
        [pltpu.VMEM((rows, 128), F32)],
        10**6,
        10**6,
        "pack",
    )(attn, proj, up, down, table, side)
    piece_second = call(
        pack_second_kernel,
        (1,),
        one_layer(1) + [VMEM_SPEC],
        VMEM_SPEC,
        shaped((rows, HALF_SECOND_COLS), BF16),
        [],
        10**6,
        10**6,
        "pack_second",
    )(attn, proj, up, down, head)
    other_bias = swap(up_bias, "narrow", 1)
    column = swap_column(piece_first, n_high)

    count = tokens.shape[0] // lax.axis_size("narrow")
    meta, frame_meta, hits = call(
        functools.partial(prepare_kernel, fast),
        None,
        [SMEM_SPEC] + [VMEM_SPEC] * 5,
        [VMEM_SPEC] * 3,
        [
            shaped((count, SEQ, 128), jnp.int32),
            shaped((count, SIDE_ROWS, 128), jnp.int32),
            shaped((count, SEQ, ROWS), BF16),
        ],
        [pltpu.VMEM((24, FRAMES), jnp.int32)],
        10**6,
        10**6,
        "prepare",
    )(*in_hbm([game_ids, flat(tokens), actions, valid_steps, rewards, end_flags]))
    column, other_bias, hits = lax.optimization_barrier((column, other_bias, hits))
    first_column = jnp.stack(column)
    first_mine = gather_plane(first_column)
    own, piece_second = lax.optimization_barrier((swap(first_column, "narrow", 1), piece_second))
    first_other = [own] + gather_cores(first_mine[1:])
    near = swap(piece_second, "wide", 4)
    near, far_piece = lax.optimization_barrier((near, piece_second))
    second_column = [piece_second, near, swap(piece_second, "wide", 8)]
    second_column += [swap(far_piece, "wide", 4 * k) for k in range(3, n_high)]
    second_column, across = lax.optimization_barrier(
        (jnp.stack(second_column), first_other[3])
    )
    first_other = first_other[0:3] + [across]
    second_mine = gather_plane(second_column)
    first_parts = in_blocks(first_mine, wide) + in_blocks(first_other, wide)

    kept_specs = [row_spec(shape) for shape, _ in KEPT]
    kept_shapes = [shaped((count,) + shape, dtype) for shape, dtype in KEPT]
    row_f32 = shaped((count, SEQ, D), F32)
    meta_spec = row_spec((SEQ, 128))
    vec_specs = [full_spec(vectors), full_spec(up_bias), full_spec(up_bias)]
    w_attention_spec = pl.BlockSpec((D, 1024), lambda i: (0, 0))
    w_ff_spec = pl.BlockSpec((D, 2048), lambda i: (0, 0))
    side_spec = pl.BlockSpec((D, 128), lambda i: (0, 0))
    hits_spec = row_spec((SEQ, ROWS))
    results = call(
        functools.partial(first_forward_kernel, fast),
        (count,),
        [hits_spec] + vec_specs + [VMEM_SPEC] * 8,
        [w_attention_spec, w_ff_spec, side_spec, row_spec((SEQ, D))] + kept_specs,
        [shaped((D, 1024), BF16), shaped((D, 2048), BF16), shaped((D, 128), BF16), row_f32]
        + kept_shapes,
        [pltpu.VMEM((D, COL_FIRST), BF16), pltpu.VMEM((SEQ, D), F32)] + FORWARD_WORK,
        4 * 10**9,
        20 * 10**6,
        "first_forward",
    )(hits, *in_hbm([vectors, up_bias, other_bias]), *resident(first_parts))
    w_attention, w_ff, side_copy, stream = results[0:4]
    kept = results[4:]
    received, side_copy = lax.optimization_barrier((second_mine[1:], side_copy))
    second_mine = second_mine[0:1] + received
    second_other = gather_cores(second_mine)
    second_parts = in_blocks(second_mine, wide) + in_blocks(second_other, wide)

    def blocks(cols):
        return pl.BlockSpec((4, 4, 16, cols), lambda i: (0, 0, 0, 0))

    def block_shapes(cols):
        return [shaped((4, 4, 16, cols), BF16)] * 2

    small_spec = pl.BlockSpec((SMALL_ROWS, 8, D), lambda i: (0, 0, 0))
    small_shape = shaped((SMALL_ROWS, 8, D), F32)
    small_scratch = pltpu.VMEM((SMALL_ROWS, 8, D), F32)
    scalar_spec = pl.BlockSpec((8, 128), lambda i: (0, 0))
    grad_stream, keep_second, send_second, small_grads, scalars = call(
        functools.partial(middle_kernel, fast),
        (count,),
        [meta_spec, row_spec((SIDE_ROWS, 128))]
        + vec_specs
        + [side_spec, row_spec((SEQ, D))]
        + [VMEM_SPEC] * 8,
        [row_spec((SEQ, D))] + [blocks(HALF_SECOND_COLS)] * 2 + [small_spec, scalar_spec],
        [row_f32] + block_shapes(HALF_SECOND_COLS) + [small_shape, shaped((8, 128), F32)],
        [
            pltpu.VMEM((D, COL_SECOND + 128), BF16),
            pltpu.VMEM((D, COL_SECOND + 128), F32),
            small_scratch,
        ]
        + [pltpu.VMEM(shape, dtype) for shape, dtype in KEPT[0:7]]
        + [pltpu.VMEM((2 * SEQ, D), BF16), pltpu.VMEM(*KEPT[8])]
        + [pltpu.VMEM((2 * SEQ, FF), BF16), pltpu.VMEM(*KEPT[10])]
        + [pltpu.VMEM((2 * SEQ, D), BF16)] * 2
        + [pltpu.VMEM(*a) for a in KEPT[13:16]]
        + FORWARD_WORK
        + BACKWARD_WORK[0:1]
        + BACKWARD_WORK[2:6]
        + [pltpu.VMEM((2 * SEQ, 768), BF16)]
        + [
            PROJ_WORK,
            pltpu.VMEM((2 * SEQ, FF), BF16),
            ONES_WORK,
            pltpu.VMEM((SEQ, D), F32),
            pltpu.VMEM((2 * SEQ, D), BF16),
            pltpu.VMEM((SEQ, D), F32),
            pltpu.VMEM((KEYS, D), BF16),
            pltpu.VMEM((SEQ, D), BF16),
            pltpu.VMEM((SEQ, 128), F32),
            pltpu.VMEM((2 * SEQ, D), BF16),
            pltpu.VMEM((SEQ, VOCAB), F32),
            pltpu.VMEM((2 * SEQ, VOCAB + 128), BF16),
            pltpu.VMEM((SIDE_ROWS, SEQ), BF16),
            pltpu.VMEM((SEQ, SIDE_ROWS), BF16),
            pltpu.VMEM((2 * SEQ, D), BF16),
        ],
        15 * 10**9,
        20 * 10**6,
        "middle",
    )(
        *in_hbm([meta, frame_meta, vectors, up_bias, other_bias]),
        side_copy,
        stream,
        *resident(second_parts),
    )
    second_sums = add_cores(keep_second, send_second, wide, n_high)

    def joined(a):
        return a.reshape((count * a.shape[1],) + a.shape[2:])

    kept_ff = (kept[8], kept[13], kept[9], kept[10], kept[12])
    grad_mid, keep_ff, send_ff, small_grads = call(
        functools.partial(ff_backward_kernel, fast),
        (count,),
        [full_spec(vectors), w_ff_spec, row_spec((SEQ, D)), small_spec]
        + [row_spec(a.shape[1:]) for a in kept_ff],
        [row_spec((SEQ, D))] + [blocks(HALF_GRAD_COLS)] * 2 + [small_spec],
        [row_f32] + block_shapes(HALF_GRAD_COLS) + [small_shape],
        [
            pltpu.VMEM((D, 2048), F32),
            small_scratch,
            pltpu.VMEM((SEQ, D), BF16),
            pltpu.VMEM((SEQ, FF), BF16),
            ONES_WORK,
            pltpu.VMEM((SEQ, FF), F32),
            pltpu.VMEM((SEQ, D), F32),
        ],
        4 * 10**9,
        10 * 10**6,
        "ff_backward",
    )(*in_hbm([vectors]), w_ff, grad_stream, small_grads, *kept_ff)
    ff_sums = add_cores(keep_ff, send_ff, wide, n_high)
    other_sums = [jnp.concatenate(pair, axis=-1) for pair in zip(second_sums, ff_sums)]
    others_received = swap_plane(other_sums)
    kept_attention = (kept[14], kept[15]) + tuple(kept[0:7])
    joined_attention = [joined(kept[7]), joined(kept[11]), joined(hits)]
    keep_rest, send_rest, small_grads = call(
        functools.partial(attention_backward_kernel, fast),
        (count,),
        [full_spec(vectors), w_attention_spec, row_spec((SEQ, D)), small_spec]
        + [row_spec(a.shape[1:]) for a in kept_attention]
        + [VMEM_SPEC] * 3
        + [ANY_SPEC],
        [blocks(HALF_GRAD_COLS)] * 2 + [pl.BlockSpec((SMALL_ROWS, D), lambda i: (0, 0))],
        block_shapes(HALF_GRAD_COLS) + [shaped((SMALL_ROWS, D), F32)],
        [pltpu.VMEM((D, 2048), F32), small_scratch, pltpu.VMEM((KEYS, D), BF16)]
        + [pltpu.VMEM((count * SEQ, D), BF16)] * 2
        + [pltpu.VMEM((count * SEQ, 768), BF16)]
        + BACKWARD_WORK[0:6]
        + [PROJ_WORK, pltpu.VMEM((SEQ, D), F32)],
        6 * 10**9,
        20 * 10**6,
        "attention_backward",
    )(
        *in_hbm([vectors]),
        w_attention,
        grad_mid,
        small_grads,
        *kept_attention,
        *joined_attention,
        other_sums[0],
    )
    others_received, keep_rest = lax.optimization_barrier((others_received, keep_rest))
    others = add_plane(other_sums[0], others_received)
    keep_rest = in_pieces(keep_rest, wide, n_high)
    received = swap(in_pieces(send_rest, wide, n_high), "narrow", 1)
    others, received = lax.optimization_barrier((others, received))
    rest_sums = [keep_rest[p].astype(F32) + received[p].astype(F32) for p in range(4)]
    rest_received = swap_plane(rest_sums)
    other_pieces = column_pieces(others)
    rest_pieces = column_pieces(add_plane(rest_sums[0], rest_received))

    grad_rest, grad_others, table_part, small = call(
        functools.partial(finish_kernel, fast),
        None,
        [VMEM_SPEC] * (2 * n_high + 1),
        [VMEM_SPEC] * 4,
        [
            shaped((rows, HALF_GRAD_COLS), F32),
            shaped((rows, HALF_GRAD_COLS + HALF_SECOND_COLS), F32),
            shaped((rows, 512), F32),
            shaped((4 * n_high, 8, 128), F32),
        ],
        [],
        10**6,
        10**6,
        "finish",
    )(*resident(rest_pieces + other_pieces), scalars)

    gathered = lax.all_to_all(small, "wide", 0, 0)
    beside = swap(gathered, "narrow", 1)
    quarters = []
    if not fast:
        total = lax.psum(small_grads, ("wide", "narrow"))
        quarters = [total.reshape(4, 8, 2, 128).transpose(0, 2, 1, 3).reshape(4, 16, 128)]
    swapped = swap(table_part, "narrow", 1)

    flat_params = [a for group in params for a in group]
    results = call(
        functools.partial(adam_kernel, fast),
        None,
        [VMEM_SPEC] * (32 + len(quarters)),
        [VMEM_SPEC] * 30,
        [shaped((1, 1), F32)] * 3 + [shaped(a.shape, F32) for a in flat_params],
        [pltpu.VMEM((SMALL_ROWS, D), F32)],
        10**6,
        10**6,
        "adam",
    )(grad_rest, grad_others, *resident([swapped, gathered, beside]), *quarters, *flat_params)
    news = list(results[3:])
    for group in (0, 2, 5, 8):
        for member in range(3 * group, 3 * group + 3):
            news[member] = flat(news[member])
    return tuple(a.reshape(()) for a in results[0:3]) + tuple(news)


def solution(mesh):
    placed = (
        P("wide", None, None),
        P("wide", None),
        P("wide"),
        P("wide", None),
        P("wide", None),
        P("wide", None),
        P(None, "wide"),
        P(None, "wide"),
        P(None, "wide"),
        P(None, None, "wide", "narrow"),
        P(None, None, "wide", "narrow"),
        P(None, None, "wide", "narrow"),
        P(None, "narrow", "wide"),
        P(None, "narrow", "wide"),
        P(None, "narrow", "wide"),
        P(None, "wide", "narrow"),
        P(None, "wide", "narrow"),
        P(None, "wide", "narrow"),
        P(None, "narrow"),
        P(None, "narrow"),
        P(None, "narrow"),
        P(None, "narrow", "wide"),
        P(None, "narrow", "wide"),
        P(None, "narrow", "wide"),
        P(),
        P(),
        P(),
        P("wide", "narrow"),
        P("wide", "narrow"),
        P("wide", "narrow"),
        P("wide", None),
        P("wide", None),
        P("wide", None),
    )
    return jax.shard_map(
        per_device,
        mesh=mesh,
        in_specs=placed,
        out_specs=(P(), P(), P()) + placed[6:],
        check_vma=False,
    )
```

```python
import functools

import jax
import jax.numpy as jnp
from jax import lax
from jax.experimental import pallas as pl
from jax.experimental.pallas import tpu as pltpu
from jax.sharding import PartitionSpec as P

D = 256
HEADS = 4
HEAD_DIM = 64
FF = 1024
VOCAB = 512
ACTIONS = 18
GAMES = 26
OBS = 16
FRAMES = 20
STEP_NUMBER = 5
FRAME_TOKENS = 17
LENGTH = 340
ROWS = 896
NVEC = 14

EPS_NORM = 1e-05
BETA_ONE = 0.5
BETA_TWO = 0.5
RATE_TABLE = 0.5
RATE_MATRIX = 0.05
RATE_VECTOR = 0.2
DECAY_RATE = 0.01
EPS_ADAM = 1e-08
CLIP_AT = 0.1

SEQ = 352
KEYS = 384
BLOCK, BLOCKS = 128, 3
TILE = 32
SIDE_ROWS = 32
QUERIES = HEADS * BLOCK
VALUE_ROWS = 80

COL_QKV, COL_PROJ, COL_UP, COL_DOWN, COL_LAYER = 0, 768, 1024, 2048, 3072
HALF_ATTENTION = ((0, 128, 0), (128, 128, 256), (256, 128, 512), (384, 128, COL_PROJ))
HALF_LAYER = HALF_ATTENTION + ((512, 512, COL_UP), (1024, 512, COL_DOWN))
COL_TABLE, COL_SMALL, COL_FIRST = 3072, 3968, 4096
HALF_FIRST = HALF_LAYER + ((1536, 512, COL_TABLE),)
HALF_FIRST_COLS = 2048
COL_HEAD, COL_SECOND = 3072, 3584
HALF_SECOND = HALF_LAYER + ((1536, 256, COL_HEAD),)
HALF_SECOND_COLS = 1792
GRAD_UP, GRAD_DOWN = 0, 1024
HALF_GRAD_FF = ((0, 512, GRAD_UP), (512, 512, GRAD_DOWN))
GRAD_TABLE, GRAD_SMALL = 1024, 1920
HALF_GRAD_REST = HALF_ATTENTION + ((512, 512, GRAD_TABLE),)
HALF_GRAD_COLS = 1024
SMALL_ROWS, SMALL_BIAS, SMALL_SIDE = 32, 14, 22

F32, BF16 = jnp.float32, jnp.bfloat16
MIB = 1024 * 1024


def dot_nn(a, b):
    return lax.dot_general(a, b, (((1,), (0,)), ((), ())), preferred_element_type=F32)


def dot_nt(a, b):
    return lax.dot_general(a, b, (((1,), (1,)), ((), ())), preferred_element_type=F32)


def dot_tn(a, b):
    return lax.dot_general(a, b, (((0,), (0,)), ((), ())), preferred_element_type=F32)


def places(fast):
    wide, core = lax.axis_index("wide"), lax.axis_index("narrow")
    return (wide if fast else 0), core, wide


def tiles(rows, size):
    return [slice(first, first + size) for first in range(0, rows, size)]


def normalise(x):
    centred = x - jnp.mean(x, axis=1, keepdims=True)
    scale = lax.rsqrt(jnp.mean(centred * centred, axis=1, keepdims=True) + EPS_NORM)
    return centred * scale, scale


def keep_norm(rows, xhat, scale, kept):
    kept[0][rows] = xhat.astype(BF16)
    kept[1][rows] = jnp.broadcast_to(scale, (TILE, 128))


def kept_norm(rows, kept):
    scale = kept[1][rows]
    return kept[0][rows].astype(F32), jnp.concatenate([scale, scale], axis=1)


def normalise_back(grad, xhat, scale, gain):
    inner = grad * gain
    mean_one = jnp.mean(inner, axis=1, keepdims=True)
    mean_two = jnp.mean(inner * xhat, axis=1, keepdims=True)
    return scale * (inner - mean_one - xhat * mean_two)


def column_sum(a):
    return jnp.sum(a, axis=0, keepdims=True)


def fold(a):
    return jnp.sum(a.reshape(a.shape[0] // 8, 8, a.shape[1]), axis=0)


def plus(total, a):
    return a if total is None else total + a


def block_lanes(i, h=None):
    if h is None:
        return slice(QUERIES * i, QUERIES * (i + 1))
    return slice(QUERIES * i + BLOCK * h, QUERIES * i + BLOCK * (h + 1))


def head_rows(h):
    return slice(HEAD_DIM * h, HEAD_DIM * (h + 1))


def spread_heads(source, target_ref):
    for h in range(HEADS):
        for i in range(BLOCKS):
            target_ref[head_rows(h), block_lanes(i, h)] = source[
                head_rows(h), BLOCK * i : BLOCK * (i + 1)
            ]


def causal_mask():
    key = lax.broadcasted_iota(jnp.int32, (BLOCK, QUERIES), 0)
    query = lax.broadcasted_iota(jnp.int32, (BLOCK, QUERIES), 1) & (BLOCK - 1)
    return jnp.where(key <= query, 0.0, -1e30)


def assemble(pieces_mine, pieces_other, place, w_ref, halves):
    me, core, _ = place
    is_first = core == 0
    for p in range(4):

        def block(z, _, p=p):
            row = pl.multiple_of((me ^ (4 * z + p)) * 16, 16)
            for src, width, dest in halves:
                mine = pieces_mine[p][z, :, src : src + width]
                other = pieces_other[p][z, :, src : src + width]
                if dest == COL_QKV:
                    mine, other = mine * 0.125, other * 0.125
                w_ref[pl.ds(row, 16), dest : dest + width] = jnp.where(is_first, mine, other)
                w_ref[pl.ds(row, 16), dest + width : dest + 2 * width] = jnp.where(
                    is_first, other, mine
                )
            return 0

        lax.fori_loop(0, 4, block, 0)


def disperse(g_ref, place, keep_ref, send_ref, halves, scaled=True):
    me, core, _ = place
    is_first = core == 0

    def block(i, _):
        p, z = i >> 2, i & 3
        row = pl.multiple_of((me ^ (4 * z + p)) * 16, 16)
        for src, width, dest in halves:
            low = g_ref[pl.ds(row, 16), dest : dest + width]
            high = g_ref[pl.ds(row, 16), dest + width : dest + 2 * width]
            if scaled and dest == COL_QKV:
                low, high = low * 0.125, high * 0.125
            keep_ref[p, z, :, src : src + width] = jnp.where(is_first, low, high).astype(BF16)
            send_ref[p, z, :, src : src + width] = jnp.where(is_first, high, low).astype(BF16)
        return 0

    lax.fori_loop(0, 16, block, 0)


def make_hits(ids, game, hits_ref):
    lane = lax.broadcasted_iota(jnp.int32, (TILE, ROWS), 1)
    for rows in tiles(SEQ, TILE):
        place = lax.broadcasted_iota(jnp.int32, (TILE, 1), 0) + (VOCAB + ACTIONS + GAMES + rows.start)
        hit = (lane == ids[rows]) | (lane == game[rows]) | (lane == place)
        hits_ref[rows] = jnp.where(hit, 1.0, 0.0).astype(BF16)


def gelu_and_slope(up):
    up = up.astype(BF16)
    square = up * up
    half = jax.nn.sigmoid(up * (BF16(1.5957691216057308) + BF16(0.0713548162726) * square))
    hidden = up * half
    slope = BF16(1.5957691216057308) + BF16(0.2140644488178) * square
    return hidden, half + hidden * (BF16(1.0) - half) * slope


def layer_forward(x_ref, w_ref, vec, bias, kept, work):
    qt_ref, kv_ref, p0, p1, p2, r_ref, ot_ref, o_ref = kept[0:8]
    h_ref, gp_ref, a_ref, c_ref = kept[9:13]
    qst_ref, vt_ref, mask_ref, wqt_ref, long_ref, u_ref, y_ref, m_ref = work
    for rows in tiles(SEQ, TILE):
        xhat, scale = normalise(x_ref[rows])
        keep_norm(rows, xhat, scale, kept[14:16])
        normed16 = (xhat * vec[0:1] + vec[1:2]).astype(BF16)
        a_ref[rows], long_ref[rows] = normed16, normed16
    kv_ref[0:SEQ] = dot_nn(long_ref[0:SEQ], w_ref[:, 256:768]).astype(BF16)
    kv_ref[SEQ:KEYS] = jnp.zeros((KEYS - SEQ, 512), BF16)
    qt_ref[...] = dot_nt(wqt_ref[...], long_ref[...]).astype(BF16)
    spread_heads(qt_ref, qst_ref)
    turned = jnp.transpose(kv_ref[:, 256:512])
    for h in range(HEADS):
        vt_ref[VALUE_ROWS * h : VALUE_ROWS * h + HEAD_DIM] = turned[head_rows(h)]
    for i, pt_ref in enumerate((p0, p1, p2)):
        seen, first = BLOCK * (i + 1), BLOCK * i
        scores = dot_nn(kv_ref[0:seen, 0:256], qst_ref[:, block_lanes(i)])
        last = scores[first:] + mask_ref[...]
        peak = jnp.max(last, axis=0, keepdims=True)
        if i:
            peak = jnp.maximum(peak, jnp.max(scores[0:first], axis=0, keepdims=True))
            pt_ref[0:first] = jnp.exp(scores[0:first] - peak).astype(BF16)
        pt_ref[first:seen] = jnp.exp(last - peak).astype(BF16)
        for h in range(HEADS):
            values = vt_ref[VALUE_ROWS * h : VALUE_ROWS * (h + 1), 0:seen]
            out = dot_nn(values, pt_ref[:, BLOCK * h : BLOCK * (h + 1)])
            inverse = 1.0 / out[HEAD_DIM : HEAD_DIM + 1]
            r_ref[h : h + 1, first:seen] = inverse
            ot_ref[head_rows(h), first:seen] = (out[0:HEAD_DIM] * inverse).astype(BF16)
    o_ref[...] = jnp.transpose(ot_ref[...])[0:SEQ]
    y_ref[...] = dot_nt(o_ref[...], w_ref[:, COL_PROJ : COL_PROJ + 256])
    for rows in tiles(SEQ, TILE):
        middle = x_ref[rows] + (y_ref[rows] + vec[2:3])
        m_ref[rows] = middle
        xhat, scale = normalise(middle)
        keep_norm(rows, xhat, scale, (kept[8], kept[13]))
        c_ref[rows] = (xhat * vec[3:4] + vec[4:5]).astype(BF16)
    u_ref[...] = dot_nn(c_ref[...], w_ref[:, COL_UP : COL_UP + FF])
    for rows in tiles(SEQ, TILE):
        for first in range(0, FF, 256):
            cols = slice(first, first + 256)
            h_ref[rows, cols], gp_ref[rows, cols] = gelu_and_slope(u_ref[rows, cols] + bias[:, cols])
    y_ref[...] = dot_nt(h_ref[...], w_ref[:, COL_DOWN : COL_DOWN + FF])


def add_gradient(g_ref, column, left, right):
    g_ref[:, column : column + right.shape[1]] += dot_tn(left, right)


def ff_backward(grad_ref, grad16_ref, w_ref, w_up, w_down, vec, kept, v_ref, v_row, bias_row, work, mid_ref, mid16_refs):
    norm_kept, gp_ref = kept
    du_ref, ones_ref, u_ref, y_ref = work
    u_ref[...] = dot_nn(grad16_ref[...], w_ref[:, w_down : w_down + FF])
    for rows in tiles(SEQ, TILE):
        du_ref[rows] = u_ref[rows].astype(BF16) * gp_ref[rows]
    bias_grad = dot_nn(ones_ref[...], du_ref[...])
    for chunk in range(4):
        v_ref[bias_row + chunk, 0:1] += bias_grad[0:1, 256 * chunk : 256 * chunk + 256]
    y_ref[...] = dot_nt(du_ref[...], w_ref[:, w_up : w_up + FF])
    totals = [None] * 3
    for rows in tiles(SEQ, TILE):
        xhat, scale = kept_norm(rows, norm_kept)
        grad = y_ref[rows]
        mid = grad_ref[rows] + normalise_back(grad, xhat, scale, vec[3:4])
        mid_ref[rows] = mid
        for mid16_ref in mid16_refs:
            mid16_ref[rows] = mid.astype(BF16)
        for i, a in enumerate((mid, grad * xhat, grad)):
            totals[i] = plus(totals[i], fold(a))
    for i in range(3):
        v_ref[v_row + 2 + i] += totals[i]


def attention_backward(mid_ref, mid16_ref, w_ref, vec, kept, v_ref, v_row, work, out_ref):
    norm_kept, (qt_ref, kv_ref, p0, p1, p2, r_ref, ot_ref) = kept
    dost_ref, qst_ref, kt_ref, dst_ref, dqt_ref, dkv_ref, dqkv_ref, proj_ref, y_ref = work
    grad_o = dot_nt(proj_ref[...], mid16_ref[...])
    kt_ref[...] = jnp.transpose(kv_ref[:, 0:256])
    deltas = []
    for h in range(HEADS):
        scaled = grad_o[head_rows(h)] * r_ref[h : h + 1]
        deltas.append(column_sum(scaled * ot_ref[head_rows(h)].astype(F32)))
        scaled = scaled.astype(BF16)
        for i in range(BLOCKS):
            dost_ref[head_rows(h), block_lanes(i, h)] = scaled[:, BLOCK * i : BLOCK * (i + 1)]
    for i, pt_ref in enumerate((p0, p1, p2)):
        seen, first = BLOCK * (i + 1), BLOCK * i
        lanes = block_lanes(i)
        delta = jnp.concatenate([a[:, first:seen] for a in deltas], axis=1)
        grad = dot_nn(kv_ref[0:seen, 256:512], dost_ref[:, lanes])
        dst_ref[0:seen, lanes] = pt_ref[...] * (grad - delta).astype(BF16)
        for h in range(HEADS):
            out = dot_nn(kt_ref[head_rows(h), 0:seen], dst_ref[0:seen, block_lanes(i, h)])
            dqt_ref[head_rows(h), first:seen] = out.astype(BF16)
        for at, left, right in (
            (0, dst_ref[0:seen, lanes], qst_ref),
            (256, pt_ref[...], dost_ref),
        ):
            out = dot_nt(left, right[:, lanes])
            if i:
                dkv_ref[0:first, at : at + 256] += out[0:first]
            dkv_ref[first:seen, at : at + 256] = out[first:]
    dqkv_ref[:, 0:256] = jnp.transpose(dqt_ref[...])[0:SEQ]
    dqkv_ref[:, 256:768] = dkv_ref[0:SEQ].astype(BF16)
    y_ref[...] = dot_nt(dqkv_ref[...], w_ref[:, COL_QKV : COL_QKV + 768])
    totals = [None] * 2
    for rows in tiles(SEQ, TILE):
        xhat, scale = kept_norm(rows, norm_kept)
        grad = y_ref[rows]
        out = mid_ref[rows] + normalise_back(grad, xhat, scale, vec[0:1])
        out_ref[rows] = out.astype(out_ref.dtype)
        for i, a in enumerate((grad * xhat, grad)):
            totals[i] = plus(totals[i], fold(a))
    for i in range(2):
        v_ref[v_row + i] += totals[i]


def own_bias(place, mine, other):
    is_first = place[1] == 0
    return jnp.concatenate(
        [jnp.where(is_first, mine, other), jnp.where(is_first, other, mine)], axis=1
    )


def prepare_kernel(
    fast, games_ref, tokens, actions, valid, rewards, ends, out, out_side, out_hits, x_ref
):
    count = out.shape[0]
    frames = tokens.shape[2]
    base = places(fast)[1] * count
    row = lax.broadcasted_iota(jnp.int32, (SEQ, frames), 0)
    start = lax.broadcasted_iota(jnp.int32, (SEQ, frames), 1) * FRAME_TOKENS
    here = jnp.where((row >= start) & (row < start + FRAME_TOKENS), 1.0, 0.0).astype(BF16)
    coming = jnp.where((row >= start - FRAME_TOKENS) & (row < start), 1.0, 0.0).astype(BF16)
    passed = jnp.sum(jnp.where(row >= start + FRAME_TOKENS, 1, 0), axis=1, keepdims=True)
    place = lax.broadcasted_iota(jnp.int32, (SEQ, 1), 0)
    spot = place - passed * FRAME_TOKENS
    lane = lax.broadcasted_iota(jnp.int32, (SEQ, 24), 1)
    wide_lane = lax.broadcasted_iota(jnp.int32, (SEQ, 128), 1)
    inside = place < LENGTH
    one_frame = (
        lax.broadcasted_iota(jnp.int32, (SIDE_ROWS, frames), 0)
        == lax.broadcasted_iota(jnp.int32, (SIDE_ROWS, frames), 1)
    )
    one_frame = jnp.where(one_frame, 1.0, 0.0).astype(BF16)
    side_lane = lax.broadcasted_iota(jnp.int32, (SIDE_ROWS, 128), 1)
    x_ref[...] = jnp.zeros(x_ref.shape, jnp.int32)
    for s in range(count):
        x_ref[0:OBS] = tokens[base + s]
        x_ref[16:17] = actions[pl.ds(base + s, 1)] + VOCAB
        x_ref[17:18] = valid[pl.ds(base + s, 1)]
        x_ref[18:19] = rewards[pl.ds(base + s, 1)]
        x_ref[19:20] = ends[pl.ds(base + s, 1)] + 3
        high = (x_ref[...] >> 4).astype(F32).astype(BF16)
        low = (x_ref[...] & 15).astype(F32).astype(BF16)
        now = dot_nt(here, high) * 16.0 + dot_nt(here, low)
        soon = dot_nt(coming, high) * 16.0 + dot_nt(coming, low)

        at_end = spot == 16
        packed = jnp.where(lane == spot, now, 0.0)
        target = jnp.where((lane == spot + 1) & (spot < 15), now, 0.0)
        target = target + jnp.where((lane == 0) & at_end, soon, 0.0)
        weight = jnp.where((lane == 17) & (spot < 15), now, 0.0)
        weight = weight + jnp.where((lane == 17) & at_end, soon, 0.0)
        packed = packed + 1024.0 * target + 1048576.0 * weight
        packed = jnp.sum(packed, axis=1, keepdims=True).astype(jnp.int32)
        ids = jnp.where(inside, packed & 1023, -1)
        game = jnp.where(inside, games_ref[base + s] + (VOCAB + ACTIONS), -1)
        target, weight = (packed >> 10) & 1023, packed >> 20
        out[s] = jnp.where(wide_lane == 2, target, jnp.where(wide_lane == 3, weight, 0))
        make_hits(ids, game, out_hits.at[s])
        by_frame = dot_nt(one_frame, high) * 16.0 + dot_nt(one_frame, low)
        result = jnp.zeros((SIDE_ROWS, 128), jnp.int32)
        for c in range(3):
            column = by_frame[:, 17 + c : 18 + c].astype(jnp.int32)
            result = jnp.where(side_lane == c, column, result)
        out_side[s] = result


def start_forward(work, w_ref):
    qst_ref, vt_ref, mask_ref, wqt_ref, long_ref = work[0:5]
    long_ref[SEQ:KEYS] = jnp.zeros((KEYS - SEQ, D), BF16)
    qst_ref[...] = jnp.zeros(qst_ref.shape, BF16)
    vt_ref[...] = jnp.ones(vt_ref.shape, BF16)
    mask_ref[...] = causal_mask()
    wqt_ref[...] = jnp.transpose(w_ref[:, 0:256])


def first_forward_kernel(fast, *refs):
    refs = (places(fast),) + refs
    place, hits_ref, vec_ref, bias_ref, bias_other = refs[0:5]
    mine, other = refs[5:9], refs[9:13]
    w_attention, w_ff, side_out, next_ref = refs[13:17]
    kept = [ref.at[0] for ref in refs[17:33]]
    w_ref, x_ref = refs[33:35]
    work = refs[35:43]
    y_ref, m_ref = work[6:8]

    @pl.when(pl.program_id(0) == 0)
    def _():
        assemble(mine, other, place, w_ref, HALF_FIRST)
        w_attention[...] = w_ref[:, 0:COL_UP]
        w_ff[...] = w_ref[:, COL_UP:COL_TABLE]
        side_out[...] = w_ref[:, COL_SMALL:]
        start_forward(work, w_ref)

    x_ref[...] = dot_nt(hits_ref[0], w_ref[:, COL_TABLE : COL_TABLE + ROWS])
    bias = own_bias(place, bias_ref[0:1], bias_other[0:1])
    vec = vec_ref[0:6]
    layer_forward(x_ref, w_ref, vec, bias, kept, work)
    for rows in tiles(SEQ, TILE):
        next_ref[0, rows] = m_ref[rows] + (y_ref[rows] + vec[5:6])


def codebook_losses(logits, meta):
    weight = meta[:, 3:4].astype(F32)
    peak = jnp.max(logits, axis=1, keepdims=True)
    expanded = jnp.exp(logits - peak)
    total = jnp.sum(expanded, axis=1, keepdims=True)
    hit = lax.broadcasted_iota(jnp.int32, logits.shape, 1) == meta[:, 2:3]
    hit = jnp.where(hit, weight, 0.0)
    return weight * (peak + jnp.log(total)), hit, expanded * (weight / total) - hit


def side_losses(side, meta):
    lane = lax.broadcasted_iota(jnp.int32, side.shape, 1)
    is_reward, is_end = lane < 3, (lane == 3) | (lane == 4)
    is_side = lane < 5
    weight = meta[:, 0:1].astype(F32)
    reward_peak = jnp.max(jnp.where(is_reward, side, -1e30), axis=1, keepdims=True)
    end_peak = jnp.max(jnp.where(is_end, side, -1e30), axis=1, keepdims=True)
    shifted = jnp.where(is_side, side - jnp.where(is_reward, reward_peak, end_peak), 0.0)
    expanded = jnp.where(is_side, jnp.exp(shifted), 0.0)
    reward_total = jnp.sum(jnp.where(is_reward, expanded, 0.0), axis=1, keepdims=True)
    end_total = jnp.sum(jnp.where(is_end, expanded, 0.0), axis=1, keepdims=True)
    hit = (lane == meta[:, 1:2]) | (lane == meta[:, 2:3])
    picked = jnp.sum(jnp.where(hit, side, 0.0), axis=1, keepdims=True)
    terms = reward_peak + jnp.log(reward_total) + end_peak + jnp.log(end_total) - picked
    grad = expanded * jnp.where(is_reward, weight / reward_total, weight / end_total)
    return weight * terms, grad - jnp.where(hit, weight, 0.0), weight


def frame_ends(shape, frame_axis):
    frame = lax.broadcasted_iota(jnp.int32, shape, frame_axis)
    row = lax.broadcasted_iota(jnp.int32, shape, 1 - frame_axis)
    hit = (row == frame * FRAME_TOKENS + OBS) & (frame < FRAMES)
    return jnp.where(hit, 1.0, 0.0).astype(BF16)


def middle_kernel(fast, *refs):
    refs = (places(fast),) + refs
    place, meta_ref, frame_ref, vec_ref, bias_ref, bias_other, side_ref, in_ref = refs[0:8]
    mine, other = refs[8:12], refs[12:16]
    grad_ref, keep_ref, send_ref, v_out, scalar_ref = refs[16:21]
    refs = refs[1:]
    w_ref, g_ref, v_ref = refs[20:23]
    kept = list(refs[23:39])
    forward_work = refs[39:47]
    u_ref, y_ref, m_ref = forward_work[5:8]
    backward_work = list(refs[47:53])
    proj_ref = refs[53]
    du_all, ones_ref, up_ref, up16_all, mid_ref, mid16_ref = refs[54:60]
    last_kept = refs[60:62]
    final_all, logit_ref, dlogit_all, pick_ref, put_ref, mid16_all = refs[62:68]
    o_all, h_all, a_all, c_all, dqkv_all = kept[7], kept[9], kept[11], kept[12], backward_work[5]
    dost_ref = backward_work[0]
    step = pl.program_id(0)

    @pl.when(step == 0)
    def _():
        assemble(mine, other, place, w_ref, HALF_SECOND)
        w_ref[:, COL_SECOND:] = side_ref[...]
        g_ref[...] = jnp.zeros(g_ref.shape, F32)
        v_ref[...] = jnp.zeros(v_ref.shape, F32)
        scalar_ref[...] = jnp.zeros(scalar_ref.shape, F32)
        start_forward(forward_work, w_ref)
        dost_ref[...] = jnp.zeros(dost_ref.shape, BF16)
        proj_ref[...] = jnp.transpose(w_ref[:, COL_PROJ : COL_PROJ + 256])
        ones_ref[...] = jnp.ones(ones_ref.shape, BF16)
        mid16_ref[SEQ:KEYS] = jnp.zeros((KEYS - SEQ, D), BF16)
        pick_ref[...] = frame_ends((SIDE_ROWS, SEQ), 0)
        put_ref[...] = frame_ends((SEQ, SIDE_ROWS), 1)

    here = pl.ds(pl.multiple_of((step & 1) * SEQ, 32), SEQ)
    for i in (7, 9, 11, 12):
        kept[i] = kept[i].at[here]
    gp_ref = kept[10]
    backward_work[5] = dqkv_all.at[here]
    du_ref, up16_ref, pair16_ref = du_all.at[here], up16_all.at[here], mid16_all.at[here]
    final_ref, dlogit_ref = final_all.at[here], dlogit_all.at[here]
    x_ref = in_ref.at[0]
    vec = vec_ref[6:12]
    bias = own_bias(place, bias_ref[1:2], bias_other[1:2])
    layer_forward(x_ref, w_ref, vec, bias, kept, forward_work)

    gain, offset = vec_ref[12:13], vec_ref[13:14]
    for rows in tiles(SEQ, TILE):
        last = m_ref[rows] + (y_ref[rows] + vec[5:6])
        xhat, scale = normalise(last)
        keep_norm(rows, xhat, scale, last_kept)
        final_ref[rows] = (xhat * gain + offset).astype(BF16)
    cols_head = slice(COL_HEAD, COL_HEAD + VOCAB + 128)
    logit_ref[...] = dot_nn(final_ref[...], w_ref[:, COL_HEAD : COL_HEAD + VOCAB])
    logs, picked = None, None
    for rows in tiles(SEQ, TILE):
        logits = logit_ref[rows]
        log, hit, grad = codebook_losses(logits, meta_ref[0, rows])
        dlogit_ref[rows, :VOCAB] = grad.astype(BF16)
        logs, picked = plus(logs, log), plus(picked, fold(hit * logits))
    acting = dot_nn(pick_ref[...], final_ref[...]).astype(BF16)
    side = dot_nn(acting, w_ref[:, COL_HEAD + VOCAB : COL_HEAD + VOCAB + 128])
    side_loss, grad, weight = side_losses(side, frame_ref[0])
    dlogit_ref[:, VOCAB:] = dot_nn(put_ref[...], grad.astype(BF16)).astype(BF16)
    loss = column_sum(logs) + column_sum(side_loss)
    loss = loss - jnp.sum(column_sum(picked), axis=1, keepdims=True)
    valid = column_sum(weight)
    scalar_lane = lax.broadcasted_iota(jnp.int32, (8, 128), 1)
    scalar_row = lax.broadcasted_iota(jnp.int32, (8, 128), 0) == 0
    scalar_ref[...] += jnp.where(
        scalar_row,
        jnp.where(scalar_lane == 0, loss, jnp.where(scalar_lane == 1, valid, 0.0)),
        0.0,
    )
    y_ref[...] = dot_nt(dlogit_ref[...], w_ref[:, cols_head])
    totals = [None] * 3
    for rows in tiles(SEQ, TILE):
        xhat, scale = kept_norm(rows, last_kept)
        grad = y_ref[rows]
        up = normalise_back(grad, xhat, scale, gain)
        up_ref[rows] = up
        up16_ref[rows] = up.astype(BF16)
        for i, a in enumerate((up, grad * xhat, grad)):
            totals[i] = plus(totals[i], fold(a))
    for i in range(3):
        v_ref[11 + i] += totals[i]
    ff_backward(
        up_ref,
        up16_ref,
        w_ref,
        COL_UP,
        COL_DOWN,
        vec,
        ((kept[8], kept[13]), gp_ref),
        v_ref,
        6,
        SMALL_BIAS + 4,
        (du_ref, ones_ref, u_ref, y_ref),
        mid_ref,
        (mid16_ref, pair16_ref),
    )
    attention_backward(
        mid_ref,
        mid16_ref,
        w_ref,
        vec,
        (kept[14:16], kept[0:7]),
        v_ref,
        6,
        (dost_ref, forward_work[0]) + tuple(backward_work[1:]) + (proj_ref, y_ref),
        grad_ref.at[0],
    )

    @pl.when(step & 1 == 1)
    def _():
        add_gradient(g_ref, COL_QKV, a_all[...], dqkv_all[...])
        add_gradient(g_ref, COL_PROJ, mid16_all[...], o_all[...])
        add_gradient(g_ref, COL_UP, c_all[...], du_all[...])
        add_gradient(g_ref, COL_DOWN, up16_all[...], h_all[...])
        add_gradient(g_ref, COL_HEAD, final_all[...], dlogit_all[...])

    @pl.when(step == pl.num_programs(0) - 1)
    def _():
        disperse(g_ref, place, keep_ref, send_ref, HALF_SECOND)
        side = jnp.transpose(g_ref[:, COL_SECOND:])
        for i in range(5):
            v_ref[SMALL_SIDE + i, 0:1] = side[i : i + 1]
        v_out[...] = v_ref[...]


def ff_backward_kernel(fast, *refs):
    vec_ref, w_ref, grad_ref, v_in = refs[0:4]
    xhat_ref, scale_ref, h_ref, gp_ref, c_ref = [ref.at[0] for ref in refs[4:9]]
    mid_ref, keep_ref, send_ref, v_out = refs[9:13]
    g_ref, v_ref, grad16_ref, du_ref, ones_ref, u_ref, y_ref = refs[13:20]
    step = pl.program_id(0)

    @pl.when(step == 0)
    def _():
        g_ref[...] = jnp.zeros(g_ref.shape, F32)
        v_ref[...] = v_in[...]
        ones_ref[...] = jnp.ones(ones_ref.shape, BF16)

    total = None
    for rows in tiles(SEQ, TILE):
        grad = grad_ref[0, rows]
        grad16_ref[rows] = grad.astype(BF16)
        total = plus(total, fold(grad))
    v_ref[5] += total
    ff_backward(
        grad_ref.at[0],
        grad16_ref,
        w_ref,
        GRAD_UP,
        GRAD_DOWN,
        vec_ref[0:6],
        ((xhat_ref, scale_ref), gp_ref),
        v_ref,
        0,
        SMALL_BIAS,
        (du_ref, ones_ref, u_ref, y_ref),
        mid_ref.at[0],
        (),
    )
    add_gradient(g_ref, GRAD_DOWN, grad16_ref[...], h_ref[...])
    add_gradient(g_ref, GRAD_UP, c_ref[...], du_ref[...])

    @pl.when(step == pl.num_programs(0) - 1)
    def _():
        disperse(g_ref, places(fast), keep_ref, send_ref, HALF_GRAD_FF, False)
        v_out[...] = v_ref[...]


def attention_backward_kernel(fast, *refs):
    vec_ref, w_ref, mid_ref, v_in = refs[0:4]
    kept = [ref.at[0] for ref in refs[4:13]]
    o_all, a_all, hits_all = refs[13:16]
    keep_ref, send_ref, v_out = refs[17:20]
    g_ref, v_ref, mid16_ref, mid16_all, out16_all, dqkv_all = refs[20:26]
    work = list(refs[26:34])
    dost_ref, qst_ref, proj_ref = work[0], work[1], work[6]
    step = pl.program_id(0)

    @pl.when(step == 0)
    def _():
        v_ref[...] = v_in[...]
        dost_ref[...] = jnp.zeros(dost_ref.shape, BF16)
        qst_ref[...] = jnp.zeros(qst_ref.shape, BF16)
        proj_ref[...] = jnp.transpose(w_ref[:, COL_PROJ : COL_PROJ + 256])
        mid16_ref[SEQ:KEYS] = jnp.zeros((KEYS - SEQ, D), BF16)

    here = pl.ds(pl.multiple_of(step * SEQ, 32), SEQ)
    all16_ref = mid16_all.at[here]
    spread_heads(kept[2], qst_ref)
    for rows in tiles(SEQ, TILE):
        mid16 = mid_ref[0, rows].astype(BF16)
        mid16_ref[rows], all16_ref[rows] = mid16, mid16
    work.insert(6, dqkv_all.at[here])
    attention_backward(
        mid_ref.at[0],
        mid16_ref,
        w_ref,
        vec_ref[0:6],
        (kept[0:2], kept[2:9]),
        v_ref,
        0,
        work,
        out16_all.at[here],
    )

    @pl.when(step == pl.num_programs(0) - 1)
    def _():
        g_ref[:, COL_QKV : COL_QKV + 768] = dot_tn(a_all[...], dqkv_all[...])
        g_ref[:, COL_PROJ : COL_PROJ + 256] = dot_tn(mid16_all[...], o_all[...])
        g_ref[:, GRAD_TABLE : GRAD_TABLE + ROWS] = dot_tn(out16_all[...], hits_all[...])
        small = jnp.sum(v_ref[...], axis=1)
        v_out[...] = small
        for block in range(16):
            quarter = small[8 * (block // 4) : 8 * (block // 4) + 8]
            g_ref[16 * block : 16 * block + 8, GRAD_SMALL:] = quarter[:, 0:128]
            g_ref[16 * block + 8 : 16 * block + 16, GRAD_SMALL:] = quarter[:, 128:256]
        disperse(g_ref, places(fast), keep_ref, send_ref, HALF_GRAD_REST)


def pack_layer(attn, proj, up, down, layer, out):
    for j in range(3):
        out[:, 128 * j : 128 * j + 128] = attn[layer, j].astype(BF16)
    out[:, 384:512] = proj[layer].astype(BF16)
    out[:, 512:1024] = up[layer].astype(BF16)
    out[:, 1024:1536] = down[layer].astype(BF16)


def pack_kernel(fast, table, attn, proj, up, down, head, side, first, second, pad_ref):
    pack_layer(attn, proj, up, down, 0, first)
    pack_layer(attn, proj, up, down, 1, second)
    second[:, 1536:1792] = head[...].astype(BF16)
    rows = side.shape[1]
    eye = (
        lax.broadcasted_iota(jnp.int32, (rows, rows), 0)
        == lax.broadcasted_iota(jnp.int32, (rows, rows), 1)
    )
    eye = jnp.where(eye, 1.0, 0.0).astype(BF16)
    pad_ref[...] = jnp.zeros(pad_ref.shape, F32)
    pad_ref[:, 0:5] = dot_nt(eye, side[...].astype(BF16))
    high = jnp.concatenate([table[:, 512:896], pad_ref[...]], axis=1)
    first[:, 1536:2048] = jnp.where(places(fast)[1] == 0, table[:, 0:512], high).astype(BF16)


def finish_kernel(fast, *refs):
    count = (len(refs) - 5) // 2
    scalar_ref = refs[2 * count]
    out_rest, out_other, out_table, out_small = refs[2 * count + 1 :]
    square = jnp.zeros((1, 1), F32)
    for pieces, out in ((refs[0:count], out_rest), (refs[count : 2 * count], out_other)):
        total = pieces[0][...]
        for piece in pieces[1:]:
            total = total + piece[...].astype(F32)
        out[...] = total
        square = square + column_sum(jnp.sum(total * total, axis=1, keepdims=True))
    small = out_rest[:, 896:1024]
    extra = column_sum(jnp.sum(small * small, axis=1, keepdims=True))
    square = square - jnp.where(places(fast)[1] == 0, 0.0, extra)
    out_table[...] = out_rest[:, 512:1024]
    lane = lax.broadcasted_iota(jnp.int32, (8, 128), 1)
    row = lax.broadcasted_iota(jnp.int32, (8, 128), 0)
    message = scalar_ref[...] + jnp.where((row == 0) & (lane == 2), square, 0.0)
    if fast:
        spot = places(fast)[2] & 3
        part = jnp.where(spot & 1 == 0, small[0:4], small[4:8])
        part = jnp.where(spot & 2 == 0, part, jnp.where(spot & 1 == 0, small[8:12], small[12:16]))
        message = jnp.concatenate([part, message[0:4]], axis=0)
    for i in range(out_small.shape[0]):
        out_small[i] = message


def adam_rule(weight, moment, second, gradient, step_rate, decay_rate):
    moment_new = BETA_ONE * moment + (1.0 - BETA_ONE) * gradient
    second_new = BETA_TWO * second + (1.0 - BETA_TWO) * gradient * gradient
    moment_hat = moment_new / (1.0 - BETA_ONE**STEP_NUMBER)
    second_hat = second_new / (1.0 - BETA_TWO**STEP_NUMBER)
    weight_new = weight - step_rate * (
        moment_hat / (jnp.sqrt(second_hat) + EPS_ADAM) + decay_rate * weight
    )
    return (weight_new, moment_new, second_new)


def adam_kernel(fast, rest, others, swapped, gathered, beside, *refs):
    rows = rest.shape[0]
    _, core, wide = places(fast)
    is_first = core == 0
    if fast:
        small_parts = jnp.where(is_first, beside[...], gathered[...])
        quarters = [
            jnp.concatenate([small_parts[4 * z + p, 0:4] for p in range(4)], axis=0)
            for z in range(4)
        ]
    else:
        quarters = [refs[0][z] for z in range(4)]
        refs = refs[1:]
    params = [refs[3 * i : 3 * i + 3] for i in range(9)]
    loss_ref, valid_ref, norm_ref = refs[27:30]
    outs = [refs[30 + 3 * i : 33 + 3 * i] for i in range(9)]
    small_ref = refs[57]
    for z in range(4):
        small_ref[8 * z : 8 * z + 8, 0:128] = quarters[z][0:8]
        small_ref[8 * z : 8 * z + 8, 128:256] = quarters[z][8:16]
    sums = []
    for source in (gathered, beside):
        line = 4 if fast else 0
        total = source[0, line : line + 1]
        for i in range(1, source.shape[0]):
            total = total + source[i, line : line + 1]
        sums.append(total)
    scalars = sums[0] + sums[1]
    small = small_ref[...]
    loss, valid, square = scalars[:, 0:1], scalars[:, 1:2], scalars[:, 2:3]
    square = square + column_sum(jnp.sum(small * small, axis=1, keepdims=True))
    inverse = 1.0 / valid
    norm = jnp.sqrt(square) * inverse
    loss_ref[...], valid_ref[...], norm_ref[...] = loss, valid, norm
    factor = jnp.minimum(1.0, CLIP_AT / (norm + 1e-06)) * inverse
    table, attn, proj, up, bias, down, vectors, head, side = range(9)

    def update(which, index, gradient, step_rate, decay_rate):
        news = adam_rule(
            *(ref[index] for ref in params[which]), factor * gradient, step_rate, decay_rate
        )
        for ref, new in zip(outs[which], news):
            ref[index] = new

    layers = ((rest, others, 1792), (others, others, 512))
    for layer, (attention, feed, at) in enumerate(layers):
        for j in range(3):
            update(attn, (layer, j), attention[:, 128 * j : 128 * j + 128], RATE_MATRIX, DECAY_RATE)
        update(proj, (layer,), attention[:, 384:512], RATE_MATRIX, DECAY_RATE)
        update(up, (layer,), feed[:, at : at + 512], RATE_MATRIX, DECAY_RATE)
        update(down, (layer,), feed[:, at + 512 : at + 1024], RATE_MATRIX, DECAY_RATE)
        for i in range(2):
            low = SMALL_BIAS + 4 * layer + i
            row = jnp.where(is_first, small[low : low + 1], small[low + 2 : low + 3])
            index = (slice(layer, layer + 1), slice(256 * i, 256 * i + 256))
            update(bias, index, row, RATE_VECTOR, 0.0)
    whole = (slice(None), slice(None))
    update(head, whole, others[:, 1536:1792], RATE_MATRIX, DECAY_RATE)
    mine, theirs = rest[:, 512:1024], swapped[:, 0:512]
    low, high = jnp.where(is_first, mine, theirs), jnp.where(is_first, theirs, mine)
    update(table, (slice(None), slice(0, 512)), low, RATE_TABLE, DECAY_RATE)
    update(table, (slice(None), slice(512, 896)), high[:, 0:384], RATE_TABLE, DECAY_RATE)
    update(vectors, whole, small[0:NVEC], RATE_VECTOR, 0.0)
    turned = pltpu.roll(small[SMALL_SIDE : SMALL_SIDE + 8], lax.rem(D - wide * rows, D), 1)
    update(side, whole, turned[0:5, 0:rows], RATE_MATRIX, DECAY_RATE)


def swap(a, axis, distance):
    size = lax.axis_size(axis)
    return lax.ppermute(a, axis, [(i, i ^ distance) for i in range(size)])


def swap_column(piece, n_high):
    return [piece] + [swap(piece, "wide", 4 * k) for k in range(1, n_high)]


def gather_plane(column):
    return [column] + [swap(column, "wide", p) for p in range(1, 4)]


def gather_cores(mine):
    return [swap(a, "narrow", 1) for a in mine]


def in_blocks(parts, wide):
    n_high, rows, cols = parts[0].shape
    if rows == 16:
        return parts
    whole = jnp.stack(parts, axis=1).reshape(4 * n_high, rows, cols)
    whole = whole[wide ^ jnp.arange(4 * n_high)].reshape(4, 4, 16, cols)
    return [whole[:, p] for p in range(4)]


def in_pieces(blocks, wide, n_high):
    cols = blocks.shape[-1]
    if n_high == 4:
        return blocks
    rows = 64 // n_high
    whole = blocks.transpose(1, 0, 2, 3).reshape(4 * n_high, rows, cols)
    whole = whole[wide ^ jnp.arange(4 * n_high)]
    return whole.reshape(n_high, 4, rows, cols).transpose(1, 0, 2, 3)


def add_cores(keep, send, wide, n_high):
    keep, send = in_pieces(keep, wide, n_high), in_pieces(send, wide, n_high)
    received = swap(send, "narrow", 1)
    return [keep[p].astype(F32) + received[p].astype(F32) for p in range(4)]


def swap_plane(sums):
    return [swap(sums[p].astype(BF16), "wide", p) for p in range(1, 4)]


def add_plane(own, received):
    for a in received:
        own = own + a.astype(F32)
    return own


def column_pieces(own):
    return [own[0]] + [swap(own[k].astype(BF16), "wide", 4 * k) for k in range(1, own.shape[0])]


def resident(arrays):
    return [pltpu.with_memory_space_constraint(a, pltpu.VMEM) for a in arrays]


def in_hbm(arrays):
    return [pltpu.with_memory_space_constraint(a, pltpu.HBM) for a in arrays]


def full_spec(a):
    return pl.BlockSpec(a.shape, lambda *_: (0,) * len(a.shape))


def row_spec(shape):
    return pl.BlockSpec((1,) + shape, lambda i: (i,) + (0,) * len(shape))


def shaped(shape, dtype):
    return jax.ShapeDtypeStruct(shape, dtype)


VMEM_SPEC = pl.BlockSpec(memory_space=pltpu.VMEM)
ANY_SPEC = pl.BlockSpec(memory_space=pl.ANY)
SMEM_SPEC = pl.BlockSpec(memory_space=pltpu.SMEM)


VMEM_MIB = {
    "pack": 58,
    "prepare": 24,
    "first_forward": 22,
    "middle": 28,
    "ff_backward": 15,
    "attention_backward": 22,
    "finish": 24,
    "adam": 20,
}


def call(kernel, grid, in_specs, out_specs, out_shape, scratch, flops, bytes_accessed, name):
    extra = {"grid": grid} if grid else {}
    return pl.pallas_call(
        kernel,
        in_specs=in_specs,
        out_specs=out_specs,
        out_shape=out_shape,
        scratch_shapes=scratch,
        compiler_params=pltpu.CompilerParams(vmem_limit_bytes=VMEM_MIB[name] * MIB),
        cost_estimate=pl.CostEstimate(
            flops=flops, bytes_accessed=bytes_accessed, transcendentals=0
        ),
        name=name,
        **extra,
    )


KEPT = (
    ((D, KEYS), BF16),
    ((KEYS, 512), BF16),
    ((BLOCK, QUERIES), BF16),
    ((2 * BLOCK, QUERIES), BF16),
    ((3 * BLOCK, QUERIES), BF16),
    ((8, KEYS), F32),
    ((D, KEYS), BF16),
    ((SEQ, D), BF16),
    ((SEQ, D), BF16),
    ((SEQ, FF), BF16),
    ((SEQ, FF), BF16),
    ((SEQ, D), BF16),
    ((SEQ, D), BF16),
    ((SEQ, 128), F32),
    ((SEQ, D), BF16),
    ((SEQ, 128), F32),
)
FORWARD_WORK = [
    pltpu.VMEM((D, BLOCKS * QUERIES), BF16),
    pltpu.VMEM((HEADS * VALUE_ROWS, KEYS), BF16),
    pltpu.VMEM((BLOCK, QUERIES), F32),
    pltpu.VMEM((D, D), BF16),
    pltpu.VMEM((KEYS, D), BF16),
    pltpu.VMEM((SEQ, FF), F32),
    pltpu.VMEM((SEQ, D), F32),
    pltpu.VMEM((SEQ, D), F32),
]
BACKWARD_WORK = [
    pltpu.VMEM((D, BLOCKS * QUERIES), BF16),
    pltpu.VMEM((D, BLOCKS * QUERIES), BF16),
    pltpu.VMEM((D, KEYS), BF16),
    pltpu.VMEM((KEYS, BLOCKS * QUERIES), BF16),
    pltpu.VMEM((D, KEYS), BF16),
    pltpu.VMEM((KEYS, 512), F32),
    pltpu.VMEM((SEQ, 768), BF16),
]
PROJ_WORK = pltpu.VMEM((D, D), BF16)
ONES_WORK = pltpu.VMEM((16, SEQ), BF16)


def per_device(
    tokens,
    actions,
    game_ids,
    valid_steps,
    rewards,
    end_flags,
    embed_table,
    table_first,
    table_second,
    attn_weight,
    attn_first,
    attn_second,
    proj_weight,
    proj_first,
    proj_second,
    up_weight,
    up_first,
    up_second,
    up_bias,
    bias_first,
    bias_second,
    down_weight,
    down_first,
    down_second,
    vectors,
    vectors_first,
    vectors_second,
    head_weight,
    head_first,
    head_second,
    side_weight,
    side_first,
    side_second,
):
    n_high = lax.axis_size("wide") // 4
    wide = lax.axis_index("wide")
    rows = side_weight.shape[0]
    fast = rows == 16

    def flat(a):
        return jnp.swapaxes(a, -1, -2)

    params = (
        (flat(embed_table), flat(table_first), flat(table_second)),
        (attn_weight, attn_first, attn_second),
        (flat(proj_weight), flat(proj_first), flat(proj_second)),
        (up_weight, up_first, up_second),
        (up_bias, bias_first, bias_second),
        (flat(down_weight), flat(down_first), flat(down_second)),
        (vectors, vectors_first, vectors_second),
        (head_weight, head_first, head_second),
        (flat(side_weight), flat(side_first), flat(side_second)),
    )
    table, attn, proj, up, _, down, _, head, side = (group[0] for group in params)

    piece_first, piece_second = call(
        functools.partial(pack_kernel, fast),
        None,
        [VMEM_SPEC] * 7,
        [VMEM_SPEC] * 2,
        [shaped((rows, HALF_FIRST_COLS), BF16), shaped((rows, HALF_SECOND_COLS), BF16)],
        [pltpu.VMEM((rows, 128), F32)],
        10**6,
        10**6,
        "pack",
    )(table, attn, proj, up, down, head, side)
    other_bias = swap(up_bias, "narrow", 1)
    column = swap_column(piece_first, n_high)

    count = tokens.shape[0] // lax.axis_size("narrow")
    meta, frame_meta, hits = call(
        functools.partial(prepare_kernel, fast),
        None,
        [SMEM_SPEC] + [VMEM_SPEC] * 5,
        [VMEM_SPEC] * 3,
        [
            shaped((count, SEQ, 128), jnp.int32),
            shaped((count, SIDE_ROWS, 128), jnp.int32),
            shaped((count, SEQ, ROWS), BF16),
        ],
        [pltpu.VMEM((24, FRAMES), jnp.int32)],
        10**6,
        10**6,
        "prepare",
    )(*in_hbm([game_ids, flat(tokens), actions, valid_steps, rewards, end_flags]))
    column, other_bias, hits = lax.optimization_barrier((column, other_bias, hits))
    first_column = jnp.stack(column)
    first_mine = gather_plane(first_column)
    own, piece_second = lax.optimization_barrier((swap(first_column, "narrow", 1), piece_second))
    first_other = [own] + gather_cores(first_mine[1:])
    near = swap(piece_second, "wide", 4)
    near, far_piece = lax.optimization_barrier((near, piece_second))
    second_column = [piece_second, near, swap(piece_second, "wide", 8)]
    second_column += [swap(far_piece, "wide", 4 * k) for k in range(3, n_high)]
    second_column, across = lax.optimization_barrier(
        (jnp.stack(second_column), first_other[3])
    )
    first_other = first_other[0:3] + [across]
    second_mine = gather_plane(second_column)
    first_parts = in_blocks(first_mine, wide) + in_blocks(first_other, wide)

    kept_specs = [row_spec(shape) for shape, _ in KEPT]
    kept_shapes = [shaped((count,) + shape, dtype) for shape, dtype in KEPT]
    row_f32 = shaped((count, SEQ, D), F32)
    meta_spec = row_spec((SEQ, 128))
    vec_specs = [full_spec(vectors), full_spec(up_bias), full_spec(up_bias)]
    w_attention_spec = pl.BlockSpec((D, 1024), lambda i: (0, 0))
    w_ff_spec = pl.BlockSpec((D, 2048), lambda i: (0, 0))
    side_spec = pl.BlockSpec((D, 128), lambda i: (0, 0))
    hits_spec = row_spec((SEQ, ROWS))
    results = call(
        functools.partial(first_forward_kernel, fast),
        (count,),
        [hits_spec] + vec_specs + [VMEM_SPEC] * 8,
        [w_attention_spec, w_ff_spec, side_spec, row_spec((SEQ, D))] + kept_specs,
        [shaped((D, 1024), BF16), shaped((D, 2048), BF16), shaped((D, 128), BF16), row_f32]
        + kept_shapes,
        [pltpu.VMEM((D, COL_FIRST), BF16), pltpu.VMEM((SEQ, D), F32)] + FORWARD_WORK,
        4 * 10**9,
        20 * 10**6,
        "first_forward",
    )(hits, *in_hbm([vectors, up_bias, other_bias]), *resident(first_parts))
    w_attention, w_ff, side_copy, stream = results[0:4]
    kept = results[4:]
    received, side_copy = lax.optimization_barrier((second_mine[1:], side_copy))
    second_mine = second_mine[0:1] + received
    second_other = gather_cores(second_mine)
    second_parts = in_blocks(second_mine, wide) + in_blocks(second_other, wide)

    def blocks(cols):
        return pl.BlockSpec((4, 4, 16, cols), lambda i: (0, 0, 0, 0))

    def block_shapes(cols):
        return [shaped((4, 4, 16, cols), BF16)] * 2

    small_spec = pl.BlockSpec((SMALL_ROWS, 8, D), lambda i: (0, 0, 0))
    small_shape = shaped((SMALL_ROWS, 8, D), F32)
    small_scratch = pltpu.VMEM((SMALL_ROWS, 8, D), F32)
    scalar_spec = pl.BlockSpec((8, 128), lambda i: (0, 0))
    grad_stream, keep_second, send_second, small_grads, scalars = call(
        functools.partial(middle_kernel, fast),
        (count,),
        [meta_spec, row_spec((SIDE_ROWS, 128))]
        + vec_specs
        + [side_spec, row_spec((SEQ, D))]
        + [VMEM_SPEC] * 8,
        [row_spec((SEQ, D))] + [blocks(HALF_SECOND_COLS)] * 2 + [small_spec, scalar_spec],
        [row_f32] + block_shapes(HALF_SECOND_COLS) + [small_shape, shaped((8, 128), F32)],
        [
            pltpu.VMEM((D, COL_SECOND + 128), BF16),
            pltpu.VMEM((D, COL_SECOND + 128), F32),
            small_scratch,
        ]
        + [pltpu.VMEM(shape, dtype) for shape, dtype in KEPT[0:7]]
        + [pltpu.VMEM((2 * SEQ, D), BF16), pltpu.VMEM(*KEPT[8])]
        + [pltpu.VMEM((2 * SEQ, FF), BF16), pltpu.VMEM(*KEPT[10])]
        + [pltpu.VMEM((2 * SEQ, D), BF16)] * 2
        + [pltpu.VMEM(*a) for a in KEPT[13:16]]
        + FORWARD_WORK
        + BACKWARD_WORK[0:1]
        + BACKWARD_WORK[2:6]
        + [pltpu.VMEM((2 * SEQ, 768), BF16)]
        + [
            PROJ_WORK,
            pltpu.VMEM((2 * SEQ, FF), BF16),
            ONES_WORK,
            pltpu.VMEM((SEQ, D), F32),
            pltpu.VMEM((2 * SEQ, D), BF16),
            pltpu.VMEM((SEQ, D), F32),
            pltpu.VMEM((KEYS, D), BF16),
            pltpu.VMEM((SEQ, D), BF16),
            pltpu.VMEM((SEQ, 128), F32),
            pltpu.VMEM((2 * SEQ, D), BF16),
            pltpu.VMEM((SEQ, VOCAB), F32),
            pltpu.VMEM((2 * SEQ, VOCAB + 128), BF16),
            pltpu.VMEM((SIDE_ROWS, SEQ), BF16),
            pltpu.VMEM((SEQ, SIDE_ROWS), BF16),
            pltpu.VMEM((2 * SEQ, D), BF16),
        ],
        15 * 10**9,
        20 * 10**6,
        "middle",
    )(
        meta,
        frame_meta,
        *in_hbm([vectors, up_bias, other_bias]),
        side_copy,
        stream,
        *resident(second_parts),
    )
    second_sums = add_cores(keep_second, send_second, wide, n_high)

    def joined(a):
        return a.reshape((count * a.shape[1],) + a.shape[2:])

    kept_ff = (kept[8], kept[13], kept[9], kept[10], kept[12])
    grad_mid, keep_ff, send_ff, small_grads = call(
        functools.partial(ff_backward_kernel, fast),
        (count,),
        [full_spec(vectors), w_ff_spec, row_spec((SEQ, D)), small_spec]
        + [row_spec(a.shape[1:]) for a in kept_ff],
        [row_spec((SEQ, D))] + [blocks(HALF_GRAD_COLS)] * 2 + [small_spec],
        [row_f32] + block_shapes(HALF_GRAD_COLS) + [small_shape],
        [
            pltpu.VMEM((D, 2048), F32),
            small_scratch,
            pltpu.VMEM((SEQ, D), BF16),
            pltpu.VMEM((SEQ, FF), BF16),
            ONES_WORK,
            pltpu.VMEM((SEQ, FF), F32),
            pltpu.VMEM((SEQ, D), F32),
        ],
        4 * 10**9,
        10 * 10**6,
        "ff_backward",
    )(*in_hbm([vectors]), w_ff, grad_stream, small_grads, *kept_ff)
    ff_sums = add_cores(keep_ff, send_ff, wide, n_high)
    other_sums = [jnp.concatenate(pair, axis=-1) for pair in zip(second_sums, ff_sums)]
    others_received = swap_plane(other_sums)
    kept_attention = (kept[14], kept[15]) + tuple(kept[0:7])
    joined_attention = [joined(kept[7]), joined(kept[11]), joined(hits)]
    keep_rest, send_rest, small_grads = call(
        functools.partial(attention_backward_kernel, fast),
        (count,),
        [full_spec(vectors), w_attention_spec, row_spec((SEQ, D)), small_spec]
        + [row_spec(a.shape[1:]) for a in kept_attention]
        + [VMEM_SPEC] * 3
        + [ANY_SPEC],
        [blocks(HALF_GRAD_COLS)] * 2 + [pl.BlockSpec((SMALL_ROWS, D), lambda i: (0, 0))],
        block_shapes(HALF_GRAD_COLS) + [shaped((SMALL_ROWS, D), F32)],
        [pltpu.VMEM((D, 2048), F32), small_scratch, pltpu.VMEM((KEYS, D), BF16)]
        + [pltpu.VMEM((count * SEQ, D), BF16)] * 2
        + [pltpu.VMEM((count * SEQ, 768), BF16)]
        + BACKWARD_WORK[0:6]
        + [PROJ_WORK, pltpu.VMEM((SEQ, D), F32)],
        6 * 10**9,
        20 * 10**6,
        "attention_backward",
    )(
        *in_hbm([vectors]),
        w_attention,
        grad_mid,
        small_grads,
        *kept_attention,
        *joined_attention,
        other_sums[0],
    )
    others_received, keep_rest = lax.optimization_barrier((others_received, keep_rest))
    others = add_plane(other_sums[0], others_received)
    keep_rest = in_pieces(keep_rest, wide, n_high)
    received = swap(in_pieces(send_rest, wide, n_high), "narrow", 1)
    others, received = lax.optimization_barrier((others, received))
    rest_sums = [keep_rest[p].astype(F32) + received[p].astype(F32) for p in range(4)]
    rest_received = swap_plane(rest_sums)
    other_pieces = column_pieces(others)
    rest_pieces = column_pieces(add_plane(rest_sums[0], rest_received))

    grad_rest, grad_others, table_part, small = call(
        functools.partial(finish_kernel, fast),
        None,
        [VMEM_SPEC] * (2 * n_high + 1),
        [VMEM_SPEC] * 4,
        [
            shaped((rows, HALF_GRAD_COLS), F32),
            shaped((rows, HALF_GRAD_COLS + HALF_SECOND_COLS), F32),
            shaped((rows, 512), F32),
            shaped((4 * n_high, 8, 128), F32),
        ],
        [],
        10**6,
        10**6,
        "finish",
    )(*resident(rest_pieces + other_pieces), scalars)

    gathered = lax.all_to_all(small, "wide", 0, 0)
    beside = swap(gathered, "narrow", 1)
    quarters = []
    if not fast:
        total = lax.psum(small_grads, ("wide", "narrow"))
        quarters = [total.reshape(4, 8, 2, 128).transpose(0, 2, 1, 3).reshape(4, 16, 128)]
    swapped = swap(table_part, "narrow", 1)

    flat_params = [a for group in params for a in group]
    results = call(
        functools.partial(adam_kernel, fast),
        None,
        [VMEM_SPEC] * (32 + len(quarters)),
        [VMEM_SPEC] * 30,
        [shaped((1, 1), F32)] * 3 + [shaped(a.shape, F32) for a in flat_params],
        [pltpu.VMEM((SMALL_ROWS, D), F32)],
        10**6,
        10**6,
        "adam",
    )(grad_rest, grad_others, *resident([swapped, gathered, beside]), *quarters, *flat_params)
    news = list(results[3:])
    for group in (0, 2, 5, 8):
        for member in range(3 * group, 3 * group + 3):
            news[member] = flat(news[member])
    return tuple(a.reshape(()) for a in results[0:3]) + tuple(news)


def solution(mesh):
    placed = (
        P("wide", None, None),
        P("wide", None),
        P("wide"),
        P("wide", None),
        P("wide", None),
        P("wide", None),
        P(None, "wide"),
        P(None, "wide"),
        P(None, "wide"),
        P(None, None, "wide", "narrow"),
        P(None, None, "wide", "narrow"),
        P(None, None, "wide", "narrow"),
        P(None, "narrow", "wide"),
        P(None, "narrow", "wide"),
        P(None, "narrow", "wide"),
        P(None, "wide", "narrow"),
        P(None, "wide", "narrow"),
        P(None, "wide", "narrow"),
        P(None, "narrow"),
        P(None, "narrow"),
        P(None, "narrow"),
        P(None, "narrow", "wide"),
        P(None, "narrow", "wide"),
        P(None, "narrow", "wide"),
        P(),
        P(),
        P(),
        P("wide", "narrow"),
        P("wide", "narrow"),
        P("wide", "narrow"),
        P("wide", None),
        P("wide", None),
        P("wide", None),
    )
    return jax.shard_map(
        per_device,
        mesh=mesh,
        in_specs=placed,
        out_specs=(P(), P(), P()) + placed[6:],
        check_vma=False,
    )
```
